32 devices in a mesh: dp: 16 (over z, x, core), fsdp: 2 (over y).
Axes of the slice: x: 2, y: 2, z: 4, core: 2. Of those that a mesh axis runs over, the one named last changes fastest.
Arguments:
- tokens: bfloat16 [32, 1024, 768], P(('dp', 'fsdp')), may hold values from -6 to 6
- teacher: bfloat16 [32, 1024, 768], P(('dp', 'fsdp')), may hold values from -6 to 6
- lengths: int32 [32], P(('dp', 'fsdp')), may hold values from 256 to 1024, as said below
- loss_mask: int32 [32, 1024], P(('dp', 'fsdp')), may hold values 0 or 1
- owners: int32 [920], replicated, may hold values from 0 to 31, as said below
- master: float32 [1632, 4096], P(('dp', 'fsdp')), as said below
- first_moment: float32 [1632, 4096], P(('dp', 'fsdp')), as said below
- second_moment: float32 [1632, 4096], P(('dp', 'fsdp')), as said below
Outputs:
- block_out: bfloat16 [32, 1024, 768], P(('dp', 'fsdp'))
- input_grad: float32 [32, 1024, 768], P(('dp', 'fsdp'))
- loss: float32 [], replicated
- new_first: float32 [1632, 4096], P(('dp', 'fsdp'))
- new_second: float32 [1632, 4096], P(('dp', 'fsdp'))
- new_master: float32 [1632, 4096], P(('dp', 'fsdp'))
The draws below stay inside these ranges and needn't reach their ends.
Inputs may be any that keep to these rules, and one draw needn't show every extreme that they name: `lengths`: one sequence has exactly 1024 valid positions and one exactly a quarter of 1024. owners[b] is the index along dp+fsdp (dp slowest) of the device that owns block b; each device owns at most 51 blocks, and some device exactly 51. `master`: device i's rows i * 51 onward hold the blocks it owns in increasing block order; its other rows, and entries past 3765320 in the flattened order, are zero. `first_moment`: same layout as master, zero where master's layout holds nothing. `second_moment`: same layout as master, zero where master's layout holds nothing and positive elsewhere.
All inputs are finite; a program needn't handle non-finite values. No bound on the sum of `loss_mask` on one device may be relied on, other than what follows from the above.
Results may differ from the reference program's by a relative error of at most 0.0028.
The reference program's roundings to bfloat16 on the way count: a program that leaves them out, or rounds other values in their place, can miss the bound.
Values may be sent and summed in bfloat16 or wider, within the bound.
No kernel may reach another device: no remote copies, remote signals or barrier semaphores. Data moves between devices by JAX's collectives and lax.ppermute only.
A program may use at most 576 MiB of HBM per device.

```python
from functools import partial
import jax
import jax.numpy as jnp
from jax import lax

D = 768
INNER = 1536
NSTATE = 128
HEADDIM = 64
KCONV = 4
SCAN_LEN = 256
SEQ_LEN = 1024
PBLOCK = 4096
STEP = 10
HEADS = 24
CONVCH = 1792
PROJ = 3352
PTOT = 3765320
NBLK = 920
CAP = 51
SEQS = 32
DEVICES = 32


def segment_ends_drawn():
    counts_list = [D * PROJ, INNER * D, CONVCH * KCONV, CONVCH, HEADS, HEADS, HEADS, D, INNER]
    bounds = []
    running = 0
    for amount in counts_list:
        running = running + amount
        bounds.append(running)
    return bounds


def owner_table(key):
    key = jax.random.fold_in(key, 101)
    keys_list = jax.random.split(key, 4)
    slots_total = DEVICES * CAP
    slot_device = jnp.arange(slots_total, dtype=jnp.int32) // CAP
    favour = jax.random.randint(keys_list[0], (DEVICES,), 0, 65536, dtype=jnp.int32)
    chosen = jax.random.randint(keys_list[1], (), 0, DEVICES, dtype=jnp.int32)
    favour = favour + jnp.where(jnp.arange(DEVICES, dtype=jnp.int32) == chosen, 131072, 0).astype(jnp.int32)
    jitter = jax.random.randint(keys_list[2], (slots_total,), 0, 65536, dtype=jnp.int32)
    scores = (jitter + favour[slot_device]) * slots_total + jnp.arange(slots_total, dtype=jnp.int32)
    ranking = jnp.argsort(-scores)
    picked = slot_device[ranking[:NBLK]]
    shuffle = jax.random.permutation(keys_list[3], NBLK)
    return picked[shuffle].astype(jnp.int32)


def slot_rows_drawn(owners):
    block_index = jnp.arange(NBLK, dtype=jnp.int32)
    matching = owners[:, None] == owners[None, :]
    earlier = block_index[None, :] < block_index[:, None]
    order_rank = jnp.sum((matching & earlier).astype(jnp.int32), axis=1).astype(jnp.int32)
    return (owners * CAP + order_rank).astype(jnp.int32)


def slot_layout(key, flat_values):
    rows_of = slot_rows_drawn(owner_table(key))
    return jnp.zeros((DEVICES * CAP, PBLOCK), jnp.float32).at[rows_of].set(flat_values.reshape(NBLK, PBLOCK))


def segment_pick(options):
    bounds = segment_ends_drawn()
    flat_index = jnp.arange(NBLK * PBLOCK, dtype=jnp.int32)
    picked = jnp.zeros((NBLK * PBLOCK,), jnp.float32)
    begin_at = 0
    for end_at, option in zip(bounds, options):
        inside = (flat_index >= begin_at) & (flat_index < end_at)
        picked = jnp.where(inside, option, picked)
        begin_at = end_at
    return picked


def grad_scales():
    base_scale = 1.0 / (D * (0.6 * SEQS * SEQ_LEN) ** 0.5)
    return [factor * base_scale for factor in [3.0, 3.5, 3.0, 3.0, 8.0, 8.0, 8.0, 3.0, 3.0]]


def draw_owners(key, part):
    return owner_table(key)


def draw_master(key, part):
    base_key = key
    key = jax.random.fold_in(key, 11)
    keys_list = jax.random.split(key, 2)
    entries = NBLK * PBLOCK
    gaussian = jax.random.normal(keys_list[0], (entries,), jnp.float32)
    uniform_draw = jax.random.uniform(keys_list[1], (entries,), jnp.float32)
    spread = 2.0 * uniform_draw - 1.0
    step_size = jnp.exp(jnp.log(0.001) + uniform_draw * jnp.log(100.0))
    options = [gaussian * D ** (-0.5), gaussian * INNER ** (-0.5), 0.8 * spread, 0.3 * spread, jnp.log(jnp.expm1(step_size)), uniform_draw * jnp.log(16.0), 0.5 + uniform_draw, 0.7 + 0.6 * uniform_draw, 0.7 + 0.6 * uniform_draw]
    return slot_layout(base_key, segment_pick(options))


def draw_first_moment(key, part):
    base_key = key
    key = jax.random.fold_in(key, 12)
    gaussian = jax.random.normal(key, (NBLK * PBLOCK,), jnp.float32)
    options = [gaussian * factor * (0.1 / 0.9) for factor in grad_scales()]
    return slot_layout(base_key, segment_pick(options))


def draw_second_moment(key, part):
    base_key = key
    key = jax.random.fold_in(key, 13)
    uniform_draw = jax.random.uniform(key, (NBLK * PBLOCK,), jnp.float32, 1.0, 4.0)
    options = [uniform_draw * factor * factor * (0.001 / 0.999) for factor in grad_scales()]
    return slot_layout(base_key, segment_pick(options))


def draw_lengths(key, part):
    key = jax.random.fold_in(key, 7)
    keys_list = jax.random.split(key, 3)
    positions = jnp.arange(SEQS, dtype=jnp.int32)
    lower = SEQ_LEN // 4 + 3 * SEQ_LEN // 4 * positions // SEQS
    upper = jnp.minimum(lower + SEQ_LEN // 4, SEQ_LEN)
    drawn = jax.random.randint(keys_list[0], (SEQS,), lower, upper + 1, dtype=jnp.int32)
    longest = jax.random.randint(keys_list[1], (), SEQS // 2, SEQS, dtype=jnp.int32)
    shortest = jax.random.randint(keys_list[2], (), 0, SEQS // 2, dtype=jnp.int32)
    drawn = jnp.where(positions == longest, SEQ_LEN, drawn)
    drawn = jnp.where(positions == shortest, SEQ_LEN // 4, drawn)
    return drawn.astype(jnp.int32)


def with_ends(values, own_key, least, high):
    longest = values.shape.index(max(values.shape))
    spots = []
    for shift in (0, 1):
        where = [jax.random.randint(jax.random.fold_in(own_key, axis), (), 0, length) for axis, length in enumerate(values.shape)]
        where[longest] = (where[longest] + shift) % values.shape[longest]
        spots.append(tuple(where))
    return values.at[spots[0]].set(least).at[spots[1]].set(high)


def block_scale(rng, extent, shards, smallest, largest):
    factor_of = 1.0
    for position, parts in shards:
        steps = jax.random.uniform(jax.random.fold_in(jax.random.fold_in(rng, 6), position), (parts,), jnp.float32, smallest / len(shards), largest / len(shards))
        factor_of = factor_of * jnp.repeat(jnp.exp(steps), extent[position] // parts).reshape((-1,) + (1,) * (len(extent) - 1 - position))
    return factor_of


def normal_values(stream_key, extent, width, bound, cuts=(), kind=jnp.bfloat16):
    values = jax.random.normal(stream_key, extent, jnp.float32) * width
    if len(cuts) > 0:
        values = block_scale(stream_key, extent, cuts, -0.22, 0.18) * values
    return jnp.clip(values, min=-bound, max=bound).astype(kind)


def setup_inputs(seed: int = 0) -> dict:
    seeds = jax.random.split(jax.random.key(seed), 9)
    return {
        "tokens": normal_values(seeds[0], (SEQS, SEQ_LEN, D), 1.0, 6.0, ((0, 32),)),
        "teacher": normal_values(seeds[1], (SEQS, SEQ_LEN, D), 1.0, 6.0, ((0, 32),)),
        "lengths": draw_lengths(jax.random.fold_in(seeds[8], 71), 0),
        "loss_mask": with_ends((jax.random.randint(seeds[3], (SEQS, SEQ_LEN), 0, 8) < 7).astype(jnp.int32), jax.random.fold_in(seeds[3], 1), 0, 1),
        "owners": draw_owners(jax.random.fold_in(seeds[8], 71), 0),
        "master": draw_master(jax.random.fold_in(seeds[8], 71), 0),
        "first_moment": draw_first_moment(jax.random.fold_in(seeds[8], 71), 0),
        "second_moment": draw_second_moment(jax.random.fold_in(seeds[8], 71), 0),
    }


@jax.custom_vjp
def low(v):
    return lax.optimization_barrier(v.astype(jnp.bfloat16)).astype(jnp.float32)

@jax.custom_vjp
def low_back(v):
    return v

def low_keep(v):
    return (low(v), None)

def low_pass(kept, grad):
    return (grad,)

def back_keep(v):
    return (v, None)

def back_low(kept, grad):
    return (low(grad),)
low.defvjp(low_keep, low_pass)
low_back.defvjp(back_keep, back_low)
PRECISE = lax.Precision.HIGHEST
NORM_EPS = 1e-05
ADAM_EPS = 1e-08
BETA_ONE = 0.9
BETA_TWO = 0.999
MATRIX_RATE = 0.03
VECTOR_RATE = 0.2
WEIGHT_DECAY = 0.1

def segment_ends():
    counts_list = [D * PROJ, INNER * D, CONVCH * KCONV, CONVCH, HEADS, HEADS, HEADS, D, INNER]
    bounds = []
    running = 0
    for amount in counts_list:
        running = running + amount
        bounds.append(running)
    return bounds

def slot_rows(owners, capacity):
    block_index = jnp.arange(owners.shape[0], dtype=jnp.int32)
    matching = owners[:, None] == owners[None, :]
    earlier = block_index[None, :] < block_index[:, None]
    order_rank = lax.optimization_barrier(jnp.sum((matching & earlier).astype(jnp.int32), axis=1)).astype(jnp.int32)
    return (owners * capacity + order_rank).astype(jnp.int32)

def unpack(flat_params):
    bounds = segment_ends()
    starts = [0] + bounds[:-1]
    segments = [flat_params[begin_at:end_at] for begin_at, end_at in zip(starts, bounds)]
    return (segments[0].reshape(D, PROJ), segments[1].reshape(INNER, D), segments[2].reshape(CONVCH, KCONV)) + tuple(segments[3:])

def block_step(head_rate, carried, pieces):
    values, deltas, inputs_b, readout = pieces
    length = deltas.shape[2]
    decays = jnp.cumsum(deltas * head_rate[None, :, None], axis=2)
    differ = decays[:, :, :, None] - decays[:, :, None, :]
    causal = jnp.arange(length)[:, None] >= jnp.arange(length)[None, :]
    within = jnp.exp(jnp.where(causal[None, None, :, :], differ, -1000000000.0))
    scaled = values * deltas[..., None]
    affinity = jnp.einsum('gtn,gsn->gts', readout, inputs_b, precision=PRECISE)
    mixing = affinity[:, None, :, :] * within
    output = jnp.einsum('ghts,ghsp->ghtp', mixing, scaled, precision=PRECISE)
    output = output + jnp.einsum('gtn,ghpn->ghtp', readout, carried, precision=PRECISE) * jnp.exp(decays)[..., None]
    tail_decay = jnp.exp(decays[:, :, -1:] - decays)
    fresh_state = jnp.einsum('gsn,ghsp->ghpn', inputs_b, scaled * tail_decay[..., None], precision=PRECISE)
    renewed = jnp.exp(decays[:, :, -1])[:, :, None, None] * carried + fresh_state
    return (renewed, output)

def mixer_layer(projected_rows, conv_weight, conv_bias, dt_bias, a_log, skip_gain, gate_gain):
    groups = projected_rows.shape[0]
    length = projected_rows.shape[1]
    gate_raw = projected_rows[..., :INNER]
    conv_in = projected_rows[..., INNER:INNER + CONVCH]
    dt_raw = projected_rows[..., INNER + CONVCH:]
    padded = jnp.pad(conv_in, ((0, 0), (KCONV - 1, 0), (0, 0)))
    conv_out = conv_bias + padded[:, 0:length, :] * conv_weight[:, 0]
    for offset in range(1, KCONV):
        conv_out = conv_out + padded[:, offset:offset + length, :] * conv_weight[:, offset]
    mixed_in = jax.nn.silu(conv_out)
    values_rows = mixed_in[..., :INNER].reshape(groups, length, HEADS, HEADDIM)
    values = jnp.transpose(values_rows, (0, 2, 1, 3))
    inputs_b = mixed_in[..., INNER:INNER + NSTATE]
    readout = mixed_in[..., INNER + NSTATE:]
    deltas = jnp.transpose(jax.nn.softplus(dt_raw + dt_bias), (0, 2, 1))
    head_rate = -jnp.exp(a_log)
    blocks = length // SCAN_LEN

    def heads_blocks(stacked):
        shaped = stacked.reshape((groups, HEADS, blocks, SCAN_LEN) + stacked.shape[3:])
        return jnp.moveaxis(shaped, 2, 0)

    def rows_blocks(stacked):
        return jnp.moveaxis(stacked.reshape((groups, blocks, SCAN_LEN) + stacked.shape[2:]), 1, 0)
    stepper = jax.checkpoint(partial(block_step, head_rate))
    initial = jnp.zeros((groups, HEADS, HEADDIM, NSTATE), jnp.float32)
    last_state, outputs = lax.scan(stepper, initial, (heads_blocks(values), heads_blocks(deltas), rows_blocks(inputs_b), rows_blocks(readout)))
    ssm_heads = jnp.moveaxis(outputs, 0, 2).reshape(groups, HEADS, length, HEADDIM)
    ssm_out = jnp.transpose(ssm_heads, (0, 2, 1, 3))
    ssm_out = ssm_out + skip_gain[:, None] * values_rows
    gated = ssm_out.reshape(groups, length, INNER) * jax.nn.silu(gate_raw)
    return gated * lax.rsqrt(lax.optimization_barrier(jnp.mean(gated * gated, axis=-1, keepdims=True)) + NORM_EPS) * gate_gain

def block_forward(params, inputs, target, weight_mask):
    rounded_params = [low(tensor) for tensor in params]
    input_weight, output_weight, conv_weight, conv_bias, dt_bias, a_log, skip_gain, norm_gain, gate_gain = rounded_params
    inverse = lax.rsqrt(lax.optimization_barrier(jnp.mean(inputs * inputs, axis=-1, keepdims=True)) + NORM_EPS)
    normed = low(inputs * inverse * norm_gain)
    projected_rows = low_back(jnp.einsum('gld,de->gle', normed, input_weight, precision=PRECISE))
    mixed_out = low(mixer_layer(projected_rows, conv_weight, conv_bias, dt_bias, a_log, skip_gain, gate_gain))
    residual_branch = low_back(jnp.einsum('gle,ed->gld', mixed_out, output_weight, precision=PRECISE))
    result = inputs + residual_branch
    misfit = result - target
    return (jnp.sum(weight_mask[..., None] * misfit * misfit), result)

def adam_update(gradient, weights, moment_one, moment_two, block_ids):
    flat_index = block_ids[:, None] * PBLOCK + jnp.arange(PBLOCK, dtype=jnp.int32)[None, :]
    matrix = flat_index < segment_ends()[1]
    step_rate = jnp.where(matrix, MATRIX_RATE, VECTOR_RATE)
    decay_rate = jnp.where(matrix, WEIGHT_DECAY, 0.0)
    first_new = BETA_ONE * moment_one + (1.0 - BETA_ONE) * gradient
    second_new = BETA_TWO * moment_two + (1.0 - BETA_TWO) * gradient * gradient
    normalized = first_new / (1.0 - BETA_ONE ** STEP) / (jnp.sqrt(second_new / (1.0 - BETA_TWO ** STEP)) + ADAM_EPS)
    weights_new = weights - step_rate * (normalized + decay_rate * weights)
    return (first_new, second_new, weights_new)

def reference(tokens, teacher, lengths, loss_mask, owners, master, first_moment, second_moment):
    slot_of_block = slot_rows(owners, CAP)
    params = unpack(master[slot_of_block].reshape(-1))
    positions = jnp.arange(SEQ_LEN, dtype=jnp.int32)
    valid_mask = (positions[None, :] < lengths[:, None]).astype(jnp.float32)
    weight_mask = valid_mask * loss_mask.astype(jnp.float32)
    group_size = 4 if SEQS % 4 == 0 else 1
    group_count = SEQS // group_size

    def regroup(stacked):
        return stacked.reshape((group_count, group_size) + stacked.shape[1:])

    def accumulate(carried, batch_rows):
        grad_sums, error_sum = carried
        inputs, target, mask_rows = batch_rows

        def forward_only(tensors, values):
            return block_forward(tensors, values, target, mask_rows)
        error_value, pullback, result = jax.vjp(forward_only, params, inputs, has_aux=True)
        grad_params, grad_inputs = pullback(jnp.ones((), jnp.float32))
        grad_sums = tuple((total_grad + fresh_grad for total_grad, fresh_grad in zip(grad_sums, grad_params)))
        return ((grad_sums, error_sum + error_value), (result, grad_inputs))
    initial = (tuple((jnp.zeros_like(tensor) for tensor in params)), jnp.zeros((), jnp.float32))
    batches = (regroup(tokens.astype(jnp.float32)), regroup(teacher.astype(jnp.float32)), regroup(weight_mask))
    (grad_sums, error_sum), (results, input_grads) = lax.scan(accumulate, initial, batches)
    results = results.reshape(SEQS, SEQ_LEN, D)
    input_grad = input_grads.reshape(SEQS, SEQ_LEN, D)
    position_count = jnp.sum(weight_mask)
    divisor = position_count * D
    block_out = (results * valid_mask[:, :, None]).astype(jnp.bfloat16)
    mean_loss = error_sum / divisor
    flat_grad = jnp.concatenate([tensor.reshape(-1) for tensor in grad_sums] + [jnp.zeros((NBLK * PBLOCK - PTOT,), jnp.float32)]) / divisor
    slots_total = master.shape[0]
    block_of_slot = jnp.zeros((slots_total,), jnp.int32).at[slot_of_block].set(jnp.arange(NBLK, dtype=jnp.int32))
    occupied = jnp.zeros((slots_total,), jnp.float32).at[slot_of_block].set(1.0)
    gradient = flat_grad.reshape(NBLK, PBLOCK)[block_of_slot] * occupied[:, None]
    new_first, new_second, new_master = adam_update(gradient, master, first_moment, second_moment, block_of_slot)
    return (block_out, input_grad, mean_loss, new_first, new_second, new_master)
```

```python
from functools import partial

import jax
import jax.numpy as jnp
from jax import lax
from jax.experimental import pallas as pl
from jax.experimental.pallas import tpu as pltpu
from jax.sharding import PartitionSpec as P

D = 768
INNER = 1536
NSTATE = 128
HEADDIM = 64
KCONV = 4
SCAN_LEN = 256
PBLOCK = 4096
STEP = 10
HEADS = 24
CONVCH = 1792
PROJ = 3352
PTOT = 3765320
NBLK = 920

LANES = 128
BROWS = PBLOCK // LANES
END_IN = D * PROJ
END_OUT = END_IN + INNER * D
MID0 = -(-END_IN // PBLOCK)
MID1 = END_OUT // PBLOCK
N0 = MID0 + NBLK - MID1
N1 = MID1 - MID0
F0_ROWS = N0 * BROWS
IN_ROWS = END_IN // LANES
HEAD_ROWS = MID0 * BROWS - IN_ROWS
TAIL_ROWS = (END_OUT - MID1 * PBLOCK) // LANES
OUT_ROWS = INNER * D // LANES
VEC_ROWS = (NBLK - MID1) * BROWS - TAIL_ROWS
VEC_AT = MID0 * BROWS + TAIL_ROWS
GROUP = 16
GROUPS = D // GROUP
GROUP_ROWS = GROUP * PROJ // LANES
COL_TILES = -(-PROJ // LANES)
WIDE = COL_TILES * LANES
OUT_TILES = D // LANES

NORM_EPS = 1e-05
ADAM_EPS = 1e-08
BETA_ONE = 0.9
BETA_TWO = 0.999
MATRIX_RATE = 0.03
VECTOR_RATE = 0.2
WEIGHT_DECAY = 0.1
PRECISE = lax.Precision.HIGHEST
AXES = ("dp", "fsdp")
VMEM_LIMIT = 60 * 1024 * 1024


def bits_of(count):
    return count.bit_length() - 1


def step_orders(dp, fsdp):
    wide = [("dp", i) for i in range(bits_of(dp))]
    narrow = [("fsdp", i) for i in range(bits_of(fsdp))]
    first = wide[:2] + narrow + wide[2:]
    second = wide[:1] + narrow + wide[1:]
    return first, second


def exchange(values, step):
    axis, bit = step
    size = lax.axis_size(axis)
    return lax.ppermute(values, axis, [(i, i ^ (1 << bit)) for i in range(size)])


def place_of(relative, order):
    shift_of = {"dp": bits_of(lax.axis_size("fsdp")), "fsdp": 0}
    place = jnp.zeros_like(relative)
    for axis, bit in order:
        place = place * 2 + ((relative >> (shift_of[axis] + bit)) & 1)
    return place


def make_plan(owners, capacity, devices, me):
    block = jnp.arange(NBLK, dtype=jnp.int32)
    mid = (block >= MID0) & (block < MID1)
    same = mid[:, None] == mid[None, :]
    before = (owners[None, :] < owners[:, None]) | (
        (owners[None, :] == owners[:, None]) & (block[None, :] < block[:, None])
    )
    order_in_class = jnp.sum((same & before).astype(jnp.int32), axis=1)
    home, slot = order_in_class % devices, order_in_class // devices
    device = jnp.arange(devices, dtype=jnp.int32)
    below = owners[None, :] < device[:, None]
    owned = owners[None, :] == device[:, None]

    def total(mask):
        return jnp.sum(mask.astype(jnp.int32), axis=1)

    start = (total(below & ~mid[None, :]), total(below & mid[None, :]))
    count = (total(owned & ~mid[None, :]), total(owned & mid[None, :]))
    early = total(owned & (block < MID0)[None, :])
    pair = 2 + max(capacity - 2, 0) // devices

    def pick(vector, index):
        return jnp.sum(jnp.where(device == index, vector, 0))

    my_start = [pick(v, me) for v in start]
    my_count = [pick(v, me) for v in count]
    my_early = pick(early, me)

    lane = jnp.arange(pair, dtype=jnp.int32)
    k0 = (device[:, None] - my_start[0]) % devices + lane[None, :] * devices
    k1 = (device[:, None] - my_start[1]) % devices + (pair - 1 - lane)[None, :] * devices
    row0 = jnp.where(k0 < my_early, k0, k0 + my_count[1])
    send_rows = jnp.where(
        k0 < my_count[0], row0, jnp.where(k1 < my_count[1], my_early + k1, 0)
    ).reshape(-1)

    slots = (-(-N0 // devices), -(-N1 // devices))

    def received(kind):
        wanted = me + devices * jnp.arange(slots[kind], dtype=jnp.int32)
        ends = start[kind] + count[kind]
        owner = jnp.sum((ends[None, :] <= wanted[:, None]).astype(jnp.int32), axis=1)
        owner = jnp.minimum(owner, devices - 1)
        base = jnp.sum(jnp.where(device[None, :] == owner[:, None], start[kind][None, :], 0), axis=1)
        turn = jnp.clip((wanted - base) // devices, 0, pair - 1)
        return owner * pair + (turn if kind == 0 else pair - 1 - turn)

    b0 = (me - start[0])[:, None] % devices + lane[None, :] * devices
    b1 = (me - start[1])[:, None] % devices + (pair - 1 - lane)[None, :] * devices
    back = jnp.where(
        b0 < count[0][:, None],
        (start[0][:, None] + b0) // devices,
        jnp.where(b1 < count[1][:, None], slots[0] + (start[1][:, None] + b1) // devices, 0),
    ).reshape(-1)

    row = jnp.arange(capacity, dtype=jnp.int32)
    is_mid = (row >= my_early) & (row < my_early + my_count[1])
    k = jnp.where(is_mid, row - my_early, jnp.where(row < my_early, row, row - my_count[1]))
    first = jnp.where(is_mid, my_start[1], my_start[0])
    turn = k // devices
    row_from = ((first + k) % devices) * pair + jnp.where(is_mid, pair - 1 - turn, turn)
    row_used = row < my_count[0] + my_count[1]
    row_from = jnp.where(row_used, row_from, 0)
    mine = (owners == me)[None, :]
    rank = jnp.sum((mine & (block[None, :] < block[:, None])).astype(jnp.int32), axis=1)
    row_block = jnp.sum(
        jnp.where(mine & (rank[None, :] == row[:, None]), block[None, :], 0), axis=1
    )
    return dict(
        home=home, slot=slot, slots=slots, pair=pair, send_rows=send_rows,
        received=(received(0), received(1)), back=back, row_from=row_from,
        row_used=row_used, row_block=row_block,
    )


ANY = pl.BlockSpec(memory_space=pl.ANY)
VMEM = pl.BlockSpec(memory_space=pltpu.VMEM)
SMEM = pl.BlockSpec(memory_space=pltpu.SMEM)


def params(**extra):
    return pltpu.CompilerParams(vmem_limit_bytes=VMEM_LIMIT, **extra)


def shape(dims, dtype):
    return jax.ShapeDtypeStruct(dims, dtype)


def send_kernel(table, master, out, flat):
    capacity = master.shape[0]
    for j in range(BROWS):
        flat[pl.ds(j, capacity, stride=BROWS), :] = master[:, j * LANES : (j + 1) * LANES]

    def step(i, carry):
        out[i] = flat[pl.ds(pl.multiple_of(table[i] * BROWS, BROWS), BROWS), :].astype(out.dtype)
        return carry

    lax.fori_loop(0, out.shape[0], step, 0)


def send_blocks(table, master):
    return pl.pallas_call(
        send_kernel,
        out_shape=shape((table.shape[0], BROWS, LANES), jnp.bfloat16),
        in_specs=[SMEM, VMEM],
        out_specs=VMEM,
        scratch_shapes=[pltpu.VMEM((master.shape[0] * BROWS, LANES), jnp.float32)],
        compiler_params=params(),
    )(table, master)


def pick_kernel(table, source, out):
    def step(i, carry):
        out[i] = source[table[i]]
        return carry

    lax.fori_loop(0, out.shape[0], step, 0)


def pick_blocks(table, source):
    return pl.pallas_call(
        pick_kernel,
        out_shape=shape((table.shape[0],) + source.shape[1:], source.dtype),
        in_specs=[SMEM, VMEM],
        out_specs=VMEM,
        compiler_params=params(),
    )(table, source)


def row_start(rho):
    return (PROJ * rho) // LANES, (PROJ * rho) % LANES


def copy_all(pairs, sem):
    copies = [pltpu.make_async_copy(a, b, sem.at[i]) for i, (a, b) in enumerate(pairs)]
    for c in copies:
        c.start()
    for c in copies:
        c.wait()


def spread_blocks(table, held, flat, count, first_row):
    def one(i):
        at = pl.multiple_of(first_row + i * BROWS, 16)
        flat[pl.ds(at, BROWS), :] = held[table[i]].astype(jnp.float32)

    def step(i, carry):
        for u in range(4):
            one(i * 4 + u)
        return carry

    lax.fori_loop(0, count // 4, step, 0)
    for i in range(count // 4 * 4, count):
        one(i)


def unpack_in_kernel(table, *refs):
    parts, (w_in, head, tail, vec, held, flat, tile, sem) = refs[:-8], refs[-8:]
    pairs, at = [], 0
    for part in parts:
        pairs.append((part, held.at[pl.ds(at, part.shape[0])]))
        at += part.shape[0]
    copy_all(pairs, sem)
    spread_blocks(table, held, flat, N0, 0)
    head[...] = flat[IN_ROWS : IN_ROWS + HEAD_ROWS, :]
    tail[...] = flat[MID0 * BROWS : MID0 * BROWS + TAIL_ROWS, :]
    vec[...] = flat[VEC_AT:F0_ROWS, :]
    lane = lax.broadcasted_iota(jnp.int32, (GROUPS, LANES), 1)

    def columns(j):
        for rho in range(GROUP):
            c, s = row_start(rho)
            x = flat[pl.ds(c + j, GROUPS, stride=GROUP_ROWS), :]
            if s:
                y = flat[pl.ds(c + j + 1, GROUPS, stride=GROUP_ROWS), :]
                x = jnp.where(
                    lane < LANES - s,
                    pltpu.roll(x, LANES - s, 1),
                    pltpu.roll(y, LANES - s, 1),
                )
            tile[pl.ds(rho, GROUPS, stride=GROUP), :] = x

    def step(j, carry):
        columns(j)
        w_in[:, pl.ds(pl.multiple_of(j * LANES, LANES), LANES)] = tile[...].astype(jnp.bfloat16)
        return carry

    lax.fori_loop(0, COL_TILES - 1, step, 0)
    columns(COL_TILES - 1)
    last = (COL_TILES - 1) * LANES
    inside = lax.broadcasted_iota(jnp.int32, (D, LANES), 1) < PROJ - last
    w_in[:, last:] = jnp.where(inside, tile[...], 0.0).astype(jnp.bfloat16)


def unpack_in(table, parts):
    held = sum(part.shape[0] for part in parts)
    return pl.pallas_call(
        unpack_in_kernel,
        out_shape=(
            shape((D, WIDE), jnp.bfloat16),
            shape((HEAD_ROWS, LANES), jnp.float32),
            shape((TAIL_ROWS, LANES), jnp.float32),
            shape((VEC_ROWS, LANES), jnp.float32),
        ),
        in_specs=[SMEM] + [ANY] * len(parts),
        out_specs=(VMEM,) * 4,
        scratch_shapes=[
            pltpu.VMEM((held, BROWS, LANES), jnp.bfloat16),
            pltpu.VMEM((F0_ROWS, LANES), jnp.float32),
            pltpu.VMEM((D, LANES), jnp.float32),
            pltpu.SemaphoreType.DMA((len(parts),)),
        ],
        compiler_params=params(),
    )(table, *parts)


def unpack_out_kernel(table, own, got, head, tail, w_out, held, flat, sem):
    half = own.shape[0]
    copy_all([(own, held.at[pl.ds(0, half)]), (got, held.at[pl.ds(half, half)])], sem)
    flat[0:HEAD_ROWS, :] = head[...]
    flat[OUT_ROWS - TAIL_ROWS : OUT_ROWS, :] = tail[...]
    spread_blocks(table, held, flat, N1, HEAD_ROWS)
    rows = 128

    def step(i, carry):
        at = pl.multiple_of(i * rows, rows)
        for j in range(OUT_TILES):
            x = flat[pl.ds(at * OUT_TILES + j, rows, stride=OUT_TILES), :]
            w_out[pl.ds(at, rows), j * LANES : (j + 1) * LANES] = x.astype(jnp.bfloat16)
        return carry

    lax.fori_loop(0, INNER // rows, step, 0)


def unpack_out(table, own, got, head, tail):
    return pl.pallas_call(
        unpack_out_kernel,
        out_shape=shape((INNER, D), jnp.bfloat16),
        in_specs=[SMEM, ANY, ANY, VMEM, VMEM],
        out_specs=VMEM,
        scratch_shapes=[
            pltpu.VMEM((2 * own.shape[0], BROWS, LANES), jnp.bfloat16),
            pltpu.VMEM((OUT_ROWS, LANES), jnp.float32),
            pltpu.SemaphoreType.DMA((2,)),
        ],
        compiler_params=params(),
    )(table, own, got, head, tail)


def scatter_blocks(table, flat, count, first_row, outs, sem):
    def step(i, carry):
        source = flat.at[pl.ds(pl.multiple_of(first_row + i * BROWS, 16), BROWS)]
        at, low = table[i], 0
        for out in outs:
            high = low + out.shape[0]

            @pl.when((at >= low) & (at < high))
            def _():
                pltpu.make_async_copy(source, out.at[at - low], sem).start()

            low = high
        return carry

    lax.fori_loop(0, count, step, 0)


def wait_rows(flat, count, first_row, sem):
    whole = flat.at[pl.ds(first_row, count * BROWS)]
    pltpu.make_async_copy(whole, whole, sem).wait()


def pack_in_kernel(table, grad, head, tail, vec, *refs):
    outs, (tiles, flat, sem, tile_sem) = refs[:-4], refs[-4:]
    copy_all(
        [
            (grad.at[:, pl.ds(j * LANES, LANES)], tiles.at[pl.ds(j * D, D)])
            for j in range(COL_TILES)
        ],
        tile_sem,
    )
    lane = lax.broadcasted_iota(jnp.int32, (GROUPS, LANES), 1)

    def load(rho, j):
        return tiles[pl.ds(j * D + rho, GROUPS, stride=GROUP), :]

    for rho in range(GROUP):
        _, s = row_start(rho)
        first = -(-PROJ * rho // LANES)
        col0 = first * LANES - PROJ * rho
        full = (PROJ - col0) // LANES

        def step(i, carry, rho=rho, first=first, col0=col0):
            x = load(rho, i)
            if col0:
                y = load(rho, i + 1)
                x = jnp.where(
                    lane < LANES - col0,
                    pltpu.roll(x, LANES - col0, 1),
                    pltpu.roll(y, LANES - col0, 1),
                )
            flat[pl.ds(first + i, GROUPS, stride=GROUP_ROWS), :] = x
            return carry

        lax.fori_loop(0, full, step, 0)
        left = PROJ - col0 - full * LANES
        if left:
            begin = col0 + full * LANES
            j, s = begin // LANES, begin % LANES
            x = pltpu.roll(load(rho, j), (LANES - s) % LANES, 1) if s else load(rho, j)
            if s + left > LANES:
                x = jnp.where(lane < LANES - s, x, pltpu.roll(load(rho, j + 1), LANES - s, 1))
            y = pltpu.roll(load(rho + 1, 0), left, 1)
            flat[pl.ds(first + full, GROUPS, stride=GROUP_ROWS), :] = jnp.where(lane < left, x, y)
    flat[IN_ROWS : IN_ROWS + HEAD_ROWS, :] = head[...]
    flat[MID0 * BROWS : MID0 * BROWS + TAIL_ROWS, :] = tail[...]
    flat[VEC_AT:F0_ROWS, :] = vec[...]
    scatter_blocks(table, flat, N0, 0, outs, sem)
    wait_rows(flat, N0, 0, sem)


def pack_in(table, grad, head, tail, vec, sizes):
    return pl.pallas_call(
        pack_in_kernel,
        out_shape=tuple(shape((n, BROWS, LANES), jnp.float32) for n in sizes),
        in_specs=[SMEM, ANY] + [VMEM] * 3,
        out_specs=(ANY,) * len(sizes),
        scratch_shapes=[
            pltpu.VMEM((COL_TILES * D, LANES), jnp.float32),
            pltpu.VMEM((F0_ROWS, LANES), jnp.float32),
            pltpu.SemaphoreType.DMA,
            pltpu.SemaphoreType.DMA((COL_TILES,)),
        ],
        compiler_params=params(),
    )(table, grad, head, tail, vec)


def pack_out_kernel(table, grad, *refs):
    outs, (head, tail, flat, sem) = refs[:-4], refs[-4:]
    rows = 128

    def step(i, carry):
        at = pl.multiple_of(i * rows, rows)
        for j in range(OUT_TILES):
            flat[pl.ds(at * OUT_TILES + j, rows, stride=OUT_TILES), :] = grad[
                pl.ds(at, rows), j * LANES : (j + 1) * LANES
            ]
        return carry

    lax.fori_loop(0, INNER // rows, step, 0)
    head[...] = flat[0:HEAD_ROWS, :]
    tail[...] = flat[OUT_ROWS - TAIL_ROWS : OUT_ROWS, :]
    scatter_blocks(table, flat, N1, HEAD_ROWS, outs, sem)
    wait_rows(flat, N1, HEAD_ROWS, sem)


def pack_out(table, grad, sizes):
    return pl.pallas_call(
        pack_out_kernel,
        out_shape=tuple(shape((n, BROWS, LANES), jnp.float32) for n in sizes)
        + (shape((HEAD_ROWS, LANES), jnp.float32), shape((TAIL_ROWS, LANES), jnp.float32)),
        in_specs=[SMEM, VMEM],
        out_specs=(ANY,) * len(sizes) + (VMEM, VMEM),
        scratch_shapes=[
            pltpu.VMEM((OUT_ROWS, LANES), jnp.float32),
            pltpu.SemaphoreType.DMA,
        ],
        compiler_params=params(),
    )(table, grad)


def adam_kernel(table, scale, got, limit, used, master, first, second, o_first, o_second, o_master, flat):
    capacity = master.shape[0]

    def step(i, carry):
        flat[pl.ds(pl.multiple_of(i * BROWS, BROWS), BROWS), :] = got[table[i]]
        return carry

    lax.fori_loop(0, capacity, step, 0)
    lane = lax.broadcasted_iota(jnp.int32, (capacity, LANES), 1)
    divisor = scale[0]
    for j in range(BROWS):
        cols = slice(j * LANES, (j + 1) * LANES)
        grad = jnp.where(used[...] > 0, flat[pl.ds(j, capacity, stride=BROWS), :], 0.0) / divisor
        matrix = lane + j * LANES < limit[...]
        weights = master[:, cols]
        new_first = BETA_ONE * first[:, cols] + (1.0 - BETA_ONE) * grad
        new_second = BETA_TWO * second[:, cols] + (1.0 - BETA_TWO) * grad * grad
        normal = (
            new_first
            / (1.0 - BETA_ONE**STEP)
            / (jnp.sqrt(new_second / (1.0 - BETA_TWO**STEP)) + ADAM_EPS)
        )
        rate = jnp.where(matrix, MATRIX_RATE, VECTOR_RATE)
        decay = jnp.where(matrix, WEIGHT_DECAY, 0.0)
        o_first[:, cols] = new_first
        o_second[:, cols] = new_second
        o_master[:, cols] = weights - rate * (normal + decay * weights)


def adam(table, divisor, got, row_block, row_used, master, first, second):
    capacity = master.shape[0]
    limit = jnp.broadcast_to((END_OUT - row_block * PBLOCK)[:, None], (capacity, LANES))
    used = jnp.broadcast_to(row_used.astype(jnp.int32)[:, None], (capacity, LANES))
    return pl.pallas_call(
        adam_kernel,
        out_shape=(shape(master.shape, jnp.float32),) * 3,
        in_specs=[SMEM, SMEM] + [VMEM] * 6,
        out_specs=(VMEM,) * 3,
        scratch_shapes=[pltpu.VMEM((capacity * BROWS, LANES), jnp.float32)],
        compiler_params=params(),
    )(table, divisor.reshape(1), got, limit, used, master, first, second)


def total_over_devices(values, steps):
    for step in steps:
        values = values + exchange(values, step)
    return values


def gather_steps(values, order):
    for step in order[:0:-1]:
        values = jnp.concatenate([values, exchange(values, step)], axis=0)
    return values, exchange(values, order[0])


def reduce_steps(keep, send, order):
    values = keep + exchange(send, order[0])
    for step in order[1:]:
        half = values.shape[0] // 2
        values = values[:half] + exchange(values[half:], step)
    return values


def block_step(head_rate, carried, pieces):
    values, deltas, inputs_b, readout = pieces
    length = deltas.shape[2]
    decays = jnp.cumsum(deltas * head_rate[None, :, None], axis=2)
    differ = decays[:, :, :, None] - decays[:, :, None, :]
    causal = jnp.arange(length)[:, None] >= jnp.arange(length)[None, :]
    within = jnp.exp(jnp.where(causal[None, None, :, :], differ, -1000000000.0))
    scaled = values * deltas[..., None]
    affinity = jnp.einsum("gtn,gsn->gts", readout, inputs_b, precision=PRECISE)
    mixing = affinity[:, None, :, :] * within
    output = jnp.einsum("ghts,ghsp->ghtp", mixing, scaled, precision=PRECISE)
    output = (
        output
        + jnp.einsum("gtn,ghpn->ghtp", readout, carried, precision=PRECISE)
        * jnp.exp(decays)[..., None]
    )
    tail_decay = jnp.exp(decays[:, :, -1:] - decays)
    fresh_state = jnp.einsum(
        "gsn,ghsp->ghpn", inputs_b, scaled * tail_decay[..., None], precision=PRECISE
    )
    renewed = jnp.exp(decays[:, :, -1])[:, :, None, None] * carried + fresh_state
    return (renewed, output)


def mixer_layer(projected_rows, conv_weight, conv_bias, dt_bias, a_log, skip_gain, gate_gain):
    groups = projected_rows.shape[0]
    length = projected_rows.shape[1]
    gate_raw = projected_rows[..., :INNER]
    conv_in = projected_rows[..., INNER : INNER + CONVCH]
    dt_raw = projected_rows[..., INNER + CONVCH :]
    padded = jnp.pad(conv_in, ((0, 0), (KCONV - 1, 0), (0, 0)))
    conv_out = conv_bias + padded[:, 0:length, :] * conv_weight[:, 0]
    for offset in range(1, KCONV):
        conv_out = conv_out + padded[:, offset : offset + length, :] * conv_weight[:, offset]
    mixed_in = jax.nn.silu(conv_out)
    values_rows = mixed_in[..., :INNER].reshape(groups, length, HEADS, HEADDIM)
    values = jnp.transpose(values_rows, (0, 2, 1, 3))
    inputs_b = mixed_in[..., INNER : INNER + NSTATE]
    readout = mixed_in[..., INNER + NSTATE :]
    deltas = jnp.transpose(jax.nn.softplus(dt_raw + dt_bias), (0, 2, 1))
    head_rate = -jnp.exp(a_log)
    blocks = length // SCAN_LEN

    def heads_blocks(stacked):
        shaped = stacked.reshape((groups, HEADS, blocks, SCAN_LEN) + stacked.shape[3:])
        return jnp.moveaxis(shaped, 2, 0)

    def rows_blocks(stacked):
        return jnp.moveaxis(stacked.reshape((groups, blocks, SCAN_LEN) + stacked.shape[2:]), 1, 0)

    stepper = jax.checkpoint(partial(block_step, head_rate))
    initial = jnp.zeros((groups, HEADS, HEADDIM, NSTATE), jnp.float32)
    last_state, outputs = lax.scan(
        stepper,
        initial,
        (heads_blocks(values), heads_blocks(deltas), rows_blocks(inputs_b), rows_blocks(readout)),
    )
    ssm_heads = jnp.moveaxis(outputs, 0, 2).reshape(groups, HEADS, length, HEADDIM)
    ssm_out = jnp.transpose(ssm_heads, (0, 2, 1, 3))
    ssm_out = ssm_out + skip_gain[:, None] * values_rows
    gated = ssm_out.reshape(groups, length, INNER) * jax.nn.silu(gate_raw)
    return gated * lax.rsqrt(jnp.mean(gated * gated, axis=-1, keepdims=True) + NORM_EPS) * gate_gain


def body(tokens, teacher, lengths, loss_mask, owners, master, first_moment, second_moment):
    capacity = master.shape[0]
    dp, fsdp = lax.axis_size("dp"), lax.axis_size("fsdp")
    devices = dp * fsdp
    me = lax.axis_index(AXES).astype(jnp.int32)
    order_a, order_b = step_orders(dp, fsdp)
    plan = make_plan(owners, capacity, devices, me)
    n0, n1 = plan["slots"]
    na = (n0 + 1) // 2
    nb = n0 - na

    sent = send_blocks(plan["send_rows"], master)
    at_home = lax.all_to_all(sent, AXES, 0, 0, tiled=True)
    mine = pick_blocks(jnp.concatenate(plan["received"]), at_home)
    parts_a = gather_steps(mine[:na], order_a)
    parts_b = gather_steps(mine[na:n0], order_b)
    own1, got1 = gather_steps(mine[n0:], order_a)
    relative = plan["home"] ^ me
    place_a, place_b = place_of(relative, order_a), place_of(relative, order_b)
    slot = plan["slot"]
    table = jnp.where(slot < na, place_a * na + slot, devices * na + place_b * nb + slot - na)
    table0 = jnp.concatenate([table[:MID0], table[MID1:]])
    table1 = (place_a * n1 + slot)[MID0:MID1]
    input_weight, head, tail, vec = unpack_in(table0, parts_a + parts_b)
    output_weight = unpack_out(table1, own1, got1, head, tail)
    vec = vec.reshape(-1)
    vectors, at = [], 0
    for size in (CONVCH * KCONV, CONVCH, HEADS, HEADS, HEADS, D, INNER):
        vectors.append(vec[at : at + size])
        at += size
    conv_weight = vectors[0].reshape(CONVCH, KCONV)
    conv_bias, dt_bias, a_log, skip_gain, norm_gain, gate_gain = vectors[1:]

    seq_length = tokens.shape[1]
    positions = jnp.arange(seq_length, dtype=jnp.int32)
    valid_mask = (positions[None, :] < lengths[:, None]).astype(jnp.float32)
    weight_mask = valid_mask * loss_mask.astype(jnp.float32)
    inputs = tokens.astype(jnp.float32)
    inverse = lax.rsqrt(jnp.mean(inputs * inputs, axis=-1, keepdims=True) + NORM_EPS)
    normed = inputs * inverse
    hidden_state = (normed * norm_gain).astype(jnp.bfloat16)
    projected_rows = jnp.einsum(
        "wpa,ar->wpr", hidden_state, input_weight, preferred_element_type=jnp.float32
    )[..., :PROJ]
    mixed_out, mixer_back = jax.vjp(
        mixer_layer, projected_rows, conv_weight, conv_bias, dt_bias, a_log, skip_gain, gate_gain
    )
    mixed_lower_half = mixed_out.astype(jnp.bfloat16)
    residual_branch = jnp.einsum(
        "qjp,pn->qjn", mixed_lower_half, output_weight, preferred_element_type=jnp.float32
    )
    result = inputs + residual_branch
    misfit = result - teacher.astype(jnp.float32)
    local_error = jnp.sum(weight_mask[:, :, None] * misfit * misfit)
    local = jnp.stack([jnp.sum(weight_mask), local_error])
    totals = total_over_devices(jnp.broadcast_to(local[:, None], (2, LANES)), order_a)
    block_out = (result * valid_mask[:, :, None]).astype(jnp.bfloat16)
    grad_result = 2.0 * weight_mask[:, :, None] * misfit
    grad_branch = grad_result.astype(jnp.bfloat16)
    grad_weight_out = jnp.einsum(
        "wtq,wtx->qx", mixed_lower_half, grad_branch, preferred_element_type=jnp.float32
    )
    dest0 = jnp.where(
        slot < na,
        place_a * na + slot,
        devices * na + place_b * nb + slot - na,
    )
    dest0 = jnp.concatenate([dest0[:MID0], dest0[MID1:]])
    half_a, half_b, half_1 = devices * na // 2, devices * nb // 2, devices * n1 // 2
    keep1, send1, head, tail = pack_out(table1, grad_weight_out, (half_1, half_1))
    sum1 = reduce_steps(keep1, send1, order_a)

    grad_mixed = jnp.einsum(
        "hqm,nm->hqn", grad_branch, output_weight, preferred_element_type=jnp.float32
    )
    grad_projected, grad_conv_w, grad_conv_b, grad_dt_bias, grad_a_log, grad_skip, grad_gate = (
        mixer_back(grad_mixed)
    )
    grad_low = jnp.pad(grad_projected.astype(jnp.bfloat16), ((0, 0), (0, 0), (0, WIDE - PROJ)))
    grad_weight_in = jnp.einsum(
        "ghp,ghj->pj", hidden_state, grad_low, preferred_element_type=jnp.float32
    )
    grad_hidden = jnp.einsum(
        "iog,hg->ioh", grad_low, input_weight, preferred_element_type=jnp.float32
    )
    grad_norm = jnp.sum(grad_hidden * normed, axis=(0, 1))
    grad_normed = grad_hidden * norm_gain
    grad_inputs = inverse * (
        grad_normed - normed * jnp.mean(grad_normed * normed, axis=-1, keepdims=True)
    )
    input_grad = grad_result + grad_inputs
    grad_vec = jnp.concatenate(
        [
            grad_conv_w.reshape(-1),
            grad_conv_b,
            grad_dt_bias,
            grad_a_log,
            grad_skip,
            grad_norm,
            grad_gate,
            jnp.zeros((NBLK * PBLOCK - PTOT,), jnp.float32),
        ]
    ).reshape(VEC_ROWS, LANES)
    keep_a, send_a, keep_b, send_b = pack_in(
        dest0, grad_weight_in, head, tail, grad_vec, (half_a, half_a, half_b, half_b)
    )
    sum_a = reduce_steps(keep_a, send_a, order_a)
    sum_b = reduce_steps(keep_b, send_b, order_b)
    back = pick_blocks(plan["back"], jnp.concatenate([sum_a, sum_b, sum1], axis=0))
    got = lax.all_to_all(back, AXES, 0, 0, tiled=True)
    divisor = totals[0, 0] * D
    new_first, new_second, new_master = adam(
        plan["row_from"],
        divisor,
        got,
        plan["row_block"],
        plan["row_used"],
        master,
        first_moment,
        second_moment,
    )
    mean_loss = totals[1, 0] / divisor
    return (block_out, input_grad, mean_loss, new_first, new_second, new_master)


def solution(mesh):
    return jax.shard_map(
        body,
        mesh=mesh,
        in_specs=(
            P(AXES, None, None),
            P(AXES, None, None),
            P(AXES),
            P(AXES, None),
            P(),
            P(AXES, None),
            P(AXES, None),
            P(AXES, None),
        ),
        out_specs=(
            P(AXES, None, None),
            P(AXES, None, None),
            P(),
            P(AXES, None),
            P(AXES, None),
            P(AXES, None),
        ),
        check_vma=False,
    )
```

```python
from functools import partial

import jax
import jax.numpy as jnp
from jax import lax
from jax.experimental import pallas as pl
from jax.experimental.pallas import tpu as pltpu
from jax.sharding import PartitionSpec as P

D = 768
INNER = 1536
NSTATE = 128
HEADDIM = 64
KCONV = 4
SCAN_LEN = 256
PBLOCK = 4096
STEP = 10
HEADS = 24
CONVCH = 1792
PROJ = 3352
PTOT = 3765320
NBLK = 920

LANES = 128
BROWS = PBLOCK // LANES
END_IN = D * PROJ
END_OUT = END_IN + INNER * D
MID0 = -(-END_IN // PBLOCK)
MID1 = END_OUT // PBLOCK
N0 = MID0 + NBLK - MID1
N1 = MID1 - MID0
F0_ROWS = N0 * BROWS
IN_ROWS = END_IN // LANES
HEAD_ROWS = MID0 * BROWS - IN_ROWS
TAIL_ROWS = (END_OUT - MID1 * PBLOCK) // LANES
OUT_ROWS = INNER * D // LANES
VEC_ROWS = (NBLK - MID1) * BROWS - TAIL_ROWS
VEC_AT = MID0 * BROWS + TAIL_ROWS
GROUP = 16
GROUPS = D // GROUP
GROUP_ROWS = GROUP * PROJ // LANES
COL_TILES = -(-PROJ // LANES)
WIDE = COL_TILES * LANES
OUT_TILES = D // LANES

NORM_EPS = 1e-05
ADAM_EPS = 1e-08
BETA_ONE = 0.9
BETA_TWO = 0.999
MATRIX_RATE = 0.03
VECTOR_RATE = 0.2
WEIGHT_DECAY = 0.1
PRECISE = lax.Precision.HIGHEST
AXES = ("dp", "fsdp")
VMEM_LIMIT = 60 * 1024 * 1024


def bits_of(count):
    return count.bit_length() - 1


def step_orders(dp, fsdp):
    wide = [("dp", i) for i in range(bits_of(dp))]
    narrow = [("fsdp", i) for i in range(bits_of(fsdp))]
    first = wide[:2] + narrow + wide[2:]
    second = wide[:1] + narrow + wide[1:]
    return first, second


def exchange(values, step):
    axis, bit = step
    size = lax.axis_size(axis)
    return lax.ppermute(values, axis, [(i, i ^ (1 << bit)) for i in range(size)])


def place_of(relative, order):
    shift_of = {"dp": bits_of(lax.axis_size("fsdp")), "fsdp": 0}
    place = jnp.zeros_like(relative)
    for axis, bit in order:
        place = place * 2 + ((relative >> (shift_of[axis] + bit)) & 1)
    return place


def make_plan(owners, capacity, devices, me):
    block = jnp.arange(NBLK, dtype=jnp.int32)
    mid = (block >= MID0) & (block < MID1)
    same = mid[:, None] == mid[None, :]
    before = (owners[None, :] < owners[:, None]) | (
        (owners[None, :] == owners[:, None]) & (block[None, :] < block[:, None])
    )
    order_in_class = jnp.sum((same & before).astype(jnp.int32), axis=1)
    home, slot = order_in_class % devices, order_in_class // devices
    device = jnp.arange(devices, dtype=jnp.int32)
    below = owners[None, :] < device[:, None]
    owned = owners[None, :] == device[:, None]

    def total(mask):
        return jnp.sum(mask.astype(jnp.int32), axis=1)

    start = (total(below & ~mid[None, :]), total(below & mid[None, :]))
    count = (total(owned & ~mid[None, :]), total(owned & mid[None, :]))
    early = total(owned & (block < MID0)[None, :])
    pair = 2 + max(capacity - 2, 0) // devices

    def pick(vector, index):
        return jnp.sum(jnp.where(device == index, vector, 0))

    my_start = [pick(v, me) for v in start]
    my_count = [pick(v, me) for v in count]
    my_early = pick(early, me)

    lane = jnp.arange(pair, dtype=jnp.int32)
    k0 = (device[:, None] - my_start[0]) % devices + lane[None, :] * devices
    k1 = (device[:, None] - my_start[1]) % devices + (pair - 1 - lane)[None, :] * devices
    row0 = jnp.where(k0 < my_early, k0, k0 + my_count[1])
    send_rows = jnp.where(
        k0 < my_count[0], row0, jnp.where(k1 < my_count[1], my_early + k1, 0)
    ).reshape(-1)

    slots = (-(-N0 // devices), -(-N1 // devices))

    def received(kind):
        wanted = me + devices * jnp.arange(slots[kind], dtype=jnp.int32)
        ends = start[kind] + count[kind]
        owner = jnp.sum((ends[None, :] <= wanted[:, None]).astype(jnp.int32), axis=1)
        owner = jnp.minimum(owner, devices - 1)
        base = jnp.sum(jnp.where(device[None, :] == owner[:, None], start[kind][None, :], 0), axis=1)
        turn = jnp.clip((wanted - base) // devices, 0, pair - 1)
        return owner * pair + (turn if kind == 0 else pair - 1 - turn)

    b0 = (me - start[0])[:, None] % devices + lane[None, :] * devices
    b1 = (me - start[1])[:, None] % devices + (pair - 1 - lane)[None, :] * devices
    back = jnp.where(
        b0 < count[0][:, None],
        (start[0][:, None] + b0) // devices,
        jnp.where(b1 < count[1][:, None], slots[0] + (start[1][:, None] + b1) // devices, 0),
    ).reshape(-1)

    row = jnp.arange(capacity, dtype=jnp.int32)
    is_mid = (row >= my_early) & (row < my_early + my_count[1])
    k = jnp.where(is_mid, row - my_early, jnp.where(row < my_early, row, row - my_count[1]))
    first = jnp.where(is_mid, my_start[1], my_start[0])
    turn = k // devices
    row_from = ((first + k) % devices) * pair + jnp.where(is_mid, pair - 1 - turn, turn)
    row_used = row < my_count[0] + my_count[1]
    row_from = jnp.where(row_used, row_from, 0)
    mine = (owners == me)[None, :]
    rank = jnp.sum((mine & (block[None, :] < block[:, None])).astype(jnp.int32), axis=1)
    row_block = jnp.sum(
        jnp.where(mine & (rank[None, :] == row[:, None]), block[None, :], 0), axis=1
    )
    return dict(
        home=home, slot=slot, slots=slots, pair=pair, send_rows=send_rows,
        received=(received(0), received(1)), back=back, row_from=row_from,
        row_used=row_used, row_block=row_block,
    )


ANY = pl.BlockSpec(memory_space=pl.ANY)
VMEM = pl.BlockSpec(memory_space=pltpu.VMEM)
SMEM = pl.BlockSpec(memory_space=pltpu.SMEM)


def params(**extra):
    return pltpu.CompilerParams(vmem_limit_bytes=VMEM_LIMIT, **extra)


def shape(dims, dtype):
    return jax.ShapeDtypeStruct(dims, dtype)


def send_kernel(table, master, out, flat):
    capacity = master.shape[0]
    for j in range(BROWS):
        flat[pl.ds(j, capacity, stride=BROWS), :] = master[:, j * LANES : (j + 1) * LANES]

    def step(i, carry):
        out[i] = flat[pl.ds(pl.multiple_of(table[i] * BROWS, BROWS), BROWS), :].astype(out.dtype)
        return carry

    lax.fori_loop(0, out.shape[0], step, 0)


def send_blocks(table, master):
    return pl.pallas_call(
        send_kernel,
        out_shape=shape((table.shape[0], BROWS, LANES), jnp.bfloat16),
        in_specs=[SMEM, VMEM],
        out_specs=VMEM,
        scratch_shapes=[pltpu.VMEM((master.shape[0] * BROWS, LANES), jnp.float32)],
        compiler_params=params(),
    )(table, master)


def pick_kernel(table, source, out):
    def step(i, carry):
        out[i] = source[table[i]]
        return carry

    lax.fori_loop(0, out.shape[0], step, 0)


def pick_blocks(table, source):
    return pl.pallas_call(
        pick_kernel,
        out_shape=shape((table.shape[0],) + source.shape[1:], source.dtype),
        in_specs=[SMEM, VMEM],
        out_specs=VMEM,
        compiler_params=params(),
    )(table, source)


def row_start(rho):
    return (PROJ * rho) // LANES, (PROJ * rho) % LANES


def copy_all(pairs, sem):
    copies = [pltpu.make_async_copy(a, b, sem.at[i]) for i, (a, b) in enumerate(pairs)]
    for c in copies:
        c.start()
    for c in copies:
        c.wait()


def spread_blocks(table, held, flat, count, first_row):
    def one(i):
        at = pl.multiple_of(first_row + i * BROWS, 16)
        flat[pl.ds(at, BROWS), :] = held[table[i]].astype(jnp.float32)

    def step(i, carry):
        for u in range(4):
            one(i * 4 + u)
        return carry

    lax.fori_loop(0, count // 4, step, 0)
    for i in range(count // 4 * 4, count):
        one(i)


def unpack_in_kernel(table, *refs):
    parts, (w_in, head, tail, vec, held, flat, tile, sem) = refs[:-8], refs[-8:]
    pairs, at = [], 0
    for part in parts:
        pairs.append((part, held.at[pl.ds(at, part.shape[0])]))
        at += part.shape[0]
    copy_all(pairs, sem)
    spread_blocks(table, held, flat, N0, 0)
    head[...] = flat[IN_ROWS : IN_ROWS + HEAD_ROWS, :]
    tail[...] = flat[MID0 * BROWS : MID0 * BROWS + TAIL_ROWS, :]
    vec[...] = flat[VEC_AT:F0_ROWS, :]
    lane = lax.broadcasted_iota(jnp.int32, (GROUPS, LANES), 1)

    def columns(j):
        for rho in range(GROUP):
            c, s = row_start(rho)
            x = flat[pl.ds(c + j, GROUPS, stride=GROUP_ROWS), :]
            if s:
                y = flat[pl.ds(c + j + 1, GROUPS, stride=GROUP_ROWS), :]
                x = jnp.where(
                    lane < LANES - s,
                    pltpu.roll(x, LANES - s, 1),
                    pltpu.roll(y, LANES - s, 1),
                )
            tile[pl.ds(rho, GROUPS, stride=GROUP), :] = x

    def step(j, carry):
        columns(j)
        w_in[:, pl.ds(pl.multiple_of(j * LANES, LANES), LANES)] = tile[...].astype(jnp.bfloat16)
        return carry

    lax.fori_loop(0, COL_TILES - 1, step, 0)
    columns(COL_TILES - 1)
    last = (COL_TILES - 1) * LANES
    inside = lax.broadcasted_iota(jnp.int32, (D, LANES), 1) < PROJ - last
    w_in[:, last:] = jnp.where(inside, tile[...], 0.0).astype(jnp.bfloat16)


def unpack_in(table, parts):
    held = sum(part.shape[0] for part in parts)
    return pl.pallas_call(
        unpack_in_kernel,
        out_shape=(
            shape((D, WIDE), jnp.bfloat16),
            shape((HEAD_ROWS, LANES), jnp.float32),
            shape((TAIL_ROWS, LANES), jnp.float32),
            shape((VEC_ROWS, LANES), jnp.float32),
        ),
        in_specs=[SMEM] + [ANY] * len(parts),
        out_specs=(VMEM,) * 4,
        scratch_shapes=[
            pltpu.VMEM((held, BROWS, LANES), jnp.bfloat16),
            pltpu.VMEM((F0_ROWS, LANES), jnp.float32),
            pltpu.VMEM((D, LANES), jnp.float32),
            pltpu.SemaphoreType.DMA((len(parts),)),
        ],
        compiler_params=params(),
    )(table, *parts)


def unpack_out_kernel(table, own, got, head, tail, w_out, held, flat, sem):
    half = own.shape[0]
    copy_all([(own, held.at[pl.ds(0, half)]), (got, held.at[pl.ds(half, half)])], sem)
    flat[0:HEAD_ROWS, :] = head[...]
    flat[OUT_ROWS - TAIL_ROWS : OUT_ROWS, :] = tail[...]
    spread_blocks(table, held, flat, N1, HEAD_ROWS)
    rows = 128

    def step(i, carry):
        at = pl.multiple_of(i * rows, rows)
        for j in range(OUT_TILES):
            x = flat[pl.ds(at * OUT_TILES + j, rows, stride=OUT_TILES), :]
            w_out[pl.ds(at, rows), j * LANES : (j + 1) * LANES] = x.astype(jnp.bfloat16)
        return carry

    lax.fori_loop(0, INNER // rows, step, 0)


def unpack_out(table, own, got, head, tail):
    return pl.pallas_call(
        unpack_out_kernel,
        out_shape=shape((INNER, D), jnp.bfloat16),
        in_specs=[SMEM, ANY, ANY, VMEM, VMEM],
        out_specs=VMEM,
        scratch_shapes=[
            pltpu.VMEM((2 * own.shape[0], BROWS, LANES), jnp.bfloat16),
            pltpu.VMEM((OUT_ROWS, LANES), jnp.float32),
            pltpu.SemaphoreType.DMA((2,)),
        ],
        compiler_params=params(),
    )(table, own, got, head, tail)


def scatter_blocks(table, flat, count, first_row, outs, sem):
    def step(i, carry):
        source = flat.at[pl.ds(pl.multiple_of(first_row + i * BROWS, 16), BROWS)]
        at, low = table[i], 0
        for out in outs:
            high = low + out.shape[0]

            @pl.when((at >= low) & (at < high))
            def _():
                pltpu.make_async_copy(source, out.at[at - low], sem).start()

            low = high
        return carry

    lax.fori_loop(0, count, step, 0)


def wait_rows(flat, count, first_row, sem):
    whole = flat.at[pl.ds(first_row, count * BROWS)]
    pltpu.make_async_copy(whole, whole, sem).wait()


def pack_in_kernel(table, grad, head, tail, vec, *refs):
    outs, (tiles, flat, sem, tile_sem) = refs[:-4], refs[-4:]
    copy_all(
        [
            (grad.at[:, pl.ds(j * LANES, LANES)], tiles.at[pl.ds(j * D, D)])
            for j in range(COL_TILES)
        ],
        tile_sem,
    )
    lane = lax.broadcasted_iota(jnp.int32, (GROUPS, LANES), 1)

    def load(rho, j):
        return tiles[pl.ds(j * D + rho, GROUPS, stride=GROUP), :]

    for rho in range(GROUP):
        _, s = row_start(rho)
        first = -(-PROJ * rho // LANES)
        col0 = first * LANES - PROJ * rho
        full = (PROJ - col0) // LANES

        def step(i, carry, rho=rho, first=first, col0=col0):
            x = load(rho, i)
            if col0:
                y = load(rho, i + 1)
                x = jnp.where(
                    lane < LANES - col0,
                    pltpu.roll(x, LANES - col0, 1),
                    pltpu.roll(y, LANES - col0, 1),
                )
            flat[pl.ds(first + i, GROUPS, stride=GROUP_ROWS), :] = x
            return carry

        lax.fori_loop(0, full, step, 0)
        left = PROJ - col0 - full * LANES
        if left:
            begin = col0 + full * LANES
            j, s = begin // LANES, begin % LANES
            x = pltpu.roll(load(rho, j), (LANES - s) % LANES, 1) if s else load(rho, j)
            if s + left > LANES:
                x = jnp.where(lane < LANES - s, x, pltpu.roll(load(rho, j + 1), LANES - s, 1))
            y = pltpu.roll(load(rho + 1, 0), left, 1)
            flat[pl.ds(first + full, GROUPS, stride=GROUP_ROWS), :] = jnp.where(lane < left, x, y)
    flat[IN_ROWS : IN_ROWS + HEAD_ROWS, :] = head[...]
    flat[MID0 * BROWS : MID0 * BROWS + TAIL_ROWS, :] = tail[...]
    flat[VEC_AT:F0_ROWS, :] = vec[...]
    scatter_blocks(table, flat, N0, 0, outs, sem)
    wait_rows(flat, N0, 0, sem)


def pack_in(table, grad, head, tail, vec, sizes):
    return pl.pallas_call(
        pack_in_kernel,
        out_shape=tuple(shape((n, BROWS, LANES), jnp.float32) for n in sizes),
        in_specs=[SMEM, ANY] + [VMEM] * 3,
        out_specs=(ANY,) * len(sizes),
        scratch_shapes=[
            pltpu.VMEM((COL_TILES * D, LANES), jnp.float32),
            pltpu.VMEM((F0_ROWS, LANES), jnp.float32),
            pltpu.SemaphoreType.DMA,
            pltpu.SemaphoreType.DMA((COL_TILES,)),
        ],
        compiler_params=params(),
    )(table, grad, head, tail, vec)


def pack_out_kernel(table, grad, *refs):
    outs, (head, tail, flat, sem) = refs[:-4], refs[-4:]
    rows = 128

    def step(i, carry):
        at = pl.multiple_of(i * rows, rows)
        for j in range(OUT_TILES):
            flat[pl.ds(at * OUT_TILES + j, rows, stride=OUT_TILES), :] = grad[
                pl.ds(at, rows), j * LANES : (j + 1) * LANES
            ]
        return carry

    lax.fori_loop(0, INNER // rows, step, 0)
    head[...] = flat[0:HEAD_ROWS, :]
    tail[...] = flat[OUT_ROWS - TAIL_ROWS : OUT_ROWS, :]
    scatter_blocks(table, flat, N1, HEAD_ROWS, outs, sem)
    wait_rows(flat, N1, HEAD_ROWS, sem)


def pack_out(table, grad, sizes):
    return pl.pallas_call(
        pack_out_kernel,
        out_shape=tuple(shape((n, BROWS, LANES), jnp.float32) for n in sizes)
        + (shape((HEAD_ROWS, LANES), jnp.float32), shape((TAIL_ROWS, LANES), jnp.float32)),
        in_specs=[SMEM, VMEM],
        out_specs=(ANY,) * len(sizes) + (VMEM, VMEM),
        scratch_shapes=[
            pltpu.VMEM((OUT_ROWS, LANES), jnp.float32),
            pltpu.SemaphoreType.DMA,
        ],
        compiler_params=params(),
    )(table, grad)


def adam_kernel(table, scale, got, limit, used, master, first, second, o_first, o_second, o_master, flat):
    capacity = master.shape[0]

    def step(i, carry):
        flat[pl.ds(pl.multiple_of(i * BROWS, BROWS), BROWS), :] = got[table[i]]
        return carry

    lax.fori_loop(0, capacity, step, 0)
    lane = lax.broadcasted_iota(jnp.int32, (capacity, LANES), 1)
    divisor = scale[0]
    for j in range(BROWS):
        cols = slice(j * LANES, (j + 1) * LANES)
        grad = jnp.where(used[...] > 0, flat[pl.ds(j, capacity, stride=BROWS), :], 0.0) / divisor
        matrix = lane + j * LANES < limit[...]
        weights = master[:, cols]
        new_first = BETA_ONE * first[:, cols] + (1.0 - BETA_ONE) * grad
        new_second = BETA_TWO * second[:, cols] + (1.0 - BETA_TWO) * grad * grad
        normal = (
            new_first
            / (1.0 - BETA_ONE**STEP)
            / (jnp.sqrt(new_second / (1.0 - BETA_TWO**STEP)) + ADAM_EPS)
        )
        rate = jnp.where(matrix, MATRIX_RATE, VECTOR_RATE)
        decay = jnp.where(matrix, WEIGHT_DECAY, 0.0)
        o_first[:, cols] = new_first
        o_second[:, cols] = new_second
        o_master[:, cols] = weights - rate * (normal + decay * weights)


def adam(table, divisor, got, row_block, row_used, master, first, second):
    capacity = master.shape[0]
    limit = jnp.broadcast_to((END_OUT - row_block * PBLOCK)[:, None], (capacity, LANES))
    used = jnp.broadcast_to(row_used.astype(jnp.int32)[:, None], (capacity, LANES))
    return pl.pallas_call(
        adam_kernel,
        out_shape=(shape(master.shape, jnp.float32),) * 3,
        in_specs=[SMEM, SMEM] + [VMEM] * 6,
        out_specs=(VMEM,) * 3,
        scratch_shapes=[pltpu.VMEM((capacity * BROWS, LANES), jnp.float32)],
        compiler_params=params(),
    )(table, divisor.reshape(1), got, limit, used, master, first, second)


def total_over_devices(values, steps):
    for step in steps:
        values = values + exchange(values, step)
    return values


def gather_steps(values, order):
    for step in order[:0:-1]:
        values = jnp.concatenate([values, exchange(values, step)], axis=0)
    return values, exchange(values, order[0])


def reduce_steps(keep, send, order):
    values = keep + exchange(send, order[0])
    for step in order[1:]:
        half = values.shape[0] // 2
        values = values[:half] + exchange(values[half:], step)
    return values


CHUNK = 128
PAIRS = HEADS // 2
MIXW = INNER + 2 * NSTATE
DT_AT = INNER + CONVCH
F32 = jnp.float32
BF16 = jnp.bfloat16
NN = (((1,), (0,)), ((), ()))
NT = (((1,), (1,)), ((), ()))


def cost(microseconds):
    return pl.CostEstimate(
        flops=int(microseconds * 1e9), bytes_accessed=int(microseconds * 3e6), transcendentals=0
    )


def dot(a, b, dims=NN):
    return lax.dot_general(a, b, dims, preferred_element_type=F32)


def split(v):
    high = v.astype(BF16)
    return high, (v - high.astype(F32)).astype(BF16)


def dot3(a, b, dims=NN):
    ah, al = a
    bh, bl = b
    return dot(ah, bh, dims) + (dot(ah, bl, dims) + dot(al, bh, dims))


def heads_spread():
    row = lax.broadcasted_iota(jnp.int32, (LANES, INNER), 0)
    col = lax.broadcasted_iota(jnp.int32, (LANES, INNER), 1)
    return ((row % 32 == col // HEADDIM) & (row < 96)).astype(BF16)


def heads_gather():
    row = lax.broadcasted_iota(jnp.int32, (INNER, LANES), 0)
    col = lax.broadcasted_iota(jnp.int32, (INNER, LANES), 1)
    return (row // HEADDIM == col).astype(BF16)


def three_parts(v):
    high = v.astype(BF16).astype(F32)
    rest = v - high
    middle = rest.astype(BF16).astype(F32)
    low = rest - middle
    return (high + pltpu.roll(middle, 32, 1) + pltpu.roll(low, 64, 1)).astype(BF16)


def triangle_sum(tri, v):
    parts = dot(tri, three_parts(v))
    lane = lax.broadcasted_iota(jnp.int32, parts.shape, 1)
    total = parts + pltpu.roll(parts, LANES - 32, 1) + pltpu.roll(parts, LANES - 64, 1)
    return jnp.where(lane < HEADS, total, 0.0)


def chunk_decays(dt, dt_bias, a_log):
    lane = lax.broadcasted_iota(jnp.int32, (CHUNK, LANES), 1)
    row = lax.broadcasted_iota(jnp.int32, (CHUNK, LANES), 0)
    shifted = dt + dt_bias
    delta = jnp.where(
        lane < HEADS, jnp.maximum(shifted, 0.0) + jnp.log1p(jnp.exp(-jnp.abs(shifted))), 0.0
    )
    rate = -jnp.exp(a_log)
    lower = (row >= lane).astype(BF16)
    cum = triangle_sum(lower, delta * rate)
    last = cum[CHUNK - 1 : CHUNK, :]
    return shifted, delta, rate, cum, last


def pair_mask():
    lane = lax.broadcasted_iota(jnp.int32, (CHUNK, LANES), 1)
    low = (lane < HEADDIM).astype(F32)
    return low.astype(BF16), (1.0 - low).astype(BF16)


def scan_forward_kernel(
    mixed, dt, gate, dt_bias, a_log, skip, gain, spread, ssm, mixed_out, states, state
):
    @pl.when(pl.program_id(0) == 0)
    def _():
        state[...] = jnp.zeros_like(state)

    states[0] = state[...]
    _, delta, _, cum, last = chunk_decays(dt[...], dt_bias[...], a_log[...])
    lane = lax.broadcasted_iota(jnp.int32, (CHUNK, LANES), 1)
    row = lax.broadcasted_iota(jnp.int32, (CHUNK, LANES), 0)
    bias = jnp.where(row >= lane, 0.0, -1e30)
    heads = lane < HEADS
    stacked = jnp.concatenate(
        [
            three_parts(delta),
            three_parts(jnp.where(heads, jnp.exp(cum), 0.0)),
            three_parts(jnp.where(heads, jnp.exp(last - cum), 0.0)),
        ],
        axis=0,
    )
    cum_t = cum.T
    inputs_b = mixed[:, INNER : INNER + NSTATE]
    readout = mixed[:, INNER + NSTATE :]
    affinity = dot3(split(readout), split(inputs_b), NT)
    readout_parts = split(readout)
    b_parts = split(inputs_b.T)
    low, high = pair_mask()
    squares = jnp.zeros((CHUNK, LANES), F32)
    for j in range(PAIRS):
        cols = slice(j * LANES, (j + 1) * LANES)
        wide = dot(stacked, spread[:, cols])
        values = mixed[:, cols]
        scaled = values * wide[:CHUNK]
        sh, sl = split(scaled)
        right_h = jnp.concatenate([sh * low, sh * high], axis=0)
        right_l = jnp.concatenate([sl * low, sl * high], axis=0)
        left = []
        for h in (2 * j, 2 * j + 1):
            within = jnp.exp(cum[:, h : h + 1] - cum_t[h : h + 1, :] + bias)
            left.append(split(affinity * within))
        left_h = jnp.concatenate([left[0][0], left[1][0]], axis=1)
        left_l = jnp.concatenate([left[0][1], left[1][1]], axis=1)
        both = dot(left_h, jnp.concatenate([right_h, right_l], axis=1))
        out = both[:, :LANES] + both[:, LANES:] + dot(left_l, right_h)
        carried = state[:, cols]
        carried_parts = split(carried)
        out = out + dot3(readout_parts, carried_parts) * wide[CHUNK : 2 * CHUNK]
        out = out + skip[:, cols] * values
        end = wide[2 * CHUNK - 1 : 2 * CHUNK]
        state[:, cols] = carried * end + dot3(b_parts, split(scaled * wide[2 * CHUNK :]))
        ssm[:, cols] = out
        g = gate[:, cols]
        gated = out * (g / (1.0 + jnp.exp(-g)))
        squares = squares + gated * gated
    rho = lax.rsqrt(jnp.sum(squares, axis=1, keepdims=True) * (1.0 / INNER) + NORM_EPS)
    for j in range(PAIRS):
        cols = slice(j * LANES, (j + 1) * LANES)
        g = gate[:, cols]
        gated = ssm[:, cols] * (g / (1.0 + jnp.exp(-g)))
        mixed_out[:, cols] = (gated * rho * gain[:, cols]).astype(BF16)


def scan_forward(mixed, projected, dt_bias, a_log, skip, gain, spread):
    length = mixed.shape[0]
    chunks = length // CHUNK
    whole = lambda v: pl.BlockSpec(v.shape, lambda i: (0,) * v.ndim)
    return pl.pallas_call(
        scan_forward_kernel,
        grid=(chunks,),
        out_shape=(
            shape((length, INNER), F32),
            shape((length, INNER), BF16),
            shape((chunks, NSTATE, INNER), F32),
        ),
        in_specs=[
            pl.BlockSpec((CHUNK, MIXW), lambda i: (i, 0)),
            pl.BlockSpec((CHUNK, LANES), lambda i: (i, DT_AT // LANES)),
            pl.BlockSpec((CHUNK, INNER), lambda i: (i, 0)),
        ]
        + [whole(v) for v in (dt_bias, a_log, skip, gain, spread)],
        out_specs=(
            pl.BlockSpec((CHUNK, INNER), lambda i: (i, 0)),
            pl.BlockSpec((CHUNK, INNER), lambda i: (i, 0)),
            pl.BlockSpec((1, NSTATE, INNER), lambda i: (i, 0, 0)),
        ),
        scratch_shapes=[pltpu.VMEM((NSTATE, INNER), F32)],
        compiler_params=params(),
        cost_estimate=cost(40),
    )(mixed, projected, projected, dt_bias, a_log, skip, gain, spread)


def scan_backward_kernel(
    mixed, dt, ssm, grad, states, dt_bias, a_log, skip, spread, gather,
    grad_mixed, grad_dt, sums, skip_sums, grad_state, left, right,
):
    @pl.when(pl.program_id(0) == 0)
    def _():
        grad_state[...] = jnp.zeros_like(grad_state)
        sums[...] = jnp.zeros_like(sums)
        skip_sums[...] = jnp.zeros_like(skip_sums)

    shifted, delta, rate, cum, last = chunk_decays(dt[...], dt_bias[...], a_log[...])
    lane = lax.broadcasted_iota(jnp.int32, (CHUNK, LANES), 1)
    row = lax.broadcasted_iota(jnp.int32, (CHUNK, LANES), 0)
    bias = jnp.where(lane >= row, 0.0, -1e30)
    heads = lane < HEADS
    stacked = jnp.concatenate(
        [
            three_parts(delta),
            three_parts(jnp.where(heads, jnp.exp(cum), 0.0)),
            three_parts(jnp.where(heads, jnp.exp(last - cum), 0.0)),
        ],
        axis=0,
    )
    cum_t = cum.T
    inputs_b = mixed[:, INNER : INNER + NSTATE]
    readout = mixed[:, INNER + NSTATE :]
    b_parts, c_parts = split(inputs_b), split(readout)
    c_turned = split(readout.T)
    affinity = dot3(b_parts, c_parts, NT)
    low, high = pair_mask()
    grad_affinity = jnp.zeros((CHUNK, CHUNK), F32)
    grad_b = jnp.zeros((CHUNK, NSTATE), F32)
    grad_c = jnp.zeros((CHUNK, NSTATE), F32)
    for j in range(PAIRS):
        cols = slice(j * LANES, (j + 1) * LANES)
        wide = dot(stacked, spread[:, cols])
        wide_delta, wide_cum, wide_tail = wide[:CHUNK], wide[CHUNK : 2 * CHUNK], wide[2 * CHUNK :]
        end = wide_cum[CHUNK - 1 :]
        values = mixed[:, cols]
        pulled = grad[:, cols]
        scaled = values * wide_delta
        sh, sl = split(scaled)
        ph, plow = split(pulled)
        x_h = jnp.concatenate([sh * low, sh * high], axis=0)
        x_l = jnp.concatenate([sl * low, sl * high], axis=0)
        pull = dot(jnp.concatenate([x_h, x_l], axis=1), jnp.concatenate([ph, ph], axis=1), NT)
        pull = pull + dot(x_h, plow, NT)
        kernels = []
        for k, h in enumerate((2 * j, 2 * j + 1)):
            within = jnp.exp(cum_t[h : h + 1, :] - cum[:, h : h + 1] + bias)
            kernels.append(split(affinity * within))
            grad_affinity = grad_affinity + within * pull[k * CHUNK : (k + 1) * CHUNK]
        kernel_h = jnp.concatenate([kernels[0][0], kernels[1][0]], axis=1)
        kernel_l = jnp.concatenate([kernels[0][1], kernels[1][1]], axis=1)
        right_h = jnp.concatenate([ph * low, ph * high], axis=0)
        right_l = jnp.concatenate([plow * low, plow * high], axis=0)
        both = dot(kernel_h, jnp.concatenate([right_h, right_l], axis=1))
        grad_scaled = both[:, :LANES] + both[:, LANES:] + dot(kernel_l, right_h)
        late = grad_state[:, cols]
        late_parts = split(late)
        early = states[0, :, cols]
        from_state = dot3(b_parts, late_parts) * wide_tail
        grad_scaled = grad_scaled + from_state
        pulled_cum = split(pulled * wide_cum)
        grad_c = grad_c + dot3(pulled_cum, split(early), NT)
        grad_b = grad_b + dot3(split(scaled * wide_tail), late_parts, NT)
        grad_state[:, cols] = late * end + dot3(c_turned, pulled_cum)
        grad_mixed[:, cols] = grad_scaled * wide_delta + skip[:, cols] * pulled
        skip_sums[:, cols] += jnp.sum(pulled * values, axis=0, keepdims=True)
        left[:, cols] = grad_scaled * values
        inner = pulled * (ssm[:, cols] - skip[:, cols] * values) - scaled * grad_scaled
        extra = jnp.sum(scaled * from_state, axis=0, keepdims=True) + end * jnp.sum(
            late * early, axis=0, keepdims=True
        )
        right[:, cols] = inner + jnp.where(row == CHUNK - 1, extra, 0.0)
    ga_parts = split(grad_affinity)
    grad_mixed[:, INNER : INNER + NSTATE] = grad_b + dot3(ga_parts, c_parts)
    grad_mixed[:, INNER + NSTATE :] = grad_c + dot3(split(grad_affinity.T), b_parts)

    def by_head(v):
        high = v.astype(BF16)
        rest = v - high.astype(F32)
        middle = rest.astype(BF16)
        low = (rest - middle.astype(F32)).astype(BF16)
        g = gather[...]
        return dot(high, g) + (dot(middle, g) + dot(low, g))

    direct = by_head(left[...])
    grad_cum = by_head(right[...])
    upper = (lane >= row).astype(BF16)
    after = triangle_sum(upper, grad_cum)
    grad_delta = direct + rate * after
    grad_raw = jnp.where(heads, grad_delta / (1.0 + jnp.exp(-shifted)), 0.0)
    grad_dt[...] = grad_raw.astype(BF16)
    sums[0:1, :] += jnp.sum(grad_raw, axis=0, keepdims=True)
    sums[1:2, :] += rate * jnp.sum(delta * after, axis=0, keepdims=True)


def scan_backward(mixed, projected, ssm, grad, states, dt_bias, a_log, skip, spread, gather):
    length = mixed.shape[0]
    chunks = length // CHUNK
    whole = lambda v: pl.BlockSpec(v.shape, lambda i: (0,) * v.ndim)
    back = lambda i: (chunks - 1 - i, 0)
    return pl.pallas_call(
        scan_backward_kernel,
        grid=(chunks,),
        out_shape=(
            shape((length, MIXW), F32),
            shape((length, LANES), BF16),
            shape((8, LANES), F32),
            shape((1, INNER), F32),
        ),
        in_specs=[
            pl.BlockSpec((CHUNK, MIXW), back),
            pl.BlockSpec((CHUNK, LANES), lambda i: (chunks - 1 - i, DT_AT // LANES)),
            pl.BlockSpec((CHUNK, INNER), back),
            pl.BlockSpec((CHUNK, INNER), back),
            pl.BlockSpec((1, NSTATE, INNER), lambda i: (chunks - 1 - i, 0, 0)),
        ]
        + [whole(v) for v in (dt_bias, a_log, skip, spread, gather)],
        out_specs=(
            pl.BlockSpec((CHUNK, MIXW), back),
            pl.BlockSpec((CHUNK, LANES), back),
            pl.BlockSpec((8, LANES), lambda i: (0, 0)),
            pl.BlockSpec((1, INNER), lambda i: (0, 0)),
        ),
        scratch_shapes=[pltpu.VMEM((NSTATE, INNER), F32)] + [pltpu.VMEM((CHUNK, INNER), F32)] * 2,
        compiler_params=params(),
        cost_estimate=cost(70),
    )(mixed, projected, ssm, grad, states, dt_bias, a_log, skip, spread, gather)


ROWS_AT_ONCE = 128


def conv_sum(padded, at, weight, bias):
    total = bias + padded[pl.ds(at + 8, ROWS_AT_ONCE), :] * weight[KCONV - 1 : KCONV]
    for k in range(KCONV - 1):
        shifted = padded[pl.ds(at + 8 - (KCONV - 1) + k, ROWS_AT_ONCE), :]
        total = total + shifted * weight[k : k + 1]
    return total


def conv_forward_kernel(conv_in, weight, bias, mixed, padded):
    length = conv_in.shape[0]
    padded[0:8, :] = jnp.zeros((8, LANES), F32)
    padded[8:, :] = conv_in[...]
    w, b = weight[...], bias[...]
    for at in range(0, length, ROWS_AT_ONCE):
        out = conv_sum(padded, at, w, b)
        mixed[at : at + ROWS_AT_ONCE, :] = out / (1.0 + jnp.exp(-out))


def conv_forward(projected, weight, bias):
    length = projected.shape[0]
    return pl.pallas_call(
        conv_forward_kernel,
        grid=(CONVCH // LANES,),
        out_shape=shape((length, CONVCH), F32),
        in_specs=[
            pl.BlockSpec((length, LANES), lambda i: (0, INNER // LANES + i)),
            pl.BlockSpec((KCONV, LANES), lambda i: (0, i)),
            pl.BlockSpec((1, LANES), lambda i: (0, i)),
        ],
        out_specs=pl.BlockSpec((length, LANES), lambda i: (0, i)),
        scratch_shapes=[pltpu.VMEM((length + 8, LANES), F32)],
        compiler_params=params(),
        cost_estimate=cost(12),
    )(projected, weight, bias)


def conv_backward_kernel(conv_in, grad, weight, bias, out, sums, padded, grads):
    length = conv_in.shape[0]
    padded[0:8, :] = jnp.zeros((8, LANES), F32)
    padded[8:, :] = conv_in[...]
    grads[length:, :] = jnp.zeros((8, LANES), F32)
    w, b = weight[...], bias[...]
    totals = [jnp.zeros((1, LANES), F32)] * (KCONV + 1)
    for at in range(0, length, ROWS_AT_ONCE):
        value = conv_sum(padded, at, w, b)
        sig = 1.0 / (1.0 + jnp.exp(-value))
        g = grad[at : at + ROWS_AT_ONCE, :] * (sig * (1.0 + value * (1.0 - sig)))
        grads[at : at + ROWS_AT_ONCE, :] = g
        for k in range(KCONV):
            shifted = padded[pl.ds(at + 8 - (KCONV - 1) + k, ROWS_AT_ONCE), :]
            totals[k] = totals[k] + jnp.sum(g * shifted, axis=0, keepdims=True)
        totals[KCONV] = totals[KCONV] + jnp.sum(g, axis=0, keepdims=True)
    for k in range(KCONV + 1):
        sums[k : k + 1, :] = totals[k]
    for at in range(0, length, ROWS_AT_ONCE):
        total = grads[pl.ds(at, ROWS_AT_ONCE), :] * w[KCONV - 1 : KCONV]
        for k in range(KCONV - 1):
            total = total + grads[pl.ds(at + KCONV - 1 - k, ROWS_AT_ONCE), :] * w[k : k + 1]
        out[at : at + ROWS_AT_ONCE, :] = total.astype(BF16)


def conv_backward(projected, grad_mixed, weight, bias):
    length = projected.shape[0]
    return pl.pallas_call(
        conv_backward_kernel,
        grid=(CONVCH // LANES,),
        out_shape=(shape((length, CONVCH), BF16), shape((8, CONVCH), F32)),
        in_specs=[
            pl.BlockSpec((length, LANES), lambda i: (0, INNER // LANES + i)),
            pl.BlockSpec((length, LANES), lambda i: (0, i)),
            pl.BlockSpec((KCONV, LANES), lambda i: (0, i)),
            pl.BlockSpec((1, LANES), lambda i: (0, i)),
        ],
        out_specs=(
            pl.BlockSpec((length, LANES), lambda i: (0, i)),
            pl.BlockSpec((8, LANES), lambda i: (0, i)),
        ),
        scratch_shapes=[pltpu.VMEM((length + 8, LANES), F32)] * 2,
        compiler_params=params(),
        cost_estimate=cost(15),
    )(projected, grad_mixed, weight, bias)


def middle_kernel(
    limit, mixed_out, w_out, tokens, teacher, mask, ssm, gate, gain,
    block_out, grad_result, grad_branch, grad_ssm, grad_gate, error, gain_sums,
):
    step = pl.program_id(0)

    @pl.when(step == 0)
    def _():
        error[...] = jnp.zeros_like(error)
        gain_sums[...] = jnp.zeros_like(gain_sums)

    rows = tokens.shape[0]
    result = tokens[...].astype(F32) + dot(mixed_out[...], w_out[...])
    position = step * rows + lax.broadcasted_iota(jnp.int32, (rows, 1), 0)
    valid = (position < limit[0]).astype(F32)
    weight = valid * mask[:, 0:1]
    block_out[...] = (result * valid).astype(BF16)
    misfit = result - teacher[...].astype(F32)
    pulled = 2.0 * weight * misfit
    grad_result[...] = pulled
    error[...] += jnp.sum(0.5 * pulled * misfit, axis=0, keepdims=True)
    low = pulled.astype(BF16)
    grad_branch[...] = low
    grad_mixed = dot(low, w_out[...], NT)
    g = gate[...]
    sig = 1.0 / (1.0 + jnp.exp(-g))
    act = g * sig
    inner = ssm[...]
    gated = inner * act
    rho = lax.rsqrt(jnp.mean(gated * gated, axis=1, keepdims=True) + NORM_EPS)
    unit = gated * rho
    gain_sums[...] += jnp.sum(unit * grad_mixed, axis=0, keepdims=True)
    grad_unit = grad_mixed * gain[...]
    share = jnp.mean(grad_unit * unit, axis=1, keepdims=True)
    grad_gated = rho * (grad_unit - unit * share)
    grad_ssm[...] = grad_gated * act
    grad_gate[...] = (grad_gated * inner * (sig * (1.0 + g * (1.0 - sig)))).astype(BF16)


def middle(limit, mixed_out, w_out, tokens, teacher, mask, ssm, projected, gain):
    length = tokens.shape[0]
    rows = 128
    by_row = lambda width: pl.BlockSpec((rows, width), lambda i: (i, 0))
    whole = lambda v: pl.BlockSpec(v.shape, lambda i: (0,) * v.ndim)
    return pl.pallas_call(
        middle_kernel,
        grid=(length // rows,),
        out_shape=(
            shape((length, D), BF16),
            shape((length, D), F32),
            shape((length, D), BF16),
            shape((length, INNER), F32),
            shape((length, INNER), BF16),
            shape((1, D), F32),
            shape((1, INNER), F32),
        ),
        in_specs=[
            SMEM,
            by_row(INNER),
            whole(w_out),
            by_row(D),
            by_row(D),
            by_row(LANES),
            by_row(INNER),
            by_row(INNER),
            whole(gain),
        ],
        out_specs=(
            by_row(D),
            by_row(D),
            by_row(D),
            by_row(INNER),
            by_row(INNER),
            pl.BlockSpec((1, D), lambda i: (0, 0)),
            pl.BlockSpec((1, INNER), lambda i: (0, 0)),
        ),
        compiler_params=params(),
        cost_estimate=cost(25),
    )(limit, mixed_out, w_out, tokens, teacher, mask, ssm, projected, gain)


def body(tokens, teacher, lengths, loss_mask, owners, master, first_moment, second_moment):
    capacity = master.shape[0]
    dp, fsdp = lax.axis_size("dp"), lax.axis_size("fsdp")
    devices = dp * fsdp
    me = lax.axis_index(AXES).astype(jnp.int32)
    order_a, order_b = step_orders(dp, fsdp)
    plan = make_plan(owners, capacity, devices, me)
    n0, n1 = plan["slots"]
    na = (n0 + 1) // 2
    nb = n0 - na

    sent = send_blocks(plan["send_rows"], master)
    at_home = lax.all_to_all(sent, AXES, 0, 0, tiled=True)
    mine = pick_blocks(jnp.concatenate(plan["received"]), at_home)
    parts_a = gather_steps(mine[:na], order_a)
    parts_b = gather_steps(mine[na:n0], order_b)
    parts_a, parts_b, mine1 = lax.optimization_barrier((parts_a, parts_b, mine[n0:]))
    own1, got1 = gather_steps(mine1, order_a)
    relative = plan["home"] ^ me
    place_a, place_b = place_of(relative, order_a), place_of(relative, order_b)
    slot = plan["slot"]
    table = jnp.where(slot < na, place_a * na + slot, devices * na + place_b * nb + slot - na)
    table0 = jnp.concatenate([table[:MID0], table[MID1:]])
    table1 = (place_a * n1 + slot)[MID0:MID1]
    input_weight, head, tail, vec = unpack_in(table0, parts_a + parts_b)
    output_weight = unpack_out(table1, own1, got1, head, tail)
    vec = vec.reshape(-1)
    vectors, at = [], 0
    for size in (CONVCH * KCONV, CONVCH, HEADS, HEADS, HEADS, D, INNER):
        vectors.append(vec[at : at + size])
        at += size
    conv_weight = vectors[0].reshape(CONVCH, KCONV)
    conv_bias, dt_bias, a_log, skip_gain, norm_gain, gate_gain = vectors[1:]

    pad_heads = lambda v: jnp.pad(v, (0, LANES - HEADS))[None]
    dt_bias, a_log = pad_heads(dt_bias), pad_heads(a_log)
    conv_weight, conv_bias, gate_gain = conv_weight.T, conv_bias[None], gate_gain[None]
    skip = jnp.repeat(skip_gain, HEADDIM)[None]
    spread, gather = heads_spread(), heads_gather()

    inputs, target = tokens[0], teacher[0]
    mask = jnp.broadcast_to(loss_mask[0].astype(F32)[:, None], (inputs.shape[0], LANES))
    wide_in = inputs.astype(F32)
    inverse = lax.rsqrt(jnp.mean(wide_in * wide_in, axis=-1, keepdims=True) + NORM_EPS)
    normed = wide_in * inverse
    hidden = (normed * norm_gain).astype(BF16)
    projected = dot(hidden, input_weight)
    mixed = conv_forward(projected, conv_weight, conv_bias)
    ssm, mixed_out, states = scan_forward(mixed, projected, dt_bias, a_log, skip, gate_gain, spread)
    block_out, grad_result, grad_branch, grad_ssm, grad_gate_raw, errors, grad_gate = middle(
        lengths, mixed_out, output_weight, inputs, target, mask, ssm, projected, gate_gain
    )
    position = jnp.arange(inputs.shape[0], dtype=jnp.int32)
    local = jnp.stack(
        [jnp.sum(jnp.where(position < lengths[0], loss_mask[0], 0)).astype(F32), jnp.sum(errors)]
    )
    totals = total_over_devices(jnp.broadcast_to(local[:, None], (2, LANES)), order_a)
    grad_weight_out = dot(mixed_out, grad_branch, (((0,), (0,)), ((), ())))
    half_a, half_b, half_1 = devices * na // 2, devices * nb // 2, devices * n1 // 2
    keep1, send1, head, tail = pack_out(table1, grad_weight_out, (half_1, half_1))
    sum1 = reduce_steps(keep1, send1, order_a)
    grad_mixed, grad_dt, sums, skip_sums = scan_backward(
        mixed, projected, ssm, grad_ssm, states, dt_bias, a_log, skip, spread, gather
    )
    grad_conv, conv_sums = conv_backward(projected, grad_mixed, conv_weight, conv_bias)
    grad_low = jnp.concatenate([grad_gate_raw, grad_conv, grad_dt], axis=1)
    grad_weight_in = dot(hidden, grad_low, (((0,), (0,)), ((), ())))
    grad_hidden = dot(grad_low, input_weight, NT)
    grad_norm = jnp.sum(grad_hidden * normed, axis=0)
    grad_normed = grad_hidden * norm_gain
    input_grad = grad_result + inverse * (
        grad_normed - normed * jnp.mean(grad_normed * normed, axis=-1, keepdims=True)
    )
    grad_vec = jnp.concatenate(
        [
            conv_sums[:KCONV].T.reshape(-1),
            conv_sums[KCONV],
            sums[0, :HEADS],
            sums[1, :HEADS],
            jnp.sum(skip_sums.reshape(HEADS, HEADDIM), axis=1),
            grad_norm,
            grad_gate[0],
            jnp.zeros((NBLK * PBLOCK - PTOT,), F32),
        ]
    ).reshape(VEC_ROWS, LANES)
    keep_a, send_a, keep_b, send_b = pack_in(
        table0, grad_weight_in, head, tail, grad_vec, (half_a, half_a, half_b, half_b)
    )
    sum_a = reduce_steps(keep_a, send_a, order_a)
    sum_b = reduce_steps(keep_b, send_b, order_b)
    back = pick_blocks(plan["back"], jnp.concatenate([sum_a, sum_b, sum1], axis=0))
    got = lax.all_to_all(back, AXES, 0, 0, tiled=True)
    divisor = totals[0, 0] * D
    new_first, new_second, new_master = adam(
        plan["row_from"],
        divisor,
        got,
        plan["row_block"],
        plan["row_used"],
        master,
        first_moment,
        second_moment,
    )
    mean_loss = totals[1, 0] / divisor
    return (block_out[None], input_grad[None], mean_loss, new_first, new_second, new_master)


def solution(mesh):
    return jax.shard_map(
        body,
        mesh=mesh,
        in_specs=(
            P(AXES, None, None),
            P(AXES, None, None),
            P(AXES),
            P(AXES, None),
            P(),
            P(AXES, None),
            P(AXES, None),
            P(AXES, None),
        ),
        out_specs=(
            P(AXES, None, None),
            P(AXES, None, None),
            P(),
            P(AXES, None),
            P(AXES, None),
            P(AXES, None),
        ),
        check_vma=False,
    )
```

```python
from functools import partial

import jax
import jax.numpy as jnp
from jax import lax
from jax.experimental import pallas as pl
from jax.experimental.pallas import tpu as pltpu
from jax.sharding import PartitionSpec as P

D = 768
INNER = 1536
NSTATE = 128
HEADDIM = 64
KCONV = 4
SCAN_LEN = 256
PBLOCK = 4096
STEP = 10
HEADS = 24
CONVCH = 1792
PROJ = 3352
PTOT = 3765320
NBLK = 920

LANES = 128
BROWS = PBLOCK // LANES
END_IN = D * PROJ
END_OUT = END_IN + INNER * D
MID0 = -(-END_IN // PBLOCK)
MID1 = END_OUT // PBLOCK
N0 = MID0 + NBLK - MID1
N1 = MID1 - MID0
F0_ROWS = N0 * BROWS
IN_ROWS = END_IN // LANES
HEAD_ROWS = MID0 * BROWS - IN_ROWS
TAIL_ROWS = (END_OUT - MID1 * PBLOCK) // LANES
OUT_ROWS = INNER * D // LANES
VEC_ROWS = (NBLK - MID1) * BROWS - TAIL_ROWS
VEC_AT = MID0 * BROWS + TAIL_ROWS
GROUP = 16
GROUPS = D // GROUP
GROUP_ROWS = GROUP * PROJ // LANES
COL_TILES = -(-PROJ // LANES)
WIDE = COL_TILES * LANES
OUT_TILES = D // LANES

NORM_EPS = 1e-05
ADAM_EPS = 1e-08
BETA_ONE = 0.9
BETA_TWO = 0.999
MATRIX_RATE = 0.03
VECTOR_RATE = 0.2
WEIGHT_DECAY = 0.1
PRECISE = lax.Precision.HIGHEST
AXES = ("dp", "fsdp")
VMEM_LIMIT = 60 * 1024 * 1024


def bits_of(count):
    return count.bit_length() - 1


def step_orders(dp, fsdp):
    wide = [("dp", i) for i in range(bits_of(dp))]
    narrow = [("fsdp", i) for i in range(bits_of(fsdp))]
    first = wide[:2] + narrow + wide[2:]
    second = wide[:1] + narrow + wide[1:]
    return first, second


def exchange(values, step):
    axis, bit = step
    size = lax.axis_size(axis)
    return lax.ppermute(values, axis, [(i, i ^ (1 << bit)) for i in range(size)])


def place_of(relative, order):
    shift_of = {"dp": bits_of(lax.axis_size("fsdp")), "fsdp": 0}
    place = jnp.zeros_like(relative)
    for axis, bit in order:
        place = place * 2 + ((relative >> (shift_of[axis] + bit)) & 1)
    return place


def make_plan(owners, capacity, devices, me):
    block = jnp.arange(NBLK, dtype=jnp.int32)
    mid = (block >= MID0) & (block < MID1)
    same = mid[:, None] == mid[None, :]
    before = (owners[None, :] < owners[:, None]) | (
        (owners[None, :] == owners[:, None]) & (block[None, :] < block[:, None])
    )
    order_in_class = jnp.sum((same & before).astype(jnp.int32), axis=1)
    home, slot = order_in_class % devices, order_in_class // devices
    device = jnp.arange(devices, dtype=jnp.int32)
    below = owners[None, :] < device[:, None]
    owned = owners[None, :] == device[:, None]

    def total(mask):
        return jnp.sum(mask.astype(jnp.int32), axis=1)

    start = (total(below & ~mid[None, :]), total(below & mid[None, :]))
    count = (total(owned & ~mid[None, :]), total(owned & mid[None, :]))
    early = total(owned & (block < MID0)[None, :])
    pair = 2 + max(capacity - 2, 0) // devices

    def pick(vector, index):
        return jnp.sum(jnp.where(device == index, vector, 0))

    my_start = [pick(v, me) for v in start]
    my_count = [pick(v, me) for v in count]
    my_early = pick(early, me)

    lane = jnp.arange(pair, dtype=jnp.int32)
    k0 = (device[:, None] - my_start[0]) % devices + lane[None, :] * devices
    k1 = (device[:, None] - my_start[1]) % devices + (pair - 1 - lane)[None, :] * devices
    row0 = jnp.where(k0 < my_early, k0, k0 + my_count[1])
    send_rows = jnp.where(
        k0 < my_count[0], row0, jnp.where(k1 < my_count[1], my_early + k1, 0)
    ).reshape(-1)

    slots = (-(-N0 // devices), -(-N1 // devices))

    def received(kind):
        wanted = me + devices * jnp.arange(slots[kind], dtype=jnp.int32)
        ends = start[kind] + count[kind]
        owner = jnp.sum((ends[None, :] <= wanted[:, None]).astype(jnp.int32), axis=1)
        owner = jnp.minimum(owner, devices - 1)
        base = jnp.sum(jnp.where(device[None, :] == owner[:, None], start[kind][None, :], 0), axis=1)
        turn = jnp.clip((wanted - base) // devices, 0, pair - 1)
        return owner * pair + (turn if kind == 0 else pair - 1 - turn)

    turns = -(-capacity // devices)

    def back_to_owners(kind):
        lane = jnp.arange(turns, dtype=jnp.int32)
        k = (me - start[kind])[:, None] % devices + lane[None, :] * devices
        at = (start[kind][:, None] + k) // devices
        return jnp.where(k < count[kind][:, None], at, 0).reshape(-1)

    row = jnp.arange(capacity, dtype=jnp.int32)
    is_mid = (row >= my_early) & (row < my_early + my_count[1])
    k = jnp.where(is_mid, row - my_early, jnp.where(row < my_early, row, row - my_count[1]))
    first = jnp.where(is_mid, my_start[1], my_start[0])
    turn = k // devices
    row_from = ((first + k) % devices) * turns + turn + jnp.where(is_mid, devices * turns, 0)
    row_used = row < my_count[0] + my_count[1]
    mine = (owners == me)[None, :]
    rank = jnp.sum((mine & (block[None, :] < block[:, None])).astype(jnp.int32), axis=1)
    row_block = jnp.sum(
        jnp.where(mine & (rank[None, :] == row[:, None]), block[None, :], 0), axis=1
    )
    row_from = jnp.where(row_block >= MID1, 2 * devices * turns + row_block - MID1, row_from)
    row_from = jnp.where(row_used, row_from, 0)
    return dict(
        home=home, slot=slot, slots=slots, pair=pair, send_rows=send_rows,
        received=(received(0), received(1)), back=(back_to_owners(0), back_to_owners(1)), row_from=row_from,
        row_used=row_used, row_block=row_block,
    )


ANY = pl.BlockSpec(memory_space=pl.ANY)
VMEM = pl.BlockSpec(memory_space=pltpu.VMEM)
SMEM = pl.BlockSpec(memory_space=pltpu.SMEM)


def params(**extra):
    return pltpu.CompilerParams(vmem_limit_bytes=VMEM_LIMIT, **extra)


def shape(dims, dtype):
    return jax.ShapeDtypeStruct(dims, dtype)


def send_kernel(table, master, out, flat):
    capacity = master.shape[0]
    for j in range(BROWS):
        flat[pl.ds(j, capacity, stride=BROWS), :] = master[:, j * LANES : (j + 1) * LANES]

    def step(i, carry):
        out[i] = flat[pl.ds(pl.multiple_of(table[i] * BROWS, BROWS), BROWS), :].astype(out.dtype)
        return carry

    lax.fori_loop(0, out.shape[0], step, 0)


def send_blocks(table, master):
    return pl.pallas_call(
        send_kernel,
        out_shape=shape((table.shape[0], BROWS, LANES), jnp.bfloat16),
        in_specs=[SMEM, VMEM],
        out_specs=VMEM,
        scratch_shapes=[pltpu.VMEM((master.shape[0] * BROWS, LANES), jnp.float32)],
        compiler_params=params(),
    )(table, master)


def pick_kernel(table, source, out):
    def step(i, carry):
        out[i] = source[table[i]]
        return carry

    lax.fori_loop(0, out.shape[0], step, 0)


def pick_blocks(table, source):
    return pl.pallas_call(
        pick_kernel,
        out_shape=shape((table.shape[0],) + source.shape[1:], source.dtype),
        in_specs=[SMEM, VMEM],
        out_specs=VMEM,
        compiler_params=params(),
    )(table, source)


def row_start(rho):
    return (PROJ * rho) // LANES, (PROJ * rho) % LANES


def copy_all(pairs, sem):
    copies = [pltpu.make_async_copy(a, b, sem.at[i]) for i, (a, b) in enumerate(pairs)]
    for c in copies:
        c.start()
    for c in copies:
        c.wait()


def spread_blocks(table, held, flat, count, first_row):
    def one(i):
        at = pl.multiple_of(first_row + i * BROWS, 16)
        flat[pl.ds(at, BROWS), :] = held[table[i]].astype(jnp.float32)

    def step(i, carry):
        for u in range(4):
            one(i * 4 + u)
        return carry

    lax.fori_loop(0, count // 4, step, 0)
    for i in range(count // 4 * 4, count):
        one(i)


def unpack_in_kernel(table, *refs):
    parts, (w_in, head, tail, vec, held, flat, tile, sem) = refs[:-8], refs[-8:]
    pairs, at = [], 0
    for part in parts:
        pairs.append((part, held.at[pl.ds(at, part.shape[0])]))
        at += part.shape[0]
    copy_all(pairs, sem)
    spread_blocks(table, held, flat, N0, 0)
    head[...] = flat[IN_ROWS : IN_ROWS + HEAD_ROWS, :]
    tail[...] = flat[MID0 * BROWS : MID0 * BROWS + TAIL_ROWS, :]
    vec[...] = flat[VEC_AT:F0_ROWS, :]
    lane = lax.broadcasted_iota(jnp.int32, (GROUPS, LANES), 1)

    def columns(j):
        for rho in range(GROUP):
            c, s = row_start(rho)
            x = flat[pl.ds(c + j, GROUPS, stride=GROUP_ROWS), :]
            if s:
                y = flat[pl.ds(c + j + 1, GROUPS, stride=GROUP_ROWS), :]
                x = jnp.where(
                    lane < LANES - s,
                    pltpu.roll(x, LANES - s, 1),
                    pltpu.roll(y, LANES - s, 1),
                )
            tile[pl.ds(rho, GROUPS, stride=GROUP), :] = x

    def step(j, carry):
        columns(j)
        w_in[:, pl.ds(pl.multiple_of(j * LANES, LANES), LANES)] = tile[...].astype(jnp.bfloat16)
        return carry

    lax.fori_loop(0, COL_TILES - 1, step, 0)
    columns(COL_TILES - 1)
    last = (COL_TILES - 1) * LANES
    inside = lax.broadcasted_iota(jnp.int32, (D, LANES), 1) < PROJ - last
    w_in[:, last:] = jnp.where(inside, tile[...], 0.0).astype(jnp.bfloat16)


def unpack_in(table, parts):
    held = sum(part.shape[0] for part in parts)
    return pl.pallas_call(
        unpack_in_kernel,
        out_shape=(
            shape((D, WIDE), jnp.bfloat16),
            shape((HEAD_ROWS, LANES), jnp.float32),
            shape((TAIL_ROWS, LANES), jnp.float32),
            shape((VEC_ROWS, LANES), jnp.float32),
        ),
        in_specs=[SMEM] + [ANY] * len(parts),
        out_specs=(VMEM,) * 4,
        scratch_shapes=[
            pltpu.VMEM((held, BROWS, LANES), jnp.bfloat16),
            pltpu.VMEM((F0_ROWS, LANES), jnp.float32),
            pltpu.VMEM((D, LANES), jnp.float32),
            pltpu.SemaphoreType.DMA((len(parts),)),
        ],
        compiler_params=params(),
    )(table, *parts)


def unpack_out_kernel(table, held, head, tail, w_out, flat):
    flat[0:HEAD_ROWS, :] = head[...]
    flat[OUT_ROWS - TAIL_ROWS : OUT_ROWS, :] = tail[...]
    spread_blocks(table, held, flat, N1, HEAD_ROWS)
    rows = 128

    def step(i, carry):
        at = pl.multiple_of(i * rows, rows)
        for j in range(OUT_TILES):
            x = flat[pl.ds(at * OUT_TILES + j, rows, stride=OUT_TILES), :]
            w_out[pl.ds(at, rows), j * LANES : (j + 1) * LANES] = x.astype(jnp.bfloat16)
        return carry

    lax.fori_loop(0, INNER // rows, step, 0)


def unpack_out(table, held, head, tail):
    return pl.pallas_call(
        unpack_out_kernel,
        out_shape=shape((INNER, D), jnp.bfloat16),
        in_specs=[SMEM] + [VMEM] * 3,
        out_specs=VMEM,
        scratch_shapes=[pltpu.VMEM((OUT_ROWS, LANES), jnp.float32)],
        compiler_params=params(),
    )(table, held, head, tail)


def permute_blocks(table, flat, count, first_row, staged):
    def one(i):
        at = pl.multiple_of(first_row + i * BROWS, 16)
        staged[table[i]] = flat[pl.ds(at, BROWS), :]

    def step(i, carry):
        for u in range(4):
            one(i * 4 + u)
        return carry

    lax.fori_loop(0, count // 4, step, 0)
    for i in range(count // 4 * 4, count):
        one(i)


def pack_in_kernel(table, grad, head, *refs):
    outs, (tiles, flat, staged, sem, tile_sem) = refs[:-5], refs[-5:]
    copy_all(
        [
            (grad.at[:, pl.ds(j * LANES, LANES)], tiles.at[pl.ds(j * D, D)])
            for j in range(COL_TILES)
        ],
        tile_sem,
    )
    lane = lax.broadcasted_iota(jnp.int32, (GROUPS, LANES), 1)

    def load(rho, j):
        return tiles[pl.ds(j * D + rho, GROUPS, stride=GROUP), :]

    for rho in range(GROUP):
        _, s = row_start(rho)
        first = -(-PROJ * rho // LANES)
        col0 = first * LANES - PROJ * rho
        full = (PROJ - col0) // LANES

        def step(i, carry, rho=rho, first=first, col0=col0):
            x = load(rho, i)
            if col0:
                y = load(rho, i + 1)
                x = jnp.where(
                    lane < LANES - col0,
                    pltpu.roll(x, LANES - col0, 1),
                    pltpu.roll(y, LANES - col0, 1),
                )
            flat[pl.ds(first + i, GROUPS, stride=GROUP_ROWS), :] = x
            return carry

        lax.fori_loop(0, full, step, 0)
        left = PROJ - col0 - full * LANES
        if left:
            begin = col0 + full * LANES
            j, s = begin // LANES, begin % LANES
            x = pltpu.roll(load(rho, j), (LANES - s) % LANES, 1) if s else load(rho, j)
            if s + left > LANES:
                x = jnp.where(lane < LANES - s, x, pltpu.roll(load(rho, j + 1), LANES - s, 1))
            y = pltpu.roll(load(rho + 1, 0), left, 1)
            flat[pl.ds(first + full, GROUPS, stride=GROUP_ROWS), :] = jnp.where(lane < left, x, y)
    flat[IN_ROWS : IN_ROWS + HEAD_ROWS, :] = head[...]
    permute_blocks(table, flat, MID0, 0, staged)
    pairs, at = [], 0
    for out in outs:
        pairs.append((staged.at[pl.ds(at, out.shape[0])], out))
        at += out.shape[0]
    copy_all(pairs, sem)


def pack_in(table, grad, head, sizes):
    return pl.pallas_call(
        pack_in_kernel,
        out_shape=tuple(shape((n, BROWS, LANES), jnp.float32) for n in sizes),
        in_specs=[SMEM, ANY, VMEM],
        out_specs=(ANY,) * len(sizes),
        scratch_shapes=[
            pltpu.VMEM((COL_TILES * D, LANES), jnp.float32),
            pltpu.VMEM((MID0 * BROWS, LANES), jnp.float32),
            pltpu.VMEM((sum(sizes), BROWS, LANES), jnp.float32),
            pltpu.SemaphoreType.DMA((len(sizes),)),
            pltpu.SemaphoreType.DMA((COL_TILES,)),
        ],
        compiler_params=params(),
    )(table, grad, head)


def pack_out_kernel(table, grad, out, head, tail, flat):
    rows = 128

    def step(i, carry):
        at = pl.multiple_of(i * rows, rows)
        for j in range(OUT_TILES):
            flat[pl.ds(at * OUT_TILES + j, rows, stride=OUT_TILES), :] = grad[
                pl.ds(at, rows), j * LANES : (j + 1) * LANES
            ]
        return carry

    lax.fori_loop(0, INNER // rows, step, 0)
    head[...] = flat[0:HEAD_ROWS, :]
    tail[...] = flat[OUT_ROWS - TAIL_ROWS : OUT_ROWS, :]
    permute_blocks(table, flat, N1, HEAD_ROWS, out)


def pack_out(table, grad, size):
    return pl.pallas_call(
        pack_out_kernel,
        out_shape=(
            shape((size, BROWS, LANES), jnp.float32),
            shape((HEAD_ROWS, LANES), jnp.float32),
            shape((TAIL_ROWS, LANES), jnp.float32),
        ),
        in_specs=[SMEM, VMEM],
        out_specs=(VMEM,) * 3,
        scratch_shapes=[pltpu.VMEM((OUT_ROWS, LANES), jnp.float32)],
        compiler_params=params(),
    )(table, grad)


def adam_kernel(table, scale, got0, got1, got2, limit, used, master, first, second, o_first, o_second, o_master, flat):
    capacity = master.shape[0]

    def step(i, carry):
        at, low = table[i], 0
        rows = pl.ds(pl.multiple_of(i * BROWS, BROWS), BROWS)
        for got in (got0, got1, got2):
            high = low + got.shape[0]

            @pl.when((at >= low) & (at < high))
            def _(got=got, low=low):
                flat[rows, :] = got[at - low]

            low = high
        return carry

    lax.fori_loop(0, capacity, step, 0)
    lane = lax.broadcasted_iota(jnp.int32, (capacity, LANES), 1)
    divisor = scale[0]
    for j in range(BROWS):
        cols = slice(j * LANES, (j + 1) * LANES)
        grad = jnp.where(used[...] > 0, flat[pl.ds(j, capacity, stride=BROWS), :], 0.0) / divisor
        matrix = lane + j * LANES < limit[...]
        weights = master[:, cols]
        new_first = BETA_ONE * first[:, cols] + (1.0 - BETA_ONE) * grad
        new_second = BETA_TWO * second[:, cols] + (1.0 - BETA_TWO) * grad * grad
        normal = (
            new_first
            / (1.0 - BETA_ONE**STEP)
            / (jnp.sqrt(new_second / (1.0 - BETA_TWO**STEP)) + ADAM_EPS)
        )
        rate = jnp.where(matrix, MATRIX_RATE, VECTOR_RATE)
        decay = jnp.where(matrix, WEIGHT_DECAY, 0.0)
        o_first[:, cols] = new_first
        o_second[:, cols] = new_second
        o_master[:, cols] = weights - rate * (normal + decay * weights)


def adam(table, divisor, got0, got1, got2, row_block, row_used, master, first, second):
    capacity = master.shape[0]
    limit = jnp.broadcast_to((END_OUT - row_block * PBLOCK)[:, None], (capacity, LANES))
    used = jnp.broadcast_to(row_used.astype(jnp.int32)[:, None], (capacity, LANES))
    return pl.pallas_call(
        adam_kernel,
        out_shape=(shape(master.shape, jnp.float32),) * 3,
        in_specs=[SMEM, SMEM] + [VMEM] * 8,
        out_specs=(VMEM,) * 3,
        scratch_shapes=[pltpu.VMEM((capacity * BROWS, LANES), jnp.float32)],
        compiler_params=params(),
    )(table, divisor.reshape(1), got0, got1, got2, limit, used, master, first, second)


def gather_steps(values, order):
    for step in order[:0:-1]:
        values = jnp.concatenate([values, exchange(values, step)], axis=0)
    return values, exchange(values, order[0])


def reduce_steps(keep, send, order):
    values = keep + exchange(send, order[0])
    for step in order[1:]:
        half = values.shape[0] // 2
        values = values[:half] + exchange(values[half:], step)
    return values


CHUNK = 128
PAIRS = HEADS // 2
MIXW = INNER + 2 * NSTATE
DT_AT = INNER + CONVCH
F32 = jnp.float32
BF16 = jnp.bfloat16
NN = (((1,), (0,)), ((), ()))
NT = (((1,), (1,)), ((), ()))


def cost(microseconds):
    return pl.CostEstimate(
        flops=int(microseconds * 1e9), bytes_accessed=int(microseconds * 3e6), transcendentals=0
    )


def dot(a, b, dims=NN):
    return lax.dot_general(a, b, dims, preferred_element_type=F32)


def split(v):
    high = v.astype(BF16)
    return high, (v - high.astype(F32)).astype(BF16)


def dot3(a, b, dims=NN):
    ah, al = a
    bh, bl = b
    return dot(ah, bh, dims) + (dot(ah, bl, dims) + dot(al, bh, dims))


def heads_spread():
    row = lax.broadcasted_iota(jnp.int32, (LANES, INNER), 0)
    col = lax.broadcasted_iota(jnp.int32, (LANES, INNER), 1)
    return ((row % 32 == col // HEADDIM) & (row < 96)).astype(BF16)


def heads_gather():
    row = lax.broadcasted_iota(jnp.int32, (INNER, LANES), 0)
    col = lax.broadcasted_iota(jnp.int32, (INNER, LANES), 1)
    return (row // HEADDIM == col).astype(BF16)


def three_parts(v):
    high = v.astype(BF16).astype(F32)
    rest = v - high
    middle = rest.astype(BF16).astype(F32)
    low = rest - middle
    return (high + pltpu.roll(middle, 32, 1) + pltpu.roll(low, 64, 1)).astype(BF16)


def triangle_sum(tri, v):
    parts = dot(tri, three_parts(v))
    lane = lax.broadcasted_iota(jnp.int32, parts.shape, 1)
    total = parts + pltpu.roll(parts, LANES - 32, 1) + pltpu.roll(parts, LANES - 64, 1)
    return jnp.where(lane < HEADS, total, 0.0)


def chunk_decays(dt, dt_bias, a_log):
    lane = lax.broadcasted_iota(jnp.int32, (CHUNK, LANES), 1)
    row = lax.broadcasted_iota(jnp.int32, (CHUNK, LANES), 0)
    shifted = dt + dt_bias
    delta = jnp.where(
        lane < HEADS, jnp.maximum(shifted, 0.0) + jnp.log1p(jnp.exp(-jnp.abs(shifted))), 0.0
    )
    rate = -jnp.exp(a_log)
    lower = (row >= lane).astype(BF16)
    cum = triangle_sum(lower, delta * rate)
    last = cum[CHUNK - 1 : CHUNK, :]
    return shifted, delta, rate, cum, last


def pair_mask():
    lane = lax.broadcasted_iota(jnp.int32, (CHUNK, LANES), 1)
    low = (lane < HEADDIM).astype(F32)
    return low.astype(BF16), (1.0 - low).astype(BF16)


def scan_forward_kernel(
    mixed, dt, gate, dt_bias, a_log, skip, gain, spread, ssm, mixed_out, states, state
):
    @pl.when(pl.program_id(0) == 0)
    def _():
        state[...] = jnp.zeros_like(state)

    states[0] = state[...]
    _, delta, _, cum, last = chunk_decays(dt[...], dt_bias[...], a_log[...])
    lane = lax.broadcasted_iota(jnp.int32, (CHUNK, LANES), 1)
    row = lax.broadcasted_iota(jnp.int32, (CHUNK, LANES), 0)
    bias = jnp.where(row >= lane, 0.0, -1e30)
    heads = lane < HEADS
    stacked = jnp.concatenate(
        [
            three_parts(delta),
            three_parts(jnp.where(heads, jnp.exp(cum), 0.0)),
            three_parts(jnp.where(heads, jnp.exp(last - cum), 0.0)),
        ],
        axis=0,
    )
    cum_t = cum.T
    inputs_b = mixed[:, INNER : INNER + NSTATE]
    readout = mixed[:, INNER + NSTATE :]
    affinity = dot3(split(readout), split(inputs_b), NT)
    readout_parts = split(readout)
    b_parts = split(inputs_b.T)
    low, high = pair_mask()
    squares = jnp.zeros((CHUNK, LANES), F32)
    for j in range(PAIRS):
        cols = slice(j * LANES, (j + 1) * LANES)
        wide = dot(stacked, spread[:, cols])
        values = mixed[:, cols]
        scaled = values * wide[:CHUNK]
        sh, sl = split(scaled)
        right_h = jnp.concatenate([sh * low, sh * high], axis=0)
        right_l = jnp.concatenate([sl * low, sl * high], axis=0)
        left = []
        for h in (2 * j, 2 * j + 1):
            within = jnp.exp(cum[:, h : h + 1] - cum_t[h : h + 1, :] + bias)
            left.append(split(affinity * within))
        left_h = jnp.concatenate([left[0][0], left[1][0]], axis=1)
        left_l = jnp.concatenate([left[0][1], left[1][1]], axis=1)
        both = dot(left_h, jnp.concatenate([right_h, right_l], axis=1))
        out = both[:, :LANES] + both[:, LANES:] + dot(left_l, right_h)
        carried = state[:, cols]
        carried_parts = split(carried)
        out = out + dot3(readout_parts, carried_parts) * wide[CHUNK : 2 * CHUNK]
        out = out + skip[:, cols] * values
        end = wide[2 * CHUNK - 1 : 2 * CHUNK]
        state[:, cols] = carried * end + dot3(b_parts, split(scaled * wide[2 * CHUNK :]))
        ssm[:, cols] = out
        g = gate[:, cols]
        gated = out * (g / (1.0 + jnp.exp(-g)))
        squares = squares + gated * gated
    rho = lax.rsqrt(jnp.sum(squares, axis=1, keepdims=True) * (1.0 / INNER) + NORM_EPS)
    for j in range(PAIRS):
        cols = slice(j * LANES, (j + 1) * LANES)
        g = gate[:, cols]
        gated = ssm[:, cols] * (g / (1.0 + jnp.exp(-g)))
        mixed_out[:, cols] = (gated * rho * gain[:, cols]).astype(BF16)


def scan_forward(mixed, projected, dt_bias, a_log, skip, gain, spread):
    length = mixed.shape[0]
    chunks = length // CHUNK
    whole = lambda v: pl.BlockSpec(v.shape, lambda i: (0,) * v.ndim)
    return pl.pallas_call(
        scan_forward_kernel,
        grid=(chunks,),
        out_shape=(
            shape((length, INNER), F32),
            shape((length, INNER), BF16),
            shape((chunks, NSTATE, INNER), F32),
        ),
        in_specs=[
            pl.BlockSpec((CHUNK, MIXW), lambda i: (i, 0)),
            pl.BlockSpec((CHUNK, LANES), lambda i: (i, DT_AT // LANES)),
            pl.BlockSpec((CHUNK, INNER), lambda i: (i, 0)),
        ]
        + [whole(v) for v in (dt_bias, a_log, skip, gain, spread)],
        out_specs=(
            pl.BlockSpec((CHUNK, INNER), lambda i: (i, 0)),
            pl.BlockSpec((CHUNK, INNER), lambda i: (i, 0)),
            pl.BlockSpec((1, NSTATE, INNER), lambda i: (i, 0, 0)),
        ),
        scratch_shapes=[pltpu.VMEM((NSTATE, INNER), F32)],
        compiler_params=params(),
        cost_estimate=cost(40),
    )(mixed, projected, projected, dt_bias, a_log, skip, gain, spread)


def scan_backward_kernel(
    mixed, dt, ssm, grad, states, dt_bias, a_log, skip, spread, gather,
    grad_mixed, grad_dt, sums, skip_sums, grad_state, left, right,
):
    @pl.when(pl.program_id(0) == 0)
    def _():
        grad_state[...] = jnp.zeros_like(grad_state)
        sums[...] = jnp.zeros_like(sums)
        skip_sums[...] = jnp.zeros_like(skip_sums)

    shifted, delta, rate, cum, last = chunk_decays(dt[...], dt_bias[...], a_log[...])
    lane = lax.broadcasted_iota(jnp.int32, (CHUNK, LANES), 1)
    row = lax.broadcasted_iota(jnp.int32, (CHUNK, LANES), 0)
    bias = jnp.where(lane >= row, 0.0, -1e30)
    heads = lane < HEADS
    stacked = jnp.concatenate(
        [
            three_parts(delta),
            three_parts(jnp.where(heads, jnp.exp(cum), 0.0)),
            three_parts(jnp.where(heads, jnp.exp(last - cum), 0.0)),
        ],
        axis=0,
    )
    cum_t = cum.T
    inputs_b = mixed[:, INNER : INNER + NSTATE]
    readout = mixed[:, INNER + NSTATE :]
    b_parts, c_parts = split(inputs_b), split(readout)
    c_turned = split(readout.T)
    affinity = dot3(b_parts, c_parts, NT)
    low, high = pair_mask()
    grad_affinity = jnp.zeros((CHUNK, CHUNK), F32)
    grad_b = jnp.zeros((CHUNK, NSTATE), F32)
    grad_c = jnp.zeros((CHUNK, NSTATE), F32)
    for j in range(PAIRS):
        cols = slice(j * LANES, (j + 1) * LANES)
        wide = dot(stacked, spread[:, cols])
        wide_delta, wide_cum, wide_tail = wide[:CHUNK], wide[CHUNK : 2 * CHUNK], wide[2 * CHUNK :]
        end = wide_cum[CHUNK - 1 :]
        values = mixed[:, cols]
        pulled = grad[:, cols]
        scaled = values * wide_delta
        sh, sl = split(scaled)
        ph, plow = split(pulled)
        x_h = jnp.concatenate([sh * low, sh * high], axis=0)
        x_l = jnp.concatenate([sl * low, sl * high], axis=0)
        pull = dot(jnp.concatenate([x_h, x_l], axis=1), jnp.concatenate([ph, ph], axis=1), NT)
        pull = pull + dot(x_h, plow, NT)
        kernels = []
        for k, h in enumerate((2 * j, 2 * j + 1)):
            within = jnp.exp(cum_t[h : h + 1, :] - cum[:, h : h + 1] + bias)
            kernels.append(split(affinity * within))
            grad_affinity = grad_affinity + within * pull[k * CHUNK : (k + 1) * CHUNK]
        kernel_h = jnp.concatenate([kernels[0][0], kernels[1][0]], axis=1)
        kernel_l = jnp.concatenate([kernels[0][1], kernels[1][1]], axis=1)
        right_h = jnp.concatenate([ph * low, ph * high], axis=0)
        right_l = jnp.concatenate([plow * low, plow * high], axis=0)
        both = dot(kernel_h, jnp.concatenate([right_h, right_l], axis=1))
        grad_scaled = both[:, :LANES] + both[:, LANES:] + dot(kernel_l, right_h)
        late = grad_state[:, cols]
        late_parts = split(late)
        early = states[0, :, cols]
        from_state = dot3(b_parts, late_parts) * wide_tail
        grad_scaled = grad_scaled + from_state
        pulled_cum = split(pulled * wide_cum)
        grad_c = grad_c + dot3(pulled_cum, split(early), NT)
        grad_b = grad_b + dot3(split(scaled * wide_tail), late_parts, NT)
        grad_state[:, cols] = late * end + dot3(c_turned, pulled_cum)
        grad_mixed[:, cols] = grad_scaled * wide_delta + skip[:, cols] * pulled
        skip_sums[:, cols] += jnp.sum(pulled * values, axis=0, keepdims=True)
        left[:, cols] = grad_scaled * values
        inner = pulled * (ssm[:, cols] - skip[:, cols] * values) - scaled * grad_scaled
        extra = jnp.sum(scaled * from_state, axis=0, keepdims=True) + end * jnp.sum(
            late * early, axis=0, keepdims=True
        )
        right[:, cols] = inner + jnp.where(row == CHUNK - 1, extra, 0.0)
    ga_parts = split(grad_affinity)
    grad_mixed[:, INNER : INNER + NSTATE] = grad_b + dot3(ga_parts, c_parts)
    grad_mixed[:, INNER + NSTATE :] = grad_c + dot3(split(grad_affinity.T), b_parts)

    def by_head(v):
        high = v.astype(BF16)
        rest = v - high.astype(F32)
        middle = rest.astype(BF16)
        low = (rest - middle.astype(F32)).astype(BF16)
        g = gather[...]
        return dot(high, g) + (dot(middle, g) + dot(low, g))

    direct = by_head(left[...])
    grad_cum = by_head(right[...])
    upper = (lane >= row).astype(BF16)
    after = triangle_sum(upper, grad_cum)
    grad_delta = direct + rate * after
    grad_raw = jnp.where(heads, grad_delta / (1.0 + jnp.exp(-shifted)), 0.0)
    grad_dt[...] = grad_raw.astype(BF16)
    sums[0:1, :] += jnp.sum(grad_raw, axis=0, keepdims=True)
    sums[1:2, :] += rate * jnp.sum(delta * after, axis=0, keepdims=True)


def scan_backward(mixed, projected, ssm, grad, states, dt_bias, a_log, skip, spread, gather):
    length = mixed.shape[0]
    chunks = length // CHUNK
    whole = lambda v: pl.BlockSpec(v.shape, lambda i: (0,) * v.ndim)
    back = lambda i: (chunks - 1 - i, 0)
    return pl.pallas_call(
        scan_backward_kernel,
        grid=(chunks,),
        out_shape=(
            shape((length, MIXW), F32),
            shape((length, LANES), BF16),
            shape((8, LANES), F32),
            shape((1, INNER), F32),
        ),
        in_specs=[
            pl.BlockSpec((CHUNK, MIXW), back),
            pl.BlockSpec((CHUNK, LANES), lambda i: (chunks - 1 - i, DT_AT // LANES)),
            pl.BlockSpec((CHUNK, INNER), back),
            pl.BlockSpec((CHUNK, INNER), back),
            pl.BlockSpec((1, NSTATE, INNER), lambda i: (chunks - 1 - i, 0, 0)),
        ]
        + [whole(v) for v in (dt_bias, a_log, skip, spread, gather)],
        out_specs=(
            pl.BlockSpec((CHUNK, MIXW), back),
            pl.BlockSpec((CHUNK, LANES), back),
            pl.BlockSpec((8, LANES), lambda i: (0, 0)),
            pl.BlockSpec((1, INNER), lambda i: (0, 0)),
        ),
        scratch_shapes=[pltpu.VMEM((NSTATE, INNER), F32)] + [pltpu.VMEM((CHUNK, INNER), F32)] * 2,
        compiler_params=params(),
        cost_estimate=cost(70),
    )(mixed, projected, ssm, grad, states, dt_bias, a_log, skip, spread, gather)


ROWS_AT_ONCE = 128


def conv_sum(padded, at, weight, bias):
    total = bias + padded[pl.ds(at + 8, ROWS_AT_ONCE), :] * weight[KCONV - 1 : KCONV]
    for k in range(KCONV - 1):
        shifted = padded[pl.ds(at + 8 - (KCONV - 1) + k, ROWS_AT_ONCE), :]
        total = total + shifted * weight[k : k + 1]
    return total


def conv_forward_kernel(conv_in, weight, bias, mixed, padded):
    length = conv_in.shape[0]
    padded[0:8, :] = jnp.zeros((8, LANES), F32)
    padded[8:, :] = conv_in[...]
    w, b = weight[...], bias[...]
    for at in range(0, length, ROWS_AT_ONCE):
        out = conv_sum(padded, at, w, b)
        mixed[at : at + ROWS_AT_ONCE, :] = out / (1.0 + jnp.exp(-out))


def conv_forward(projected, weight, bias):
    length = projected.shape[0]
    return pl.pallas_call(
        conv_forward_kernel,
        grid=(CONVCH // LANES,),
        out_shape=shape((length, CONVCH), F32),
        in_specs=[
            pl.BlockSpec((length, LANES), lambda i: (0, INNER // LANES + i)),
            pl.BlockSpec((KCONV, LANES), lambda i: (0, i)),
            pl.BlockSpec((1, LANES), lambda i: (0, i)),
        ],
        out_specs=pl.BlockSpec((length, LANES), lambda i: (0, i)),
        scratch_shapes=[pltpu.VMEM((length + 8, LANES), F32)],
        compiler_params=params(),
        cost_estimate=cost(12),
    )(projected, weight, bias)


def conv_backward_kernel(conv_in, grad, weight, bias, out, sums, padded, grads):
    length = conv_in.shape[0]
    padded[0:8, :] = jnp.zeros((8, LANES), F32)
    padded[8:, :] = conv_in[...]
    grads[length:, :] = jnp.zeros((8, LANES), F32)
    w, b = weight[...], bias[...]
    totals = [jnp.zeros((1, LANES), F32)] * (KCONV + 1)
    for at in range(0, length, ROWS_AT_ONCE):
        value = conv_sum(padded, at, w, b)
        sig = 1.0 / (1.0 + jnp.exp(-value))
        g = grad[at : at + ROWS_AT_ONCE, :] * (sig * (1.0 + value * (1.0 - sig)))
        grads[at : at + ROWS_AT_ONCE, :] = g
        for k in range(KCONV):
            shifted = padded[pl.ds(at + 8 - (KCONV - 1) + k, ROWS_AT_ONCE), :]
            totals[k] = totals[k] + jnp.sum(g * shifted, axis=0, keepdims=True)
        totals[KCONV] = totals[KCONV] + jnp.sum(g, axis=0, keepdims=True)
    for k in range(KCONV + 1):
        sums[k : k + 1, :] = totals[k]
    for at in range(0, length, ROWS_AT_ONCE):
        total = grads[pl.ds(at, ROWS_AT_ONCE), :] * w[KCONV - 1 : KCONV]
        for k in range(KCONV - 1):
            total = total + grads[pl.ds(at + KCONV - 1 - k, ROWS_AT_ONCE), :] * w[k : k + 1]
        out[at : at + ROWS_AT_ONCE, :] = total.astype(BF16)


def conv_backward(projected, grad_mixed, weight, bias):
    length = projected.shape[0]
    return pl.pallas_call(
        conv_backward_kernel,
        grid=(CONVCH // LANES,),
        out_shape=(shape((length, CONVCH), BF16), shape((8, CONVCH), F32)),
        in_specs=[
            pl.BlockSpec((length, LANES), lambda i: (0, INNER // LANES + i)),
            pl.BlockSpec((length, LANES), lambda i: (0, i)),
            pl.BlockSpec((KCONV, LANES), lambda i: (0, i)),
            pl.BlockSpec((1, LANES), lambda i: (0, i)),
        ],
        out_specs=(
            pl.BlockSpec((length, LANES), lambda i: (0, i)),
            pl.BlockSpec((8, LANES), lambda i: (0, i)),
        ),
        scratch_shapes=[pltpu.VMEM((length + 8, LANES), F32)] * 2,
        compiler_params=params(),
        cost_estimate=cost(15),
    )(projected, grad_mixed, weight, bias)


def middle_kernel(
    limit, mixed_out, w_out, tokens, teacher, mask, ssm, gate, gain,
    block_out, grad_result, grad_branch, grad_ssm, grad_gate, error, gain_sums,
):
    step = pl.program_id(0)

    @pl.when(step == 0)
    def _():
        error[...] = jnp.zeros_like(error)
        gain_sums[...] = jnp.zeros_like(gain_sums)

    rows = tokens.shape[0]
    result = tokens[...].astype(F32) + dot(mixed_out[...], w_out[...])
    position = step * rows + lax.broadcasted_iota(jnp.int32, (rows, 1), 0)
    valid = (position < limit[0]).astype(F32)
    weight = valid * mask[:, 0:1]
    block_out[...] = (result * valid).astype(BF16)
    misfit = result - teacher[...].astype(F32)
    pulled = 2.0 * weight * misfit
    grad_result[...] = pulled
    error[...] += jnp.sum(0.5 * pulled * misfit, axis=0, keepdims=True)
    low = pulled.astype(BF16)
    grad_branch[...] = low
    grad_mixed = dot(low, w_out[...], NT)
    g = gate[...]
    sig = 1.0 / (1.0 + jnp.exp(-g))
    act = g * sig
    inner = ssm[...]
    gated = inner * act
    rho = lax.rsqrt(jnp.mean(gated * gated, axis=1, keepdims=True) + NORM_EPS)
    unit = gated * rho
    gain_sums[...] += jnp.sum(unit * grad_mixed, axis=0, keepdims=True)
    grad_unit = grad_mixed * gain[...]
    share = jnp.mean(grad_unit * unit, axis=1, keepdims=True)
    grad_gated = rho * (grad_unit - unit * share)
    grad_ssm[...] = grad_gated * act
    grad_gate[...] = (grad_gated * inner * (sig * (1.0 + g * (1.0 - sig)))).astype(BF16)


def middle(limit, mixed_out, w_out, tokens, teacher, mask, ssm, projected, gain):
    length = tokens.shape[0]
    rows = 128
    by_row = lambda width: pl.BlockSpec((rows, width), lambda i: (i, 0))
    whole = lambda v: pl.BlockSpec(v.shape, lambda i: (0,) * v.ndim)
    return pl.pallas_call(
        middle_kernel,
        grid=(length // rows,),
        out_shape=(
            shape((length, D), BF16),
            shape((length, D), F32),
            shape((length, D), BF16),
            shape((length, INNER), F32),
            shape((length, INNER), BF16),
            shape((1, D), F32),
            shape((1, INNER), F32),
        ),
        in_specs=[
            SMEM,
            by_row(INNER),
            whole(w_out),
            by_row(D),
            by_row(D),
            by_row(LANES),
            by_row(INNER),
            by_row(INNER),
            whole(gain),
        ],
        out_specs=(
            by_row(D),
            by_row(D),
            by_row(D),
            by_row(INNER),
            by_row(INNER),
            pl.BlockSpec((1, D), lambda i: (0, 0)),
            pl.BlockSpec((1, INNER), lambda i: (0, 0)),
        ),
        compiler_params=params(),
        cost_estimate=cost(25),
    )(limit, mixed_out, w_out, tokens, teacher, mask, ssm, projected, gain)


def body(tokens, teacher, lengths, loss_mask, owners, master, first_moment, second_moment):
    capacity = master.shape[0]
    dp, fsdp = lax.axis_size("dp"), lax.axis_size("fsdp")
    devices = dp * fsdp
    me = lax.axis_index(AXES).astype(jnp.int32)
    order_a, order_b = step_orders(dp, fsdp)
    plan = make_plan(owners, capacity, devices, me)
    n0, n1 = plan["slots"]
    na = (n0 + 1) // 2
    nb = n0 - na

    sent = send_blocks(plan["send_rows"], master)
    at_home = lax.all_to_all(sent, AXES, 0, 0, tiled=True)
    mine = pick_blocks(jnp.concatenate(plan["received"]), at_home)
    parts_a = gather_steps(mine[:na], order_a)
    parts_b = gather_steps(mine[na:n0], order_b)
    parts_a, parts_b, mine1 = lax.optimization_barrier((parts_a, parts_b, mine[n0:]))
    held1 = lax.all_gather(mine1, AXES, axis=0, tiled=True)
    relative = plan["home"] ^ me
    place_a, place_b = place_of(relative, order_a), place_of(relative, order_b)
    slot = plan["slot"]
    table = jnp.where(slot < na, place_a * na + slot, devices * na + place_b * nb + slot - na)
    table0 = jnp.concatenate([table[:MID0], table[MID1:]])
    table1 = (plan["home"] * n1 + slot)[MID0:MID1]
    input_weight, head, tail, vec = unpack_in(table0, parts_a + parts_b)
    output_weight = unpack_out(table1, held1, head, tail)
    vec = vec.reshape(-1)
    vectors, at = [], 0
    for size in (CONVCH * KCONV, CONVCH, HEADS, HEADS, HEADS, D, INNER):
        vectors.append(vec[at : at + size])
        at += size
    conv_weight = vectors[0].reshape(CONVCH, KCONV)
    conv_bias, dt_bias, a_log, skip_gain, norm_gain, gate_gain = vectors[1:]

    pad_heads = lambda v: jnp.pad(v, (0, LANES - HEADS))[None]
    dt_bias, a_log = pad_heads(dt_bias), pad_heads(a_log)
    conv_weight, conv_bias, gate_gain = conv_weight.T, conv_bias[None], gate_gain[None]
    skip = jnp.repeat(skip_gain, HEADDIM)[None]
    spread, gather = heads_spread(), heads_gather()

    inputs, target = tokens[0], teacher[0]
    mask = jnp.broadcast_to(loss_mask[0].astype(F32)[:, None], (inputs.shape[0], LANES))
    wide_in = inputs.astype(F32)
    inverse = lax.rsqrt(jnp.mean(wide_in * wide_in, axis=-1, keepdims=True) + NORM_EPS)
    normed = wide_in * inverse
    hidden = (normed * norm_gain).astype(BF16)
    projected = dot(hidden, input_weight)
    mixed = conv_forward(projected, conv_weight, conv_bias)
    ssm, mixed_out, states = scan_forward(mixed, projected, dt_bias, a_log, skip, gate_gain, spread)
    block_out, grad_result, grad_branch, grad_ssm, grad_gate_raw, errors, grad_gate = middle(
        lengths, mixed_out, output_weight, inputs, target, mask, ssm, projected, gate_gain
    )
    position = jnp.arange(inputs.shape[0], dtype=jnp.int32)
    counted = jnp.sum(jnp.where(position < lengths[0], loss_mask[0], 0)).astype(F32)
    local = jnp.concatenate([errors.reshape(-1, LANES), jnp.broadcast_to(counted, (2, LANES))])
    grad_weight_out = dot(mixed_out, grad_branch, (((0,), (0,)), ((), ())))
    half_a, half_b = devices * na // 2, devices * nb // 2
    packed1, head, tail = pack_out(table1, grad_weight_out, devices * n1)
    grad_ssm, packed1, local = lax.optimization_barrier((grad_ssm, packed1, local))
    locals_all = lax.all_gather(local[None], AXES, axis=0, tiled=True)
    sum1 = lax.psum_scatter(packed1, AXES, scatter_dimension=0, tiled=True)
    grad_mixed, grad_dt, sums, skip_sums = scan_backward(
        mixed, projected, ssm, grad_ssm, states, dt_bias, a_log, skip, spread, gather
    )
    grad_conv, conv_sums = conv_backward(projected, grad_mixed, conv_weight, conv_bias)
    back1 = pick_blocks(plan["back"][1], sum1)
    got1 = lax.all_to_all(back1, AXES, 0, 0, tiled=True)
    grad_low = jnp.concatenate([grad_gate_raw, grad_conv, grad_dt], axis=1)
    grad_weight_in = dot(hidden, grad_low, (((0,), (0,)), ((), ())))
    grad_weight_in, locals_all, sum1 = lax.optimization_barrier((grad_weight_in, locals_all, sum1))
    keep_a, send_a, keep_b, send_b = pack_in(
        table0, grad_weight_in, head, (half_a, half_a, half_b, half_b)
    )
    grad_hidden = dot(grad_low, input_weight, NT)
    grad_norm = jnp.sum(grad_hidden * normed, axis=0)
    grad_normed = grad_hidden * norm_gain
    input_grad = grad_result + inverse * (
        grad_normed - normed * jnp.mean(grad_normed * normed, axis=-1, keepdims=True)
    )
    grad_vec = jnp.concatenate(
        [
            conv_sums[:KCONV].T.reshape(-1),
            conv_sums[KCONV],
            sums[0, :HEADS],
            sums[1, :HEADS],
            jnp.sum(skip_sums.reshape(HEADS, HEADDIM), axis=1),
            grad_norm,
            grad_gate[0],
            jnp.zeros((NBLK * PBLOCK - PTOT,), F32),
        ]
    ).reshape(VEC_ROWS, LANES)
    grad_vec = jnp.concatenate([tail, grad_vec]).reshape(NBLK - MID1, BROWS, LANES)
    sum2 = lax.psum(grad_vec, AXES)
    sum_a = reduce_steps(keep_a, send_a, order_a)
    sum_b = reduce_steps(keep_b, send_b, order_b)
    back0 = pick_blocks(plan["back"][0], jnp.concatenate([sum_a, sum_b], axis=0))
    got0 = lax.all_to_all(back0, AXES, 0, 0, tiled=True)
    error_sum = jnp.sum(locals_all[:, : D // LANES])
    divisor = jnp.sum(locals_all[:, D // LANES, 0]) * D
    new_first, new_second, new_master = adam(
        plan["row_from"],
        divisor,
        got0,
        got1,
        sum2,
        plan["row_block"],
        plan["row_used"],
        master,
        first_moment,
        second_moment,
    )
    mean_loss = error_sum / divisor
    return (block_out[None], input_grad[None], mean_loss, new_first, new_second, new_master)


def solution(mesh):
    return jax.shard_map(
        body,
        mesh=mesh,
        in_specs=(
            P(AXES, None, None),
            P(AXES, None, None),
            P(AXES),
            P(AXES, None),
            P(),
            P(AXES, None),
            P(AXES, None),
            P(AXES, None),
        ),
        out_specs=(
            P(AXES, None, None),
            P(AXES, None, None),
            P(),
            P(AXES, None),
            P(AXES, None),
            P(AXES, None),
        ),
        check_vma=False,
    )
```

```python
from functools import partial

import jax
import jax.numpy as jnp
from jax import lax
from jax.experimental import pallas as pl
from jax.experimental.pallas import tpu as pltpu
from jax.sharding import PartitionSpec as P

D = 768
INNER = 1536
NSTATE = 128
HEADDIM = 64
KCONV = 4
SCAN_LEN = 256
PBLOCK = 4096
STEP = 10
HEADS = 24
CONVCH = 1792
PROJ = 3352
PTOT = 3765320
NBLK = 920

LANES = 128
BROWS = PBLOCK // LANES
END_IN = D * PROJ
END_OUT = END_IN + INNER * D
MID0 = -(-END_IN // PBLOCK)
MID1 = END_OUT // PBLOCK
N0 = MID0 + NBLK - MID1
N1 = MID1 - MID0
F0_ROWS = N0 * BROWS
IN_ROWS = END_IN // LANES
HEAD_ROWS = MID0 * BROWS - IN_ROWS
TAIL_ROWS = (END_OUT - MID1 * PBLOCK) // LANES
OUT_ROWS = INNER * D // LANES
VEC_ROWS = (NBLK - MID1) * BROWS - TAIL_ROWS
VEC_AT = MID0 * BROWS + TAIL_ROWS
GROUP = 16
GROUPS = D // GROUP
GROUP_ROWS = GROUP * PROJ // LANES
COL_TILES = -(-PROJ // LANES)
WIDE = COL_TILES * LANES
OUT_TILES = D // LANES

NORM_EPS = 1e-05
ADAM_EPS = 1e-08
BETA_ONE = 0.9
BETA_TWO = 0.999
MATRIX_RATE = 0.03
VECTOR_RATE = 0.2
WEIGHT_DECAY = 0.1
PRECISE = lax.Precision.HIGHEST
AXES = ("dp", "fsdp")
VMEM_LIMIT = 60 * 1024 * 1024


def bits_of(count):
    return count.bit_length() - 1


def step_orders(dp, fsdp):
    wide = [("dp", i) for i in range(bits_of(dp))]
    narrow = [("fsdp", i) for i in range(bits_of(fsdp))]
    first = wide[:2] + narrow + wide[2:]
    second = wide[:1] + narrow + wide[1:]
    return first, second


def exchange(values, step):
    axis, bit = step
    size = lax.axis_size(axis)
    return lax.ppermute(values, axis, [(i, i ^ (1 << bit)) for i in range(size)])


def place_of(relative, order):
    shift_of = {"dp": bits_of(lax.axis_size("fsdp")), "fsdp": 0}
    place = jnp.zeros_like(relative)
    for axis, bit in order:
        place = place * 2 + ((relative >> (shift_of[axis] + bit)) & 1)
    return place


def make_plan(owners, capacity, devices, me):
    block = jnp.arange(NBLK, dtype=jnp.int32)
    mid = (block >= MID0) & (block < MID1)
    same = mid[:, None] == mid[None, :]
    before = (owners[None, :] < owners[:, None]) | (
        (owners[None, :] == owners[:, None]) & (block[None, :] < block[:, None])
    )
    order_in_class = jnp.sum((same & before).astype(jnp.int32), axis=1)
    home, slot = order_in_class % devices, order_in_class // devices
    device = jnp.arange(devices, dtype=jnp.int32)
    below = owners[None, :] < device[:, None]
    owned = owners[None, :] == device[:, None]

    def total(mask):
        return jnp.sum(mask.astype(jnp.int32), axis=1)

    start = (total(below & ~mid[None, :]), total(below & mid[None, :]))
    count = (total(owned & ~mid[None, :]), total(owned & mid[None, :]))
    early = total(owned & (block < MID0)[None, :])
    pair = 2 + max(capacity - 2, 0) // devices

    def pick(vector, index):
        return jnp.sum(jnp.where(device == index, vector, 0))

    my_start = [pick(v, me) for v in start]
    my_count = [pick(v, me) for v in count]
    my_early = pick(early, me)

    lane = jnp.arange(pair, dtype=jnp.int32)
    k0 = (device[:, None] - my_start[0]) % devices + lane[None, :] * devices
    k1 = (device[:, None] - my_start[1]) % devices + (pair - 1 - lane)[None, :] * devices
    row0 = jnp.where(k0 < my_early, k0, k0 + my_count[1])
    send_rows = jnp.where(
        k0 < my_count[0], row0, jnp.where(k1 < my_count[1], my_early + k1, 0)
    ).reshape(-1)

    slots = (-(-N0 // devices), -(-N1 // devices))

    def received(kind):
        wanted = me + devices * jnp.arange(slots[kind], dtype=jnp.int32)
        ends = start[kind] + count[kind]
        owner = jnp.sum((ends[None, :] <= wanted[:, None]).astype(jnp.int32), axis=1)
        owner = jnp.minimum(owner, devices - 1)
        base = jnp.sum(jnp.where(device[None, :] == owner[:, None], start[kind][None, :], 0), axis=1)
        turn = jnp.clip((wanted - base) // devices, 0, pair - 1)
        return owner * pair + (turn if kind == 0 else pair - 1 - turn)

    turns = -(-capacity // devices)

    def back_to_owners(kind):
        lane = jnp.arange(turns, dtype=jnp.int32)
        k = (me - start[kind])[:, None] % devices + lane[None, :] * devices
        at = (start[kind][:, None] + k) // devices
        return jnp.where(k < count[kind][:, None], at, 0).reshape(-1)

    row = jnp.arange(capacity, dtype=jnp.int32)
    is_mid = (row >= my_early) & (row < my_early + my_count[1])
    k = jnp.where(is_mid, row - my_early, jnp.where(row < my_early, row, row - my_count[1]))
    first = jnp.where(is_mid, my_start[1], my_start[0])
    turn = k // devices
    row_from = ((first + k) % devices) * turns + turn + jnp.where(is_mid, devices * turns, 0)
    row_used = row < my_count[0] + my_count[1]
    mine = (owners == me)[None, :]
    rank = jnp.sum((mine & (block[None, :] < block[:, None])).astype(jnp.int32), axis=1)
    row_block = jnp.sum(
        jnp.where(mine & (rank[None, :] == row[:, None]), block[None, :], 0), axis=1
    )
    row_from = jnp.where(row_block >= MID1, 2 * devices * turns + row_block - MID1, row_from)
    row_from = jnp.where(row_used, row_from, 0)
    return dict(
        home=home, slot=slot, slots=slots, pair=pair, send_rows=send_rows,
        received=(received(0), received(1)), back=(back_to_owners(0), back_to_owners(1)), row_from=row_from,
        row_used=row_used, row_block=row_block,
    )


ANY = pl.BlockSpec(memory_space=pl.ANY)
VMEM = pl.BlockSpec(memory_space=pltpu.VMEM)
SMEM = pl.BlockSpec(memory_space=pltpu.SMEM)


def params(**extra):
    return pltpu.CompilerParams(vmem_limit_bytes=VMEM_LIMIT, **extra)


def shape(dims, dtype):
    return jax.ShapeDtypeStruct(dims, dtype)


def send_kernel(table, master, out, flat):
    capacity = master.shape[0]
    for j in range(BROWS):
        flat[pl.ds(j, capacity, stride=BROWS), :] = master[:, j * LANES : (j + 1) * LANES]

    def step(i, carry):
        out[i] = flat[pl.ds(pl.multiple_of(table[i] * BROWS, BROWS), BROWS), :].astype(out.dtype)
        return carry

    lax.fori_loop(0, out.shape[0], step, 0)


def send_blocks(table, master):
    return pl.pallas_call(
        send_kernel,
        out_shape=shape((table.shape[0], BROWS, LANES), jnp.bfloat16),
        in_specs=[SMEM, VMEM],
        out_specs=VMEM,
        scratch_shapes=[pltpu.VMEM((master.shape[0] * BROWS, LANES), jnp.float32)],
        compiler_params=params(),
    )(table, master)


def pick_kernel(table, source, out):
    def step(i, carry):
        out[i] = source[table[i]]
        return carry

    lax.fori_loop(0, out.shape[0], step, 0)


def pick_blocks(table, source):
    return pl.pallas_call(
        pick_kernel,
        out_shape=shape((table.shape[0],) + source.shape[1:], source.dtype),
        in_specs=[SMEM, VMEM],
        out_specs=VMEM,
        compiler_params=params(),
    )(table, source)


def row_start(rho):
    return (PROJ * rho) // LANES, (PROJ * rho) % LANES


def copy_all(pairs, sem):
    copies = [pltpu.make_async_copy(a, b, sem.at[i]) for i, (a, b) in enumerate(pairs)]
    for c in copies:
        c.start()
    for c in copies:
        c.wait()


def spread_blocks(table, held, flat, count, first_row):
    def one(i):
        at = pl.multiple_of(first_row + i * BROWS, 16)
        flat[pl.ds(at, BROWS), :] = held[table[i]].astype(jnp.float32)

    def step(i, carry):
        for u in range(4):
            one(i * 4 + u)
        return carry

    lax.fori_loop(0, count // 4, step, 0)
    for i in range(count // 4 * 4, count):
        one(i)


def unpack_in_kernel(table, *refs):
    parts, (w_in, head, tail, vec, held, flat, tile, sem) = refs[:-8], refs[-8:]
    pairs, at = [], 0
    for part in parts:
        pairs.append((part, held.at[pl.ds(at, part.shape[0])]))
        at += part.shape[0]
    copy_all(pairs, sem)
    spread_blocks(table, held, flat, N0, 0)
    head[...] = flat[IN_ROWS : IN_ROWS + HEAD_ROWS, :]
    tail[...] = flat[MID0 * BROWS : MID0 * BROWS + TAIL_ROWS, :]
    vec[...] = flat[VEC_AT:F0_ROWS, :]
    lane = lax.broadcasted_iota(jnp.int32, (GROUPS, LANES), 1)

    def columns(j):
        for rho in range(GROUP):
            c, s = row_start(rho)
            x = flat[pl.ds(c + j, GROUPS, stride=GROUP_ROWS), :]
            if s:
                y = flat[pl.ds(c + j + 1, GROUPS, stride=GROUP_ROWS), :]
                x = jnp.where(
                    lane < LANES - s,
                    pltpu.roll(x, LANES - s, 1),
                    pltpu.roll(y, LANES - s, 1),
                )
            tile[pl.ds(rho, GROUPS, stride=GROUP), :] = x

    def step(j, carry):
        columns(j)
        w_in[:, pl.ds(pl.multiple_of(j * LANES, LANES), LANES)] = tile[...].astype(jnp.bfloat16)
        return carry

    lax.fori_loop(0, COL_TILES - 1, step, 0)
    columns(COL_TILES - 1)
    last = (COL_TILES - 1) * LANES
    inside = lax.broadcasted_iota(jnp.int32, (D, LANES), 1) < PROJ - last
    w_in[:, last:] = jnp.where(inside, tile[...], 0.0).astype(jnp.bfloat16)


def unpack_in(table, parts):
    held = sum(part.shape[0] for part in parts)
    return pl.pallas_call(
        unpack_in_kernel,
        out_shape=(
            shape((D, WIDE), jnp.bfloat16),
            shape((HEAD_ROWS, LANES), jnp.float32),
            shape((TAIL_ROWS, LANES), jnp.float32),
            shape((VEC_ROWS, LANES), jnp.float32),
        ),
        in_specs=[SMEM] + [ANY] * len(parts),
        out_specs=(VMEM,) * 4,
        scratch_shapes=[
            pltpu.VMEM((held, BROWS, LANES), jnp.bfloat16),
            pltpu.VMEM((F0_ROWS, LANES), jnp.float32),
            pltpu.VMEM((D, LANES), jnp.float32),
            pltpu.SemaphoreType.DMA((len(parts),)),
        ],
        compiler_params=params(),
    )(table, *parts)


def unpack_out_kernel(table, held, head, tail, w_out, flat):
    flat[0:HEAD_ROWS, :] = head[...]
    flat[OUT_ROWS - TAIL_ROWS : OUT_ROWS, :] = tail[...]
    spread_blocks(table, held, flat, N1, HEAD_ROWS)
    rows = 128

    def step(i, carry):
        at = pl.multiple_of(i * rows, rows)
        for j in range(OUT_TILES):
            x = flat[pl.ds(at * OUT_TILES + j, rows, stride=OUT_TILES), :]
            w_out[pl.ds(at, rows), j * LANES : (j + 1) * LANES] = x.astype(jnp.bfloat16)
        return carry

    lax.fori_loop(0, INNER // rows, step, 0)


def unpack_out(table, held, head, tail):
    return pl.pallas_call(
        unpack_out_kernel,
        out_shape=shape((INNER, D), jnp.bfloat16),
        in_specs=[SMEM] + [VMEM] * 3,
        out_specs=VMEM,
        scratch_shapes=[pltpu.VMEM((OUT_ROWS, LANES), jnp.float32)],
        compiler_params=params(),
    )(table, held, head, tail)


def permute_blocks(table, flat, count, first_row, staged):
    def one(i):
        at = pl.multiple_of(first_row + i * BROWS, 16)
        staged[table[i]] = flat[pl.ds(at, BROWS), :]

    def step(i, carry):
        for u in range(4):
            one(i * 4 + u)
        return carry

    lax.fori_loop(0, count // 4, step, 0)
    for i in range(count // 4 * 4, count):
        one(i)


def pack_in_kernel(table, grad, head, *refs):
    outs, (tiles, flat, staged, sem, tile_sem) = refs[:-5], refs[-5:]
    copy_all(
        [
            (grad.at[:, pl.ds(j * LANES, LANES)], tiles.at[pl.ds(j * D, D)])
            for j in range(COL_TILES)
        ],
        tile_sem,
    )
    lane = lax.broadcasted_iota(jnp.int32, (GROUPS, LANES), 1)

    def load(rho, j):
        return tiles[pl.ds(j * D + rho, GROUPS, stride=GROUP), :]

    def whole(rho, i):
        first = -(-PROJ * rho // LANES)
        col0 = first * LANES - PROJ * rho
        x = load(rho, i)
        if col0:
            x = jnp.where(
                lane < LANES - col0,
                pltpu.roll(x, LANES - col0, 1),
                pltpu.roll(load(rho, i + 1), LANES - col0, 1),
            )
        flat[pl.ds(first + i, GROUPS, stride=GROUP_ROWS), :] = x

    def step(i, carry):
        for rho in range(GROUP):
            whole(rho, i)
        return carry

    common = (PROJ - LANES + 1) // LANES
    lax.fori_loop(0, common, step, 0)
    for rho in range(GROUP):
        first = -(-PROJ * rho // LANES)
        col0 = first * LANES - PROJ * rho
        full = (PROJ - col0) // LANES
        for i in range(common, full):
            whole(rho, i)
        left = PROJ - col0 - full * LANES
        if left:
            begin = col0 + full * LANES
            j, s = begin // LANES, begin % LANES
            x = pltpu.roll(load(rho, j), LANES - s, 1) if s else load(rho, j)
            if s + left > LANES:
                x = jnp.where(lane < LANES - s, x, pltpu.roll(load(rho, j + 1), LANES - s, 1))
            y = pltpu.roll(load(rho + 1, 0), left, 1)
            flat[pl.ds(first + full, GROUPS, stride=GROUP_ROWS), :] = jnp.where(lane < left, x, y)
    flat[IN_ROWS : IN_ROWS + HEAD_ROWS, :] = head[...]
    permute_blocks(table, flat, MID0, 0, staged)
    pairs, at = [], 0
    for out in outs:
        pairs.append((staged.at[pl.ds(at, out.shape[0])], out))
        at += out.shape[0]
    copy_all(pairs, sem)


def pack_in(table, grad, head, sizes):
    return pl.pallas_call(
        pack_in_kernel,
        out_shape=tuple(shape((n, BROWS, LANES), jnp.float32) for n in sizes),
        in_specs=[SMEM, ANY, VMEM],
        out_specs=(ANY,) * len(sizes),
        scratch_shapes=[
            pltpu.VMEM((COL_TILES * D, LANES), jnp.float32),
            pltpu.VMEM((MID0 * BROWS, LANES), jnp.float32),
            pltpu.VMEM((sum(sizes), BROWS, LANES), jnp.float32),
            pltpu.SemaphoreType.DMA((len(sizes),)),
            pltpu.SemaphoreType.DMA((COL_TILES,)),
        ],
        compiler_params=params(),
    )(table, grad, head)


def pack_out_kernel(table, grad, local, out, head, tail, flat, *, slots):
    rows = 128

    def step(i, carry):
        at = pl.multiple_of(i * rows, rows)
        for j in range(OUT_TILES):
            flat[pl.ds(at * OUT_TILES + j, rows, stride=OUT_TILES), :] = grad[
                pl.ds(at, rows), j * LANES : (j + 1) * LANES
            ]
        return carry

    lax.fori_loop(0, INNER // rows, step, 0)
    head[...] = flat[0:HEAD_ROWS, :]
    tail[...] = flat[OUT_ROWS - TAIL_ROWS : OUT_ROWS, :]
    permute_blocks(table, flat, N1, HEAD_ROWS, out)

    def add_local(i, carry):
        out[i * slots + slots - 1, 0:8, :] = local[...]
        return carry

    lax.fori_loop(0, out.shape[0] // slots, add_local, 0)


def pack_out(table, grad, local, devices, slots):
    return pl.pallas_call(
        partial(pack_out_kernel, slots=slots),
        out_shape=(
            shape((devices * slots, BROWS, LANES), jnp.float32),
            shape((HEAD_ROWS, LANES), jnp.float32),
            shape((TAIL_ROWS, LANES), jnp.float32),
        ),
        in_specs=[SMEM, VMEM, VMEM],
        out_specs=(VMEM,) * 3,
        scratch_shapes=[pltpu.VMEM((OUT_ROWS, LANES), jnp.float32)],
        compiler_params=params(),
    )(table, grad, local)


def adam_kernel(table, scale, got0, got1, got2, limit, used, master, first, second, o_first, o_second, o_master, flat):
    capacity = master.shape[0]

    def step(i, carry):
        at, low = table[i], 0
        rows = pl.ds(pl.multiple_of(i * BROWS, BROWS), BROWS)
        for got in (got0, got1, got2):
            high = low + got.shape[0]

            @pl.when((at >= low) & (at < high))
            def _(got=got, low=low):
                flat[rows, :] = got[at - low]

            low = high
        return carry

    lax.fori_loop(0, capacity, step, 0)
    lane = lax.broadcasted_iota(jnp.int32, (capacity, LANES), 1)
    divisor = scale[0]
    for j in range(BROWS):
        cols = slice(j * LANES, (j + 1) * LANES)
        grad = jnp.where(used[...] > 0, flat[pl.ds(j, capacity, stride=BROWS), :], 0.0) / divisor
        matrix = lane + j * LANES < limit[...]
        weights = master[:, cols]
        new_first = BETA_ONE * first[:, cols] + (1.0 - BETA_ONE) * grad
        new_second = BETA_TWO * second[:, cols] + (1.0 - BETA_TWO) * grad * grad
        normal = (
            new_first
            / (1.0 - BETA_ONE**STEP)
            / (jnp.sqrt(new_second / (1.0 - BETA_TWO**STEP)) + ADAM_EPS)
        )
        rate = jnp.where(matrix, MATRIX_RATE, VECTOR_RATE)
        decay = jnp.where(matrix, WEIGHT_DECAY, 0.0)
        o_first[:, cols] = new_first
        o_second[:, cols] = new_second
        o_master[:, cols] = weights - rate * (normal + decay * weights)


def adam(table, divisor, got0, got1, got2, row_block, row_used, master, first, second):
    capacity = master.shape[0]
    limit = jnp.broadcast_to((END_OUT - row_block * PBLOCK)[:, None], (capacity, LANES))
    used = jnp.broadcast_to(row_used.astype(jnp.int32)[:, None], (capacity, LANES))
    return pl.pallas_call(
        adam_kernel,
        out_shape=(shape(master.shape, jnp.float32),) * 3,
        in_specs=[SMEM, SMEM] + [VMEM] * 8,
        out_specs=(VMEM,) * 3,
        scratch_shapes=[pltpu.VMEM((capacity * BROWS, LANES), jnp.float32)],
        compiler_params=params(),
    )(table, divisor.reshape(1), got0, got1, got2, limit, used, master, first, second)


def gather_steps(values, order):
    for step in order[:0:-1]:
        values = jnp.concatenate([values, exchange(values, step)], axis=0)
    return values, exchange(values, order[0])


def reduce_step(values, step, extra=None):
    half = values.shape[0] // 2
    if extra is None:
        return values[:half] + exchange(values[half:], step)
    got = exchange(jnp.concatenate([values[half:], extra]), step)
    return values[:half] + got[:half], extra + got[half:]


CHUNK = 128
PAIRS = HEADS // 2
MIXW = INNER + 2 * NSTATE
DT_AT = INNER + CONVCH
F32 = jnp.float32
BF16 = jnp.bfloat16
NN = (((1,), (0,)), ((), ()))
NT = (((1,), (1,)), ((), ()))


def cost(microseconds):
    return pl.CostEstimate(
        flops=int(microseconds * 1e9), bytes_accessed=int(microseconds * 3e6), transcendentals=0
    )


def dot(a, b, dims=NN):
    return lax.dot_general(a, b, dims, preferred_element_type=F32)


def split(v):
    high = v.astype(BF16)
    return high, (v - high.astype(F32)).astype(BF16)


def dot3(a, b, dims=NN):
    ah, al = a
    bh, bl = b
    return dot(ah, bh, dims) + (dot(ah, bl, dims) + dot(al, bh, dims))


def heads_spread():
    row = lax.broadcasted_iota(jnp.int32, (LANES, INNER), 0)
    col = lax.broadcasted_iota(jnp.int32, (LANES, INNER), 1)
    return ((row % 32 == col // HEADDIM) & (row < 96)).astype(BF16)


def heads_gather():
    row = lax.broadcasted_iota(jnp.int32, (INNER, LANES), 0)
    col = lax.broadcasted_iota(jnp.int32, (INNER, LANES), 1)
    return (row // HEADDIM == col).astype(BF16)


def three_parts(v):
    high = v.astype(BF16).astype(F32)
    rest = v - high
    middle = rest.astype(BF16).astype(F32)
    low = rest - middle
    return (high + pltpu.roll(middle, 32, 1) + pltpu.roll(low, 64, 1)).astype(BF16)


def triangle_sum(tri, v):
    parts = dot(tri, three_parts(v))
    lane = lax.broadcasted_iota(jnp.int32, parts.shape, 1)
    total = parts + pltpu.roll(parts, LANES - 32, 1) + pltpu.roll(parts, LANES - 64, 1)
    return jnp.where(lane < HEADS, total, 0.0)


def chunk_decays(dt, dt_bias, a_log):
    lane = lax.broadcasted_iota(jnp.int32, (CHUNK, LANES), 1)
    row = lax.broadcasted_iota(jnp.int32, (CHUNK, LANES), 0)
    shifted = dt + dt_bias
    delta = jnp.where(
        lane < HEADS, jnp.maximum(shifted, 0.0) + jnp.log1p(jnp.exp(-jnp.abs(shifted))), 0.0
    )
    rate = -jnp.exp(a_log)
    lower = (row >= lane).astype(BF16)
    cum = triangle_sum(lower, delta * rate)
    last = cum[CHUNK - 1 : CHUNK, :]
    return shifted, delta, rate, cum, last


def pair_mask():
    lane = lax.broadcasted_iota(jnp.int32, (CHUNK, LANES), 1)
    low = (lane < HEADDIM).astype(F32)
    return low.astype(BF16), (1.0 - low).astype(BF16)


def scan_forward_kernel(
    mixed, dt, gate, dt_bias, a_log, skip, gain, spread, ssm, mixed_out, states, state
):
    @pl.when(pl.program_id(0) == 0)
    def _():
        state[...] = jnp.zeros_like(state)

    states[0] = state[...]
    _, delta, _, cum, last = chunk_decays(dt[...], dt_bias[...], a_log[...])
    lane = lax.broadcasted_iota(jnp.int32, (CHUNK, LANES), 1)
    row = lax.broadcasted_iota(jnp.int32, (CHUNK, LANES), 0)
    bias = jnp.where(row >= lane, 0.0, -1e30)
    heads = lane < HEADS
    stacked = jnp.concatenate(
        [
            three_parts(delta),
            three_parts(jnp.where(heads, jnp.exp(cum), 0.0)),
            three_parts(jnp.where(heads, jnp.exp(last - cum), 0.0)),
        ],
        axis=0,
    )
    cum_t = cum.T
    inputs_b = mixed[:, INNER : INNER + NSTATE]
    readout = mixed[:, INNER + NSTATE :]
    affinity = dot3(split(readout), split(inputs_b), NT)
    readout_parts = split(readout)
    b_parts = split(inputs_b.T)
    low, high = pair_mask()
    squares = jnp.zeros((CHUNK, LANES), F32)
    for j in range(PAIRS):
        cols = slice(j * LANES, (j + 1) * LANES)
        wide = dot(stacked, spread[:, cols])
        values = mixed[:, cols]
        scaled = values * wide[:CHUNK]
        sh, sl = split(scaled)
        right_h = jnp.concatenate([sh * low, sh * high], axis=0)
        right_l = jnp.concatenate([sl * low, sl * high], axis=0)
        left = []
        for h in (2 * j, 2 * j + 1):
            within = jnp.exp(cum[:, h : h + 1] - cum_t[h : h + 1, :] + bias)
            left.append(split(affinity * within))
        left_h = jnp.concatenate([left[0][0], left[1][0]], axis=1)
        left_l = jnp.concatenate([left[0][1], left[1][1]], axis=1)
        both = dot(left_h, jnp.concatenate([right_h, right_l], axis=1))
        out = both[:, :LANES] + both[:, LANES:] + dot(left_l, right_h)
        carried = state[:, cols]
        carried_parts = split(carried)
        out = out + dot3(readout_parts, carried_parts) * wide[CHUNK : 2 * CHUNK]
        out = out + skip[:, cols] * values
        end = wide[2 * CHUNK - 1 : 2 * CHUNK]
        state[:, cols] = carried * end + dot3(b_parts, split(scaled * wide[2 * CHUNK :]))
        ssm[:, cols] = out
        g = gate[:, cols]
        gated = out * (g / (1.0 + jnp.exp(-g)))
        squares = squares + gated * gated
    rho = lax.rsqrt(jnp.sum(squares, axis=1, keepdims=True) * (1.0 / INNER) + NORM_EPS)
    for j in range(PAIRS):
        cols = slice(j * LANES, (j + 1) * LANES)
        g = gate[:, cols]
        gated = ssm[:, cols] * (g / (1.0 + jnp.exp(-g)))
        mixed_out[:, cols] = (gated * rho * gain[:, cols]).astype(BF16)


def scan_forward(mixed, projected, dt_bias, a_log, skip, gain, spread):
    length = mixed.shape[0]
    chunks = length // CHUNK
    whole = lambda v: pl.BlockSpec(v.shape, lambda i: (0,) * v.ndim)
    return pl.pallas_call(
        scan_forward_kernel,
        grid=(chunks,),
        out_shape=(
            shape((length, INNER), F32),
            shape((length, INNER), BF16),
            shape((chunks, NSTATE, INNER), F32),
        ),
        in_specs=[
            pl.BlockSpec((CHUNK, MIXW), lambda i: (i, 0)),
            pl.BlockSpec((CHUNK, LANES), lambda i: (i, DT_AT // LANES)),
            pl.BlockSpec((CHUNK, INNER), lambda i: (i, 0)),
        ]
        + [whole(v) for v in (dt_bias, a_log, skip, gain, spread)],
        out_specs=(
            pl.BlockSpec((CHUNK, INNER), lambda i: (i, 0)),
            pl.BlockSpec((CHUNK, INNER), lambda i: (i, 0)),
            pl.BlockSpec((1, NSTATE, INNER), lambda i: (i, 0, 0)),
        ),
        scratch_shapes=[pltpu.VMEM((NSTATE, INNER), F32)],
        compiler_params=params(),
        cost_estimate=cost(40),
    )(mixed, projected, projected, dt_bias, a_log, skip, gain, spread)


def scan_backward_kernel(
    mixed, dt, ssm, grad, states, dt_bias, a_log, skip, spread, gather,
    grad_mixed, grad_dt, sums, skip_sums, grad_state, left, right,
):
    @pl.when(pl.program_id(0) == 0)
    def _():
        grad_state[...] = jnp.zeros_like(grad_state)
        sums[...] = jnp.zeros_like(sums)
        skip_sums[...] = jnp.zeros_like(skip_sums)

    shifted, delta, rate, cum, last = chunk_decays(dt[...], dt_bias[...], a_log[...])
    lane = lax.broadcasted_iota(jnp.int32, (CHUNK, LANES), 1)
    row = lax.broadcasted_iota(jnp.int32, (CHUNK, LANES), 0)
    bias = jnp.where(lane >= row, 0.0, -1e30)
    heads = lane < HEADS
    stacked = jnp.concatenate(
        [
            three_parts(delta),
            three_parts(jnp.where(heads, jnp.exp(cum), 0.0)),
            three_parts(jnp.where(heads, jnp.exp(last - cum), 0.0)),
        ],
        axis=0,
    )
    cum_t = cum.T
    inputs_b = mixed[:, INNER : INNER + NSTATE]
    readout = mixed[:, INNER + NSTATE :]
    b_parts, c_parts = split(inputs_b), split(readout)
    c_turned = split(readout.T)
    affinity = dot3(b_parts, c_parts, NT)
    low, high = pair_mask()
    grad_affinity = jnp.zeros((CHUNK, CHUNK), F32)
    grad_b = jnp.zeros((CHUNK, NSTATE), F32)
    grad_c = jnp.zeros((CHUNK, NSTATE), F32)
    for j in range(PAIRS):
        cols = slice(j * LANES, (j + 1) * LANES)
        wide = dot(stacked, spread[:, cols])
        wide_delta, wide_cum, wide_tail = wide[:CHUNK], wide[CHUNK : 2 * CHUNK], wide[2 * CHUNK :]
        end = wide_cum[CHUNK - 1 :]
        values = mixed[:, cols]
        pulled = grad[:, cols]
        scaled = values * wide_delta
        sh, sl = split(scaled)
        ph, plow = split(pulled)
        x_h = jnp.concatenate([sh * low, sh * high], axis=0)
        x_l = jnp.concatenate([sl * low, sl * high], axis=0)
        pull = dot(jnp.concatenate([x_h, x_l], axis=1), jnp.concatenate([ph, ph], axis=1), NT)
        pull = pull + dot(x_h, plow, NT)
        kernels = []
        for k, h in enumerate((2 * j, 2 * j + 1)):
            within = jnp.exp(cum_t[h : h + 1, :] - cum[:, h : h + 1] + bias)
            kernels.append(split(affinity * within))
            grad_affinity = grad_affinity + within * pull[k * CHUNK : (k + 1) * CHUNK]
        kernel_h = jnp.concatenate([kernels[0][0], kernels[1][0]], axis=1)
        kernel_l = jnp.concatenate([kernels[0][1], kernels[1][1]], axis=1)
        right_h = jnp.concatenate([ph * low, ph * high], axis=0)
        right_l = jnp.concatenate([plow * low, plow * high], axis=0)
        both = dot(kernel_h, jnp.concatenate([right_h, right_l], axis=1))
        grad_scaled = both[:, :LANES] + both[:, LANES:] + dot(kernel_l, right_h)
        late = grad_state[:, cols]
        late_parts = split(late)
        early = states[0, :, cols]
        from_state = dot3(b_parts, late_parts) * wide_tail
        grad_scaled = grad_scaled + from_state
        pulled_cum = split(pulled * wide_cum)
        grad_c = grad_c + dot3(pulled_cum, split(early), NT)
        grad_b = grad_b + dot3(split(scaled * wide_tail), late_parts, NT)
        grad_state[:, cols] = late * end + dot3(c_turned, pulled_cum)
        grad_mixed[:, cols] = grad_scaled * wide_delta + skip[:, cols] * pulled
        skip_sums[:, cols] += jnp.sum(pulled * values, axis=0, keepdims=True)
        left[:, cols] = grad_scaled * values
        inner = pulled * (ssm[:, cols] - skip[:, cols] * values) - scaled * grad_scaled
        extra = jnp.sum(scaled * from_state, axis=0, keepdims=True) + end * jnp.sum(
            late * early, axis=0, keepdims=True
        )
        right[:, cols] = inner + jnp.where(row == CHUNK - 1, extra, 0.0)
    ga_parts = split(grad_affinity)
    grad_mixed[:, INNER : INNER + NSTATE] = grad_b + dot3(ga_parts, c_parts)
    grad_mixed[:, INNER + NSTATE :] = grad_c + dot3(split(grad_affinity.T), b_parts)

    def by_head(v):
        high = v.astype(BF16)
        rest = v - high.astype(F32)
        middle = rest.astype(BF16)
        low = (rest - middle.astype(F32)).astype(BF16)
        g = gather[...]
        return dot(high, g) + (dot(middle, g) + dot(low, g))

    direct = by_head(left[...])
    grad_cum = by_head(right[...])
    upper = (lane >= row).astype(BF16)
    after = triangle_sum(upper, grad_cum)
    grad_delta = direct + rate * after
    grad_raw = jnp.where(heads, grad_delta / (1.0 + jnp.exp(-shifted)), 0.0)
    grad_dt[...] = grad_raw.astype(BF16)
    sums[0:1, :] += jnp.sum(grad_raw, axis=0, keepdims=True)
    sums[1:2, :] += rate * jnp.sum(delta * after, axis=0, keepdims=True)


def scan_backward(mixed, projected, ssm, grad, states, dt_bias, a_log, skip, spread, gather):
    length = mixed.shape[0]
    chunks = length // CHUNK
    whole = lambda v: pl.BlockSpec(v.shape, lambda i: (0,) * v.ndim)
    back = lambda i: (chunks - 1 - i, 0)
    return pl.pallas_call(
        scan_backward_kernel,
        grid=(chunks,),
        out_shape=(
            shape((length, MIXW), F32),
            shape((length, LANES), BF16),
            shape((8, LANES), F32),
            shape((1, INNER), F32),
        ),
        in_specs=[
            pl.BlockSpec((CHUNK, MIXW), back),
            pl.BlockSpec((CHUNK, LANES), lambda i: (chunks - 1 - i, DT_AT // LANES)),
            pl.BlockSpec((CHUNK, INNER), back),
            pl.BlockSpec((CHUNK, INNER), back),
            pl.BlockSpec((1, NSTATE, INNER), lambda i: (chunks - 1 - i, 0, 0)),
        ]
        + [whole(v) for v in (dt_bias, a_log, skip, spread, gather)],
        out_specs=(
            pl.BlockSpec((CHUNK, MIXW), back),
            pl.BlockSpec((CHUNK, LANES), back),
            pl.BlockSpec((8, LANES), lambda i: (0, 0)),
            pl.BlockSpec((1, INNER), lambda i: (0, 0)),
        ),
        scratch_shapes=[pltpu.VMEM((NSTATE, INNER), F32)] + [pltpu.VMEM((CHUNK, INNER), F32)] * 2,
        compiler_params=params(),
        cost_estimate=cost(70),
    )(mixed, projected, ssm, grad, states, dt_bias, a_log, skip, spread, gather)


ROWS_AT_ONCE = 128


def conv_sum(padded, at, weight, bias):
    total = bias + padded[pl.ds(at + 8, ROWS_AT_ONCE), :] * weight[KCONV - 1 : KCONV]
    for k in range(KCONV - 1):
        shifted = padded[pl.ds(at + 8 - (KCONV - 1) + k, ROWS_AT_ONCE), :]
        total = total + shifted * weight[k : k + 1]
    return total


def conv_forward_kernel(conv_in, weight, bias, mixed, padded):
    length = conv_in.shape[0]
    padded[0:8, :] = jnp.zeros((8, LANES), F32)
    padded[8:, :] = conv_in[...]
    w, b = weight[...], bias[...]
    for at in range(0, length, ROWS_AT_ONCE):
        out = conv_sum(padded, at, w, b)
        mixed[at : at + ROWS_AT_ONCE, :] = out / (1.0 + jnp.exp(-out))


def conv_forward(projected, weight, bias):
    length = projected.shape[0]
    return pl.pallas_call(
        conv_forward_kernel,
        grid=(CONVCH // LANES,),
        out_shape=shape((length, CONVCH), F32),
        in_specs=[
            pl.BlockSpec((length, LANES), lambda i: (0, INNER // LANES + i)),
            pl.BlockSpec((KCONV, LANES), lambda i: (0, i)),
            pl.BlockSpec((1, LANES), lambda i: (0, i)),
        ],
        out_specs=pl.BlockSpec((length, LANES), lambda i: (0, i)),
        scratch_shapes=[pltpu.VMEM((length + 8, LANES), F32)],
        compiler_params=params(),
        cost_estimate=cost(12),
    )(projected, weight, bias)


def conv_backward_kernel(conv_in, grad, weight, bias, out, sums, padded, grads):
    length = conv_in.shape[0]
    padded[0:8, :] = jnp.zeros((8, LANES), F32)
    padded[8:, :] = conv_in[...]
    grads[length:, :] = jnp.zeros((8, LANES), F32)
    w, b = weight[...], bias[...]
    totals = [jnp.zeros((1, LANES), F32)] * (KCONV + 1)
    for at in range(0, length, ROWS_AT_ONCE):
        value = conv_sum(padded, at, w, b)
        sig = 1.0 / (1.0 + jnp.exp(-value))
        g = grad[at : at + ROWS_AT_ONCE, :] * (sig * (1.0 + value * (1.0 - sig)))
        grads[at : at + ROWS_AT_ONCE, :] = g
        for k in range(KCONV):
            shifted = padded[pl.ds(at + 8 - (KCONV - 1) + k, ROWS_AT_ONCE), :]
            totals[k] = totals[k] + jnp.sum(g * shifted, axis=0, keepdims=True)
        totals[KCONV] = totals[KCONV] + jnp.sum(g, axis=0, keepdims=True)
    for k in range(KCONV + 1):
        sums[k : k + 1, :] = totals[k]
    for at in range(0, length, ROWS_AT_ONCE):
        total = grads[pl.ds(at, ROWS_AT_ONCE), :] * w[KCONV - 1 : KCONV]
        for k in range(KCONV - 1):
            total = total + grads[pl.ds(at + KCONV - 1 - k, ROWS_AT_ONCE), :] * w[k : k + 1]
        out[at : at + ROWS_AT_ONCE, :] = total.astype(BF16)


def conv_backward(projected, grad_mixed, weight, bias):
    length = projected.shape[0]
    return pl.pallas_call(
        conv_backward_kernel,
        grid=(CONVCH // LANES,),
        out_shape=(shape((length, CONVCH), BF16), shape((8, CONVCH), F32)),
        in_specs=[
            pl.BlockSpec((length, LANES), lambda i: (0, INNER // LANES + i)),
            pl.BlockSpec((length, LANES), lambda i: (0, i)),
            pl.BlockSpec((KCONV, LANES), lambda i: (0, i)),
            pl.BlockSpec((1, LANES), lambda i: (0, i)),
        ],
        out_specs=(
            pl.BlockSpec((length, LANES), lambda i: (0, i)),
            pl.BlockSpec((8, LANES), lambda i: (0, i)),
        ),
        scratch_shapes=[pltpu.VMEM((length + 8, LANES), F32)] * 2,
        compiler_params=params(),
        cost_estimate=cost(15),
    )(projected, grad_mixed, weight, bias)


def middle_kernel(
    limit, mixed_out, w_out, tokens, teacher, mask, ssm, gate, gain,
    block_out, grad_result, grad_branch, grad_ssm, grad_gate, error, gain_sums,
):
    step = pl.program_id(0)

    @pl.when(step == 0)
    def _():
        error[...] = jnp.zeros_like(error)
        gain_sums[...] = jnp.zeros_like(gain_sums)

    rows = tokens.shape[0]
    result = tokens[...].astype(F32) + dot(mixed_out[...], w_out[...])
    position = step * rows + lax.broadcasted_iota(jnp.int32, (rows, 1), 0)
    valid = (position < limit[0]).astype(F32)
    weight = valid * mask[:, 0:1]
    block_out[...] = (result * valid).astype(BF16)
    misfit = result - teacher[...].astype(F32)
    pulled = 2.0 * weight * misfit
    grad_result[...] = pulled
    error[...] += jnp.sum(0.5 * pulled * misfit, axis=0, keepdims=True)
    low = pulled.astype(BF16)
    grad_branch[...] = low
    grad_mixed = dot(low, w_out[...], NT)
    g = gate[...]
    sig = 1.0 / (1.0 + jnp.exp(-g))
    act = g * sig
    inner = ssm[...]
    gated = inner * act
    rho = lax.rsqrt(jnp.mean(gated * gated, axis=1, keepdims=True) + NORM_EPS)
    unit = gated * rho
    gain_sums[...] += jnp.sum(unit * grad_mixed, axis=0, keepdims=True)
    grad_unit = grad_mixed * gain[...]
    share = jnp.mean(grad_unit * unit, axis=1, keepdims=True)
    grad_gated = rho * (grad_unit - unit * share)
    grad_ssm[...] = grad_gated * act
    grad_gate[...] = (grad_gated * inner * (sig * (1.0 + g * (1.0 - sig)))).astype(BF16)


def middle(limit, mixed_out, w_out, tokens, teacher, mask, ssm, projected, gain):
    length = tokens.shape[0]
    rows = 128
    by_row = lambda width: pl.BlockSpec((rows, width), lambda i: (i, 0))
    whole = lambda v: pl.BlockSpec(v.shape, lambda i: (0,) * v.ndim)
    return pl.pallas_call(
        middle_kernel,
        grid=(length // rows,),
        out_shape=(
            shape((length, D), BF16),
            shape((length, D), F32),
            shape((length, D), BF16),
            shape((length, INNER), F32),
            shape((length, INNER), BF16),
            shape((1, D), F32),
            shape((1, INNER), F32),
        ),
        in_specs=[
            SMEM,
            by_row(INNER),
            whole(w_out),
            by_row(D),
            by_row(D),
            by_row(LANES),
            by_row(INNER),
            by_row(INNER),
            whole(gain),
        ],
        out_specs=(
            by_row(D),
            by_row(D),
            by_row(D),
            by_row(INNER),
            by_row(INNER),
            pl.BlockSpec((1, D), lambda i: (0, 0)),
            pl.BlockSpec((1, INNER), lambda i: (0, 0)),
        ),
        compiler_params=params(),
        cost_estimate=cost(25),
    )(limit, mixed_out, w_out, tokens, teacher, mask, ssm, projected, gain)


def body(tokens, teacher, lengths, loss_mask, owners, master, first_moment, second_moment):
    capacity = master.shape[0]
    dp, fsdp = lax.axis_size("dp"), lax.axis_size("fsdp")
    devices = dp * fsdp
    me = lax.axis_index(AXES).astype(jnp.int32)
    order_a, order_b = step_orders(dp, fsdp)
    plan = make_plan(owners, capacity, devices, me)
    n0, n1 = plan["slots"]
    na = (n0 + 1) // 2
    nb = n0 - na

    sent = send_blocks(plan["send_rows"], master)
    at_home = lax.all_to_all(sent, AXES, 0, 0, tiled=True)
    mine = pick_blocks(jnp.concatenate(plan["received"]), at_home)
    parts_a = gather_steps(mine[:na], order_a)
    parts_b = gather_steps(mine[na:n0], order_b)
    parts_a, parts_b, mine1 = lax.optimization_barrier((parts_a, parts_b, mine[n0:]))
    held1 = lax.all_gather(mine1, AXES, axis=0, tiled=True)
    relative = plan["home"] ^ me
    place_a, place_b = place_of(relative, order_a), place_of(relative, order_b)
    slot = plan["slot"]
    table = jnp.where(slot < na, place_a * na + slot, devices * na + place_b * nb + slot - na)
    table0 = jnp.concatenate([table[:MID0], table[MID1:]])
    table1 = (plan["home"] * n1 + slot)[MID0:MID1]
    input_weight, head, tail, vec = unpack_in(table0, parts_a + parts_b)
    output_weight = unpack_out(table1, held1, head, tail)
    vec = vec.reshape(-1)
    vectors, at = [], 0
    for size in (CONVCH * KCONV, CONVCH, HEADS, HEADS, HEADS, D, INNER):
        vectors.append(vec[at : at + size])
        at += size
    conv_weight = vectors[0].reshape(CONVCH, KCONV)
    conv_bias, dt_bias, a_log, skip_gain, norm_gain, gate_gain = vectors[1:]

    pad_heads = lambda v: jnp.pad(v, (0, LANES - HEADS))[None]
    dt_bias, a_log = pad_heads(dt_bias), pad_heads(a_log)
    conv_weight, conv_bias, gate_gain = conv_weight.T, conv_bias[None], gate_gain[None]
    skip = jnp.repeat(skip_gain, HEADDIM)[None]
    spread, gather = heads_spread(), heads_gather()

    inputs, target = tokens[0], teacher[0]
    mask = jnp.broadcast_to(loss_mask[0].astype(F32)[:, None], (inputs.shape[0], LANES))
    wide_in = inputs.astype(F32)
    inverse = lax.rsqrt(jnp.mean(wide_in * wide_in, axis=-1, keepdims=True) + NORM_EPS)
    normed = wide_in * inverse
    hidden = (normed * norm_gain).astype(BF16)
    projected = dot(hidden, input_weight)
    mixed = conv_forward(projected, conv_weight, conv_bias)
    ssm, mixed_out, states = scan_forward(mixed, projected, dt_bias, a_log, skip, gate_gain, spread)
    block_out, grad_result, grad_branch, grad_ssm, grad_gate_raw, errors, grad_gate = middle(
        lengths, mixed_out, output_weight, inputs, target, mask, ssm, projected, gate_gain
    )
    position = jnp.arange(inputs.shape[0], dtype=jnp.int32)
    counted = jnp.sum(jnp.where(position < lengths[0], loss_mask[0], 0)).astype(F32)
    local = jnp.concatenate([errors.reshape(-1, LANES), jnp.broadcast_to(counted, (2, LANES))])
    grad_weight_out = dot(mixed_out, grad_branch, (((0,), (0,)), ((), ())))
    half_a, half_b = devices * na // 2, devices * nb // 2
    packed1, head, tail = pack_out(
        (plan["home"] * (n1 + 1) + slot)[MID0:MID1], grad_weight_out, local, devices, n1 + 1
    )
    grad_ssm, packed1 = lax.optimization_barrier((grad_ssm, packed1))
    sum1 = lax.psum_scatter(packed1, AXES, scatter_dimension=0, tiled=True)
    grad_mixed, grad_dt, sums, skip_sums = scan_backward(
        mixed, projected, ssm, grad_ssm, states, dt_bias, a_log, skip, spread, gather
    )
    grad_conv, conv_sums = conv_backward(projected, grad_mixed, conv_weight, conv_bias)
    grad_low = jnp.concatenate([grad_gate_raw, grad_conv, grad_dt], axis=1)
    grad_weight_in = dot(hidden, grad_low, (((0,), (0,)), ((), ())))
    keep_a, send_a, keep_b, send_b = pack_in(
        table0, grad_weight_in, head, (half_a, half_a, half_b, half_b)
    )
    grad_hidden = dot(grad_low, input_weight, NT)
    grad_norm = jnp.sum(grad_hidden * normed, axis=0)
    grad_normed = grad_hidden * norm_gain
    input_grad = grad_result + inverse * (
        grad_normed - normed * jnp.mean(grad_normed * normed, axis=-1, keepdims=True)
    )
    grad_vec = jnp.concatenate(
        [
            conv_sums[:KCONV].T.reshape(-1),
            conv_sums[KCONV],
            sums[0, :HEADS],
            sums[1, :HEADS],
            jnp.sum(skip_sums.reshape(HEADS, HEADDIM), axis=1),
            grad_norm,
            grad_gate[0],
            jnp.zeros((NBLK * PBLOCK - PTOT,), F32),
        ]
    ).reshape(VEC_ROWS, LANES)
    grad_vec = jnp.concatenate([tail, grad_vec]).reshape(NBLK - MID1, BROWS, LANES)
    sum_a = keep_a + exchange(send_a, order_a[0])
    sum_b = keep_b + exchange(send_b, order_b[0])
    sum_a = reduce_step(sum_a, order_a[1])
    sum_b = reduce_step(sum_b, order_b[1])
    back1 = pick_blocks(plan["back"][1], sum1)
    got1 = lax.all_to_all(back1, AXES, 0, 0, tiled=True)
    for step in order_a[:2]:
        grad_vec = grad_vec + exchange(grad_vec, step)
    sum_a, sum_b, grad_vec, got1, input_grad = lax.optimization_barrier(
        (sum_a, sum_b, grad_vec, got1, input_grad)
    )
    for step_a, step_b in zip(order_a[2:], order_b[2:]):
        sum_a, grad_vec = reduce_step(sum_a, step_a, grad_vec)
        sum_b = reduce_step(sum_b, step_b)
    back0 = pick_blocks(plan["back"][0], jnp.concatenate([sum_a, sum_b], axis=0))
    got0 = lax.all_to_all(back0, AXES, 0, 0, tiled=True)
    error_sum = jnp.sum(sum1[n1, : D // LANES])
    divisor = sum1[n1, D // LANES, 0] * D
    new_first, new_second, new_master = adam(
        plan["row_from"],
        divisor,
        got0,
        got1,
        grad_vec,
        plan["row_block"],
        plan["row_used"],
        master,
        first_moment,
        second_moment,
    )
    mean_loss = error_sum / divisor
    return (block_out[None], input_grad[None], mean_loss, new_first, new_second, new_master)


def solution(mesh):
    return jax.shard_map(
        body,
        mesh=mesh,
        in_specs=(
            P(AXES, None, None),
            P(AXES, None, None),
            P(AXES),
            P(AXES, None),
            P(),
            P(AXES, None),
            P(AXES, None),
            P(AXES, None),
        ),
        out_specs=(
            P(AXES, None, None),
            P(AXES, None, None),
            P(),
            P(AXES, None),
            P(AXES, None),
            P(AXES, None),
        ),
        check_vma=False,
    )
```

```python
from functools import partial

import jax
import jax.numpy as jnp
from jax import lax
from jax.experimental import pallas as pl
from jax.experimental.pallas import tpu as pltpu
from jax.sharding import PartitionSpec as P

D = 768
INNER = 1536
NSTATE = 128
HEADDIM = 64
KCONV = 4
SCAN_LEN = 256
PBLOCK = 4096
STEP = 10
HEADS = 24
CONVCH = 1792
PROJ = 3352
PTOT = 3765320
NBLK = 920

LANES = 128
BROWS = PBLOCK // LANES
END_IN = D * PROJ
END_OUT = END_IN + INNER * D
MID0 = -(-END_IN // PBLOCK)
MID1 = END_OUT // PBLOCK
N0 = MID0 + NBLK - MID1
N1 = MID1 - MID0
F0_ROWS = N0 * BROWS
IN_ROWS = END_IN // LANES
HEAD_ROWS = MID0 * BROWS - IN_ROWS
TAIL_ROWS = (END_OUT - MID1 * PBLOCK) // LANES
OUT_ROWS = INNER * D // LANES
VEC_ROWS = (NBLK - MID1) * BROWS - TAIL_ROWS
VEC_AT = MID0 * BROWS + TAIL_ROWS
GROUP = 16
GROUPS = D // GROUP
GROUP_ROWS = GROUP * PROJ // LANES
COL_TILES = -(-PROJ // LANES)
WIDE = COL_TILES * LANES
OUT_TILES = D // LANES

NORM_EPS = 1e-05
ADAM_EPS = 1e-08
BETA_ONE = 0.9
BETA_TWO = 0.999
MATRIX_RATE = 0.03
VECTOR_RATE = 0.2
WEIGHT_DECAY = 0.1
PRECISE = lax.Precision.HIGHEST
AXES = ("dp", "fsdp")
VMEM_LIMIT = 60 * 1024 * 1024


def bits_of(count):
    return count.bit_length() - 1


def step_orders(dp, fsdp):
    wide = [("dp", i) for i in range(bits_of(dp))]
    narrow = [("fsdp", i) for i in range(bits_of(fsdp))]
    first = wide[:2] + narrow + wide[2:]
    second = wide[:1] + narrow + wide[1:]
    return first, second


def exchange(values, step):
    axis, bit = step
    size = lax.axis_size(axis)
    return lax.ppermute(values, axis, [(i, i ^ (1 << bit)) for i in range(size)])


def place_of(relative, order):
    shift_of = {"dp": bits_of(lax.axis_size("fsdp")), "fsdp": 0}
    place = jnp.zeros_like(relative)
    for axis, bit in order:
        place = place * 2 + ((relative >> (shift_of[axis] + bit)) & 1)
    return place


def make_plan(owners, capacity, devices, me):
    block = jnp.arange(NBLK, dtype=jnp.int32)
    mid = (block >= MID0) & (block < MID1)
    same = mid[:, None] == mid[None, :]
    before = (owners[None, :] < owners[:, None]) | (
        (owners[None, :] == owners[:, None]) & (block[None, :] < block[:, None])
    )
    order_in_class = jnp.sum((same & before).astype(jnp.int32), axis=1)
    home, slot = order_in_class % devices, order_in_class // devices
    device = jnp.arange(devices, dtype=jnp.int32)
    below = owners[None, :] < device[:, None]
    owned = owners[None, :] == device[:, None]

    def total(mask):
        return jnp.sum(mask.astype(jnp.int32), axis=1)

    start = (total(below & ~mid[None, :]), total(below & mid[None, :]))
    count = (total(owned & ~mid[None, :]), total(owned & mid[None, :]))
    early = total(owned & (block < MID0)[None, :])
    pair = 2 + max(capacity - 2, 0) // devices

    def pick(vector, index):
        return jnp.sum(jnp.where(device == index, vector, 0))

    my_start = [pick(v, me) for v in start]
    my_count = [pick(v, me) for v in count]
    my_early = pick(early, me)

    lane = jnp.arange(pair, dtype=jnp.int32)
    k0 = (device[:, None] - my_start[0]) % devices + lane[None, :] * devices
    k1 = (device[:, None] - my_start[1]) % devices + (pair - 1 - lane)[None, :] * devices
    row0 = jnp.where(k0 < my_early, k0, k0 + my_count[1])
    send_rows = jnp.where(
        k0 < my_count[0], row0, jnp.where(k1 < my_count[1], my_early + k1, 0)
    ).reshape(-1)

    slots = (-(-N0 // devices), -(-N1 // devices))

    def received(kind):
        wanted = me + devices * jnp.arange(slots[kind], dtype=jnp.int32)
        ends = start[kind] + count[kind]
        owner = jnp.sum((ends[None, :] <= wanted[:, None]).astype(jnp.int32), axis=1)
        owner = jnp.minimum(owner, devices - 1)
        base = jnp.sum(jnp.where(device[None, :] == owner[:, None], start[kind][None, :], 0), axis=1)
        turn = jnp.clip((wanted - base) // devices, 0, pair - 1)
        return owner * pair + (turn if kind == 0 else pair - 1 - turn)

    turns = -(-capacity // devices)

    def back_to_owners(kind):
        lane = jnp.arange(turns, dtype=jnp.int32)
        k = (me - start[kind])[:, None] % devices + lane[None, :] * devices
        at = (start[kind][:, None] + k) // devices
        return jnp.where(k < count[kind][:, None], at, 0).reshape(-1)

    row = jnp.arange(capacity, dtype=jnp.int32)
    is_mid = (row >= my_early) & (row < my_early + my_count[1])
    k = jnp.where(is_mid, row - my_early, jnp.where(row < my_early, row, row - my_count[1]))
    first = jnp.where(is_mid, my_start[1], my_start[0])
    turn = k // devices
    row_from = ((first + k) % devices) * turns + turn + jnp.where(is_mid, devices * turns, 0)
    row_used = row < my_count[0] + my_count[1]
    mine = (owners == me)[None, :]
    rank = jnp.sum((mine & (block[None, :] < block[:, None])).astype(jnp.int32), axis=1)
    row_block = jnp.sum(
        jnp.where(mine & (rank[None, :] == row[:, None]), block[None, :], 0), axis=1
    )
    row_from = jnp.where(row_block >= MID1, 2 * devices * turns + row_block - MID1, row_from)
    row_from = jnp.where(row_used, row_from, 0)
    return dict(
        home=home, slot=slot, slots=slots, pair=pair, send_rows=send_rows,
        received=(received(0), received(1)), back=(back_to_owners(0), back_to_owners(1)), row_from=row_from,
        row_used=row_used, row_block=row_block,
    )


ANY = pl.BlockSpec(memory_space=pl.ANY)
VMEM = pl.BlockSpec(memory_space=pltpu.VMEM)
SMEM = pl.BlockSpec(memory_space=pltpu.SMEM)


def params(**extra):
    return pltpu.CompilerParams(vmem_limit_bytes=VMEM_LIMIT, **extra)


def shape(dims, dtype):
    return jax.ShapeDtypeStruct(dims, dtype)


def send_kernel(table, master, out, flat):
    capacity = master.shape[0]
    for j in range(BROWS):
        flat[pl.ds(j, capacity, stride=BROWS), :] = master[:, j * LANES : (j + 1) * LANES]

    def step(i, carry):
        out[i] = flat[pl.ds(pl.multiple_of(table[i] * BROWS, BROWS), BROWS), :].astype(out.dtype)
        return carry

    lax.fori_loop(0, out.shape[0], step, 0)


def send_blocks(table, master):
    return pl.pallas_call(
        send_kernel,
        out_shape=shape((table.shape[0], BROWS, LANES), jnp.bfloat16),
        in_specs=[SMEM, VMEM],
        out_specs=VMEM,
        scratch_shapes=[pltpu.VMEM((master.shape[0] * BROWS, LANES), jnp.float32)],
        compiler_params=params(),
    )(table, master)


def pick_kernel(table, source, out):
    def step(i, carry):
        out[i] = source[table[i]]
        return carry

    lax.fori_loop(0, out.shape[0], step, 0)


def pick_blocks(table, source):
    return pl.pallas_call(
        pick_kernel,
        out_shape=shape((table.shape[0],) + source.shape[1:], source.dtype),
        in_specs=[SMEM, VMEM],
        out_specs=VMEM,
        compiler_params=params(),
    )(table, source)


def row_start(rho):
    return (PROJ * rho) // LANES, (PROJ * rho) % LANES


def copy_all(pairs, sem):
    copies = [pltpu.make_async_copy(a, b, sem.at[i]) for i, (a, b) in enumerate(pairs)]
    for c in copies:
        c.start()
    for c in copies:
        c.wait()


def spread_blocks(table, held, flat, count, first_row):
    def one(i):
        at = pl.multiple_of(first_row + i * BROWS, 16)
        flat[pl.ds(at, BROWS), :] = held[table[i]].astype(jnp.float32)

    def step(i, carry):
        for u in range(4):
            one(i * 4 + u)
        return carry

    lax.fori_loop(0, count // 4, step, 0)
    for i in range(count // 4 * 4, count):
        one(i)


def unpack_in_kernel(table, *refs):
    parts, (w_in, head, tail, vec, held, flat, tile, sem) = refs[:-8], refs[-8:]
    pairs, at = [], 0
    for part in parts:
        pairs.append((part, held.at[pl.ds(at, part.shape[0])]))
        at += part.shape[0]
    copy_all(pairs, sem)
    spread_blocks(table, held, flat, N0, 0)
    head[...] = flat[IN_ROWS : IN_ROWS + HEAD_ROWS, :]
    tail[...] = flat[MID0 * BROWS : MID0 * BROWS + TAIL_ROWS, :]
    vec[...] = flat[VEC_AT:F0_ROWS, :]
    lane = lax.broadcasted_iota(jnp.int32, (GROUPS, LANES), 1)

    def columns(j):
        for rho in range(GROUP):
            c, s = row_start(rho)
            x = flat[pl.ds(c + j, GROUPS, stride=GROUP_ROWS), :]
            if s:
                y = flat[pl.ds(c + j + 1, GROUPS, stride=GROUP_ROWS), :]
                x = jnp.where(
                    lane < LANES - s,
                    pltpu.roll(x, LANES - s, 1),
                    pltpu.roll(y, LANES - s, 1),
                )
            tile[pl.ds(rho, GROUPS, stride=GROUP), :] = x

    def step(j, carry):
        columns(j)
        w_in[:, pl.ds(pl.multiple_of(j * LANES, LANES), LANES)] = tile[...].astype(jnp.bfloat16)
        return carry

    lax.fori_loop(0, COL_TILES - 1, step, 0)
    columns(COL_TILES - 1)
    last = (COL_TILES - 1) * LANES
    inside = lax.broadcasted_iota(jnp.int32, (D, LANES), 1) < PROJ - last
    w_in[:, last:] = jnp.where(inside, tile[...], 0.0).astype(jnp.bfloat16)


def unpack_in(table, parts):
    held = sum(part.shape[0] for part in parts)
    return pl.pallas_call(
        unpack_in_kernel,
        out_shape=(
            shape((D, WIDE), jnp.bfloat16),
            shape((HEAD_ROWS, LANES), jnp.float32),
            shape((TAIL_ROWS, LANES), jnp.float32),
            shape((VEC_ROWS, LANES), jnp.float32),
        ),
        in_specs=[SMEM] + [ANY] * len(parts),
        out_specs=(VMEM,) * 4,
        scratch_shapes=[
            pltpu.VMEM((held, BROWS, LANES), jnp.bfloat16),
            pltpu.VMEM((F0_ROWS, LANES), jnp.float32),
            pltpu.VMEM((D, LANES), jnp.float32),
            pltpu.SemaphoreType.DMA((len(parts),)),
        ],
        compiler_params=params(),
    )(table, *parts)


def unpack_out_kernel(table, held, head, tail, w_out, flat):
    flat[0:HEAD_ROWS, :] = head[...]
    flat[OUT_ROWS - TAIL_ROWS : OUT_ROWS, :] = tail[...]
    spread_blocks(table, held, flat, N1, HEAD_ROWS)
    rows = 128

    def step(i, carry):
        at = pl.multiple_of(i * rows, rows)
        for j in range(OUT_TILES):
            x = flat[pl.ds(at * OUT_TILES + j, rows, stride=OUT_TILES), :]
            w_out[pl.ds(at, rows), j * LANES : (j + 1) * LANES] = x.astype(jnp.bfloat16)
        return carry

    lax.fori_loop(0, INNER // rows, step, 0)


def unpack_out(table, held, head, tail):
    return pl.pallas_call(
        unpack_out_kernel,
        out_shape=shape((INNER, D), jnp.bfloat16),
        in_specs=[SMEM] + [VMEM] * 3,
        out_specs=VMEM,
        scratch_shapes=[pltpu.VMEM((OUT_ROWS, LANES), jnp.float32)],
        compiler_params=params(),
    )(table, held, head, tail)


def permute_blocks(table, flat, count, first_row, staged):
    def one(i):
        at = pl.multiple_of(first_row + i * BROWS, 16)
        staged[table[i]] = flat[pl.ds(at, BROWS), :]

    def step(i, carry):
        for u in range(4):
            one(i * 4 + u)
        return carry

    lax.fori_loop(0, count // 4, step, 0)
    for i in range(count // 4 * 4, count):
        one(i)


def pack_in_kernel(table, hidden, grad, head, *refs):
    outs, (turned, tiles, flat, staged, sem) = refs[:-5], refs[-5:]
    turned[...] = hidden[...].T
    lane = lax.broadcasted_iota(jnp.int32, (GROUPS, LANES), 1)

    def product(p, count):
        at = p * 2 * LANES
        at = at if isinstance(at, int) else pl.multiple_of(at, 2 * LANES)
        return jnp.dot(
            turned[...], grad[:, pl.ds(at, count * LANES)], preferred_element_type=jnp.float32
        )

    def put(p, value):
        for k in range(value.shape[1] // LANES):
            at = (p * 2 + k) * D
            at = at if isinstance(at, int) else pl.multiple_of(at, D)
            tiles[pl.ds(at, D), :] = value[:, k * LANES : (k + 1) * LANES]

    def load(rho, j):
        return tiles[pl.ds(j * D + rho, GROUPS, stride=GROUP), :]

    def whole(rho, i):
        first = -(-PROJ * rho // LANES)
        col0 = first * LANES - PROJ * rho
        x = load(rho, i)
        if col0:
            x = jnp.where(
                lane < LANES - col0,
                pltpu.roll(x, LANES - col0, 1),
                pltpu.roll(load(rho, i + 1), LANES - col0, 1),
            )
        flat[pl.ds(first + i, GROUPS, stride=GROUP_ROWS), :] = x

    put(0, product(0, 2))
    put(1, product(1, 2))
    pairs = COL_TILES // 2

    def step(p, carry):
        for i in range(2):
            for rho in range(GROUP):
                whole(rho, p * 2 + i)
        put(p + 2, product(p + 2, 2))
        return carry

    lax.fori_loop(0, pairs - 2, step, 0)
    put(pairs, product(pairs, COL_TILES % 2))
    for rho in range(GROUP):
        first = -(-PROJ * rho // LANES)
        col0 = first * LANES - PROJ * rho
        full = (PROJ - col0) // LANES
        for i in range((pairs - 2) * 2, full):
            whole(rho, i)
        left = PROJ - col0 - full * LANES
        if left:
            begin = col0 + full * LANES
            j, s = begin // LANES, begin % LANES
            x = pltpu.roll(load(rho, j), LANES - s, 1) if s else load(rho, j)
            if s + left > LANES:
                x = jnp.where(lane < LANES - s, x, pltpu.roll(load(rho, j + 1), LANES - s, 1))
            y = pltpu.roll(load(rho + 1, 0), left, 1)
            flat[pl.ds(first + full, GROUPS, stride=GROUP_ROWS), :] = jnp.where(lane < left, x, y)
    flat[IN_ROWS : IN_ROWS + HEAD_ROWS, :] = head[...]
    permute_blocks(table, flat, MID0, 0, staged)
    copies, at = [], 0
    for out in outs:
        copies.append((staged.at[pl.ds(at, out.shape[0])], out))
        at += out.shape[0]
    copy_all(copies, sem)


def pack_in(table, hidden, grad, head, sizes):
    return pl.pallas_call(
        pack_in_kernel,
        out_shape=tuple(shape((n, BROWS, LANES), jnp.float32) for n in sizes),
        in_specs=[SMEM, VMEM, VMEM, VMEM],
        out_specs=(ANY,) * len(sizes),
        scratch_shapes=[
            pltpu.VMEM((D, hidden.shape[0]), jnp.bfloat16),
            pltpu.VMEM((COL_TILES * D, LANES), jnp.float32),
            pltpu.VMEM((MID0 * BROWS, LANES), jnp.float32),
            pltpu.VMEM((sum(sizes), BROWS, LANES), jnp.float32),
            pltpu.SemaphoreType.DMA((len(sizes),)),
        ],
        compiler_params=params(),
    )(table, hidden, grad, head)


def pack_out_kernel(table, grad, local, out, head, tail, flat, *, slots):
    rows = 128

    def step(i, carry):
        at = pl.multiple_of(i * rows, rows)
        for j in range(OUT_TILES):
            flat[pl.ds(at * OUT_TILES + j, rows, stride=OUT_TILES), :] = grad[
                pl.ds(at, rows), j * LANES : (j + 1) * LANES
            ]
        return carry

    lax.fori_loop(0, INNER // rows, step, 0)
    head[...] = flat[0:HEAD_ROWS, :]
    tail[...] = flat[OUT_ROWS - TAIL_ROWS : OUT_ROWS, :]
    permute_blocks(table, flat, N1, HEAD_ROWS, out)

    def add_local(i, carry):
        out[i * slots + slots - 1, 0:8, :] = local[...]
        return carry

    lax.fori_loop(0, out.shape[0] // slots, add_local, 0)


def pack_out(table, grad, local, devices, slots):
    return pl.pallas_call(
        partial(pack_out_kernel, slots=slots),
        out_shape=(
            shape((devices * slots, BROWS, LANES), jnp.float32),
            shape((HEAD_ROWS, LANES), jnp.float32),
            shape((TAIL_ROWS, LANES), jnp.float32),
        ),
        in_specs=[SMEM, VMEM, VMEM],
        out_specs=(VMEM,) * 3,
        scratch_shapes=[pltpu.VMEM((OUT_ROWS, LANES), jnp.float32)],
        compiler_params=params(),
    )(table, grad, local)


def adam_kernel(table, scale, got0, got1, got2, limit, used, master, first, second, o_first, o_second, o_master, flat):
    capacity = master.shape[0]

    def step(i, carry):
        at, low = table[i], 0
        rows = pl.ds(pl.multiple_of(i * BROWS, BROWS), BROWS)
        for got in (got0, got1, got2):
            high = low + got.shape[0]

            @pl.when((at >= low) & (at < high))
            def _(got=got, low=low):
                flat[rows, :] = got[at - low]

            low = high
        return carry

    lax.fori_loop(0, capacity, step, 0)
    lane = lax.broadcasted_iota(jnp.int32, (capacity, LANES), 1)
    divisor = scale[0]
    for j in range(BROWS):
        cols = slice(j * LANES, (j + 1) * LANES)
        grad = jnp.where(used[...] > 0, flat[pl.ds(j, capacity, stride=BROWS), :], 0.0) / divisor
        matrix = lane + j * LANES < limit[...]
        weights = master[:, cols]
        new_first = BETA_ONE * first[:, cols] + (1.0 - BETA_ONE) * grad
        new_second = BETA_TWO * second[:, cols] + (1.0 - BETA_TWO) * grad * grad
        normal = (
            new_first
            / (1.0 - BETA_ONE**STEP)
            / (jnp.sqrt(new_second / (1.0 - BETA_TWO**STEP)) + ADAM_EPS)
        )
        rate = jnp.where(matrix, MATRIX_RATE, VECTOR_RATE)
        decay = jnp.where(matrix, WEIGHT_DECAY, 0.0)
        o_first[:, cols] = new_first
        o_second[:, cols] = new_second
        o_master[:, cols] = weights - rate * (normal + decay * weights)


def adam(table, divisor, got0, got1, got2, row_block, row_used, master, first, second):
    capacity = master.shape[0]
    limit = jnp.broadcast_to((END_OUT - row_block * PBLOCK)[:, None], (capacity, LANES))
    used = jnp.broadcast_to(row_used.astype(jnp.int32)[:, None], (capacity, LANES))
    return pl.pallas_call(
        adam_kernel,
        out_shape=(shape(master.shape, jnp.float32),) * 3,
        in_specs=[SMEM, SMEM] + [VMEM] * 8,
        out_specs=(VMEM,) * 3,
        scratch_shapes=[pltpu.VMEM((capacity * BROWS, LANES), jnp.float32)],
        compiler_params=params(),
    )(table, divisor.reshape(1), got0, got1, got2, limit, used, master, first, second)


def gather_steps(values, order):
    for step in order[:0:-1]:
        values = jnp.concatenate([values, exchange(values, step)], axis=0)
    return values, exchange(values, order[0])


def reduce_step(values, step, extra=None):
    half = values.shape[0] // 2
    if extra is None:
        return values[:half] + exchange(values[half:], step)
    got = exchange(jnp.concatenate([values[half:], extra]), step)
    return values[:half] + got[:half], extra + got[half:]


CHUNK = 128
PAIRS = HEADS // 2
MIXW = INNER + 2 * NSTATE
DT_AT = INNER + CONVCH
F32 = jnp.float32
BF16 = jnp.bfloat16
NN = (((1,), (0,)), ((), ()))
NT = (((1,), (1,)), ((), ()))


def cost(microseconds):
    return pl.CostEstimate(
        flops=int(microseconds * 1e9), bytes_accessed=int(microseconds * 3e6), transcendentals=0
    )


def dot(a, b, dims=NN):
    return lax.dot_general(a, b, dims, preferred_element_type=F32)


def split(v):
    high = v.astype(BF16)
    return high, (v - high.astype(F32)).astype(BF16)


def dot3(a, b, dims=NN):
    ah, al = a
    bh, bl = b
    return dot(ah, bh, dims) + (dot(ah, bl, dims) + dot(al, bh, dims))


def heads_gather():
    row = lax.broadcasted_iota(jnp.int32, (INNER, LANES), 0)
    col = lax.broadcasted_iota(jnp.int32, (INNER, LANES), 1)
    return (row // HEADDIM == col).astype(BF16)


def three_parts(v):
    high = v.astype(BF16).astype(F32)
    rest = v - high
    middle = rest.astype(BF16).astype(F32)
    low = rest - middle
    return (high + pltpu.roll(middle, 32, 1) + pltpu.roll(low, 64, 1)).astype(BF16)


def triangle_sum(tri, v):
    parts = dot(tri, three_parts(v))
    lane = lax.broadcasted_iota(jnp.int32, parts.shape, 1)
    total = parts + pltpu.roll(parts, LANES - 32, 1) + pltpu.roll(parts, LANES - 64, 1)
    return jnp.where(lane < HEADS, total, 0.0)


def chunk_decays(dt, dt_bias, a_log):
    lane = lax.broadcasted_iota(jnp.int32, (CHUNK, LANES), 1)
    row = lax.broadcasted_iota(jnp.int32, (CHUNK, LANES), 0)
    shifted = dt + dt_bias
    delta = jnp.where(
        lane < HEADS, jnp.maximum(shifted, 0.0) + jnp.log1p(jnp.exp(-jnp.abs(shifted))), 0.0
    )
    rate = -jnp.exp(a_log)
    lower = (row >= lane).astype(BF16)
    cum = triangle_sum(lower, delta * rate)
    last = cum[CHUNK - 1 : CHUNK, :]
    return shifted, delta, rate, cum, last


def pair_mask():
    lane = lax.broadcasted_iota(jnp.int32, (CHUNK, LANES), 1)
    low = (lane < HEADDIM).astype(F32)
    return low.astype(BF16), (1.0 - low).astype(BF16)


QUADS = HEADS // 4
QWIDTH = 4 * HEADDIM


def sigmoid(v):
    return 0.5 * jnp.tanh(0.5 * v) + 0.5


def silu(v):
    return v * sigmoid(v)


def side_by_side(v):
    high, low = split(v)
    return jnp.concatenate([high, low], axis=1), high


def dot_parts(a, b):
    ahl, ah = a
    bh, bl = b
    return dot(ahl, jnp.concatenate([bh, bh], axis=0)) + dot(ah, bl)


def dot_turned(a, b):
    ah, al = a
    bh, bl = b
    both = dot(ah, jnp.concatenate([bh, bl], axis=0), NT)
    n = bh.shape[0]
    return both[:, :n] + both[:, n:] + dot(al, bh, NT)


def widen(delta, cum, quad):
    lane = lax.broadcasted_iota(jnp.int32, (CHUNK, LANES), 1)
    over = lambda v, h: jnp.broadcast_to(v[:, h : h + 1], (CHUNK, LANES))
    first = 4 * quad
    columns = [over(cum, first + k) for k in range(4)]
    rates = [over(delta, first + k) for k in range(4)]
    pair = lambda vs: jnp.concatenate(
        [jnp.where(lane < HEADDIM, vs[0], vs[1]), jnp.where(lane < HEADDIM, vs[2], vs[3])], axis=1
    )
    return pair(rates), pair(columns), columns


def pair_rows(parts, j, low, high):
    cols = slice(j * LANES, (j + 1) * LANES)
    return [jnp.concatenate([p[:, cols] * low, p[:, cols] * high], axis=0) for p in parts]


def scan_forward_kernel(
    mixed, dt, gate, dt_bias, a_log, skip, gain, ssm, mixed_out, states, state
):
    @pl.when(pl.program_id(0) == 0)
    def _():
        state[...] = jnp.zeros_like(state)

    states[0] = state[...]
    _, delta, _, cum, last = chunk_decays(dt[...], dt_bias[...], a_log[...])
    lane = lax.broadcasted_iota(jnp.int32, (CHUNK, LANES), 1)
    row = lax.broadcasted_iota(jnp.int32, (CHUNK, LANES), 0)
    bias = jnp.where(row >= lane, 0.0, -1e30)
    cum_t = cum.T
    inputs_b = mixed[:, INNER : INNER + NSTATE]
    readout = mixed[:, INNER + NSTATE :]
    affinity = dot3(split(readout), split(inputs_b), NT)
    readout_parts = side_by_side(readout)
    b_parts = side_by_side(inputs_b.T)
    low, high = pair_mask()
    squares = jnp.zeros((CHUNK, LANES), F32)
    for quad in range(QUADS):
        cols = slice(quad * QWIDTH, (quad + 1) * QWIDTH)
        wide_delta, wide_cum, columns = widen(delta, cum, quad)
        values = mixed[:, cols]
        scaled = values * wide_delta
        parts = split(scaled)
        outs = []
        for j in range(2):
            right_h, right_l = pair_rows(parts, j, low, high)
            left = []
            for k in range(2):
                h = 4 * quad + 2 * j + k
                within = jnp.exp(columns[2 * j + k] - cum_t[h : h + 1, :] + bias)
                left.append(split(affinity * within))
            left_h = jnp.concatenate([left[0][0], left[1][0]], axis=1)
            left_l = jnp.concatenate([left[0][1], left[1][1]], axis=1)
            both = dot(left_h, jnp.concatenate([right_h, right_l], axis=1))
            outs.append(both[:, :LANES] + both[:, LANES:] + dot(left_l, right_h))
        carried = state[:, cols]
        grown = jnp.exp(wide_cum)
        out = jnp.concatenate(outs, axis=1) + dot_parts(readout_parts, split(carried)) * grown
        out = out + skip[:, cols] * values
        tail = jnp.exp(wide_cum[CHUNK - 1 :] - wide_cum)
        state[:, cols] = carried * grown[CHUNK - 1 :] + dot_parts(b_parts, split(scaled * tail))
        ssm[:, cols] = out
        gated = out * silu(gate[:, cols])
        squares = squares + gated[:, :LANES] * gated[:, :LANES] + gated[:, LANES:] * gated[:, LANES:]
    rho = lax.rsqrt(jnp.sum(squares, axis=1, keepdims=True) * (1.0 / INNER) + NORM_EPS)
    for j in range(PAIRS):
        cols = slice(j * LANES, (j + 1) * LANES)
        gated = ssm[:, cols] * silu(gate[:, cols])
        mixed_out[:, cols] = (gated * rho * gain[:, cols]).astype(BF16)


def scan_forward(mixed, projected, dt_bias, a_log, skip, gain):
    length = mixed.shape[0]
    chunks = length // CHUNK
    whole = lambda v: pl.BlockSpec(v.shape, lambda i: (0,) * v.ndim)
    return pl.pallas_call(
        scan_forward_kernel,
        grid=(chunks,),
        out_shape=(
            shape((length, INNER), F32),
            shape((length, INNER), BF16),
            shape((chunks, NSTATE, INNER), F32),
        ),
        in_specs=[
            pl.BlockSpec((CHUNK, MIXW), lambda i: (i, 0)),
            pl.BlockSpec((CHUNK, LANES), lambda i: (i, DT_AT // LANES)),
            pl.BlockSpec((CHUNK, INNER), lambda i: (i, 0)),
        ]
        + [whole(v) for v in (dt_bias, a_log, skip, gain)],
        out_specs=(
            pl.BlockSpec((CHUNK, INNER), lambda i: (i, 0)),
            pl.BlockSpec((CHUNK, INNER), lambda i: (i, 0)),
            pl.BlockSpec((1, NSTATE, INNER), lambda i: (i, 0, 0)),
        ),
        scratch_shapes=[pltpu.VMEM((NSTATE, INNER), F32)],
        compiler_params=params(),
        cost_estimate=cost(40),
    )(mixed, projected, projected, dt_bias, a_log, skip, gain)


def scan_backward_kernel(
    mixed, dt, ssm, grad, states, dt_bias, a_log, skip, gather, held,
    grad_mixed, grad_dt, sums, skip_sums, grad_state, left, right,
):
    @pl.when(pl.program_id(0) == 0)
    def _():
        grad_state[...] = jnp.zeros_like(grad_state)
        sums[...] = jnp.zeros_like(sums)
        skip_sums[...] = jnp.zeros_like(skip_sums)

    shifted, delta, rate, cum, last = chunk_decays(dt[...], dt_bias[...], a_log[...])
    lane = lax.broadcasted_iota(jnp.int32, (CHUNK, LANES), 1)
    row = lax.broadcasted_iota(jnp.int32, (CHUNK, LANES), 0)
    bias = jnp.where(lane >= row, 0.0, -1e30)
    heads = lane < HEADS
    cum_t = cum.T
    inputs_b = mixed[:, INNER : INNER + NSTATE]
    readout = mixed[:, INNER + NSTATE :]
    b_parts, c_parts = split(inputs_b), split(readout)
    b_wide = side_by_side(inputs_b)
    c_turned = side_by_side(readout.T)
    affinity = dot3(b_parts, c_parts, NT)
    low, high = pair_mask()
    grad_affinity = jnp.zeros((CHUNK, CHUNK), F32)
    grad_b = jnp.zeros((CHUNK, NSTATE), F32)
    grad_c = jnp.zeros((CHUNK, NSTATE), F32)
    last_row = lax.broadcasted_iota(jnp.int32, (CHUNK, QWIDTH), 0) == CHUNK - 1
    for quad in range(QUADS):
        cols = slice(quad * QWIDTH, (quad + 1) * QWIDTH)
        wide_delta, wide_cum, columns = widen(delta, cum, quad)
        grown = jnp.exp(wide_cum)
        tail = jnp.exp(wide_cum[CHUNK - 1 :] - wide_cum)
        end = grown[CHUNK - 1 :]
        values = mixed[:, cols]
        pulled = grad[:, cols]
        scaled = values * wide_delta
        x_parts, p_parts = split(scaled), split(pulled)
        outs = []
        for j in range(2):
            half = slice(j * LANES, (j + 1) * LANES)
            xh, xl = x_parts[0][:, half], x_parts[1][:, half]
            right_h, right_l = pair_rows(p_parts, j, low, high)
            pull = dot(
                jnp.concatenate([xh, xl], axis=1),
                jnp.concatenate([right_h, right_h], axis=1),
                NT,
            ) + dot(xh, right_l, NT)
            kernels = []
            for k in range(2):
                h = 4 * quad + 2 * j + k
                within = jnp.exp(cum_t[h : h + 1, :] - columns[2 * j + k] + bias)
                kernels.append(split(affinity * within))
                grad_affinity = grad_affinity + within * pull[:, k * CHUNK : (k + 1) * CHUNK]
            kernel_h = jnp.concatenate([kernels[0][0], kernels[1][0]], axis=1)
            kernel_l = jnp.concatenate([kernels[0][1], kernels[1][1]], axis=1)
            both = dot(kernel_h, jnp.concatenate([right_h, right_l], axis=1))
            outs.append(both[:, :LANES] + both[:, LANES:] + dot(kernel_l, right_h))
        late = grad_state[:, cols]
        late_parts = split(late)
        early = states[0, :, cols]
        from_state = dot_parts(b_wide, late_parts) * tail
        grad_scaled = jnp.concatenate(outs, axis=1) + from_state
        pulled_cum = split(pulled * grown)
        grad_c = grad_c + dot_turned(pulled_cum, split(early))
        grad_b = grad_b + dot_turned(split(scaled * tail), late_parts)
        grad_state[:, cols] = late * end + dot_parts(c_turned, pulled_cum)
        grad_mixed[:, cols] = grad_scaled * wide_delta + skip[:, cols] * pulled
        skip_sums[:, cols] += jnp.sum(pulled * values, axis=0, keepdims=True)
        left[:, cols] = grad_scaled * values
        inner = pulled * (ssm[:, cols] - skip[:, cols] * values) - scaled * grad_scaled
        extra = jnp.sum(scaled * from_state, axis=0, keepdims=True) + end * jnp.sum(
            late * early, axis=0, keepdims=True
        )
        right[:, cols] = inner + jnp.where(last_row, extra, 0.0)
    ga_parts = split(grad_affinity)
    grad_mixed[:, INNER : INNER + NSTATE] = grad_b + dot3(ga_parts, c_parts)
    grad_mixed[:, INNER + NSTATE :] = grad_c + dot3(split(grad_affinity.T), b_parts)

    def by_head(v):
        high, low = split(v)
        g = gather[...]
        return dot(high, g) + dot(low, g)

    direct = by_head(left[...])
    grad_cum = by_head(right[...])
    upper = (lane >= row).astype(BF16)
    after = triangle_sum(upper, grad_cum)
    grad_delta = direct + rate * after
    grad_raw = jnp.where(heads, grad_delta * sigmoid(shifted), 0.0)
    grad_dt[...] = grad_raw.astype(BF16)
    sums[0:1, :] += jnp.sum(grad_raw, axis=0, keepdims=True)
    sums[1:2, :] += rate * jnp.sum(delta * after, axis=0, keepdims=True)


def scan_backward(mixed, projected, ssm, grad, states, dt_bias, a_log, skip, gather, held):
    length = mixed.shape[0]
    chunks = length // CHUNK
    whole = lambda v: pl.BlockSpec(v.shape, lambda i: (0,) * v.ndim)
    back = lambda i: (chunks - 1 - i, 0)
    return pl.pallas_call(
        scan_backward_kernel,
        grid=(chunks,),
        out_shape=(
            shape((length, MIXW), F32),
            shape(held.shape, BF16),
            shape((8, LANES), F32),
            shape((1, INNER), F32),
        ),
        in_specs=[
            pl.BlockSpec((CHUNK, MIXW), back),
            pl.BlockSpec((CHUNK, LANES), lambda i: (chunks - 1 - i, DT_AT // LANES)),
            pl.BlockSpec((CHUNK, INNER), back),
            pl.BlockSpec((CHUNK, INNER), back),
            pl.BlockSpec((1, NSTATE, INNER), lambda i: (chunks - 1 - i, 0, 0)),
        ]
        + [whole(v) for v in (dt_bias, a_log, skip, gather)]
        + [ANY],
        out_specs=(
            pl.BlockSpec((CHUNK, MIXW), back),
            pl.BlockSpec((CHUNK, LANES), lambda i: (chunks - 1 - i, DT_AT // LANES)),
            pl.BlockSpec((8, LANES), lambda i: (0, 0)),
            pl.BlockSpec((1, INNER), lambda i: (0, 0)),
        ),
        scratch_shapes=[pltpu.VMEM((NSTATE, INNER), F32)] + [pltpu.VMEM((CHUNK, INNER), F32)] * 2,
        compiler_params=params(),
        input_output_aliases={9: 1},
        cost_estimate=cost(35),
    )(mixed, projected, ssm, grad, states, dt_bias, a_log, skip, gather, held)


ROWS_AT_ONCE = 128
CONV_TILES = 2


def down(v, before, by):
    moved = pltpu.roll(v, by, 0)
    row = lax.broadcasted_iota(jnp.int32, (8, LANES), 0)
    top = jnp.where(row < by, pltpu.roll(before, by, 0), moved[:8])
    return jnp.concatenate([top, moved[8:]], axis=0)


def up(v, after, by):
    rows = v.shape[0]
    moved = pltpu.roll(v, rows - by, 0)
    row = lax.broadcasted_iota(jnp.int32, (8, LANES), 0)
    end = jnp.where(row < 8 - by, moved[rows - 8 :], pltpu.roll(after, 8 - by, 0))
    return jnp.concatenate([moved[: rows - 8], end], axis=0)


def conv_terms(conv_in, at, cols):
    rows = conv_in[at : at + ROWS_AT_ONCE, cols]
    before = conv_in[at - 8 : at, cols] if at else jnp.zeros((8, LANES), F32)
    return [down(rows, before, KCONV - 1 - k) for k in range(KCONV - 1)] + [rows]


def conv_sum(terms, weight, bias):
    total = bias + terms[KCONV - 1] * weight[KCONV - 1 : KCONV]
    for k in range(KCONV - 1):
        total = total + terms[k] * weight[k : k + 1]
    return total


def conv_forward_kernel(conv_in, weight, bias, mixed):
    for tile in range(CONV_TILES):
        cols = slice(tile * LANES, (tile + 1) * LANES)
        w, b = weight[:, cols], bias[:, cols]
        for at in range(0, conv_in.shape[0], ROWS_AT_ONCE):
            mixed[at : at + ROWS_AT_ONCE, cols] = silu(conv_sum(conv_terms(conv_in, at, cols), w, b))


def conv_forward(projected, weight, bias):
    length = projected.shape[0]
    width = CONV_TILES * LANES
    return pl.pallas_call(
        conv_forward_kernel,
        grid=(CONVCH // width,),
        out_shape=shape((length, CONVCH), F32),
        in_specs=[
            pl.BlockSpec((length, width), lambda i: (0, INNER // width + i)),
            pl.BlockSpec((KCONV, width), lambda i: (0, i)),
            pl.BlockSpec((1, width), lambda i: (0, i)),
        ],
        out_specs=pl.BlockSpec((length, width), lambda i: (0, i)),
        compiler_params=params(),
        cost_estimate=cost(10),
    )(projected, weight, bias)


def conv_backward_kernel(conv_in, grad, weight, bias, held, out, sums):
    length = conv_in.shape[0]
    for tile in range(CONV_TILES):
        cols = slice(tile * LANES, (tile + 1) * LANES)
        w, b = weight[:, cols], bias[:, cols]
        totals = [jnp.zeros((1, LANES), F32)] * (KCONV + 1)
        after = jnp.zeros((8, LANES), F32)
        for at in range(length - ROWS_AT_ONCE, -1, -ROWS_AT_ONCE):
            terms = conv_terms(conv_in, at, cols)
            value = conv_sum(terms, w, b)
            sig = sigmoid(value)
            g = grad[at : at + ROWS_AT_ONCE, cols] * (sig * (1.0 + value * (1.0 - sig)))
            for k in range(KCONV):
                totals[k] = totals[k] + jnp.sum(g * terms[k], axis=0, keepdims=True)
            totals[KCONV] = totals[KCONV] + jnp.sum(g, axis=0, keepdims=True)
            total = g * w[KCONV - 1 : KCONV]
            for k in range(KCONV - 1):
                total = total + up(g, after, KCONV - 1 - k) * w[k : k + 1]
            after = g[:8]
            out[at : at + ROWS_AT_ONCE, cols] = total.astype(BF16)
        for k in range(KCONV + 1):
            sums[k : k + 1, cols] = totals[k]


def conv_backward(projected, grad_mixed, weight, bias, held):
    length = projected.shape[0]
    width = CONV_TILES * LANES
    return pl.pallas_call(
        conv_backward_kernel,
        grid=(CONVCH // width,),
        out_shape=(shape(held.shape, BF16), shape((8, CONVCH), F32)),
        in_specs=[
            pl.BlockSpec((length, width), lambda i: (0, INNER // width + i)),
            pl.BlockSpec((length, width), lambda i: (0, i)),
            pl.BlockSpec((KCONV, width), lambda i: (0, i)),
            pl.BlockSpec((1, width), lambda i: (0, i)),
            ANY,
        ],
        out_specs=(
            pl.BlockSpec((length, width), lambda i: (0, INNER // width + i)),
            pl.BlockSpec((8, width), lambda i: (0, i)),
        ),
        input_output_aliases={4: 0},
        compiler_params=params(),
        cost_estimate=cost(12),
    )(projected, grad_mixed, weight, bias, held)


def middle_kernel(
    limit, mixed_out, w_out, tokens, teacher, mask, ssm, gate, gain,
    block_out, grad_result, grad_branch, grad_ssm, grad_gate, error, gain_sums,
):
    step = pl.program_id(0)

    @pl.when(step == 0)
    def _():
        error[...] = jnp.zeros_like(error)
        gain_sums[...] = jnp.zeros_like(gain_sums)

    rows = tokens.shape[0]
    result = tokens[...].astype(F32) + dot(mixed_out[...], w_out[...])
    position = step * rows + lax.broadcasted_iota(jnp.int32, (rows, 1), 0)
    valid = (position < limit[0]).astype(F32)
    weight = valid * mask[:, 0:1]
    block_out[...] = (result * valid).astype(BF16)
    misfit = result - teacher[...].astype(F32)
    pulled = 2.0 * weight * misfit
    grad_result[...] = pulled
    error[...] += jnp.sum(0.5 * pulled * misfit, axis=0, keepdims=True)
    low = pulled.astype(BF16)
    grad_branch[...] = low
    grad_mixed = dot(low, w_out[...], NT)
    g = gate[...]
    sig = sigmoid(g)
    act = g * sig
    inner = ssm[...]
    gated = inner * act
    rho = lax.rsqrt(jnp.mean(gated * gated, axis=1, keepdims=True) + NORM_EPS)
    unit = gated * rho
    gain_sums[...] += jnp.sum(unit * grad_mixed, axis=0, keepdims=True)
    grad_unit = grad_mixed * gain[...]
    share = jnp.mean(grad_unit * unit, axis=1, keepdims=True)
    grad_gated = rho * (grad_unit - unit * share)
    grad_ssm[...] = grad_gated * act
    grad_gate[...] = (grad_gated * inner * (sig * (1.0 + g * (1.0 - sig)))).astype(BF16)


def middle(limit, mixed_out, w_out, tokens, teacher, mask, ssm, projected, gain):
    length = tokens.shape[0]
    rows = 256
    by_row = lambda width: pl.BlockSpec((rows, width), lambda i: (i, 0))
    whole = lambda v: pl.BlockSpec(v.shape, lambda i: (0,) * v.ndim)
    return pl.pallas_call(
        middle_kernel,
        grid=(length // rows,),
        out_shape=(
            shape((length, D), BF16),
            shape((length, D), F32),
            shape((length, D), BF16),
            shape((length, INNER), F32),
            shape((length, WIDE), BF16),
            shape((1, D), F32),
            shape((1, INNER), F32),
        ),
        in_specs=[
            SMEM,
            by_row(INNER),
            whole(w_out),
            by_row(D),
            by_row(D),
            by_row(LANES),
            by_row(INNER),
            by_row(INNER),
            whole(gain),
        ],
        out_specs=(
            by_row(D),
            by_row(D),
            by_row(D),
            by_row(INNER),
            by_row(INNER),
            pl.BlockSpec((1, D), lambda i: (0, 0)),
            pl.BlockSpec((1, INNER), lambda i: (0, 0)),
        ),
        compiler_params=params(),
        cost_estimate=cost(25),
    )(limit, mixed_out, w_out, tokens, teacher, mask, ssm, projected, gain)


def body(tokens, teacher, lengths, loss_mask, owners, master, first_moment, second_moment):
    capacity = master.shape[0]
    dp, fsdp = lax.axis_size("dp"), lax.axis_size("fsdp")
    devices = dp * fsdp
    me = lax.axis_index(AXES).astype(jnp.int32)
    order_a, order_b = step_orders(dp, fsdp)
    plan = make_plan(owners, capacity, devices, me)
    n0, n1 = plan["slots"]
    na = (n0 + 1) // 2
    nb = n0 - na

    sent = send_blocks(plan["send_rows"], master)
    at_home = lax.all_to_all(sent, AXES, 0, 0, tiled=True)
    mine = pick_blocks(jnp.concatenate(plan["received"]), at_home)
    parts_a = gather_steps(mine[:na], order_a)
    parts_b = gather_steps(mine[na:n0], order_b)
    parts_a, parts_b, mine1 = lax.optimization_barrier((parts_a, parts_b, mine[n0:]))
    held1 = lax.all_gather(mine1, AXES, axis=0, tiled=True)
    relative = plan["home"] ^ me
    place_a, place_b = place_of(relative, order_a), place_of(relative, order_b)
    slot = plan["slot"]
    table = jnp.where(slot < na, place_a * na + slot, devices * na + place_b * nb + slot - na)
    table0 = jnp.concatenate([table[:MID0], table[MID1:]])
    table1 = (plan["home"] * n1 + slot)[MID0:MID1]
    input_weight, head, tail, vec = unpack_in(table0, parts_a + parts_b)
    output_weight = unpack_out(table1, held1, head, tail)
    vec = vec.reshape(-1)
    vectors, at = [], 0
    for size in (CONVCH * KCONV, CONVCH, HEADS, HEADS, HEADS, D, INNER):
        vectors.append(vec[at : at + size])
        at += size
    conv_weight = vectors[0].reshape(CONVCH, KCONV)
    conv_bias, dt_bias, a_log, skip_gain, norm_gain, gate_gain = vectors[1:]

    pad_heads = lambda v: jnp.pad(v, (0, LANES - HEADS))[None]
    dt_bias, a_log = pad_heads(dt_bias), pad_heads(a_log)
    conv_weight, conv_bias, gate_gain = conv_weight.T, conv_bias[None], gate_gain[None]
    skip = jnp.repeat(skip_gain, HEADDIM)[None]
    gather = heads_gather()

    inputs, target = tokens[0], teacher[0]
    mask = jnp.broadcast_to(loss_mask[0].astype(F32)[:, None], (inputs.shape[0], LANES))
    wide_in = inputs.astype(F32)
    inverse = lax.rsqrt(jnp.mean(wide_in * wide_in, axis=-1, keepdims=True) + NORM_EPS)
    normed = wide_in * inverse
    hidden = (normed * norm_gain).astype(BF16)
    projected = dot(hidden, input_weight)
    mixed = conv_forward(projected, conv_weight, conv_bias)
    ssm, mixed_out, states = scan_forward(mixed, projected, dt_bias, a_log, skip, gate_gain)
    block_out, grad_result, grad_branch, grad_ssm, grad_low, errors, grad_gate = middle(
        lengths, mixed_out, output_weight, inputs, target, mask, ssm, projected, gate_gain
    )
    position = jnp.arange(inputs.shape[0], dtype=jnp.int32)
    counted = jnp.sum(jnp.where(position < lengths[0], loss_mask[0], 0)).astype(F32)
    local = jnp.concatenate([errors.reshape(-1, LANES), jnp.broadcast_to(counted, (2, LANES))])
    grad_weight_out = dot(mixed_out, grad_branch, (((0,), (0,)), ((), ())))
    half_a, half_b = devices * na // 2, devices * nb // 2
    packed1, head, tail = pack_out(
        (plan["home"] * (n1 + 1) + slot)[MID0:MID1], grad_weight_out, local, devices, n1 + 1
    )
    grad_ssm, packed1 = lax.optimization_barrier((grad_ssm, packed1))
    sum1 = lax.psum_scatter(packed1, "dp", scatter_dimension=0, tiled=True)
    grad_mixed, grad_low, sums, skip_sums = scan_backward(
        mixed, projected, ssm, grad_ssm, states, dt_bias, a_log, skip, gather, grad_low
    )
    grad_low, conv_sums = conv_backward(projected, grad_mixed, conv_weight, conv_bias, grad_low)
    grad_low, sum1 = lax.optimization_barrier((grad_low, sum1))
    for bit in reversed(range(bits_of(fsdp))):
        half = sum1.shape[0] // 2
        upper = (lax.axis_index("fsdp") >> bit) & 1
        parts = sum1.reshape((2, half) + sum1.shape[1:])
        kept = lax.dynamic_index_in_dim(parts, upper, 0, keepdims=False)
        given = lax.dynamic_index_in_dim(parts, 1 - upper, 0, keepdims=False)
        sum1 = kept + exchange(given, ("fsdp", bit))
    keep_a, send_a, keep_b, send_b = pack_in(
        table0, hidden, grad_low, head, (half_a, half_a, half_b, half_b)
    )
    grad_hidden = dot(grad_low, input_weight, NT)
    grad_norm = jnp.sum(grad_hidden * normed, axis=0)
    grad_normed = grad_hidden * norm_gain
    input_grad = grad_result + inverse * (
        grad_normed - normed * jnp.mean(grad_normed * normed, axis=-1, keepdims=True)
    )
    grad_vec = jnp.concatenate(
        [
            conv_sums[:KCONV].T.reshape(-1),
            conv_sums[KCONV],
            sums[0, :HEADS],
            sums[1, :HEADS],
            jnp.sum(skip_sums.reshape(HEADS, HEADDIM), axis=1),
            grad_norm,
            grad_gate[0],
            jnp.zeros((NBLK * PBLOCK - PTOT,), F32),
        ]
    ).reshape(VEC_ROWS, LANES)
    grad_vec = jnp.concatenate([tail, grad_vec]).reshape(NBLK - MID1, BROWS, LANES)
    sum_a = keep_a + exchange(send_a, order_a[0])
    sum_b = keep_b + exchange(send_b, order_b[0])
    sum_a = reduce_step(sum_a, order_a[1])
    sum_b = reduce_step(sum_b, order_b[1])
    back1 = pick_blocks(plan["back"][1], sum1)
    got1 = lax.all_to_all(back1, AXES, 0, 0, tiled=True)
    for step in order_a[:2]:
        grad_vec = grad_vec + exchange(grad_vec, step)
    sum_a, sum_b, grad_vec, got1, input_grad = lax.optimization_barrier(
        (sum_a, sum_b, grad_vec, got1, input_grad)
    )
    for step_a, step_b in zip(order_a[2:], order_b[2:]):
        sum_a, grad_vec = reduce_step(sum_a, step_a, grad_vec)
        sum_b = reduce_step(sum_b, step_b)
    back0 = pick_blocks(plan["back"][0], jnp.concatenate([sum_a, sum_b], axis=0))
    got0 = lax.all_to_all(back0, AXES, 0, 0, tiled=True)
    error_sum = jnp.sum(sum1[n1, : D // LANES])
    divisor = sum1[n1, D // LANES, 0] * D
    new_first, new_second, new_master = adam(
        plan["row_from"],
        divisor,
        got0,
        got1,
        grad_vec,
        plan["row_block"],
        plan["row_used"],
        master,
        first_moment,
        second_moment,
    )
    mean_loss = error_sum / divisor
    return (block_out[None], input_grad[None], mean_loss, new_first, new_second, new_master)


def solution(mesh):
    return jax.shard_map(
        body,
        mesh=mesh,
        in_specs=(
            P(AXES, None, None),
            P(AXES, None, None),
            P(AXES),
            P(AXES, None),
            P(),
            P(AXES, None),
            P(AXES, None),
            P(AXES, None),
        ),
        out_specs=(
            P(AXES, None, None),
            P(AXES, None, None),
            P(),
            P(AXES, None),
            P(AXES, None),
            P(AXES, None),
        ),
        check_vma=False,
    )
```

```python
from functools import partial

import jax
import jax.numpy as jnp
import numpy as np
from jax import lax
from jax.experimental import pallas as pl
from jax.experimental.pallas import tpu as pltpu
from jax.sharding import PartitionSpec as P

D = 768
INNER = 1536
NSTATE = 128
HEADDIM = 64
KCONV = 4
SCAN_LEN = 256
PBLOCK = 4096
STEP = 10
HEADS = 24
CONVCH = 1792
PROJ = 3352
PTOT = 3765320
NBLK = 920

LANES = 128
BROWS = PBLOCK // LANES
UNIT = 8
UNITS = BROWS // UNIT
END_IN = D * PROJ
END_OUT = END_IN + INNER * D
MID0 = -(-END_IN // PBLOCK)
MID1 = END_OUT // PBLOCK
N0 = MID0 + NBLK - MID1
N1 = MID1 - MID0
F0_ROWS = N0 * BROWS
IN_ROWS = END_IN // LANES
HEAD_ROWS = MID0 * BROWS - IN_ROWS
TAIL_ROWS = (END_OUT - MID1 * PBLOCK) // LANES
OUT_ROWS = INNER * D // LANES
VEC_ROWS = (NBLK - MID1) * BROWS - TAIL_ROWS
VEC_AT = MID0 * BROWS + TAIL_ROWS
GROUP = 16
GROUPS = D // GROUP
GROUP_ROWS = GROUP * PROJ // LANES
COL_TILES = -(-PROJ // LANES)
WIDE = COL_TILES * LANES
OUT_TILES = D // LANES

NORM_EPS = 1e-05
ADAM_EPS = 1e-08
BETA_ONE = 0.9
BETA_TWO = 0.999
MATRIX_RATE = 0.03
VECTOR_RATE = 0.2
WEIGHT_DECAY = 0.1
PRECISE = lax.Precision.HIGHEST
AXES = ("dp", "fsdp")
VMEM_LIMIT = 60 * 1024 * 1024


def bits_of(count):
    return count.bit_length() - 1


def step_orders(dp, fsdp):
    wide = [("dp", i) for i in range(bits_of(dp))]
    narrow = [("fsdp", i) for i in range(bits_of(fsdp))]
    first = wide[:2] + narrow + wide[2:]
    second = wide[:1] + narrow + wide[1:]
    third = wide[:1] + wide[2:] + wide[1:2] + narrow
    return first, second, third


def cut(total, orders):
    base, more = divmod(total, len(orders))
    streams, at = [], 0
    for i, order in enumerate(orders):
        size = base + (i < more)
        if size:
            streams.append((at, size, order))
        at += size
    return streams


def exchange(values, step):
    axis, bit = step
    size = lax.axis_size(axis)
    return lax.ppermute(values, axis, [(i, i ^ (1 << bit)) for i in range(size)])


def place_of(relative, order):
    shift_of = {"dp": bits_of(lax.axis_size("fsdp")), "fsdp": 0}
    place = jnp.zeros_like(relative)
    for axis, bit in order:
        place = place * 2 + ((relative >> (shift_of[axis] + bit)) & 1)
    return place


def make_plan(owners, capacity, devices, me):
    block = jnp.arange(NBLK, dtype=jnp.int32)
    mid = (block >= MID0) & (block < MID1)
    same = mid[:, None] == mid[None, :]
    before = (owners[None, :] < owners[:, None]) | (
        (owners[None, :] == owners[:, None]) & (block[None, :] < block[:, None])
    )
    order_in_class = jnp.sum((same & before).astype(jnp.int32), axis=1)
    home, slot = order_in_class % devices, order_in_class // devices
    device = jnp.arange(devices, dtype=jnp.int32)
    below = owners[None, :] < device[:, None]
    owned = owners[None, :] == device[:, None]

    def total(mask):
        return jnp.sum(mask.astype(jnp.int32), axis=1)

    start = (total(below & ~mid[None, :]), total(below & mid[None, :]))
    count = (total(owned & ~mid[None, :]), total(owned & mid[None, :]))
    early = total(owned & (block < MID0)[None, :])
    pair = 2 + max(capacity - 2, 0) // devices

    def pick(vector, index):
        return jnp.sum(jnp.where(device == index, vector, 0))

    my_start = [pick(v, me) for v in start]
    my_count = [pick(v, me) for v in count]
    my_early = pick(early, me)

    lane = jnp.arange(pair, dtype=jnp.int32)
    k0 = (device[:, None] - my_start[0]) % devices + lane[None, :] * devices
    k1 = (device[:, None] - my_start[1]) % devices + (pair - 1 - lane)[None, :] * devices
    row0 = jnp.where(k0 < my_early, k0, k0 + my_count[1])
    send_rows = jnp.where(
        k0 < my_count[0], row0, jnp.where(k1 < my_count[1], my_early + k1, 0)
    ).reshape(-1)

    slots = (-(-N0 // devices), -(-N1 // devices))

    def received(kind):
        wanted = me + devices * jnp.arange(slots[kind], dtype=jnp.int32)
        ends = start[kind] + count[kind]
        owner = jnp.sum((ends[None, :] <= wanted[:, None]).astype(jnp.int32), axis=1)
        owner = jnp.minimum(owner, devices - 1)
        base = jnp.sum(jnp.where(device[None, :] == owner[:, None], start[kind][None, :], 0), axis=1)
        turn = jnp.clip((wanted - base) // devices, 0, pair - 1)
        return owner * pair + (turn if kind == 0 else pair - 1 - turn)

    back_pair = (UNITS * capacity + 2 * (devices - 1)) // devices
    unit = UNITS * order_in_class[:, None] + jnp.arange(UNITS, dtype=jnp.int32)[None, :]
    unit_home, unit_slot = unit % devices, unit // devices
    unit_slots = (-(-UNITS * N0 // devices), -(-UNITS * N1 // devices))
    lane = jnp.arange(back_pair, dtype=jnp.int32)

    def units_back(kind):
        turn = lane if kind == 0 else back_pair - 1 - lane
        first = UNITS * start[kind][:, None]
        k = (me - first) % devices + turn[None, :] * devices
        return k < UNITS * count[kind][:, None], (first + k) // devices

    valid0, slot0 = units_back(0)
    valid1, slot1 = units_back(1)
    back = jnp.where(valid0, slot0, jnp.where(valid1, unit_slots[0] + slot1, 0)).reshape(-1)

    row = jnp.arange(capacity, dtype=jnp.int32)
    is_mid = (row >= my_early) & (row < my_early + my_count[1])
    k = jnp.where(is_mid, row - my_early, jnp.where(row < my_early, row, row - my_count[1]))
    first = UNITS * jnp.where(is_mid, my_start[1], my_start[0])
    k = UNITS * k[:, None] + jnp.arange(UNITS, dtype=jnp.int32)[None, :]
    turn = k // devices
    row_from = ((first[:, None] + k) % devices) * back_pair + jnp.where(
        is_mid[:, None], back_pair - 1 - turn, turn
    )
    row_used = row < my_count[0] + my_count[1]
    mine = (owners == me)[None, :]
    rank = jnp.sum((mine & (block[None, :] < block[:, None])).astype(jnp.int32), axis=1)
    row_block = jnp.sum(
        jnp.where(mine & (rank[None, :] == row[:, None]), block[None, :], 0), axis=1
    )
    late = devices * back_pair + UNITS * (row_block - MID1)
    late = late[:, None] + jnp.arange(UNITS, dtype=jnp.int32)[None, :]
    row_from = jnp.where((row_block >= MID1)[:, None], late, row_from)
    row_from = jnp.where(row_used[:, None], row_from, 0).reshape(-1)
    return dict(
        home=home, slot=slot, slots=slots, pair=pair, send_rows=send_rows,
        received=(received(0), received(1)), unit_home=unit_home, unit_slot=unit_slot,
        unit_slots=unit_slots, back=back, row_from=row_from,
        row_used=row_used, row_block=row_block,
    )


def stream_places(home, slot, me, streams, devices):
    relative = home ^ me
    place = jnp.zeros_like(slot)
    for begin, size, order in streams:
        inside = (slot >= begin) & (slot < begin + size)
        at = devices * begin + place_of(relative, order) * size + slot - begin
        place = jnp.where(inside, at, place)
    return place


ANY = pl.BlockSpec(memory_space=pl.ANY)
VMEM = pl.BlockSpec(memory_space=pltpu.VMEM)
SMEM = pl.BlockSpec(memory_space=pltpu.SMEM)


def params(**extra):
    return pltpu.CompilerParams(vmem_limit_bytes=VMEM_LIMIT, **extra)


def shape(dims, dtype):
    return jax.ShapeDtypeStruct(dims, dtype)


def send_kernel(table, master, out, flat):
    capacity = master.shape[0]
    for j in range(BROWS):
        flat[pl.ds(j, capacity, stride=BROWS), :] = master[:, j * LANES : (j + 1) * LANES]

    def step(i, carry):
        out[i] = flat[pl.ds(pl.multiple_of(table[i] * BROWS, BROWS), BROWS), :].astype(out.dtype)
        return carry

    lax.fori_loop(0, out.shape[0], step, 0)


def send_blocks(table, master):
    return pl.pallas_call(
        send_kernel,
        out_shape=shape((table.shape[0], BROWS, LANES), jnp.bfloat16),
        in_specs=[SMEM, VMEM],
        out_specs=VMEM,
        scratch_shapes=[pltpu.VMEM((master.shape[0] * BROWS, LANES), jnp.float32)],
        compiler_params=params(),
    )(table, master)


def pick_kernel(table, source, *outs):
    at = 0
    for out in outs:

        def step(i, carry, out=out, at=at):
            out[i] = source[table[at + i]]
            return carry

        lax.fori_loop(0, out.shape[0], step, 0)
        at += out.shape[0]


def pick_blocks(table, source, sizes):
    return pl.pallas_call(
        pick_kernel,
        out_shape=tuple(shape((n,) + source.shape[1:], source.dtype) for n in sizes),
        in_specs=[SMEM, VMEM],
        out_specs=(VMEM,) * len(sizes),
        compiler_params=params(),
    )(table, source)


def back_kernel(table, *refs):
    sources, (out, held) = refs[:-2], refs[-2:]
    at = 0
    for i in range(0, len(sources), 2):
        n = sources[i].shape[0]
        held[at : at + n] = sources[i][...] + sources[i + 1][...]
        at += n

    def step(i, carry):
        for u in range(8):
            out[i * 8 + u] = held[table[i * 8 + u]]
        return carry

    total = out.shape[0]
    lax.fori_loop(0, total // 8, step, 0)


def units_to_owners(table, sources):
    return pl.pallas_call(
        back_kernel,
        out_shape=shape((table.shape[0], UNIT, LANES), jnp.float32),
        in_specs=[SMEM] + [VMEM] * len(sources),
        out_specs=VMEM,
        scratch_shapes=[
            pltpu.VMEM((sum(s.shape[0] for s in sources[::2]), UNIT, LANES), jnp.float32)
        ],
        compiler_params=params(),
    )(table, *sources)


def row_start(rho):
    return (PROJ * rho) // LANES, (PROJ * rho) % LANES


def copy_all(pairs, sem):
    copies = [pltpu.make_async_copy(a, b, sem.at[i]) for i, (a, b) in enumerate(pairs)]
    for c in copies:
        c.start()
    for c in copies:
        c.wait()


def spread_blocks(table, held, flat, count, first_row):
    def one(i):
        at = pl.multiple_of(first_row + i * BROWS, 16)
        flat[pl.ds(at, BROWS), :] = held[table[i]].astype(jnp.float32)

    def step(i, carry):
        for u in range(4):
            one(i * 4 + u)
        return carry

    lax.fori_loop(0, count // 4, step, 0)
    for i in range(count // 4 * 4, count):
        one(i)


def unpack_vectors(flat, conv_weight, conv_bias, heads, skip, norm_gain, gate_gain):
    bf16, f32 = jnp.bfloat16, jnp.float32
    tiles = CONVCH // LANES
    row = lax.broadcasted_iota(jnp.int32, (LANES, LANES), 0)
    col = lax.broadcasted_iota(jnp.int32, (LANES, LANES), 1)
    per_tile = LANES // KCONV
    for k in range(KCONV):
        total = jnp.zeros((tiles, LANES), f32)
        for q in range(KCONV):
            rows = flat[pl.ds(VEC_AT + q, tiles, stride=KCONV), :].astype(bf16)
            chosen = (row == KCONV * (col % per_tile) + k) & (col // per_tile == q)
            total = total + jnp.dot(rows, chosen.astype(bf16), preferred_element_type=f32)
        for i in range(tiles):
            conv_weight[k : k + 1, i * LANES : (i + 1) * LANES] = total[i : i + 1, :]
    bias_at = VEC_AT + tiles * KCONV
    for i in range(tiles):
        conv_bias[:, i * LANES : (i + 1) * LANES] = flat[bias_at + i : bias_at + i + 1, :]
    at = bias_at + tiles
    lane = lax.broadcasted_iota(jnp.int32, (8, LANES), 1)
    first = flat[at : at + 8, :]
    three = []
    for i in range(3):
        moved = pltpu.roll(first, LANES - i * HEADS, 1) if i else first
        three.append(jnp.where(lane < HEADS, moved, 0.0))
        heads[i : i + 1, :] = three[i][0:1, :]
    for j in range(INNER // LANES):
        h = lax.broadcasted_iota(jnp.int32, (LANES, LANES), 0)
        c = lax.broadcasted_iota(jnp.int32, (LANES, LANES), 1) + j * LANES
        spread = (h == c // HEADDIM).astype(bf16)
        wide = jnp.dot(three[2].astype(bf16), spread, preferred_element_type=f32)
        skip[:, j * LANES : (j + 1) * LANES] = wide[0:1, :]
    shift = 3 * HEADS
    for out, begin, width in ((norm_gain, at, D), (gate_gain, at + D // LANES, INNER)):
        for j in range(width // LANES):
            x = pltpu.roll(flat[begin + j : begin + j + 1, :], LANES - shift, 1)
            y = pltpu.roll(flat[begin + j + 1 : begin + j + 2, :], LANES - shift, 1)
            out[:, j * LANES : (j + 1) * LANES] = jnp.where(lane[0:1] < LANES - shift, x, y)


def unpack_in_kernel(table, *refs):
    parts, (w_in, head, tail, *vectors), (held, flat, tile, sem) = refs[:-13], refs[-13:-4], refs[-4:]
    pairs, at = [], 0
    for part in parts:
        pairs.append((part, held.at[pl.ds(at, part.shape[0])]))
        at += part.shape[0]
    copy_all(pairs, sem)
    spread_blocks(table, held, flat, N0, 0)
    head[...] = flat[IN_ROWS : IN_ROWS + HEAD_ROWS, :]
    tail[...] = flat[MID0 * BROWS : MID0 * BROWS + TAIL_ROWS, :]
    unpack_vectors(flat, *vectors)
    lane = lax.broadcasted_iota(jnp.int32, (GROUPS, LANES), 1)

    def columns(j):
        for rho in range(GROUP):
            c, s = row_start(rho)
            x = flat[pl.ds(c + j, GROUPS, stride=GROUP_ROWS), :]
            if s:
                y = flat[pl.ds(c + j + 1, GROUPS, stride=GROUP_ROWS), :]
                x = jnp.where(
                    lane < LANES - s,
                    pltpu.roll(x, LANES - s, 1),
                    pltpu.roll(y, LANES - s, 1),
                )
            tile[pl.ds(rho, GROUPS, stride=GROUP), :] = x

    def step(j, carry):
        columns(j)
        w_in[:, pl.ds(pl.multiple_of(j * LANES, LANES), LANES)] = tile[...].astype(jnp.bfloat16)
        return carry

    lax.fori_loop(0, COL_TILES - 1, step, 0)
    columns(COL_TILES - 1)
    last = (COL_TILES - 1) * LANES
    inside = lax.broadcasted_iota(jnp.int32, (D, LANES), 1) < PROJ - last
    w_in[:, last:] = jnp.where(inside, tile[...], 0.0).astype(jnp.bfloat16)


def unpack_in(table, parts):
    held = sum(part.shape[0] for part in parts)
    return pl.pallas_call(
        unpack_in_kernel,
        out_shape=(
            shape((D, WIDE), jnp.bfloat16),
            shape((HEAD_ROWS, LANES), jnp.float32),
            shape((TAIL_ROWS, LANES), jnp.float32),
            shape((KCONV, CONVCH), jnp.float32),
            shape((1, CONVCH), jnp.float32),
            shape((8, LANES), jnp.float32),
            shape((1, INNER), jnp.float32),
            shape((1, D), jnp.float32),
            shape((1, INNER), jnp.float32),
        ),
        in_specs=[SMEM] + [ANY] * len(parts),
        out_specs=(VMEM,) * 9,
        scratch_shapes=[
            pltpu.VMEM((held, BROWS, LANES), jnp.bfloat16),
            pltpu.VMEM((F0_ROWS, LANES), jnp.float32),
            pltpu.VMEM((D, LANES), jnp.float32),
            pltpu.SemaphoreType.DMA((len(parts),)),
        ],
        compiler_params=params(),
    )(table, *parts)


def unpack_out_kernel(table, held, head, tail, w_out, flat):
    flat[0:HEAD_ROWS, :] = head[...]
    flat[OUT_ROWS - TAIL_ROWS : OUT_ROWS, :] = tail[...]
    spread_blocks(table, held, flat, N1, HEAD_ROWS)
    rows = 128

    def step(i, carry):
        at = pl.multiple_of(i * rows, rows)
        for j in range(OUT_TILES):
            x = flat[pl.ds(at * OUT_TILES + j, rows, stride=OUT_TILES), :]
            w_out[pl.ds(at, rows), j * LANES : (j + 1) * LANES] = x.astype(jnp.bfloat16)
        return carry

    lax.fori_loop(0, INNER // rows, step, 0)


def unpack_out(table, held, head, tail):
    return pl.pallas_call(
        unpack_out_kernel,
        out_shape=shape((INNER, D), jnp.bfloat16),
        in_specs=[SMEM] + [VMEM] * 3,
        out_specs=VMEM,
        scratch_shapes=[pltpu.VMEM((OUT_ROWS, LANES), jnp.float32)],
        compiler_params=params(),
    )(table, held, head, tail)


def permute_units(table, flat, count, first_row, staged):
    many = 16

    def step(i, carry):
        for u in range(many):
            at = pl.multiple_of(first_row + (i * many + u) * UNIT, UNIT)
            staged[table[i * many + u]] = flat[pl.ds(at, UNIT), :]
        return carry

    lax.fori_loop(0, count // many, step, 0)
    for i in range(count // many * many, count):
        staged[table[i]] = flat[first_row + i * UNIT : first_row + (i + 1) * UNIT, :]


def pack_in_kernel(table, hidden, grad, head, *refs):
    outs, (turned, tiles, flat, staged, sem) = refs[:-5], refs[-5:]
    turned[...] = hidden[...].T
    lane = lax.broadcasted_iota(jnp.int32, (GROUPS, LANES), 1)

    def product(p, count):
        at = p * 2 * LANES
        at = at if isinstance(at, int) else pl.multiple_of(at, 2 * LANES)
        return jnp.dot(
            turned[...], grad[:, pl.ds(at, count * LANES)], preferred_element_type=jnp.float32
        )

    def put(p, value):
        for k in range(value.shape[1] // LANES):
            at = (p * 2 + k) * D
            at = at if isinstance(at, int) else pl.multiple_of(at, D)
            tiles[pl.ds(at, D), :] = value[:, k * LANES : (k + 1) * LANES]

    def load(rho, j):
        return tiles[pl.ds(j * D + rho, GROUPS, stride=GROUP), :]

    def whole(rho, i):
        first = -(-PROJ * rho // LANES)
        col0 = first * LANES - PROJ * rho
        x = load(rho, i)
        if col0:
            x = jnp.where(
                lane < LANES - col0,
                pltpu.roll(x, LANES - col0, 1),
                pltpu.roll(load(rho, i + 1), LANES - col0, 1),
            )
        flat[pl.ds(first + i, GROUPS, stride=GROUP_ROWS), :] = x

    put(0, product(0, 2))
    put(1, product(1, 2))
    pairs = COL_TILES // 2

    def step(p, carry):
        for i in range(2):
            for rho in range(GROUP):
                whole(rho, p * 2 + i)
        put(p + 2, product(p + 2, 2))
        return carry

    lax.fori_loop(0, pairs - 2, step, 0)
    put(pairs, product(pairs, COL_TILES % 2))
    for rho in range(GROUP):
        first = -(-PROJ * rho // LANES)
        col0 = first * LANES - PROJ * rho
        full = (PROJ - col0) // LANES
        for i in range((pairs - 2) * 2, full):
            whole(rho, i)
        left = PROJ - col0 - full * LANES
        if left:
            begin = col0 + full * LANES
            j, s = begin // LANES, begin % LANES
            x = pltpu.roll(load(rho, j), LANES - s, 1) if s else load(rho, j)
            if s + left > LANES:
                x = jnp.where(lane < LANES - s, x, pltpu.roll(load(rho, j + 1), LANES - s, 1))
            y = pltpu.roll(load(rho + 1, 0), left, 1)
            flat[pl.ds(first + full, GROUPS, stride=GROUP_ROWS), :] = jnp.where(lane < left, x, y)
    flat[IN_ROWS : IN_ROWS + HEAD_ROWS, :] = head[...]
    permute_units(table, flat, MID0 * UNITS, 0, staged)
    copies, at = [], 0
    for out in outs:
        copies.append((staged.at[pl.ds(at, out.shape[0])], out))
        at += out.shape[0]
    copy_all(copies, sem)


def pack_in(table, hidden, grad, head, sizes):
    return pl.pallas_call(
        pack_in_kernel,
        out_shape=tuple(shape((n, UNIT, LANES), jnp.float32) for n in sizes),
        in_specs=[SMEM, VMEM, VMEM, VMEM],
        out_specs=(ANY,) * len(sizes),
        scratch_shapes=[
            pltpu.VMEM((D, hidden.shape[0]), jnp.bfloat16),
            pltpu.VMEM((COL_TILES * D, LANES), jnp.float32),
            pltpu.VMEM((MID0 * BROWS, LANES), jnp.float32),
            pltpu.VMEM((sum(sizes), UNIT, LANES), jnp.float32),
            pltpu.SemaphoreType.DMA((len(sizes),)),
        ],
        compiler_params=params(),
    )(table, hidden, grad, head)


def pack_out_kernel(table, grad, local, out, head, tail, flat, *, slots):
    rows = 128

    def step(i, carry):
        at = pl.multiple_of(i * rows, rows)
        for j in range(OUT_TILES):
            flat[pl.ds(at * OUT_TILES + j, rows, stride=OUT_TILES), :] = grad[
                pl.ds(at, rows), j * LANES : (j + 1) * LANES
            ]
        return carry

    lax.fori_loop(0, INNER // rows, step, 0)
    head[...] = flat[0:HEAD_ROWS, :]
    tail[...] = flat[OUT_ROWS - TAIL_ROWS : OUT_ROWS, :]
    permute_units(table, flat, N1 * UNITS, HEAD_ROWS, out)

    def add_local(i, carry):
        out[i * slots + slots - 1] = local[...]
        return carry

    lax.fori_loop(0, out.shape[0] // slots, add_local, 0)


def pack_out(table, grad, local, devices, slots):
    return pl.pallas_call(
        partial(pack_out_kernel, slots=slots),
        out_shape=(
            shape((devices * slots, UNIT, LANES), jnp.float32),
            shape((HEAD_ROWS, LANES), jnp.float32),
            shape((TAIL_ROWS, LANES), jnp.float32),
        ),
        in_specs=[SMEM, VMEM, VMEM],
        out_specs=(VMEM,) * 3,
        scratch_shapes=[pltpu.VMEM((OUT_ROWS, LANES), jnp.float32)],
        compiler_params=params(),
    )(table, grad, local)


def adam_kernel(table, scale, got, late, limit, used, master, first, second, o_first, o_second, o_master, flat, held):
    capacity = master.shape[0]

    def step(i, carry):
        for u in range(UNITS):
            at = table[i * UNITS + u]
            rows = pl.ds(pl.multiple_of(i * BROWS + u * UNIT, UNIT), UNIT)
            flat[rows, :] = held[at]
        return carry

    held[0 : got.shape[0]] = got[...]
    held[got.shape[0] :] = late[...]
    lax.fori_loop(0, capacity, step, 0)
    lane = lax.broadcasted_iota(jnp.int32, (capacity, LANES), 1)
    divisor = scale[0]
    for j in range(BROWS):
        cols = slice(j * LANES, (j + 1) * LANES)
        grad = jnp.where(used[...] > 0, flat[pl.ds(j, capacity, stride=BROWS), :], 0.0) / divisor
        matrix = lane + j * LANES < limit[...]
        weights = master[:, cols]
        new_first = BETA_ONE * first[:, cols] + (1.0 - BETA_ONE) * grad
        new_second = BETA_TWO * second[:, cols] + (1.0 - BETA_TWO) * grad * grad
        normal = (
            new_first
            / (1.0 - BETA_ONE**STEP)
            / (jnp.sqrt(new_second / (1.0 - BETA_TWO**STEP)) + ADAM_EPS)
        )
        rate = jnp.where(matrix, MATRIX_RATE, VECTOR_RATE)
        decay = jnp.where(matrix, WEIGHT_DECAY, 0.0)
        o_first[:, cols] = new_first
        o_second[:, cols] = new_second
        o_master[:, cols] = weights - rate * (normal + decay * weights)


def adam(table, divisor, got, late, row_block, row_used, master, first, second):
    capacity = master.shape[0]
    limit = jnp.broadcast_to((END_OUT - row_block * PBLOCK)[:, None], (capacity, LANES))
    used = jnp.broadcast_to(row_used.astype(jnp.int32)[:, None], (capacity, LANES))
    return pl.pallas_call(
        adam_kernel,
        out_shape=(shape(master.shape, jnp.float32),) * 3,
        in_specs=[SMEM, SMEM] + [VMEM] * 7,
        out_specs=(VMEM,) * 3,
        scratch_shapes=[
            pltpu.VMEM((capacity * BROWS, LANES), jnp.float32),
            pltpu.VMEM((got.shape[0] + late.shape[0], UNIT, LANES), jnp.float32),
        ],
        compiler_params=params(),
    )(table, divisor.reshape(1), got, late, limit, used, master, first, second)


def gather_steps(values, order):
    for step in order[:0:-1]:
        values = jnp.concatenate([values, exchange(values, step)], axis=0)
    return values, exchange(values, order[0])


def reduce_step(values, step, extra=None):
    half = values.shape[0] // 2
    if extra is None:
        return values[:half] + exchange(values[half:], step)
    got = exchange(jnp.concatenate([values[half:], extra]), step)
    return values[:half] + got[:half], extra + got[half:]


CHUNK = 128
PAIRS = HEADS // 2
MIXW = INNER + 2 * NSTATE
DT_AT = INNER + CONVCH
F32 = jnp.float32
BF16 = jnp.bfloat16
NN = (((1,), (0,)), ((), ()))
NT = (((1,), (1,)), ((), ()))


def cost(microseconds):
    return pl.CostEstimate(
        flops=int(microseconds * 1e9), bytes_accessed=int(microseconds * 3e6), transcendentals=0
    )


def dot(a, b, dims=NN):
    return lax.dot_general(a, b, dims, preferred_element_type=F32)


def split(v):
    high = v.astype(BF16)
    return high, (v - high.astype(F32)).astype(BF16)


def dot3(a, b, dims=NN):
    ah, al = a
    bh, bl = b
    return dot(ah, bh, dims) + (dot(ah, bl, dims) + dot(al, bh, dims))


def heads_gather():
    return jnp.asarray(np.repeat(np.eye(HEADS, LANES, dtype=np.float32), HEADDIM, axis=0), BF16)


def three_parts(v):
    high = v.astype(BF16).astype(F32)
    rest = v - high
    middle = rest.astype(BF16).astype(F32)
    low = rest - middle
    return (high + pltpu.roll(middle, 32, 1) + pltpu.roll(low, 64, 1)).astype(BF16)


def triangle_sum(tri, v):
    parts = dot(tri, three_parts(v))
    lane = lax.broadcasted_iota(jnp.int32, parts.shape, 1)
    total = parts + pltpu.roll(parts, LANES - 32, 1) + pltpu.roll(parts, LANES - 64, 1)
    return jnp.where(lane < HEADS, total, 0.0)


def chunk_decays(dt, dt_bias, a_log):
    lane = lax.broadcasted_iota(jnp.int32, (CHUNK, LANES), 1)
    row = lax.broadcasted_iota(jnp.int32, (CHUNK, LANES), 0)
    shifted = dt + dt_bias
    delta = jnp.where(
        lane < HEADS, jnp.maximum(shifted, 0.0) + jnp.log1p(jnp.exp(-jnp.abs(shifted))), 0.0
    )
    rate = -jnp.exp(a_log)
    lower = (row >= lane).astype(BF16)
    cum = triangle_sum(lower, delta * rate)
    last = cum[CHUNK - 1 : CHUNK, :]
    return shifted, delta, rate, cum, last


def pair_mask():
    lane = lax.broadcasted_iota(jnp.int32, (CHUNK, LANES), 1)
    low = (lane < HEADDIM).astype(F32)
    return low.astype(BF16), (1.0 - low).astype(BF16)


QUADS = HEADS // 4
QWIDTH = 4 * HEADDIM


def sigmoid(v):
    return 0.5 * jnp.tanh(0.5 * v) + 0.5


def silu(v):
    return v * sigmoid(v)


def side_by_side(v):
    high, low = split(v)
    return jnp.concatenate([high, low], axis=1), high


def dot_parts(a, b):
    ahl, ah = a
    bh, bl = b
    return dot(ahl, jnp.concatenate([bh, bh], axis=0)) + dot(ah, bl)


def dot_turned(a, b):
    ah, al = a
    bh, bl = b
    both = dot(ah, jnp.concatenate([bh, bl], axis=0), NT)
    n = bh.shape[0]
    return both[:, :n] + both[:, n:] + dot(al, bh, NT)


def widen(delta, cum, quad):
    lane = lax.broadcasted_iota(jnp.int32, (CHUNK, LANES), 1)
    over = lambda v, h: jnp.broadcast_to(v[:, h : h + 1], (CHUNK, LANES))
    first = 4 * quad
    columns = [over(cum, first + k) for k in range(4)]
    rates = [over(delta, first + k) for k in range(4)]
    pair = lambda vs: jnp.concatenate(
        [jnp.where(lane < HEADDIM, vs[0], vs[1]), jnp.where(lane < HEADDIM, vs[2], vs[3])], axis=1
    )
    return pair(rates), pair(columns), columns


def pair_rows(parts, j, low, high):
    cols = slice(j * LANES, (j + 1) * LANES)
    return [jnp.concatenate([p[:, cols] * low, p[:, cols] * high], axis=0) for p in parts]


def scan_forward_kernel(
    mixed, dt, gate, dt_bias, a_log, skip, gain, ssm, mixed_out, states, state
):
    @pl.when(pl.program_id(0) == 0)
    def _():
        state[...] = jnp.zeros_like(state)

    states[0] = state[...]
    _, delta, _, cum, last = chunk_decays(dt[...], dt_bias[...], a_log[...])
    lane = lax.broadcasted_iota(jnp.int32, (CHUNK, LANES), 1)
    row = lax.broadcasted_iota(jnp.int32, (CHUNK, LANES), 0)
    bias = jnp.where(row >= lane, 0.0, -1e30)
    cum_t = cum.T
    inputs_b = mixed[:, INNER : INNER + NSTATE]
    readout = mixed[:, INNER + NSTATE :]
    affinity = dot3(split(readout), split(inputs_b), NT)
    readout_parts = side_by_side(readout)
    b_parts = side_by_side(inputs_b.T)
    low, high = pair_mask()
    squares = jnp.zeros((CHUNK, LANES), F32)
    for quad in range(QUADS):
        cols = slice(quad * QWIDTH, (quad + 1) * QWIDTH)
        wide_delta, wide_cum, columns = widen(delta, cum, quad)
        values = mixed[:, cols]
        scaled = values * wide_delta
        parts = split(scaled)
        outs = []
        for j in range(2):
            right_h, right_l = pair_rows(parts, j, low, high)
            left = []
            for k in range(2):
                h = 4 * quad + 2 * j + k
                within = jnp.exp(columns[2 * j + k] - cum_t[h : h + 1, :] + bias)
                left.append(split(affinity * within))
            left_h = jnp.concatenate([left[0][0], left[1][0]], axis=1)
            left_l = jnp.concatenate([left[0][1], left[1][1]], axis=1)
            both = dot(left_h, jnp.concatenate([right_h, right_l], axis=1))
            outs.append(both[:, :LANES] + both[:, LANES:] + dot(left_l, right_h))
        carried = state[:, cols]
        grown = jnp.exp(wide_cum)
        out = jnp.concatenate(outs, axis=1) + dot_parts(readout_parts, split(carried)) * grown
        out = out + skip[:, cols] * values
        tail = jnp.exp(wide_cum[CHUNK - 1 :] - wide_cum)
        state[:, cols] = carried * grown[CHUNK - 1 :] + dot_parts(b_parts, split(scaled * tail))
        ssm[:, cols] = out
        gated = out * silu(gate[:, cols])
        squares = squares + gated[:, :LANES] * gated[:, :LANES] + gated[:, LANES:] * gated[:, LANES:]
    rho = lax.rsqrt(jnp.sum(squares, axis=1, keepdims=True) * (1.0 / INNER) + NORM_EPS)
    for j in range(PAIRS):
        cols = slice(j * LANES, (j + 1) * LANES)
        gated = ssm[:, cols] * silu(gate[:, cols])
        mixed_out[:, cols] = (gated * rho * gain[:, cols]).astype(BF16)


def scan_forward(mixed, projected, dt_bias, a_log, skip, gain):
    length = mixed.shape[0]
    chunks = length // CHUNK
    whole = lambda v: pl.BlockSpec(v.shape, lambda i: (0,) * v.ndim)
    return pl.pallas_call(
        scan_forward_kernel,
        grid=(chunks,),
        out_shape=(
            shape((length, INNER), F32),
            shape((length, INNER), BF16),
            shape((chunks, NSTATE, INNER), F32),
        ),
        in_specs=[
            pl.BlockSpec((CHUNK, MIXW), lambda i: (i, 0)),
            pl.BlockSpec((CHUNK, LANES), lambda i: (i, DT_AT // LANES)),
            pl.BlockSpec((CHUNK, INNER), lambda i: (i, 0)),
        ]
        + [whole(v) for v in (dt_bias, a_log, skip, gain)],
        out_specs=(
            pl.BlockSpec((CHUNK, INNER), lambda i: (i, 0)),
            pl.BlockSpec((CHUNK, INNER), lambda i: (i, 0)),
            pl.BlockSpec((1, NSTATE, INNER), lambda i: (i, 0, 0)),
        ),
        scratch_shapes=[pltpu.VMEM((NSTATE, INNER), F32)],
        compiler_params=params(),
        cost_estimate=cost(40),
    )(mixed, projected, projected, dt_bias, a_log, skip, gain)


def scan_backward_kernel(
    mixed, dt, ssm, grad, states, dt_bias, a_log, skip, gather, held,
    grad_mixed, grad_dt, sums, skip_sums, grad_state, left, right,
):
    @pl.when(pl.program_id(0) == 0)
    def _():
        grad_state[...] = jnp.zeros_like(grad_state)
        sums[...] = jnp.zeros_like(sums)
        skip_sums[...] = jnp.zeros_like(skip_sums)

    shifted, delta, rate, cum, last = chunk_decays(dt[...], dt_bias[...], a_log[...])
    lane = lax.broadcasted_iota(jnp.int32, (CHUNK, LANES), 1)
    row = lax.broadcasted_iota(jnp.int32, (CHUNK, LANES), 0)
    bias = jnp.where(lane >= row, 0.0, -1e30)
    heads = lane < HEADS
    cum_t = cum.T
    inputs_b = mixed[:, INNER : INNER + NSTATE]
    readout = mixed[:, INNER + NSTATE :]
    b_parts, c_parts = split(inputs_b), split(readout)
    b_wide = side_by_side(inputs_b)
    c_turned = side_by_side(readout.T)
    affinity = dot3(b_parts, c_parts, NT)
    low, high = pair_mask()
    grad_affinity = jnp.zeros((CHUNK, CHUNK), F32)
    grad_b = jnp.zeros((CHUNK, NSTATE), F32)
    grad_c = jnp.zeros((CHUNK, NSTATE), F32)
    last_row = lax.broadcasted_iota(jnp.int32, (CHUNK, QWIDTH), 0) == CHUNK - 1
    for quad in range(QUADS):
        cols = slice(quad * QWIDTH, (quad + 1) * QWIDTH)
        wide_delta, wide_cum, columns = widen(delta, cum, quad)
        grown = jnp.exp(wide_cum)
        tail = jnp.exp(wide_cum[CHUNK - 1 :] - wide_cum)
        end = grown[CHUNK - 1 :]
        values = mixed[:, cols]
        pulled = grad[:, cols]
        scaled = values * wide_delta
        x_parts, p_parts = split(scaled), split(pulled)
        outs = []
        for j in range(2):
            half = slice(j * LANES, (j + 1) * LANES)
            xh, xl = x_parts[0][:, half], x_parts[1][:, half]
            right_h, right_l = pair_rows(p_parts, j, low, high)
            pull = dot(
                jnp.concatenate([xh, xl], axis=1),
                jnp.concatenate([right_h, right_h], axis=1),
                NT,
            ) + dot(xh, right_l, NT)
            kernels = []
            for k in range(2):
                h = 4 * quad + 2 * j + k
                within = jnp.exp(cum_t[h : h + 1, :] - columns[2 * j + k] + bias)
                kernels.append(split(affinity * within))
                grad_affinity = grad_affinity + within * pull[:, k * CHUNK : (k + 1) * CHUNK]
            kernel_h = jnp.concatenate([kernels[0][0], kernels[1][0]], axis=1)
            kernel_l = jnp.concatenate([kernels[0][1], kernels[1][1]], axis=1)
            both = dot(kernel_h, jnp.concatenate([right_h, right_l], axis=1))
            outs.append(both[:, :LANES] + both[:, LANES:] + dot(kernel_l, right_h))
        late = grad_state[:, cols]
        late_parts = split(late)
        early = states[0, :, cols]
        from_state = dot_parts(b_wide, late_parts) * tail
        grad_scaled = jnp.concatenate(outs, axis=1) + from_state
        pulled_cum = split(pulled * grown)
        grad_c = grad_c + dot_turned(pulled_cum, split(early))
        grad_b = grad_b + dot_turned(split(scaled * tail), late_parts)
        grad_state[:, cols] = late * end + dot_parts(c_turned, pulled_cum)
        grad_mixed[:, cols] = grad_scaled * wide_delta + skip[:, cols] * pulled
        skip_sums[:, cols] += jnp.sum(pulled * values, axis=0, keepdims=True)
        left[:, cols] = grad_scaled * values
        inner = pulled * (ssm[:, cols] - skip[:, cols] * values) - scaled * grad_scaled
        extra = jnp.sum(scaled * from_state, axis=0, keepdims=True) + end * jnp.sum(
            late * early, axis=0, keepdims=True
        )
        right[:, cols] = inner + jnp.where(last_row, extra, 0.0)
    ga_parts = split(grad_affinity)
    grad_mixed[:, INNER : INNER + NSTATE] = grad_b + dot3(ga_parts, c_parts)
    grad_mixed[:, INNER + NSTATE :] = grad_c + dot3(split(grad_affinity.T), b_parts)

    def by_head(v):
        high, low = split(v)
        g = gather[...]
        return dot(high, g) + dot(low, g)

    direct = by_head(left[...])
    grad_cum = by_head(right[...])
    upper = (lane >= row).astype(BF16)
    after = triangle_sum(upper, grad_cum)
    grad_delta = direct + rate * after
    grad_raw = jnp.where(heads, grad_delta * sigmoid(shifted), 0.0)
    grad_dt[...] = grad_raw.astype(BF16)
    sums[0:1, :] += jnp.sum(grad_raw, axis=0, keepdims=True)
    sums[1:2, :] += rate * jnp.sum(delta * after, axis=0, keepdims=True)


def scan_backward(mixed, projected, ssm, grad, states, dt_bias, a_log, skip, gather, held):
    length = mixed.shape[0]
    chunks = length // CHUNK
    whole = lambda v: pl.BlockSpec(v.shape, lambda i: (0,) * v.ndim)
    back = lambda i: (chunks - 1 - i, 0)
    return pl.pallas_call(
        scan_backward_kernel,
        grid=(chunks,),
        out_shape=(
            shape((length, MIXW), F32),
            shape(held.shape, BF16),
            shape((8, LANES), F32),
            shape((1, INNER), F32),
        ),
        in_specs=[
            pl.BlockSpec((CHUNK, MIXW), back),
            pl.BlockSpec((CHUNK, LANES), lambda i: (chunks - 1 - i, DT_AT // LANES)),
            pl.BlockSpec((CHUNK, INNER), back),
            pl.BlockSpec((CHUNK, INNER), back),
            pl.BlockSpec((1, NSTATE, INNER), lambda i: (chunks - 1 - i, 0, 0)),
        ]
        + [whole(v) for v in (dt_bias, a_log, skip, gather)]
        + [ANY],
        out_specs=(
            pl.BlockSpec((CHUNK, MIXW), back),
            pl.BlockSpec((CHUNK, LANES), lambda i: (chunks - 1 - i, DT_AT // LANES)),
            pl.BlockSpec((8, LANES), lambda i: (0, 0)),
            pl.BlockSpec((1, INNER), lambda i: (0, 0)),
        ),
        scratch_shapes=[pltpu.VMEM((NSTATE, INNER), F32)] + [pltpu.VMEM((CHUNK, INNER), F32)] * 2,
        compiler_params=params(),
        input_output_aliases={9: 1},
        cost_estimate=cost(35),
    )(mixed, projected, ssm, grad, states, dt_bias, a_log, skip, gather, held)


ROWS_AT_ONCE = 128
CONV_TILES = 2


def down(v, before, by):
    moved = pltpu.roll(v, by, 0)
    row = lax.broadcasted_iota(jnp.int32, (8, LANES), 0)
    top = jnp.where(row < by, pltpu.roll(before, by, 0), moved[:8])
    return jnp.concatenate([top, moved[8:]], axis=0)


def up(v, after, by):
    rows = v.shape[0]
    moved = pltpu.roll(v, rows - by, 0)
    row = lax.broadcasted_iota(jnp.int32, (8, LANES), 0)
    end = jnp.where(row < 8 - by, moved[rows - 8 :], pltpu.roll(after, 8 - by, 0))
    return jnp.concatenate([moved[: rows - 8], end], axis=0)


def conv_terms(conv_in, at, cols):
    rows = conv_in[at : at + ROWS_AT_ONCE, cols]
    before = conv_in[at - 8 : at, cols] if at else jnp.zeros((8, LANES), F32)
    return [down(rows, before, KCONV - 1 - k) for k in range(KCONV - 1)] + [rows]


def conv_sum(terms, weight, bias):
    total = bias + terms[KCONV - 1] * weight[KCONV - 1 : KCONV]
    for k in range(KCONV - 1):
        total = total + terms[k] * weight[k : k + 1]
    return total


def conv_forward_kernel(conv_in, weight, bias, mixed):
    for tile in range(CONV_TILES):
        cols = slice(tile * LANES, (tile + 1) * LANES)
        w, b = weight[:, cols], bias[:, cols]
        for at in range(0, conv_in.shape[0], ROWS_AT_ONCE):
            mixed[at : at + ROWS_AT_ONCE, cols] = silu(conv_sum(conv_terms(conv_in, at, cols), w, b))


def conv_forward(projected, weight, bias):
    length = projected.shape[0]
    width = CONV_TILES * LANES
    return pl.pallas_call(
        conv_forward_kernel,
        grid=(CONVCH // width,),
        out_shape=shape((length, CONVCH), F32),
        in_specs=[
            pl.BlockSpec((length, width), lambda i: (0, INNER // width + i)),
            pl.BlockSpec((KCONV, width), lambda i: (0, i)),
            pl.BlockSpec((1, width), lambda i: (0, i)),
        ],
        out_specs=pl.BlockSpec((length, width), lambda i: (0, i)),
        compiler_params=params(),
        cost_estimate=cost(10),
    )(projected, weight, bias)


def conv_backward_kernel(conv_in, grad, weight, bias, held, out, sums):
    length = conv_in.shape[0]
    for tile in range(CONV_TILES):
        cols = slice(tile * LANES, (tile + 1) * LANES)
        w, b = weight[:, cols], bias[:, cols]
        totals = [jnp.zeros((1, LANES), F32)] * (KCONV + 1)
        after = jnp.zeros((8, LANES), F32)
        for at in range(length - ROWS_AT_ONCE, -1, -ROWS_AT_ONCE):
            terms = conv_terms(conv_in, at, cols)
            value = conv_sum(terms, w, b)
            sig = sigmoid(value)
            g = grad[at : at + ROWS_AT_ONCE, cols] * (sig * (1.0 + value * (1.0 - sig)))
            for k in range(KCONV):
                totals[k] = totals[k] + jnp.sum(g * terms[k], axis=0, keepdims=True)
            totals[KCONV] = totals[KCONV] + jnp.sum(g, axis=0, keepdims=True)
            total = g * w[KCONV - 1 : KCONV]
            for k in range(KCONV - 1):
                total = total + up(g, after, KCONV - 1 - k) * w[k : k + 1]
            after = g[:8]
            out[at : at + ROWS_AT_ONCE, cols] = total.astype(BF16)
        for k in range(KCONV + 1):
            sums[k : k + 1, cols] = totals[k]


def conv_backward(projected, grad_mixed, weight, bias, held):
    length = projected.shape[0]
    width = CONV_TILES * LANES
    return pl.pallas_call(
        conv_backward_kernel,
        grid=(CONVCH // width,),
        out_shape=(shape(held.shape, BF16), shape((8, CONVCH), F32)),
        in_specs=[
            pl.BlockSpec((length, width), lambda i: (0, INNER // width + i)),
            pl.BlockSpec((length, width), lambda i: (0, i)),
            pl.BlockSpec((KCONV, width), lambda i: (0, i)),
            pl.BlockSpec((1, width), lambda i: (0, i)),
            ANY,
        ],
        out_specs=(
            pl.BlockSpec((length, width), lambda i: (0, INNER // width + i)),
            pl.BlockSpec((8, width), lambda i: (0, i)),
        ),
        input_output_aliases={4: 0},
        compiler_params=params(),
        cost_estimate=cost(12),
    )(projected, grad_mixed, weight, bias, held)


def middle_kernel(
    limit, mixed_out, w_out, tokens, teacher, mask, ssm, gate, gain,
    block_out, grad_result, grad_branch, grad_ssm, grad_gate, error, gain_sums,
):
    step = pl.program_id(0)

    @pl.when(step == 0)
    def _():
        error[...] = jnp.zeros_like(error)
        gain_sums[...] = jnp.zeros_like(gain_sums)

    rows = tokens.shape[0]
    result = tokens[...].astype(F32) + dot(mixed_out[...], w_out[...])
    position = step * rows + lax.broadcasted_iota(jnp.int32, (rows, 1), 0)
    valid = (position < limit[0]).astype(F32)
    weight = valid * mask[:, 0:1]
    block_out[...] = (result * valid).astype(BF16)
    misfit = result - teacher[...].astype(F32)
    pulled = 2.0 * weight * misfit
    grad_result[...] = pulled
    error[...] += jnp.sum(0.5 * pulled * misfit, axis=0, keepdims=True)
    low = pulled.astype(BF16)
    grad_branch[...] = low
    grad_mixed = dot(low, w_out[...], NT)
    g = gate[...]
    sig = sigmoid(g)
    act = g * sig
    inner = ssm[...]
    gated = inner * act
    rho = lax.rsqrt(jnp.mean(gated * gated, axis=1, keepdims=True) + NORM_EPS)
    unit = gated * rho
    gain_sums[...] += jnp.sum(unit * grad_mixed, axis=0, keepdims=True)
    grad_unit = grad_mixed * gain[...]
    share = jnp.mean(grad_unit * unit, axis=1, keepdims=True)
    grad_gated = rho * (grad_unit - unit * share)
    grad_ssm[...] = grad_gated * act
    grad_gate[...] = (grad_gated * inner * (sig * (1.0 + g * (1.0 - sig)))).astype(BF16)


def middle(limit, mixed_out, w_out, tokens, teacher, mask, ssm, projected, gain):
    length = tokens.shape[0]
    rows = 256
    by_row = lambda width: pl.BlockSpec((rows, width), lambda i: (i, 0))
    whole = lambda v: pl.BlockSpec(v.shape, lambda i: (0,) * v.ndim)
    return pl.pallas_call(
        middle_kernel,
        grid=(length // rows,),
        out_shape=(
            shape((length, D), BF16),
            shape((length, D), F32),
            shape((length, D), BF16),
            shape((length, INNER), F32),
            shape((length, WIDE), BF16),
            shape((1, D), F32),
            shape((1, INNER), F32),
        ),
        in_specs=[
            SMEM,
            by_row(INNER),
            whole(w_out),
            by_row(D),
            by_row(D),
            by_row(LANES),
            by_row(INNER),
            by_row(INNER),
            whole(gain),
        ],
        out_specs=(
            by_row(D),
            by_row(D),
            by_row(D),
            by_row(INNER),
            by_row(INNER),
            pl.BlockSpec((1, D), lambda i: (0, 0)),
            pl.BlockSpec((1, INNER), lambda i: (0, 0)),
        ),
        compiler_params=params(),
        cost_estimate=cost(25),
    )(limit, mixed_out, w_out, tokens, teacher, mask, ssm, projected, gain)


def body(tokens, teacher, lengths, loss_mask, owners, master, first_moment, second_moment):
    capacity = master.shape[0]
    dp, fsdp = lax.axis_size("dp"), lax.axis_size("fsdp")
    devices = dp * fsdp
    me = lax.axis_index(AXES).astype(jnp.int32)
    x_first, y_first, z_first = step_orders(dp, fsdp)
    plan = make_plan(owners, capacity, devices, me)
    n0, n1 = plan["slots"]

    streams = cut(n0, (x_first, y_first, z_first))
    sent = send_blocks(plan["send_rows"], master)
    at_home = lax.all_to_all(sent, AXES, 0, 0, tiled=True)
    sizes = [size for _, size, _ in streams] + [n1]
    *mine, mine1 = pick_blocks(jnp.concatenate(plan["received"]), at_home, sizes)
    parts = []
    for values, (_, _, order) in zip(mine, streams):
        parts += gather_steps(values, order)
    *parts, mine1 = lax.optimization_barrier((*parts, mine1))
    held1 = lax.all_gather(mine1, AXES, axis=0, tiled=True)
    table = stream_places(plan["home"], plan["slot"], me, streams, devices)
    table0 = jnp.concatenate([table[:MID0], table[MID1:]])
    table1 = (plan["home"] * n1 + plan["slot"])[MID0:MID1]
    input_weight, head, tail, conv_weight, conv_bias, heads, skip, norm_gain, gate_gain = unpack_in(
        table0, parts
    )
    output_weight = unpack_out(table1, held1, head, tail)
    dt_bias, a_log = heads[0:1], heads[1:2]
    gather = heads_gather()

    inputs, target = tokens[0], teacher[0]
    mask = jnp.broadcast_to(loss_mask[0].astype(F32)[:, None], (inputs.shape[0], LANES))
    wide_in = inputs.astype(F32)
    inverse = lax.rsqrt(jnp.mean(wide_in * wide_in, axis=-1, keepdims=True) + NORM_EPS)
    normed = wide_in * inverse
    hidden = (normed * norm_gain).astype(BF16)
    projected = dot(hidden, input_weight)
    mixed = conv_forward(projected, conv_weight, conv_bias)
    ssm, mixed_out, states = scan_forward(mixed, projected, dt_bias, a_log, skip, gate_gain)
    block_out, grad_result, grad_branch, grad_ssm, grad_low, errors, grad_gate = middle(
        lengths, mixed_out, output_weight, inputs, target, mask, ssm, projected, gate_gain
    )
    position = jnp.arange(inputs.shape[0], dtype=jnp.int32)
    counted = jnp.sum(jnp.where(position < lengths[0], loss_mask[0], 0)).astype(F32)
    local = jnp.concatenate([errors.reshape(-1, LANES), jnp.broadcast_to(counted, (2, LANES))])
    grad_weight_out = dot(mixed_out, grad_branch, (((0,), (0,)), ((), ())))
    u0, u1 = plan["unit_slots"]
    unit_streams = cut(u0, (x_first, y_first, x_first, y_first, z_first))
    unit_table = stream_places(plan["unit_home"], plan["unit_slot"], me, unit_streams, devices)
    unit_table1 = plan["unit_home"] * (u1 + 1) + plan["unit_slot"]
    packed1, head, tail = pack_out(
        unit_table1[MID0:MID1].reshape(-1), grad_weight_out, local, devices, u1 + 1
    )
    grad_ssm, packed1 = lax.optimization_barrier((grad_ssm, packed1))
    sum1 = lax.psum_scatter(packed1, "dp", scatter_dimension=0, tiled=True)
    grad_mixed, grad_low, sums, skip_sums = scan_backward(
        mixed, projected, ssm, grad_ssm, states, dt_bias, a_log, skip, gather, grad_low
    )
    grad_low, conv_sums = conv_backward(projected, grad_mixed, conv_weight, conv_bias, grad_low)
    halves = []
    for _, size, _ in unit_streams:
        halves += [devices * size // 2] * 2
    packed = pack_in(unit_table[:MID0].reshape(-1), hidden, grad_low, head, halves)
    grad_hidden = dot(grad_low, input_weight, NT)
    grad_norm = jnp.sum(grad_hidden * normed, axis=0)
    grad_normed = grad_hidden * norm_gain
    input_grad = grad_result + inverse * (
        grad_normed - normed * jnp.mean(grad_normed * normed, axis=-1, keepdims=True)
    )
    grad_vec = jnp.concatenate(
        [
            conv_sums[:KCONV].T.reshape(-1),
            conv_sums[KCONV],
            sums[0, :HEADS],
            sums[1, :HEADS],
            jnp.sum(skip_sums.reshape(HEADS, HEADDIM), axis=1),
            grad_norm,
            grad_gate[0],
            jnp.zeros((NBLK * PBLOCK - PTOT,), F32),
        ]
    ).reshape(VEC_ROWS, LANES)
    grad_vec = jnp.concatenate([tail, grad_vec]).reshape((NBLK - MID1) * UNITS, UNIT, LANES)
    sums = []
    for i, (_, _, order) in enumerate(unit_streams):
        sums.append(reduce_step(packed[2 * i] + exchange(packed[2 * i + 1], order[0]), order[1]))
    for step in x_first[:2]:
        grad_vec = grad_vec + exchange(grad_vec, step)
    sums[0], grad_vec, input_grad = lax.optimization_barrier((sums[0], grad_vec, input_grad))
    for k in range(2, len(x_first) - 1):
        sums[0], grad_vec = reduce_step(sums[0], x_first[k], grad_vec)
        for i in range(1, len(sums)):
            sums[i] = reduce_step(sums[i], unit_streams[i][2][k])
    ends = []
    for i, values in enumerate(sums):
        half = values.shape[0] // 2
        given, step = values[half:], unit_streams[i][2][-1]
        if i == 0:
            got = exchange(jnp.concatenate([given, grad_vec]), step)
            grad_vec = grad_vec + got[half:]
            got = got[:half]
        else:
            got = exchange(given, step)
        ends += [values[:half], got]
    kept1 = sum1
    for bit in reversed(range(bits_of(fsdp))):
        half = kept1.shape[0] // 2
        upper = (lax.axis_index("fsdp") >> bit) & 1
        halves = kept1.reshape((2, half) + kept1.shape[1:])
        given = lax.dynamic_index_in_dim(halves, 1 - upper, 0, keepdims=False)
        kept1 = lax.dynamic_index_in_dim(halves, upper, 0, keepdims=False)
        got1 = exchange(given, ("fsdp", bit))
        if bit:
            kept1 = kept1 + got1
    back = units_to_owners(plan["back"], ends + [kept1, got1])
    got = lax.all_to_all(back, AXES, 0, 0, tiled=True)
    local_sums = kept1[u1] + got1[u1]
    error_sum = jnp.sum(local_sums[: D // LANES])
    divisor = local_sums[D // LANES, 0] * D
    new_first, new_second, new_master = adam(
        plan["row_from"],
        divisor,
        got,
        grad_vec,
        plan["row_block"],
        plan["row_used"],
        master,
        first_moment,
        second_moment,
    )
    mean_loss = error_sum / divisor
    return (block_out[None], input_grad[None], mean_loss, new_first, new_second, new_master)


def solution(mesh):
    return jax.shard_map(
        body,
        mesh=mesh,
        in_specs=(
            P(AXES, None, None),
            P(AXES, None, None),
            P(AXES),
            P(AXES, None),
            P(),
            P(AXES, None),
            P(AXES, None),
            P(AXES, None),
        ),
        out_specs=(
            P(AXES, None, None),
            P(AXES, None, None),
            P(),
            P(AXES, None),
            P(AXES, None),
            P(AXES, None),
        ),
        check_vma=False,
    )
```

```python
from functools import partial

import jax
import jax.numpy as jnp
import numpy as np
from jax import lax
from jax.experimental import pallas as pl
from jax.experimental.pallas import tpu as pltpu
from jax.sharding import PartitionSpec as P

D = 768
INNER = 1536
NSTATE = 128
HEADDIM = 64
KCONV = 4
SCAN_LEN = 256
PBLOCK = 4096
STEP = 10
HEADS = 24
CONVCH = 1792
PROJ = 3352
PTOT = 3765320
NBLK = 920

LANES = 128
BROWS = PBLOCK // LANES
UNIT = 8
UNITS = BROWS // UNIT
END_IN = D * PROJ
END_OUT = END_IN + INNER * D
MID0 = -(-END_IN // PBLOCK)
MID1 = END_OUT // PBLOCK
N0 = MID0 + NBLK - MID1
N1 = MID1 - MID0
F0_ROWS = N0 * BROWS
IN_ROWS = END_IN // LANES
HEAD_ROWS = MID0 * BROWS - IN_ROWS
TAIL_ROWS = (END_OUT - MID1 * PBLOCK) // LANES
OUT_ROWS = INNER * D // LANES
VEC_ROWS = (NBLK - MID1) * BROWS - TAIL_ROWS
VEC_AT = MID0 * BROWS + TAIL_ROWS
GROUP = 16
GROUPS = D // GROUP
GROUP_ROWS = GROUP * PROJ // LANES
COL_TILES = -(-PROJ // LANES)
WIDE = COL_TILES * LANES
OUT_TILES = D // LANES

NORM_EPS = 1e-05
ADAM_EPS = 1e-08
BETA_ONE = 0.9
BETA_TWO = 0.999
MATRIX_RATE = 0.03
VECTOR_RATE = 0.2
WEIGHT_DECAY = 0.1
PRECISE = lax.Precision.HIGHEST
AXES = ("dp", "fsdp")
VMEM_LIMIT = 60 * 1024 * 1024


def bits_of(count):
    return count.bit_length() - 1


def step_orders(dp, fsdp):
    wide = [("dp", i) for i in range(bits_of(dp))]
    narrow = [("fsdp", i) for i in range(bits_of(fsdp))]
    first = wide[:2] + narrow + wide[2:]
    second = wide[:1] + narrow + wide[1:]
    third = wide[:1] + wide[2:] + wide[1:2] + narrow
    return first, second, third


def cut(total, orders):
    base, more = divmod(total, len(orders))
    streams, at = [], 0
    for i, order in enumerate(orders):
        size = base + (i < more)
        if size:
            streams.append((at, size, order))
        at += size
    return streams


def exchange(values, step):
    axis, bit = step
    size = lax.axis_size(axis)
    return lax.ppermute(values, axis, [(i, i ^ (1 << bit)) for i in range(size)])


def place_of(relative, order):
    shift_of = {"dp": bits_of(lax.axis_size("fsdp")), "fsdp": 0}
    place = jnp.zeros_like(relative)
    for axis, bit in order:
        place = place * 2 + ((relative >> (shift_of[axis] + bit)) & 1)
    return place


def class_counts(owners, devices):
    block = jnp.arange(NBLK, dtype=jnp.int32)
    mid = ((block >= MID0) & (block < MID1))[None, :]
    device = jnp.arange(devices, dtype=jnp.int32)
    below = owners[None, :] < device[:, None]
    owned = owners[None, :] == device[:, None]

    def total(mask):
        return jnp.sum(mask.astype(jnp.int32), axis=1)

    start = (total(below & ~mid), total(below & mid))
    count = (total(owned & ~mid), total(owned & mid))
    return start, count, total(owned & (block < MID0)[None, :])


def my_counts(owners, me):
    block = jnp.arange(NBLK, dtype=jnp.int32)
    mid = (block >= MID0) & (block < MID1)
    below, owned = owners < me, owners == me
    total = lambda mask: jnp.sum(mask.astype(jnp.int32))
    start = (total(below & ~mid), total(below & mid))
    count = (total(owned & ~mid), total(owned & mid))
    return start, count, total(owned & (block < MID0))


def pair_lanes(capacity, devices):
    return 2 + max(capacity - 2, 0) // devices


def send_plan(owners, capacity, devices, me):
    start, count, early = my_counts(owners, me)
    pair = pair_lanes(capacity, devices)
    device = jnp.arange(devices, dtype=jnp.int32)
    lane = jnp.arange(pair, dtype=jnp.int32)
    k0 = (device[:, None] - start[0]) % devices + lane[None, :] * devices
    k1 = (device[:, None] - start[1]) % devices + (pair - 1 - lane)[None, :] * devices
    row0 = jnp.where(k0 < early, k0, k0 + count[1])
    rows = jnp.where(k0 < count[0], row0, jnp.where(k1 < count[1], early + k1, 0))
    return rows.reshape(-1)


def make_plan(owners, capacity, devices, me):
    block = jnp.arange(NBLK, dtype=jnp.int32)
    mid = (block >= MID0) & (block < MID1)
    same = mid[:, None] == mid[None, :]
    before = (owners[None, :] < owners[:, None]) | (
        (owners[None, :] == owners[:, None]) & (block[None, :] < block[:, None])
    )
    order_in_class = jnp.sum((same & before).astype(jnp.int32), axis=1)
    home, slot = order_in_class % devices, order_in_class // devices
    device = jnp.arange(devices, dtype=jnp.int32)
    start, count, _ = class_counts(owners, devices)
    my_start, my_count, my_early = my_counts(owners, me)
    pair = pair_lanes(capacity, devices)

    slots = (-(-N0 // devices), -(-N1 // devices))

    def received(kind):
        wanted = me + devices * jnp.arange(slots[kind], dtype=jnp.int32)
        ends = start[kind] + count[kind]
        owner = jnp.sum((ends[None, :] <= wanted[:, None]).astype(jnp.int32), axis=1)
        owner = jnp.minimum(owner, devices - 1)
        base = jnp.sum(jnp.where(device[None, :] == owner[:, None], start[kind][None, :], 0), axis=1)
        turn = jnp.clip((wanted - base) // devices, 0, pair - 1)
        return owner * pair + (turn if kind == 0 else pair - 1 - turn)

    back_pair = (UNITS * capacity + 2 * (devices - 1)) // devices
    unit = UNITS * order_in_class[:, None] + jnp.arange(UNITS, dtype=jnp.int32)[None, :]
    unit_home, unit_slot = unit % devices, unit // devices
    unit_slots = (-(-UNITS * N0 // devices), -(-UNITS * N1 // devices))
    lane = jnp.arange(back_pair, dtype=jnp.int32)

    def units_back(kind):
        turn = lane if kind == 0 else back_pair - 1 - lane
        first = UNITS * start[kind][:, None]
        k = (me - first) % devices + turn[None, :] * devices
        return k < UNITS * count[kind][:, None], (first + k) // devices

    valid0, slot0 = units_back(0)
    valid1, slot1 = units_back(1)
    back = jnp.where(valid0, slot0, jnp.where(valid1, unit_slots[0] + slot1, 0)).reshape(-1)

    row = jnp.arange(capacity, dtype=jnp.int32)
    is_mid = (row >= my_early) & (row < my_early + my_count[1])
    k = jnp.where(is_mid, row - my_early, jnp.where(row < my_early, row, row - my_count[1]))
    first = UNITS * jnp.where(is_mid, my_start[1], my_start[0])
    k = UNITS * k[:, None] + jnp.arange(UNITS, dtype=jnp.int32)[None, :]
    turn = k // devices
    row_from = ((first[:, None] + k) % devices) * back_pair + jnp.where(
        is_mid[:, None], back_pair - 1 - turn, turn
    )
    row_used = row < my_count[0] + my_count[1]
    mine = (owners == me)[None, :]
    rank = jnp.sum((mine & (block[None, :] < block[:, None])).astype(jnp.int32), axis=1)
    row_block = jnp.sum(
        jnp.where(mine & (rank[None, :] == row[:, None]), block[None, :], 0), axis=1
    )
    late = devices * back_pair + UNITS * (row_block - MID1)
    late = late[:, None] + jnp.arange(UNITS, dtype=jnp.int32)[None, :]
    row_from = jnp.where((row_block >= MID1)[:, None], late, row_from)
    row_from = jnp.where(row_used[:, None], row_from, 0).reshape(-1)
    return dict(
        home=home, slot=slot, slots=slots,
        received=(received(0), received(1)), unit_home=unit_home, unit_slot=unit_slot,
        unit_slots=unit_slots, back=back, row_from=row_from,
        row_used=row_used, row_block=row_block,
    )


def stream_places(home, slot, me, streams, devices):
    relative = home ^ me
    place = jnp.zeros_like(slot)
    for begin, size, order in streams:
        inside = (slot >= begin) & (slot < begin + size)
        at = devices * begin + place_of(relative, order) * size + slot - begin
        place = jnp.where(inside, at, place)
    return place


def cost(microseconds):
    return pl.CostEstimate(
        flops=int(microseconds * 1e9), bytes_accessed=int(microseconds * 3e6), transcendentals=0
    )


ANY = pl.BlockSpec(memory_space=pl.ANY)
VMEM = pl.BlockSpec(memory_space=pltpu.VMEM)
SMEM = pl.BlockSpec(memory_space=pltpu.SMEM)


def params(**extra):
    return pltpu.CompilerParams(vmem_limit_bytes=VMEM_LIMIT, **extra)


def shape(dims, dtype):
    return jax.ShapeDtypeStruct(dims, dtype)


def send_kernel(table, master, out, flat):
    capacity = master.shape[0]
    for j in range(BROWS):
        flat[pl.ds(j, capacity, stride=BROWS), :] = master[:, j * LANES : (j + 1) * LANES]

    def step(i, carry):
        out[i] = flat[pl.ds(pl.multiple_of(table[i] * BROWS, BROWS), BROWS), :].astype(out.dtype)
        return carry

    lax.fori_loop(0, out.shape[0], step, 0)


def send_blocks(table, master):
    return pl.pallas_call(
        send_kernel,
        out_shape=shape((table.shape[0], BROWS, LANES), jnp.bfloat16),
        in_specs=[SMEM, VMEM],
        out_specs=VMEM,
        scratch_shapes=[pltpu.VMEM((master.shape[0] * BROWS, LANES), jnp.float32)],
        compiler_params=params(),
    )(table, master)


def pick_kernel(table, source, *outs):
    at = 0
    for out in outs:

        def step(i, carry, out=out, at=at):
            out[i] = source[table[at + i]]
            return carry

        lax.fori_loop(0, out.shape[0], step, 0)
        at += out.shape[0]


def pick_blocks(table, source, sizes):
    return pl.pallas_call(
        pick_kernel,
        out_shape=tuple(shape((n,) + source.shape[1:], source.dtype) for n in sizes),
        in_specs=[SMEM, VMEM],
        out_specs=(VMEM,) * len(sizes),
        compiler_params=params(),
    )(table, source)


def back_kernel(table, *refs):
    sources, (out, held) = refs[:-2], refs[-2:]
    at = 0
    for i in range(0, len(sources), 2):
        n = sources[i].shape[0]
        held[at : at + n] = sources[i][...] + sources[i + 1][...]
        at += n

    def step(i, carry):
        for u in range(8):
            out[i * 8 + u] = held[table[i * 8 + u]]
        return carry

    total = out.shape[0]
    lax.fori_loop(0, total // 8, step, 0)


def units_to_owners(table, sources):
    return pl.pallas_call(
        back_kernel,
        out_shape=shape((table.shape[0], UNIT, LANES), jnp.float32),
        in_specs=[SMEM] + [VMEM] * len(sources),
        out_specs=VMEM,
        scratch_shapes=[
            pltpu.VMEM((sum(s.shape[0] for s in sources[::2]), UNIT, LANES), jnp.float32)
        ],
        compiler_params=params(),
    )(table, *sources)


def row_start(rho):
    return (PROJ * rho) // LANES, (PROJ * rho) % LANES


def copy_all(pairs, sem):
    copies = [pltpu.make_async_copy(a, b, sem.at[i]) for i, (a, b) in enumerate(pairs)]
    for c in copies:
        c.start()
    for c in copies:
        c.wait()


def spread_blocks(table, held, flat, count, first_row):
    def one(i):
        at = pl.multiple_of(first_row + i * BROWS, 16)
        flat[pl.ds(at, BROWS), :] = held[table[i]].astype(jnp.float32)

    def step(i, carry):
        for u in range(4):
            one(i * 4 + u)
        return carry

    lax.fori_loop(0, count // 4, step, 0)
    for i in range(count // 4 * 4, count):
        one(i)


def unpack_vectors(flat, conv_weight, conv_bias, heads, skip, norm_gain, gate_gain):
    bf16, f32 = jnp.bfloat16, jnp.float32
    tiles = CONVCH // LANES
    row = lax.broadcasted_iota(jnp.int32, (LANES, LANES), 0)
    col = lax.broadcasted_iota(jnp.int32, (LANES, LANES), 1)
    per_tile = LANES // KCONV
    for k in range(KCONV):
        total = jnp.zeros((tiles, LANES), f32)
        for q in range(KCONV):
            rows = flat[pl.ds(VEC_AT + q, tiles, stride=KCONV), :].astype(bf16)
            chosen = (row == KCONV * (col % per_tile) + k) & (col // per_tile == q)
            total = total + jnp.dot(rows, chosen.astype(bf16), preferred_element_type=f32)
        for i in range(tiles):
            conv_weight[k : k + 1, i * LANES : (i + 1) * LANES] = total[i : i + 1, :]
    bias_at = VEC_AT + tiles * KCONV
    for i in range(tiles):
        conv_bias[:, i * LANES : (i + 1) * LANES] = flat[bias_at + i : bias_at + i + 1, :]
    at = bias_at + tiles
    lane = lax.broadcasted_iota(jnp.int32, (8, LANES), 1)
    first = flat[at : at + 8, :]
    three = []
    for i in range(3):
        moved = pltpu.roll(first, LANES - i * HEADS, 1) if i else first
        three.append(jnp.where(lane < HEADS, moved, 0.0))
        heads[i : i + 1, :] = three[i][0:1, :]
    for j in range(INNER // LANES):
        h = lax.broadcasted_iota(jnp.int32, (LANES, LANES), 0)
        c = lax.broadcasted_iota(jnp.int32, (LANES, LANES), 1) + j * LANES
        spread = (h == c // HEADDIM).astype(bf16)
        wide = jnp.dot(three[2].astype(bf16), spread, preferred_element_type=f32)
        skip[:, j * LANES : (j + 1) * LANES] = wide[0:1, :]
    shift = 3 * HEADS
    for out, begin, width in ((norm_gain, at, D), (gate_gain, at + D // LANES, INNER)):
        for j in range(width // LANES):
            x = pltpu.roll(flat[begin + j : begin + j + 1, :], LANES - shift, 1)
            y = pltpu.roll(flat[begin + j + 1 : begin + j + 2, :], LANES - shift, 1)
            out[:, j * LANES : (j + 1) * LANES] = jnp.where(lane[0:1] < LANES - shift, x, y)


def unpack_in_kernel(table, *refs):
    parts, (w_in, head, tail, *vectors), (held, flat, tile, sem) = refs[:-13], refs[-13:-4], refs[-4:]
    pairs, at = [], 0
    for part in parts:
        pairs.append((part, held.at[pl.ds(at, part.shape[0])]))
        at += part.shape[0]
    copy_all(pairs, sem)
    spread_blocks(table, held, flat, N0, 0)
    head[...] = flat[IN_ROWS : IN_ROWS + HEAD_ROWS, :]
    tail[...] = flat[MID0 * BROWS : MID0 * BROWS + TAIL_ROWS, :]
    unpack_vectors(flat, *vectors)
    lane = lax.broadcasted_iota(jnp.int32, (GROUPS, LANES), 1)

    def columns(j):
        for rho in range(GROUP):
            c, s = row_start(rho)
            x = flat[pl.ds(c + j, GROUPS, stride=GROUP_ROWS), :]
            if s:
                y = flat[pl.ds(c + j + 1, GROUPS, stride=GROUP_ROWS), :]
                x = jnp.where(
                    lane < LANES - s,
                    pltpu.roll(x, LANES - s, 1),
                    pltpu.roll(y, LANES - s, 1),
                )
            tile[pl.ds(rho, GROUPS, stride=GROUP), :] = x

    def step(j, carry):
        columns(j)
        w_in[:, pl.ds(pl.multiple_of(j * LANES, LANES), LANES)] = tile[...].astype(jnp.bfloat16)
        return carry

    lax.fori_loop(0, COL_TILES - 1, step, 0)
    columns(COL_TILES - 1)
    last = (COL_TILES - 1) * LANES
    inside = lax.broadcasted_iota(jnp.int32, (D, LANES), 1) < PROJ - last
    w_in[:, last:] = jnp.where(inside, tile[...], 0.0).astype(jnp.bfloat16)


def unpack_in(table, parts):
    held = sum(part.shape[0] for part in parts)
    return pl.pallas_call(
        unpack_in_kernel,
        out_shape=(
            shape((D, WIDE), jnp.bfloat16),
            shape((HEAD_ROWS, LANES), jnp.float32),
            shape((TAIL_ROWS, LANES), jnp.float32),
            shape((KCONV, CONVCH), jnp.float32),
            shape((1, CONVCH), jnp.float32),
            shape((8, LANES), jnp.float32),
            shape((1, INNER), jnp.float32),
            shape((1, D), jnp.float32),
            shape((1, INNER), jnp.float32),
        ),
        in_specs=[SMEM] + [ANY] * len(parts),
        out_specs=(VMEM,) * 9,
        scratch_shapes=[
            pltpu.VMEM((held, BROWS, LANES), jnp.bfloat16),
            pltpu.VMEM((F0_ROWS, LANES), jnp.float32),
            pltpu.VMEM((D, LANES), jnp.float32),
            pltpu.SemaphoreType.DMA((len(parts),)),
        ],
        compiler_params=params(),
        cost_estimate=cost(16),
    )(table, *parts)


def unpack_out_kernel(table, own, got, head, tail, w_out, flat, held, sem):
    half = own.shape[0]
    copy_all([(own, held.at[pl.ds(0, half)]), (got, held.at[pl.ds(half, half)])], sem)
    flat[0:HEAD_ROWS, :] = head[...]
    flat[OUT_ROWS - TAIL_ROWS : OUT_ROWS, :] = tail[...]
    spread_blocks(table, held, flat, N1, HEAD_ROWS)
    rows = 128

    def step(i, carry):
        at = pl.multiple_of(i * rows, rows)
        for j in range(OUT_TILES):
            x = flat[pl.ds(at * OUT_TILES + j, rows, stride=OUT_TILES), :]
            w_out[pl.ds(at, rows), j * LANES : (j + 1) * LANES] = x.astype(jnp.bfloat16)
        return carry

    lax.fori_loop(0, INNER // rows, step, 0)


def unpack_out(table, own, got, head, tail):
    return pl.pallas_call(
        unpack_out_kernel,
        out_shape=shape((INNER, D), jnp.bfloat16),
        in_specs=[SMEM, ANY, ANY, VMEM, VMEM],
        out_specs=VMEM,
        scratch_shapes=[
            pltpu.VMEM((OUT_ROWS, LANES), jnp.float32),
            pltpu.VMEM((2 * own.shape[0], BROWS, LANES), jnp.bfloat16),
            pltpu.SemaphoreType.DMA((2,)),
        ],
        compiler_params=params(),
    )(table, own, got, head, tail)


def permute_units(table, flat, count, first_row, staged):
    many = 16

    def step(i, carry):
        for u in range(many):
            at = pl.multiple_of(first_row + (i * many + u) * UNIT, UNIT)
            staged[table[i * many + u]] = flat[pl.ds(at, UNIT), :]
        return carry

    lax.fori_loop(0, count // many, step, 0)
    for i in range(count // many * many, count):
        staged[table[i]] = flat[first_row + i * UNIT : first_row + (i + 1) * UNIT, :]


def pack_in_kernel(table, hidden, grad, head, *refs):
    outs, (turned, tiles, flat, staged, sem) = refs[:-5], refs[-5:]
    turned[...] = hidden[...].T
    lane = lax.broadcasted_iota(jnp.int32, (GROUPS, LANES), 1)

    def product(p, count):
        at = p * 2 * LANES
        at = at if isinstance(at, int) else pl.multiple_of(at, 2 * LANES)
        return jnp.dot(
            turned[...], grad[:, pl.ds(at, count * LANES)], preferred_element_type=jnp.float32
        )

    def put(p, value):
        for k in range(value.shape[1] // LANES):
            at = (p * 2 + k) * D
            at = at if isinstance(at, int) else pl.multiple_of(at, D)
            tiles[pl.ds(at, D), :] = value[:, k * LANES : (k + 1) * LANES]

    def load(rho, j):
        return tiles[pl.ds(j * D + rho, GROUPS, stride=GROUP), :]

    def whole(rho, i):
        first = -(-PROJ * rho // LANES)
        col0 = first * LANES - PROJ * rho
        x = load(rho, i)
        if col0:
            x = jnp.where(
                lane < LANES - col0,
                pltpu.roll(x, LANES - col0, 1),
                pltpu.roll(load(rho, i + 1), LANES - col0, 1),
            )
        flat[pl.ds(first + i, GROUPS, stride=GROUP_ROWS), :] = x

    put(0, product(0, 2))
    put(1, product(1, 2))
    pairs = COL_TILES // 2

    def step(p, carry):
        for i in range(2):
            for rho in range(GROUP):
                whole(rho, p * 2 + i)
        put(p + 2, product(p + 2, 2))
        return carry

    lax.fori_loop(0, pairs - 2, step, 0)
    put(pairs, product(pairs, COL_TILES % 2))
    for rho in range(GROUP):
        first = -(-PROJ * rho // LANES)
        col0 = first * LANES - PROJ * rho
        full = (PROJ - col0) // LANES
        for i in range((pairs - 2) * 2, full):
            whole(rho, i)
        left = PROJ - col0 - full * LANES
        if left:
            begin = col0 + full * LANES
            j, s = begin // LANES, begin % LANES
            x = pltpu.roll(load(rho, j), LANES - s, 1) if s else load(rho, j)
            if s + left > LANES:
                x = jnp.where(lane < LANES - s, x, pltpu.roll(load(rho, j + 1), LANES - s, 1))
            y = pltpu.roll(load(rho + 1, 0), left, 1)
            flat[pl.ds(first + full, GROUPS, stride=GROUP_ROWS), :] = jnp.where(lane < left, x, y)
    flat[IN_ROWS : IN_ROWS + HEAD_ROWS, :] = head[...]
    permute_units(table, flat, MID0 * UNITS, 0, staged)
    copies, at = [], 0
    for out in outs:
        copies.append((staged.at[pl.ds(at, out.shape[0])], out))
        at += out.shape[0]
    copy_all(copies, sem)


def pack_in(table, hidden, grad, head, sizes):
    return pl.pallas_call(
        pack_in_kernel,
        out_shape=tuple(shape((n, UNIT, LANES), jnp.float32) for n in sizes),
        in_specs=[SMEM, VMEM, VMEM, VMEM],
        out_specs=(ANY,) * len(sizes),
        scratch_shapes=[
            pltpu.VMEM((D, hidden.shape[0]), jnp.bfloat16),
            pltpu.VMEM((COL_TILES * D, LANES), jnp.float32),
            pltpu.VMEM((MID0 * BROWS, LANES), jnp.float32),
            pltpu.VMEM((sum(sizes), UNIT, LANES), jnp.float32),
            pltpu.SemaphoreType.DMA((len(sizes),)),
        ],
        compiler_params=params(),
        cost_estimate=cost(20),
    )(table, hidden, grad, head)


def pack_out_kernel(table, grad, local, keep, send, head, tail, flat, out, sem, *, slots):
    rows = 128

    def step(i, carry):
        at = pl.multiple_of(i * rows, rows)
        for j in range(OUT_TILES):
            flat[pl.ds(at * OUT_TILES + j, rows, stride=OUT_TILES), :] = grad[
                pl.ds(at, rows), j * LANES : (j + 1) * LANES
            ]
        return carry

    lax.fori_loop(0, INNER // rows, step, 0)
    head[...] = flat[0:HEAD_ROWS, :]
    tail[...] = flat[OUT_ROWS - TAIL_ROWS : OUT_ROWS, :]
    permute_units(table, flat, N1 * UNITS, HEAD_ROWS, out)

    def add_local(i, carry):
        out[i * slots + slots - 1] = local[...]
        return carry

    lax.fori_loop(0, out.shape[0] // slots, add_local, 0)
    half = keep.shape[0]
    copy_all([(out.at[pl.ds(0, half)], keep), (out.at[pl.ds(half, half)], send)], sem)


def pack_out(table, grad, local, devices, slots):
    return pl.pallas_call(
        partial(pack_out_kernel, slots=slots),
        out_shape=(
            shape((devices * slots // 2, UNIT, LANES), jnp.float32),
            shape((devices * slots // 2, UNIT, LANES), jnp.float32),
            shape((HEAD_ROWS, LANES), jnp.float32),
            shape((TAIL_ROWS, LANES), jnp.float32),
        ),
        in_specs=[SMEM, VMEM, VMEM],
        out_specs=(ANY, ANY, VMEM, VMEM),
        scratch_shapes=[
            pltpu.VMEM((OUT_ROWS, LANES), jnp.float32),
            pltpu.VMEM((devices * slots, UNIT, LANES), jnp.float32),
            pltpu.SemaphoreType.DMA((2,)),
        ],
        compiler_params=params(),
    )(table, grad, local)


def adam_kernel(table, scale, got, late, limit, used, master, first, second, o_first, o_second, o_master, flat, held):
    capacity = master.shape[0]

    def step(i, carry):
        for u in range(UNITS):
            at = table[i * UNITS + u]
            rows = pl.ds(pl.multiple_of(i * BROWS + u * UNIT, UNIT), UNIT)
            flat[rows, :] = held[at]
        return carry

    held[0 : got.shape[0]] = got[...]
    held[got.shape[0] :] = late[...]
    lax.fori_loop(0, capacity, step, 0)
    lane = lax.broadcasted_iota(jnp.int32, (capacity, LANES), 1)
    divisor = scale[0]
    for j in range(BROWS):
        cols = slice(j * LANES, (j + 1) * LANES)
        grad = jnp.where(used[...] > 0, flat[pl.ds(j, capacity, stride=BROWS), :], 0.0) / divisor
        matrix = lane + j * LANES < limit[...]
        weights = master[:, cols]
        new_first = BETA_ONE * first[:, cols] + (1.0 - BETA_ONE) * grad
        new_second = BETA_TWO * second[:, cols] + (1.0 - BETA_TWO) * grad * grad
        normal = (
            new_first
            / (1.0 - BETA_ONE**STEP)
            / (jnp.sqrt(new_second / (1.0 - BETA_TWO**STEP)) + ADAM_EPS)
        )
        rate = jnp.where(matrix, MATRIX_RATE, VECTOR_RATE)
        decay = jnp.where(matrix, WEIGHT_DECAY, 0.0)
        o_first[:, cols] = new_first
        o_second[:, cols] = new_second
        o_master[:, cols] = weights - rate * (normal + decay * weights)


def adam(table, divisor, got, late, limit, used, master, first, second):
    capacity = master.shape[0]
    return pl.pallas_call(
        adam_kernel,
        out_shape=(shape(master.shape, jnp.float32),) * 3,
        in_specs=[SMEM, SMEM] + [VMEM] * 7,
        out_specs=(VMEM,) * 3,
        scratch_shapes=[
            pltpu.VMEM((capacity * BROWS, LANES), jnp.float32),
            pltpu.VMEM((got.shape[0] + late.shape[0], UNIT, LANES), jnp.float32),
        ],
        compiler_params=params(),
    )(table, divisor.reshape(1), got, late, limit, used, master, first, second)


def doubled(values, step):
    return jnp.concatenate([values, exchange(values, step)], axis=0)


def gather_steps(values, order):
    for step in order[:0:-1]:
        values = doubled(values, step)
    return values, exchange(values, order[0])


def reduce_step(values, step, extra=None):
    half = values.shape[0] // 2
    if extra is None:
        return values[:half] + exchange(values[half:], step)
    got = exchange(jnp.concatenate([values[half:], extra]), step)
    return values[:half] + got[:half], extra + got[half:]


CHUNK = 128
PAIRS = HEADS // 2
MIXW = INNER + 2 * NSTATE
DT_AT = INNER + CONVCH
F32 = jnp.float32
BF16 = jnp.bfloat16
NN = (((1,), (0,)), ((), ()))
NT = (((1,), (1,)), ((), ()))


def dot(a, b, dims=NN):
    return lax.dot_general(a, b, dims, preferred_element_type=F32)


def split(v):
    high = v.astype(BF16)
    return high, (v - high.astype(F32)).astype(BF16)


def dot3(a, b, dims=NN):
    ah, al = a
    bh, bl = b
    return dot(ah, bh, dims) + (dot(ah, bl, dims) + dot(al, bh, dims))


def heads_gather():
    return jnp.asarray(np.repeat(np.eye(HEADS, LANES, dtype=np.float32), HEADDIM, axis=0), BF16)


def three_parts(v):
    high = v.astype(BF16).astype(F32)
    rest = v - high
    middle = rest.astype(BF16).astype(F32)
    low = rest - middle
    return (high + pltpu.roll(middle, 32, 1) + pltpu.roll(low, 64, 1)).astype(BF16)


def triangle_sum(tri, v):
    parts = dot(tri, three_parts(v))
    lane = lax.broadcasted_iota(jnp.int32, parts.shape, 1)
    total = parts + pltpu.roll(parts, LANES - 32, 1) + pltpu.roll(parts, LANES - 64, 1)
    return jnp.where(lane < HEADS, total, 0.0)


def chunk_decays(dt, dt_bias, a_log):
    lane = lax.broadcasted_iota(jnp.int32, (CHUNK, LANES), 1)
    row = lax.broadcasted_iota(jnp.int32, (CHUNK, LANES), 0)
    shifted = dt + dt_bias
    delta = jnp.where(
        lane < HEADS, jnp.maximum(shifted, 0.0) + jnp.log1p(jnp.exp(-jnp.abs(shifted))), 0.0
    )
    rate = -jnp.exp(a_log)
    lower = (row >= lane).astype(BF16)
    cum = triangle_sum(lower, delta * rate)
    last = cum[CHUNK - 1 : CHUNK, :]
    return shifted, delta, rate, cum, last


def pair_mask():
    lane = lax.broadcasted_iota(jnp.int32, (CHUNK, LANES), 1)
    low = (lane < HEADDIM).astype(F32)
    return low.astype(BF16), (1.0 - low).astype(BF16)


QUADS = HEADS // 4
QWIDTH = 4 * HEADDIM


def sigmoid(v):
    return 0.5 * jnp.tanh(0.5 * v) + 0.5


def silu(v):
    return v * sigmoid(v)


def side_by_side(v):
    high, low = split(v)
    return jnp.concatenate([high, low], axis=1), high


def dot_parts(a, b):
    ahl, ah = a
    bh, bl = b
    return dot(ahl, jnp.concatenate([bh, bh], axis=0)) + dot(ah, bl)


def dot_turned(a, b):
    ah, al = a
    bh, bl = b
    both = dot(ah, jnp.concatenate([bh, bl], axis=0), NT)
    n = bh.shape[0]
    return both[:, :n] + both[:, n:] + dot(al, bh, NT)


def widen(delta, cum, quad):
    lane = lax.broadcasted_iota(jnp.int32, (CHUNK, LANES), 1)
    over = lambda v, h: jnp.broadcast_to(v[:, h : h + 1], (CHUNK, LANES))
    first = 4 * quad
    columns = [over(cum, first + k) for k in range(4)]
    rates = [over(delta, first + k) for k in range(4)]
    pair = lambda vs: jnp.concatenate(
        [jnp.where(lane < HEADDIM, vs[0], vs[1]), jnp.where(lane < HEADDIM, vs[2], vs[3])], axis=1
    )
    return pair(rates), pair(columns), columns


def pair_rows(parts, j, low, high):
    cols = slice(j * LANES, (j + 1) * LANES)
    return [jnp.concatenate([p[:, cols] * low, p[:, cols] * high], axis=0) for p in parts]


def scan_forward_kernel(
    mixed, dt, gate, dt_bias, a_log, skip, gain, ssm, mixed_out, states, state
):
    @pl.when(pl.program_id(0) == 0)
    def _():
        state[...] = jnp.zeros_like(state)

    states[0] = state[...]
    _, delta, _, cum, last = chunk_decays(dt[...], dt_bias[...], a_log[...])
    lane = lax.broadcasted_iota(jnp.int32, (CHUNK, LANES), 1)
    row = lax.broadcasted_iota(jnp.int32, (CHUNK, LANES), 0)
    bias = jnp.where(row >= lane, 0.0, -1e30)
    cum_t = cum.T
    inputs_b = mixed[:, INNER : INNER + NSTATE]
    readout = mixed[:, INNER + NSTATE :]
    affinity = dot3(split(readout), split(inputs_b), NT)
    readout_parts = side_by_side(readout)
    b_parts = side_by_side(inputs_b.T)
    low, high = pair_mask()
    squares = jnp.zeros((CHUNK, LANES), F32)
    for quad in range(QUADS):
        cols = slice(quad * QWIDTH, (quad + 1) * QWIDTH)
        wide_delta, wide_cum, columns = widen(delta, cum, quad)
        values = mixed[:, cols]
        scaled = values * wide_delta
        parts = split(scaled)
        outs = []
        for j in range(2):
            right_h, right_l = pair_rows(parts, j, low, high)
            left = []
            for k in range(2):
                h = 4 * quad + 2 * j + k
                within = jnp.exp(columns[2 * j + k] - cum_t[h : h + 1, :] + bias)
                left.append(split(affinity * within))
            left_h = jnp.concatenate([left[0][0], left[1][0]], axis=1)
            left_l = jnp.concatenate([left[0][1], left[1][1]], axis=1)
            both = dot(left_h, jnp.concatenate([right_h, right_l], axis=1))
            outs.append(both[:, :LANES] + both[:, LANES:] + dot(left_l, right_h))
        carried = state[:, cols]
        grown = jnp.exp(wide_cum)
        out = jnp.concatenate(outs, axis=1) + dot_parts(readout_parts, split(carried)) * grown
        out = out + skip[:, cols] * values
        tail = jnp.exp(wide_cum[CHUNK - 1 :] - wide_cum)
        state[:, cols] = carried * grown[CHUNK - 1 :] + dot_parts(b_parts, split(scaled * tail))
        ssm[:, cols] = out
        gated = out * silu(gate[:, cols])
        squares = squares + gated[:, :LANES] * gated[:, :LANES] + gated[:, LANES:] * gated[:, LANES:]
    rho = lax.rsqrt(jnp.sum(squares, axis=1, keepdims=True) * (1.0 / INNER) + NORM_EPS)
    for j in range(PAIRS):
        cols = slice(j * LANES, (j + 1) * LANES)
        gated = ssm[:, cols] * silu(gate[:, cols])
        mixed_out[:, cols] = (gated * rho * gain[:, cols]).astype(BF16)


def scan_forward(mixed, projected, dt_bias, a_log, skip, gain):
    length = mixed.shape[0]
    chunks = length // CHUNK
    whole = lambda v: pl.BlockSpec(v.shape, lambda i: (0,) * v.ndim)
    return pl.pallas_call(
        scan_forward_kernel,
        grid=(chunks,),
        out_shape=(
            shape((length, INNER), F32),
            shape((length, INNER), BF16),
            shape((chunks, NSTATE, INNER), F32),
        ),
        in_specs=[
            pl.BlockSpec((CHUNK, MIXW), lambda i: (i, 0)),
            pl.BlockSpec((CHUNK, LANES), lambda i: (i, DT_AT // LANES)),
            pl.BlockSpec((CHUNK, INNER), lambda i: (i, 0)),
        ]
        + [whole(v) for v in (dt_bias, a_log, skip, gain)],
        out_specs=(
            pl.BlockSpec((CHUNK, INNER), lambda i: (i, 0)),
            pl.BlockSpec((CHUNK, INNER), lambda i: (i, 0)),
            pl.BlockSpec((1, NSTATE, INNER), lambda i: (i, 0, 0)),
        ),
        scratch_shapes=[pltpu.VMEM((NSTATE, INNER), F32)],
        compiler_params=params(),
        cost_estimate=cost(40),
    )(mixed, projected, projected, dt_bias, a_log, skip, gain)


def scan_backward_kernel(
    mixed, dt, ssm, grad, states, dt_bias, a_log, skip, gather, held,
    grad_mixed, grad_dt, sums, skip_sums, grad_state, left, right,
):
    @pl.when(pl.program_id(0) == 0)
    def _():
        grad_state[...] = jnp.zeros_like(grad_state)
        sums[...] = jnp.zeros_like(sums)
        skip_sums[...] = jnp.zeros_like(skip_sums)

    shifted, delta, rate, cum, last = chunk_decays(dt[...], dt_bias[...], a_log[...])
    lane = lax.broadcasted_iota(jnp.int32, (CHUNK, LANES), 1)
    row = lax.broadcasted_iota(jnp.int32, (CHUNK, LANES), 0)
    bias = jnp.where(lane >= row, 0.0, -1e30)
    heads = lane < HEADS
    cum_t = cum.T
    inputs_b = mixed[:, INNER : INNER + NSTATE]
    readout = mixed[:, INNER + NSTATE :]
    b_parts, c_parts = split(inputs_b), split(readout)
    b_wide = side_by_side(inputs_b)
    c_turned = side_by_side(readout.T)
    affinity = dot3(b_parts, c_parts, NT)
    low, high = pair_mask()
    grad_affinity = jnp.zeros((CHUNK, CHUNK), F32)
    grad_b = jnp.zeros((CHUNK, NSTATE), F32)
    grad_c = jnp.zeros((CHUNK, NSTATE), F32)
    last_row = lax.broadcasted_iota(jnp.int32, (CHUNK, QWIDTH), 0) == CHUNK - 1
    for quad in range(QUADS):
        cols = slice(quad * QWIDTH, (quad + 1) * QWIDTH)
        wide_delta, wide_cum, columns = widen(delta, cum, quad)
        grown = jnp.exp(wide_cum)
        tail = jnp.exp(wide_cum[CHUNK - 1 :] - wide_cum)
        end = grown[CHUNK - 1 :]
        values = mixed[:, cols]
        pulled = grad[:, cols]
        scaled = values * wide_delta
        x_parts, p_parts = split(scaled), split(pulled)
        outs = []
        for j in range(2):
            half = slice(j * LANES, (j + 1) * LANES)
            xh, xl = x_parts[0][:, half], x_parts[1][:, half]
            right_h, right_l = pair_rows(p_parts, j, low, high)
            pull = dot(
                jnp.concatenate([xh, xl], axis=1),
                jnp.concatenate([right_h, right_h], axis=1),
                NT,
            ) + dot(xh, right_l, NT)
            kernels = []
            for k in range(2):
                h = 4 * quad + 2 * j + k
                within = jnp.exp(cum_t[h : h + 1, :] - columns[2 * j + k] + bias)
                kernels.append(split(affinity * within))
                grad_affinity = grad_affinity + within * pull[:, k * CHUNK : (k + 1) * CHUNK]
            kernel_h = jnp.concatenate([kernels[0][0], kernels[1][0]], axis=1)
            kernel_l = jnp.concatenate([kernels[0][1], kernels[1][1]], axis=1)
            both = dot(kernel_h, jnp.concatenate([right_h, right_l], axis=1))
            outs.append(both[:, :LANES] + both[:, LANES:] + dot(kernel_l, right_h))
        late = grad_state[:, cols]
        late_parts = split(late)
        early = states[0, :, cols]
        from_state = dot_parts(b_wide, late_parts) * tail
        grad_scaled = jnp.concatenate(outs, axis=1) + from_state
        pulled_cum = split(pulled * grown)
        grad_c = grad_c + dot_turned(pulled_cum, split(early))
        grad_b = grad_b + dot_turned(split(scaled * tail), late_parts)
        grad_state[:, cols] = late * end + dot_parts(c_turned, pulled_cum)
        grad_mixed[:, cols] = grad_scaled * wide_delta + skip[:, cols] * pulled
        skip_sums[:, cols] += jnp.sum(pulled * values, axis=0, keepdims=True)
        left[:, cols] = grad_scaled * values
        inner = pulled * (ssm[:, cols] - skip[:, cols] * values) - scaled * grad_scaled
        extra = jnp.sum(scaled * from_state, axis=0, keepdims=True) + end * jnp.sum(
            late * early, axis=0, keepdims=True
        )
        right[:, cols] = inner + jnp.where(last_row, extra, 0.0)
    ga_parts = split(grad_affinity)
    grad_mixed[:, INNER : INNER + NSTATE] = grad_b + dot3(ga_parts, c_parts)
    grad_mixed[:, INNER + NSTATE :] = grad_c + dot3(split(grad_affinity.T), b_parts)

    def by_head(v):
        high, low = split(v)
        g = gather[...]
        return dot(high, g) + dot(low, g)

    direct = by_head(left[...])
    grad_cum = by_head(right[...])
    upper = (lane >= row).astype(BF16)
    after = triangle_sum(upper, grad_cum)
    grad_delta = direct + rate * after
    grad_raw = jnp.where(heads, grad_delta * sigmoid(shifted), 0.0)
    grad_dt[...] = grad_raw.astype(BF16)
    sums[0:1, :] += jnp.sum(grad_raw, axis=0, keepdims=True)
    sums[1:2, :] += rate * jnp.sum(delta * after, axis=0, keepdims=True)


def scan_backward(mixed, projected, ssm, grad, states, dt_bias, a_log, skip, gather, held):
    length = mixed.shape[0]
    chunks = length // CHUNK
    whole = lambda v: pl.BlockSpec(v.shape, lambda i: (0,) * v.ndim)
    back = lambda i: (chunks - 1 - i, 0)
    return pl.pallas_call(
        scan_backward_kernel,
        grid=(chunks,),
        out_shape=(
            shape((length, MIXW), F32),
            shape(held.shape, BF16),
            shape((8, LANES), F32),
            shape((1, INNER), F32),
        ),
        in_specs=[
            pl.BlockSpec((CHUNK, MIXW), back),
            pl.BlockSpec((CHUNK, LANES), lambda i: (chunks - 1 - i, DT_AT // LANES)),
            pl.BlockSpec((CHUNK, INNER), back),
            pl.BlockSpec((CHUNK, INNER), back),
            pl.BlockSpec((1, NSTATE, INNER), lambda i: (chunks - 1 - i, 0, 0)),
        ]
        + [whole(v) for v in (dt_bias, a_log, skip, gather)]
        + [ANY],
        out_specs=(
            pl.BlockSpec((CHUNK, MIXW), back),
            pl.BlockSpec((CHUNK, LANES), lambda i: (chunks - 1 - i, DT_AT // LANES)),
            pl.BlockSpec((8, LANES), lambda i: (0, 0)),
            pl.BlockSpec((1, INNER), lambda i: (0, 0)),
        ),
        scratch_shapes=[pltpu.VMEM((NSTATE, INNER), F32)] + [pltpu.VMEM((CHUNK, INNER), F32)] * 2,
        compiler_params=params(),
        input_output_aliases={9: 1},
        cost_estimate=cost(35),
    )(mixed, projected, ssm, grad, states, dt_bias, a_log, skip, gather, held)


ROWS_AT_ONCE = 128
CONV_TILES = 2


def down(v, before, by):
    moved = pltpu.roll(v, by, 0)
    row = lax.broadcasted_iota(jnp.int32, (8, LANES), 0)
    top = jnp.where(row < by, pltpu.roll(before, by, 0), moved[:8])
    return jnp.concatenate([top, moved[8:]], axis=0)


def up(v, after, by):
    rows = v.shape[0]
    moved = pltpu.roll(v, rows - by, 0)
    row = lax.broadcasted_iota(jnp.int32, (8, LANES), 0)
    end = jnp.where(row < 8 - by, moved[rows - 8 :], pltpu.roll(after, 8 - by, 0))
    return jnp.concatenate([moved[: rows - 8], end], axis=0)


def conv_terms(conv_in, at, cols):
    rows = conv_in[at : at + ROWS_AT_ONCE, cols]
    before = conv_in[at - 8 : at, cols] if at else jnp.zeros((8, LANES), F32)
    return [down(rows, before, KCONV - 1 - k) for k in range(KCONV - 1)] + [rows]


def conv_sum(terms, weight, bias):
    total = bias + terms[KCONV - 1] * weight[KCONV - 1 : KCONV]
    for k in range(KCONV - 1):
        total = total + terms[k] * weight[k : k + 1]
    return total


def conv_forward_kernel(conv_in, weight, bias, mixed):
    for tile in range(CONV_TILES):
        cols = slice(tile * LANES, (tile + 1) * LANES)
        w, b = weight[:, cols], bias[:, cols]
        for at in range(0, conv_in.shape[0], ROWS_AT_ONCE):
            mixed[at : at + ROWS_AT_ONCE, cols] = silu(conv_sum(conv_terms(conv_in, at, cols), w, b))


def conv_forward(projected, weight, bias):
    length = projected.shape[0]
    width = CONV_TILES * LANES
    return pl.pallas_call(
        conv_forward_kernel,
        grid=(CONVCH // width,),
        out_shape=shape((length, CONVCH), F32),
        in_specs=[
            pl.BlockSpec((length, width), lambda i: (0, INNER // width + i)),
            pl.BlockSpec((KCONV, width), lambda i: (0, i)),
            pl.BlockSpec((1, width), lambda i: (0, i)),
        ],
        out_specs=pl.BlockSpec((length, width), lambda i: (0, i)),
        compiler_params=params(),
        cost_estimate=cost(10),
    )(projected, weight, bias)


def conv_backward_kernel(conv_in, grad, weight, bias, held, out, sums):
    length = conv_in.shape[0]
    for tile in range(CONV_TILES):
        cols = slice(tile * LANES, (tile + 1) * LANES)
        w, b = weight[:, cols], bias[:, cols]
        totals = [jnp.zeros((1, LANES), F32)] * (KCONV + 1)
        after = jnp.zeros((8, LANES), F32)
        for at in range(length - ROWS_AT_ONCE, -1, -ROWS_AT_ONCE):
            terms = conv_terms(conv_in, at, cols)
            value = conv_sum(terms, w, b)
            sig = sigmoid(value)
            g = grad[at : at + ROWS_AT_ONCE, cols] * (sig * (1.0 + value * (1.0 - sig)))
            for k in range(KCONV):
                totals[k] = totals[k] + jnp.sum(g * terms[k], axis=0, keepdims=True)
            totals[KCONV] = totals[KCONV] + jnp.sum(g, axis=0, keepdims=True)
            total = g * w[KCONV - 1 : KCONV]
            for k in range(KCONV - 1):
                total = total + up(g, after, KCONV - 1 - k) * w[k : k + 1]
            after = g[:8]
            out[at : at + ROWS_AT_ONCE, cols] = total.astype(BF16)
        for k in range(KCONV + 1):
            sums[k : k + 1, cols] = totals[k]


def conv_backward(projected, grad_mixed, weight, bias, held):
    length = projected.shape[0]
    width = CONV_TILES * LANES
    return pl.pallas_call(
        conv_backward_kernel,
        grid=(CONVCH // width,),
        out_shape=(shape(held.shape, BF16), shape((8, CONVCH), F32)),
        in_specs=[
            pl.BlockSpec((length, width), lambda i: (0, INNER // width + i)),
            pl.BlockSpec((length, width), lambda i: (0, i)),
            pl.BlockSpec((KCONV, width), lambda i: (0, i)),
            pl.BlockSpec((1, width), lambda i: (0, i)),
            ANY,
        ],
        out_specs=(
            pl.BlockSpec((length, width), lambda i: (0, INNER // width + i)),
            pl.BlockSpec((8, width), lambda i: (0, i)),
        ),
        input_output_aliases={4: 0},
        compiler_params=params(),
        cost_estimate=cost(12),
    )(projected, grad_mixed, weight, bias, held)


def middle_kernel(
    limit, mixed_out, w_out, tokens, teacher, mask, ssm, gate, gain,
    block_out, grad_result, grad_branch, grad_ssm, grad_gate, error, gain_sums,
):
    step = pl.program_id(0)

    @pl.when(step == 0)
    def _():
        error[...] = jnp.zeros_like(error)
        gain_sums[...] = jnp.zeros_like(gain_sums)

    rows = tokens.shape[0]
    result = tokens[...].astype(F32) + dot(mixed_out[...], w_out[...])
    position = step * rows + lax.broadcasted_iota(jnp.int32, (rows, 1), 0)
    valid = (position < limit[0]).astype(F32)
    weight = valid * mask[:, 0:1]
    block_out[...] = (result * valid).astype(BF16)
    misfit = result - teacher[...].astype(F32)
    pulled = 2.0 * weight * misfit
    grad_result[...] = pulled
    error[...] += jnp.sum(0.5 * pulled * misfit, axis=0, keepdims=True)
    low = pulled.astype(BF16)
    grad_branch[...] = low
    grad_mixed = dot(low, w_out[...], NT)
    g = gate[...]
    sig = sigmoid(g)
    act = g * sig
    inner = ssm[...]
    gated = inner * act
    rho = lax.rsqrt(jnp.mean(gated * gated, axis=1, keepdims=True) + NORM_EPS)
    unit = gated * rho
    gain_sums[...] += jnp.sum(unit * grad_mixed, axis=0, keepdims=True)
    grad_unit = grad_mixed * gain[...]
    share = jnp.mean(grad_unit * unit, axis=1, keepdims=True)
    grad_gated = rho * (grad_unit - unit * share)
    grad_ssm[...] = grad_gated * act
    grad_gate[...] = (grad_gated * inner * (sig * (1.0 + g * (1.0 - sig)))).astype(BF16)


def middle(limit, mixed_out, w_out, tokens, teacher, mask, ssm, projected, gain):
    length = tokens.shape[0]
    rows = 256
    by_row = lambda width: pl.BlockSpec((rows, width), lambda i: (i, 0))
    whole = lambda v: pl.BlockSpec(v.shape, lambda i: (0,) * v.ndim)
    return pl.pallas_call(
        middle_kernel,
        grid=(length // rows,),
        out_shape=(
            shape((length, D), BF16),
            shape((length, D), F32),
            shape((length, D), BF16),
            shape((length, INNER), F32),
            shape((length, WIDE), BF16),
            shape((1, D), F32),
            shape((1, INNER), F32),
        ),
        in_specs=[
            SMEM,
            by_row(INNER),
            whole(w_out),
            by_row(D),
            by_row(D),
            by_row(LANES),
            by_row(INNER),
            by_row(INNER),
            whole(gain),
        ],
        out_specs=(
            by_row(D),
            by_row(D),
            by_row(D),
            by_row(INNER),
            by_row(INNER),
            pl.BlockSpec((1, D), lambda i: (0, 0)),
            pl.BlockSpec((1, INNER), lambda i: (0, 0)),
        ),
        compiler_params=params(),
        cost_estimate=cost(25),
    )(limit, mixed_out, w_out, tokens, teacher, mask, ssm, projected, gain)


def body(tokens, teacher, lengths, loss_mask, owners, master, first_moment, second_moment):
    capacity = master.shape[0]
    dp, fsdp = lax.axis_size("dp"), lax.axis_size("fsdp")
    devices = dp * fsdp
    me = lax.axis_index(AXES).astype(jnp.int32)
    x_first, y_first, z_first = step_orders(dp, fsdp)
    tie = lambda *values: lax.optimization_barrier(values)

    sent = send_blocks(send_plan(owners, capacity, devices, me), master)
    at_home = lax.all_to_all(sent, AXES, 0, 0, tiled=True)
    owners, tokens, loss_mask, _ = tie(owners, tokens, loss_mask, sent)
    plan = make_plan(owners, capacity, devices, me)
    n0, n1 = plan["slots"]
    streams = cut(n0, (x_first, y_first, z_first))
    table = stream_places(plan["home"], plan["slot"], me, streams, devices)
    table0 = jnp.concatenate([table[:MID0], table[MID1:]])
    table1 = (place_of(plan["home"] ^ me, x_first) * n1 + plan["slot"])[MID0:MID1]
    u0, u1 = plan["unit_slots"]
    unit_streams = cut(u0, (x_first, y_first, x_first, y_first, z_first))
    unit_table = stream_places(plan["unit_home"], plan["unit_slot"], me, unit_streams, devices)
    unit_table = unit_table[:MID0].reshape(-1)
    unit_table1 = place_of(plan["unit_home"] ^ me, x_first) * (u1 + 1) + plan["unit_slot"]
    unit_table1 = unit_table1[MID0:MID1].reshape(-1)
    inputs, target = tokens[0], teacher[0]
    mask = jnp.broadcast_to(loss_mask[0].astype(F32)[:, None], (inputs.shape[0], LANES))
    wide_in = inputs.astype(F32)
    inverse = lax.rsqrt(jnp.mean(wide_in * wide_in, axis=-1, keepdims=True) + NORM_EPS)
    position = jnp.arange(inputs.shape[0], dtype=jnp.int32)
    counted = jnp.sum(jnp.where(position < lengths[0], loss_mask[0], 0)).astype(F32)
    limit = jnp.broadcast_to((END_OUT - plan["row_block"] * PBLOCK)[:, None], (capacity, LANES))
    used = jnp.broadcast_to(plan["row_used"].astype(jnp.int32)[:, None], (capacity, LANES))
    received = jnp.concatenate(plan["received"])
    (at_home, table0, table1, unit_table, unit_table1, mask, inverse, counted, limit, used,
     received, back_table, row_from) = tie(
        at_home, table0, table1, unit_table, unit_table1, mask, inverse, counted, limit, used,
        received, plan["back"], plan["row_from"],
    )
    sizes = [size for _, size, _ in streams] + [n1]
    *mine, mine1 = pick_blocks(received, at_home, sizes)
    parts = []
    for values, (_, _, order) in zip(mine, streams):
        parts += gather_steps(values, order)
    *parts, mine1 = tie(*parts, mine1)
    late_steps = x_first[:0:-1]
    for step in late_steps[: max(len(late_steps) - 4, 0)]:
        mine1 = doubled(mine1, step)
    late_steps = late_steps[-4:]
    input_weight, head, tail, conv_weight, conv_bias, heads, skip, norm_gain, gate_gain = unpack_in(
        table0, parts
    )
    if late_steps[-4:-3]:
        mine1, input_weight = tie(doubled(mine1, late_steps[-4]), input_weight)
    dt_bias, a_log = heads[0:1], heads[1:2]
    gather = heads_gather()
    normed = wide_in * inverse
    hidden = (normed * norm_gain).astype(BF16)
    projected = dot(hidden, input_weight)
    if late_steps[-3:-2]:
        mine1, projected = tie(doubled(mine1, late_steps[-3]), projected)
    mixed = conv_forward(projected, conv_weight, conv_bias)
    if late_steps[-2:-1]:
        mine1, mixed = tie(doubled(mine1, late_steps[-2]), mixed)
    ssm, mixed_out, states = scan_forward(mixed, projected, dt_bias, a_log, skip, gate_gain)
    if late_steps:
        mine1, mixed_out = tie(doubled(mine1, late_steps[-1]), mixed_out)
    output_weight = unpack_out(table1, mine1, exchange(mine1, x_first[0]), head, tail)
    block_out, grad_result, grad_branch, grad_ssm, grad_low, errors, grad_gate = middle(
        lengths, mixed_out, output_weight, inputs, target, mask, ssm, projected, gate_gain
    )
    local = jnp.concatenate([errors.reshape(-1, LANES), jnp.broadcast_to(counted, (2, LANES))])
    grad_weight_out = dot(mixed_out, grad_branch, (((0,), (0,)), ((), ())))
    keep1, send1, head, tail = pack_out(unit_table1, grad_weight_out, local, devices, u1 + 1)
    sum1 = keep1 + exchange(send1, x_first[0])
    grad_ssm, sum1 = tie(grad_ssm, sum1)
    sum1 = reduce_step(sum1, x_first[1])
    grad_mixed, grad_low, sums, skip_sums = scan_backward(
        mixed, projected, ssm, grad_ssm, states, dt_bias, a_log, skip, gather, grad_low
    )
    grad_low, conv_sums = conv_backward(projected, grad_mixed, conv_weight, conv_bias, grad_low)
    grad_low, sum1 = tie(grad_low, sum1)
    halves = []
    for _, size, _ in unit_streams:
        halves += [devices * size // 2] * 2
    packed = list(pack_in(unit_table, hidden, grad_low, head, halves))
    if len(x_first) > 3:
        sum1 = reduce_step(sum1, x_first[2])
        packed[0], sum1 = tie(packed[0], sum1)
    reduced = [
        packed[2 * i] + exchange(packed[2 * i + 1], order[0])
        for i, (_, _, order) in enumerate(unit_streams)
    ]
    reduced[0], grad_low, conv_sums, sums, skip_sums, grad_gate = tie(
        reduced[0], grad_low, conv_sums, sums, skip_sums, grad_gate
    )
    grad_hidden = dot(grad_low, input_weight, NT)
    grad_norm = jnp.sum(grad_hidden * normed, axis=0)
    grad_normed = grad_hidden * norm_gain
    input_grad = grad_result + inverse * (
        grad_normed - normed * jnp.mean(grad_normed * normed, axis=-1, keepdims=True)
    )
    grad_vec = jnp.concatenate(
        [
            conv_sums[:KCONV].T.reshape(-1),
            conv_sums[KCONV],
            sums[0, :HEADS],
            sums[1, :HEADS],
            jnp.sum(skip_sums.reshape(HEADS, HEADDIM), axis=1),
            grad_norm,
            grad_gate[0],
            jnp.zeros((NBLK * PBLOCK - PTOT,), F32),
        ]
    ).reshape(VEC_ROWS, LANES)
    grad_vec = jnp.concatenate([tail, grad_vec]).reshape((NBLK - MID1) * UNITS, UNIT, LANES)
    reduced = [reduce_step(v, order[1]) for v, (_, _, order) in zip(reduced, unit_streams)]
    for step in x_first[:2]:
        grad_vec = grad_vec + exchange(grad_vec, step)
    reduced[0], grad_vec, input_grad = tie(reduced[0], grad_vec, input_grad)
    for k in range(2, len(x_first) - 1):
        reduced[0], grad_vec = reduce_step(reduced[0], x_first[k], grad_vec)
        for i in range(1, len(reduced)):
            reduced[i] = reduce_step(reduced[i], unit_streams[i][2][k])
    for step in x_first[3:-1]:
        sum1 = reduce_step(sum1, step)
    ends = []
    for i, values in enumerate(reduced + [sum1]):
        half = values.shape[0] // 2
        given, step = values[half:], (unit_streams[i][2] if i < len(reduced) else x_first)[-1]
        if i == 0:
            got = exchange(jnp.concatenate([given, grad_vec]), step)
            grad_vec = grad_vec + got[half:]
            got = got[:half]
        else:
            got = exchange(given, step)
        ends += [values[:half], got]
    back = units_to_owners(back_table, ends)
    got = lax.all_to_all(back, AXES, 0, 0, tiled=True)
    local_sums = ends[-2][u1] + ends[-1][u1]
    error_sum = jnp.sum(local_sums[: D // LANES])
    divisor = local_sums[D // LANES, 0] * D
    new_first, new_second, new_master = adam(
        row_from,
        divisor,
        got,
        grad_vec,
        limit,
        used,
        master,
        first_moment,
        second_moment,
    )
    mean_loss = error_sum / divisor
    return (block_out[None], input_grad[None], mean_loss, new_first, new_second, new_master)


def solution(mesh):
    return jax.shard_map(
        body,
        mesh=mesh,
        in_specs=(
            P(AXES, None, None),
            P(AXES, None, None),
            P(AXES),
            P(AXES, None),
            P(),
            P(AXES, None),
            P(AXES, None),
            P(AXES, None),
        ),
        out_specs=(
            P(AXES, None, None),
            P(AXES, None, None),
            P(),
            P(AXES, None),
            P(AXES, None),
            P(AXES, None),
        ),
        check_vma=False,
    )
```

```python
from functools import partial

import jax
import jax.numpy as jnp
import numpy as np
from jax import lax
from jax.experimental import pallas as pl
from jax.experimental.pallas import tpu as pltpu
from jax.sharding import PartitionSpec as P

D = 768
INNER = 1536
NSTATE = 128
HEADDIM = 64
KCONV = 4
SCAN_LEN = 256
PBLOCK = 4096
STEP = 10
HEADS = 24
CONVCH = 1792
PROJ = 3352
PTOT = 3765320
NBLK = 920

LANES = 128
BROWS = PBLOCK // LANES
UNIT = 8
UNITS = BROWS // UNIT
END_IN = D * PROJ
END_OUT = END_IN + INNER * D
MID0 = -(-END_IN // PBLOCK)
MID1 = END_OUT // PBLOCK
N0 = MID0 + NBLK - MID1
N1 = MID1 - MID0
F0_ROWS = N0 * BROWS
IN_ROWS = END_IN // LANES
HEAD_ROWS = MID0 * BROWS - IN_ROWS
TAIL_ROWS = (END_OUT - MID1 * PBLOCK) // LANES
OUT_ROWS = INNER * D // LANES
VEC_ROWS = (NBLK - MID1) * BROWS - TAIL_ROWS
VEC_AT = MID0 * BROWS + TAIL_ROWS
GROUP = 16
GROUPS = D // GROUP
GROUP_ROWS = GROUP * PROJ // LANES
COL_TILES = -(-PROJ // LANES)
WIDE = COL_TILES * LANES
OUT_TILES = D // LANES

NORM_EPS = 1e-05
ADAM_EPS = 1e-08
BETA_ONE = 0.9
BETA_TWO = 0.999
MATRIX_RATE = 0.03
VECTOR_RATE = 0.2
WEIGHT_DECAY = 0.1
PRECISE = lax.Precision.HIGHEST
AXES = ("dp", "fsdp")
VMEM_LIMIT = 60 * 1024 * 1024


def bits_of(count):
    return count.bit_length() - 1


def step_orders(dp, fsdp):
    wide = [("dp", i) for i in range(bits_of(dp))]
    narrow = [("fsdp", i) for i in range(bits_of(fsdp))]
    first = wide[:2] + narrow + wide[2:]
    second = wide[:1] + narrow + wide[1:]
    third = wide[:1] + wide[2:] + wide[1:2] + narrow
    return first, second, third


def cut(total, orders):
    base, more = divmod(total, len(orders))
    streams, at = [], 0
    for i, order in enumerate(orders):
        size = base + (i < more)
        if size:
            streams.append((at, size, order))
        at += size
    return streams


def exchange(values, step):
    axis, bit = step
    size = lax.axis_size(axis)
    return lax.ppermute(values, axis, [(i, i ^ (1 << bit)) for i in range(size)])


def place_of(relative, order):
    shift_of = {"dp": bits_of(lax.axis_size("fsdp")), "fsdp": 0}
    place = jnp.zeros_like(relative)
    for axis, bit in order:
        place = place * 2 + ((relative >> (shift_of[axis] + bit)) & 1)
    return place


def class_counts(owners, devices):
    block = jnp.arange(NBLK, dtype=jnp.int32)
    mid = ((block >= MID0) & (block < MID1))[None, :]
    device = jnp.arange(devices, dtype=jnp.int32)
    below = owners[None, :] < device[:, None]
    owned = owners[None, :] == device[:, None]

    def total(mask):
        return jnp.sum(mask.astype(jnp.int32), axis=1)

    start = (total(below & ~mid), total(below & mid))
    count = (total(owned & ~mid), total(owned & mid))
    return start, count, total(owned & (block < MID0)[None, :])


def my_counts(owners, me):
    block = jnp.arange(NBLK, dtype=jnp.int32)
    mid = (block >= MID0) & (block < MID1)
    below, owned = owners < me, owners == me
    total = lambda mask: jnp.sum(mask.astype(jnp.int32))
    start = (total(below & ~mid), total(below & mid))
    count = (total(owned & ~mid), total(owned & mid))
    return start, count, total(owned & (block < MID0))


def pair_lanes(capacity, devices):
    return 2 + max(capacity - 2, 0) // devices


def make_plan(owners, capacity, devices, me):
    block = jnp.arange(NBLK, dtype=jnp.int32)
    mid = (block >= MID0) & (block < MID1)
    same = mid[:, None] == mid[None, :]
    before = (owners[None, :] < owners[:, None]) | (
        (owners[None, :] == owners[:, None]) & (block[None, :] < block[:, None])
    )
    order_in_class = jnp.sum((same & before).astype(jnp.int32), axis=1)
    home, slot = order_in_class % devices, order_in_class // devices
    device = jnp.arange(devices, dtype=jnp.int32)
    start, count, _ = class_counts(owners, devices)
    my_start, my_count, my_early = my_counts(owners, me)
    pair = pair_lanes(capacity, devices)

    slots = (-(-N0 // devices), -(-N1 // devices))

    def received(kind):
        wanted = me + devices * jnp.arange(slots[kind], dtype=jnp.int32)
        ends = start[kind] + count[kind]
        owner = jnp.sum((ends[None, :] <= wanted[:, None]).astype(jnp.int32), axis=1)
        owner = jnp.minimum(owner, devices - 1)
        base = jnp.sum(jnp.where(device[None, :] == owner[:, None], start[kind][None, :], 0), axis=1)
        turn = jnp.clip((wanted - base) // devices, 0, pair - 1)
        return owner * pair + (turn if kind == 0 else pair - 1 - turn)

    back_pair = (UNITS * capacity + 2 * (devices - 1)) // devices
    unit = UNITS * order_in_class[:, None] + jnp.arange(UNITS, dtype=jnp.int32)[None, :]
    unit_home, unit_slot = unit % devices, unit // devices
    unit_slots = (-(-UNITS * N0 // devices), -(-UNITS * N1 // devices))
    lane = jnp.arange(back_pair, dtype=jnp.int32)

    def units_back(kind):
        turn = lane if kind == 0 else back_pair - 1 - lane
        first = UNITS * start[kind][:, None]
        k = (me - first) % devices + turn[None, :] * devices
        return k < UNITS * count[kind][:, None], (first + k) // devices

    valid0, slot0 = units_back(0)
    valid1, slot1 = units_back(1)
    back = jnp.where(valid0, slot0, jnp.where(valid1, unit_slots[0] + slot1, 0)).reshape(-1)

    row = jnp.arange(capacity, dtype=jnp.int32)
    is_mid = (row >= my_early) & (row < my_early + my_count[1])
    k = jnp.where(is_mid, row - my_early, jnp.where(row < my_early, row, row - my_count[1]))
    first = UNITS * jnp.where(is_mid, my_start[1], my_start[0])
    k = UNITS * k[:, None] + jnp.arange(UNITS, dtype=jnp.int32)[None, :]
    turn = k // devices
    row_from = ((first[:, None] + k) % devices) * back_pair + jnp.where(
        is_mid[:, None], back_pair - 1 - turn, turn
    )
    row_used = row < my_count[0] + my_count[1]
    mine = (owners == me)[None, :]
    rank = jnp.sum((mine & (block[None, :] < block[:, None])).astype(jnp.int32), axis=1)
    row_block = jnp.sum(
        jnp.where(mine & (rank[None, :] == row[:, None]), block[None, :], 0), axis=1
    )
    late = devices * back_pair + UNITS * (row_block - MID1)
    late = late[:, None] + jnp.arange(UNITS, dtype=jnp.int32)[None, :]
    row_from = jnp.where((row_block >= MID1)[:, None], late, row_from)
    row_from = jnp.where(row_used[:, None], row_from, 0).reshape(-1)
    return dict(
        home=home, slot=slot, slots=slots,
        received=(received(0), received(1)), unit_home=unit_home, unit_slot=unit_slot,
        unit_slots=unit_slots, back=back, row_from=row_from,
        row_used=row_used, row_block=row_block,
    )


def stream_places(home, slot, me, streams, devices):
    relative = home ^ me
    place = jnp.zeros_like(slot)
    for begin, size, order in streams:
        inside = (slot >= begin) & (slot < begin + size)
        at = devices * begin + place_of(relative, order) * size + slot - begin
        place = jnp.where(inside, at, place)
    return place


def cost(microseconds):
    return pl.CostEstimate(
        flops=int(microseconds * 1e9), bytes_accessed=int(microseconds * 3e6), transcendentals=0
    )


ANY = pl.BlockSpec(memory_space=pl.ANY)
VMEM = pl.BlockSpec(memory_space=pltpu.VMEM)
SMEM = pl.BlockSpec(memory_space=pltpu.SMEM)


def params(**extra):
    return pltpu.CompilerParams(vmem_limit_bytes=VMEM_LIMIT, **extra)


def shape(dims, dtype):
    return jax.ShapeDtypeStruct(dims, dtype)


def send_kernel(my_index, owners, master, out, flat, *, devices):
    capacity = master.shape[0]
    me = my_index[0]
    for j in range(BROWS):
        flat[pl.ds(j, capacity, stride=BROWS), :] = master[:, j * LANES : (j + 1) * LANES]
    held = owners[...]
    block = lax.broadcasted_iota(jnp.int32, held.shape, 0) * LANES + lax.broadcasted_iota(
        jnp.int32, held.shape, 1
    )
    mid = (block >= MID0) & (block < MID1)
    below, owned = held < me, held == me

    def total(mask):
        return jnp.sum(jnp.where(mask, 1.0, 0.0)).astype(jnp.int32)

    start0, start1 = total(below & ~mid), total(below & mid)
    count0, count1 = total(owned & ~mid), total(owned & mid)
    early = total(owned & (block < MID0))
    pair = out.shape[0] // devices
    positive = devices * NBLK

    def step(home, carry):
        for s in range(pair):
            k0 = lax.rem(home - start0 + positive, devices) + s * devices
            k1 = lax.rem(home - start1 + positive, devices) + (pair - 1 - s) * devices
            row0 = jnp.where(k0 < early, k0, k0 + count1)
            row = jnp.where(k0 < count0, row0, jnp.where(k1 < count1, early + k1, 0))
            rows = pl.ds(pl.multiple_of(row * BROWS, BROWS), BROWS)
            out[home * pair + s] = flat[rows, :].astype(out.dtype)
        return carry

    lax.fori_loop(0, devices, step, 0)


def send_blocks(owners, master, devices, me):
    rows = -(-NBLK // (8 * LANES)) * 8
    held = jnp.pad(owners, (0, rows * LANES - NBLK), constant_values=1 << 20).reshape(rows, LANES)
    count = devices * pair_lanes(master.shape[0], devices)
    return pl.pallas_call(
        partial(send_kernel, devices=devices),
        out_shape=shape((count, BROWS, LANES), jnp.bfloat16),
        in_specs=[SMEM, VMEM, VMEM],
        out_specs=VMEM,
        scratch_shapes=[pltpu.VMEM((master.shape[0] * BROWS, LANES), jnp.float32)],
        compiler_params=params(),
    )(me.reshape(1), held, master)


def pick_kernel(table, source, *outs):
    at = 0
    for out in outs:

        def step(i, carry, out=out, at=at):
            out[i] = source[table[at + i]]
            return carry

        lax.fori_loop(0, out.shape[0], step, 0)
        at += out.shape[0]


def pick_blocks(table, source, sizes):
    return pl.pallas_call(
        pick_kernel,
        out_shape=tuple(shape((n,) + source.shape[1:], source.dtype) for n in sizes),
        in_specs=[SMEM, VMEM],
        out_specs=(VMEM,) * len(sizes),
        compiler_params=params(),
    )(table, source)


def back_kernel(table, *refs):
    sources, (out, held) = refs[:-2], refs[-2:]
    at = 0
    for i in range(0, len(sources), 2):
        n = sources[i].shape[0]
        held[at : at + n] = sources[i][...] + sources[i + 1][...]
        at += n

    def step(i, carry):
        for u in range(8):
            out[i * 8 + u] = held[table[i * 8 + u]]
        return carry

    total = out.shape[0]
    lax.fori_loop(0, total // 8, step, 0)


def units_to_owners(table, sources):
    return pl.pallas_call(
        back_kernel,
        out_shape=shape((table.shape[0], UNIT, LANES), jnp.float32),
        in_specs=[SMEM] + [VMEM] * len(sources),
        out_specs=VMEM,
        scratch_shapes=[
            pltpu.VMEM((sum(s.shape[0] for s in sources[::2]), UNIT, LANES), jnp.float32)
        ],
        compiler_params=params(),
    )(table, *sources)


def row_start(rho):
    return (PROJ * rho) // LANES, (PROJ * rho) % LANES


def copy_all(pairs, sem):
    copies = [pltpu.make_async_copy(a, b, sem.at[i]) for i, (a, b) in enumerate(pairs)]
    for c in copies:
        c.start()
    for c in copies:
        c.wait()


def spread_blocks(table, held, flat, count, first_row):
    def one(i):
        at = pl.multiple_of(first_row + i * BROWS, 16)
        flat[pl.ds(at, BROWS), :] = held[table[i]].astype(jnp.float32)

    def step(i, carry):
        for u in range(4):
            one(i * 4 + u)
        return carry

    lax.fori_loop(0, count // 4, step, 0)
    for i in range(count // 4 * 4, count):
        one(i)


def unpack_vectors(flat, conv_weight, conv_bias, heads, skip, norm_gain, gate_gain):
    bf16, f32 = jnp.bfloat16, jnp.float32
    tiles = CONVCH // LANES
    row = lax.broadcasted_iota(jnp.int32, (LANES, LANES), 0)
    col = lax.broadcasted_iota(jnp.int32, (LANES, LANES), 1)
    per_tile = LANES // KCONV
    for k in range(KCONV):
        total = jnp.zeros((tiles, LANES), f32)
        for q in range(KCONV):
            rows = flat[pl.ds(VEC_AT + q, tiles, stride=KCONV), :].astype(bf16)
            chosen = (row == KCONV * (col % per_tile) + k) & (col // per_tile == q)
            total = total + jnp.dot(rows, chosen.astype(bf16), preferred_element_type=f32)
        for i in range(tiles):
            conv_weight[k : k + 1, i * LANES : (i + 1) * LANES] = total[i : i + 1, :]
    bias_at = VEC_AT + tiles * KCONV
    for i in range(tiles):
        conv_bias[:, i * LANES : (i + 1) * LANES] = flat[bias_at + i : bias_at + i + 1, :]
    at = bias_at + tiles
    lane = lax.broadcasted_iota(jnp.int32, (8, LANES), 1)
    first = flat[at : at + 8, :]
    three = []
    for i in range(3):
        moved = pltpu.roll(first, LANES - i * HEADS, 1) if i else first
        three.append(jnp.where(lane < HEADS, moved, 0.0))
        heads[i : i + 1, :] = three[i][0:1, :]
    for j in range(INNER // LANES):
        h = lax.broadcasted_iota(jnp.int32, (LANES, LANES), 0)
        c = lax.broadcasted_iota(jnp.int32, (LANES, LANES), 1) + j * LANES
        spread = (h == c // HEADDIM).astype(bf16)
        wide = jnp.dot(three[2].astype(bf16), spread, preferred_element_type=f32)
        skip[:, j * LANES : (j + 1) * LANES] = wide[0:1, :]
    shift = 3 * HEADS
    for out, begin, width in ((norm_gain, at, D), (gate_gain, at + D // LANES, INNER)):
        for j in range(width // LANES):
            x = pltpu.roll(flat[begin + j : begin + j + 1, :], LANES - shift, 1)
            y = pltpu.roll(flat[begin + j + 1 : begin + j + 2, :], LANES - shift, 1)
            out[:, j * LANES : (j + 1) * LANES] = jnp.where(lane[0:1] < LANES - shift, x, y)


def unpack_in_kernel(table, *refs):
    parts, (w_in, head, tail, *vectors), (held, flat, tile, sem) = refs[:-13], refs[-13:-4], refs[-4:]
    pairs, at = [], 0
    for part in parts:
        pairs.append((part, held.at[pl.ds(at, part.shape[0])]))
        at += part.shape[0]
    copy_all(pairs, sem)
    spread_blocks(table, held, flat, N0, 0)
    head[...] = flat[IN_ROWS : IN_ROWS + HEAD_ROWS, :]
    tail[...] = flat[MID0 * BROWS : MID0 * BROWS + TAIL_ROWS, :]
    unpack_vectors(flat, *vectors)
    lane = lax.broadcasted_iota(jnp.int32, (GROUPS, LANES), 1)

    def columns(j):
        for rho in range(GROUP):
            c, s = row_start(rho)
            x = flat[pl.ds(c + j, GROUPS, stride=GROUP_ROWS), :]
            if s:
                y = flat[pl.ds(c + j + 1, GROUPS, stride=GROUP_ROWS), :]
                x = jnp.where(
                    lane < LANES - s,
                    pltpu.roll(x, LANES - s, 1),
                    pltpu.roll(y, LANES - s, 1),
                )
            tile[pl.ds(rho, GROUPS, stride=GROUP), :] = x

    def step(j, carry):
        columns(j)
        w_in[:, pl.ds(pl.multiple_of(j * LANES, LANES), LANES)] = tile[...].astype(jnp.bfloat16)
        return carry

    lax.fori_loop(0, COL_TILES - 1, step, 0)
    columns(COL_TILES - 1)
    last = (COL_TILES - 1) * LANES
    inside = lax.broadcasted_iota(jnp.int32, (D, LANES), 1) < PROJ - last
    w_in[:, last:] = jnp.where(inside, tile[...], 0.0).astype(jnp.bfloat16)


def unpack_in(table, parts):
    held = sum(part.shape[0] for part in parts)
    return pl.pallas_call(
        unpack_in_kernel,
        out_shape=(
            shape((D, WIDE), jnp.bfloat16),
            shape((HEAD_ROWS, LANES), jnp.float32),
            shape((TAIL_ROWS, LANES), jnp.float32),
            shape((KCONV, CONVCH), jnp.float32),
            shape((1, CONVCH), jnp.float32),
            shape((8, LANES), jnp.float32),
            shape((1, INNER), jnp.float32),
            shape((1, D), jnp.float32),
            shape((1, INNER), jnp.float32),
        ),
        in_specs=[SMEM] + [ANY] * len(parts),
        out_specs=(VMEM,) * 9,
        scratch_shapes=[
            pltpu.VMEM((held, BROWS, LANES), jnp.bfloat16),
            pltpu.VMEM((F0_ROWS, LANES), jnp.float32),
            pltpu.VMEM((D, LANES), jnp.float32),
            pltpu.SemaphoreType.DMA((len(parts),)),
        ],
        compiler_params=params(),
        cost_estimate=cost(16),
    )(table, *parts)


def unpack_out_kernel(table, own, got, head, tail, w_out, flat, held, sem):
    half = own.shape[0]
    copy_all([(own, held.at[pl.ds(0, half)]), (got, held.at[pl.ds(half, half)])], sem)
    flat[0:HEAD_ROWS, :] = head[...]
    flat[OUT_ROWS - TAIL_ROWS : OUT_ROWS, :] = tail[...]
    spread_blocks(table, held, flat, N1, HEAD_ROWS)
    rows = 128

    def step(i, carry):
        at = pl.multiple_of(i * rows, rows)
        for j in range(OUT_TILES):
            x = flat[pl.ds(at * OUT_TILES + j, rows, stride=OUT_TILES), :]
            w_out[pl.ds(at, rows), j * LANES : (j + 1) * LANES] = x.astype(jnp.bfloat16)
        return carry

    lax.fori_loop(0, INNER // rows, step, 0)


def unpack_out(table, own, got, head, tail):
    return pl.pallas_call(
        unpack_out_kernel,
        out_shape=shape((INNER, D), jnp.bfloat16),
        in_specs=[SMEM, ANY, ANY, VMEM, VMEM],
        out_specs=VMEM,
        scratch_shapes=[
            pltpu.VMEM((OUT_ROWS, LANES), jnp.float32),
            pltpu.VMEM((2 * own.shape[0], BROWS, LANES), jnp.bfloat16),
            pltpu.SemaphoreType.DMA((2,)),
        ],
        compiler_params=params(),
    )(table, own, got, head, tail)


def permute_units(table, flat, count, first_row, staged):
    many = 16

    def step(i, carry):
        for u in range(many):
            at = pl.multiple_of(first_row + (i * many + u) * UNIT, UNIT)
            staged[table[i * many + u]] = flat[pl.ds(at, UNIT), :]
        return carry

    lax.fori_loop(0, count // many, step, 0)
    for i in range(count // many * many, count):
        staged[table[i]] = flat[first_row + i * UNIT : first_row + (i + 1) * UNIT, :]


def pack_in_kernel(table, hidden, grad, head, *refs):
    outs, (turned, tiles, flat, staged, sem) = refs[:-5], refs[-5:]
    turned[...] = hidden[...].T
    lane = lax.broadcasted_iota(jnp.int32, (GROUPS, LANES), 1)

    def product(p, count):
        at = p * 2 * LANES
        at = at if isinstance(at, int) else pl.multiple_of(at, 2 * LANES)
        return jnp.dot(
            turned[...], grad[:, pl.ds(at, count * LANES)], preferred_element_type=jnp.float32
        )

    def put(p, value):
        for k in range(value.shape[1] // LANES):
            at = (p * 2 + k) * D
            at = at if isinstance(at, int) else pl.multiple_of(at, D)
            tiles[pl.ds(at, D), :] = value[:, k * LANES : (k + 1) * LANES]

    def load(rho, j):
        return tiles[pl.ds(j * D + rho, GROUPS, stride=GROUP), :]

    def whole(rho, i):
        first = -(-PROJ * rho // LANES)
        col0 = first * LANES - PROJ * rho
        x = load(rho, i)
        if col0:
            x = jnp.where(
                lane < LANES - col0,
                pltpu.roll(x, LANES - col0, 1),
                pltpu.roll(load(rho, i + 1), LANES - col0, 1),
            )
        flat[pl.ds(first + i, GROUPS, stride=GROUP_ROWS), :] = x

    put(0, product(0, 2))
    put(1, product(1, 2))
    pairs = COL_TILES // 2

    def step(p, carry):
        for i in range(2):
            for rho in range(GROUP):
                whole(rho, p * 2 + i)
        put(p + 2, product(p + 2, 2))
        return carry

    lax.fori_loop(0, pairs - 2, step, 0)
    put(pairs, product(pairs, COL_TILES % 2))
    for rho in range(GROUP):
        first = -(-PROJ * rho // LANES)
        col0 = first * LANES - PROJ * rho
        full = (PROJ - col0) // LANES
        for i in range((pairs - 2) * 2, full):
            whole(rho, i)
        left = PROJ - col0 - full * LANES
        if left:
            begin = col0 + full * LANES
            j, s = begin // LANES, begin % LANES
            x = pltpu.roll(load(rho, j), LANES - s, 1) if s else load(rho, j)
            if s + left > LANES:
                x = jnp.where(lane < LANES - s, x, pltpu.roll(load(rho, j + 1), LANES - s, 1))
            y = pltpu.roll(load(rho + 1, 0), left, 1)
            flat[pl.ds(first + full, GROUPS, stride=GROUP_ROWS), :] = jnp.where(lane < left, x, y)
    flat[IN_ROWS : IN_ROWS + HEAD_ROWS, :] = head[...]
    permute_units(table, flat, MID0 * UNITS, 0, staged)
    copies, at = [], 0
    for out in outs:
        copies.append((staged.at[pl.ds(at, out.shape[0])], out))
        at += out.shape[0]
    copy_all(copies, sem)


def pack_in(table, hidden, grad, head, sizes):
    return pl.pallas_call(
        pack_in_kernel,
        out_shape=tuple(shape((n, UNIT, LANES), jnp.float32) for n in sizes),
        in_specs=[SMEM, VMEM, VMEM, VMEM],
        out_specs=(ANY,) * len(sizes),
        scratch_shapes=[
            pltpu.VMEM((D, hidden.shape[0]), jnp.bfloat16),
            pltpu.VMEM((COL_TILES * D, LANES), jnp.float32),
            pltpu.VMEM((MID0 * BROWS, LANES), jnp.float32),
            pltpu.VMEM((sum(sizes), UNIT, LANES), jnp.float32),
            pltpu.SemaphoreType.DMA((len(sizes),)),
        ],
        compiler_params=params(),
        cost_estimate=cost(20),
    )(table, hidden, grad, head)


def pack_out_kernel(table, grad, local, keep, send, head, tail, flat, out, sem, *, slots):
    rows = 128

    def step(i, carry):
        at = pl.multiple_of(i * rows, rows)
        for j in range(OUT_TILES):
            flat[pl.ds(at * OUT_TILES + j, rows, stride=OUT_TILES), :] = grad[
                pl.ds(at, rows), j * LANES : (j + 1) * LANES
            ]
        return carry

    lax.fori_loop(0, INNER // rows, step, 0)
    head[...] = flat[0:HEAD_ROWS, :]
    tail[...] = flat[OUT_ROWS - TAIL_ROWS : OUT_ROWS, :]
    permute_units(table, flat, N1 * UNITS, HEAD_ROWS, out)

    def add_local(i, carry):
        out[i * slots + slots - 1] = local[...]
        return carry

    lax.fori_loop(0, out.shape[0] // slots, add_local, 0)
    half = keep.shape[0]
    copy_all([(out.at[pl.ds(0, half)], keep), (out.at[pl.ds(half, half)], send)], sem)


def pack_out(table, grad, local, devices, slots):
    return pl.pallas_call(
        partial(pack_out_kernel, slots=slots),
        out_shape=(
            shape((devices * slots // 2, UNIT, LANES), jnp.float32),
            shape((devices * slots // 2, UNIT, LANES), jnp.float32),
            shape((HEAD_ROWS, LANES), jnp.float32),
            shape((TAIL_ROWS, LANES), jnp.float32),
        ),
        in_specs=[SMEM, VMEM, VMEM],
        out_specs=(ANY, ANY, VMEM, VMEM),
        scratch_shapes=[
            pltpu.VMEM((OUT_ROWS, LANES), jnp.float32),
            pltpu.VMEM((devices * slots, UNIT, LANES), jnp.float32),
            pltpu.SemaphoreType.DMA((2,)),
        ],
        compiler_params=params(),
    )(table, grad, local)


def adam_kernel(table, scale, got, late, limit, used, master, first, second, o_first, o_second, o_master, flat, held):
    capacity = master.shape[0]

    def step(i, carry):
        for u in range(UNITS):
            at = table[i * UNITS + u]
            rows = pl.ds(pl.multiple_of(i * BROWS + u * UNIT, UNIT), UNIT)
            flat[rows, :] = held[at]
        return carry

    held[0 : got.shape[0]] = got[...]
    held[got.shape[0] :] = late[...]
    lax.fori_loop(0, capacity, step, 0)
    lane = lax.broadcasted_iota(jnp.int32, (capacity, LANES), 1)
    divisor = scale[0]
    for j in range(BROWS):
        cols = slice(j * LANES, (j + 1) * LANES)
        grad = jnp.where(used[...] > 0, flat[pl.ds(j, capacity, stride=BROWS), :], 0.0) / divisor
        matrix = lane + j * LANES < limit[...]
        weights = master[:, cols]
        new_first = BETA_ONE * first[:, cols] + (1.0 - BETA_ONE) * grad
        new_second = BETA_TWO * second[:, cols] + (1.0 - BETA_TWO) * grad * grad
        normal = (
            new_first
            / (1.0 - BETA_ONE**STEP)
            / (jnp.sqrt(new_second / (1.0 - BETA_TWO**STEP)) + ADAM_EPS)
        )
        rate = jnp.where(matrix, MATRIX_RATE, VECTOR_RATE)
        decay = jnp.where(matrix, WEIGHT_DECAY, 0.0)
        o_first[:, cols] = new_first
        o_second[:, cols] = new_second
        o_master[:, cols] = weights - rate * (normal + decay * weights)


def adam(table, divisor, got, late, limit, used, master, first, second):
    capacity = master.shape[0]
    return pl.pallas_call(
        adam_kernel,
        out_shape=(shape(master.shape, jnp.float32),) * 3,
        in_specs=[SMEM, SMEM] + [VMEM] * 7,
        out_specs=(VMEM,) * 3,
        scratch_shapes=[
            pltpu.VMEM((capacity * BROWS, LANES), jnp.float32),
            pltpu.VMEM((got.shape[0] + late.shape[0], UNIT, LANES), jnp.float32),
        ],
        compiler_params=params(),
    )(table, divisor.reshape(1), got, late, limit, used, master, first, second)


def doubled(values, step):
    return jnp.concatenate([values, exchange(values, step)], axis=0)


def gather_steps(values, order):
    for step in order[:0:-1]:
        values = doubled(values, step)
    return values, exchange(values, order[0])


def reduce_step(values, step, extra=None):
    half = values.shape[0] // 2
    if extra is None:
        return values[:half] + exchange(values[half:], step)
    got = exchange(jnp.concatenate([values[half:], extra]), step)
    return values[:half] + got[:half], extra + got[half:]


CHUNK = 128
PAIRS = HEADS // 2
MIXW = INNER + 2 * NSTATE
DT_AT = INNER + CONVCH
F32 = jnp.float32
BF16 = jnp.bfloat16
NN = (((1,), (0,)), ((), ()))
NT = (((1,), (1,)), ((), ()))


def dot(a, b, dims=NN):
    return lax.dot_general(a, b, dims, preferred_element_type=F32)


def split(v):
    high = v.astype(BF16)
    return high, (v - high.astype(F32)).astype(BF16)


def dot3(a, b, dims=NN):
    ah, al = a
    bh, bl = b
    return dot(ah, bh, dims) + (dot(ah, bl, dims) + dot(al, bh, dims))


def heads_gather():
    return jnp.asarray(np.repeat(np.eye(HEADS, LANES, dtype=np.float32), HEADDIM, axis=0), BF16)


def three_parts(v):
    high = v.astype(BF16).astype(F32)
    rest = v - high
    middle = rest.astype(BF16).astype(F32)
    low = rest - middle
    return (high + pltpu.roll(middle, 32, 1) + pltpu.roll(low, 64, 1)).astype(BF16)


def triangle_sum(tri, v):
    parts = dot(tri, three_parts(v))
    lane = lax.broadcasted_iota(jnp.int32, parts.shape, 1)
    total = parts + pltpu.roll(parts, LANES - 32, 1) + pltpu.roll(parts, LANES - 64, 1)
    return jnp.where(lane < HEADS, total, 0.0)


def chunk_decays(dt, dt_bias, a_log):
    lane = lax.broadcasted_iota(jnp.int32, (CHUNK, LANES), 1)
    row = lax.broadcasted_iota(jnp.int32, (CHUNK, LANES), 0)
    shifted = dt + dt_bias
    delta = jnp.where(
        lane < HEADS, jnp.maximum(shifted, 0.0) + jnp.log1p(jnp.exp(-jnp.abs(shifted))), 0.0
    )
    rate = -jnp.exp(a_log)
    lower = (row >= lane).astype(BF16)
    cum = triangle_sum(lower, delta * rate)
    last = cum[CHUNK - 1 : CHUNK, :]
    return shifted, delta, rate, cum, last


def pair_mask():
    lane = lax.broadcasted_iota(jnp.int32, (CHUNK, LANES), 1)
    low = (lane < HEADDIM).astype(F32)
    return low.astype(BF16), (1.0 - low).astype(BF16)


QUADS = HEADS // 4
QWIDTH = 4 * HEADDIM


def sigmoid(v):
    return 0.5 * jnp.tanh(0.5 * v) + 0.5


def silu(v):
    return v * sigmoid(v)


def side_by_side(v):
    high, low = split(v)
    return jnp.concatenate([high, low], axis=1), high


def dot_parts(a, b):
    ahl, ah = a
    bh, bl = b
    return dot(ahl, jnp.concatenate([bh, bh], axis=0)) + dot(ah, bl)


def dot_turned(a, b):
    ah, al = a
    bh, bl = b
    both = dot(ah, jnp.concatenate([bh, bl], axis=0), NT)
    n = bh.shape[0]
    return both[:, :n] + both[:, n:] + dot(al, bh, NT)


def widen(delta, cum, quad):
    lane = lax.broadcasted_iota(jnp.int32, (CHUNK, LANES), 1)
    over = lambda v, h: jnp.broadcast_to(v[:, h : h + 1], (CHUNK, LANES))
    first = 4 * quad
    columns = [over(cum, first + k) for k in range(4)]
    rates = [over(delta, first + k) for k in range(4)]
    pair = lambda vs: jnp.concatenate(
        [jnp.where(lane < HEADDIM, vs[0], vs[1]), jnp.where(lane < HEADDIM, vs[2], vs[3])], axis=1
    )
    return pair(rates), pair(columns), columns


def pair_rows(parts, j, low, high):
    cols = slice(j * LANES, (j + 1) * LANES)
    return [jnp.concatenate([p[:, cols] * low, p[:, cols] * high], axis=0) for p in parts]


def scan_forward_kernel(
    mixed, dt, gate, dt_bias, a_log, skip, gain, ssm, mixed_out, states, state
):
    @pl.when(pl.program_id(0) == 0)
    def _():
        state[...] = jnp.zeros_like(state)

    states[0] = state[...]
    _, delta, _, cum, last = chunk_decays(dt[...], dt_bias[...], a_log[...])
    lane = lax.broadcasted_iota(jnp.int32, (CHUNK, LANES), 1)
    row = lax.broadcasted_iota(jnp.int32, (CHUNK, LANES), 0)
    bias = jnp.where(row >= lane, 0.0, -1e30)
    cum_t = cum.T
    inputs_b = mixed[:, INNER : INNER + NSTATE]
    readout = mixed[:, INNER + NSTATE :]
    affinity = dot3(split(readout), split(inputs_b), NT)
    readout_parts = side_by_side(readout)
    b_parts = side_by_side(inputs_b.T)
    low, high = pair_mask()
    squares = jnp.zeros((CHUNK, LANES), F32)
    for quad in range(QUADS):
        cols = slice(quad * QWIDTH, (quad + 1) * QWIDTH)
        wide_delta, wide_cum, columns = widen(delta, cum, quad)
        values = mixed[:, cols]
        scaled = values * wide_delta
        parts = split(scaled)
        outs = []
        for j in range(2):
            right_h, right_l = pair_rows(parts, j, low, high)
            left = []
            for k in range(2):
                h = 4 * quad + 2 * j + k
                within = jnp.exp(columns[2 * j + k] - cum_t[h : h + 1, :] + bias)
                left.append(split(affinity * within))
            left_h = jnp.concatenate([left[0][0], left[1][0]], axis=1)
            left_l = jnp.concatenate([left[0][1], left[1][1]], axis=1)
            both = dot(left_h, jnp.concatenate([right_h, right_l], axis=1))
            outs.append(both[:, :LANES] + both[:, LANES:] + dot(left_l, right_h))
        carried = state[:, cols]
        grown = jnp.exp(wide_cum)
        out = jnp.concatenate(outs, axis=1) + dot_parts(readout_parts, split(carried)) * grown
        out = out + skip[:, cols] * values
        tail = jnp.exp(wide_cum[CHUNK - 1 :] - wide_cum)
        state[:, cols] = carried * grown[CHUNK - 1 :] + dot_parts(b_parts, split(scaled * tail))
        ssm[:, cols] = out
        gated = out * silu(gate[:, cols])
        squares = squares + gated[:, :LANES] * gated[:, :LANES] + gated[:, LANES:] * gated[:, LANES:]
    rho = lax.rsqrt(jnp.sum(squares, axis=1, keepdims=True) * (1.0 / INNER) + NORM_EPS)
    for j in range(PAIRS):
        cols = slice(j * LANES, (j + 1) * LANES)
        gated = ssm[:, cols] * silu(gate[:, cols])
        mixed_out[:, cols] = (gated * rho * gain[:, cols]).astype(BF16)


def scan_forward(mixed, projected, dt_bias, a_log, skip, gain):
    length = mixed.shape[0]
    chunks = length // CHUNK
    whole = lambda v: pl.BlockSpec(v.shape, lambda i: (0,) * v.ndim)
    return pl.pallas_call(
        scan_forward_kernel,
        grid=(chunks,),
        out_shape=(
            shape((length, INNER), F32),
            shape((length, INNER), BF16),
            shape((chunks, NSTATE, INNER), F32),
        ),
        in_specs=[
            pl.BlockSpec((CHUNK, MIXW), lambda i: (i, 0)),
            pl.BlockSpec((CHUNK, LANES), lambda i: (i, DT_AT // LANES)),
            pl.BlockSpec((CHUNK, INNER), lambda i: (i, 0)),
        ]
        + [whole(v) for v in (dt_bias, a_log, skip, gain)],
        out_specs=(
            pl.BlockSpec((CHUNK, INNER), lambda i: (i, 0)),
            pl.BlockSpec((CHUNK, INNER), lambda i: (i, 0)),
            pl.BlockSpec((1, NSTATE, INNER), lambda i: (i, 0, 0)),
        ),
        scratch_shapes=[pltpu.VMEM((NSTATE, INNER), F32)],
        compiler_params=params(),
        cost_estimate=cost(40),
    )(mixed, projected, projected, dt_bias, a_log, skip, gain)


def scan_backward_kernel(
    mixed, dt, ssm, grad, states, dt_bias, a_log, skip, gather, held,
    grad_mixed, grad_dt, sums, skip_sums, grad_state, left, right,
):
    @pl.when(pl.program_id(0) == 0)
    def _():
        grad_state[...] = jnp.zeros_like(grad_state)
        sums[...] = jnp.zeros_like(sums)
        skip_sums[...] = jnp.zeros_like(skip_sums)

    shifted, delta, rate, cum, last = chunk_decays(dt[...], dt_bias[...], a_log[...])
    lane = lax.broadcasted_iota(jnp.int32, (CHUNK, LANES), 1)
    row = lax.broadcasted_iota(jnp.int32, (CHUNK, LANES), 0)
    bias = jnp.where(lane >= row, 0.0, -1e30)
    heads = lane < HEADS
    cum_t = cum.T
    inputs_b = mixed[:, INNER : INNER + NSTATE]
    readout = mixed[:, INNER + NSTATE :]
    b_parts, c_parts = split(inputs_b), split(readout)
    b_wide = side_by_side(inputs_b)
    c_turned = side_by_side(readout.T)
    affinity = dot3(b_parts, c_parts, NT)
    low, high = pair_mask()
    grad_affinity = jnp.zeros((CHUNK, CHUNK), F32)
    grad_b = jnp.zeros((CHUNK, NSTATE), F32)
    grad_c = jnp.zeros((CHUNK, NSTATE), F32)
    last_row = lax.broadcasted_iota(jnp.int32, (CHUNK, QWIDTH), 0) == CHUNK - 1
    for quad in range(QUADS):
        cols = slice(quad * QWIDTH, (quad + 1) * QWIDTH)
        wide_delta, wide_cum, columns = widen(delta, cum, quad)
        grown = jnp.exp(wide_cum)
        tail = jnp.exp(wide_cum[CHUNK - 1 :] - wide_cum)
        end = grown[CHUNK - 1 :]
        values = mixed[:, cols]
        pulled = grad[:, cols]
        scaled = values * wide_delta
        x_parts, p_parts = split(scaled), split(pulled)
        outs = []
        for j in range(2):
            half = slice(j * LANES, (j + 1) * LANES)
            xh, xl = x_parts[0][:, half], x_parts[1][:, half]
            right_h, right_l = pair_rows(p_parts, j, low, high)
            pull = dot(
                jnp.concatenate([xh, xl], axis=1),
                jnp.concatenate([right_h, right_h], axis=1),
                NT,
            ) + dot(xh, right_l, NT)
            kernels = []
            for k in range(2):
                h = 4 * quad + 2 * j + k
                within = jnp.exp(cum_t[h : h + 1, :] - columns[2 * j + k] + bias)
                kernels.append(split(affinity * within))
                grad_affinity = grad_affinity + within * pull[:, k * CHUNK : (k + 1) * CHUNK]
            kernel_h = jnp.concatenate([kernels[0][0], kernels[1][0]], axis=1)
            kernel_l = jnp.concatenate([kernels[0][1], kernels[1][1]], axis=1)
            both = dot(kernel_h, jnp.concatenate([right_h, right_l], axis=1))
            outs.append(both[:, :LANES] + both[:, LANES:] + dot(kernel_l, right_h))
        late = grad_state[:, cols]
        late_parts = split(late)
        early = states[0, :, cols]
        from_state = dot_parts(b_wide, late_parts) * tail
        grad_scaled = jnp.concatenate(outs, axis=1) + from_state
        pulled_cum = split(pulled * grown)
        grad_c = grad_c + dot_turned(pulled_cum, split(early))
        grad_b = grad_b + dot_turned(split(scaled * tail), late_parts)
        grad_state[:, cols] = late * end + dot_parts(c_turned, pulled_cum)
        grad_mixed[:, cols] = grad_scaled * wide_delta + skip[:, cols] * pulled
        skip_sums[:, cols] += jnp.sum(pulled * values, axis=0, keepdims=True)
        left[:, cols] = grad_scaled * values
        inner = pulled * (ssm[:, cols] - skip[:, cols] * values) - scaled * grad_scaled
        extra = jnp.sum(scaled * from_state, axis=0, keepdims=True) + end * jnp.sum(
            late * early, axis=0, keepdims=True
        )
        right[:, cols] = inner + jnp.where(last_row, extra, 0.0)
    ga_parts = split(grad_affinity)
    grad_mixed[:, INNER : INNER + NSTATE] = grad_b + dot3(ga_parts, c_parts)
    grad_mixed[:, INNER + NSTATE :] = grad_c + dot3(split(grad_affinity.T), b_parts)

    def by_head(v):
        high, low = split(v)
        g = gather[...]
        return dot(high, g) + dot(low, g)

    direct = by_head(left[...])
    grad_cum = by_head(right[...])
    upper = (lane >= row).astype(BF16)
    after = triangle_sum(upper, grad_cum)
    grad_delta = direct + rate * after
    grad_raw = jnp.where(heads, grad_delta * sigmoid(shifted), 0.0)
    grad_dt[...] = grad_raw.astype(BF16)
    sums[0:1, :] += jnp.sum(grad_raw, axis=0, keepdims=True)
    sums[1:2, :] += rate * jnp.sum(delta * after, axis=0, keepdims=True)


def scan_backward(mixed, projected, ssm, grad, states, dt_bias, a_log, skip, gather, held):
    length = mixed.shape[0]
    chunks = length // CHUNK
    whole = lambda v: pl.BlockSpec(v.shape, lambda i: (0,) * v.ndim)
    back = lambda i: (chunks - 1 - i, 0)
    return pl.pallas_call(
        scan_backward_kernel,
        grid=(chunks,),
        out_shape=(
            shape((length, MIXW), F32),
            shape(held.shape, BF16),
            shape((8, LANES), F32),
            shape((1, INNER), F32),
        ),
        in_specs=[
            pl.BlockSpec((CHUNK, MIXW), back),
            pl.BlockSpec((CHUNK, LANES), lambda i: (chunks - 1 - i, DT_AT // LANES)),
            pl.BlockSpec((CHUNK, INNER), back),
            pl.BlockSpec((CHUNK, INNER), back),
            pl.BlockSpec((1, NSTATE, INNER), lambda i: (chunks - 1 - i, 0, 0)),
        ]
        + [whole(v) for v in (dt_bias, a_log, skip, gather)]
        + [ANY],
        out_specs=(
            pl.BlockSpec((CHUNK, MIXW), back),
            pl.BlockSpec((CHUNK, LANES), lambda i: (chunks - 1 - i, DT_AT // LANES)),
            pl.BlockSpec((8, LANES), lambda i: (0, 0)),
            pl.BlockSpec((1, INNER), lambda i: (0, 0)),
        ),
        scratch_shapes=[pltpu.VMEM((NSTATE, INNER), F32)] + [pltpu.VMEM((CHUNK, INNER), F32)] * 2,
        compiler_params=params(),
        input_output_aliases={9: 1},
        cost_estimate=cost(35),
    )(mixed, projected, ssm, grad, states, dt_bias, a_log, skip, gather, held)


ROWS_AT_ONCE = 128
CONV_TILES = 2


def down(v, before, by):
    moved = pltpu.roll(v, by, 0)
    row = lax.broadcasted_iota(jnp.int32, (8, LANES), 0)
    top = jnp.where(row < by, pltpu.roll(before, by, 0), moved[:8])
    return jnp.concatenate([top, moved[8:]], axis=0)


def up(v, after, by):
    rows = v.shape[0]
    moved = pltpu.roll(v, rows - by, 0)
    row = lax.broadcasted_iota(jnp.int32, (8, LANES), 0)
    end = jnp.where(row < 8 - by, moved[rows - 8 :], pltpu.roll(after, 8 - by, 0))
    return jnp.concatenate([moved[: rows - 8], end], axis=0)


def conv_terms(conv_in, at, cols):
    rows = conv_in[at : at + ROWS_AT_ONCE, cols]
    before = conv_in[at - 8 : at, cols] if at else jnp.zeros((8, LANES), F32)
    return [down(rows, before, KCONV - 1 - k) for k in range(KCONV - 1)] + [rows]


def conv_sum(terms, weight, bias):
    total = bias + terms[KCONV - 1] * weight[KCONV - 1 : KCONV]
    for k in range(KCONV - 1):
        total = total + terms[k] * weight[k : k + 1]
    return total


def conv_forward_kernel(conv_in, weight, bias, mixed):
    for tile in range(CONV_TILES):
        cols = slice(tile * LANES, (tile + 1) * LANES)
        w, b = weight[:, cols], bias[:, cols]
        for at in range(0, conv_in.shape[0], ROWS_AT_ONCE):
            mixed[at : at + ROWS_AT_ONCE, cols] = silu(conv_sum(conv_terms(conv_in, at, cols), w, b))


def conv_forward(projected, weight, bias):
    length = projected.shape[0]
    width = CONV_TILES * LANES
    return pl.pallas_call(
        conv_forward_kernel,
        grid=(CONVCH // width,),
        out_shape=shape((length, CONVCH), F32),
        in_specs=[
            pl.BlockSpec((length, width), lambda i: (0, INNER // width + i)),
            pl.BlockSpec((KCONV, width), lambda i: (0, i)),
            pl.BlockSpec((1, width), lambda i: (0, i)),
        ],
        out_specs=pl.BlockSpec((length, width), lambda i: (0, i)),
        compiler_params=params(),
        cost_estimate=cost(10),
    )(projected, weight, bias)


def conv_backward_kernel(conv_in, grad, weight, bias, held, out, sums):
    length = conv_in.shape[0]
    for tile in range(CONV_TILES):
        cols = slice(tile * LANES, (tile + 1) * LANES)
        w, b = weight[:, cols], bias[:, cols]
        totals = [jnp.zeros((1, LANES), F32)] * (KCONV + 1)
        after = jnp.zeros((8, LANES), F32)
        for at in range(length - ROWS_AT_ONCE, -1, -ROWS_AT_ONCE):
            terms = conv_terms(conv_in, at, cols)
            value = conv_sum(terms, w, b)
            sig = sigmoid(value)
            g = grad[at : at + ROWS_AT_ONCE, cols] * (sig * (1.0 + value * (1.0 - sig)))
            for k in range(KCONV):
                totals[k] = totals[k] + jnp.sum(g * terms[k], axis=0, keepdims=True)
            totals[KCONV] = totals[KCONV] + jnp.sum(g, axis=0, keepdims=True)
            total = g * w[KCONV - 1 : KCONV]
            for k in range(KCONV - 1):
                total = total + up(g, after, KCONV - 1 - k) * w[k : k + 1]
            after = g[:8]
            out[at : at + ROWS_AT_ONCE, cols] = total.astype(BF16)
        for k in range(KCONV + 1):
            sums[k : k + 1, cols] = totals[k]


def conv_backward(projected, grad_mixed, weight, bias, held):
    length = projected.shape[0]
    width = CONV_TILES * LANES
    return pl.pallas_call(
        conv_backward_kernel,
        grid=(CONVCH // width,),
        out_shape=(shape(held.shape, BF16), shape((8, CONVCH), F32)),
        in_specs=[
            pl.BlockSpec((length, width), lambda i: (0, INNER // width + i)),
            pl.BlockSpec((length, width), lambda i: (0, i)),
            pl.BlockSpec((KCONV, width), lambda i: (0, i)),
            pl.BlockSpec((1, width), lambda i: (0, i)),
            ANY,
        ],
        out_specs=(
            pl.BlockSpec((length, width), lambda i: (0, INNER // width + i)),
            pl.BlockSpec((8, width), lambda i: (0, i)),
        ),
        input_output_aliases={4: 0},
        compiler_params=params(),
        cost_estimate=cost(12),
    )(projected, grad_mixed, weight, bias, held)


def middle_kernel(
    limit, mixed_out, w_out, tokens, teacher, mask, ssm, gate, gain,
    block_out, grad_result, grad_branch, grad_ssm, grad_gate, error, gain_sums,
):
    step = pl.program_id(0)

    @pl.when(step == 0)
    def _():
        error[...] = jnp.zeros_like(error)
        gain_sums[...] = jnp.zeros_like(gain_sums)

    rows = tokens.shape[0]
    result = tokens[...].astype(F32) + dot(mixed_out[...], w_out[...])
    position = step * rows + lax.broadcasted_iota(jnp.int32, (rows, 1), 0)
    valid = (position < limit[0]).astype(F32)
    weight = valid * mask[:, 0:1]
    block_out[...] = (result * valid).astype(BF16)
    misfit = result - teacher[...].astype(F32)
    pulled = 2.0 * weight * misfit
    grad_result[...] = pulled
    error[...] += jnp.sum(0.5 * pulled * misfit, axis=0, keepdims=True)
    low = pulled.astype(BF16)
    grad_branch[...] = low
    grad_mixed = dot(low, w_out[...], NT)
    g = gate[...]
    sig = sigmoid(g)
    act = g * sig
    inner = ssm[...]
    gated = inner * act
    rho = lax.rsqrt(jnp.mean(gated * gated, axis=1, keepdims=True) + NORM_EPS)
    unit = gated * rho
    gain_sums[...] += jnp.sum(unit * grad_mixed, axis=0, keepdims=True)
    grad_unit = grad_mixed * gain[...]
    share = jnp.mean(grad_unit * unit, axis=1, keepdims=True)
    grad_gated = rho * (grad_unit - unit * share)
    grad_ssm[...] = grad_gated * act
    grad_gate[...] = (grad_gated * inner * (sig * (1.0 + g * (1.0 - sig)))).astype(BF16)


def middle(limit, mixed_out, w_out, tokens, teacher, mask, ssm, projected, gain):
    length = tokens.shape[0]
    rows = 256
    by_row = lambda width: pl.BlockSpec((rows, width), lambda i: (i, 0))
    whole = lambda v: pl.BlockSpec(v.shape, lambda i: (0,) * v.ndim)
    return pl.pallas_call(
        middle_kernel,
        grid=(length // rows,),
        out_shape=(
            shape((length, D), BF16),
            shape((length, D), F32),
            shape((length, D), BF16),
            shape((length, INNER), F32),
            shape((length, WIDE), BF16),
            shape((1, D), F32),
            shape((1, INNER), F32),
        ),
        in_specs=[
            SMEM,
            by_row(INNER),
            whole(w_out),
            by_row(D),
            by_row(D),
            by_row(LANES),
            by_row(INNER),
            by_row(INNER),
            whole(gain),
        ],
        out_specs=(
            by_row(D),
            by_row(D),
            by_row(D),
            by_row(INNER),
            by_row(INNER),
            pl.BlockSpec((1, D), lambda i: (0, 0)),
            pl.BlockSpec((1, INNER), lambda i: (0, 0)),
        ),
        compiler_params=params(),
        cost_estimate=cost(25),
    )(limit, mixed_out, w_out, tokens, teacher, mask, ssm, projected, gain)


def body(tokens, teacher, lengths, loss_mask, owners, master, first_moment, second_moment):
    capacity = master.shape[0]
    dp, fsdp = lax.axis_size("dp"), lax.axis_size("fsdp")
    devices = dp * fsdp
    me = lax.axis_index(AXES).astype(jnp.int32)
    x_first, y_first, z_first = step_orders(dp, fsdp)
    tie = lambda *values: lax.optimization_barrier(values)

    sent = send_blocks(owners, master, devices, me)
    at_home = lax.all_to_all(sent, AXES, 0, 0, tiled=True)
    owners, tokens, loss_mask, _ = tie(owners, tokens, loss_mask, sent)
    plan = make_plan(owners, capacity, devices, me)
    n0, n1 = plan["slots"]
    streams = cut(n0, (x_first, y_first, z_first))
    table = stream_places(plan["home"], plan["slot"], me, streams, devices)
    table0 = jnp.concatenate([table[:MID0], table[MID1:]])
    table1 = (place_of(plan["home"] ^ me, x_first) * n1 + plan["slot"])[MID0:MID1]
    u0, u1 = plan["unit_slots"]
    unit_streams = cut(u0, (x_first, y_first, x_first, y_first, z_first))
    unit_table = stream_places(plan["unit_home"], plan["unit_slot"], me, unit_streams, devices)
    unit_table = unit_table[:MID0].reshape(-1)
    unit_table1 = place_of(plan["unit_home"] ^ me, x_first) * (u1 + 1) + plan["unit_slot"]
    unit_table1 = unit_table1[MID0:MID1].reshape(-1)
    inputs, target = tokens[0], teacher[0]
    mask = jnp.broadcast_to(loss_mask[0].astype(F32)[:, None], (inputs.shape[0], LANES))
    wide_in = inputs.astype(F32)
    inverse = lax.rsqrt(jnp.mean(wide_in * wide_in, axis=-1, keepdims=True) + NORM_EPS)
    position = jnp.arange(inputs.shape[0], dtype=jnp.int32)
    counted = jnp.sum(jnp.where(position < lengths[0], loss_mask[0], 0)).astype(F32)
    limit = jnp.broadcast_to((END_OUT - plan["row_block"] * PBLOCK)[:, None], (capacity, LANES))
    used = jnp.broadcast_to(plan["row_used"].astype(jnp.int32)[:, None], (capacity, LANES))
    received = jnp.concatenate(plan["received"])
    (at_home, table0, table1, unit_table, unit_table1, inverse, counted, received, back_table,
     row_from) = tie(
        at_home, table0, table1, unit_table, unit_table1, inverse, counted, received,
        plan["back"], plan["row_from"],
    )
    sizes = [size for _, size, _ in streams] + [n1]
    *mine, mine1 = pick_blocks(received, at_home, sizes)
    parts = []
    for values, (_, _, order) in zip(mine, streams):
        parts += gather_steps(values, order)
    *parts, mine1, mask, limit, used = tie(*parts, mine1, mask, limit, used)
    late_steps = x_first[:0:-1]
    for step in late_steps[: max(len(late_steps) - 4, 0)]:
        mine1 = doubled(mine1, step)
    late_steps = late_steps[-4:]
    input_weight, head, tail, conv_weight, conv_bias, heads, skip, norm_gain, gate_gain = unpack_in(
        table0, parts
    )
    if late_steps[-4:-3]:
        mine1, input_weight = tie(doubled(mine1, late_steps[-4]), input_weight)
    dt_bias, a_log = heads[0:1], heads[1:2]
    gather = heads_gather()
    normed = wide_in * inverse
    hidden = (normed * norm_gain).astype(BF16)
    projected = dot(hidden, input_weight)
    if late_steps[-3:-2]:
        mine1, projected = tie(doubled(mine1, late_steps[-3]), projected)
    mixed = conv_forward(projected, conv_weight, conv_bias)
    if late_steps[-2:-1]:
        mine1, mixed = tie(doubled(mine1, late_steps[-2]), mixed)
    ssm, mixed_out, states = scan_forward(mixed, projected, dt_bias, a_log, skip, gate_gain)
    if late_steps:
        mine1, mixed_out = tie(doubled(mine1, late_steps[-1]), mixed_out)
    output_weight = unpack_out(table1, mine1, exchange(mine1, x_first[0]), head, tail)
    block_out, grad_result, grad_branch, grad_ssm, grad_low, errors, grad_gate = middle(
        lengths, mixed_out, output_weight, inputs, target, mask, ssm, projected, gate_gain
    )
    local = jnp.concatenate([errors.reshape(-1, LANES), jnp.broadcast_to(counted, (2, LANES))])
    grad_weight_out = dot(mixed_out, grad_branch, (((0,), (0,)), ((), ())))
    keep1, send1, head, tail = pack_out(unit_table1, grad_weight_out, local, devices, u1 + 1)
    sum1 = keep1 + exchange(send1, x_first[0])
    grad_ssm, sum1 = tie(grad_ssm, sum1)
    sum1 = reduce_step(sum1, x_first[1])
    grad_mixed, grad_low, sums, skip_sums = scan_backward(
        mixed, projected, ssm, grad_ssm, states, dt_bias, a_log, skip, gather, grad_low
    )
    grad_mixed, sum1 = tie(grad_mixed, sum1)
    if len(x_first) > 3:
        sum1 = reduce_step(sum1, x_first[2])
    grad_low, conv_sums = conv_backward(projected, grad_mixed, conv_weight, conv_bias, grad_low)
    grad_low, sum1 = tie(grad_low, sum1)
    halves = []
    for _, size, _ in unit_streams:
        halves += [devices * size // 2] * 2
    packed = list(pack_in(unit_table, hidden, grad_low, head, halves))
    reduced = [
        packed[2 * i] + exchange(packed[2 * i + 1], order[0])
        for i, (_, _, order) in enumerate(unit_streams)
    ]
    reduced[0], grad_low, conv_sums, sums, skip_sums, grad_gate = tie(
        reduced[0], grad_low, conv_sums, sums, skip_sums, grad_gate
    )
    grad_hidden = dot(grad_low, input_weight, NT)
    grad_norm = jnp.sum(grad_hidden * normed, axis=0)
    grad_normed = grad_hidden * norm_gain
    input_grad = grad_result + inverse * (
        grad_normed - normed * jnp.mean(grad_normed * normed, axis=-1, keepdims=True)
    )
    grad_vec = jnp.concatenate(
        [
            conv_sums[:KCONV].T.reshape(-1),
            conv_sums[KCONV],
            sums[0, :HEADS],
            sums[1, :HEADS],
            jnp.sum(skip_sums.reshape(HEADS, HEADDIM), axis=1),
            grad_norm,
            grad_gate[0],
            jnp.zeros((NBLK * PBLOCK - PTOT,), F32),
        ]
    ).reshape(VEC_ROWS, LANES)
    grad_vec = jnp.concatenate([tail, grad_vec]).reshape((NBLK - MID1) * UNITS, UNIT, LANES)
    reduced = [reduce_step(v, order[1]) for v, (_, _, order) in zip(reduced, unit_streams)]
    for step in x_first[:2]:
        grad_vec = grad_vec + exchange(grad_vec, step)
    first = [0, 1, len(reduced) - 1] if len(reduced) > 2 else [0]
    *tied, grad_vec, input_grad = tie(*[reduced[i] for i in first], grad_vec, input_grad)
    for i, values in zip(first, tied):
        reduced[i] = values
    for k in range(2, len(x_first) - 1):
        reduced[0], grad_vec = reduce_step(reduced[0], x_first[k], grad_vec)
        for i in range(1, len(reduced)):
            reduced[i] = reduce_step(reduced[i], unit_streams[i][2][k])
    for step in x_first[3:-1]:
        sum1 = reduce_step(sum1, step)
    ends = []
    for i, values in enumerate(reduced + [sum1]):
        half = values.shape[0] // 2
        given, step = values[half:], (unit_streams[i][2] if i < len(reduced) else x_first)[-1]
        if i == 0:
            got = exchange(jnp.concatenate([given, grad_vec]), step)
            grad_vec = grad_vec + got[half:]
            got = got[:half]
        else:
            got = exchange(given, step)
        ends += [values[:half], got]
    back = units_to_owners(back_table, ends)
    got = lax.all_to_all(back, AXES, 0, 0, tiled=True)
    local_sums = ends[-2][u1] + ends[-1][u1]
    error_sum = jnp.sum(local_sums[: D // LANES])
    divisor = local_sums[D // LANES, 0] * D
    new_first, new_second, new_master = adam(
        row_from,
        divisor,
        got,
        grad_vec,
        limit,
        used,
        master,
        first_moment,
        second_moment,
    )
    mean_loss = error_sum / divisor
    return (block_out[None], input_grad[None], mean_loss, new_first, new_second, new_master)


def solution(mesh):
    return jax.shard_map(
        body,
        mesh=mesh,
        in_specs=(
            P(AXES, None, None),
            P(AXES, None, None),
            P(AXES),
            P(AXES, None),
            P(),
            P(AXES, None),
            P(AXES, None),
            P(AXES, None),
        ),
        out_specs=(
            P(AXES, None, None),
            P(AXES, None, None),
            P(),
            P(AXES, None),
            P(AXES, None),
            P(AXES, None),
        ),
        check_vma=False,
    )
```

```python
from functools import partial

import jax
import jax.numpy as jnp
import numpy as np
from jax import lax
from jax.experimental import pallas as pl
from jax.experimental.pallas import tpu as pltpu
from jax.sharding import PartitionSpec as P

D = 768
INNER = 1536
NSTATE = 128
HEADDIM = 64
KCONV = 4
SCAN_LEN = 256
PBLOCK = 4096
STEP = 10
HEADS = 24
CONVCH = 1792
PROJ = 3352
PTOT = 3765320
NBLK = 920

LANES = 128
BROWS = PBLOCK // LANES
UNIT = 8
UNITS = BROWS // UNIT
END_IN = D * PROJ
END_OUT = END_IN + INNER * D
MID0 = -(-END_IN // PBLOCK)
MID1 = END_OUT // PBLOCK
N0 = MID0 + NBLK - MID1
N1 = MID1 - MID0
F0_ROWS = N0 * BROWS
IN_ROWS = END_IN // LANES
HEAD_ROWS = MID0 * BROWS - IN_ROWS
TAIL_ROWS = (END_OUT - MID1 * PBLOCK) // LANES
OUT_ROWS = INNER * D // LANES
VEC_ROWS = (NBLK - MID1) * BROWS - TAIL_ROWS
VEC_AT = MID0 * BROWS + TAIL_ROWS
GROUP = 16
GROUPS = D // GROUP
GROUP_ROWS = GROUP * PROJ // LANES
COL_TILES = -(-PROJ // LANES)
WIDE = COL_TILES * LANES
OUT_TILES = D // LANES

NORM_EPS = 1e-05
ADAM_EPS = 1e-08
BETA_ONE = 0.9
BETA_TWO = 0.999
MATRIX_RATE = 0.03
VECTOR_RATE = 0.2
WEIGHT_DECAY = 0.1
PRECISE = lax.Precision.HIGHEST
AXES = ("dp", "fsdp")
VMEM_LIMIT = 60 * 1024 * 1024


def bits_of(count):
    return count.bit_length() - 1


def step_orders(dp, fsdp):
    wide = [("dp", i) for i in range(bits_of(dp))]
    narrow = [("fsdp", i) for i in range(bits_of(fsdp))]
    first = wide[:2] + narrow + wide[2:]
    second = wide[:1] + narrow + wide[1:]
    third = wide[:1] + wide[2:] + wide[1:2] + narrow
    return first, second, third


def cut(total, orders):
    base, more = divmod(total, len(orders))
    streams, at = [], 0
    for i, order in enumerate(orders):
        size = base + (i < more)
        if size:
            streams.append((at, size, order))
        at += size
    return streams


def exchange(values, step):
    axis, bit = step
    size = lax.axis_size(axis)
    return lax.ppermute(values, axis, [(i, i ^ (1 << bit)) for i in range(size)])


def place_of(relative, order):
    shift_of = {"dp": bits_of(lax.axis_size("fsdp")), "fsdp": 0}
    place = jnp.zeros_like(relative)
    for axis, bit in order:
        place = place * 2 + ((relative >> (shift_of[axis] + bit)) & 1)
    return place


def class_counts(owners, devices):
    block = jnp.arange(NBLK, dtype=jnp.int32)
    mid = ((block >= MID0) & (block < MID1))[None, :]
    device = jnp.arange(devices, dtype=jnp.int32)
    below = owners[None, :] < device[:, None]
    owned = owners[None, :] == device[:, None]

    def total(mask):
        return jnp.sum(mask.astype(jnp.int32), axis=1)

    start = (total(below & ~mid), total(below & mid))
    count = (total(owned & ~mid), total(owned & mid))
    return start, count, total(owned & (block < MID0)[None, :])


def my_counts(owners, me):
    block = jnp.arange(NBLK, dtype=jnp.int32)
    mid = (block >= MID0) & (block < MID1)
    below, owned = owners < me, owners == me
    total = lambda mask: jnp.sum(mask.astype(jnp.int32))
    start = (total(below & ~mid), total(below & mid))
    count = (total(owned & ~mid), total(owned & mid))
    return start, count, total(owned & (block < MID0))


def pair_lanes(capacity, devices):
    return 2 + max(capacity - 2, 0) // devices


def make_plan(owners, capacity, devices, me):
    block = jnp.arange(NBLK, dtype=jnp.int32)
    mid = (block >= MID0) & (block < MID1)
    same = mid[:, None] == mid[None, :]
    before = (owners[None, :] < owners[:, None]) | (
        (owners[None, :] == owners[:, None]) & (block[None, :] < block[:, None])
    )
    order_in_class = jnp.sum((same & before).astype(jnp.int32), axis=1)
    home, slot = order_in_class % devices, order_in_class // devices
    device = jnp.arange(devices, dtype=jnp.int32)
    start, count, _ = class_counts(owners, devices)
    my_start, my_count, my_early = my_counts(owners, me)
    pair = pair_lanes(capacity, devices)

    slots = (-(-N0 // devices), -(-N1 // devices))

    def received(kind):
        wanted = me + devices * jnp.arange(slots[kind], dtype=jnp.int32)
        ends = start[kind] + count[kind]
        owner = jnp.sum((ends[None, :] <= wanted[:, None]).astype(jnp.int32), axis=1)
        owner = jnp.minimum(owner, devices - 1)
        base = jnp.sum(jnp.where(device[None, :] == owner[:, None], start[kind][None, :], 0), axis=1)
        turn = jnp.clip((wanted - base) // devices, 0, pair - 1)
        return owner * pair + (turn if kind == 0 else pair - 1 - turn)

    back_pair = (UNITS * capacity + 2 * (devices - 1)) // devices
    unit = UNITS * order_in_class[:, None] + jnp.arange(UNITS, dtype=jnp.int32)[None, :]
    unit_home, unit_slot = unit % devices, unit // devices
    unit_slots = (-(-UNITS * N0 // devices), -(-UNITS * N1 // devices))
    lane = jnp.arange(back_pair, dtype=jnp.int32)

    def units_back(kind):
        turn = lane if kind == 0 else back_pair - 1 - lane
        first = UNITS * start[kind][:, None]
        k = (me - first) % devices + turn[None, :] * devices
        return k < UNITS * count[kind][:, None], (first + k) // devices

    valid0, slot0 = units_back(0)
    valid1, slot1 = units_back(1)
    back = jnp.where(valid0, slot0, jnp.where(valid1, unit_slots[0] + slot1, 0)).reshape(-1)

    row = jnp.arange(capacity, dtype=jnp.int32)
    is_mid = (row >= my_early) & (row < my_early + my_count[1])
    k = jnp.where(is_mid, row - my_early, jnp.where(row < my_early, row, row - my_count[1]))
    first = UNITS * jnp.where(is_mid, my_start[1], my_start[0])
    k = UNITS * k[:, None] + jnp.arange(UNITS, dtype=jnp.int32)[None, :]
    turn = k // devices
    row_from = ((first[:, None] + k) % devices) * back_pair + jnp.where(
        is_mid[:, None], back_pair - 1 - turn, turn
    )
    row_used = row < my_count[0] + my_count[1]
    mine = (owners == me)[None, :]
    rank = jnp.sum((mine & (block[None, :] < block[:, None])).astype(jnp.int32), axis=1)
    row_block = jnp.sum(
        jnp.where(mine & (rank[None, :] == row[:, None]), block[None, :], 0), axis=1
    )
    late = devices * back_pair + UNITS * (row_block - MID1)
    late = late[:, None] + jnp.arange(UNITS, dtype=jnp.int32)[None, :]
    row_from = jnp.where((row_block >= MID1)[:, None], late, row_from)
    row_from = jnp.where(row_used[:, None], row_from, 0).reshape(-1)
    return dict(
        home=home, slot=slot, slots=slots,
        received=(received(0), received(1)), unit_home=unit_home, unit_slot=unit_slot,
        unit_slots=unit_slots, back=back, row_from=row_from,
        row_used=row_used, row_block=row_block,
    )


def stream_places(home, slot, me, streams, devices):
    relative = home ^ me
    place = jnp.zeros_like(slot)
    for begin, size, order in streams:
        inside = (slot >= begin) & (slot < begin + size)
        at = devices * begin + place_of(relative, order) * size + slot - begin
        place = jnp.where(inside, at, place)
    return place


def cost(microseconds):
    return pl.CostEstimate(
        flops=int(microseconds * 1e9), bytes_accessed=int(microseconds * 3e6), transcendentals=0
    )


ANY = pl.BlockSpec(memory_space=pl.ANY)
VMEM = pl.BlockSpec(memory_space=pltpu.VMEM)
SMEM = pl.BlockSpec(memory_space=pltpu.SMEM)


def params(**extra):
    return pltpu.CompilerParams(vmem_limit_bytes=VMEM_LIMIT, **extra)


def shape(dims, dtype):
    return jax.ShapeDtypeStruct(dims, dtype)


def send_kernel(my_index, owners, master, out, flat, *, devices):
    capacity = master.shape[0]
    me = my_index[0]
    for j in range(BROWS):
        flat[pl.ds(j, capacity, stride=BROWS), :] = master[:, j * LANES : (j + 1) * LANES]
    held = owners[...]
    block = lax.broadcasted_iota(jnp.int32, held.shape, 0) * LANES + lax.broadcasted_iota(
        jnp.int32, held.shape, 1
    )
    mid = (block >= MID0) & (block < MID1)
    below, owned = held < me, held == me

    def total(mask):
        return jnp.sum(jnp.where(mask, 1.0, 0.0)).astype(jnp.int32)

    start0, start1 = total(below & ~mid), total(below & mid)
    count0, count1 = total(owned & ~mid), total(owned & mid)
    early = total(owned & (block < MID0))
    pair = out.shape[0] // devices
    positive = devices * NBLK

    def step(home, carry):
        for s in range(pair):
            k0 = lax.rem(home - start0 + positive, devices) + s * devices
            k1 = lax.rem(home - start1 + positive, devices) + (pair - 1 - s) * devices
            row0 = jnp.where(k0 < early, k0, k0 + count1)
            row = jnp.where(k0 < count0, row0, jnp.where(k1 < count1, early + k1, 0))
            rows = pl.ds(pl.multiple_of(row * BROWS, BROWS), BROWS)
            out[home * pair + s] = flat[rows, :].astype(out.dtype)
        return carry

    lax.fori_loop(0, devices, step, 0)


def send_blocks(owners, master, devices, me):
    rows = -(-NBLK // (8 * LANES)) * 8
    held = jnp.pad(owners, (0, rows * LANES - NBLK), constant_values=1 << 20).reshape(rows, LANES)
    count = devices * pair_lanes(master.shape[0], devices)
    return pl.pallas_call(
        partial(send_kernel, devices=devices),
        out_shape=shape((count, BROWS, LANES), jnp.bfloat16),
        in_specs=[SMEM, VMEM, VMEM],
        out_specs=VMEM,
        scratch_shapes=[pltpu.VMEM((master.shape[0] * BROWS, LANES), jnp.float32)],
        compiler_params=params(),
    )(me.reshape(1), held, master)


def pick_kernel(table, source, *outs):
    at = 0
    for out in outs:

        def step(i, carry, out=out, at=at):
            out[i] = source[table[at + i]]
            return carry

        lax.fori_loop(0, out.shape[0], step, 0)
        at += out.shape[0]


def pick_blocks(table, source, sizes):
    return pl.pallas_call(
        pick_kernel,
        out_shape=tuple(shape((n,) + source.shape[1:], source.dtype) for n in sizes),
        in_specs=[SMEM, VMEM],
        out_specs=(VMEM,) * len(sizes),
        compiler_params=params(),
    )(table, source)


def back_kernel(table, *refs):
    sources, (out, held) = refs[:-2], refs[-2:]
    at = 0
    for i in range(0, len(sources), 2):
        n = sources[i].shape[0]
        held[at : at + n] = sources[i][...] + sources[i + 1][...]
        at += n

    def step(i, carry):
        for u in range(8):
            out[i * 8 + u] = held[table[i * 8 + u]]
        return carry

    total = out.shape[0]
    lax.fori_loop(0, total // 8, step, 0)


def units_to_owners(table, sources):
    return pl.pallas_call(
        back_kernel,
        out_shape=shape((table.shape[0], UNIT, LANES), jnp.float32),
        in_specs=[SMEM] + [VMEM] * len(sources),
        out_specs=VMEM,
        scratch_shapes=[
            pltpu.VMEM((sum(s.shape[0] for s in sources[::2]), UNIT, LANES), jnp.float32)
        ],
        compiler_params=params(),
    )(table, *sources)


def row_start(rho):
    return (PROJ * rho) // LANES, (PROJ * rho) % LANES


def copy_all(pairs, sem):
    copies = [pltpu.make_async_copy(a, b, sem.at[i]) for i, (a, b) in enumerate(pairs)]
    for c in copies:
        c.start()
    for c in copies:
        c.wait()


def spread_blocks(table, held, flat, count, first_row):
    def one(i):
        at = pl.multiple_of(first_row + i * BROWS, 16)
        flat[pl.ds(at, BROWS), :] = held[table[i]].astype(jnp.float32)

    def step(i, carry):
        for u in range(4):
            one(i * 4 + u)
        return carry

    lax.fori_loop(0, count // 4, step, 0)
    for i in range(count // 4 * 4, count):
        one(i)


def unpack_vectors(flat, conv_weight, conv_bias, heads, skip, norm_gain, gate_gain):
    bf16, f32 = jnp.bfloat16, jnp.float32
    tiles = CONVCH // LANES
    row = lax.broadcasted_iota(jnp.int32, (LANES, LANES), 0)
    col = lax.broadcasted_iota(jnp.int32, (LANES, LANES), 1)
    per_tile = LANES // KCONV
    for k in range(KCONV):
        total = jnp.zeros((tiles, LANES), f32)
        for q in range(KCONV):
            rows = flat[pl.ds(VEC_AT + q, tiles, stride=KCONV), :].astype(bf16)
            chosen = (row == KCONV * (col % per_tile) + k) & (col // per_tile == q)
            total = total + jnp.dot(rows, chosen.astype(bf16), preferred_element_type=f32)
        for i in range(tiles):
            conv_weight[k : k + 1, i * LANES : (i + 1) * LANES] = total[i : i + 1, :]
    bias_at = VEC_AT + tiles * KCONV
    for i in range(tiles):
        conv_bias[:, i * LANES : (i + 1) * LANES] = flat[bias_at + i : bias_at + i + 1, :]
    at = bias_at + tiles
    lane = lax.broadcasted_iota(jnp.int32, (8, LANES), 1)
    first = flat[at : at + 8, :]
    three = []
    for i in range(3):
        moved = pltpu.roll(first, LANES - i * HEADS, 1) if i else first
        three.append(jnp.where(lane < HEADS, moved, 0.0))
        heads[i : i + 1, :] = three[i][0:1, :]
    for j in range(INNER // LANES):
        h = lax.broadcasted_iota(jnp.int32, (LANES, LANES), 0)
        c = lax.broadcasted_iota(jnp.int32, (LANES, LANES), 1) + j * LANES
        spread = (h == c // HEADDIM).astype(bf16)
        wide = jnp.dot(three[2].astype(bf16), spread, preferred_element_type=f32)
        skip[:, j * LANES : (j + 1) * LANES] = wide[0:1, :]
    shift = 3 * HEADS
    for out, begin, width in ((norm_gain, at, D), (gate_gain, at + D // LANES, INNER)):
        for j in range(width // LANES):
            x = pltpu.roll(flat[begin + j : begin + j + 1, :], LANES - shift, 1)
            y = pltpu.roll(flat[begin + j + 1 : begin + j + 2, :], LANES - shift, 1)
            out[:, j * LANES : (j + 1) * LANES] = jnp.where(lane[0:1] < LANES - shift, x, y)


def unpack_in_kernel(table, *refs):
    parts, (w_in, head, tail, *vectors), (held, flat, tile, sem) = refs[:-13], refs[-13:-4], refs[-4:]
    pairs, at = [], 0
    for part in parts:
        pairs.append((part, held.at[pl.ds(at, part.shape[0])]))
        at += part.shape[0]
    copy_all(pairs, sem)
    spread_blocks(table, held, flat, N0, 0)
    head[...] = flat[IN_ROWS : IN_ROWS + HEAD_ROWS, :]
    tail[...] = flat[MID0 * BROWS : MID0 * BROWS + TAIL_ROWS, :]
    unpack_vectors(flat, *vectors)
    lane = lax.broadcasted_iota(jnp.int32, (GROUPS, LANES), 1)

    def columns(j):
        for rho in range(GROUP):
            c, s = row_start(rho)
            x = flat[pl.ds(c + j, GROUPS, stride=GROUP_ROWS), :]
            if s:
                y = flat[pl.ds(c + j + 1, GROUPS, stride=GROUP_ROWS), :]
                x = jnp.where(
                    lane < LANES - s,
                    pltpu.roll(x, LANES - s, 1),
                    pltpu.roll(y, LANES - s, 1),
                )
            tile[pl.ds(rho, GROUPS, stride=GROUP), :] = x

    def step(j, carry):
        columns(j)
        w_in[:, pl.ds(pl.multiple_of(j * LANES, LANES), LANES)] = tile[...].astype(jnp.bfloat16)
        return carry

    lax.fori_loop(0, COL_TILES - 1, step, 0)
    columns(COL_TILES - 1)
    last = (COL_TILES - 1) * LANES
    inside = lax.broadcasted_iota(jnp.int32, (D, LANES), 1) < PROJ - last
    w_in[:, last:] = jnp.where(inside, tile[...], 0.0).astype(jnp.bfloat16)


def unpack_in(table, parts):
    held = sum(part.shape[0] for part in parts)
    return pl.pallas_call(
        unpack_in_kernel,
        out_shape=(
            shape((D, WIDE), jnp.bfloat16),
            shape((HEAD_ROWS, LANES), jnp.float32),
            shape((TAIL_ROWS, LANES), jnp.float32),
            shape((KCONV, CONVCH), jnp.float32),
            shape((1, CONVCH), jnp.float32),
            shape((8, LANES), jnp.float32),
            shape((1, INNER), jnp.float32),
            shape((1, D), jnp.float32),
            shape((1, INNER), jnp.float32),
        ),
        in_specs=[SMEM] + [ANY] * len(parts),
        out_specs=(VMEM,) * 9,
        scratch_shapes=[
            pltpu.VMEM((held, BROWS, LANES), jnp.bfloat16),
            pltpu.VMEM((F0_ROWS, LANES), jnp.float32),
            pltpu.VMEM((D, LANES), jnp.float32),
            pltpu.SemaphoreType.DMA((len(parts),)),
        ],
        compiler_params=params(),
        cost_estimate=cost(16),
    )(table, *parts)


def unpack_out_kernel(table, own, got, head, tail, w_out, flat, held, sem):
    half = own.shape[0]
    copy_all([(own, held.at[pl.ds(0, half)]), (got, held.at[pl.ds(half, half)])], sem)
    flat[0:HEAD_ROWS, :] = head[...]
    flat[OUT_ROWS - TAIL_ROWS : OUT_ROWS, :] = tail[...]
    spread_blocks(table, held, flat, N1, HEAD_ROWS)
    rows = 128

    def step(i, carry):
        at = pl.multiple_of(i * rows, rows)
        for j in range(OUT_TILES):
            x = flat[pl.ds(at * OUT_TILES + j, rows, stride=OUT_TILES), :]
            w_out[pl.ds(at, rows), j * LANES : (j + 1) * LANES] = x.astype(jnp.bfloat16)
        return carry

    lax.fori_loop(0, INNER // rows, step, 0)


def unpack_out(table, own, got, head, tail):
    return pl.pallas_call(
        unpack_out_kernel,
        out_shape=shape((INNER, D), jnp.bfloat16),
        in_specs=[SMEM, ANY, ANY, VMEM, VMEM],
        out_specs=VMEM,
        scratch_shapes=[
            pltpu.VMEM((OUT_ROWS, LANES), jnp.float32),
            pltpu.VMEM((2 * own.shape[0], BROWS, LANES), jnp.bfloat16),
            pltpu.SemaphoreType.DMA((2,)),
        ],
        compiler_params=params(),
    )(table, own, got, head, tail)


def permute_units(table, flat, count, first_row, staged):
    many = 16

    def step(i, carry):
        for u in range(many):
            at = pl.multiple_of(first_row + (i * many + u) * UNIT, UNIT)
            staged[table[i * many + u]] = flat[pl.ds(at, UNIT), :]
        return carry

    lax.fori_loop(0, count // many, step, 0)
    for i in range(count // many * many, count):
        staged[table[i]] = flat[first_row + i * UNIT : first_row + (i + 1) * UNIT, :]


def pack_in_kernel(table, hidden, grad, head, *refs):
    outs, (turned, tiles, flat, staged, sem) = refs[:-5], refs[-5:]
    turned[...] = hidden[...].T
    lane = lax.broadcasted_iota(jnp.int32, (GROUPS, LANES), 1)

    def product(p, count):
        at = p * 2 * LANES
        at = at if isinstance(at, int) else pl.multiple_of(at, 2 * LANES)
        return jnp.dot(
            turned[...], grad[:, pl.ds(at, count * LANES)], preferred_element_type=jnp.float32
        )

    def put(p, value):
        for k in range(value.shape[1] // LANES):
            at = (p * 2 + k) * D
            at = at if isinstance(at, int) else pl.multiple_of(at, D)
            tiles[pl.ds(at, D), :] = value[:, k * LANES : (k + 1) * LANES]

    def load(rho, j):
        return tiles[pl.ds(j * D + rho, GROUPS, stride=GROUP), :]

    def whole(rho, i):
        first = -(-PROJ * rho // LANES)
        col0 = first * LANES - PROJ * rho
        x = load(rho, i)
        if col0:
            x = jnp.where(
                lane < LANES - col0,
                pltpu.roll(x, LANES - col0, 1),
                pltpu.roll(load(rho, i + 1), LANES - col0, 1),
            )
        flat[pl.ds(first + i, GROUPS, stride=GROUP_ROWS), :] = x

    put(0, product(0, 2))
    put(1, product(1, 2))
    pairs = COL_TILES // 2

    def step(p, carry):
        for i in range(2):
            for rho in range(GROUP):
                whole(rho, p * 2 + i)
        put(p + 2, product(p + 2, 2))
        return carry

    lax.fori_loop(0, pairs - 2, step, 0)
    put(pairs, product(pairs, COL_TILES % 2))
    for rho in range(GROUP):
        first = -(-PROJ * rho // LANES)
        col0 = first * LANES - PROJ * rho
        full = (PROJ - col0) // LANES
        for i in range((pairs - 2) * 2, full):
            whole(rho, i)
        left = PROJ - col0 - full * LANES
        if left:
            begin = col0 + full * LANES
            j, s = begin // LANES, begin % LANES
            x = pltpu.roll(load(rho, j), LANES - s, 1) if s else load(rho, j)
            if s + left > LANES:
                x = jnp.where(lane < LANES - s, x, pltpu.roll(load(rho, j + 1), LANES - s, 1))
            y = pltpu.roll(load(rho + 1, 0), left, 1)
            flat[pl.ds(first + full, GROUPS, stride=GROUP_ROWS), :] = jnp.where(lane < left, x, y)
    flat[IN_ROWS : IN_ROWS + HEAD_ROWS, :] = head[...]
    permute_units(table, flat, MID0 * UNITS, 0, staged)
    copies, at = [], 0
    for out in outs:
        copies.append((staged.at[pl.ds(at, out.shape[0])], out))
        at += out.shape[0]
    copy_all(copies, sem)


def pack_in(table, hidden, grad, head, sizes):
    return pl.pallas_call(
        pack_in_kernel,
        out_shape=tuple(shape((n, UNIT, LANES), jnp.float32) for n in sizes),
        in_specs=[SMEM, VMEM, VMEM, VMEM],
        out_specs=(ANY,) * len(sizes),
        scratch_shapes=[
            pltpu.VMEM((D, hidden.shape[0]), jnp.bfloat16),
            pltpu.VMEM((COL_TILES * D, LANES), jnp.float32),
            pltpu.VMEM((MID0 * BROWS, LANES), jnp.float32),
            pltpu.VMEM((sum(sizes), UNIT, LANES), jnp.float32),
            pltpu.SemaphoreType.DMA((len(sizes),)),
        ],
        compiler_params=params(),
        cost_estimate=cost(20),
    )(table, hidden, grad, head)


def pack_out_kernel(table, grad, local, keep, send, head, tail, flat, out, sem, *, slots):
    rows = 128

    def step(i, carry):
        at = pl.multiple_of(i * rows, rows)
        for j in range(OUT_TILES):
            flat[pl.ds(at * OUT_TILES + j, rows, stride=OUT_TILES), :] = grad[
                pl.ds(at, rows), j * LANES : (j + 1) * LANES
            ]
        return carry

    lax.fori_loop(0, INNER // rows, step, 0)
    head[...] = flat[0:HEAD_ROWS, :]
    tail[...] = flat[OUT_ROWS - TAIL_ROWS : OUT_ROWS, :]
    permute_units(table, flat, N1 * UNITS, HEAD_ROWS, out)

    def add_local(i, carry):
        out[i * slots + slots - 1] = local[...]
        return carry

    lax.fori_loop(0, out.shape[0] // slots, add_local, 0)
    half = keep.shape[0]
    copy_all([(out.at[pl.ds(0, half)], keep), (out.at[pl.ds(half, half)], send)], sem)


def pack_out(table, grad, local, devices, slots):
    return pl.pallas_call(
        partial(pack_out_kernel, slots=slots),
        out_shape=(
            shape((devices * slots // 2, UNIT, LANES), jnp.float32),
            shape((devices * slots // 2, UNIT, LANES), jnp.float32),
            shape((HEAD_ROWS, LANES), jnp.float32),
            shape((TAIL_ROWS, LANES), jnp.float32),
        ),
        in_specs=[SMEM, VMEM, VMEM],
        out_specs=(ANY, ANY, VMEM, VMEM),
        scratch_shapes=[
            pltpu.VMEM((OUT_ROWS, LANES), jnp.float32),
            pltpu.VMEM((devices * slots, UNIT, LANES), jnp.float32),
            pltpu.SemaphoreType.DMA((2,)),
        ],
        compiler_params=params(),
    )(table, grad, local)


def adam_kernel(table, scale, got, late, limit, used, master, first, second, o_first, o_second, o_master, flat, held):
    capacity = master.shape[0]

    def step(i, carry):
        for u in range(UNITS):
            at = table[i * UNITS + u]
            rows = pl.ds(pl.multiple_of(i * BROWS + u * UNIT, UNIT), UNIT)
            flat[rows, :] = held[at]
        return carry

    held[0 : got.shape[0]] = got[...]
    held[got.shape[0] :] = late[...]
    lax.fori_loop(0, capacity, step, 0)
    lane = lax.broadcasted_iota(jnp.int32, (capacity, LANES), 1)
    divisor = scale[0]
    for j in range(BROWS):
        cols = slice(j * LANES, (j + 1) * LANES)
        grad = jnp.where(used[...] > 0, flat[pl.ds(j, capacity, stride=BROWS), :], 0.0) / divisor
        matrix = lane + j * LANES < limit[...]
        weights = master[:, cols]
        new_first = BETA_ONE * first[:, cols] + (1.0 - BETA_ONE) * grad
        new_second = BETA_TWO * second[:, cols] + (1.0 - BETA_TWO) * grad * grad
        normal = (
            new_first
            / (1.0 - BETA_ONE**STEP)
            / (jnp.sqrt(new_second / (1.0 - BETA_TWO**STEP)) + ADAM_EPS)
        )
        rate = jnp.where(matrix, MATRIX_RATE, VECTOR_RATE)
        decay = jnp.where(matrix, WEIGHT_DECAY, 0.0)
        o_first[:, cols] = new_first
        o_second[:, cols] = new_second
        o_master[:, cols] = weights - rate * (normal + decay * weights)


def adam(table, divisor, got, late, limit, used, master, first, second):
    capacity = master.shape[0]
    return pl.pallas_call(
        adam_kernel,
        out_shape=(shape(master.shape, jnp.float32),) * 3,
        in_specs=[SMEM, SMEM] + [VMEM] * 7,
        out_specs=(VMEM,) * 3,
        scratch_shapes=[
            pltpu.VMEM((capacity * BROWS, LANES), jnp.float32),
            pltpu.VMEM((got.shape[0] + late.shape[0], UNIT, LANES), jnp.float32),
        ],
        compiler_params=params(),
    )(table, divisor.reshape(1), got, late, limit, used, master, first, second)


def doubled(values, step):
    return jnp.concatenate([values, exchange(values, step)], axis=0)


def gather_steps(values, order):
    for step in order[:0:-1]:
        values = doubled(values, step)
    return values, exchange(values, order[0])


def reduce_step(values, step, extra=None):
    half = values.shape[0] // 2
    if extra is None:
        return values[:half] + exchange(values[half:], step)
    got = exchange(jnp.concatenate([values[half:], extra]), step)
    return values[:half] + got[:half], extra + got[half:]


CHUNK = 128
PAIRS = HEADS // 2
MIXW = INNER + 2 * NSTATE
DT_AT = INNER + CONVCH
F32 = jnp.float32
BF16 = jnp.bfloat16
NN = (((1,), (0,)), ((), ()))
NT = (((1,), (1,)), ((), ()))


def dot(a, b, dims=NN):
    return lax.dot_general(a, b, dims, preferred_element_type=F32)


def split(v):
    high = v.astype(BF16)
    return high, (v - high.astype(F32)).astype(BF16)


def dot3(a, b, dims=NN):
    ah, al = a
    bh, bl = b
    return dot(ah, bh, dims) + (dot(ah, bl, dims) + dot(al, bh, dims))


def heads_gather():
    return jnp.asarray(np.repeat(np.eye(HEADS, LANES, dtype=np.float32), HEADDIM, axis=0), BF16)


def three_parts(v):
    high = v.astype(BF16).astype(F32)
    rest = v - high
    middle = rest.astype(BF16).astype(F32)
    low = rest - middle
    return (high + pltpu.roll(middle, 32, 1) + pltpu.roll(low, 64, 1)).astype(BF16)


def triangle_sum(tri, v):
    parts = dot(tri, three_parts(v))
    lane = lax.broadcasted_iota(jnp.int32, parts.shape, 1)
    total = parts + pltpu.roll(parts, LANES - 32, 1) + pltpu.roll(parts, LANES - 64, 1)
    return jnp.where(lane < HEADS, total, 0.0)


def chunk_decays(dt, dt_bias, a_log):
    lane = lax.broadcasted_iota(jnp.int32, (CHUNK, LANES), 1)
    row = lax.broadcasted_iota(jnp.int32, (CHUNK, LANES), 0)
    shifted = dt + dt_bias
    delta = jnp.where(
        lane < HEADS, jnp.maximum(shifted, 0.0) + jnp.log1p(jnp.exp(-jnp.abs(shifted))), 0.0
    )
    rate = -jnp.exp(a_log)
    lower = (row >= lane).astype(BF16)
    cum = triangle_sum(lower, delta * rate)
    last = cum[CHUNK - 1 : CHUNK, :]
    return shifted, delta, rate, cum, last


def pair_mask():
    lane = lax.broadcasted_iota(jnp.int32, (CHUNK, LANES), 1)
    low = (lane < HEADDIM).astype(F32)
    return low.astype(BF16), (1.0 - low).astype(BF16)


QUADS = HEADS // 4
QWIDTH = 4 * HEADDIM


def sigmoid(v):
    return 0.5 * jnp.tanh(0.5 * v) + 0.5


def silu(v):
    return v * sigmoid(v)


def side_by_side(v):
    high, low = split(v)
    return jnp.concatenate([high, low], axis=1), high


def dot_parts(a, b):
    ahl, ah = a
    bh, bl = b
    return dot(ahl, jnp.concatenate([bh, bh], axis=0)) + dot(ah, bl)


def dot_turned(a, b):
    ah, al = a
    bh, bl = b
    both = dot(ah, jnp.concatenate([bh, bl], axis=0), NT)
    n = bh.shape[0]
    return both[:, :n] + both[:, n:] + dot(al, bh, NT)


def widen(delta, cum, quad):
    lane = lax.broadcasted_iota(jnp.int32, (CHUNK, LANES), 1)
    over = lambda v, h: jnp.broadcast_to(v[:, h : h + 1], (CHUNK, LANES))
    first = 4 * quad
    columns = [over(cum, first + k) for k in range(4)]
    rates = [over(delta, first + k) for k in range(4)]
    pair = lambda vs: jnp.concatenate(
        [jnp.where(lane < HEADDIM, vs[0], vs[1]), jnp.where(lane < HEADDIM, vs[2], vs[3])], axis=1
    )
    return pair(rates), pair(columns), columns


def pair_rows(parts, j, low, high):
    cols = slice(j * LANES, (j + 1) * LANES)
    return [jnp.concatenate([p[:, cols] * low, p[:, cols] * high], axis=0) for p in parts]


def scan_forward_kernel(
    mixed, dt, gate, dt_bias, a_log, skip, gain, ssm, mixed_out, states, state
):
    @pl.when(pl.program_id(0) == 0)
    def _():
        state[...] = jnp.zeros_like(state)

    states[0] = state[...]
    _, delta, _, cum, last = chunk_decays(dt[...], dt_bias[...], a_log[...])
    lane = lax.broadcasted_iota(jnp.int32, (CHUNK, LANES), 1)
    row = lax.broadcasted_iota(jnp.int32, (CHUNK, LANES), 0)
    bias = jnp.where(row >= lane, 0.0, -1e30)
    cum_t = cum.T
    inputs_b = mixed[:, INNER : INNER + NSTATE]
    readout = mixed[:, INNER + NSTATE :]
    affinity = dot3(split(readout), split(inputs_b), NT)
    readout_parts = side_by_side(readout)
    b_parts = side_by_side(inputs_b.T)
    low, high = pair_mask()
    squares = jnp.zeros((CHUNK, LANES), F32)
    for quad in range(QUADS):
        cols = slice(quad * QWIDTH, (quad + 1) * QWIDTH)
        wide_delta, wide_cum, columns = widen(delta, cum, quad)
        values = mixed[:, cols]
        scaled = values * wide_delta
        parts = split(scaled)
        outs = []
        for j in range(2):
            right_h, right_l = pair_rows(parts, j, low, high)
            left = []
            for k in range(2):
                h = 4 * quad + 2 * j + k
                within = jnp.exp(columns[2 * j + k] - cum_t[h : h + 1, :] + bias)
                left.append(split(affinity * within))
            left_h = jnp.concatenate([left[0][0], left[1][0]], axis=1)
            left_l = jnp.concatenate([left[0][1], left[1][1]], axis=1)
            both = dot(left_h, jnp.concatenate([right_h, right_l], axis=1))
            outs.append(both[:, :LANES] + both[:, LANES:] + dot(left_l, right_h))
        carried = state[:, cols]
        grown = jnp.exp(wide_cum)
        out = jnp.concatenate(outs, axis=1) + dot_parts(readout_parts, split(carried)) * grown
        out = out + skip[:, cols] * values
        tail = jnp.exp(wide_cum[CHUNK - 1 :] - wide_cum)
        state[:, cols] = carried * grown[CHUNK - 1 :] + dot_parts(b_parts, split(scaled * tail))
        ssm[:, cols] = out
        gated = out * silu(gate[:, cols])
        squares = squares + gated[:, :LANES] * gated[:, :LANES] + gated[:, LANES:] * gated[:, LANES:]
    rho = lax.rsqrt(jnp.sum(squares, axis=1, keepdims=True) * (1.0 / INNER) + NORM_EPS)
    for j in range(PAIRS):
        cols = slice(j * LANES, (j + 1) * LANES)
        gated = ssm[:, cols] * silu(gate[:, cols])
        mixed_out[:, cols] = (gated * rho * gain[:, cols]).astype(BF16)


def scan_forward(mixed, projected, dt_bias, a_log, skip, gain):
    length = mixed.shape[0]
    chunks = length // CHUNK
    whole = lambda v: pl.BlockSpec(v.shape, lambda i: (0,) * v.ndim)
    return pl.pallas_call(
        scan_forward_kernel,
        grid=(chunks,),
        out_shape=(
            shape((length, INNER), F32),
            shape((length, INNER), BF16),
            shape((chunks, NSTATE, INNER), F32),
        ),
        in_specs=[
            pl.BlockSpec((CHUNK, MIXW), lambda i: (i, 0)),
            pl.BlockSpec((CHUNK, LANES), lambda i: (i, DT_AT // LANES)),
            pl.BlockSpec((CHUNK, INNER), lambda i: (i, 0)),
        ]
        + [whole(v) for v in (dt_bias, a_log, skip, gain)],
        out_specs=(
            pl.BlockSpec((CHUNK, INNER), lambda i: (i, 0)),
            pl.BlockSpec((CHUNK, INNER), lambda i: (i, 0)),
            pl.BlockSpec((1, NSTATE, INNER), lambda i: (i, 0, 0)),
        ),
        scratch_shapes=[pltpu.VMEM((NSTATE, INNER), F32)],
        compiler_params=params(),
        cost_estimate=cost(40),
    )(mixed, projected, projected, dt_bias, a_log, skip, gain)


def scan_backward_kernel(
    mixed, dt, ssm, grad, states, dt_bias, a_log, skip, gather, held,
    grad_mixed, grad_dt, sums, skip_sums, grad_state, left, right,
):
    @pl.when(pl.program_id(0) == 0)
    def _():
        grad_state[...] = jnp.zeros_like(grad_state)
        sums[...] = jnp.zeros_like(sums)
        skip_sums[...] = jnp.zeros_like(skip_sums)

    shifted, delta, rate, cum, last = chunk_decays(dt[...], dt_bias[...], a_log[...])
    lane = lax.broadcasted_iota(jnp.int32, (CHUNK, LANES), 1)
    row = lax.broadcasted_iota(jnp.int32, (CHUNK, LANES), 0)
    bias = jnp.where(lane >= row, 0.0, -1e30)
    heads = lane < HEADS
    cum_t = cum.T
    inputs_b = mixed[:, INNER : INNER + NSTATE]
    readout = mixed[:, INNER + NSTATE :]
    b_parts, c_parts = split(inputs_b), split(readout)
    b_wide = side_by_side(inputs_b)
    c_turned = side_by_side(readout.T)
    affinity = dot3(b_parts, c_parts, NT)
    low, high = pair_mask()
    grad_affinity = jnp.zeros((CHUNK, CHUNK), F32)
    grad_b = jnp.zeros((CHUNK, NSTATE), F32)
    grad_c = jnp.zeros((CHUNK, NSTATE), F32)
    last_row = lax.broadcasted_iota(jnp.int32, (CHUNK, QWIDTH), 0) == CHUNK - 1
    for quad in range(QUADS):
        cols = slice(quad * QWIDTH, (quad + 1) * QWIDTH)
        wide_delta, wide_cum, columns = widen(delta, cum, quad)
        grown = jnp.exp(wide_cum)
        tail = jnp.exp(wide_cum[CHUNK - 1 :] - wide_cum)
        end = grown[CHUNK - 1 :]
        values = mixed[:, cols]
        pulled = grad[:, cols]
        scaled = values * wide_delta
        x_parts, p_parts = split(scaled), split(pulled)
        outs = []
        for j in range(2):
            half = slice(j * LANES, (j + 1) * LANES)
            xh, xl = x_parts[0][:, half], x_parts[1][:, half]
            right_h, right_l = pair_rows(p_parts, j, low, high)
            pull = dot(
                jnp.concatenate([xh, xl], axis=1),
                jnp.concatenate([right_h, right_h], axis=1),
                NT,
            ) + dot(xh, right_l, NT)
            kernels = []
            for k in range(2):
                h = 4 * quad + 2 * j + k
                within = jnp.exp(cum_t[h : h + 1, :] - columns[2 * j + k] + bias)
                kernels.append(split(affinity * within))
                grad_affinity = grad_affinity + within * pull[:, k * CHUNK : (k + 1) * CHUNK]
            kernel_h = jnp.concatenate([kernels[0][0], kernels[1][0]], axis=1)
            kernel_l = jnp.concatenate([kernels[0][1], kernels[1][1]], axis=1)
            both = dot(kernel_h, jnp.concatenate([right_h, right_l], axis=1))
            outs.append(both[:, :LANES] + both[:, LANES:] + dot(kernel_l, right_h))
        late = grad_state[:, cols]
        late_parts = split(late)
        early = states[0, :, cols]
        from_state = dot_parts(b_wide, late_parts) * tail
        grad_scaled = jnp.concatenate(outs, axis=1) + from_state
        pulled_cum = split(pulled * grown)
        grad_c = grad_c + dot_turned(pulled_cum, split(early))
        grad_b = grad_b + dot_turned(split(scaled * tail), late_parts)
        grad_state[:, cols] = late * end + dot_parts(c_turned, pulled_cum)
        grad_mixed[:, cols] = grad_scaled * wide_delta + skip[:, cols] * pulled
        skip_sums[:, cols] += jnp.sum(pulled * values, axis=0, keepdims=True)
        left[:, cols] = grad_scaled * values
        inner = pulled * (ssm[:, cols] - skip[:, cols] * values) - scaled * grad_scaled
        extra = jnp.sum(scaled * from_state, axis=0, keepdims=True) + end * jnp.sum(
            late * early, axis=0, keepdims=True
        )
        right[:, cols] = inner + jnp.where(last_row, extra, 0.0)
    ga_parts = split(grad_affinity)
    grad_mixed[:, INNER : INNER + NSTATE] = grad_b + dot3(ga_parts, c_parts)
    grad_mixed[:, INNER + NSTATE :] = grad_c + dot3(split(grad_affinity.T), b_parts)

    def by_head(v):
        high, low = split(v)
        g = gather[...]
        return dot(high, g) + dot(low, g)

    direct = by_head(left[...])
    grad_cum = by_head(right[...])
    upper = (lane >= row).astype(BF16)
    after = triangle_sum(upper, grad_cum)
    grad_delta = direct + rate * after
    grad_raw = jnp.where(heads, grad_delta * sigmoid(shifted), 0.0)
    grad_dt[...] = grad_raw.astype(BF16)
    sums[0:1, :] += jnp.sum(grad_raw, axis=0, keepdims=True)
    sums[1:2, :] += rate * jnp.sum(delta * after, axis=0, keepdims=True)


def scan_backward(mixed, projected, ssm, grad, states, dt_bias, a_log, skip, gather, held):
    length = mixed.shape[0]
    chunks = length // CHUNK
    whole = lambda v: pl.BlockSpec(v.shape, lambda i: (0,) * v.ndim)
    back = lambda i: (chunks - 1 - i, 0)
    return pl.pallas_call(
        scan_backward_kernel,
        grid=(chunks,),
        out_shape=(
            shape((length, MIXW), F32),
            shape(held.shape, BF16),
            shape((8, LANES), F32),
            shape((1, INNER), F32),
        ),
        in_specs=[
            pl.BlockSpec((CHUNK, MIXW), back),
            pl.BlockSpec((CHUNK, LANES), lambda i: (chunks - 1 - i, DT_AT // LANES)),
            pl.BlockSpec((CHUNK, INNER), back),
            pl.BlockSpec((CHUNK, INNER), back),
            pl.BlockSpec((1, NSTATE, INNER), lambda i: (chunks - 1 - i, 0, 0)),
        ]
        + [whole(v) for v in (dt_bias, a_log, skip, gather)]
        + [ANY],
        out_specs=(
            pl.BlockSpec((CHUNK, MIXW), back),
            pl.BlockSpec((CHUNK, LANES), lambda i: (chunks - 1 - i, DT_AT // LANES)),
            pl.BlockSpec((8, LANES), lambda i: (0, 0)),
            pl.BlockSpec((1, INNER), lambda i: (0, 0)),
        ),
        scratch_shapes=[pltpu.VMEM((NSTATE, INNER), F32)] + [pltpu.VMEM((CHUNK, INNER), F32)] * 2,
        compiler_params=params(),
        input_output_aliases={9: 1},
        cost_estimate=cost(35),
    )(mixed, projected, ssm, grad, states, dt_bias, a_log, skip, gather, held)


ROWS_AT_ONCE = 128
CONV_TILES = 2


def down(v, before, by):
    moved = pltpu.roll(v, by, 0)
    row = lax.broadcasted_iota(jnp.int32, (8, LANES), 0)
    top = jnp.where(row < by, pltpu.roll(before, by, 0), moved[:8])
    return jnp.concatenate([top, moved[8:]], axis=0)


def up(v, after, by):
    rows = v.shape[0]
    moved = pltpu.roll(v, rows - by, 0)
    row = lax.broadcasted_iota(jnp.int32, (8, LANES), 0)
    end = jnp.where(row < 8 - by, moved[rows - 8 :], pltpu.roll(after, 8 - by, 0))
    return jnp.concatenate([moved[: rows - 8], end], axis=0)


def conv_terms(conv_in, at, cols):
    rows = conv_in[at : at + ROWS_AT_ONCE, cols]
    before = conv_in[at - 8 : at, cols] if at else jnp.zeros((8, LANES), F32)
    return [down(rows, before, KCONV - 1 - k) for k in range(KCONV - 1)] + [rows]


def conv_sum(terms, weight, bias):
    total = bias + terms[KCONV - 1] * weight[KCONV - 1 : KCONV]
    for k in range(KCONV - 1):
        total = total + terms[k] * weight[k : k + 1]
    return total


def conv_forward_kernel(conv_in, weight, bias, mixed):
    for tile in range(CONV_TILES):
        cols = slice(tile * LANES, (tile + 1) * LANES)
        w, b = weight[:, cols], bias[:, cols]
        for at in range(0, conv_in.shape[0], ROWS_AT_ONCE):
            mixed[at : at + ROWS_AT_ONCE, cols] = silu(conv_sum(conv_terms(conv_in, at, cols), w, b))


def conv_forward(projected, weight, bias):
    length = projected.shape[0]
    width = CONV_TILES * LANES
    return pl.pallas_call(
        conv_forward_kernel,
        grid=(CONVCH // width,),
        out_shape=shape((length, CONVCH), F32),
        in_specs=[
            pl.BlockSpec((length, width), lambda i: (0, INNER // width + i)),
            pl.BlockSpec((KCONV, width), lambda i: (0, i)),
            pl.BlockSpec((1, width), lambda i: (0, i)),
        ],
        out_specs=pl.BlockSpec((length, width), lambda i: (0, i)),
        compiler_params=params(),
        cost_estimate=cost(10),
    )(projected, weight, bias)


def conv_backward_kernel(conv_in, grad, weight, bias, held, out, sums):
    length = conv_in.shape[0]
    for tile in range(CONV_TILES):
        cols = slice(tile * LANES, (tile + 1) * LANES)
        w, b = weight[:, cols], bias[:, cols]
        totals = [jnp.zeros((1, LANES), F32)] * (KCONV + 1)
        after = jnp.zeros((8, LANES), F32)
        for at in range(length - ROWS_AT_ONCE, -1, -ROWS_AT_ONCE):
            terms = conv_terms(conv_in, at, cols)
            value = conv_sum(terms, w, b)
            sig = sigmoid(value)
            g = grad[at : at + ROWS_AT_ONCE, cols] * (sig * (1.0 + value * (1.0 - sig)))
            for k in range(KCONV):
                totals[k] = totals[k] + jnp.sum(g * terms[k], axis=0, keepdims=True)
            totals[KCONV] = totals[KCONV] + jnp.sum(g, axis=0, keepdims=True)
            total = g * w[KCONV - 1 : KCONV]
            for k in range(KCONV - 1):
                total = total + up(g, after, KCONV - 1 - k) * w[k : k + 1]
            after = g[:8]
            out[at : at + ROWS_AT_ONCE, cols] = total.astype(BF16)
        for k in range(KCONV + 1):
            sums[k : k + 1, cols] = totals[k]


def conv_backward(projected, grad_mixed, weight, bias, held):
    length = projected.shape[0]
    width = CONV_TILES * LANES
    return pl.pallas_call(
        conv_backward_kernel,
        grid=(CONVCH // width,),
        out_shape=(shape(held.shape, BF16), shape((8, CONVCH), F32)),
        in_specs=[
            pl.BlockSpec((length, width), lambda i: (0, INNER // width + i)),
            pl.BlockSpec((length, width), lambda i: (0, i)),
            pl.BlockSpec((KCONV, width), lambda i: (0, i)),
            pl.BlockSpec((1, width), lambda i: (0, i)),
            ANY,
        ],
        out_specs=(
            pl.BlockSpec((length, width), lambda i: (0, INNER // width + i)),
            pl.BlockSpec((8, width), lambda i: (0, i)),
        ),
        input_output_aliases={4: 0},
        compiler_params=params(),
        cost_estimate=cost(12),
    )(projected, grad_mixed, weight, bias, held)


def middle_kernel(
    limit, mixed_out, w_out, tokens, teacher, mask, ssm, gate, gain,
    block_out, grad_result, grad_branch, grad_ssm, grad_gate, error, gain_sums,
):
    step = pl.program_id(0)

    @pl.when(step == 0)
    def _():
        error[...] = jnp.zeros_like(error)
        gain_sums[...] = jnp.zeros_like(gain_sums)

    rows = tokens.shape[0]
    result = tokens[...].astype(F32) + dot(mixed_out[...], w_out[...])
    position = step * rows + lax.broadcasted_iota(jnp.int32, (rows, 1), 0)
    valid = (position < limit[0]).astype(F32)
    weight = valid * mask[:, 0:1]
    block_out[...] = (result * valid).astype(BF16)
    misfit = result - teacher[...].astype(F32)
    pulled = 2.0 * weight * misfit
    grad_result[...] = pulled
    error[...] += jnp.sum(0.5 * pulled * misfit, axis=0, keepdims=True)
    low = pulled.astype(BF16)
    grad_branch[...] = low
    grad_mixed = dot(low, w_out[...], NT)
    g = gate[...]
    sig = sigmoid(g)
    act = g * sig
    inner = ssm[...]
    gated = inner * act
    rho = lax.rsqrt(jnp.mean(gated * gated, axis=1, keepdims=True) + NORM_EPS)
    unit = gated * rho
    gain_sums[...] += jnp.sum(unit * grad_mixed, axis=0, keepdims=True)
    grad_unit = grad_mixed * gain[...]
    share = jnp.mean(grad_unit * unit, axis=1, keepdims=True)
    grad_gated = rho * (grad_unit - unit * share)
    grad_ssm[...] = grad_gated * act
    grad_gate[...] = (grad_gated * inner * (sig * (1.0 + g * (1.0 - sig)))).astype(BF16)


def middle(limit, mixed_out, w_out, tokens, teacher, mask, ssm, projected, gain):
    length = tokens.shape[0]
    rows = 256
    by_row = lambda width: pl.BlockSpec((rows, width), lambda i: (i, 0))
    whole = lambda v: pl.BlockSpec(v.shape, lambda i: (0,) * v.ndim)
    return pl.pallas_call(
        middle_kernel,
        grid=(length // rows,),
        out_shape=(
            shape((length, D), BF16),
            shape((length, D), F32),
            shape((length, D), BF16),
            shape((length, INNER), F32),
            shape((length, WIDE), BF16),
            shape((1, D), F32),
            shape((1, INNER), F32),
        ),
        in_specs=[
            SMEM,
            by_row(INNER),
            whole(w_out),
            by_row(D),
            by_row(D),
            by_row(LANES),
            by_row(INNER),
            by_row(INNER),
            whole(gain),
        ],
        out_specs=(
            by_row(D),
            by_row(D),
            by_row(D),
            by_row(INNER),
            by_row(INNER),
            pl.BlockSpec((1, D), lambda i: (0, 0)),
            pl.BlockSpec((1, INNER), lambda i: (0, 0)),
        ),
        compiler_params=params(),
        cost_estimate=cost(25),
    )(limit, mixed_out, w_out, tokens, teacher, mask, ssm, projected, gain)


def input_kernel(grad_low, w_in, tokens, norm_gain, grad_result, out, sums):
    @pl.when(pl.program_id(0) == 0)
    def _():
        sums[...] = jnp.zeros_like(sums)

    x = tokens[...].astype(F32)
    inverse = lax.rsqrt(jnp.mean(x * x, axis=1, keepdims=True) + NORM_EPS)
    unit = x * inverse
    grad_hidden = dot(grad_low[...], w_in[...], NT)
    sums[...] += jnp.sum(grad_hidden * unit, axis=0, keepdims=True)
    pulled = grad_hidden * norm_gain[...]
    share = jnp.mean(pulled * unit, axis=1, keepdims=True)
    out[...] = grad_result[...] + inverse * (pulled - unit * share)


def input_backward(grad_low, w_in, tokens, norm_gain, grad_result):
    length = tokens.shape[0]
    rows = 256
    by_row = lambda width: pl.BlockSpec((rows, width), lambda i: (i, 0))
    whole = lambda v: pl.BlockSpec(v.shape, lambda i: (0,) * v.ndim)
    return pl.pallas_call(
        input_kernel,
        grid=(length // rows,),
        out_shape=(shape((length, D), F32), shape((1, D), F32)),
        in_specs=[by_row(WIDE), whole(w_in), by_row(D), whole(norm_gain), by_row(D)],
        out_specs=(by_row(D), pl.BlockSpec((1, D), lambda i: (0, 0))),
        compiler_params=params(),
        cost_estimate=cost(15),
    )(grad_low, w_in, tokens, norm_gain, grad_result)


def vector_kernel(tail, conv_sums, sums, skip_sums, norm_sums, gate_sums, gather, out, taps):
    tiles = CONVCH // LANES
    out[...] = jnp.zeros_like(out)
    out[0:TAIL_ROWS, :] = tail[...]
    for k in range(KCONV):
        for i in range(tiles):
            taps[k * 16 + i : k * 16 + i + 1, :] = conv_sums[k : k + 1, i * LANES : (i + 1) * LANES]
    row = lax.broadcasted_iota(jnp.int32, (LANES, LANES), 0)
    col = lax.broadcasted_iota(jnp.int32, (LANES, LANES), 1)
    per_tile = LANES // KCONV

    def exact(v, chosen):
        high = v.astype(BF16)
        rest = v - high.astype(F32)
        middle = rest.astype(BF16)
        low = (rest - middle.astype(F32)).astype(BF16)
        return dot(high, chosen) + (dot(middle, chosen) + dot(low, chosen))

    for q in range(KCONV):
        total = jnp.zeros((tiles, LANES), F32)
        for k in range(KCONV):
            chosen = (col == KCONV * (row % per_tile) + k) & (row // per_tile == q)
            total = total + exact(taps[k * 16 : k * 16 + tiles, :], chosen.astype(BF16))
        out[pl.ds(TAIL_ROWS + q, tiles, stride=KCONV), :] = total
    bias_at = TAIL_ROWS + tiles * KCONV
    for i in range(tiles):
        out[bias_at + i : bias_at + i + 1, :] = conv_sums[KCONV : KCONV + 1, i * LANES : (i + 1) * LANES]
    lane = lax.broadcasted_iota(jnp.int32, (1, LANES), 1)
    skip = exact(jnp.broadcast_to(skip_sums[...], (8, INNER)), gather[...])[0:1, :]
    parts = [sums[0:1, :], sums[1:2, :], skip]
    parts = [jnp.where(lane < HEADS, v, 0.0) for v in parts]
    before = parts[0] + pltpu.roll(parts[1], HEADS, 1) + pltpu.roll(parts[2], 2 * HEADS, 1)
    at, shift = bias_at + tiles, 3 * HEADS
    for source in (norm_sums, gate_sums):
        for j in range(source.shape[1] // LANES):
            here = pltpu.roll(source[:, j * LANES : (j + 1) * LANES], shift, 1)
            out[at : at + 1, :] = jnp.where(lane < shift, before, here)
            before = here
            at += 1
    out[at : at + 1, :] = jnp.where(lane < shift, before, 0.0)


def pack_vectors(tail, conv_sums, sums, skip_sums, norm_sums, gate_sums, gather):
    return pl.pallas_call(
        vector_kernel,
        out_shape=shape(((NBLK - MID1) * BROWS, LANES), F32),
        in_specs=[VMEM] * 7,
        out_specs=VMEM,
        scratch_shapes=[pltpu.VMEM((KCONV * 16, LANES), F32)],
        compiler_params=params(),
    )(tail, conv_sums, sums, skip_sums, norm_sums, gate_sums, gather)


def body(tokens, teacher, lengths, loss_mask, owners, master, first_moment, second_moment):
    capacity = master.shape[0]
    dp, fsdp = lax.axis_size("dp"), lax.axis_size("fsdp")
    devices = dp * fsdp
    me = lax.axis_index(AXES).astype(jnp.int32)
    x_first, y_first, z_first = step_orders(dp, fsdp)
    tie = lambda *values: lax.optimization_barrier(values)

    sent = send_blocks(owners, master, devices, me)
    at_home = lax.all_to_all(sent, AXES, 0, 0, tiled=True)
    owners, tokens, loss_mask, _ = tie(owners, tokens, loss_mask, sent)
    plan = make_plan(owners, capacity, devices, me)
    n0, n1 = plan["slots"]
    streams = cut(n0, (x_first, y_first, z_first))
    table = stream_places(plan["home"], plan["slot"], me, streams, devices)
    table0 = jnp.concatenate([table[:MID0], table[MID1:]])
    table1 = (place_of(plan["home"] ^ me, x_first) * n1 + plan["slot"])[MID0:MID1]
    u0, u1 = plan["unit_slots"]
    unit_streams = cut(u0, (x_first, y_first, x_first, y_first, z_first))
    unit_table = stream_places(plan["unit_home"], plan["unit_slot"], me, unit_streams, devices)
    unit_table = unit_table[:MID0].reshape(-1)
    unit_table1 = place_of(plan["unit_home"] ^ me, x_first) * (u1 + 1) + plan["unit_slot"]
    unit_table1 = unit_table1[MID0:MID1].reshape(-1)
    inputs, target = tokens[0], teacher[0]
    mask = jnp.broadcast_to(loss_mask[0].astype(F32)[:, None], (inputs.shape[0], LANES))
    wide_in = inputs.astype(F32)
    inverse = lax.rsqrt(jnp.mean(wide_in * wide_in, axis=-1, keepdims=True) + NORM_EPS)
    position = jnp.arange(inputs.shape[0], dtype=jnp.int32)
    counted = jnp.sum(jnp.where(position < lengths[0], loss_mask[0], 0)).astype(F32)
    limit = jnp.broadcast_to((END_OUT - plan["row_block"] * PBLOCK)[:, None], (capacity, LANES))
    used = jnp.broadcast_to(plan["row_used"].astype(jnp.int32)[:, None], (capacity, LANES))
    received = jnp.concatenate(plan["received"])
    (at_home, table0, table1, unit_table, unit_table1, inverse, counted, received, back_table,
     row_from) = tie(
        at_home, table0, table1, unit_table, unit_table1, inverse, counted, received,
        plan["back"], plan["row_from"],
    )
    sizes = [size for _, size, _ in streams] + [n1]
    *mine, mine1 = pick_blocks(received, at_home, sizes)
    parts = []
    for values, (_, _, order) in zip(mine, streams):
        parts += gather_steps(values, order)
    *parts, mine1, mask, limit, used = tie(*parts, mine1, mask, limit, used)
    late_steps = x_first[:0:-1]
    for step in late_steps[: max(len(late_steps) - 4, 0)]:
        mine1 = doubled(mine1, step)
    late_steps = late_steps[-4:]
    input_weight, head, tail, conv_weight, conv_bias, heads, skip, norm_gain, gate_gain = unpack_in(
        table0, parts
    )
    if late_steps[-4:-3]:
        mine1, input_weight = tie(doubled(mine1, late_steps[-4]), input_weight)
    dt_bias, a_log = heads[0:1], heads[1:2]
    gather = heads_gather()
    hidden = (wide_in * inverse * norm_gain).astype(BF16)
    projected = dot(hidden, input_weight)
    if late_steps[-3:-2]:
        mine1, projected = tie(doubled(mine1, late_steps[-3]), projected)
    mixed = conv_forward(projected, conv_weight, conv_bias)
    if late_steps[-2:-1]:
        mine1, mixed = tie(doubled(mine1, late_steps[-2]), mixed)
    ssm, mixed_out, states = scan_forward(mixed, projected, dt_bias, a_log, skip, gate_gain)
    if late_steps:
        mine1, mixed_out = tie(doubled(mine1, late_steps[-1]), mixed_out)
    output_weight = unpack_out(table1, mine1, exchange(mine1, x_first[0]), head, tail)
    block_out, grad_result, grad_branch, grad_ssm, grad_low, errors, grad_gate = middle(
        lengths, mixed_out, output_weight, inputs, target, mask, ssm, projected, gate_gain
    )
    local = jnp.concatenate([errors.reshape(-1, LANES), jnp.broadcast_to(counted, (2, LANES))])
    grad_weight_out = dot(mixed_out, grad_branch, (((0,), (0,)), ((), ())))
    keep1, send1, head, tail = pack_out(unit_table1, grad_weight_out, local, devices, u1 + 1)
    sum1 = keep1 + exchange(send1, x_first[0])
    grad_ssm, sum1 = tie(grad_ssm, sum1)
    sum1 = reduce_step(sum1, x_first[1])
    grad_mixed, grad_low, sums, skip_sums = scan_backward(
        mixed, projected, ssm, grad_ssm, states, dt_bias, a_log, skip, gather, grad_low
    )
    grad_mixed, sum1 = tie(grad_mixed, sum1)
    if len(x_first) > 3:
        sum1 = reduce_step(sum1, x_first[2])
    grad_low, conv_sums = conv_backward(projected, grad_mixed, conv_weight, conv_bias, grad_low)
    grad_low, sum1 = tie(grad_low, sum1)
    halves = []
    for _, size, _ in unit_streams:
        halves += [devices * size // 2] * 2
    packed = list(pack_in(unit_table, hidden, grad_low, head, halves))
    reduced = [
        packed[2 * i] + exchange(packed[2 * i + 1], order[0])
        for i, (_, _, order) in enumerate(unit_streams)
    ]
    *reduced, grad_low, conv_sums, tail = tie(*reduced, grad_low, conv_sums, tail)
    reduced = [reduce_step(v, order[1]) for v, (_, _, order) in zip(reduced, unit_streams)]
    input_grad, norm_sums = input_backward(grad_low, input_weight, inputs, norm_gain, grad_result)
    grad_vec = pack_vectors(tail, conv_sums, sums, skip_sums, norm_sums, grad_gate, gather)
    grad_vec = grad_vec.reshape((NBLK - MID1) * UNITS, UNIT, LANES)
    for step in x_first[:2]:
        grad_vec = grad_vec + exchange(grad_vec, step)
    *reduced, sum1, grad_vec, input_grad = tie(*reduced, sum1, grad_vec, input_grad)
    for k in range(2, len(x_first) - 1):
        reduced[0], grad_vec = reduce_step(reduced[0], x_first[k], grad_vec)
        for i in range(1, len(reduced)):
            reduced[i] = reduce_step(reduced[i], unit_streams[i][2][k])
    for step in x_first[3:-1]:
        sum1 = reduce_step(sum1, step)
    ends = []
    for i, values in enumerate(reduced + [sum1]):
        half = values.shape[0] // 2
        given, step = values[half:], (unit_streams[i][2] if i < len(reduced) else x_first)[-1]
        if i == 0:
            got = exchange(jnp.concatenate([given, grad_vec]), step)
            grad_vec = grad_vec + got[half:]
            got = got[:half]
        else:
            got = exchange(given, step)
        ends += [values[:half], got]
    back = units_to_owners(back_table, ends)
    got = lax.all_to_all(back, AXES, 0, 0, tiled=True)
    local_sums = ends[-2][u1] + ends[-1][u1]
    error_sum = jnp.sum(local_sums[: D // LANES])
    divisor = local_sums[D // LANES, 0] * D
    new_first, new_second, new_master = adam(
        row_from,
        divisor,
        got,
        grad_vec,
        limit,
        used,
        master,
        first_moment,
        second_moment,
    )
    mean_loss = error_sum / divisor
    return (block_out[None], input_grad[None], mean_loss, new_first, new_second, new_master)


def solution(mesh):
    return jax.shard_map(
        body,
        mesh=mesh,
        in_specs=(
            P(AXES, None, None),
            P(AXES, None, None),
            P(AXES),
            P(AXES, None),
            P(),
            P(AXES, None),
            P(AXES, None),
            P(AXES, None),
        ),
        out_specs=(
            P(AXES, None, None),
            P(AXES, None, None),
            P(),
            P(AXES, None),
            P(AXES, None),
            P(AXES, None),
        ),
        check_vma=False,
    )
```

```python
from functools import partial

import jax
import jax.numpy as jnp
import numpy as np
from jax import lax
from jax.experimental import pallas as pl
from jax.experimental.pallas import tpu as pltpu
from jax.sharding import PartitionSpec as P

D = 768
INNER = 1536
NSTATE = 128
HEADDIM = 64
KCONV = 4
SCAN_LEN = 256
PBLOCK = 4096
STEP = 10
HEADS = 24
CONVCH = 1792
PROJ = 3352
PTOT = 3765320
NBLK = 920

LANES = 128
BROWS = PBLOCK // LANES
UNIT = 8
UNITS = BROWS // UNIT
END_IN = D * PROJ
END_OUT = END_IN + INNER * D
MID0 = -(-END_IN // PBLOCK)
MID1 = END_OUT // PBLOCK
N0 = MID0 + NBLK - MID1
N1 = MID1 - MID0
F0_ROWS = N0 * BROWS
IN_ROWS = END_IN // LANES
HEAD_ROWS = MID0 * BROWS - IN_ROWS
TAIL_ROWS = (END_OUT - MID1 * PBLOCK) // LANES
OUT_ROWS = INNER * D // LANES
VEC_ROWS = (NBLK - MID1) * BROWS - TAIL_ROWS
VEC_AT = MID0 * BROWS + TAIL_ROWS
GROUP = 16
GROUPS = D // GROUP
GROUP_ROWS = GROUP * PROJ // LANES
COL_TILES = -(-PROJ // LANES)
WIDE = COL_TILES * LANES
OUT_TILES = D // LANES

NORM_EPS = 1e-05
ADAM_EPS = 1e-08
BETA_ONE = 0.9
BETA_TWO = 0.999
MATRIX_RATE = 0.03
VECTOR_RATE = 0.2
WEIGHT_DECAY = 0.1
PRECISE = lax.Precision.HIGHEST
AXES = ("dp", "fsdp")
VMEM_LIMIT = 60 * 1024 * 1024


def bits_of(count):
    return count.bit_length() - 1


def step_orders(dp, fsdp):
    wide = [("dp", i) for i in range(bits_of(dp))]
    narrow = [("fsdp", i) for i in range(bits_of(fsdp))]
    first = wide[:2] + narrow + wide[2:]
    second = wide[:1] + narrow + wide[1:]
    third = wide[:1] + wide[2:] + wide[1:2] + narrow
    return first, second, third


def cut(total, orders):
    base, more = divmod(total, len(orders))
    streams, at = [], 0
    for i, order in enumerate(orders):
        size = base + (i < more)
        if size:
            streams.append((at, size, order))
        at += size
    return streams


def exchange(values, step):
    axis, bit = step
    size = lax.axis_size(axis)
    return lax.ppermute(values, axis, [(i, i ^ (1 << bit)) for i in range(size)])


def place_of(relative, order):
    shift_of = {"dp": bits_of(lax.axis_size("fsdp")), "fsdp": 0}
    place = jnp.zeros_like(relative)
    for axis, bit in order:
        place = place * 2 + ((relative >> (shift_of[axis] + bit)) & 1)
    return place


def class_counts(owners, devices):
    block = jnp.arange(NBLK, dtype=jnp.int32)
    mid = ((block >= MID0) & (block < MID1))[None, :]
    device = jnp.arange(devices, dtype=jnp.int32)
    below = owners[None, :] < device[:, None]
    owned = owners[None, :] == device[:, None]

    def total(mask):
        return jnp.sum(mask.astype(jnp.int32), axis=1)

    start = (total(below & ~mid), total(below & mid))
    count = (total(owned & ~mid), total(owned & mid))
    return start, count, total(owned & (block < MID0)[None, :])


def my_counts(owners, me):
    block = jnp.arange(NBLK, dtype=jnp.int32)
    mid = (block >= MID0) & (block < MID1)
    below, owned = owners < me, owners == me
    total = lambda mask: jnp.sum(mask.astype(jnp.int32))
    start = (total(below & ~mid), total(below & mid))
    count = (total(owned & ~mid), total(owned & mid))
    return start, count, total(owned & (block < MID0))


def pair_lanes(capacity, devices):
    return 2 + max(capacity - 2, 0) // devices


def make_plan(owners, capacity, devices, me):
    block = jnp.arange(NBLK, dtype=jnp.int32)
    mid = (block >= MID0) & (block < MID1)
    same = mid[:, None] == mid[None, :]
    before = (owners[None, :] < owners[:, None]) | (
        (owners[None, :] == owners[:, None]) & (block[None, :] < block[:, None])
    )
    order_in_class = jnp.sum((same & before).astype(jnp.int32), axis=1)
    home, slot = order_in_class % devices, order_in_class // devices
    device = jnp.arange(devices, dtype=jnp.int32)
    start, count, _ = class_counts(owners, devices)
    my_start, my_count, my_early = my_counts(owners, me)
    pair = pair_lanes(capacity, devices)

    slots = (-(-N0 // devices), -(-N1 // devices))

    def received(kind):
        wanted = me + devices * jnp.arange(slots[kind], dtype=jnp.int32)
        ends = start[kind] + count[kind]
        owner = jnp.sum((ends[None, :] <= wanted[:, None]).astype(jnp.int32), axis=1)
        owner = jnp.minimum(owner, devices - 1)
        base = jnp.sum(jnp.where(device[None, :] == owner[:, None], start[kind][None, :], 0), axis=1)
        turn = jnp.clip((wanted - base) // devices, 0, pair - 1)
        return owner * pair + (turn if kind == 0 else pair - 1 - turn)

    back_pair = (UNITS * capacity + 2 * (devices - 1)) // devices
    unit = UNITS * order_in_class[:, None] + jnp.arange(UNITS, dtype=jnp.int32)[None, :]
    unit_home, unit_slot = unit % devices, unit // devices
    unit_slots = (-(-UNITS * N0 // devices), -(-UNITS * N1 // devices))
    lane = jnp.arange(back_pair, dtype=jnp.int32)

    def units_back(kind):
        turn = lane if kind == 0 else back_pair - 1 - lane
        first = UNITS * start[kind][:, None]
        k = (me - first) % devices + turn[None, :] * devices
        return k < UNITS * count[kind][:, None], (first + k) // devices

    valid0, slot0 = units_back(0)
    valid1, slot1 = units_back(1)
    back = jnp.where(valid0, slot0, jnp.where(valid1, unit_slots[0] + slot1, 0)).reshape(-1)

    row = jnp.arange(capacity, dtype=jnp.int32)
    is_mid = (row >= my_early) & (row < my_early + my_count[1])
    k = jnp.where(is_mid, row - my_early, jnp.where(row < my_early, row, row - my_count[1]))
    first = UNITS * jnp.where(is_mid, my_start[1], my_start[0])
    k = UNITS * k[:, None] + jnp.arange(UNITS, dtype=jnp.int32)[None, :]
    turn = k // devices
    row_from = ((first[:, None] + k) % devices) * back_pair + jnp.where(
        is_mid[:, None], back_pair - 1 - turn, turn
    )
    row_used = row < my_count[0] + my_count[1]
    mine = (owners == me)[None, :]
    rank = jnp.sum((mine & (block[None, :] < block[:, None])).astype(jnp.int32), axis=1)
    row_block = jnp.sum(
        jnp.where(mine & (rank[None, :] == row[:, None]), block[None, :], 0), axis=1
    )
    late = devices * back_pair + UNITS * (row_block - MID1)
    late = late[:, None] + jnp.arange(UNITS, dtype=jnp.int32)[None, :]
    row_from = jnp.where((row_block >= MID1)[:, None], late, row_from)
    row_from = jnp.where(row_used[:, None], row_from, 0).reshape(-1)
    return dict(
        home=home, slot=slot, slots=slots,
        received=(received(0), received(1)), unit_home=unit_home, unit_slot=unit_slot,
        unit_slots=unit_slots, back=back, row_from=row_from,
        row_used=row_used, row_block=row_block,
    )


def stream_places(home, slot, me, streams, devices):
    relative = home ^ me
    place = jnp.zeros_like(slot)
    for begin, size, order in streams:
        inside = (slot >= begin) & (slot < begin + size)
        at = devices * begin + place_of(relative, order) * size + slot - begin
        place = jnp.where(inside, at, place)
    return place


def cost(microseconds):
    return pl.CostEstimate(
        flops=int(microseconds * 1e9), bytes_accessed=int(microseconds * 3e6), transcendentals=0
    )


ANY = pl.BlockSpec(memory_space=pl.ANY)
VMEM = pl.BlockSpec(memory_space=pltpu.VMEM)
SMEM = pl.BlockSpec(memory_space=pltpu.SMEM)


def params(**extra):
    return pltpu.CompilerParams(vmem_limit_bytes=VMEM_LIMIT, **extra)


def shape(dims, dtype):
    return jax.ShapeDtypeStruct(dims, dtype)


def send_kernel(my_index, owners, master, out, flat, *, devices):
    capacity = master.shape[0]
    me = my_index[0]
    for j in range(BROWS):
        flat[pl.ds(j, capacity, stride=BROWS), :] = master[:, j * LANES : (j + 1) * LANES]
    held = owners[...]
    block = lax.broadcasted_iota(jnp.int32, held.shape, 0) * LANES + lax.broadcasted_iota(
        jnp.int32, held.shape, 1
    )
    mid = (block >= MID0) & (block < MID1)
    below, owned = held < me, held == me

    def total(mask):
        return jnp.sum(jnp.where(mask, 1.0, 0.0)).astype(jnp.int32)

    start0, start1 = total(below & ~mid), total(below & mid)
    count0, count1 = total(owned & ~mid), total(owned & mid)
    early = total(owned & (block < MID0))
    pair = out.shape[0] // devices
    positive = devices * NBLK

    def step(home, carry):
        for s in range(pair):
            k0 = lax.rem(home - start0 + positive, devices) + s * devices
            k1 = lax.rem(home - start1 + positive, devices) + (pair - 1 - s) * devices
            row0 = jnp.where(k0 < early, k0, k0 + count1)
            row = jnp.where(k0 < count0, row0, jnp.where(k1 < count1, early + k1, 0))
            rows = pl.ds(pl.multiple_of(row * BROWS, BROWS), BROWS)
            out[home * pair + s] = flat[rows, :].astype(out.dtype)
        return carry

    lax.fori_loop(0, devices, step, 0)


def send_blocks(owners, master, devices, me):
    rows = -(-NBLK // (8 * LANES)) * 8
    held = jnp.pad(owners, (0, rows * LANES - NBLK), constant_values=1 << 20).reshape(rows, LANES)
    count = devices * pair_lanes(master.shape[0], devices)
    return pl.pallas_call(
        partial(send_kernel, devices=devices),
        out_shape=shape((count, BROWS, LANES), jnp.bfloat16),
        in_specs=[SMEM, VMEM, VMEM],
        out_specs=VMEM,
        scratch_shapes=[pltpu.VMEM((master.shape[0] * BROWS, LANES), jnp.float32)],
        compiler_params=params(),
    )(me.reshape(1), held, master)


def pick_kernel(table, source, *outs):
    at = 0
    for out in outs:

        def step(i, carry, out=out, at=at):
            out[i] = source[table[at + i]]
            return carry

        lax.fori_loop(0, out.shape[0], step, 0)
        at += out.shape[0]


def pick_blocks(table, source, sizes):
    return pl.pallas_call(
        pick_kernel,
        out_shape=tuple(shape((n,) + source.shape[1:], source.dtype) for n in sizes),
        in_specs=[SMEM, VMEM],
        out_specs=(VMEM,) * len(sizes),
        compiler_params=params(),
    )(table, source)


def back_kernel(table, *refs):
    sources, (out, held) = refs[:-2], refs[-2:]
    at = 0
    for i in range(0, len(sources), 2):
        n = sources[i].shape[0]
        held[at : at + n] = sources[i][...] + sources[i + 1][...]
        at += n

    def step(i, carry):
        for u in range(8):
            out[i * 8 + u] = held[table[i * 8 + u]]
        return carry

    total = out.shape[0]
    lax.fori_loop(0, total // 8, step, 0)


def units_to_owners(table, sources):
    return pl.pallas_call(
        back_kernel,
        out_shape=shape((table.shape[0], UNIT, LANES), jnp.float32),
        in_specs=[SMEM] + [VMEM] * len(sources),
        out_specs=VMEM,
        scratch_shapes=[
            pltpu.VMEM((sum(s.shape[0] for s in sources[::2]), UNIT, LANES), jnp.float32)
        ],
        compiler_params=params(),
    )(table, *sources)


def row_start(rho):
    return (PROJ * rho) // LANES, (PROJ * rho) % LANES


def copy_all(pairs, sem):
    copies = [pltpu.make_async_copy(a, b, sem.at[i]) for i, (a, b) in enumerate(pairs)]
    for c in copies:
        c.start()
    for c in copies:
        c.wait()


def spread_blocks(table, held, flat, count, first_row):
    def one(i):
        at = pl.multiple_of(first_row + i * BROWS, 16)
        flat[pl.ds(at, BROWS), :] = held[table[i]].astype(jnp.float32)

    def step(i, carry):
        for u in range(4):
            one(i * 4 + u)
        return carry

    lax.fori_loop(0, count // 4, step, 0)
    for i in range(count // 4 * 4, count):
        one(i)


def unpack_vectors(flat, conv_weight, conv_bias, heads, skip, norm_gain, gate_gain):
    bf16, f32 = jnp.bfloat16, jnp.float32
    tiles = CONVCH // LANES
    row = lax.broadcasted_iota(jnp.int32, (LANES, LANES), 0)
    col = lax.broadcasted_iota(jnp.int32, (LANES, LANES), 1)
    per_tile = LANES // KCONV
    for k in range(KCONV):
        total = jnp.zeros((tiles, LANES), f32)
        for q in range(KCONV):
            rows = flat[pl.ds(VEC_AT + q, tiles, stride=KCONV), :].astype(bf16)
            chosen = (row == KCONV * (col % per_tile) + k) & (col // per_tile == q)
            total = total + jnp.dot(rows, chosen.astype(bf16), preferred_element_type=f32)
        for i in range(tiles):
            conv_weight[k : k + 1, i * LANES : (i + 1) * LANES] = total[i : i + 1, :]
    bias_at = VEC_AT + tiles * KCONV
    for i in range(tiles):
        conv_bias[:, i * LANES : (i + 1) * LANES] = flat[bias_at + i : bias_at + i + 1, :]
    at = bias_at + tiles
    lane = lax.broadcasted_iota(jnp.int32, (8, LANES), 1)
    first = flat[at : at + 8, :]
    three = []
    for i in range(3):
        moved = pltpu.roll(first, LANES - i * HEADS, 1) if i else first
        three.append(jnp.where(lane < HEADS, moved, 0.0))
        heads[i : i + 1, :] = three[i][0:1, :]
    for j in range(INNER // LANES):
        h = lax.broadcasted_iota(jnp.int32, (LANES, LANES), 0)
        c = lax.broadcasted_iota(jnp.int32, (LANES, LANES), 1) + j * LANES
        spread = (h == c // HEADDIM).astype(bf16)
        wide = jnp.dot(three[2].astype(bf16), spread, preferred_element_type=f32)
        skip[:, j * LANES : (j + 1) * LANES] = wide[0:1, :]
    shift = 3 * HEADS
    for out, begin, width in ((norm_gain, at, D), (gate_gain, at + D // LANES, INNER)):
        for j in range(width // LANES):
            x = pltpu.roll(flat[begin + j : begin + j + 1, :], LANES - shift, 1)
            y = pltpu.roll(flat[begin + j + 1 : begin + j + 2, :], LANES - shift, 1)
            out[:, j * LANES : (j + 1) * LANES] = jnp.where(lane[0:1] < LANES - shift, x, y)


def unpack_in_kernel(table, *refs):
    parts, (w_in, head, tail, *vectors), (held, flat, tile, sem) = refs[:-13], refs[-13:-4], refs[-4:]
    pairs, at = [], 0
    for part in parts:
        pairs.append((part, held.at[pl.ds(at, part.shape[0])]))
        at += part.shape[0]
    copy_all(pairs, sem)
    spread_blocks(table, held, flat, N0, 0)
    head[...] = flat[IN_ROWS : IN_ROWS + HEAD_ROWS, :]
    tail[...] = flat[MID0 * BROWS : MID0 * BROWS + TAIL_ROWS, :]
    unpack_vectors(flat, *vectors)
    lane = lax.broadcasted_iota(jnp.int32, (GROUPS, LANES), 1)

    def columns(j):
        for rho in range(GROUP):
            c, s = row_start(rho)
            x = flat[pl.ds(c + j, GROUPS, stride=GROUP_ROWS), :]
            if s:
                y = flat[pl.ds(c + j + 1, GROUPS, stride=GROUP_ROWS), :]
                x = jnp.where(
                    lane < LANES - s,
                    pltpu.roll(x, LANES - s, 1),
                    pltpu.roll(y, LANES - s, 1),
                )
            tile[pl.ds(rho, GROUPS, stride=GROUP), :] = x

    def step(j, carry):
        columns(j)
        w_in[:, pl.ds(pl.multiple_of(j * LANES, LANES), LANES)] = tile[...].astype(jnp.bfloat16)
        return carry

    lax.fori_loop(0, COL_TILES - 1, step, 0)
    columns(COL_TILES - 1)
    last = (COL_TILES - 1) * LANES
    inside = lax.broadcasted_iota(jnp.int32, (D, LANES), 1) < PROJ - last
    w_in[:, last:] = jnp.where(inside, tile[...], 0.0).astype(jnp.bfloat16)


def unpack_in(table, parts):
    held = sum(part.shape[0] for part in parts)
    return pl.pallas_call(
        unpack_in_kernel,
        out_shape=(
            shape((D, WIDE), jnp.bfloat16),
            shape((HEAD_ROWS, LANES), jnp.float32),
            shape((TAIL_ROWS, LANES), jnp.float32),
            shape((KCONV, CONVCH), jnp.float32),
            shape((1, CONVCH), jnp.float32),
            shape((8, LANES), jnp.float32),
            shape((1, INNER), jnp.float32),
            shape((1, D), jnp.float32),
            shape((1, INNER), jnp.float32),
        ),
        in_specs=[SMEM] + [ANY] * len(parts),
        out_specs=(VMEM,) * 9,
        scratch_shapes=[
            pltpu.VMEM((held, BROWS, LANES), jnp.bfloat16),
            pltpu.VMEM((F0_ROWS, LANES), jnp.float32),
            pltpu.VMEM((D, LANES), jnp.float32),
            pltpu.SemaphoreType.DMA((len(parts),)),
        ],
        compiler_params=params(),
        cost_estimate=cost(16),
    )(table, *parts)


def unpack_out_kernel(table, own, got, head, tail, w_out, flat, held, sem):
    half = own.shape[0]
    copy_all([(own, held.at[pl.ds(0, half)]), (got, held.at[pl.ds(half, half)])], sem)
    flat[0:HEAD_ROWS, :] = head[...]
    flat[OUT_ROWS - TAIL_ROWS : OUT_ROWS, :] = tail[...]
    spread_blocks(table, held, flat, N1, HEAD_ROWS)
    rows = 128

    def step(i, carry):
        at = pl.multiple_of(i * rows, rows)
        for j in range(OUT_TILES):
            x = flat[pl.ds(at * OUT_TILES + j, rows, stride=OUT_TILES), :]
            w_out[pl.ds(at, rows), j * LANES : (j + 1) * LANES] = x.astype(jnp.bfloat16)
        return carry

    lax.fori_loop(0, INNER // rows, step, 0)


def unpack_out(table, own, got, head, tail):
    return pl.pallas_call(
        unpack_out_kernel,
        out_shape=shape((INNER, D), jnp.bfloat16),
        in_specs=[SMEM, ANY, ANY, VMEM, VMEM],
        out_specs=VMEM,
        scratch_shapes=[
            pltpu.VMEM((OUT_ROWS, LANES), jnp.float32),
            pltpu.VMEM((2 * own.shape[0], BROWS, LANES), jnp.bfloat16),
            pltpu.SemaphoreType.DMA((2,)),
        ],
        compiler_params=params(),
    )(table, own, got, head, tail)


def permute_units(table, flat, count, first_row, staged):
    many = 16

    def step(i, carry):
        for u in range(many):
            at = pl.multiple_of(first_row + (i * many + u) * UNIT, UNIT)
            staged[table[i * many + u]] = flat[pl.ds(at, UNIT), :]
        return carry

    lax.fori_loop(0, count // many, step, 0)
    for i in range(count // many * many, count):
        staged[table[i]] = flat[first_row + i * UNIT : first_row + (i + 1) * UNIT, :]


def pack_in_kernel(table, hidden, grad, head, *refs):
    outs, (turned, tiles, flat, staged, sem) = refs[:-5], refs[-5:]
    turned[...] = hidden[...].T
    lane = lax.broadcasted_iota(jnp.int32, (GROUPS, LANES), 1)

    def product(p, count):
        at = p * 2 * LANES
        at = at if isinstance(at, int) else pl.multiple_of(at, 2 * LANES)
        return jnp.dot(
            turned[...], grad[:, pl.ds(at, count * LANES)], preferred_element_type=jnp.float32
        )

    def put(p, value):
        for k in range(value.shape[1] // LANES):
            at = (p * 2 + k) * D
            at = at if isinstance(at, int) else pl.multiple_of(at, D)
            tiles[pl.ds(at, D), :] = value[:, k * LANES : (k + 1) * LANES]

    def load(rho, j):
        return tiles[pl.ds(j * D + rho, GROUPS, stride=GROUP), :]

    def whole(rho, i):
        first = -(-PROJ * rho // LANES)
        col0 = first * LANES - PROJ * rho
        x = load(rho, i)
        if col0:
            x = jnp.where(
                lane < LANES - col0,
                pltpu.roll(x, LANES - col0, 1),
                pltpu.roll(load(rho, i + 1), LANES - col0, 1),
            )
        flat[pl.ds(first + i, GROUPS, stride=GROUP_ROWS), :] = x

    put(0, product(0, 2))
    put(1, product(1, 2))
    pairs = COL_TILES // 2

    def step(p, carry):
        for i in range(2):
            for rho in range(GROUP):
                whole(rho, p * 2 + i)
        put(p + 2, product(p + 2, 2))
        return carry

    lax.fori_loop(0, pairs - 2, step, 0)
    put(pairs, product(pairs, COL_TILES % 2))
    for rho in range(GROUP):
        first = -(-PROJ * rho // LANES)
        col0 = first * LANES - PROJ * rho
        full = (PROJ - col0) // LANES
        for i in range((pairs - 2) * 2, full):
            whole(rho, i)
        left = PROJ - col0 - full * LANES
        if left:
            begin = col0 + full * LANES
            j, s = begin // LANES, begin % LANES
            x = pltpu.roll(load(rho, j), LANES - s, 1) if s else load(rho, j)
            if s + left > LANES:
                x = jnp.where(lane < LANES - s, x, pltpu.roll(load(rho, j + 1), LANES - s, 1))
            y = pltpu.roll(load(rho + 1, 0), left, 1)
            flat[pl.ds(first + full, GROUPS, stride=GROUP_ROWS), :] = jnp.where(lane < left, x, y)
    flat[IN_ROWS : IN_ROWS + HEAD_ROWS, :] = head[...]
    permute_units(table, flat, MID0 * UNITS, 0, staged)
    copies, at = [], 0
    for out in outs:
        copies.append((staged.at[pl.ds(at, out.shape[0])], out))
        at += out.shape[0]
    copy_all(copies, sem)


def pack_in(table, hidden, grad, head, sizes):
    return pl.pallas_call(
        pack_in_kernel,
        out_shape=tuple(shape((n, UNIT, LANES), jnp.float32) for n in sizes),
        in_specs=[SMEM, VMEM, VMEM, VMEM],
        out_specs=(ANY,) * len(sizes),
        scratch_shapes=[
            pltpu.VMEM((D, hidden.shape[0]), jnp.bfloat16),
            pltpu.VMEM((COL_TILES * D, LANES), jnp.float32),
            pltpu.VMEM((MID0 * BROWS, LANES), jnp.float32),
            pltpu.VMEM((sum(sizes), UNIT, LANES), jnp.float32),
            pltpu.SemaphoreType.DMA((len(sizes),)),
        ],
        compiler_params=params(),
        cost_estimate=cost(20),
    )(table, hidden, grad, head)


def pack_out_kernel(table, grad, local, keep, send, head, tail, flat, out, sem, *, slots):
    rows = 128

    def step(i, carry):
        at = pl.multiple_of(i * rows, rows)
        for j in range(OUT_TILES):
            flat[pl.ds(at * OUT_TILES + j, rows, stride=OUT_TILES), :] = grad[
                pl.ds(at, rows), j * LANES : (j + 1) * LANES
            ]
        return carry

    lax.fori_loop(0, INNER // rows, step, 0)
    head[...] = flat[0:HEAD_ROWS, :]
    tail[...] = flat[OUT_ROWS - TAIL_ROWS : OUT_ROWS, :]
    permute_units(table, flat, N1 * UNITS, HEAD_ROWS, out)

    def add_local(i, carry):
        out[i * slots + slots - 1] = local[...]
        return carry

    lax.fori_loop(0, out.shape[0] // slots, add_local, 0)
    half = keep.shape[0]
    copy_all([(out.at[pl.ds(0, half)], keep), (out.at[pl.ds(half, half)], send)], sem)


def pack_out(table, grad, local, devices, slots):
    return pl.pallas_call(
        partial(pack_out_kernel, slots=slots),
        out_shape=(
            shape((devices * slots // 2, UNIT, LANES), jnp.float32),
            shape((devices * slots // 2, UNIT, LANES), jnp.float32),
            shape((HEAD_ROWS, LANES), jnp.float32),
            shape((TAIL_ROWS, LANES), jnp.float32),
        ),
        in_specs=[SMEM, VMEM, VMEM],
        out_specs=(ANY, ANY, VMEM, VMEM),
        scratch_shapes=[
            pltpu.VMEM((OUT_ROWS, LANES), jnp.float32),
            pltpu.VMEM((devices * slots, UNIT, LANES), jnp.float32),
            pltpu.SemaphoreType.DMA((2,)),
        ],
        compiler_params=params(),
    )(table, grad, local)


def adam_kernel(table, scale, got, late, limit, used, master, first, second, o_first, o_second, o_master, flat, held):
    capacity = master.shape[0]

    def step(i, carry):
        for u in range(UNITS):
            at = table[i * UNITS + u]
            rows = pl.ds(pl.multiple_of(i * BROWS + u * UNIT, UNIT), UNIT)
            flat[rows, :] = held[at]
        return carry

    held[0 : got.shape[0]] = got[...]
    held[got.shape[0] :] = late[...]
    lax.fori_loop(0, capacity, step, 0)
    lane = lax.broadcasted_iota(jnp.int32, (capacity, LANES), 1)
    divisor = scale[0]
    for j in range(BROWS):
        cols = slice(j * LANES, (j + 1) * LANES)
        grad = jnp.where(used[...] > 0, flat[pl.ds(j, capacity, stride=BROWS), :], 0.0) / divisor
        matrix = lane + j * LANES < limit[...]
        weights = master[:, cols]
        new_first = BETA_ONE * first[:, cols] + (1.0 - BETA_ONE) * grad
        new_second = BETA_TWO * second[:, cols] + (1.0 - BETA_TWO) * grad * grad
        normal = (
            new_first
            / (1.0 - BETA_ONE**STEP)
            / (jnp.sqrt(new_second / (1.0 - BETA_TWO**STEP)) + ADAM_EPS)
        )
        rate = jnp.where(matrix, MATRIX_RATE, VECTOR_RATE)
        decay = jnp.where(matrix, WEIGHT_DECAY, 0.0)
        o_first[:, cols] = new_first
        o_second[:, cols] = new_second
        o_master[:, cols] = weights - rate * (normal + decay * weights)


def adam(table, divisor, got, late, limit, used, master, first, second):
    capacity = master.shape[0]
    return pl.pallas_call(
        adam_kernel,
        out_shape=(shape(master.shape, jnp.float32),) * 3,
        in_specs=[SMEM, SMEM] + [VMEM] * 7,
        out_specs=(VMEM,) * 3,
        scratch_shapes=[
            pltpu.VMEM((capacity * BROWS, LANES), jnp.float32),
            pltpu.VMEM((got.shape[0] + late.shape[0], UNIT, LANES), jnp.float32),
        ],
        compiler_params=params(),
    )(table, divisor.reshape(1), got, late, limit, used, master, first, second)


def doubled(values, step):
    return jnp.concatenate([values, exchange(values, step)], axis=0)


def gather_steps(values, order):
    for step in order[:0:-1]:
        values = doubled(values, step)
    return values, exchange(values, order[0])


def reduce_step(values, step, extra=None):
    half = values.shape[0] // 2
    if extra is None:
        return values[:half] + exchange(values[half:], step)
    got = exchange(jnp.concatenate([values[half:], extra]), step)
    return values[:half] + got[:half], extra + got[half:]


CHUNK = 128
PAIRS = HEADS // 2
MIXW = INNER + 2 * NSTATE
DT_AT = INNER + CONVCH
F32 = jnp.float32
BF16 = jnp.bfloat16
NN = (((1,), (0,)), ((), ()))
NT = (((1,), (1,)), ((), ()))


def dot(a, b, dims=NN):
    return lax.dot_general(a, b, dims, preferred_element_type=F32)


def split(v):
    high = v.astype(BF16)
    return high, (v - high.astype(F32)).astype(BF16)


def dot3(a, b, dims=NN):
    ah, al = a
    bh, bl = b
    return dot(ah, bh, dims) + (dot(ah, bl, dims) + dot(al, bh, dims))


def heads_gather():
    return jnp.asarray(np.repeat(np.eye(HEADS, LANES, dtype=np.float32), HEADDIM, axis=0), BF16)


def three_parts(v):
    high = v.astype(BF16).astype(F32)
    rest = v - high
    middle = rest.astype(BF16).astype(F32)
    low = rest - middle
    return (high + pltpu.roll(middle, 32, 1) + pltpu.roll(low, 64, 1)).astype(BF16)


def triangle_sum(tri, v):
    parts = dot(tri, three_parts(v))
    lane = lax.broadcasted_iota(jnp.int32, parts.shape, 1)
    total = parts + pltpu.roll(parts, LANES - 32, 1) + pltpu.roll(parts, LANES - 64, 1)
    return jnp.where(lane < HEADS, total, 0.0)


def chunk_decays(dt, dt_bias, a_log):
    lane = lax.broadcasted_iota(jnp.int32, (CHUNK, LANES), 1)
    row = lax.broadcasted_iota(jnp.int32, (CHUNK, LANES), 0)
    shifted = dt + dt_bias
    delta = jnp.where(
        lane < HEADS, jnp.maximum(shifted, 0.0) + jnp.log1p(jnp.exp(-jnp.abs(shifted))), 0.0
    )
    rate = -jnp.exp(a_log)
    lower = (row >= lane).astype(BF16)
    cum = triangle_sum(lower, delta * rate)
    last = cum[CHUNK - 1 : CHUNK, :]
    return shifted, delta, rate, cum, last


def pair_mask():
    lane = lax.broadcasted_iota(jnp.int32, (CHUNK, LANES), 1)
    low = (lane < HEADDIM).astype(F32)
    return low.astype(BF16), (1.0 - low).astype(BF16)


QUADS = HEADS // 4
QWIDTH = 4 * HEADDIM


def sigmoid(v):
    return 0.5 * jnp.tanh(0.5 * v) + 0.5


def silu(v):
    return v * sigmoid(v)


def side_by_side(v):
    high, low = split(v)
    return jnp.concatenate([high, low], axis=1), high


def dot_parts(a, b):
    ahl, ah = a
    bh, bl = b
    return dot(ahl, jnp.concatenate([bh, bh], axis=0)) + dot(ah, bl)


def dot_turned(a, b):
    ah, al = a
    bh, bl = b
    both = dot(ah, jnp.concatenate([bh, bl], axis=0), NT)
    n = bh.shape[0]
    return both[:, :n] + both[:, n:] + dot(al, bh, NT)


def widen(delta, cum, quad):
    lane = lax.broadcasted_iota(jnp.int32, (CHUNK, LANES), 1)
    over = lambda v, h: jnp.broadcast_to(v[:, h : h + 1], (CHUNK, LANES))
    first = 4 * quad
    columns = [over(cum, first + k) for k in range(4)]
    rates = [over(delta, first + k) for k in range(4)]
    pair = lambda vs: jnp.concatenate(
        [jnp.where(lane < HEADDIM, vs[0], vs[1]), jnp.where(lane < HEADDIM, vs[2], vs[3])], axis=1
    )
    return pair(rates), pair(columns), columns


def pair_rows(parts, j, low, high):
    cols = slice(j * LANES, (j + 1) * LANES)
    return [jnp.concatenate([p[:, cols] * low, p[:, cols] * high], axis=0) for p in parts]


def scan_forward_kernel(
    mixed, dt, gate, dt_bias, a_log, skip, gain, ssm, mixed_out, states, state
):
    @pl.when(pl.program_id(0) == 0)
    def _():
        state[...] = jnp.zeros_like(state)

    states[0] = state[...]
    _, delta, _, cum, last = chunk_decays(dt[...], dt_bias[...], a_log[...])
    lane = lax.broadcasted_iota(jnp.int32, (CHUNK, LANES), 1)
    row = lax.broadcasted_iota(jnp.int32, (CHUNK, LANES), 0)
    bias = jnp.where(row >= lane, 0.0, -1e30)
    cum_t = cum.T
    inputs_b = mixed[:, INNER : INNER + NSTATE]
    readout = mixed[:, INNER + NSTATE :]
    affinity = dot3(split(readout), split(inputs_b), NT)
    readout_parts = side_by_side(readout)
    b_parts = side_by_side(inputs_b.T)
    low, high = pair_mask()
    squares = jnp.zeros((CHUNK, LANES), F32)
    for quad in range(QUADS):
        cols = slice(quad * QWIDTH, (quad + 1) * QWIDTH)
        wide_delta, wide_cum, columns = widen(delta, cum, quad)
        values = mixed[:, cols]
        scaled = values * wide_delta
        parts = split(scaled)
        outs = []
        for j in range(2):
            right_h, right_l = pair_rows(parts, j, low, high)
            left = []
            for k in range(2):
                h = 4 * quad + 2 * j + k
                within = jnp.exp(columns[2 * j + k] - cum_t[h : h + 1, :] + bias)
                left.append(split(affinity * within))
            left_h = jnp.concatenate([left[0][0], left[1][0]], axis=1)
            left_l = jnp.concatenate([left[0][1], left[1][1]], axis=1)
            both = dot(left_h, jnp.concatenate([right_h, right_l], axis=1))
            outs.append(both[:, :LANES] + both[:, LANES:] + dot(left_l, right_h))
        carried = state[:, cols]
        grown = jnp.exp(wide_cum)
        out = jnp.concatenate(outs, axis=1) + dot_parts(readout_parts, split(carried)) * grown
        out = out + skip[:, cols] * values
        tail = jnp.exp(wide_cum[CHUNK - 1 :] - wide_cum)
        state[:, cols] = carried * grown[CHUNK - 1 :] + dot_parts(b_parts, split(scaled * tail))
        ssm[:, cols] = out
        gated = out * silu(gate[:, cols])
        squares = squares + gated[:, :LANES] * gated[:, :LANES] + gated[:, LANES:] * gated[:, LANES:]
    rho = lax.rsqrt(jnp.sum(squares, axis=1, keepdims=True) * (1.0 / INNER) + NORM_EPS)
    for j in range(PAIRS):
        cols = slice(j * LANES, (j + 1) * LANES)
        gated = ssm[:, cols] * silu(gate[:, cols])
        mixed_out[:, cols] = (gated * rho * gain[:, cols]).astype(BF16)


def scan_forward(mixed, projected, dt_bias, a_log, skip, gain):
    length = mixed.shape[0]
    chunks = length // CHUNK
    whole = lambda v: pl.BlockSpec(v.shape, lambda i: (0,) * v.ndim)
    return pl.pallas_call(
        scan_forward_kernel,
        grid=(chunks,),
        out_shape=(
            shape((length, INNER), F32),
            shape((length, INNER), BF16),
            shape((chunks, NSTATE, INNER), F32),
        ),
        in_specs=[
            pl.BlockSpec((CHUNK, MIXW), lambda i: (i, 0)),
            pl.BlockSpec((CHUNK, LANES), lambda i: (i, DT_AT // LANES)),
            pl.BlockSpec((CHUNK, INNER), lambda i: (i, 0)),
        ]
        + [whole(v) for v in (dt_bias, a_log, skip, gain)],
        out_specs=(
            pl.BlockSpec((CHUNK, INNER), lambda i: (i, 0)),
            pl.BlockSpec((CHUNK, INNER), lambda i: (i, 0)),
            pl.BlockSpec((1, NSTATE, INNER), lambda i: (i, 0, 0)),
        ),
        scratch_shapes=[pltpu.VMEM((NSTATE, INNER), F32)],
        compiler_params=params(),
        cost_estimate=cost(40),
    )(mixed, projected, projected, dt_bias, a_log, skip, gain)


def scan_backward_kernel(
    mixed, dt, ssm, grad, states, dt_bias, a_log, skip, gather, held,
    grad_mixed, grad_dt, sums, skip_sums, grad_state, left, right,
):
    @pl.when(pl.program_id(0) == 0)
    def _():
        grad_state[...] = jnp.zeros_like(grad_state)
        sums[...] = jnp.zeros_like(sums)
        skip_sums[...] = jnp.zeros_like(skip_sums)

    shifted, delta, rate, cum, last = chunk_decays(dt[...], dt_bias[...], a_log[...])
    lane = lax.broadcasted_iota(jnp.int32, (CHUNK, LANES), 1)
    row = lax.broadcasted_iota(jnp.int32, (CHUNK, LANES), 0)
    bias = jnp.where(lane >= row, 0.0, -1e30)
    heads = lane < HEADS
    cum_t = cum.T
    inputs_b = mixed[:, INNER : INNER + NSTATE]
    readout = mixed[:, INNER + NSTATE :]
    b_parts, c_parts = split(inputs_b), split(readout)
    b_wide = side_by_side(inputs_b)
    c_turned = side_by_side(readout.T)
    affinity = dot3(b_parts, c_parts, NT)
    low, high = pair_mask()
    grad_affinity = jnp.zeros((CHUNK, CHUNK), F32)
    grad_b = jnp.zeros((CHUNK, NSTATE), F32)
    grad_c = jnp.zeros((CHUNK, NSTATE), F32)
    last_row = lax.broadcasted_iota(jnp.int32, (CHUNK, QWIDTH), 0) == CHUNK - 1
    for quad in range(QUADS):
        cols = slice(quad * QWIDTH, (quad + 1) * QWIDTH)
        wide_delta, wide_cum, columns = widen(delta, cum, quad)
        grown = jnp.exp(wide_cum)
        tail = jnp.exp(wide_cum[CHUNK - 1 :] - wide_cum)
        end = grown[CHUNK - 1 :]
        values = mixed[:, cols]
        pulled = grad[:, cols]
        scaled = values * wide_delta
        x_parts, p_parts = split(scaled), split(pulled)
        outs = []
        for j in range(2):
            half = slice(j * LANES, (j + 1) * LANES)
            xh, xl = x_parts[0][:, half], x_parts[1][:, half]
            right_h, right_l = pair_rows(p_parts, j, low, high)
            pull = dot(
                jnp.concatenate([xh, xl], axis=1),
                jnp.concatenate([right_h, right_h], axis=1),
                NT,
            ) + dot(xh, right_l, NT)
            kernels = []
            for k in range(2):
                h = 4 * quad + 2 * j + k
                within = jnp.exp(cum_t[h : h + 1, :] - columns[2 * j + k] + bias)
                kernels.append(split(affinity * within))
                grad_affinity = grad_affinity + within * pull[:, k * CHUNK : (k + 1) * CHUNK]
            kernel_h = jnp.concatenate([kernels[0][0], kernels[1][0]], axis=1)
            kernel_l = jnp.concatenate([kernels[0][1], kernels[1][1]], axis=1)
            both = dot(kernel_h, jnp.concatenate([right_h, right_l], axis=1))
            outs.append(both[:, :LANES] + both[:, LANES:] + dot(kernel_l, right_h))
        late = grad_state[:, cols]
        late_parts = split(late)
        early = states[0, :, cols]
        from_state = dot_parts(b_wide, late_parts) * tail
        grad_scaled = jnp.concatenate(outs, axis=1) + from_state
        pulled_cum = split(pulled * grown)
        grad_c = grad_c + dot_turned(pulled_cum, split(early))
        grad_b = grad_b + dot_turned(split(scaled * tail), late_parts)
        grad_state[:, cols] = late * end + dot_parts(c_turned, pulled_cum)
        grad_mixed[:, cols] = grad_scaled * wide_delta + skip[:, cols] * pulled
        skip_sums[:, cols] += jnp.sum(pulled * values, axis=0, keepdims=True)
        left[:, cols] = grad_scaled * values
        inner = pulled * (ssm[:, cols] - skip[:, cols] * values) - scaled * grad_scaled
        extra = jnp.sum(scaled * from_state, axis=0, keepdims=True) + end * jnp.sum(
            late * early, axis=0, keepdims=True
        )
        right[:, cols] = inner + jnp.where(last_row, extra, 0.0)
    ga_parts = split(grad_affinity)
    grad_mixed[:, INNER : INNER + NSTATE] = grad_b + dot3(ga_parts, c_parts)
    grad_mixed[:, INNER + NSTATE :] = grad_c + dot3(split(grad_affinity.T), b_parts)

    def by_head(v):
        high, low = split(v)
        g = gather[...]
        return dot(high, g) + dot(low, g)

    direct = by_head(left[...])
    grad_cum = by_head(right[...])
    upper = (lane >= row).astype(BF16)
    after = triangle_sum(upper, grad_cum)
    grad_delta = direct + rate * after
    grad_raw = jnp.where(heads, grad_delta * sigmoid(shifted), 0.0)
    grad_dt[...] = grad_raw.astype(BF16)
    sums[0:1, :] += jnp.sum(grad_raw, axis=0, keepdims=True)
    sums[1:2, :] += rate * jnp.sum(delta * after, axis=0, keepdims=True)


def scan_backward(mixed, projected, ssm, grad, states, dt_bias, a_log, skip, gather, held):
    length = mixed.shape[0]
    chunks = length // CHUNK
    whole = lambda v: pl.BlockSpec(v.shape, lambda i: (0,) * v.ndim)
    back = lambda i: (chunks - 1 - i, 0)
    return pl.pallas_call(
        scan_backward_kernel,
        grid=(chunks,),
        out_shape=(
            shape((length, MIXW), F32),
            shape(held.shape, BF16),
            shape((8, LANES), F32),
            shape((1, INNER), F32),
        ),
        in_specs=[
            pl.BlockSpec((CHUNK, MIXW), back),
            pl.BlockSpec((CHUNK, LANES), lambda i: (chunks - 1 - i, DT_AT // LANES)),
            pl.BlockSpec((CHUNK, INNER), back),
            pl.BlockSpec((CHUNK, INNER), back),
            pl.BlockSpec((1, NSTATE, INNER), lambda i: (chunks - 1 - i, 0, 0)),
        ]
        + [whole(v) for v in (dt_bias, a_log, skip, gather)]
        + [ANY],
        out_specs=(
            pl.BlockSpec((CHUNK, MIXW), back),
            pl.BlockSpec((CHUNK, LANES), lambda i: (chunks - 1 - i, DT_AT // LANES)),
            pl.BlockSpec((8, LANES), lambda i: (0, 0)),
            pl.BlockSpec((1, INNER), lambda i: (0, 0)),
        ),
        scratch_shapes=[pltpu.VMEM((NSTATE, INNER), F32)] + [pltpu.VMEM((CHUNK, INNER), F32)] * 2,
        compiler_params=params(),
        input_output_aliases={9: 1},
        cost_estimate=cost(35),
    )(mixed, projected, ssm, grad, states, dt_bias, a_log, skip, gather, held)


ROWS_AT_ONCE = 128
CONV_TILES = 2


def down(v, before, by):
    moved = pltpu.roll(v, by, 0)
    row = lax.broadcasted_iota(jnp.int32, (8, LANES), 0)
    top = jnp.where(row < by, pltpu.roll(before, by, 0), moved[:8])
    return jnp.concatenate([top, moved[8:]], axis=0)


def up(v, after, by):
    rows = v.shape[0]
    moved = pltpu.roll(v, rows - by, 0)
    row = lax.broadcasted_iota(jnp.int32, (8, LANES), 0)
    end = jnp.where(row < 8 - by, moved[rows - 8 :], pltpu.roll(after, 8 - by, 0))
    return jnp.concatenate([moved[: rows - 8], end], axis=0)


def conv_terms(conv_in, at, cols):
    rows = conv_in[at : at + ROWS_AT_ONCE, cols]
    before = conv_in[at - 8 : at, cols] if at else jnp.zeros((8, LANES), F32)
    return [down(rows, before, KCONV - 1 - k) for k in range(KCONV - 1)] + [rows]


def conv_sum(terms, weight, bias):
    total = bias + terms[KCONV - 1] * weight[KCONV - 1 : KCONV]
    for k in range(KCONV - 1):
        total = total + terms[k] * weight[k : k + 1]
    return total


def conv_forward_kernel(conv_in, weight, bias, mixed):
    for tile in range(CONV_TILES):
        cols = slice(tile * LANES, (tile + 1) * LANES)
        w, b = weight[:, cols], bias[:, cols]
        for at in range(0, conv_in.shape[0], ROWS_AT_ONCE):
            mixed[at : at + ROWS_AT_ONCE, cols] = silu(conv_sum(conv_terms(conv_in, at, cols), w, b))


def conv_forward(projected, weight, bias):
    length = projected.shape[0]
    width = CONV_TILES * LANES
    return pl.pallas_call(
        conv_forward_kernel,
        grid=(CONVCH // width,),
        out_shape=shape((length, CONVCH), F32),
        in_specs=[
            pl.BlockSpec((length, width), lambda i: (0, INNER // width + i)),
            pl.BlockSpec((KCONV, width), lambda i: (0, i)),
            pl.BlockSpec((1, width), lambda i: (0, i)),
        ],
        out_specs=pl.BlockSpec((length, width), lambda i: (0, i)),
        compiler_params=params(),
        cost_estimate=cost(10),
    )(projected, weight, bias)


def conv_backward_kernel(conv_in, grad, weight, bias, held, out, sums):
    length = conv_in.shape[0]
    for tile in range(CONV_TILES):
        cols = slice(tile * LANES, (tile + 1) * LANES)
        w, b = weight[:, cols], bias[:, cols]
        totals = [jnp.zeros((1, LANES), F32)] * (KCONV + 1)
        after = jnp.zeros((8, LANES), F32)
        for at in range(length - ROWS_AT_ONCE, -1, -ROWS_AT_ONCE):
            terms = conv_terms(conv_in, at, cols)
            value = conv_sum(terms, w, b)
            sig = sigmoid(value)
            g = grad[at : at + ROWS_AT_ONCE, cols] * (sig * (1.0 + value * (1.0 - sig)))
            for k in range(KCONV):
                totals[k] = totals[k] + jnp.sum(g * terms[k], axis=0, keepdims=True)
            totals[KCONV] = totals[KCONV] + jnp.sum(g, axis=0, keepdims=True)
            total = g * w[KCONV - 1 : KCONV]
            for k in range(KCONV - 1):
                total = total + up(g, after, KCONV - 1 - k) * w[k : k + 1]
            after = g[:8]
            out[at : at + ROWS_AT_ONCE, cols] = total.astype(BF16)
        for k in range(KCONV + 1):
            sums[k : k + 1, cols] = totals[k]


def conv_backward(projected, grad_mixed, weight, bias, held):
    length = projected.shape[0]
    width = CONV_TILES * LANES
    return pl.pallas_call(
        conv_backward_kernel,
        grid=(CONVCH // width,),
        out_shape=(shape(held.shape, BF16), shape((8, CONVCH), F32)),
        in_specs=[
            pl.BlockSpec((length, width), lambda i: (0, INNER // width + i)),
            pl.BlockSpec((length, width), lambda i: (0, i)),
            pl.BlockSpec((KCONV, width), lambda i: (0, i)),
            pl.BlockSpec((1, width), lambda i: (0, i)),
            ANY,
        ],
        out_specs=(
            pl.BlockSpec((length, width), lambda i: (0, INNER // width + i)),
            pl.BlockSpec((8, width), lambda i: (0, i)),
        ),
        input_output_aliases={4: 0},
        compiler_params=params(),
        cost_estimate=cost(12),
    )(projected, grad_mixed, weight, bias, held)


def middle_kernel(
    limit, mixed_out, w_out, tokens, teacher, mask, ssm, gate, gain,
    block_out, grad_result, grad_branch, grad_ssm, grad_gate, error, gain_sums,
):
    step = pl.program_id(0)

    @pl.when(step == 0)
    def _():
        error[...] = jnp.zeros_like(error)
        gain_sums[...] = jnp.zeros_like(gain_sums)

    rows = tokens.shape[0]
    result = tokens[...].astype(F32) + dot(mixed_out[...], w_out[...])
    position = step * rows + lax.broadcasted_iota(jnp.int32, (rows, 1), 0)
    valid = (position < limit[0]).astype(F32)
    weight = valid * mask[:, 0:1]
    block_out[...] = (result * valid).astype(BF16)
    misfit = result - teacher[...].astype(F32)
    pulled = 2.0 * weight * misfit
    grad_result[...] = pulled
    error[...] += jnp.sum(0.5 * pulled * misfit, axis=0, keepdims=True)
    low = pulled.astype(BF16)
    grad_branch[...] = low
    grad_mixed = dot(low, w_out[...], NT)
    g = gate[...]
    sig = sigmoid(g)
    act = g * sig
    inner = ssm[...]
    gated = inner * act
    rho = lax.rsqrt(jnp.mean(gated * gated, axis=1, keepdims=True) + NORM_EPS)
    unit = gated * rho
    gain_sums[...] += jnp.sum(unit * grad_mixed, axis=0, keepdims=True)
    grad_unit = grad_mixed * gain[...]
    share = jnp.mean(grad_unit * unit, axis=1, keepdims=True)
    grad_gated = rho * (grad_unit - unit * share)
    grad_ssm[...] = grad_gated * act
    grad_gate[...] = (grad_gated * inner * (sig * (1.0 + g * (1.0 - sig)))).astype(BF16)


def middle(limit, mixed_out, w_out, tokens, teacher, mask, ssm, projected, gain):
    length = tokens.shape[0]
    rows = 256
    by_row = lambda width: pl.BlockSpec((rows, width), lambda i: (i, 0))
    whole = lambda v: pl.BlockSpec(v.shape, lambda i: (0,) * v.ndim)
    return pl.pallas_call(
        middle_kernel,
        grid=(length // rows,),
        out_shape=(
            shape((length, D), BF16),
            shape((length, D), F32),
            shape((length, D), BF16),
            shape((length, INNER), F32),
            shape((length, WIDE), BF16),
            shape((1, D), F32),
            shape((1, INNER), F32),
        ),
        in_specs=[
            SMEM,
            by_row(INNER),
            whole(w_out),
            by_row(D),
            by_row(D),
            by_row(LANES),
            by_row(INNER),
            by_row(INNER),
            whole(gain),
        ],
        out_specs=(
            by_row(D),
            by_row(D),
            by_row(D),
            by_row(INNER),
            by_row(INNER),
            pl.BlockSpec((1, D), lambda i: (0, 0)),
            pl.BlockSpec((1, INNER), lambda i: (0, 0)),
        ),
        compiler_params=params(),
        cost_estimate=cost(25),
    )(limit, mixed_out, w_out, tokens, teacher, mask, ssm, projected, gain)


def input_kernel(grad_low, w_in, tokens, norm_gain, grad_result, out, sums):
    @pl.when(pl.program_id(0) == 0)
    def _():
        sums[...] = jnp.zeros_like(sums)

    x = tokens[...].astype(F32)
    inverse = lax.rsqrt(jnp.mean(x * x, axis=1, keepdims=True) + NORM_EPS)
    unit = x * inverse
    grad_hidden = dot(grad_low[...], w_in[...], NT)
    sums[...] += jnp.sum(grad_hidden * unit, axis=0, keepdims=True)
    pulled = grad_hidden * norm_gain[...]
    share = jnp.mean(pulled * unit, axis=1, keepdims=True)
    out[...] = grad_result[...] + inverse * (pulled - unit * share)


def input_backward(grad_low, w_in, tokens, norm_gain, grad_result):
    length = tokens.shape[0]
    rows = 256
    by_row = lambda width: pl.BlockSpec((rows, width), lambda i: (i, 0))
    whole = lambda v: pl.BlockSpec(v.shape, lambda i: (0,) * v.ndim)
    return pl.pallas_call(
        input_kernel,
        grid=(length // rows,),
        out_shape=(shape((length, D), F32), shape((1, D), F32)),
        in_specs=[by_row(WIDE), whole(w_in), by_row(D), whole(norm_gain), by_row(D)],
        out_specs=(by_row(D), pl.BlockSpec((1, D), lambda i: (0, 0))),
        compiler_params=params(),
        cost_estimate=cost(15),
    )(grad_low, w_in, tokens, norm_gain, grad_result)


def vector_kernel(tail, conv_sums, sums, skip_sums, norm_sums, gate_sums, gather, out, taps):
    tiles = CONVCH // LANES
    out[...] = jnp.zeros_like(out)
    out[0:TAIL_ROWS, :] = tail[...]
    for k in range(KCONV):
        for i in range(tiles):
            taps[k * 16 + i : k * 16 + i + 1, :] = conv_sums[k : k + 1, i * LANES : (i + 1) * LANES]
    row = lax.broadcasted_iota(jnp.int32, (LANES, LANES), 0)
    col = lax.broadcasted_iota(jnp.int32, (LANES, LANES), 1)
    per_tile = LANES // KCONV

    def exact(v, chosen):
        high = v.astype(BF16)
        rest = v - high.astype(F32)
        middle = rest.astype(BF16)
        low = (rest - middle.astype(F32)).astype(BF16)
        return dot(high, chosen) + (dot(middle, chosen) + dot(low, chosen))

    for q in range(KCONV):
        total = jnp.zeros((tiles, LANES), F32)
        for k in range(KCONV):
            chosen = (col == KCONV * (row % per_tile) + k) & (row // per_tile == q)
            total = total + exact(taps[k * 16 : k * 16 + tiles, :], chosen.astype(BF16))
        out[pl.ds(TAIL_ROWS + q, tiles, stride=KCONV), :] = total
    bias_at = TAIL_ROWS + tiles * KCONV
    for i in range(tiles):
        out[bias_at + i : bias_at + i + 1, :] = conv_sums[KCONV : KCONV + 1, i * LANES : (i + 1) * LANES]
    lane = lax.broadcasted_iota(jnp.int32, (1, LANES), 1)
    skip = exact(jnp.broadcast_to(skip_sums[...], (8, INNER)), gather[...])[0:1, :]
    parts = [sums[0:1, :], sums[1:2, :], skip]
    parts = [jnp.where(lane < HEADS, v, 0.0) for v in parts]
    before = parts[0] + pltpu.roll(parts[1], HEADS, 1) + pltpu.roll(parts[2], 2 * HEADS, 1)
    at, shift = bias_at + tiles, 3 * HEADS
    for source in (norm_sums, gate_sums):
        for j in range(source.shape[1] // LANES):
            here = pltpu.roll(source[:, j * LANES : (j + 1) * LANES], shift, 1)
            out[at : at + 1, :] = jnp.where(lane < shift, before, here)
            before = here
            at += 1
    out[at : at + 1, :] = jnp.where(lane < shift, before, 0.0)


def pack_vectors(tail, conv_sums, sums, skip_sums, norm_sums, gate_sums, gather):
    return pl.pallas_call(
        vector_kernel,
        out_shape=shape(((NBLK - MID1) * BROWS, LANES), F32),
        in_specs=[VMEM] * 7,
        out_specs=VMEM,
        scratch_shapes=[pltpu.VMEM((KCONV * 16, LANES), F32)],
        compiler_params=params(),
    )(tail, conv_sums, sums, skip_sums, norm_sums, gate_sums, gather)


def body(tokens, teacher, lengths, loss_mask, owners, master, first_moment, second_moment):
    capacity = master.shape[0]
    dp, fsdp = lax.axis_size("dp"), lax.axis_size("fsdp")
    devices = dp * fsdp
    me = lax.axis_index(AXES).astype(jnp.int32)
    x_first, y_first, z_first = step_orders(dp, fsdp)
    tie = lambda *values: lax.optimization_barrier(values)

    sent = send_blocks(owners, master, devices, me)
    at_home = lax.all_to_all(sent, AXES, 0, 0, tiled=True)
    owners, tokens, loss_mask, _ = tie(owners, tokens, loss_mask, sent)
    plan = make_plan(owners, capacity, devices, me)
    n0, n1 = plan["slots"]
    streams = cut(n0, (x_first, y_first, z_first))
    table = stream_places(plan["home"], plan["slot"], me, streams, devices)
    table0 = jnp.concatenate([table[:MID0], table[MID1:]])
    table1 = (place_of(plan["home"] ^ me, x_first) * n1 + plan["slot"])[MID0:MID1]
    u0, u1 = plan["unit_slots"]
    unit_streams = cut(u0, (x_first, y_first, x_first, y_first, z_first))
    unit_table = stream_places(plan["unit_home"], plan["unit_slot"], me, unit_streams, devices)
    unit_table = unit_table[:MID0].reshape(-1)
    unit_table1 = place_of(plan["unit_home"] ^ me, x_first) * (u1 + 1) + plan["unit_slot"]
    unit_table1 = unit_table1[MID0:MID1].reshape(-1)
    inputs, target = tokens[0], teacher[0]
    mask = jnp.broadcast_to(loss_mask[0].astype(F32)[:, None], (inputs.shape[0], LANES))
    wide_in = inputs.astype(F32)
    inverse = lax.rsqrt(jnp.mean(wide_in * wide_in, axis=-1, keepdims=True) + NORM_EPS)
    position = jnp.arange(inputs.shape[0], dtype=jnp.int32)
    counted = jnp.sum(jnp.where(position < lengths[0], loss_mask[0], 0)).astype(F32)
    limit = jnp.broadcast_to((END_OUT - plan["row_block"] * PBLOCK)[:, None], (capacity, LANES))
    used = jnp.broadcast_to(plan["row_used"].astype(jnp.int32)[:, None], (capacity, LANES))
    received = jnp.concatenate(plan["received"])
    (at_home, table0, table1, unit_table, unit_table1, inverse, counted, received, back_table,
     row_from) = tie(
        at_home, table0, table1, unit_table, unit_table1, inverse, counted, received,
        plan["back"], plan["row_from"],
    )
    sizes = [size for _, size, _ in streams] + [n1]
    *mine, mine1 = pick_blocks(received, at_home, sizes)
    parts = []
    for values, (_, _, order) in zip(mine, streams):
        parts += gather_steps(values, order)
    *parts, mine1, mask, limit, used = tie(*parts, mine1, mask, limit, used)
    late_steps = x_first[:0:-1]
    for step in late_steps[: max(len(late_steps) - 4, 0)]:
        mine1 = doubled(mine1, step)
    late_steps = late_steps[-4:]
    input_weight, head, tail, conv_weight, conv_bias, heads, skip, norm_gain, gate_gain = unpack_in(
        table0, parts
    )
    if late_steps[-4:-3]:
        mine1, input_weight = tie(doubled(mine1, late_steps[-4]), input_weight)
    dt_bias, a_log = heads[0:1], heads[1:2]
    gather = heads_gather()
    hidden = (wide_in * inverse * norm_gain).astype(BF16)
    projected = dot(hidden, input_weight)
    if late_steps[-3:-2]:
        mine1, projected = tie(doubled(mine1, late_steps[-3]), projected)
    mixed = conv_forward(projected, conv_weight, conv_bias)
    if late_steps[-2:-1]:
        mine1, mixed = tie(doubled(mine1, late_steps[-2]), mixed)
    ssm, mixed_out, states = scan_forward(mixed, projected, dt_bias, a_log, skip, gate_gain)
    if late_steps:
        mine1, mixed_out = tie(doubled(mine1, late_steps[-1]), mixed_out)
    output_weight = unpack_out(table1, mine1, exchange(mine1, x_first[0]), head, tail)
    block_out, grad_result, grad_branch, grad_ssm, grad_low, errors, grad_gate = middle(
        lengths, mixed_out, output_weight, inputs, target, mask, ssm, projected, gate_gain
    )
    local = jnp.concatenate([errors.reshape(-1, LANES), jnp.broadcast_to(counted, (2, LANES))])
    grad_weight_out = dot(mixed_out, grad_branch, (((0,), (0,)), ((), ())))
    keep1, send1, head, tail = pack_out(unit_table1, grad_weight_out, local, devices, u1 + 1)
    sum1 = keep1 + exchange(send1, x_first[0])
    grad_ssm, sum1 = tie(grad_ssm, sum1)
    sum1 = reduce_step(sum1, x_first[1])
    grad_mixed, grad_low, sums, skip_sums = scan_backward(
        mixed, projected, ssm, grad_ssm, states, dt_bias, a_log, skip, gather, grad_low
    )
    grad_mixed, sum1 = tie(grad_mixed, sum1)
    if len(x_first) > 3:
        sum1 = reduce_step(sum1, x_first[2])
    grad_low, conv_sums = conv_backward(projected, grad_mixed, conv_weight, conv_bias, grad_low)
    grad_low, sum1 = tie(grad_low, sum1)
    halves = []
    for _, size, _ in unit_streams:
        halves += [devices * size // 2] * 2
    packed = list(pack_in(unit_table, hidden, grad_low, head, halves))
    reduced = [
        packed[2 * i] + exchange(packed[2 * i + 1], order[0])
        for i, (_, _, order) in enumerate(unit_streams)
    ]
    *reduced, grad_low, conv_sums, tail = tie(*reduced, grad_low, conv_sums, tail)
    reduced = [reduce_step(v, order[1]) for v, (_, _, order) in zip(reduced, unit_streams)]
    input_grad, norm_sums = input_backward(grad_low, input_weight, inputs, norm_gain, grad_result)
    grad_vec = pack_vectors(tail, conv_sums, sums, skip_sums, norm_sums, grad_gate, gather)
    grad_vec = grad_vec.reshape((NBLK - MID1) * UNITS, UNIT, LANES)
    *reduced, sum1, grad_vec, input_grad = tie(*reduced, sum1, grad_vec, input_grad)
    for k in range(2, len(x_first) - 1):
        reduced[0], grad_vec = reduce_step(reduced[0], x_first[k], grad_vec)
        for i in range(1, len(reduced)):
            reduced[i] = reduce_step(reduced[i], unit_streams[i][2][k])
    for step in x_first[3:-1]:
        sum1 = reduce_step(sum1, step)
    ends = []
    for i, values in enumerate(reduced + [sum1]):
        half = values.shape[0] // 2
        given, step = values[half:], (unit_streams[i][2] if i < len(reduced) else x_first)[-1]
        if i == 0:
            got = exchange(jnp.concatenate([given, grad_vec]), step)
            grad_vec = grad_vec + got[half:]
            got = got[:half]
        else:
            got = exchange(given, step)
        ends += [values[:half], got]
    back = units_to_owners(back_table, ends)
    back, grad_vec = tie(back, grad_vec)
    got = lax.all_to_all(back, AXES, 0, 0, tiled=True)
    for step in x_first[:2]:
        grad_vec = grad_vec + exchange(grad_vec, step)
    local_sums = ends[-2][u1] + ends[-1][u1]
    error_sum = jnp.sum(local_sums[: D // LANES])
    divisor = local_sums[D // LANES, 0] * D
    new_first, new_second, new_master = adam(
        row_from,
        divisor,
        got,
        grad_vec,
        limit,
        used,
        master,
        first_moment,
        second_moment,
    )
    mean_loss = error_sum / divisor
    return (block_out[None], input_grad[None], mean_loss, new_first, new_second, new_master)


def solution(mesh):
    return jax.shard_map(
        body,
        mesh=mesh,
        in_specs=(
            P(AXES, None, None),
            P(AXES, None, None),
            P(AXES),
            P(AXES, None),
            P(),
            P(AXES, None),
            P(AXES, None),
            P(AXES, None),
        ),
        out_specs=(
            P(AXES, None, None),
            P(AXES, None, None),
            P(),
            P(AXES, None),
            P(AXES, None),
            P(AXES, None),
        ),
        check_vma=False,
    )
```

```python
from functools import partial

import jax
import jax.numpy as jnp
import numpy as np
from jax import lax
from jax.experimental import pallas as pl
from jax.experimental.pallas import tpu as pltpu
from jax.sharding import PartitionSpec as P

D = 768
INNER = 1536
NSTATE = 128
HEADDIM = 64
KCONV = 4
SCAN_LEN = 256
PBLOCK = 4096
STEP = 10
HEADS = 24
CONVCH = 1792
PROJ = 3352
PTOT = 3765320
NBLK = 920

LANES = 128
BROWS = PBLOCK // LANES
UNIT = 8
UNITS = BROWS // UNIT
END_IN = D * PROJ
END_OUT = END_IN + INNER * D
MID0 = -(-END_IN // PBLOCK)
MID1 = END_OUT // PBLOCK
N0 = MID0 + NBLK - MID1
N1 = MID1 - MID0
F0_ROWS = N0 * BROWS
IN_ROWS = END_IN // LANES
HEAD_ROWS = MID0 * BROWS - IN_ROWS
TAIL_ROWS = (END_OUT - MID1 * PBLOCK) // LANES
OUT_ROWS = INNER * D // LANES
VEC_ROWS = (NBLK - MID1) * BROWS - TAIL_ROWS
VEC_AT = MID0 * BROWS + TAIL_ROWS
GROUP = 16
GROUPS = D // GROUP
GROUP_ROWS = GROUP * PROJ // LANES
COL_TILES = -(-PROJ // LANES)
WIDE = COL_TILES * LANES
OUT_TILES = D // LANES

NORM_EPS = 1e-05
ADAM_EPS = 1e-08
BETA_ONE = 0.9
BETA_TWO = 0.999
MATRIX_RATE = 0.03
VECTOR_RATE = 0.2
WEIGHT_DECAY = 0.1
PRECISE = lax.Precision.HIGHEST
AXES = ("dp", "fsdp")
VMEM_LIMIT = 60 * 1024 * 1024


def bits_of(count):
    return count.bit_length() - 1


def step_orders(dp, fsdp):
    wide = [("dp", i) for i in range(bits_of(dp))]
    narrow = [("fsdp", i) for i in range(bits_of(fsdp))]
    first = wide[:2] + narrow + wide[2:]
    second = wide[:1] + narrow + wide[1:]
    third = wide[:1] + wide[2:] + wide[1:2] + narrow
    return first, second, third


def cut(total, orders):
    base, more = divmod(total, len(orders))
    streams, at = [], 0
    for i, order in enumerate(orders):
        size = base + (i < more)
        if size:
            streams.append((at, size, order))
        at += size
    return streams


def exchange(values, step):
    axis, bit = step
    size = lax.axis_size(axis)
    return lax.ppermute(values, axis, [(i, i ^ (1 << bit)) for i in range(size)])


def place_of(relative, order):
    shift_of = {"dp": bits_of(lax.axis_size("fsdp")), "fsdp": 0}
    place = jnp.zeros_like(relative)
    for axis, bit in order:
        place = place * 2 + ((relative >> (shift_of[axis] + bit)) & 1)
    return place


def class_counts(owners, devices):
    block = jnp.arange(NBLK, dtype=jnp.int32)
    mid = ((block >= MID0) & (block < MID1))[None, :]
    device = jnp.arange(devices, dtype=jnp.int32)
    below = owners[None, :] < device[:, None]
    owned = owners[None, :] == device[:, None]

    def total(mask):
        return jnp.sum(mask.astype(jnp.int32), axis=1)

    start = (total(below & ~mid), total(below & mid))
    count = (total(owned & ~mid), total(owned & mid))
    return start, count, total(owned & (block < MID0)[None, :])


def my_counts(owners, me):
    block = jnp.arange(NBLK, dtype=jnp.int32)
    mid = (block >= MID0) & (block < MID1)
    below, owned = owners < me, owners == me
    total = lambda mask: jnp.sum(mask.astype(jnp.int32))
    start = (total(below & ~mid), total(below & mid))
    count = (total(owned & ~mid), total(owned & mid))
    return start, count, total(owned & (block < MID0))


def pair_lanes(capacity, devices):
    return 2 + max(capacity - 2, 0) // devices


def make_plan(owners, capacity, devices, me):
    block = jnp.arange(NBLK, dtype=jnp.int32)
    mid = (block >= MID0) & (block < MID1)
    same = mid[:, None] == mid[None, :]
    before = (owners[None, :] < owners[:, None]) | (
        (owners[None, :] == owners[:, None]) & (block[None, :] < block[:, None])
    )
    order_in_class = jnp.sum((same & before).astype(jnp.int32), axis=1)
    home, slot = order_in_class % devices, order_in_class // devices
    device = jnp.arange(devices, dtype=jnp.int32)
    start, count, _ = class_counts(owners, devices)
    my_start, my_count, my_early = my_counts(owners, me)
    pair = pair_lanes(capacity, devices)

    slots = (-(-N0 // devices), -(-N1 // devices))

    def received(kind):
        wanted = me + devices * jnp.arange(slots[kind], dtype=jnp.int32)
        ends = start[kind] + count[kind]
        owner = jnp.sum((ends[None, :] <= wanted[:, None]).astype(jnp.int32), axis=1)
        owner = jnp.minimum(owner, devices - 1)
        base = jnp.sum(jnp.where(device[None, :] == owner[:, None], start[kind][None, :], 0), axis=1)
        turn = jnp.clip((wanted - base) // devices, 0, pair - 1)
        return owner * pair + (turn if kind == 0 else pair - 1 - turn)

    back_pair = (UNITS * capacity + 2 * (devices - 1)) // devices
    unit = UNITS * order_in_class[:, None] + jnp.arange(UNITS, dtype=jnp.int32)[None, :]
    unit_home, unit_slot = unit % devices, unit // devices
    unit_slots = (-(-UNITS * N0 // devices), -(-UNITS * N1 // devices))
    lane = jnp.arange(back_pair, dtype=jnp.int32)

    def units_back(kind):
        turn = lane if kind == 0 else back_pair - 1 - lane
        first = UNITS * start[kind][:, None]
        k = (me - first) % devices + turn[None, :] * devices
        return k < UNITS * count[kind][:, None], (first + k) // devices

    valid0, slot0 = units_back(0)
    valid1, slot1 = units_back(1)
    back = jnp.where(valid0, slot0, jnp.where(valid1, unit_slots[0] + slot1, 0)).reshape(-1)

    row = jnp.arange(capacity, dtype=jnp.int32)
    is_mid = (row >= my_early) & (row < my_early + my_count[1])
    k = jnp.where(is_mid, row - my_early, jnp.where(row < my_early, row, row - my_count[1]))
    first = UNITS * jnp.where(is_mid, my_start[1], my_start[0])
    k = UNITS * k[:, None] + jnp.arange(UNITS, dtype=jnp.int32)[None, :]
    turn = k // devices
    row_from = ((first[:, None] + k) % devices) * back_pair + jnp.where(
        is_mid[:, None], back_pair - 1 - turn, turn
    )
    row_used = row < my_count[0] + my_count[1]
    mine = (owners == me)[None, :]
    rank = jnp.sum((mine & (block[None, :] < block[:, None])).astype(jnp.int32), axis=1)
    row_block = jnp.sum(
        jnp.where(mine & (rank[None, :] == row[:, None]), block[None, :], 0), axis=1
    )
    late = devices * back_pair + UNITS * (row_block - MID1)
    late = late[:, None] + jnp.arange(UNITS, dtype=jnp.int32)[None, :]
    row_from = jnp.where((row_block >= MID1)[:, None], late, row_from)
    row_from = jnp.where(row_used[:, None], row_from, 0).reshape(-1)
    return dict(
        home=home, slot=slot, slots=slots,
        received=(received(0), received(1)), unit_home=unit_home, unit_slot=unit_slot,
        unit_slots=unit_slots, back=back, row_from=row_from,
        row_used=row_used, row_block=row_block,
    )


def stream_places(home, slot, me, streams, devices):
    relative = home ^ me
    place = jnp.zeros_like(slot)
    for begin, size, order in streams:
        inside = (slot >= begin) & (slot < begin + size)
        at = devices * begin + place_of(relative, order) * size + slot - begin
        place = jnp.where(inside, at, place)
    return place


def cost(microseconds):
    return pl.CostEstimate(
        flops=int(microseconds * 1e9), bytes_accessed=int(microseconds * 3e6), transcendentals=0
    )


ANY = pl.BlockSpec(memory_space=pl.ANY)
VMEM = pl.BlockSpec(memory_space=pltpu.VMEM)
SMEM = pl.BlockSpec(memory_space=pltpu.SMEM)


def params(**extra):
    return pltpu.CompilerParams(vmem_limit_bytes=VMEM_LIMIT, **extra)


def shape(dims, dtype):
    return jax.ShapeDtypeStruct(dims, dtype)


def send_kernel(my_index, owners, master, out, flat, *, devices):
    capacity = master.shape[0]
    me = my_index[0]
    for j in range(BROWS):
        flat[pl.ds(j, capacity, stride=BROWS), :] = master[:, j * LANES : (j + 1) * LANES]
    held = owners[...]
    block = lax.broadcasted_iota(jnp.int32, held.shape, 0) * LANES + lax.broadcasted_iota(
        jnp.int32, held.shape, 1
    )
    mid = (block >= MID0) & (block < MID1)
    below, owned = held < me, held == me

    def total(mask):
        return jnp.sum(jnp.where(mask, 1.0, 0.0)).astype(jnp.int32)

    start0, start1 = total(below & ~mid), total(below & mid)
    count0, count1 = total(owned & ~mid), total(owned & mid)
    early = total(owned & (block < MID0))
    pair = out.shape[0] // devices
    positive = devices * NBLK

    def step(home, carry):
        for s in range(pair):
            k0 = lax.rem(home - start0 + positive, devices) + s * devices
            k1 = lax.rem(home - start1 + positive, devices) + (pair - 1 - s) * devices
            row0 = jnp.where(k0 < early, k0, k0 + count1)
            row = jnp.where(k0 < count0, row0, jnp.where(k1 < count1, early + k1, 0))
            rows = pl.ds(pl.multiple_of(row * BROWS, BROWS), BROWS)
            out[home * pair + s] = flat[rows, :].astype(out.dtype)
        return carry

    lax.fori_loop(0, devices, step, 0)


def send_blocks(owners, master, devices, me):
    rows = -(-NBLK // (8 * LANES)) * 8
    held = jnp.pad(owners, (0, rows * LANES - NBLK), constant_values=1 << 20).reshape(rows, LANES)
    count = devices * pair_lanes(master.shape[0], devices)
    return pl.pallas_call(
        partial(send_kernel, devices=devices),
        out_shape=shape((count, BROWS, LANES), jnp.bfloat16),
        in_specs=[SMEM, VMEM, VMEM],
        out_specs=VMEM,
        scratch_shapes=[pltpu.VMEM((master.shape[0] * BROWS, LANES), jnp.float32)],
        compiler_params=params(),
    )(me.reshape(1), held, master)


def pick_kernel(table, source, *outs):
    at = 0
    for out in outs:

        def step(i, carry, out=out, at=at):
            out[i] = source[table[at + i]]
            return carry

        lax.fori_loop(0, out.shape[0], step, 0)
        at += out.shape[0]


def pick_blocks(table, source, sizes):
    return pl.pallas_call(
        pick_kernel,
        out_shape=tuple(shape((n,) + source.shape[1:], source.dtype) for n in sizes),
        in_specs=[SMEM, VMEM],
        out_specs=(VMEM,) * len(sizes),
        compiler_params=params(),
    )(table, source)


def back_kernel(table, *refs):
    sources, (out, held) = refs[:-2], refs[-2:]
    at = 0
    for i in range(0, len(sources), 2):
        n = sources[i].shape[0]
        held[at : at + n] = sources[i][...] + sources[i + 1][...]
        at += n

    def step(i, carry):
        for u in range(8):
            out[i * 8 + u] = held[table[i * 8 + u]]
        return carry

    total = out.shape[0]
    lax.fori_loop(0, total // 8, step, 0)


def units_to_owners(table, sources):
    return pl.pallas_call(
        back_kernel,
        out_shape=shape((table.shape[0], UNIT, LANES), jnp.float32),
        in_specs=[SMEM] + [VMEM] * len(sources),
        out_specs=VMEM,
        scratch_shapes=[
            pltpu.VMEM((sum(s.shape[0] for s in sources[::2]), UNIT, LANES), jnp.float32)
        ],
        compiler_params=params(),
    )(table, *sources)


def row_start(rho):
    return (PROJ * rho) // LANES, (PROJ * rho) % LANES


def copy_all(pairs, sem):
    copies = [pltpu.make_async_copy(a, b, sem.at[i]) for i, (a, b) in enumerate(pairs)]
    for c in copies:
        c.start()
    for c in copies:
        c.wait()


def spread_blocks(table, held, flat, count, first_row):
    def one(i):
        at = pl.multiple_of(first_row + i * BROWS, 16)
        flat[pl.ds(at, BROWS), :] = held[table[i]].astype(jnp.float32)

    def step(i, carry):
        for u in range(4):
            one(i * 4 + u)
        return carry

    lax.fori_loop(0, count // 4, step, 0)
    for i in range(count // 4 * 4, count):
        one(i)


def unpack_vectors(flat, conv_weight, conv_bias, heads, skip, norm_gain, gate_gain):
    bf16, f32 = jnp.bfloat16, jnp.float32
    tiles = CONVCH // LANES
    row = lax.broadcasted_iota(jnp.int32, (LANES, LANES), 0)
    col = lax.broadcasted_iota(jnp.int32, (LANES, LANES), 1)
    per_tile = LANES // KCONV
    for k in range(KCONV):
        total = jnp.zeros((tiles, LANES), f32)
        for q in range(KCONV):
            rows = flat[pl.ds(VEC_AT + q, tiles, stride=KCONV), :].astype(bf16)
            chosen = (row == KCONV * (col % per_tile) + k) & (col // per_tile == q)
            total = total + jnp.dot(rows, chosen.astype(bf16), preferred_element_type=f32)
        for i in range(tiles):
            conv_weight[k : k + 1, i * LANES : (i + 1) * LANES] = total[i : i + 1, :]
    bias_at = VEC_AT + tiles * KCONV
    for i in range(tiles):
        conv_bias[:, i * LANES : (i + 1) * LANES] = flat[bias_at + i : bias_at + i + 1, :]
    at = bias_at + tiles
    lane = lax.broadcasted_iota(jnp.int32, (8, LANES), 1)
    first = flat[at : at + 8, :]
    three = []
    for i in range(3):
        moved = pltpu.roll(first, LANES - i * HEADS, 1) if i else first
        three.append(jnp.where(lane < HEADS, moved, 0.0))
        heads[i : i + 1, :] = three[i][0:1, :]
    for j in range(INNER // LANES):
        h = lax.broadcasted_iota(jnp.int32, (LANES, LANES), 0)
        c = lax.broadcasted_iota(jnp.int32, (LANES, LANES), 1) + j * LANES
        spread = (h == c // HEADDIM).astype(bf16)
        wide = jnp.dot(three[2].astype(bf16), spread, preferred_element_type=f32)
        skip[:, j * LANES : (j + 1) * LANES] = wide[0:1, :]
    shift = 3 * HEADS
    for out, begin, width in ((norm_gain, at, D), (gate_gain, at + D // LANES, INNER)):
        for j in range(width // LANES):
            x = pltpu.roll(flat[begin + j : begin + j + 1, :], LANES - shift, 1)
            y = pltpu.roll(flat[begin + j + 1 : begin + j + 2, :], LANES - shift, 1)
            out[:, j * LANES : (j + 1) * LANES] = jnp.where(lane[0:1] < LANES - shift, x, y)


def unpack_in_kernel(table, *refs):
    parts, (w_in, head, tail, *vectors), (held, flat, tile, sem) = refs[:-13], refs[-13:-4], refs[-4:]
    pairs, at = [], 0
    for part in parts:
        pairs.append((part, held.at[pl.ds(at, part.shape[0])]))
        at += part.shape[0]
    copy_all(pairs, sem)
    spread_blocks(table, held, flat, N0, 0)
    head[...] = flat[IN_ROWS : IN_ROWS + HEAD_ROWS, :]
    tail[...] = flat[MID0 * BROWS : MID0 * BROWS + TAIL_ROWS, :]
    unpack_vectors(flat, *vectors)
    lane = lax.broadcasted_iota(jnp.int32, (GROUPS, LANES), 1)

    def columns(j):
        for rho in range(GROUP):
            c, s = row_start(rho)
            x = flat[pl.ds(c + j, GROUPS, stride=GROUP_ROWS), :]
            if s:
                y = flat[pl.ds(c + j + 1, GROUPS, stride=GROUP_ROWS), :]
                x = jnp.where(
                    lane < LANES - s,
                    pltpu.roll(x, LANES - s, 1),
                    pltpu.roll(y, LANES - s, 1),
                )
            tile[pl.ds(rho, GROUPS, stride=GROUP), :] = x

    def step(j, carry):
        columns(j)
        w_in[:, pl.ds(pl.multiple_of(j * LANES, LANES), LANES)] = tile[...].astype(jnp.bfloat16)
        return carry

    lax.fori_loop(0, COL_TILES - 1, step, 0)
    columns(COL_TILES - 1)
    last = (COL_TILES - 1) * LANES
    inside = lax.broadcasted_iota(jnp.int32, (D, LANES), 1) < PROJ - last
    w_in[:, last:] = jnp.where(inside, tile[...], 0.0).astype(jnp.bfloat16)


def unpack_in(table, parts):
    held = sum(part.shape[0] for part in parts)
    return pl.pallas_call(
        unpack_in_kernel,
        out_shape=(
            shape((D, WIDE), jnp.bfloat16),
            shape((HEAD_ROWS, LANES), jnp.float32),
            shape((TAIL_ROWS, LANES), jnp.float32),
            shape((KCONV, CONVCH), jnp.float32),
            shape((1, CONVCH), jnp.float32),
            shape((8, LANES), jnp.float32),
            shape((1, INNER), jnp.float32),
            shape((1, D), jnp.float32),
            shape((1, INNER), jnp.float32),
        ),
        in_specs=[SMEM] + [ANY] * len(parts),
        out_specs=(VMEM,) * 9,
        scratch_shapes=[
            pltpu.VMEM((held, BROWS, LANES), jnp.bfloat16),
            pltpu.VMEM((F0_ROWS, LANES), jnp.float32),
            pltpu.VMEM((D, LANES), jnp.float32),
            pltpu.SemaphoreType.DMA((len(parts),)),
        ],
        compiler_params=params(),
        cost_estimate=cost(16),
    )(table, *parts)


def unpack_out_kernel(table, own, got, head, tail, w_out, flat, held, sem):
    half = own.shape[0]
    copy_all([(own, held.at[pl.ds(0, half)]), (got, held.at[pl.ds(half, half)])], sem)
    flat[0:HEAD_ROWS, :] = head[...]
    flat[OUT_ROWS - TAIL_ROWS : OUT_ROWS, :] = tail[...]
    spread_blocks(table, held, flat, N1, HEAD_ROWS)
    rows = 128

    def step(i, carry):
        at = pl.multiple_of(i * rows, rows)
        for j in range(OUT_TILES):
            x = flat[pl.ds(at * OUT_TILES + j, rows, stride=OUT_TILES), :]
            w_out[pl.ds(at, rows), j * LANES : (j + 1) * LANES] = x.astype(jnp.bfloat16)
        return carry

    lax.fori_loop(0, INNER // rows, step, 0)


def unpack_out(table, own, got, head, tail):
    return pl.pallas_call(
        unpack_out_kernel,
        out_shape=shape((INNER, D), jnp.bfloat16),
        in_specs=[SMEM, ANY, ANY, VMEM, VMEM],
        out_specs=VMEM,
        scratch_shapes=[
            pltpu.VMEM((OUT_ROWS, LANES), jnp.float32),
            pltpu.VMEM((2 * own.shape[0], BROWS, LANES), jnp.bfloat16),
            pltpu.SemaphoreType.DMA((2,)),
        ],
        compiler_params=params(),
    )(table, own, got, head, tail)


def permute_units(table, flat, count, first_row, staged):
    many = 16

    def step(i, carry):
        for u in range(many):
            at = pl.multiple_of(first_row + (i * many + u) * UNIT, UNIT)
            staged[table[i * many + u]] = flat[pl.ds(at, UNIT), :]
        return carry

    lax.fori_loop(0, count // many, step, 0)
    for i in range(count // many * many, count):
        staged[table[i]] = flat[first_row + i * UNIT : first_row + (i + 1) * UNIT, :]


def pack_in_kernel(table, hidden, grad, head, *refs):
    outs, (turned, tiles, flat, staged, sem) = refs[:-5], refs[-5:]
    turned[...] = hidden[...].T
    lane = lax.broadcasted_iota(jnp.int32, (GROUPS, LANES), 1)

    def product(p, count):
        at = p * 2 * LANES
        at = at if isinstance(at, int) else pl.multiple_of(at, 2 * LANES)
        return jnp.dot(
            turned[...], grad[:, pl.ds(at, count * LANES)], preferred_element_type=jnp.float32
        )

    def put(p, value):
        for k in range(value.shape[1] // LANES):
            at = (p * 2 + k) * D
            at = at if isinstance(at, int) else pl.multiple_of(at, D)
            tiles[pl.ds(at, D), :] = value[:, k * LANES : (k + 1) * LANES]

    def load(rho, j):
        return tiles[pl.ds(j * D + rho, GROUPS, stride=GROUP), :]

    def whole(rho, i):
        first = -(-PROJ * rho // LANES)
        col0 = first * LANES - PROJ * rho
        x = load(rho, i)
        if col0:
            x = jnp.where(
                lane < LANES - col0,
                pltpu.roll(x, LANES - col0, 1),
                pltpu.roll(load(rho, i + 1), LANES - col0, 1),
            )
        flat[pl.ds(first + i, GROUPS, stride=GROUP_ROWS), :] = x

    put(0, product(0, 2))
    put(1, product(1, 2))
    pairs = COL_TILES // 2

    def step(p, carry):
        for i in range(2):
            for rho in range(GROUP):
                whole(rho, p * 2 + i)
        put(p + 2, product(p + 2, 2))
        return carry

    lax.fori_loop(0, pairs - 2, step, 0)
    put(pairs, product(pairs, COL_TILES % 2))
    for rho in range(GROUP):
        first = -(-PROJ * rho // LANES)
        col0 = first * LANES - PROJ * rho
        full = (PROJ - col0) // LANES
        for i in range((pairs - 2) * 2, full):
            whole(rho, i)
        left = PROJ - col0 - full * LANES
        if left:
            begin = col0 + full * LANES
            j, s = begin // LANES, begin % LANES
            x = pltpu.roll(load(rho, j), LANES - s, 1) if s else load(rho, j)
            if s + left > LANES:
                x = jnp.where(lane < LANES - s, x, pltpu.roll(load(rho, j + 1), LANES - s, 1))
            y = pltpu.roll(load(rho + 1, 0), left, 1)
            flat[pl.ds(first + full, GROUPS, stride=GROUP_ROWS), :] = jnp.where(lane < left, x, y)
    flat[IN_ROWS : IN_ROWS + HEAD_ROWS, :] = head[...]
    permute_units(table, flat, MID0 * UNITS, 0, staged)
    copies, at = [], 0
    for out in outs:
        copies.append((staged.at[pl.ds(at, out.shape[0])], out))
        at += out.shape[0]
    copy_all(copies, sem)


def pack_in(table, hidden, grad, head, sizes):
    return pl.pallas_call(
        pack_in_kernel,
        out_shape=tuple(shape((n, UNIT, LANES), jnp.float32) for n in sizes),
        in_specs=[SMEM, VMEM, VMEM, VMEM],
        out_specs=(ANY,) * len(sizes),
        scratch_shapes=[
            pltpu.VMEM((D, hidden.shape[0]), jnp.bfloat16),
            pltpu.VMEM((COL_TILES * D, LANES), jnp.float32),
            pltpu.VMEM((MID0 * BROWS, LANES), jnp.float32),
            pltpu.VMEM((sum(sizes), UNIT, LANES), jnp.float32),
            pltpu.SemaphoreType.DMA((len(sizes),)),
        ],
        compiler_params=params(),
        cost_estimate=cost(20),
    )(table, hidden, grad, head)


def pack_out_kernel(
    table, mixed_out, grad, local, keep, send, head, tail, turned, flat, out, sem, *, slots
):
    rows = 256

    def step(i, carry):
        at = pl.multiple_of(i * rows, rows)
        turned[...] = mixed_out[:, pl.ds(at, rows)].T
        product = jnp.dot(turned[...], grad[...], preferred_element_type=jnp.float32)
        for j in range(OUT_TILES):
            flat[pl.ds(at * OUT_TILES + j, rows, stride=OUT_TILES), :] = product[
                :, j * LANES : (j + 1) * LANES
            ]
        return carry

    lax.fori_loop(0, INNER // rows, step, 0)
    head[...] = flat[0:HEAD_ROWS, :]
    tail[...] = flat[OUT_ROWS - TAIL_ROWS : OUT_ROWS, :]
    permute_units(table, flat, N1 * UNITS, HEAD_ROWS, out)

    def add_local(i, carry):
        out[i * slots + slots - 1] = local[...]
        return carry

    lax.fori_loop(0, out.shape[0] // slots, add_local, 0)
    half = keep.shape[0]
    copy_all([(out.at[pl.ds(0, half)], keep), (out.at[pl.ds(half, half)], send)], sem)


def pack_out(table, mixed_out, grad, local, devices, slots):
    return pl.pallas_call(
        partial(pack_out_kernel, slots=slots),
        out_shape=(
            shape((devices * slots // 2, UNIT, LANES), jnp.float32),
            shape((devices * slots // 2, UNIT, LANES), jnp.float32),
            shape((HEAD_ROWS, LANES), jnp.float32),
            shape((TAIL_ROWS, LANES), jnp.float32),
        ),
        in_specs=[SMEM, VMEM, VMEM, VMEM],
        out_specs=(ANY, ANY, VMEM, VMEM),
        scratch_shapes=[
            pltpu.VMEM((256, mixed_out.shape[0]), jnp.bfloat16),
            pltpu.VMEM((OUT_ROWS, LANES), jnp.float32),
            pltpu.VMEM((devices * slots, UNIT, LANES), jnp.float32),
            pltpu.SemaphoreType.DMA((2,)),
        ],
        compiler_params=params(),
    )(table, mixed_out, grad, local)


def adam_kernel(table, scale, got, late, limit, used, master, first, second, o_first, o_second, o_master, flat, held):
    capacity = master.shape[0]

    def step(i, carry):
        for u in range(UNITS):
            at = table[i * UNITS + u]
            rows = pl.ds(pl.multiple_of(i * BROWS + u * UNIT, UNIT), UNIT)
            flat[rows, :] = held[at]
        return carry

    held[0 : got.shape[0]] = got[...]
    held[got.shape[0] :] = late[...]
    lax.fori_loop(0, capacity, step, 0)
    lane = lax.broadcasted_iota(jnp.int32, (capacity, LANES), 1)
    divisor = scale[0]
    for j in range(BROWS):
        cols = slice(j * LANES, (j + 1) * LANES)
        grad = jnp.where(used[...] > 0, flat[pl.ds(j, capacity, stride=BROWS), :], 0.0) / divisor
        matrix = lane + j * LANES < limit[...]
        weights = master[:, cols]
        new_first = BETA_ONE * first[:, cols] + (1.0 - BETA_ONE) * grad
        new_second = BETA_TWO * second[:, cols] + (1.0 - BETA_TWO) * grad * grad
        normal = (
            new_first
            / (1.0 - BETA_ONE**STEP)
            / (jnp.sqrt(new_second / (1.0 - BETA_TWO**STEP)) + ADAM_EPS)
        )
        rate = jnp.where(matrix, MATRIX_RATE, VECTOR_RATE)
        decay = jnp.where(matrix, WEIGHT_DECAY, 0.0)
        o_first[:, cols] = new_first
        o_second[:, cols] = new_second
        o_master[:, cols] = weights - rate * (normal + decay * weights)


def adam(table, divisor, got, late, limit, used, master, first, second):
    capacity = master.shape[0]
    return pl.pallas_call(
        adam_kernel,
        out_shape=(shape(master.shape, jnp.float32),) * 3,
        in_specs=[SMEM, SMEM] + [VMEM] * 7,
        out_specs=(VMEM,) * 3,
        scratch_shapes=[
            pltpu.VMEM((capacity * BROWS, LANES), jnp.float32),
            pltpu.VMEM((got.shape[0] + late.shape[0], UNIT, LANES), jnp.float32),
        ],
        compiler_params=params(),
    )(table, divisor.reshape(1), got, late, limit, used, master, first, second)


def doubled(values, step):
    return jnp.concatenate([values, exchange(values, step)], axis=0)


def gather_steps(values, order):
    for step in order[:0:-1]:
        values = doubled(values, step)
    return values, exchange(values, order[0])


def reduce_step(kept, got, step, extra=None):
    half = kept.shape[0] // 2
    given = kept[half:] + got[half:]
    if extra is None:
        return kept[:half] + got[:half], exchange(given, step)
    arrived = exchange(jnp.concatenate([given, extra]), step)
    return kept[:half] + got[:half], arrived[:half], extra + arrived[half:]


CHUNK = 128
PAIRS = HEADS // 2
MIXW = INNER + 2 * NSTATE
DT_AT = INNER + CONVCH
F32 = jnp.float32
BF16 = jnp.bfloat16
NN = (((1,), (0,)), ((), ()))
NT = (((1,), (1,)), ((), ()))


def dot(a, b, dims=NN):
    return lax.dot_general(a, b, dims, preferred_element_type=F32)


def split(v):
    high = v.astype(BF16)
    return high, (v - high.astype(F32)).astype(BF16)


def dot3(a, b, dims=NN):
    ah, al = a
    bh, bl = b
    return dot(ah, bh, dims) + (dot(ah, bl, dims) + dot(al, bh, dims))


def heads_gather():
    return jnp.asarray(np.repeat(np.eye(HEADS, LANES, dtype=np.float32), HEADDIM, axis=0), BF16)


def three_parts(v):
    high = v.astype(BF16).astype(F32)
    rest = v - high
    middle = rest.astype(BF16).astype(F32)
    low = rest - middle
    return (high + pltpu.roll(middle, 32, 1) + pltpu.roll(low, 64, 1)).astype(BF16)


def triangle_sum(tri, v):
    parts = dot(tri, three_parts(v))
    lane = lax.broadcasted_iota(jnp.int32, parts.shape, 1)
    total = parts + pltpu.roll(parts, LANES - 32, 1) + pltpu.roll(parts, LANES - 64, 1)
    return jnp.where(lane < HEADS, total, 0.0)


def chunk_decays(dt, dt_bias, a_log):
    lane = lax.broadcasted_iota(jnp.int32, (CHUNK, LANES), 1)
    row = lax.broadcasted_iota(jnp.int32, (CHUNK, LANES), 0)
    shifted = dt + dt_bias
    delta = jnp.where(
        lane < HEADS, jnp.maximum(shifted, 0.0) + jnp.log1p(jnp.exp(-jnp.abs(shifted))), 0.0
    )
    rate = -jnp.exp(a_log)
    lower = (row >= lane).astype(BF16)
    cum = triangle_sum(lower, delta * rate)
    last = cum[CHUNK - 1 : CHUNK, :]
    return shifted, delta, rate, cum, last


def pair_mask():
    lane = lax.broadcasted_iota(jnp.int32, (CHUNK, LANES), 1)
    low = (lane < HEADDIM).astype(F32)
    return low.astype(BF16), (1.0 - low).astype(BF16)


QUADS = HEADS // 4
QWIDTH = 4 * HEADDIM


def sigmoid(v):
    return 0.5 * jnp.tanh(0.5 * v) + 0.5


def silu(v):
    return v * sigmoid(v)


def side_by_side(v):
    high, low = split(v)
    return jnp.concatenate([high, low], axis=1), high


def dot_parts(a, b):
    ahl, ah = a
    bh, bl = b
    return dot(ahl, jnp.concatenate([bh, bh], axis=0)) + dot(ah, bl)


def dot_turned(a, b):
    ah, al = a
    bh, bl = b
    both = dot(ah, jnp.concatenate([bh, bl], axis=0), NT)
    n = bh.shape[0]
    return both[:, :n] + both[:, n:] + dot(al, bh, NT)


def widen(delta, cum, quad):
    lane = lax.broadcasted_iota(jnp.int32, (CHUNK, LANES), 1)
    over = lambda v, h: jnp.broadcast_to(v[:, h : h + 1], (CHUNK, LANES))
    first = 4 * quad
    columns = [over(cum, first + k) for k in range(4)]
    rates = [over(delta, first + k) for k in range(4)]
    pair = lambda vs: jnp.concatenate(
        [jnp.where(lane < HEADDIM, vs[0], vs[1]), jnp.where(lane < HEADDIM, vs[2], vs[3])], axis=1
    )
    return pair(rates), pair(columns), columns


def pair_rows(parts, j, low, high):
    cols = slice(j * LANES, (j + 1) * LANES)
    return [jnp.concatenate([p[:, cols] * low, p[:, cols] * high], axis=0) for p in parts]


def scan_chunk(mixed, dt, dt_bias, a_log, skip, state, put):
    _, delta, _, cum, last = chunk_decays(dt, dt_bias, a_log)
    lane = lax.broadcasted_iota(jnp.int32, (CHUNK, LANES), 1)
    row = lax.broadcasted_iota(jnp.int32, (CHUNK, LANES), 0)
    bias = jnp.where(row >= lane, 0.0, -1e30)
    cum_t = cum.T
    inputs_b = mixed[:, INNER : INNER + NSTATE]
    readout = mixed[:, INNER + NSTATE :]
    affinity = dot3(split(readout), split(inputs_b), NT)
    readout_parts = side_by_side(readout)
    b_parts = side_by_side(inputs_b.T)
    low, high = pair_mask()
    for quad in range(QUADS):
        cols = slice(quad * QWIDTH, (quad + 1) * QWIDTH)
        wide_delta, wide_cum, columns = widen(delta, cum, quad)
        values = mixed[:, cols]
        scaled = values * wide_delta
        parts = split(scaled)
        outs = []
        for j in range(2):
            right_h, right_l = pair_rows(parts, j, low, high)
            left = []
            for k in range(2):
                h = 4 * quad + 2 * j + k
                within = jnp.exp(columns[2 * j + k] - cum_t[h : h + 1, :] + bias)
                left.append(split(affinity * within))
            left_h = jnp.concatenate([left[0][0], left[1][0]], axis=1)
            left_l = jnp.concatenate([left[0][1], left[1][1]], axis=1)
            both = dot(left_h, jnp.concatenate([right_h, right_l], axis=1))
            outs.append(both[:, :LANES] + both[:, LANES:] + dot(left_l, right_h))
        carried = state[:, cols]
        grown = jnp.exp(wide_cum)
        out = jnp.concatenate(outs, axis=1) + dot_parts(readout_parts, split(carried)) * grown
        tail = jnp.exp(wide_cum[CHUNK - 1 :] - wide_cum)
        state[:, cols] = carried * grown[CHUNK - 1 :] + dot_parts(b_parts, split(scaled * tail))
        put(quad, out + skip[:, cols] * values)


FORWARD_ROWS = 2 * CHUNK


def forward_kernel(
    tokens, w_in, norm_gain, conv_weight, conv_bias, dt_bias, a_log, skip, gain,
    hidden, projected, mixed, ssm, mixed_out, states, state, before,
):
    @pl.when(pl.program_id(0) == 0)
    def _():
        state[...] = jnp.zeros_like(state)
        before[...] = jnp.zeros_like(before)

    x = tokens[...].astype(F32)
    inverse = lax.rsqrt(jnp.mean(x * x, axis=1, keepdims=True) + NORM_EPS)
    h = (x * inverse * norm_gain[...]).astype(BF16)
    hidden[...] = h
    projected[:, DT_AT:] = dot(h, w_in[:, DT_AT:])
    wide = 2 * LANES
    for tile in range(CONVCH // wide):
        at = tile * wide
        product = dot(h, w_in[:, INNER + at : INNER + at + wide])
        projected[:, INNER + at : INNER + at + wide] = product
        for half in range(2):
            cols = slice(at + half * LANES, at + (half + 1) * LANES)
            rows = product[:, half * LANES : (half + 1) * LANES]
            earlier = before[:, cols]
            terms = [down(rows, earlier, KCONV - 1 - k) for k in range(KCONV - 1)] + [rows]
            before[:, cols] = rows[FORWARD_ROWS - 8 :]
            mixed[:, cols] = silu(conv_sum(terms, conv_weight[:, cols], conv_bias[:, cols]))
    for tile in range(INNER // wide):
        cols = slice(tile * wide, (tile + 1) * wide)
        projected[:, cols] = dot(h, w_in[:, cols])
    for sub in range(FORWARD_ROWS // CHUNK):
        rows = slice(sub * CHUNK, (sub + 1) * CHUNK)
        states[sub] = state[...]
        squares = [jnp.zeros((CHUNK, LANES), F32)]

        def put(quad, out, rows=rows, squares=squares):
            cols = slice(quad * QWIDTH, (quad + 1) * QWIDTH)
            ssm[rows, cols] = out
            gated = out * silu(projected[rows, cols])
            first, second = gated[:, :LANES], gated[:, LANES:]
            squares[0] = squares[0] + first * first + second * second

        scan_chunk(
            mixed[rows, :], projected[rows, DT_AT:], dt_bias[...], a_log[...], skip, state, put
        )
        rho = lax.rsqrt(jnp.sum(squares[0], axis=1, keepdims=True) * (1.0 / INNER) + NORM_EPS)
        for j in range(PAIRS):
            cols = slice(j * LANES, (j + 1) * LANES)
            gated = ssm[rows, cols] * silu(projected[rows, cols])
            mixed_out[rows, cols] = (gated * rho * gain[:, cols]).astype(BF16)


def forward(tokens, w_in, norm_gain, conv_weight, conv_bias, dt_bias, a_log, skip, gain):
    length = tokens.shape[0]
    by_row = lambda width: pl.BlockSpec((FORWARD_ROWS, width), lambda i: (i, 0))
    whole = lambda v: pl.BlockSpec(v.shape, lambda i: (0,) * v.ndim)
    per_step = FORWARD_ROWS // CHUNK
    return pl.pallas_call(
        forward_kernel,
        grid=(length // FORWARD_ROWS,),
        out_shape=(
            shape((length, D), BF16),
            shape((length, WIDE), F32),
            shape((length, MIXW), F32),
            shape((length, INNER), F32),
            shape((length, INNER), BF16),
            shape((length // CHUNK, NSTATE, INNER), F32),
        ),
        in_specs=[by_row(D)]
        + [
            whole(v)
            for v in (w_in, norm_gain, conv_weight, conv_bias, dt_bias, a_log, skip, gain)
        ],
        out_specs=(
            by_row(D),
            by_row(WIDE),
            by_row(MIXW),
            by_row(INNER),
            by_row(INNER),
            pl.BlockSpec((per_step, NSTATE, INNER), lambda i: (i, 0, 0)),
        ),
        scratch_shapes=[pltpu.VMEM((NSTATE, INNER), F32), pltpu.VMEM((8, MIXW), F32)],
        compiler_params=params(),
        cost_estimate=cost(33),
    )(tokens, w_in, norm_gain, conv_weight, conv_bias, dt_bias, a_log, skip, gain)


def scan_backward_kernel(
    mixed, dt, ssm, grad, states, dt_bias, a_log, skip, gather, held,
    grad_mixed, grad_dt, sums, skip_sums, grad_state, left, right,
):
    @pl.when(pl.program_id(0) == 0)
    def _():
        grad_state[...] = jnp.zeros_like(grad_state)
        sums[...] = jnp.zeros_like(sums)
        skip_sums[...] = jnp.zeros_like(skip_sums)

    shifted, delta, rate, cum, last = chunk_decays(dt[...], dt_bias[...], a_log[...])
    lane = lax.broadcasted_iota(jnp.int32, (CHUNK, LANES), 1)
    row = lax.broadcasted_iota(jnp.int32, (CHUNK, LANES), 0)
    bias = jnp.where(lane >= row, 0.0, -1e30)
    heads = lane < HEADS
    cum_t = cum.T
    inputs_b = mixed[:, INNER : INNER + NSTATE]
    readout = mixed[:, INNER + NSTATE :]
    b_parts, c_parts = split(inputs_b), split(readout)
    b_wide = side_by_side(inputs_b)
    c_turned = side_by_side(readout.T)
    affinity = dot3(b_parts, c_parts, NT)
    low, high = pair_mask()
    grad_affinity = jnp.zeros((CHUNK, CHUNK), F32)
    grad_b = jnp.zeros((CHUNK, NSTATE), F32)
    grad_c = jnp.zeros((CHUNK, NSTATE), F32)
    last_row = lax.broadcasted_iota(jnp.int32, (CHUNK, QWIDTH), 0) == CHUNK - 1
    for quad in range(QUADS):
        cols = slice(quad * QWIDTH, (quad + 1) * QWIDTH)
        wide_delta, wide_cum, columns = widen(delta, cum, quad)
        grown = jnp.exp(wide_cum)
        tail = jnp.exp(wide_cum[CHUNK - 1 :] - wide_cum)
        end = grown[CHUNK - 1 :]
        values = mixed[:, cols]
        pulled = grad[:, cols]
        scaled = values * wide_delta
        x_parts, p_parts = split(scaled), split(pulled)
        outs = []
        for j in range(2):
            half = slice(j * LANES, (j + 1) * LANES)
            xh, xl = x_parts[0][:, half], x_parts[1][:, half]
            right_h, right_l = pair_rows(p_parts, j, low, high)
            pull = dot(
                jnp.concatenate([xh, xl], axis=1),
                jnp.concatenate([right_h, right_h], axis=1),
                NT,
            ) + dot(xh, right_l, NT)
            kernels = []
            for k in range(2):
                h = 4 * quad + 2 * j + k
                within = jnp.exp(cum_t[h : h + 1, :] - columns[2 * j + k] + bias)
                kernels.append(split(affinity * within))
                grad_affinity = grad_affinity + within * pull[:, k * CHUNK : (k + 1) * CHUNK]
            kernel_h = jnp.concatenate([kernels[0][0], kernels[1][0]], axis=1)
            kernel_l = jnp.concatenate([kernels[0][1], kernels[1][1]], axis=1)
            both = dot(kernel_h, jnp.concatenate([right_h, right_l], axis=1))
            outs.append(both[:, :LANES] + both[:, LANES:] + dot(kernel_l, right_h))
        late = grad_state[:, cols]
        late_parts = split(late)
        early = states[0, :, cols]
        from_state = dot_parts(b_wide, late_parts) * tail
        grad_scaled = jnp.concatenate(outs, axis=1) + from_state
        pulled_cum = split(pulled * grown)
        grad_c = grad_c + dot_turned(pulled_cum, split(early))
        grad_b = grad_b + dot_turned(split(scaled * tail), late_parts)
        grad_state[:, cols] = late * end + dot_parts(c_turned, pulled_cum)
        grad_mixed[:, cols] = grad_scaled * wide_delta + skip[:, cols] * pulled
        skip_sums[:, cols] += jnp.sum(pulled * values, axis=0, keepdims=True)
        left[:, cols] = grad_scaled * values
        inner = pulled * (ssm[:, cols] - skip[:, cols] * values) - scaled * grad_scaled
        extra = jnp.sum(scaled * from_state, axis=0, keepdims=True) + end * jnp.sum(
            late * early, axis=0, keepdims=True
        )
        right[:, cols] = inner + jnp.where(last_row, extra, 0.0)
    ga_parts = split(grad_affinity)
    grad_mixed[:, INNER : INNER + NSTATE] = grad_b + dot3(ga_parts, c_parts)
    grad_mixed[:, INNER + NSTATE :] = grad_c + dot3(split(grad_affinity.T), b_parts)

    def by_head(v):
        high, low = split(v)
        g = gather[...]
        return dot(high, g) + dot(low, g)

    direct = by_head(left[...])
    grad_cum = by_head(right[...])
    upper = (lane >= row).astype(BF16)
    after = triangle_sum(upper, grad_cum)
    grad_delta = direct + rate * after
    grad_raw = jnp.where(heads, grad_delta * sigmoid(shifted), 0.0)
    grad_dt[...] = grad_raw.astype(BF16)
    sums[0:1, :] += jnp.sum(grad_raw, axis=0, keepdims=True)
    sums[1:2, :] += rate * jnp.sum(delta * after, axis=0, keepdims=True)


def scan_backward(mixed, projected, ssm, grad, states, dt_bias, a_log, skip, gather, held):
    length = mixed.shape[0]
    chunks = length // CHUNK
    whole = lambda v: pl.BlockSpec(v.shape, lambda i: (0,) * v.ndim)
    back = lambda i: (chunks - 1 - i, 0)
    return pl.pallas_call(
        scan_backward_kernel,
        grid=(chunks,),
        out_shape=(
            shape((length, MIXW), F32),
            shape(held.shape, BF16),
            shape((8, LANES), F32),
            shape((1, INNER), F32),
        ),
        in_specs=[
            pl.BlockSpec((CHUNK, MIXW), back),
            pl.BlockSpec((CHUNK, LANES), lambda i: (chunks - 1 - i, DT_AT // LANES)),
            pl.BlockSpec((CHUNK, INNER), back),
            pl.BlockSpec((CHUNK, INNER), back),
            pl.BlockSpec((1, NSTATE, INNER), lambda i: (chunks - 1 - i, 0, 0)),
        ]
        + [whole(v) for v in (dt_bias, a_log, skip, gather)]
        + [ANY],
        out_specs=(
            pl.BlockSpec((CHUNK, MIXW), back),
            pl.BlockSpec((CHUNK, LANES), lambda i: (chunks - 1 - i, DT_AT // LANES)),
            pl.BlockSpec((8, LANES), lambda i: (0, 0)),
            pl.BlockSpec((1, INNER), lambda i: (0, 0)),
        ),
        scratch_shapes=[pltpu.VMEM((NSTATE, INNER), F32)] + [pltpu.VMEM((CHUNK, INNER), F32)] * 2,
        compiler_params=params(),
        input_output_aliases={9: 1},
        cost_estimate=cost(35),
    )(mixed, projected, ssm, grad, states, dt_bias, a_log, skip, gather, held)


ROWS_AT_ONCE = 128
CONV_TILES = 2


def down(v, before, by):
    moved = pltpu.roll(v, by, 0)
    row = lax.broadcasted_iota(jnp.int32, (8, LANES), 0)
    top = jnp.where(row < by, pltpu.roll(before, by, 0), moved[:8])
    return jnp.concatenate([top, moved[8:]], axis=0)


def up(v, after, by):
    rows = v.shape[0]
    moved = pltpu.roll(v, rows - by, 0)
    row = lax.broadcasted_iota(jnp.int32, (8, LANES), 0)
    end = jnp.where(row < 8 - by, moved[rows - 8 :], pltpu.roll(after, 8 - by, 0))
    return jnp.concatenate([moved[: rows - 8], end], axis=0)


def conv_terms(conv_in, at, cols):
    rows = conv_in[at : at + ROWS_AT_ONCE, cols]
    before = conv_in[at - 8 : at, cols] if at else jnp.zeros((8, LANES), F32)
    return [down(rows, before, KCONV - 1 - k) for k in range(KCONV - 1)] + [rows]


def conv_sum(terms, weight, bias):
    total = bias + terms[KCONV - 1] * weight[KCONV - 1 : KCONV]
    for k in range(KCONV - 1):
        total = total + terms[k] * weight[k : k + 1]
    return total


def conv_backward_kernel(conv_in, grad, weight, bias, held, out, sums):
    length = conv_in.shape[0]
    for tile in range(CONV_TILES):
        cols = slice(tile * LANES, (tile + 1) * LANES)
        w, b = weight[:, cols], bias[:, cols]
        totals = [jnp.zeros((1, LANES), F32)] * (KCONV + 1)
        after = jnp.zeros((8, LANES), F32)
        for at in range(length - ROWS_AT_ONCE, -1, -ROWS_AT_ONCE):
            terms = conv_terms(conv_in, at, cols)
            value = conv_sum(terms, w, b)
            sig = sigmoid(value)
            g = grad[at : at + ROWS_AT_ONCE, cols] * (sig * (1.0 + value * (1.0 - sig)))
            for k in range(KCONV):
                totals[k] = totals[k] + jnp.sum(g * terms[k], axis=0, keepdims=True)
            totals[KCONV] = totals[KCONV] + jnp.sum(g, axis=0, keepdims=True)
            total = g * w[KCONV - 1 : KCONV]
            for k in range(KCONV - 1):
                total = total + up(g, after, KCONV - 1 - k) * w[k : k + 1]
            after = g[:8]
            out[at : at + ROWS_AT_ONCE, cols] = total.astype(BF16)
        for k in range(KCONV + 1):
            sums[k : k + 1, cols] = totals[k]


def conv_backward(projected, grad_mixed, weight, bias, held):
    length = projected.shape[0]
    width = CONV_TILES * LANES
    return pl.pallas_call(
        conv_backward_kernel,
        grid=(CONVCH // width,),
        out_shape=(shape(held.shape, BF16), shape((8, CONVCH), F32)),
        in_specs=[
            pl.BlockSpec((length, width), lambda i: (0, INNER // width + i)),
            pl.BlockSpec((length, width), lambda i: (0, i)),
            pl.BlockSpec((KCONV, width), lambda i: (0, i)),
            pl.BlockSpec((1, width), lambda i: (0, i)),
            ANY,
        ],
        out_specs=(
            pl.BlockSpec((length, width), lambda i: (0, INNER // width + i)),
            pl.BlockSpec((8, width), lambda i: (0, i)),
        ),
        input_output_aliases={4: 0},
        compiler_params=params(),
        cost_estimate=cost(12),
    )(projected, grad_mixed, weight, bias, held)


def middle_kernel(
    limit, mixed_out, w_out, tokens, teacher, mask, ssm, gate, gain,
    block_out, grad_result, grad_branch, grad_ssm, grad_gate, error, gain_sums,
):
    step = pl.program_id(0)

    @pl.when(step == 0)
    def _():
        error[...] = jnp.zeros_like(error)
        gain_sums[...] = jnp.zeros_like(gain_sums)

    rows = tokens.shape[0]
    result = tokens[...].astype(F32) + dot(mixed_out[...], w_out[...])
    position = step * rows + lax.broadcasted_iota(jnp.int32, (rows, 1), 0)
    valid = (position < limit[0]).astype(F32)
    weight = valid * mask[:, 0:1]
    block_out[...] = (result * valid).astype(BF16)
    misfit = result - teacher[...].astype(F32)
    pulled = 2.0 * weight * misfit
    grad_result[...] = pulled
    error[...] += jnp.sum(0.5 * pulled * misfit, axis=0, keepdims=True)
    low = pulled.astype(BF16)
    grad_branch[...] = low
    grad_mixed = dot(low, w_out[...], NT)
    g = gate[...]
    sig = sigmoid(g)
    act = g * sig
    inner = ssm[...]
    gated = inner * act
    rho = lax.rsqrt(jnp.mean(gated * gated, axis=1, keepdims=True) + NORM_EPS)
    unit = gated * rho
    gain_sums[...] += jnp.sum(unit * grad_mixed, axis=0, keepdims=True)
    grad_unit = grad_mixed * gain[...]
    share = jnp.mean(grad_unit * unit, axis=1, keepdims=True)
    grad_gated = rho * (grad_unit - unit * share)
    grad_ssm[...] = grad_gated * act
    grad_gate[...] = (grad_gated * inner * (sig * (1.0 + g * (1.0 - sig)))).astype(BF16)


def middle(limit, mixed_out, w_out, tokens, teacher, mask, ssm, projected, gain):
    length = tokens.shape[0]
    rows = 256
    by_row = lambda width: pl.BlockSpec((rows, width), lambda i: (i, 0))
    whole = lambda v: pl.BlockSpec(v.shape, lambda i: (0,) * v.ndim)
    return pl.pallas_call(
        middle_kernel,
        grid=(length // rows,),
        out_shape=(
            shape((length, D), BF16),
            shape((length, D), F32),
            shape((length, D), BF16),
            shape((length, INNER), F32),
            shape((length, WIDE), BF16),
            shape((1, D), F32),
            shape((1, INNER), F32),
        ),
        in_specs=[
            SMEM,
            by_row(INNER),
            whole(w_out),
            by_row(D),
            by_row(D),
            by_row(LANES),
            by_row(INNER),
            by_row(INNER),
            whole(gain),
        ],
        out_specs=(
            by_row(D),
            by_row(D),
            by_row(D),
            by_row(INNER),
            by_row(INNER),
            pl.BlockSpec((1, D), lambda i: (0, 0)),
            pl.BlockSpec((1, INNER), lambda i: (0, 0)),
        ),
        compiler_params=params(),
        cost_estimate=cost(25),
    )(limit, mixed_out, w_out, tokens, teacher, mask, ssm, projected, gain)


def input_kernel(grad_low, w_in, tokens, norm_gain, grad_result, out, sums):
    @pl.when(pl.program_id(0) == 0)
    def _():
        sums[...] = jnp.zeros_like(sums)

    x = tokens[...].astype(F32)
    inverse = lax.rsqrt(jnp.mean(x * x, axis=1, keepdims=True) + NORM_EPS)
    unit = x * inverse
    grad_hidden = dot(grad_low[...], w_in[...], NT)
    sums[...] += jnp.sum(grad_hidden * unit, axis=0, keepdims=True)
    pulled = grad_hidden * norm_gain[...]
    share = jnp.mean(pulled * unit, axis=1, keepdims=True)
    out[...] = grad_result[...] + inverse * (pulled - unit * share)


def input_backward(grad_low, w_in, tokens, norm_gain, grad_result):
    length = tokens.shape[0]
    rows = 256
    by_row = lambda width: pl.BlockSpec((rows, width), lambda i: (i, 0))
    whole = lambda v: pl.BlockSpec(v.shape, lambda i: (0,) * v.ndim)
    return pl.pallas_call(
        input_kernel,
        grid=(length // rows,),
        out_shape=(shape((length, D), F32), shape((1, D), F32)),
        in_specs=[by_row(WIDE), whole(w_in), by_row(D), whole(norm_gain), by_row(D)],
        out_specs=(by_row(D), pl.BlockSpec((1, D), lambda i: (0, 0))),
        compiler_params=params(),
        cost_estimate=cost(15),
    )(grad_low, w_in, tokens, norm_gain, grad_result)


def vector_kernel(tail, conv_sums, sums, skip_sums, norm_sums, gate_sums, gather, out, taps):
    tiles = CONVCH // LANES
    out[...] = jnp.zeros_like(out)
    out[0:TAIL_ROWS, :] = tail[...]
    for k in range(KCONV):
        for i in range(tiles):
            taps[k * 16 + i : k * 16 + i + 1, :] = conv_sums[k : k + 1, i * LANES : (i + 1) * LANES]
    row = lax.broadcasted_iota(jnp.int32, (LANES, LANES), 0)
    col = lax.broadcasted_iota(jnp.int32, (LANES, LANES), 1)
    per_tile = LANES // KCONV

    def exact(v, chosen):
        high = v.astype(BF16)
        rest = v - high.astype(F32)
        middle = rest.astype(BF16)
        low = (rest - middle.astype(F32)).astype(BF16)
        return dot(high, chosen) + (dot(middle, chosen) + dot(low, chosen))

    for q in range(KCONV):
        total = jnp.zeros((tiles, LANES), F32)
        for k in range(KCONV):
            chosen = (col == KCONV * (row % per_tile) + k) & (row // per_tile == q)
            total = total + exact(taps[k * 16 : k * 16 + tiles, :], chosen.astype(BF16))
        out[pl.ds(TAIL_ROWS + q, tiles, stride=KCONV), :] = total
    bias_at = TAIL_ROWS + tiles * KCONV
    for i in range(tiles):
        out[bias_at + i : bias_at + i + 1, :] = conv_sums[KCONV : KCONV + 1, i * LANES : (i + 1) * LANES]
    lane = lax.broadcasted_iota(jnp.int32, (1, LANES), 1)
    skip = exact(jnp.broadcast_to(skip_sums[...], (8, INNER)), gather[...])[0:1, :]
    parts = [sums[0:1, :], sums[1:2, :], skip]
    parts = [jnp.where(lane < HEADS, v, 0.0) for v in parts]
    before = parts[0] + pltpu.roll(parts[1], HEADS, 1) + pltpu.roll(parts[2], 2 * HEADS, 1)
    at, shift = bias_at + tiles, 3 * HEADS
    for source in (norm_sums, gate_sums):
        for j in range(source.shape[1] // LANES):
            here = pltpu.roll(source[:, j * LANES : (j + 1) * LANES], shift, 1)
            out[at : at + 1, :] = jnp.where(lane < shift, before, here)
            before = here
            at += 1
    out[at : at + 1, :] = jnp.where(lane < shift, before, 0.0)


def pack_vectors(tail, conv_sums, sums, skip_sums, norm_sums, gate_sums, gather):
    return pl.pallas_call(
        vector_kernel,
        out_shape=shape(((NBLK - MID1) * BROWS, LANES), F32),
        in_specs=[VMEM] * 7,
        out_specs=VMEM,
        scratch_shapes=[pltpu.VMEM((KCONV * 16, LANES), F32)],
        compiler_params=params(),
    )(tail, conv_sums, sums, skip_sums, norm_sums, gate_sums, gather)


def body(tokens, teacher, lengths, loss_mask, owners, master, first_moment, second_moment):
    capacity = master.shape[0]
    dp, fsdp = lax.axis_size("dp"), lax.axis_size("fsdp")
    devices = dp * fsdp
    me = lax.axis_index(AXES).astype(jnp.int32)
    x_first, y_first, z_first = step_orders(dp, fsdp)
    tie = lambda *values: lax.optimization_barrier(values)

    sent = send_blocks(owners, master, devices, me)
    at_home = lax.all_to_all(sent, AXES, 0, 0, tiled=True)
    owners, tokens, loss_mask, _ = tie(owners, tokens, loss_mask, sent)
    plan = make_plan(owners, capacity, devices, me)
    n0, n1 = plan["slots"]
    streams = cut(n0, (x_first, y_first, z_first))
    table = stream_places(plan["home"], plan["slot"], me, streams, devices)
    table0 = jnp.concatenate([table[:MID0], table[MID1:]])
    table1 = (place_of(plan["home"] ^ me, x_first) * n1 + plan["slot"])[MID0:MID1]
    u0, u1 = plan["unit_slots"]
    unit_streams = cut(u0, (x_first, y_first, x_first, y_first, z_first))
    unit_table = stream_places(plan["unit_home"], plan["unit_slot"], me, unit_streams, devices)
    unit_table = unit_table[:MID0].reshape(-1)
    unit_table1 = place_of(plan["unit_home"] ^ me, x_first) * (u1 + 1) + plan["unit_slot"]
    unit_table1 = unit_table1[MID0:MID1].reshape(-1)
    inputs, target = tokens[0], teacher[0]
    mask = jnp.broadcast_to(loss_mask[0].astype(F32)[:, None], (inputs.shape[0], LANES))
    position = jnp.arange(inputs.shape[0], dtype=jnp.int32)
    counted = jnp.sum(jnp.where(position < lengths[0], loss_mask[0], 0)).astype(F32)
    limit = jnp.broadcast_to((END_OUT - plan["row_block"] * PBLOCK)[:, None], (capacity, LANES))
    used = jnp.broadcast_to(plan["row_used"].astype(jnp.int32)[:, None], (capacity, LANES))
    received = jnp.concatenate(plan["received"])
    (at_home, table0, table1, unit_table, unit_table1, counted, received, back_table,
     row_from) = tie(
        at_home, table0, table1, unit_table, unit_table1, counted, received,
        plan["back"], plan["row_from"],
    )
    sizes = [size for _, size, _ in streams] + [n1]
    *mine, mine1 = pick_blocks(received, at_home, sizes)
    steps1 = x_first[::-1]
    ride = max(len(steps1) - 3, 0)
    for step in steps1[:ride]:
        n = mine[0].shape[0]
        arrived = exchange(jnp.concatenate([mine[0], mine1]), step)
        mine[0] = jnp.concatenate([mine[0], arrived[:n]])
        mine1 = jnp.concatenate([mine1, arrived[n:]])
    parts = []
    for i, (values, (_, _, order)) in enumerate(zip(mine, streams)):
        for step in order[:0:-1][ride if i == 0 else 0 :]:
            values = doubled(values, step)
        parts += [values, exchange(values, order[0])]
    *parts, mine1, mask, limit, used = tie(*parts, mine1, mask, limit, used)
    input_weight, head, tail, conv_weight, conv_bias, heads, skip, norm_gain, gate_gain = unpack_in(
        table0, parts
    )
    for step in steps1[ride:-2]:
        mine1, input_weight = tie(doubled(mine1, step), input_weight)
    dt_bias, a_log = heads[0:1], heads[1:2]
    gather = heads_gather()
    hidden, projected, mixed, ssm, mixed_out, states = forward(
        inputs, input_weight, norm_gain, conv_weight, conv_bias, dt_bias, a_log, skip, gate_gain
    )
    for step in steps1[max(ride, len(steps1) - 2) : -1]:
        mine1, mixed_out = tie(doubled(mine1, step), mixed_out)
    output_weight = unpack_out(table1, mine1, exchange(mine1, x_first[0]), head, tail)
    block_out, grad_result, grad_branch, grad_ssm, grad_low, errors, grad_gate = middle(
        lengths, mixed_out, output_weight, inputs, target, mask, ssm, projected, gate_gain
    )
    local = jnp.concatenate([errors.reshape(-1, LANES), jnp.broadcast_to(counted, (2, LANES))])
    keep1, send1, head, tail = pack_out(
        unit_table1, mixed_out, grad_branch, local, devices, u1 + 1
    )
    got1 = exchange(send1, x_first[0])
    grad_ssm, keep1, got1 = tie(grad_ssm, keep1, got1)
    keep1, got1 = reduce_step(keep1, got1, x_first[1])
    grad_mixed, grad_low, sums, skip_sums = scan_backward(
        mixed, projected, ssm, grad_ssm, states, dt_bias, a_log, skip, gather, grad_low
    )
    grad_mixed, keep1, got1 = tie(grad_mixed, keep1, got1)
    steps1 = x_first[2:]
    for step in steps1[:1]:
        keep1, got1 = reduce_step(keep1, got1, step)
    grad_low, conv_sums = conv_backward(projected, grad_mixed, conv_weight, conv_bias, grad_low)
    grad_low, keep1, got1 = tie(grad_low, keep1, got1)
    for step in steps1[1:2]:
        keep1, got1 = reduce_step(keep1, got1, step)
    halves = []
    for _, size, _ in unit_streams:
        halves += [devices * size // 2] * 2
    packed = list(pack_in(unit_table, hidden, grad_low, head, halves))
    packed[0], keep1, got1 = tie(packed[0], keep1, got1)
    kept = packed[::2]
    got = [exchange(v, order[0]) for v, (_, _, order) in zip(packed[1::2], unit_streams)]
    *got, grad_low, conv_sums, tail = tie(*got, grad_low, conv_sums, tail)
    for i, (_, _, order) in enumerate(unit_streams):
        kept[i], got[i] = reduce_step(kept[i], got[i], order[1])
    for step in steps1[2:3]:
        keep1, got1 = reduce_step(keep1, got1, step)
    input_grad, norm_sums = input_backward(grad_low, input_weight, inputs, norm_gain, grad_result)
    grad_vec = pack_vectors(tail, conv_sums, sums, skip_sums, norm_sums, grad_gate, gather)
    grad_vec = grad_vec.reshape((NBLK - MID1) * UNITS, UNIT, LANES)
    *got, got1, grad_vec, input_grad = tie(*got, got1, grad_vec, input_grad)
    for step in steps1[3:]:
        keep1, got1 = reduce_step(keep1, got1, step)
    for k in range(2, len(x_first)):
        for i, (_, _, order) in enumerate(unit_streams):
            if i == 0:
                kept[i], got[i], grad_vec = reduce_step(kept[i], got[i], order[k], grad_vec)
            else:
                kept[i], got[i] = reduce_step(kept[i], got[i], order[k])
    ends = [v for pair in zip(kept + [keep1], got + [got1]) for v in pair]
    back = units_to_owners(back_table, ends)
    back, grad_vec = tie(back, grad_vec)
    returned = lax.all_to_all(back, AXES, 0, 0, tiled=True)
    for step in x_first[:2]:
        grad_vec = grad_vec + exchange(grad_vec, step)
    local_sums = ends[-2][u1] + ends[-1][u1]
    error_sum = jnp.sum(local_sums[: D // LANES])
    divisor = local_sums[D // LANES, 0] * D
    new_first, new_second, new_master = adam(
        row_from,
        divisor,
        returned,
        grad_vec,
        limit,
        used,
        master,
        first_moment,
        second_moment,
    )
    mean_loss = error_sum / divisor
    return (block_out[None], input_grad[None], mean_loss, new_first, new_second, new_master)


def solution(mesh):
    return jax.shard_map(
        body,
        mesh=mesh,
        in_specs=(
            P(AXES, None, None),
            P(AXES, None, None),
            P(AXES),
            P(AXES, None),
            P(),
            P(AXES, None),
            P(AXES, None),
            P(AXES, None),
        ),
        out_specs=(
            P(AXES, None, None),
            P(AXES, None, None),
            P(),
            P(AXES, None),
            P(AXES, None),
            P(AXES, None),
        ),
        check_vma=False,
    )
```

```python
from functools import partial

import jax
import jax.numpy as jnp
import numpy as np
from jax import lax
from jax.experimental import pallas as pl
from jax.experimental.pallas import tpu as pltpu
from jax.sharding import PartitionSpec as P

D = 768
INNER = 1536
NSTATE = 128
HEADDIM = 64
KCONV = 4
SCAN_LEN = 256
PBLOCK = 4096
STEP = 10
HEADS = 24
CONVCH = 1792
PROJ = 3352
PTOT = 3765320
NBLK = 920

LANES = 128
BROWS = PBLOCK // LANES
UNIT = 8
UNITS = BROWS // UNIT
END_IN = D * PROJ
END_OUT = END_IN + INNER * D
MID0 = -(-END_IN // PBLOCK)
MID1 = END_OUT // PBLOCK
N0 = MID0 + NBLK - MID1
N1 = MID1 - MID0
F0_ROWS = N0 * BROWS
IN_ROWS = END_IN // LANES
HEAD_ROWS = MID0 * BROWS - IN_ROWS
TAIL_ROWS = (END_OUT - MID1 * PBLOCK) // LANES
OUT_ROWS = INNER * D // LANES
VEC_ROWS = (NBLK - MID1) * BROWS - TAIL_ROWS
VEC_AT = MID0 * BROWS + TAIL_ROWS
GROUP = 16
GROUPS = D // GROUP
GROUP_ROWS = GROUP * PROJ // LANES
COL_TILES = -(-PROJ // LANES)
WIDE = COL_TILES * LANES
OUT_TILES = D // LANES

NORM_EPS = 1e-05
ADAM_EPS = 1e-08
BETA_ONE = 0.9
BETA_TWO = 0.999
MATRIX_RATE = 0.03
VECTOR_RATE = 0.2
WEIGHT_DECAY = 0.1
PRECISE = lax.Precision.HIGHEST
AXES = ("dp", "fsdp")
VMEM_LIMIT = 60 * 1024 * 1024


def bits_of(count):
    return count.bit_length() - 1


def step_orders(dp, fsdp):
    wide = [("dp", i) for i in range(bits_of(dp))]
    narrow = [("fsdp", i) for i in range(bits_of(fsdp))]
    first = wide[:2] + narrow + wide[2:]
    second = wide[:1] + narrow + wide[1:]
    third = wide[:1] + wide[2:] + wide[1:2] + narrow
    return first, second, third


def cut(sizes, orders):
    streams, at = [], 0
    for size, order in zip(sizes, orders):
        if size:
            streams.append((at, size, order))
        at += size
    return streams


def even(total, parts):
    return [total // parts + (i < total % parts) for i in range(parts)]


def exchange(values, *steps):
    axes = {axis for axis, _ in steps}
    if len(axes) == 1:
        (axis,) = axes
        mask = sum(1 << bit for _, bit in steps)
        pairs = [(i, i ^ mask) for i in range(lax.axis_size(axis))]
        return lax.ppermute(values, axis, pairs)
    low = bits_of(lax.axis_size("fsdp"))
    mask = sum(1 << (bit + (low if axis == "dp" else 0)) for axis, bit in steps)
    count = lax.axis_size("dp") * lax.axis_size("fsdp")
    return lax.ppermute(values, AXES, [(i, i ^ mask) for i in range(count)])


def place_of(relative, order):
    shift_of = {"dp": bits_of(lax.axis_size("fsdp")), "fsdp": 0}
    place = jnp.zeros_like(relative)
    for axis, bit in order:
        place = place * 2 + ((relative >> (shift_of[axis] + bit)) & 1)
    return place


def class_counts(owners, devices):
    block = jnp.arange(NBLK, dtype=jnp.int32)
    mid = ((block >= MID0) & (block < MID1))[None, :]
    device = jnp.arange(devices, dtype=jnp.int32)
    below = owners[None, :] < device[:, None]
    owned = owners[None, :] == device[:, None]

    def total(mask):
        return jnp.sum(mask.astype(jnp.int32), axis=1)

    start = (total(below & ~mid), total(below & mid))
    count = (total(owned & ~mid), total(owned & mid))
    return start, count, total(owned & (block < MID0)[None, :])


def my_counts(owners, me):
    block = jnp.arange(NBLK, dtype=jnp.int32)
    mid = (block >= MID0) & (block < MID1)
    below, owned = owners < me, owners == me
    total = lambda mask: jnp.sum(mask.astype(jnp.int32))
    start = (total(below & ~mid), total(below & mid))
    count = (total(owned & ~mid), total(owned & mid))
    return start, count, total(owned & (block < MID0))


def pair_lanes(capacity, devices):
    return -(-capacity // devices)


def make_plan(owners, capacity, devices, me):
    block = jnp.arange(NBLK, dtype=jnp.int32)
    mid = (block >= MID0) & (block < MID1)
    same = mid[:, None] == mid[None, :]
    before = (owners[None, :] < owners[:, None]) | (
        (owners[None, :] == owners[:, None]) & (block[None, :] < block[:, None])
    )
    order = jnp.sum(before.astype(jnp.int32), axis=1)
    order_in_class = jnp.sum((same & before).astype(jnp.int32), axis=1)
    home, slot = order % devices, order // devices
    device = jnp.arange(devices, dtype=jnp.int32)
    start, count, _ = class_counts(owners, devices)
    my_start, my_count, my_early = my_counts(owners, me)
    pair = pair_lanes(capacity, devices)

    slots = -(-NBLK // devices)
    wanted = me + devices * jnp.arange(slots, dtype=jnp.int32)
    first = start[0] + start[1]
    ends = first + count[0] + count[1]
    owner = jnp.sum((ends[None, :] <= wanted[:, None]).astype(jnp.int32), axis=1)
    owner = jnp.minimum(owner, devices - 1)
    base = jnp.sum(jnp.where(device[None, :] == owner[:, None], first[None, :], 0), axis=1)
    received = owner * pair + jnp.clip((wanted - base) // devices, 0, pair - 1)

    back_pair = (UNITS * capacity + 2 * (devices - 1)) // devices
    unit = UNITS * order_in_class[:, None] + jnp.arange(UNITS, dtype=jnp.int32)[None, :]
    unit_home, unit_slot = unit % devices, unit // devices
    unit_slots = (-(-UNITS * N0 // devices), -(-UNITS * N1 // devices))
    lane = jnp.arange(back_pair, dtype=jnp.int32)

    def units_back(kind):
        turn = lane if kind == 0 else back_pair - 1 - lane
        first = UNITS * start[kind][:, None]
        k = (me - first) % devices + turn[None, :] * devices
        return k < UNITS * count[kind][:, None], (first + k) // devices

    valid0, slot0 = units_back(0)
    valid1, slot1 = units_back(1)
    back = jnp.where(valid0, slot0, jnp.where(valid1, unit_slots[0] + slot1, 0)).reshape(-1)

    row = jnp.arange(capacity, dtype=jnp.int32)
    is_mid = (row >= my_early) & (row < my_early + my_count[1])
    k = jnp.where(is_mid, row - my_early, jnp.where(row < my_early, row, row - my_count[1]))
    first = UNITS * jnp.where(is_mid, my_start[1], my_start[0])
    k = UNITS * k[:, None] + jnp.arange(UNITS, dtype=jnp.int32)[None, :]
    turn = k // devices
    row_from = ((first[:, None] + k) % devices) * back_pair + jnp.where(
        is_mid[:, None], back_pair - 1 - turn, turn
    )
    row_used = row < my_count[0] + my_count[1]
    mine = (owners == me)[None, :]
    rank = jnp.sum((mine & (block[None, :] < block[:, None])).astype(jnp.int32), axis=1)
    row_block = jnp.sum(
        jnp.where(mine & (rank[None, :] == row[:, None]), block[None, :], 0), axis=1
    )
    late = devices * back_pair + UNITS * (row_block - MID1)
    late = late[:, None] + jnp.arange(UNITS, dtype=jnp.int32)[None, :]
    row_from = jnp.where((row_block >= MID1)[:, None], late, row_from)
    row_from = jnp.where(row_used[:, None], row_from, 0).reshape(-1)
    return dict(
        home=home, slot=slot, slots=slots,
        received=received, unit_home=unit_home, unit_slot=unit_slot,
        unit_slots=unit_slots, back=back, row_from=row_from,
        row_used=row_used, row_block=row_block,
    )


def stream_places(home, slot, me, streams, devices):
    relative = home ^ me
    place = jnp.zeros_like(slot)
    for begin, size, order in streams:
        inside = (slot >= begin) & (slot < begin + size)
        at = devices * begin + place_of(relative, order) * size + slot - begin
        place = jnp.where(inside, at, place)
    return place


def cost(microseconds):
    return pl.CostEstimate(
        flops=int(microseconds * 1e9), bytes_accessed=int(microseconds * 3e6), transcendentals=0
    )


ANY = pl.BlockSpec(memory_space=pl.ANY)
VMEM = pl.BlockSpec(memory_space=pltpu.VMEM)
SMEM = pl.BlockSpec(memory_space=pltpu.SMEM)


def params(**extra):
    return pltpu.CompilerParams(vmem_limit_bytes=VMEM_LIMIT, **extra)


def shape(dims, dtype):
    return jax.ShapeDtypeStruct(dims, dtype)


def send_kernel(my_index, owners, master, out, flat, *, devices):
    capacity = master.shape[0]
    me = my_index[0]
    for j in range(BROWS):
        flat[pl.ds(j, capacity, stride=BROWS), :] = master[:, j * LANES : (j + 1) * LANES]
    held = owners[...]
    below, owned = held < me, held == me

    def total(mask):
        return jnp.sum(jnp.where(mask, 1.0, 0.0)).astype(jnp.int32)

    start, count = total(below), total(owned)
    pair = out.shape[0] // devices

    def step(home, carry):
        for s in range(pair):
            k = lax.rem(home - start + devices * NBLK, devices) + s * devices
            row = jnp.where(k < count, k, 0)
            rows = pl.ds(pl.multiple_of(row * BROWS, BROWS), BROWS)
            out[home * pair + s] = flat[rows, :].astype(out.dtype)
        return carry

    lax.fori_loop(0, devices, step, 0)


def send_blocks(owners, master, devices, me):
    rows = -(-NBLK // (8 * LANES)) * 8
    held = jnp.pad(owners, (0, rows * LANES - NBLK), constant_values=1 << 20).reshape(rows, LANES)
    count = devices * pair_lanes(master.shape[0], devices)
    return pl.pallas_call(
        partial(send_kernel, devices=devices),
        out_shape=shape((count, BROWS, LANES), jnp.bfloat16),
        in_specs=[SMEM, VMEM, VMEM],
        out_specs=VMEM,
        scratch_shapes=[pltpu.VMEM((master.shape[0] * BROWS, LANES), jnp.float32)],
        compiler_params=params(),
    )(me.reshape(1), held, master)


def pick_kernel(table, source, *outs):
    at = 0
    for out in outs:

        def step(i, carry, out=out, at=at):
            out[i] = source[table[at + i]]
            return carry

        lax.fori_loop(0, out.shape[0], step, 0)
        at += out.shape[0]


def pick_blocks(table, source, sizes):
    return pl.pallas_call(
        pick_kernel,
        out_shape=tuple(shape((n,) + source.shape[1:], source.dtype) for n in sizes),
        in_specs=[SMEM, VMEM],
        out_specs=(VMEM,) * len(sizes),
        compiler_params=params(),
    )(table, source)


def back_kernel(table, *refs, sizes):
    sources, (out, held) = refs[:-2], refs[-2:]
    at = i = 0
    for size in sizes:
        n = sources[i].shape[0]
        total = sources[i][...]
        for k in range(1, size):
            total = total + sources[i + k][0:n]
        held[at : at + n] = total
        at += n
        i += size

    def step(i, carry):
        for u in range(8):
            out[i * 8 + u] = held[table[i * 8 + u]]
        return carry

    total = out.shape[0]
    lax.fori_loop(0, total // 8, step, 0)


def units_to_owners(table, groups):
    return pl.pallas_call(
        partial(back_kernel, sizes=[len(g) for g in groups]),
        out_shape=shape((table.shape[0], UNIT, LANES), jnp.float32),
        in_specs=[SMEM] + [VMEM] * sum(len(g) for g in groups),
        out_specs=VMEM,
        scratch_shapes=[pltpu.VMEM((sum(g[0].shape[0] for g in groups), UNIT, LANES), jnp.float32)],
        compiler_params=params(),
    )(table, *[v for g in groups for v in g])


def fold_kernel(*refs, streams, extra):
    sources, outs = refs[: 2 * streams + extra], refs[2 * streams + extra :]
    at = 0
    for i in range(streams):
        kept, got = sources[2 * i], sources[2 * i + 1]
        n = kept.shape[0] // 4
        for p in range(4):
            outs[p][at : at + n] = kept[p * n : (p + 1) * n] + got[p * n : (p + 1) * n]
        at += n
    if extra:
        for p in range(1, 4):
            outs[p][at:] = sources[-1][...]


def fold(pairs, extra=None):
    n = sum(kept.shape[0] // 4 for kept, _ in pairs)
    more = 0 if extra is None else extra.shape[0]
    values = [v for pair in pairs for v in pair] + ([] if extra is None else [extra])
    return pl.pallas_call(
        partial(fold_kernel, streams=len(pairs), extra=int(extra is not None)),
        out_shape=[shape((n + (more if p else 0), UNIT, LANES), jnp.float32) for p in range(4)],
        in_specs=[VMEM] * len(values),
        out_specs=[VMEM] * 4,
        compiler_params=params(),
    )(*values)


def exchange_quarters(given, steps):
    return [exchange(given[1], steps[1]), exchange(given[2], steps[0]), exchange(given[3], *steps)]


def row_start(rho):
    return (PROJ * rho) // LANES, (PROJ * rho) % LANES


def copy_all(pairs, sem):
    copies = [pltpu.make_async_copy(a, b, sem.at[i]) for i, (a, b) in enumerate(pairs)]
    for c in copies:
        c.start()
    for c in copies:
        c.wait()


def spread_blocks(table, first, held, flat, count, first_row):
    def one(i):
        at = pl.multiple_of(first_row + i * BROWS, 16)
        flat[pl.ds(at, BROWS), :] = held[table[first + i]].astype(jnp.float32)

    def step(i, carry):
        for u in range(4):
            one(i * 4 + u)
        return carry

    lax.fori_loop(0, count // 4, step, 0)
    for i in range(count // 4 * 4, count):
        one(i)


def unpack_vectors(flat, conv_weight, conv_bias, heads, skip, norm_gain, gate_gain):
    bf16, f32 = jnp.bfloat16, jnp.float32
    tiles = CONVCH // LANES
    row = lax.broadcasted_iota(jnp.int32, (LANES, LANES), 0)
    col = lax.broadcasted_iota(jnp.int32, (LANES, LANES), 1)
    per_tile = LANES // KCONV
    for k in range(KCONV):
        total = jnp.zeros((tiles, LANES), f32)
        for q in range(KCONV):
            rows = flat[pl.ds(VEC_AT + q, tiles, stride=KCONV), :].astype(bf16)
            chosen = (row == KCONV * (col % per_tile) + k) & (col // per_tile == q)
            total = total + jnp.dot(rows, chosen.astype(bf16), preferred_element_type=f32)
        for i in range(tiles):
            conv_weight[k : k + 1, i * LANES : (i + 1) * LANES] = total[i : i + 1, :]
    bias_at = VEC_AT + tiles * KCONV
    for i in range(tiles):
        conv_bias[:, i * LANES : (i + 1) * LANES] = flat[bias_at + i : bias_at + i + 1, :]
    at = bias_at + tiles
    lane = lax.broadcasted_iota(jnp.int32, (8, LANES), 1)
    first = flat[at : at + 8, :]
    three = []
    for i in range(3):
        moved = pltpu.roll(first, LANES - i * HEADS, 1) if i else first
        three.append(jnp.where(lane < HEADS, moved, 0.0))
        heads[i : i + 1, :] = three[i][0:1, :]
    for j in range(INNER // LANES):
        h = lax.broadcasted_iota(jnp.int32, (LANES, LANES), 0)
        c = lax.broadcasted_iota(jnp.int32, (LANES, LANES), 1) + j * LANES
        spread = (h == c // HEADDIM).astype(bf16)
        wide = jnp.dot(three[2].astype(bf16), spread, preferred_element_type=f32)
        skip[:, j * LANES : (j + 1) * LANES] = wide[0:1, :]
    shift = 3 * HEADS
    for out, begin, width in ((norm_gain, at, D), (gate_gain, at + D // LANES, INNER)):
        for j in range(width // LANES):
            x = pltpu.roll(flat[begin + j : begin + j + 1, :], LANES - shift, 1)
            y = pltpu.roll(flat[begin + j + 1 : begin + j + 2, :], LANES - shift, 1)
            out[:, j * LANES : (j + 1) * LANES] = jnp.where(lane[0:1] < LANES - shift, x, y)


def unpack_kernel(table, *refs):
    parts, outs, scratch = refs[:-13], refs[-13:-5], refs[-5:]
    w_in, w_out, *vectors = outs
    held, flat, flat_out, tile, sem = scratch
    pairs, at = [], 0
    for part in parts:
        pairs.append((part, held.at[pl.ds(at, part.shape[0])]))
        at += part.shape[0]
    copy_all(pairs, sem)
    spread_blocks(table, 0, held, flat, MID0, 0)
    spread_blocks(table, MID1, held, flat, NBLK - MID1, MID0 * BROWS)
    spread_blocks(table, MID0, held, flat_out, N1, HEAD_ROWS)
    flat_out[0:HEAD_ROWS, :] = flat[IN_ROWS : IN_ROWS + HEAD_ROWS, :]
    flat_out[OUT_ROWS - TAIL_ROWS :, :] = flat[MID0 * BROWS : MID0 * BROWS + TAIL_ROWS, :]
    unpack_vectors(flat, *vectors)
    rows = 128

    def out_step(i, carry):
        at = pl.multiple_of(i * rows, rows)
        for j in range(OUT_TILES):
            x = flat_out[pl.ds(at * OUT_TILES + j, rows, stride=OUT_TILES), :]
            w_out[pl.ds(at, rows), j * LANES : (j + 1) * LANES] = x.astype(jnp.bfloat16)
        return carry

    lax.fori_loop(0, INNER // rows, out_step, 0)
    lane = lax.broadcasted_iota(jnp.int32, (GROUPS, LANES), 1)

    def columns(j):
        for rho in range(GROUP):
            c, s = row_start(rho)
            x = flat[pl.ds(c + j, GROUPS, stride=GROUP_ROWS), :]
            if s:
                y = flat[pl.ds(c + j + 1, GROUPS, stride=GROUP_ROWS), :]
                x = jnp.where(
                    lane < LANES - s,
                    pltpu.roll(x, LANES - s, 1),
                    pltpu.roll(y, LANES - s, 1),
                )
            tile[pl.ds(rho, GROUPS, stride=GROUP), :] = x

    def step(j, carry):
        columns(j)
        w_in[:, pl.ds(pl.multiple_of(j * LANES, LANES), LANES)] = tile[...].astype(jnp.bfloat16)
        return carry

    lax.fori_loop(0, COL_TILES - 1, step, 0)
    columns(COL_TILES - 1)
    last = (COL_TILES - 1) * LANES
    inside = lax.broadcasted_iota(jnp.int32, (D, LANES), 1) < PROJ - last
    w_in[:, last:] = jnp.where(inside, tile[...], 0.0).astype(jnp.bfloat16)


def unpack(table, parts):
    held = sum(part.shape[0] for part in parts)
    f32 = jnp.float32
    return pl.pallas_call(
        unpack_kernel,
        out_shape=(
            shape((D, WIDE), jnp.bfloat16),
            shape((INNER, D), jnp.bfloat16),
            shape((KCONV, CONVCH), f32),
            shape((1, CONVCH), f32),
            shape((8, LANES), f32),
            shape((1, INNER), f32),
            shape((1, D), f32),
            shape((1, INNER), f32),
        ),
        in_specs=[SMEM] + [ANY] * len(parts),
        out_specs=(VMEM,) * 8,
        scratch_shapes=[
            pltpu.VMEM((held, BROWS, LANES), jnp.bfloat16),
            pltpu.VMEM((F0_ROWS, LANES), f32),
            pltpu.VMEM((OUT_ROWS, LANES), f32),
            pltpu.VMEM((D, LANES), f32),
            pltpu.SemaphoreType.DMA((len(parts),)),
        ],
        compiler_params=params(),
        cost_estimate=cost(20),
    )(table, *parts)


def permute_units(table, flat, count, first_row, staged):
    many = 16

    def step(i, carry):
        for u in range(many):
            at = pl.multiple_of(first_row + (i * many + u) * UNIT, UNIT)
            staged[table[i * many + u]] = flat[pl.ds(at, UNIT), :]
        return carry

    lax.fori_loop(0, count // many, step, 0)
    for i in range(count // many * many, count):
        staged[table[i]] = flat[first_row + i * UNIT : first_row + (i + 1) * UNIT, :]


def pack_in_kernel(table, hidden, grad, head, *refs):
    outs, (turned, tiles, flat, staged, held, sem, read_sem) = refs[:-7], refs[-7:]

    def read(p):
        width = 2 * LANES
        at = p * width
        if isinstance(p, int):
            width = min(width, WIDE - at)
        else:
            at = pl.multiple_of(at, width)
        cols = pl.ds(at, width)
        return pltpu.make_async_copy(grad.at[:, cols], held.at[:, cols], read_sem.at[p])

    for p in range(-(-COL_TILES // 2)):
        read(p).start()
    turned[...] = hidden[...].T
    lane = lax.broadcasted_iota(jnp.int32, (GROUPS, LANES), 1)

    def product(p, count):
        read(p).wait()
        at = p * 2 * LANES
        at = at if isinstance(at, int) else pl.multiple_of(at, 2 * LANES)
        return jnp.dot(
            turned[...], held[:, pl.ds(at, count * LANES)], preferred_element_type=jnp.float32
        )

    def put(p, value):
        for k in range(value.shape[1] // LANES):
            at = (p * 2 + k) * D
            at = at if isinstance(at, int) else pl.multiple_of(at, D)
            tiles[pl.ds(at, D), :] = value[:, k * LANES : (k + 1) * LANES]

    def load(rho, j):
        return tiles[pl.ds(j * D + rho, GROUPS, stride=GROUP), :]

    def whole(rho, i):
        first = -(-PROJ * rho // LANES)
        col0 = first * LANES - PROJ * rho
        x = load(rho, i)
        if col0:
            x = jnp.where(
                lane < LANES - col0,
                pltpu.roll(x, LANES - col0, 1),
                pltpu.roll(load(rho, i + 1), LANES - col0, 1),
            )
        flat[pl.ds(first + i, GROUPS, stride=GROUP_ROWS), :] = x

    put(0, product(0, 2))
    put(1, product(1, 2))
    pairs = COL_TILES // 2

    def step(p, carry):
        for i in range(2):
            for rho in range(GROUP):
                whole(rho, p * 2 + i)
        put(p + 2, product(p + 2, 2))
        return carry

    lax.fori_loop(0, pairs - 2, step, 0)
    put(pairs, product(pairs, COL_TILES % 2))
    for rho in range(GROUP):
        first = -(-PROJ * rho // LANES)
        col0 = first * LANES - PROJ * rho
        full = (PROJ - col0) // LANES
        for i in range((pairs - 2) * 2, full):
            whole(rho, i)
        left = PROJ - col0 - full * LANES
        if left:
            begin = col0 + full * LANES
            j, s = begin // LANES, begin % LANES
            x = pltpu.roll(load(rho, j), LANES - s, 1) if s else load(rho, j)
            if s + left > LANES:
                x = jnp.where(lane < LANES - s, x, pltpu.roll(load(rho, j + 1), LANES - s, 1))
            y = pltpu.roll(load(rho + 1, 0), left, 1)
            flat[pl.ds(first + full, GROUPS, stride=GROUP_ROWS), :] = jnp.where(lane < left, x, y)
    flat[IN_ROWS : IN_ROWS + HEAD_ROWS, :] = head[...]
    permute_units(table, flat, MID0 * UNITS, 0, staged)
    copies, at = [], 0
    for out in outs:
        copies.append((staged.at[pl.ds(at, out.shape[0])], out))
        at += out.shape[0]
    copy_all(copies, sem)


def pack_in(table, hidden, grad, head, sizes):
    return pl.pallas_call(
        pack_in_kernel,
        out_shape=tuple(shape((n, UNIT, LANES), jnp.float32) for n in sizes),
        in_specs=[SMEM, VMEM, ANY, VMEM],
        out_specs=(ANY,) * len(sizes),
        scratch_shapes=[
            pltpu.VMEM((D, hidden.shape[0]), jnp.bfloat16),
            pltpu.VMEM((COL_TILES * D, LANES), jnp.float32),
            pltpu.VMEM((MID0 * BROWS, LANES), jnp.float32),
            pltpu.VMEM((sum(sizes), UNIT, LANES), jnp.float32),
            pltpu.VMEM(grad.shape, jnp.bfloat16),
            pltpu.SemaphoreType.DMA((len(sizes),)),
            pltpu.SemaphoreType.DMA((-(-COL_TILES // 2),)),
        ],
        compiler_params=params(),
        cost_estimate=cost(20),
    )(table, hidden, grad, head)


def pack_out_kernel(
    table, mixed_out, grad, local, keep, send, head, tail, turned, flat, out, sem, *, slots
):
    rows = 256

    def step(i, carry):
        at = pl.multiple_of(i * rows, rows)
        turned[...] = mixed_out[:, pl.ds(at, rows)].T
        product = jnp.dot(turned[...], grad[...], preferred_element_type=jnp.float32)
        for j in range(OUT_TILES):
            flat[pl.ds(at * OUT_TILES + j, rows, stride=OUT_TILES), :] = product[
                :, j * LANES : (j + 1) * LANES
            ]
        return carry

    lax.fori_loop(0, INNER // rows, step, 0)
    head[...] = flat[0:HEAD_ROWS, :]
    tail[...] = flat[OUT_ROWS - TAIL_ROWS : OUT_ROWS, :]
    permute_units(table, flat, N1 * UNITS, HEAD_ROWS, out)

    def add_local(i, carry):
        out[i * slots + slots - 1] = local[...]
        return carry

    lax.fori_loop(0, out.shape[0] // slots, add_local, 0)
    half = keep.shape[0]
    copy_all([(out.at[pl.ds(0, half)], keep), (out.at[pl.ds(half, half)], send)], sem)


def pack_out(table, mixed_out, grad, local, devices, slots):
    return pl.pallas_call(
        partial(pack_out_kernel, slots=slots),
        out_shape=(
            shape((devices * slots // 2, UNIT, LANES), jnp.float32),
            shape((devices * slots // 2, UNIT, LANES), jnp.float32),
            shape((HEAD_ROWS, LANES), jnp.float32),
            shape((TAIL_ROWS, LANES), jnp.float32),
        ),
        in_specs=[SMEM, VMEM, VMEM, VMEM],
        out_specs=(ANY, ANY, VMEM, VMEM),
        scratch_shapes=[
            pltpu.VMEM((256, mixed_out.shape[0]), jnp.bfloat16),
            pltpu.VMEM((OUT_ROWS, LANES), jnp.float32),
            pltpu.VMEM((devices * slots, UNIT, LANES), jnp.float32),
            pltpu.SemaphoreType.DMA((2,)),
        ],
        compiler_params=params(),
    )(table, mixed_out, grad, local)


def adam_kernel(
    table, row_block, row_used, scale, got, late, master, first, second,
    o_first, o_second, o_master, flat, held, limit, used,
):
    capacity = master.shape[0]

    def step(i, carry):
        for u in range(UNITS):
            at = table[i * UNITS + u]
            rows = pl.ds(pl.multiple_of(i * BROWS + u * UNIT, UNIT), UNIT)
            flat[rows, :] = held[at]
        limit[pl.ds(i, 1), :] = jnp.full((1, LANES), END_OUT - row_block[i] * PBLOCK, jnp.int32)
        used[pl.ds(i, 1), :] = jnp.full((1, LANES), row_used[i], jnp.int32)
        return carry

    held[0 : got.shape[0]] = got[...]
    held[got.shape[0] :] = late[...]
    lax.fori_loop(0, capacity, step, 0)
    lane = lax.broadcasted_iota(jnp.int32, (capacity, LANES), 1)
    divisor = scale[0]
    for j in range(BROWS):
        cols = slice(j * LANES, (j + 1) * LANES)
        grad = jnp.where(used[...] > 0, flat[pl.ds(j, capacity, stride=BROWS), :], 0.0) / divisor
        matrix = lane + j * LANES < limit[...]
        weights = master[:, cols]
        new_first = BETA_ONE * first[:, cols] + (1.0 - BETA_ONE) * grad
        new_second = BETA_TWO * second[:, cols] + (1.0 - BETA_TWO) * grad * grad
        normal = (
            new_first
            / (1.0 - BETA_ONE**STEP)
            / (jnp.sqrt(new_second / (1.0 - BETA_TWO**STEP)) + ADAM_EPS)
        )
        rate = jnp.where(matrix, MATRIX_RATE, VECTOR_RATE)
        decay = jnp.where(matrix, WEIGHT_DECAY, 0.0)
        o_first[:, cols] = new_first
        o_second[:, cols] = new_second
        o_master[:, cols] = weights - rate * (normal + decay * weights)


def adam(table, row_block, row_used, divisor, got, late, master, first, second):
    capacity = master.shape[0]
    return pl.pallas_call(
        adam_kernel,
        out_shape=(shape(master.shape, jnp.float32),) * 3,
        in_specs=[SMEM] * 4 + [VMEM] * 5,
        out_specs=(VMEM,) * 3,
        scratch_shapes=[
            pltpu.VMEM((capacity * BROWS, LANES), jnp.float32),
            pltpu.VMEM((got.shape[0] + late.shape[0], UNIT, LANES), jnp.float32),
            pltpu.VMEM((capacity, LANES), jnp.int32),
            pltpu.VMEM((capacity, LANES), jnp.int32),
        ],
        compiler_params=params(),
    )(
        table, row_block, row_used.astype(jnp.int32), divisor.reshape(1), got, late, master, first, second
    )


def doubled(values, step):
    return jnp.concatenate([values, exchange(values, step)], axis=0)


def gather_steps(values, order):
    for step in order[:0:-1]:
        values = doubled(values, step)
    return values, exchange(values, order[0])


def reduce_step(kept, got, step, extra=None):
    half = kept.shape[0] // 2
    given = kept[half:] + got[half:]
    if extra is None:
        return kept[:half] + got[:half], exchange(given, step)
    arrived = exchange(jnp.concatenate([given, extra]), step)
    return kept[:half] + got[:half], arrived[:half], extra + arrived[half:]


CHUNK = 128
PAIRS = HEADS // 2
MIXW = INNER + 2 * NSTATE
DT_AT = INNER + CONVCH
F32 = jnp.float32
BF16 = jnp.bfloat16
NN = (((1,), (0,)), ((), ()))
NT = (((1,), (1,)), ((), ()))


def dot(a, b, dims=NN):
    return lax.dot_general(a, b, dims, preferred_element_type=F32)


def split(v):
    high = v.astype(BF16)
    return high, (v - high.astype(F32)).astype(BF16)


def dot3(a, b, dims=NN):
    ah, al = a
    bh, bl = b
    return dot(ah, bh, dims) + (dot(ah, bl, dims) + dot(al, bh, dims))


def heads_gather():
    return jnp.asarray(np.repeat(np.eye(HEADS, LANES, dtype=np.float32), HEADDIM, axis=0), BF16)


def three_parts(v):
    high = v.astype(BF16).astype(F32)
    rest = v - high
    middle = rest.astype(BF16).astype(F32)
    low = rest - middle
    return (high + pltpu.roll(middle, 32, 1) + pltpu.roll(low, 64, 1)).astype(BF16)


def triangle_sum(tri, v):
    parts = dot(tri, three_parts(v))
    lane = lax.broadcasted_iota(jnp.int32, parts.shape, 1)
    total = parts + pltpu.roll(parts, LANES - 32, 1) + pltpu.roll(parts, LANES - 64, 1)
    return jnp.where(lane < HEADS, total, 0.0)


def chunk_decays(dt, dt_bias, a_log):
    lane = lax.broadcasted_iota(jnp.int32, (CHUNK, LANES), 1)
    row = lax.broadcasted_iota(jnp.int32, (CHUNK, LANES), 0)
    shifted = dt + dt_bias
    delta = jnp.where(
        lane < HEADS, jnp.maximum(shifted, 0.0) + jnp.log1p(jnp.exp(-jnp.abs(shifted))), 0.0
    )
    rate = -jnp.exp(a_log)
    lower = (row >= lane).astype(BF16)
    cum = triangle_sum(lower, delta * rate)
    last = cum[CHUNK - 1 : CHUNK, :]
    return shifted, delta, rate, cum, last


def pair_mask():
    lane = lax.broadcasted_iota(jnp.int32, (CHUNK, LANES), 1)
    low = (lane < HEADDIM).astype(F32)
    return low.astype(BF16), (1.0 - low).astype(BF16)


QUADS = HEADS // 4
QWIDTH = 4 * HEADDIM


def sigmoid(v):
    return 0.5 * jnp.tanh(0.5 * v) + 0.5


def silu(v):
    return v * sigmoid(v)


def side_by_side(v):
    high, low = split(v)
    return jnp.concatenate([high, low], axis=1), high


def dot_parts(a, b):
    ahl, ah = a
    bh, bl = b
    return dot(ahl, jnp.concatenate([bh, bh], axis=0)) + dot(ah, bl)


def dot_turned(a, b):
    ah, al = a
    bh, bl = b
    both = dot(ah, jnp.concatenate([bh, bl], axis=0), NT)
    n = bh.shape[0]
    return both[:, :n] + both[:, n:] + dot(al, bh, NT)


def widen(delta, cum, quad):
    lane = lax.broadcasted_iota(jnp.int32, (CHUNK, LANES), 1)
    over = lambda v, h: jnp.broadcast_to(v[:, h : h + 1], (CHUNK, LANES))
    first = 4 * quad
    columns = [over(cum, first + k) for k in range(4)]
    rates = [over(delta, first + k) for k in range(4)]
    pair = lambda vs: jnp.concatenate(
        [jnp.where(lane < HEADDIM, vs[0], vs[1]), jnp.where(lane < HEADDIM, vs[2], vs[3])], axis=1
    )
    return pair(rates), pair(columns), columns


def pair_rows(parts, j, low, high):
    cols = slice(j * LANES, (j + 1) * LANES)
    return [jnp.concatenate([p[:, cols] * low, p[:, cols] * high], axis=0) for p in parts]


def scan_chunk(mixed, dt, dt_bias, a_log, skip, state, put):
    _, delta, _, cum, last = chunk_decays(dt, dt_bias, a_log)
    lane = lax.broadcasted_iota(jnp.int32, (CHUNK, LANES), 1)
    row = lax.broadcasted_iota(jnp.int32, (CHUNK, LANES), 0)
    bias = jnp.where(row >= lane, 0.0, -1e30)
    cum_t = cum.T
    inputs_b = mixed[:, INNER : INNER + NSTATE]
    readout = mixed[:, INNER + NSTATE :]
    affinity = dot3(split(readout), split(inputs_b), NT)
    readout_parts = side_by_side(readout)
    b_parts = side_by_side(inputs_b.T)
    low, high = pair_mask()
    for quad in range(QUADS):
        cols = slice(quad * QWIDTH, (quad + 1) * QWIDTH)
        wide_delta, wide_cum, columns = widen(delta, cum, quad)
        values = mixed[:, cols]
        scaled = values * wide_delta
        parts = split(scaled)
        outs = []
        for j in range(2):
            right_h, right_l = pair_rows(parts, j, low, high)
            left = []
            for k in range(2):
                h = 4 * quad + 2 * j + k
                within = jnp.exp(columns[2 * j + k] - cum_t[h : h + 1, :] + bias)
                left.append(split(affinity * within))
            left_h = jnp.concatenate([left[0][0], left[1][0]], axis=1)
            left_l = jnp.concatenate([left[0][1], left[1][1]], axis=1)
            both = dot(left_h, jnp.concatenate([right_h, right_l], axis=1))
            outs.append(both[:, :LANES] + both[:, LANES:] + dot(left_l, right_h))
        carried = state[:, cols]
        grown = jnp.exp(wide_cum)
        out = jnp.concatenate(outs, axis=1) + dot_parts(readout_parts, split(carried)) * grown
        tail = jnp.exp(wide_cum[CHUNK - 1 :] - wide_cum)
        state[:, cols] = carried * grown[CHUNK - 1 :] + dot_parts(b_parts, split(scaled * tail))
        put(quad, out + skip[:, cols] * values)


FORWARD_ROWS = 2 * CHUNK


def forward_kernel(
    tokens, w_in, norm_gain, conv_weight, conv_bias, dt_bias, a_log, skip, gain,
    hidden, projected, mixed, ssm, mixed_out, states, state, before,
):
    @pl.when(pl.program_id(0) == 0)
    def _():
        state[...] = jnp.zeros_like(state)
        before[...] = jnp.zeros_like(before)

    x = tokens[...].astype(F32)
    inverse = lax.rsqrt(jnp.mean(x * x, axis=1, keepdims=True) + NORM_EPS)
    h = (x * inverse * norm_gain[...]).astype(BF16)
    hidden[...] = h
    projected[:, DT_AT:] = dot(h, w_in[:, DT_AT:])
    wide = 2 * LANES
    for tile in range(CONVCH // wide):
        at = tile * wide
        product = dot(h, w_in[:, INNER + at : INNER + at + wide])
        projected[:, INNER + at : INNER + at + wide] = product
        for half in range(2):
            cols = slice(at + half * LANES, at + (half + 1) * LANES)
            rows = product[:, half * LANES : (half + 1) * LANES]
            earlier = before[:, cols]
            terms = [down(rows, earlier, KCONV - 1 - k) for k in range(KCONV - 1)] + [rows]
            before[:, cols] = rows[FORWARD_ROWS - 8 :]
            mixed[:, cols] = silu(conv_sum(terms, conv_weight[:, cols], conv_bias[:, cols]))
    for tile in range(INNER // wide):
        cols = slice(tile * wide, (tile + 1) * wide)
        projected[:, cols] = dot(h, w_in[:, cols])
    for sub in range(FORWARD_ROWS // CHUNK):
        rows = slice(sub * CHUNK, (sub + 1) * CHUNK)
        states[sub] = state[...]
        squares = [jnp.zeros((CHUNK, LANES), F32)]

        def put(quad, out, rows=rows, squares=squares):
            cols = slice(quad * QWIDTH, (quad + 1) * QWIDTH)
            ssm[rows, cols] = out
            gated = out * silu(projected[rows, cols])
            first, second = gated[:, :LANES], gated[:, LANES:]
            squares[0] = squares[0] + first * first + second * second

        scan_chunk(
            mixed[rows, :], projected[rows, DT_AT:], dt_bias[...], a_log[...], skip, state, put
        )
        rho = lax.rsqrt(jnp.sum(squares[0], axis=1, keepdims=True) * (1.0 / INNER) + NORM_EPS)
        for j in range(PAIRS):
            cols = slice(j * LANES, (j + 1) * LANES)
            gated = ssm[rows, cols] * silu(projected[rows, cols])
            mixed_out[rows, cols] = (gated * rho * gain[:, cols]).astype(BF16)


def forward(tokens, w_in, norm_gain, conv_weight, conv_bias, dt_bias, a_log, skip, gain):
    length = tokens.shape[0]
    by_row = lambda width: pl.BlockSpec((FORWARD_ROWS, width), lambda i: (i, 0))
    whole = lambda v: pl.BlockSpec(v.shape, lambda i: (0,) * v.ndim)
    per_step = FORWARD_ROWS // CHUNK
    return pl.pallas_call(
        forward_kernel,
        grid=(length // FORWARD_ROWS,),
        out_shape=(
            shape((length, D), BF16),
            shape((length, WIDE), F32),
            shape((length, MIXW), F32),
            shape((length, INNER), F32),
            shape((length, INNER), BF16),
            shape((length // CHUNK, NSTATE, INNER), F32),
        ),
        in_specs=[by_row(D)]
        + [
            whole(v)
            for v in (w_in, norm_gain, conv_weight, conv_bias, dt_bias, a_log, skip, gain)
        ],
        out_specs=(
            by_row(D),
            by_row(WIDE),
            by_row(MIXW),
            by_row(INNER),
            by_row(INNER),
            pl.BlockSpec((per_step, NSTATE, INNER), lambda i: (i, 0, 0)),
        ),
        scratch_shapes=[pltpu.VMEM((NSTATE, INNER), F32), pltpu.VMEM((8, MIXW), F32)],
        compiler_params=params(),
        cost_estimate=cost(33),
    )(tokens, w_in, norm_gain, conv_weight, conv_bias, dt_bias, a_log, skip, gain)


def scan_backward_kernel(
    mixed, dt, ssm, grad, states, dt_bias, a_log, skip, gather, held,
    grad_mixed, grad_dt, sums, skip_sums, grad_state, left, right,
):
    @pl.when(pl.program_id(0) == 0)
    def _():
        grad_state[...] = jnp.zeros_like(grad_state)
        sums[...] = jnp.zeros_like(sums)
        skip_sums[...] = jnp.zeros_like(skip_sums)

    shifted, delta, rate, cum, last = chunk_decays(dt[...], dt_bias[...], a_log[...])
    lane = lax.broadcasted_iota(jnp.int32, (CHUNK, LANES), 1)
    row = lax.broadcasted_iota(jnp.int32, (CHUNK, LANES), 0)
    bias = jnp.where(lane >= row, 0.0, -1e30)
    heads = lane < HEADS
    cum_t = cum.T
    inputs_b = mixed[:, INNER : INNER + NSTATE]
    readout = mixed[:, INNER + NSTATE :]
    b_parts, c_parts = split(inputs_b), split(readout)
    b_wide = side_by_side(inputs_b)
    c_turned = side_by_side(readout.T)
    affinity = dot3(b_parts, c_parts, NT)
    low, high = pair_mask()
    grad_affinity = jnp.zeros((CHUNK, CHUNK), F32)
    grad_b = jnp.zeros((CHUNK, NSTATE), F32)
    grad_c = jnp.zeros((CHUNK, NSTATE), F32)
    last_row = lax.broadcasted_iota(jnp.int32, (CHUNK, QWIDTH), 0) == CHUNK - 1
    for quad in range(QUADS):
        cols = slice(quad * QWIDTH, (quad + 1) * QWIDTH)
        wide_delta, wide_cum, columns = widen(delta, cum, quad)
        grown = jnp.exp(wide_cum)
        tail = jnp.exp(wide_cum[CHUNK - 1 :] - wide_cum)
        end = grown[CHUNK - 1 :]
        values = mixed[:, cols]
        pulled = grad[:, cols]
        scaled = values * wide_delta
        x_parts, p_parts = split(scaled), split(pulled)
        outs = []
        for j in range(2):
            half = slice(j * LANES, (j + 1) * LANES)
            xh, xl = x_parts[0][:, half], x_parts[1][:, half]
            right_h, right_l = pair_rows(p_parts, j, low, high)
            pull = dot(
                jnp.concatenate([xh, xl], axis=1),
                jnp.concatenate([right_h, right_h], axis=1),
                NT,
            ) + dot(xh, right_l, NT)
            kernels = []
            for k in range(2):
                h = 4 * quad + 2 * j + k
                within = jnp.exp(cum_t[h : h + 1, :] - columns[2 * j + k] + bias)
                kernels.append(split(affinity * within))
                grad_affinity = grad_affinity + within * pull[:, k * CHUNK : (k + 1) * CHUNK]
            kernel_h = jnp.concatenate([kernels[0][0], kernels[1][0]], axis=1)
            kernel_l = jnp.concatenate([kernels[0][1], kernels[1][1]], axis=1)
            both = dot(kernel_h, jnp.concatenate([right_h, right_l], axis=1))
            outs.append(both[:, :LANES] + both[:, LANES:] + dot(kernel_l, right_h))
        late = grad_state[:, cols]
        late_parts = split(late)
        early = states[0, :, cols]
        from_state = dot_parts(b_wide, late_parts) * tail
        grad_scaled = jnp.concatenate(outs, axis=1) + from_state
        pulled_cum = split(pulled * grown)
        grad_c = grad_c + dot_turned(pulled_cum, split(early))
        grad_b = grad_b + dot_turned(split(scaled * tail), late_parts)
        grad_state[:, cols] = late * end + dot_parts(c_turned, pulled_cum)
        grad_mixed[:, cols] = grad_scaled * wide_delta + skip[:, cols] * pulled
        skip_sums[:, cols] += jnp.sum(pulled * values, axis=0, keepdims=True)
        left[:, cols] = grad_scaled * values
        inner = pulled * (ssm[:, cols] - skip[:, cols] * values) - scaled * grad_scaled
        extra = jnp.sum(scaled * from_state, axis=0, keepdims=True) + end * jnp.sum(
            late * early, axis=0, keepdims=True
        )
        right[:, cols] = inner + jnp.where(last_row, extra, 0.0)
    ga_parts = split(grad_affinity)
    grad_mixed[:, INNER : INNER + NSTATE] = grad_b + dot3(ga_parts, c_parts)
    grad_mixed[:, INNER + NSTATE :] = grad_c + dot3(split(grad_affinity.T), b_parts)

    def by_head(v):
        high, low = split(v)
        g = gather[...]
        return dot(high, g) + dot(low, g)

    direct = by_head(left[...])
    grad_cum = by_head(right[...])
    upper = (lane >= row).astype(BF16)
    after = triangle_sum(upper, grad_cum)
    grad_delta = direct + rate * after
    grad_raw = jnp.where(heads, grad_delta * sigmoid(shifted), 0.0)
    grad_dt[...] = grad_raw.astype(BF16)
    sums[0:1, :] += jnp.sum(grad_raw, axis=0, keepdims=True)
    sums[1:2, :] += rate * jnp.sum(delta * after, axis=0, keepdims=True)


def scan_backward(mixed, projected, ssm, grad, states, dt_bias, a_log, skip, gather, held):
    length = mixed.shape[0]
    chunks = length // CHUNK
    whole = lambda v: pl.BlockSpec(v.shape, lambda i: (0,) * v.ndim)
    back = lambda i: (chunks - 1 - i, 0)
    return pl.pallas_call(
        scan_backward_kernel,
        grid=(chunks,),
        out_shape=(
            shape((length, MIXW), F32),
            shape(held.shape, BF16),
            shape((8, LANES), F32),
            shape((1, INNER), F32),
        ),
        in_specs=[
            pl.BlockSpec((CHUNK, MIXW), back),
            pl.BlockSpec((CHUNK, LANES), lambda i: (chunks - 1 - i, DT_AT // LANES)),
            pl.BlockSpec((CHUNK, INNER), back),
            pl.BlockSpec((CHUNK, INNER), back),
            pl.BlockSpec((1, NSTATE, INNER), lambda i: (chunks - 1 - i, 0, 0)),
        ]
        + [whole(v) for v in (dt_bias, a_log, skip, gather)]
        + [ANY],
        out_specs=(
            pl.BlockSpec((CHUNK, MIXW), back),
            pl.BlockSpec((CHUNK, LANES), lambda i: (chunks - 1 - i, DT_AT // LANES)),
            pl.BlockSpec((8, LANES), lambda i: (0, 0)),
            pl.BlockSpec((1, INNER), lambda i: (0, 0)),
        ),
        scratch_shapes=[pltpu.VMEM((NSTATE, INNER), F32)] + [pltpu.VMEM((CHUNK, INNER), F32)] * 2,
        compiler_params=params(),
        input_output_aliases={9: 1},
        cost_estimate=cost(35),
    )(mixed, projected, ssm, grad, states, dt_bias, a_log, skip, gather, held)


ROWS_AT_ONCE = 128
CONV_TILES = 2


def down(v, before, by):
    moved = pltpu.roll(v, by, 0)
    row = lax.broadcasted_iota(jnp.int32, (8, LANES), 0)
    top = jnp.where(row < by, pltpu.roll(before, by, 0), moved[:8])
    return jnp.concatenate([top, moved[8:]], axis=0)


def up(v, after, by):
    rows = v.shape[0]
    moved = pltpu.roll(v, rows - by, 0)
    row = lax.broadcasted_iota(jnp.int32, (8, LANES), 0)
    end = jnp.where(row < 8 - by, moved[rows - 8 :], pltpu.roll(after, 8 - by, 0))
    return jnp.concatenate([moved[: rows - 8], end], axis=0)


def conv_terms(conv_in, at, cols):
    rows = conv_in[at : at + ROWS_AT_ONCE, cols]
    before = conv_in[at - 8 : at, cols] if at else jnp.zeros((8, LANES), F32)
    return [down(rows, before, KCONV - 1 - k) for k in range(KCONV - 1)] + [rows]


def conv_sum(terms, weight, bias):
    total = bias + terms[KCONV - 1] * weight[KCONV - 1 : KCONV]
    for k in range(KCONV - 1):
        total = total + terms[k] * weight[k : k + 1]
    return total


def conv_backward_kernel(conv_in, grad, weight, bias, held, out, sums):
    length = conv_in.shape[0]
    for tile in range(CONV_TILES):
        cols = slice(tile * LANES, (tile + 1) * LANES)
        w, b = weight[:, cols], bias[:, cols]
        totals = [jnp.zeros((1, LANES), F32)] * (KCONV + 1)
        after = jnp.zeros((8, LANES), F32)
        for at in range(length - ROWS_AT_ONCE, -1, -ROWS_AT_ONCE):
            terms = conv_terms(conv_in, at, cols)
            value = conv_sum(terms, w, b)
            sig = sigmoid(value)
            g = grad[at : at + ROWS_AT_ONCE, cols] * (sig * (1.0 + value * (1.0 - sig)))
            for k in range(KCONV):
                totals[k] = totals[k] + jnp.sum(g * terms[k], axis=0, keepdims=True)
            totals[KCONV] = totals[KCONV] + jnp.sum(g, axis=0, keepdims=True)
            total = g * w[KCONV - 1 : KCONV]
            for k in range(KCONV - 1):
                total = total + up(g, after, KCONV - 1 - k) * w[k : k + 1]
            after = g[:8]
            out[at : at + ROWS_AT_ONCE, cols] = total.astype(BF16)
        for k in range(KCONV + 1):
            sums[k : k + 1, cols] = totals[k]


def conv_backward(projected, grad_mixed, weight, bias, held):
    length = projected.shape[0]
    width = CONV_TILES * LANES
    return pl.pallas_call(
        conv_backward_kernel,
        grid=(CONVCH // width,),
        out_shape=(shape(held.shape, BF16), shape((8, CONVCH), F32)),
        in_specs=[
            pl.BlockSpec((length, width), lambda i: (0, INNER // width + i)),
            pl.BlockSpec((length, width), lambda i: (0, i)),
            pl.BlockSpec((KCONV, width), lambda i: (0, i)),
            pl.BlockSpec((1, width), lambda i: (0, i)),
            ANY,
        ],
        out_specs=(
            pl.BlockSpec((length, width), lambda i: (0, INNER // width + i)),
            pl.BlockSpec((8, width), lambda i: (0, i)),
        ),
        input_output_aliases={4: 0},
        compiler_params=params(),
        cost_estimate=cost(12),
    )(projected, grad_mixed, weight, bias, held)


def loss_kernel(
    limit, mixed_out, w_out, tokens, teacher, mask, block_out, grad_result, grad_branch, error
):
    step = pl.program_id(0)

    @pl.when(step == 0)
    def _():
        error[...] = jnp.zeros_like(error)

    rows = tokens.shape[0]
    result = tokens[...].astype(F32) + dot(mixed_out[...], w_out[...])
    position = step * rows + lax.broadcasted_iota(jnp.int32, (rows, 1), 0)
    valid = (position < limit[0]).astype(F32)
    turned = jnp.broadcast_to(mask[...].astype(F32), (LANES, rows)).T
    weight = valid * turned[:, 0:1]
    block_out[...] = (result * valid).astype(BF16)
    misfit = result - teacher[...].astype(F32)
    pulled = 2.0 * weight * misfit
    grad_result[...] = pulled
    error[...] += jnp.sum(0.5 * pulled * misfit, axis=0, keepdims=True)
    grad_branch[...] = pulled.astype(BF16)


def loss_part(limit, mixed_out, w_out, tokens, teacher, mask):
    length = tokens.shape[0]
    rows = 256
    by_row = lambda width: pl.BlockSpec((rows, width), lambda i: (i, 0))
    return pl.pallas_call(
        loss_kernel,
        grid=(length // rows,),
        out_shape=(
            shape((length, D), BF16),
            shape((length, D), F32),
            shape((length, D), BF16),
            shape((1, D), F32),
        ),
        in_specs=[
            SMEM,
            by_row(INNER),
            pl.BlockSpec(w_out.shape, lambda i: (0, 0)),
            by_row(D),
            by_row(D),
            pl.BlockSpec((1, rows), lambda i: (0, i)),
        ],
        out_specs=(by_row(D), by_row(D), by_row(D), pl.BlockSpec((1, D), lambda i: (0, 0))),
        compiler_params=params(),
        cost_estimate=cost(8),
    )(limit, mixed_out, w_out, tokens, teacher, mask)


def gate_kernel(grad_branch, w_out, ssm, gate, gain, grad_ssm, grad_gate, gain_sums):
    @pl.when(pl.program_id(0) == 0)
    def _():
        gain_sums[...] = jnp.zeros_like(gain_sums)

    grad_mixed = dot(grad_branch[...], w_out[...], NT)
    g = gate[...]
    sig = sigmoid(g)
    act = g * sig
    inner = ssm[...]
    gated = inner * act
    rho = lax.rsqrt(jnp.mean(gated * gated, axis=1, keepdims=True) + NORM_EPS)
    unit = gated * rho
    gain_sums[...] += jnp.sum(unit * grad_mixed, axis=0, keepdims=True)
    grad_unit = grad_mixed * gain[...]
    share = jnp.mean(grad_unit * unit, axis=1, keepdims=True)
    grad_gated = rho * (grad_unit - unit * share)
    grad_ssm[...] = grad_gated * act
    grad_gate[...] = (grad_gated * inner * (sig * (1.0 + g * (1.0 - sig)))).astype(BF16)


def gate_part(grad_branch, w_out, ssm, projected, gain):
    length = ssm.shape[0]
    rows = 256
    by_row = lambda width: pl.BlockSpec((rows, width), lambda i: (i, 0))
    whole = lambda v: pl.BlockSpec(v.shape, lambda i: (0,) * v.ndim)
    return pl.pallas_call(
        gate_kernel,
        grid=(length // rows,),
        out_shape=(shape((length, INNER), F32), shape((length, WIDE), BF16), shape((1, INNER), F32)),
        in_specs=[by_row(D), whole(w_out), by_row(INNER), by_row(INNER), whole(gain)],
        out_specs=(by_row(INNER), by_row(INNER), pl.BlockSpec((1, INNER), lambda i: (0, 0))),
        compiler_params=params(),
        cost_estimate=cost(12),
    )(grad_branch, w_out, ssm, projected, gain)


def input_kernel(grad_low, w_in, tokens, norm_gain, grad_result, out, sums):
    @pl.when(pl.program_id(0) == 0)
    def _():
        sums[...] = jnp.zeros_like(sums)

    x = tokens[...].astype(F32)
    inverse = lax.rsqrt(jnp.mean(x * x, axis=1, keepdims=True) + NORM_EPS)
    unit = x * inverse
    grad_hidden = dot(grad_low[...], w_in[...], NT)
    sums[...] += jnp.sum(grad_hidden * unit, axis=0, keepdims=True)
    pulled = grad_hidden * norm_gain[...]
    share = jnp.mean(pulled * unit, axis=1, keepdims=True)
    out[...] = grad_result[...] + inverse * (pulled - unit * share)


def input_backward(grad_low, w_in, tokens, norm_gain, grad_result):
    length = tokens.shape[0]
    rows = 256
    by_row = lambda width: pl.BlockSpec((rows, width), lambda i: (i, 0))
    whole = lambda v: pl.BlockSpec(v.shape, lambda i: (0,) * v.ndim)
    return pl.pallas_call(
        input_kernel,
        grid=(length // rows,),
        out_shape=(shape((length, D), F32), shape((1, D), F32)),
        in_specs=[by_row(WIDE), whole(w_in), by_row(D), whole(norm_gain), by_row(D)],
        out_specs=(by_row(D), pl.BlockSpec((1, D), lambda i: (0, 0))),
        compiler_params=params(),
        cost_estimate=cost(15),
    )(grad_low, w_in, tokens, norm_gain, grad_result)


def vector_kernel(tail, conv_sums, sums, skip_sums, norm_sums, gate_sums, gather, out, taps):
    tiles = CONVCH // LANES
    out[...] = jnp.zeros_like(out)
    out[0:TAIL_ROWS, :] = tail[...]
    for k in range(KCONV):
        for i in range(tiles):
            taps[k * 16 + i : k * 16 + i + 1, :] = conv_sums[k : k + 1, i * LANES : (i + 1) * LANES]
    row = lax.broadcasted_iota(jnp.int32, (LANES, LANES), 0)
    col = lax.broadcasted_iota(jnp.int32, (LANES, LANES), 1)
    per_tile = LANES // KCONV

    def exact(v, chosen):
        high = v.astype(BF16)
        rest = v - high.astype(F32)
        middle = rest.astype(BF16)
        low = (rest - middle.astype(F32)).astype(BF16)
        return dot(high, chosen) + (dot(middle, chosen) + dot(low, chosen))

    for q in range(KCONV):
        total = jnp.zeros((tiles, LANES), F32)
        for k in range(KCONV):
            chosen = (col == KCONV * (row % per_tile) + k) & (row // per_tile == q)
            total = total + exact(taps[k * 16 : k * 16 + tiles, :], chosen.astype(BF16))
        out[pl.ds(TAIL_ROWS + q, tiles, stride=KCONV), :] = total
    bias_at = TAIL_ROWS + tiles * KCONV
    for i in range(tiles):
        out[bias_at + i : bias_at + i + 1, :] = conv_sums[KCONV : KCONV + 1, i * LANES : (i + 1) * LANES]
    lane = lax.broadcasted_iota(jnp.int32, (1, LANES), 1)
    skip = exact(jnp.broadcast_to(skip_sums[...], (8, INNER)), gather[...])[0:1, :]
    parts = [sums[0:1, :], sums[1:2, :], skip]
    parts = [jnp.where(lane < HEADS, v, 0.0) for v in parts]
    before = parts[0] + pltpu.roll(parts[1], HEADS, 1) + pltpu.roll(parts[2], 2 * HEADS, 1)
    at, shift = bias_at + tiles, 3 * HEADS
    for source in (norm_sums, gate_sums):
        for j in range(source.shape[1] // LANES):
            here = pltpu.roll(source[:, j * LANES : (j + 1) * LANES], shift, 1)
            out[at : at + 1, :] = jnp.where(lane < shift, before, here)
            before = here
            at += 1
    out[at : at + 1, :] = jnp.where(lane < shift, before, 0.0)


def pack_vectors(tail, conv_sums, sums, skip_sums, norm_sums, gate_sums, gather):
    return pl.pallas_call(
        vector_kernel,
        out_shape=shape(((NBLK - MID1) * BROWS, LANES), F32),
        in_specs=[VMEM] * 7,
        out_specs=VMEM,
        scratch_shapes=[pltpu.VMEM((KCONV * 16, LANES), F32)],
        compiler_params=params(),
    )(tail, conv_sums, sums, skip_sums, norm_sums, gate_sums, gather)


def body(tokens, teacher, lengths, loss_mask, owners, master, first_moment, second_moment):
    capacity = master.shape[0]
    dp, fsdp = lax.axis_size("dp"), lax.axis_size("fsdp")
    devices = dp * fsdp
    me = lax.axis_index(AXES).astype(jnp.int32)
    x_first, y_first, z_first = step_orders(dp, fsdp)
    tie = lambda *values: lax.optimization_barrier(values)

    sent = send_blocks(owners, master, devices, me)
    at_home = lax.all_to_all(sent, AXES, 0, 0, tiled=True)
    owners, tokens, loss_mask, _ = tie(owners, tokens, loss_mask, sent)
    plan = make_plan(owners, capacity, devices, me)
    streams = cut(even(plan["slots"], 3), (x_first, y_first, z_first))
    table = stream_places(plan["home"], plan["slot"], me, streams, devices)
    u0, u1 = plan["unit_slots"]
    sizes = [3 * u0 // 16] * 4
    unit_streams = cut(sizes + [u0 - sum(sizes)], (x_first, y_first, x_first, y_first, z_first))
    unit_table = stream_places(plan["unit_home"], plan["unit_slot"], me, unit_streams, devices)
    unit_table = unit_table[:MID0].reshape(-1)
    unit_table1 = place_of(plan["unit_home"] ^ me, x_first) * (u1 + 1) + plan["unit_slot"]
    unit_table1 = unit_table1[MID0:MID1].reshape(-1)
    inputs, target = tokens[0], teacher[0]
    position = jnp.arange(inputs.shape[0], dtype=jnp.int32)
    counted = jnp.sum(jnp.where(position < lengths[0], loss_mask[0], 0)).astype(F32)
    (at_home, table, unit_table, unit_table1, counted, received, back_table, row_from, row_block,
     row_used) = tie(
        at_home, table, unit_table, unit_table1, counted, plan["received"], plan["back"],
        plan["row_from"], plan["row_block"], plan["row_used"],
    )
    mine = pick_blocks(received, at_home, [size for _, size, _ in streams])
    parts = []
    for values, (_, _, order) in zip(mine, streams):
        parts += gather_steps(values, order)
    input_weight, output_weight, conv_weight, conv_bias, heads, skip, norm_gain, gate_gain = unpack(
        table, parts
    )
    dt_bias, a_log = heads[0:1], heads[1:2]
    gather = heads_gather()
    hidden, projected, mixed, ssm, mixed_out, states = forward(
        inputs, input_weight, norm_gain, conv_weight, conv_bias, dt_bias, a_log, skip, gate_gain
    )
    block_out, grad_result, grad_branch, errors = loss_part(
        lengths, mixed_out, output_weight, inputs, target, loss_mask
    )
    local = jnp.concatenate([errors.reshape(-1, LANES), jnp.broadcast_to(counted, (2, LANES))])
    keep1, send1, head, tail = pack_out(
        unit_table1, mixed_out, grad_branch, local, devices, u1 + 1
    )
    grad_branch, send1 = tie(grad_branch, send1)
    got1 = exchange(send1, x_first[0])
    grad_ssm, grad_low, grad_gate = gate_part(grad_branch, output_weight, ssm, projected, gate_gain)
    grad_ssm, keep1, got1 = tie(grad_ssm, keep1, got1)
    keep1, got1 = reduce_step(keep1, got1, x_first[1])
    grad_mixed, grad_low, sums, skip_sums = scan_backward(
        mixed, projected, ssm, grad_ssm, states, dt_bias, a_log, skip, gather, grad_low
    )
    grad_mixed, keep1, got1 = tie(grad_mixed, keep1, got1)
    steps1 = x_first[2:]
    for step in steps1[:1]:
        keep1, got1 = reduce_step(keep1, got1, step)
    grad_low, conv_sums = conv_backward(projected, grad_mixed, conv_weight, conv_bias, grad_low)
    grad_low, keep1, got1 = tie(grad_low, keep1, got1)
    for step in steps1[1:2]:
        keep1, got1 = reduce_step(keep1, got1, step)
    halves = []
    for _, size, _ in unit_streams:
        halves += [devices * size // 2] * 2
    packed = list(pack_in(unit_table, hidden, grad_low, head, halves))
    packed[0], keep1, got1 = tie(packed[0], keep1, got1)
    kept = packed[::2]
    got = [exchange(v, order[0]) for v, (_, _, order) in zip(packed[1::2], unit_streams)]
    *got, grad_low, conv_sums, tail = tie(*got, grad_low, conv_sums, tail)
    for i, (_, _, order) in enumerate(unit_streams):
        kept[i], got[i] = reduce_step(kept[i], got[i], order[1])
    for step in steps1[2:3]:
        keep1, got1 = reduce_step(keep1, got1, step)
    input_grad, norm_sums = input_backward(grad_low, input_weight, inputs, norm_gain, grad_result)
    grad_vec = pack_vectors(tail, conv_sums, sums, skip_sums, norm_sums, grad_gate, gather)
    grad_vec = grad_vec.reshape((NBLK - MID1) * UNITS, UNIT, LANES)
    *got, got1, grad_vec, input_grad = tie(*got, got1, grad_vec, input_grad)
    for step in steps1[3:]:
        keep1, got1 = reduce_step(keep1, got1, step)
    for k in range(2, len(x_first) - 2):
        for i, (_, _, order) in enumerate(unit_streams):
            if i == 0:
                kept[i], got[i], grad_vec = reduce_step(kept[i], got[i], order[k], grad_vec)
            else:
                kept[i], got[i] = reduce_step(kept[i], got[i], order[k])
    last = len(unit_streams) - 1
    pairs = list(zip(kept, got))
    stay, *given = given_all = fold(pairs[:last], grad_vec)
    arrived = exchange_quarters(given_all, x_first[-2:])
    end = fold(pairs[last:])
    end_arrived = exchange_quarters(end, z_first[-2:])
    n = stay.shape[0]
    back = units_to_owners(
        back_table, [[stay, *arrived], [end[0], *end_arrived], [keep1, got1]]
    )
    grad_vec = grad_vec + (arrived[0][n:] + (arrived[1][n:] + arrived[2][n:]))
    back, grad_vec = tie(back, grad_vec)
    returned = lax.all_to_all(back, AXES, 0, 0, tiled=True)
    for step in x_first[:2]:
        grad_vec = grad_vec + exchange(grad_vec, step)
    local_sums = keep1[u1] + got1[u1]
    error_sum = jnp.sum(local_sums[: D // LANES])
    divisor = local_sums[D // LANES, 0] * D
    new_first, new_second, new_master = adam(
        row_from,
        row_block,
        row_used,
        divisor,
        returned,
        grad_vec,
        master,
        first_moment,
        second_moment,
    )
    mean_loss = error_sum / divisor
    return (block_out[None], input_grad[None], mean_loss, new_first, new_second, new_master)


def solution(mesh):
    return jax.shard_map(
        body,
        mesh=mesh,
        in_specs=(
            P(AXES, None, None),
            P(AXES, None, None),
            P(AXES),
            P(AXES, None),
            P(),
            P(AXES, None),
            P(AXES, None),
            P(AXES, None),
        ),
        out_specs=(
            P(AXES, None, None),
            P(AXES, None, None),
            P(),
            P(AXES, None),
            P(AXES, None),
            P(AXES, None),
        ),
        check_vma=False,
    )
```

```python
from functools import partial

import jax
import jax.numpy as jnp
import numpy as np
from jax import lax
from jax.experimental import pallas as pl
from jax.experimental.pallas import tpu as pltpu
from jax.sharding import PartitionSpec as P

D = 768
INNER = 1536
NSTATE = 128
HEADDIM = 64
KCONV = 4
SCAN_LEN = 256
PBLOCK = 4096
STEP = 10
HEADS = 24
CONVCH = 1792
PROJ = 3352
PTOT = 3765320
NBLK = 920

LANES = 128
BROWS = PBLOCK // LANES
UNIT = 8
UNITS = BROWS // UNIT
END_IN = D * PROJ
END_OUT = END_IN + INNER * D
MID0 = -(-END_IN // PBLOCK)
MID1 = END_OUT // PBLOCK
N0 = MID0 + NBLK - MID1
N1 = MID1 - MID0
F0_ROWS = N0 * BROWS
IN_ROWS = END_IN // LANES
HEAD_ROWS = MID0 * BROWS - IN_ROWS
TAIL_ROWS = (END_OUT - MID1 * PBLOCK) // LANES
OUT_ROWS = INNER * D // LANES
VEC_ROWS = (NBLK - MID1) * BROWS - TAIL_ROWS
VEC_AT = MID0 * BROWS + TAIL_ROWS
GROUP = 16
GROUPS = D // GROUP
GROUP_ROWS = GROUP * PROJ // LANES
COL_TILES = -(-PROJ // LANES)
WIDE = COL_TILES * LANES
OUT_TILES = D // LANES

NORM_EPS = 1e-05
ADAM_EPS = 1e-08
BETA_ONE = 0.9
BETA_TWO = 0.999
MATRIX_RATE = 0.03
VECTOR_RATE = 0.2
WEIGHT_DECAY = 0.1
PRECISE = lax.Precision.HIGHEST
AXES = ("dp", "fsdp")
VMEM_LIMIT = 60 * 1024 * 1024


def bits_of(count):
    return count.bit_length() - 1


def step_orders(dp, fsdp):
    wide = [("dp", i) for i in range(bits_of(dp))]
    narrow = [("fsdp", i) for i in range(bits_of(fsdp))]
    first = wide[:2] + narrow + wide[2:]
    second = wide[:1] + narrow + wide[1:]
    third = wide[:1] + wide[2:] + wide[1:2] + narrow
    return first, second, third


def cut(sizes, orders):
    streams, at = [], 0
    for size, order in zip(sizes, orders):
        if size:
            streams.append((at, size, order))
        at += size
    return streams


def even(total, parts):
    return [total // parts + (i < total % parts) for i in range(parts)]


def exchange(values, *steps):
    axes = {axis for axis, _ in steps}
    if len(axes) == 1:
        (axis,) = axes
        mask = sum(1 << bit for _, bit in steps)
        pairs = [(i, i ^ mask) for i in range(lax.axis_size(axis))]
        return lax.ppermute(values, axis, pairs)
    low = bits_of(lax.axis_size("fsdp"))
    mask = sum(1 << (bit + (low if axis == "dp" else 0)) for axis, bit in steps)
    count = lax.axis_size("dp") * lax.axis_size("fsdp")
    return lax.ppermute(values, AXES, [(i, i ^ mask) for i in range(count)])


def place_of(relative, order):
    shift_of = {"dp": bits_of(lax.axis_size("fsdp")), "fsdp": 0}
    place = jnp.zeros_like(relative)
    for axis, bit in order:
        place = place * 2 + ((relative >> (shift_of[axis] + bit)) & 1)
    return place


def class_counts(owners, devices):
    block = jnp.arange(NBLK, dtype=jnp.int32)
    mid = ((block >= MID0) & (block < MID1))[None, :]
    device = jnp.arange(devices, dtype=jnp.int32)
    below = owners[None, :] < device[:, None]
    owned = owners[None, :] == device[:, None]

    def total(mask):
        return jnp.sum(mask.astype(jnp.int32), axis=1)

    start = (total(below & ~mid), total(below & mid))
    count = (total(owned & ~mid), total(owned & mid))
    return start, count, total(owned & (block < MID0)[None, :])


def my_counts(owners, me):
    block = jnp.arange(NBLK, dtype=jnp.int32)
    mid = (block >= MID0) & (block < MID1)
    below, owned = owners < me, owners == me
    total = lambda mask: jnp.sum(mask.astype(jnp.int32))
    start = (total(below & ~mid), total(below & mid))
    count = (total(owned & ~mid), total(owned & mid))
    return start, count, total(owned & (block < MID0))


def pair_lanes(capacity, devices):
    return -(-capacity // devices)


def make_plan(owners, capacity, devices, me):
    block = jnp.arange(NBLK, dtype=jnp.int32)
    mid = (block >= MID0) & (block < MID1)
    same = mid[:, None] == mid[None, :]
    before = (owners[None, :] < owners[:, None]) | (
        (owners[None, :] == owners[:, None]) & (block[None, :] < block[:, None])
    )
    order = jnp.sum(before.astype(jnp.int32), axis=1)
    order_in_class = jnp.sum((same & before).astype(jnp.int32), axis=1)
    home, slot = order % devices, order // devices
    device = jnp.arange(devices, dtype=jnp.int32)
    start, count, _ = class_counts(owners, devices)
    my_start, my_count, my_early = my_counts(owners, me)
    pair = pair_lanes(capacity, devices)

    slots = -(-NBLK // devices)
    wanted = me + devices * jnp.arange(slots, dtype=jnp.int32)
    first = start[0] + start[1]
    ends = first + count[0] + count[1]
    owner = jnp.sum((ends[None, :] <= wanted[:, None]).astype(jnp.int32), axis=1)
    owner = jnp.minimum(owner, devices - 1)
    base = jnp.sum(jnp.where(device[None, :] == owner[:, None], first[None, :], 0), axis=1)
    received = owner * pair + jnp.clip((wanted - base) // devices, 0, pair - 1)

    back_pair = (UNITS * capacity + 2 * (devices - 1)) // devices
    unit = UNITS * order_in_class[:, None] + jnp.arange(UNITS, dtype=jnp.int32)[None, :]
    unit_home, unit_slot = unit % devices, unit // devices
    unit_slots = (-(-UNITS * N0 // devices), -(-UNITS * N1 // devices))
    lane = jnp.arange(back_pair, dtype=jnp.int32)

    def units_back(kind):
        turn = lane if kind == 0 else back_pair - 1 - lane
        first = UNITS * start[kind][:, None]
        k = (me - first) % devices + turn[None, :] * devices
        return k < UNITS * count[kind][:, None], (first + k) // devices

    valid0, slot0 = units_back(0)
    valid1, slot1 = units_back(1)
    back = jnp.where(valid0, slot0, jnp.where(valid1, unit_slots[0] + slot1, 0)).reshape(-1)

    row = jnp.arange(capacity, dtype=jnp.int32)
    is_mid = (row >= my_early) & (row < my_early + my_count[1])
    k = jnp.where(is_mid, row - my_early, jnp.where(row < my_early, row, row - my_count[1]))
    first = UNITS * jnp.where(is_mid, my_start[1], my_start[0])
    k = UNITS * k[:, None] + jnp.arange(UNITS, dtype=jnp.int32)[None, :]
    turn = k // devices
    row_from = ((first[:, None] + k) % devices) * back_pair + jnp.where(
        is_mid[:, None], back_pair - 1 - turn, turn
    )
    row_used = row < my_count[0] + my_count[1]
    mine = (owners == me)[None, :]
    rank = jnp.sum((mine & (block[None, :] < block[:, None])).astype(jnp.int32), axis=1)
    row_block = jnp.sum(
        jnp.where(mine & (rank[None, :] == row[:, None]), block[None, :], 0), axis=1
    )
    late = devices * back_pair + UNITS * (row_block - MID1)
    late = late[:, None] + jnp.arange(UNITS, dtype=jnp.int32)[None, :]
    row_from = jnp.where((row_block >= MID1)[:, None], late, row_from)
    row_from = jnp.where(row_used[:, None], row_from, 0).reshape(-1)
    return dict(
        home=home, slot=slot, slots=slots,
        received=received, unit_home=unit_home, unit_slot=unit_slot,
        unit_slots=unit_slots, back=back, row_from=row_from,
        row_used=row_used, row_block=row_block,
    )


def stream_places(home, slot, me, streams, devices):
    relative = home ^ me
    place = jnp.zeros_like(slot)
    for begin, size, order in streams:
        inside = (slot >= begin) & (slot < begin + size)
        at = devices * begin + place_of(relative, order) * size + slot - begin
        place = jnp.where(inside, at, place)
    return place


def cost(microseconds):
    return pl.CostEstimate(
        flops=int(microseconds * 1e9), bytes_accessed=int(microseconds * 3e6), transcendentals=0
    )


ANY = pl.BlockSpec(memory_space=pl.ANY)
VMEM = pl.BlockSpec(memory_space=pltpu.VMEM)
SMEM = pl.BlockSpec(memory_space=pltpu.SMEM)


def params(**extra):
    return pltpu.CompilerParams(vmem_limit_bytes=VMEM_LIMIT, **extra)


def shape(dims, dtype):
    return jax.ShapeDtypeStruct(dims, dtype)


def send_kernel(my_index, owners, master, out, flat, *, devices):
    capacity = master.shape[0]
    me = my_index[0]
    for j in range(BROWS):
        flat[pl.ds(j, capacity, stride=BROWS), :] = master[:, j * LANES : (j + 1) * LANES]
    held = owners[...]
    below, owned = held < me, held == me

    def total(mask):
        return jnp.sum(jnp.where(mask, 1.0, 0.0)).astype(jnp.int32)

    start, count = total(below), total(owned)
    pair = out.shape[0] // devices

    def step(home, carry):
        for s in range(pair):
            k = lax.rem(home - start + devices * NBLK, devices) + s * devices
            row = jnp.where(k < count, k, 0)
            rows = pl.ds(pl.multiple_of(row * BROWS, BROWS), BROWS)
            out[home * pair + s] = flat[rows, :].astype(out.dtype)
        return carry

    lax.fori_loop(0, devices, step, 0)


def send_blocks(owners, master, devices, me):
    rows = -(-NBLK // (8 * LANES)) * 8
    held = jnp.pad(owners, (0, rows * LANES - NBLK), constant_values=1 << 20).reshape(rows, LANES)
    count = devices * pair_lanes(master.shape[0], devices)
    return pl.pallas_call(
        partial(send_kernel, devices=devices),
        out_shape=shape((count, BROWS, LANES), jnp.bfloat16),
        in_specs=[SMEM, VMEM, VMEM],
        out_specs=VMEM,
        scratch_shapes=[pltpu.VMEM((master.shape[0] * BROWS, LANES), jnp.float32)],
        compiler_params=params(),
    )(me.reshape(1), held, master)


def pick_kernel(table, source, *outs):
    at = 0
    for out in outs:

        def step(i, carry, out=out, at=at):
            out[i] = source[table[at + i]]
            return carry

        lax.fori_loop(0, out.shape[0], step, 0)
        at += out.shape[0]


def pick_blocks(table, source, sizes):
    return pl.pallas_call(
        pick_kernel,
        out_shape=tuple(shape((n,) + source.shape[1:], source.dtype) for n in sizes),
        in_specs=[SMEM, VMEM],
        out_specs=(VMEM,) * len(sizes),
        compiler_params=params(),
    )(table, source)


def back_kernel(table, *refs, sizes):
    sources, (out, held) = refs[:-2], refs[-2:]
    at = i = 0
    for size in sizes:
        n = sources[i].shape[0]
        total = sources[i][...]
        for k in range(1, size):
            total = total + sources[i + k][0:n]
        held[at : at + n] = total
        at += n
        i += size

    def step(i, carry):
        for u in range(8):
            out[i * 8 + u] = held[table[i * 8 + u]]
        return carry

    total = out.shape[0]
    lax.fori_loop(0, total // 8, step, 0)


def units_to_owners(table, groups):
    return pl.pallas_call(
        partial(back_kernel, sizes=[len(g) for g in groups]),
        out_shape=shape((table.shape[0], UNIT, LANES), jnp.float32),
        in_specs=[SMEM] + [VMEM] * sum(len(g) for g in groups),
        out_specs=VMEM,
        scratch_shapes=[pltpu.VMEM((sum(g[0].shape[0] for g in groups), UNIT, LANES), jnp.float32)],
        compiler_params=params(),
    )(table, *[v for g in groups for v in g])


def fold_kernel(*refs, sizes, extra):
    sources, outs = refs[: sum(sizes) + extra], refs[sum(sizes) + extra :]
    at = i = 0
    for size in sizes:
        n = sources[i].shape[0] // 4
        for p in range(4):
            rows = slice(p * n, (p + 1) * n)
            total = sources[i][rows]
            for k in range(1, size):
                total = total + sources[i + k][rows]
            outs[p][at : at + n] = total
        at += n
        i += size
    if extra:
        for p in range(1, 4):
            outs[p][at:] = sources[-1][...]


def fold(groups, extra=None):
    n = sum(g[0].shape[0] // 4 for g in groups)
    more = 0 if extra is None else extra.shape[0]
    values = [v for g in groups for v in g] + ([] if extra is None else [extra])
    return pl.pallas_call(
        partial(fold_kernel, sizes=[len(g) for g in groups], extra=int(extra is not None)),
        out_shape=[shape((n + (more if p else 0), UNIT, LANES), jnp.float32) for p in range(4)],
        in_specs=[VMEM] * len(values),
        out_specs=[VMEM] * 4,
        compiler_params=params(),
    )(*values)


def exchange_quarters(given, steps):
    return [exchange(given[1], steps[1]), exchange(given[2], steps[0]), exchange(given[3], *steps)]


def row_start(rho):
    return (PROJ * rho) // LANES, (PROJ * rho) % LANES


def copy_all(pairs, sem):
    copies = [pltpu.make_async_copy(a, b, sem.at[i]) for i, (a, b) in enumerate(pairs)]
    for c in copies:
        c.start()
    for c in copies:
        c.wait()


def spread_blocks(table, first, held, flat, count, first_row):
    def one(i):
        at = pl.multiple_of(first_row + i * BROWS, 16)
        flat[pl.ds(at, BROWS), :] = held[table[first + i]].astype(jnp.float32)

    def step(i, carry):
        for u in range(4):
            one(i * 4 + u)
        return carry

    lax.fori_loop(0, count // 4, step, 0)
    for i in range(count // 4 * 4, count):
        one(i)


def unpack_vectors(flat, conv_weight, conv_bias, dt_bias, a_log, skip, norm_gain, gate_gain):
    bf16, f32 = jnp.bfloat16, jnp.float32
    tiles = CONVCH // LANES
    row = lax.broadcasted_iota(jnp.int32, (LANES, LANES), 0)
    col = lax.broadcasted_iota(jnp.int32, (LANES, LANES), 1)
    per_tile = LANES // KCONV
    for k in range(KCONV):
        total = jnp.zeros((tiles, LANES), f32)
        for q in range(KCONV):
            rows = flat[pl.ds(VEC_AT + q, tiles, stride=KCONV), :].astype(bf16)
            chosen = (row == KCONV * (col % per_tile) + k) & (col // per_tile == q)
            total = total + jnp.dot(rows, chosen.astype(bf16), preferred_element_type=f32)
        for i in range(tiles):
            conv_weight[k : k + 1, i * LANES : (i + 1) * LANES] = total[i : i + 1, :]
    bias_at = VEC_AT + tiles * KCONV
    for i in range(tiles):
        conv_bias[:, i * LANES : (i + 1) * LANES] = flat[bias_at + i : bias_at + i + 1, :]
    at = bias_at + tiles
    lane = lax.broadcasted_iota(jnp.int32, (8, LANES), 1)
    first = flat[at : at + 8, :]
    three = []
    for i in range(3):
        moved = pltpu.roll(first, LANES - i * HEADS, 1) if i else first
        three.append(jnp.where(lane < HEADS, moved, 0.0))
    dt_bias[...] = three[0][0:1, :]
    a_log[...] = three[1][0:1, :]
    for j in range(INNER // LANES):
        h = lax.broadcasted_iota(jnp.int32, (LANES, LANES), 0)
        c = lax.broadcasted_iota(jnp.int32, (LANES, LANES), 1) + j * LANES
        spread = (h == c // HEADDIM).astype(bf16)
        wide = jnp.dot(three[2].astype(bf16), spread, preferred_element_type=f32)
        skip[:, j * LANES : (j + 1) * LANES] = wide[0:1, :]
    shift = 3 * HEADS
    for out, begin, width in ((norm_gain, at, D), (gate_gain, at + D // LANES, INNER)):
        for j in range(width // LANES):
            x = pltpu.roll(flat[begin + j : begin + j + 1, :], LANES - shift, 1)
            y = pltpu.roll(flat[begin + j + 1 : begin + j + 2, :], LANES - shift, 1)
            out[:, j * LANES : (j + 1) * LANES] = jnp.where(lane[0:1] < LANES - shift, x, y)


def unpack_kernel(table, *refs):
    parts, outs, scratch = refs[:-14], refs[-14:-5], refs[-5:]
    w_in, w_out, *vectors = outs
    held, flat, flat_out, tile, sem = scratch
    pairs, at = [], 0
    for part in parts:
        pairs.append((part, held.at[pl.ds(at, part.shape[0])]))
        at += part.shape[0]
    copy_all(pairs, sem)
    spread_blocks(table, 0, held, flat, MID0, 0)
    spread_blocks(table, MID1, held, flat, NBLK - MID1, MID0 * BROWS)
    spread_blocks(table, MID0, held, flat_out, N1, HEAD_ROWS)
    flat_out[0:HEAD_ROWS, :] = flat[IN_ROWS : IN_ROWS + HEAD_ROWS, :]
    flat_out[OUT_ROWS - TAIL_ROWS :, :] = flat[MID0 * BROWS : MID0 * BROWS + TAIL_ROWS, :]
    unpack_vectors(flat, *vectors)
    rows = 128

    def out_step(i, carry):
        at = pl.multiple_of(i * rows, rows)
        for j in range(OUT_TILES):
            x = flat_out[pl.ds(at * OUT_TILES + j, rows, stride=OUT_TILES), :]
            w_out[pl.ds(at, rows), j * LANES : (j + 1) * LANES] = x.astype(jnp.bfloat16)
        return carry

    lax.fori_loop(0, INNER // rows, out_step, 0)
    lane = lax.broadcasted_iota(jnp.int32, (GROUPS, LANES), 1)

    def columns(j):
        for rho in range(GROUP):
            c, s = row_start(rho)
            x = flat[pl.ds(c + j, GROUPS, stride=GROUP_ROWS), :]
            if s:
                y = flat[pl.ds(c + j + 1, GROUPS, stride=GROUP_ROWS), :]
                x = jnp.where(
                    lane < LANES - s,
                    pltpu.roll(x, LANES - s, 1),
                    pltpu.roll(y, LANES - s, 1),
                )
            tile[pl.ds(rho, GROUPS, stride=GROUP), :] = x

    def step(j, carry):
        columns(j)
        w_in[:, pl.ds(pl.multiple_of(j * LANES, LANES), LANES)] = tile[...].astype(jnp.bfloat16)
        return carry

    lax.fori_loop(0, COL_TILES - 1, step, 0)
    columns(COL_TILES - 1)
    last = (COL_TILES - 1) * LANES
    inside = lax.broadcasted_iota(jnp.int32, (D, LANES), 1) < PROJ - last
    w_in[:, last:] = jnp.where(inside, tile[...], 0.0).astype(jnp.bfloat16)


def unpack(table, parts):
    held = sum(part.shape[0] for part in parts)
    f32 = jnp.float32
    return pl.pallas_call(
        unpack_kernel,
        out_shape=(
            shape((D, WIDE), jnp.bfloat16),
            shape((INNER, D), jnp.bfloat16),
            shape((KCONV, CONVCH), f32),
            shape((1, CONVCH), f32),
            shape((1, LANES), f32),
            shape((1, LANES), f32),
            shape((1, INNER), f32),
            shape((1, D), f32),
            shape((1, INNER), f32),
        ),
        in_specs=[SMEM] + [ANY] * len(parts),
        out_specs=(VMEM,) * 9,
        scratch_shapes=[
            pltpu.VMEM((held, BROWS, LANES), jnp.bfloat16),
            pltpu.VMEM((F0_ROWS, LANES), f32),
            pltpu.VMEM((OUT_ROWS, LANES), f32),
            pltpu.VMEM((D, LANES), f32),
            pltpu.SemaphoreType.DMA((len(parts),)),
        ],
        compiler_params=params(),
        cost_estimate=cost(20),
    )(table, *parts)


def permute_units(table, flat, count, first_row, staged):
    many = 16

    def step(i, carry):
        for u in range(many):
            at = pl.multiple_of(first_row + (i * many + u) * UNIT, UNIT)
            staged[table[i * many + u]] = flat[pl.ds(at, UNIT), :]
        return carry

    lax.fori_loop(0, count // many, step, 0)
    for i in range(count // many * many, count):
        staged[table[i]] = flat[first_row + i * UNIT : first_row + (i + 1) * UNIT, :]


def pack_in_kernel(table, hidden, grad, head, *refs):
    outs, (turned, tiles, flat, staged, sem) = refs[:-5], refs[-5:]
    turned[...] = hidden[...].T
    lane = lax.broadcasted_iota(jnp.int32, (GROUPS, LANES), 1)

    def product(p, count):
        at = p * 2 * LANES
        at = at if isinstance(at, int) else pl.multiple_of(at, 2 * LANES)
        return jnp.dot(
            turned[...], grad[:, pl.ds(at, count * LANES)], preferred_element_type=jnp.float32
        )

    def put(p, value):
        for k in range(value.shape[1] // LANES):
            at = (p * 2 + k) * D
            at = at if isinstance(at, int) else pl.multiple_of(at, D)
            tiles[pl.ds(at, D), :] = value[:, k * LANES : (k + 1) * LANES]

    def load(rho, j):
        return tiles[pl.ds(j * D + rho, GROUPS, stride=GROUP), :]

    def whole(rho, i):
        first = -(-PROJ * rho // LANES)
        col0 = first * LANES - PROJ * rho
        x = load(rho, i)
        if col0:
            x = jnp.where(
                lane < LANES - col0,
                pltpu.roll(x, LANES - col0, 1),
                pltpu.roll(load(rho, i + 1), LANES - col0, 1),
            )
        flat[pl.ds(first + i, GROUPS, stride=GROUP_ROWS), :] = x

    put(0, product(0, 2))
    put(1, product(1, 2))
    pairs = COL_TILES // 2

    def step(p, carry):
        for i in range(2):
            for rho in range(GROUP):
                whole(rho, p * 2 + i)
        put(p + 2, product(p + 2, 2))
        return carry

    lax.fori_loop(0, pairs - 2, step, 0)
    put(pairs, product(pairs, COL_TILES % 2))
    for rho in range(GROUP):
        first = -(-PROJ * rho // LANES)
        col0 = first * LANES - PROJ * rho
        full = (PROJ - col0) // LANES
        for i in range((pairs - 2) * 2, full):
            whole(rho, i)
        left = PROJ - col0 - full * LANES
        if left:
            begin = col0 + full * LANES
            j, s = begin // LANES, begin % LANES
            x = pltpu.roll(load(rho, j), LANES - s, 1) if s else load(rho, j)
            if s + left > LANES:
                x = jnp.where(lane < LANES - s, x, pltpu.roll(load(rho, j + 1), LANES - s, 1))
            y = pltpu.roll(load(rho + 1, 0), left, 1)
            flat[pl.ds(first + full, GROUPS, stride=GROUP_ROWS), :] = jnp.where(lane < left, x, y)
    flat[IN_ROWS : IN_ROWS + HEAD_ROWS, :] = head[...]
    permute_units(table, flat, MID0 * UNITS, 0, staged)
    copies, at = [], 0
    for out in outs:
        copies.append((staged.at[pl.ds(at, out.shape[0])], out))
        at += out.shape[0]
    copy_all(copies, sem)


def pack_in(table, hidden, grad, head, sizes):
    return pl.pallas_call(
        pack_in_kernel,
        out_shape=tuple(shape((n, UNIT, LANES), jnp.float32) for n in sizes),
        in_specs=[SMEM, VMEM, VMEM, VMEM],
        out_specs=(ANY,) * len(sizes),
        scratch_shapes=[
            pltpu.VMEM((D, hidden.shape[0]), jnp.bfloat16),
            pltpu.VMEM((COL_TILES * D, LANES), jnp.float32),
            pltpu.VMEM((MID0 * BROWS, LANES), jnp.float32),
            pltpu.VMEM((sum(sizes), UNIT, LANES), jnp.float32),
            pltpu.SemaphoreType.DMA((len(sizes),)),
        ],
        compiler_params=params(),
        cost_estimate=cost(20),
    )(table, hidden, grad, head)


def pack_out_kernel(
    table, mixed_out, grad, local, keep, send, head, tail, turned, flat, out, sem, *, slots
):
    rows = 256

    def step(i, carry):
        at = pl.multiple_of(i * rows, rows)
        turned[...] = mixed_out[:, pl.ds(at, rows)].T
        product = jnp.dot(turned[...], grad[...], preferred_element_type=jnp.float32)
        for j in range(OUT_TILES):
            flat[pl.ds(at * OUT_TILES + j, rows, stride=OUT_TILES), :] = product[
                :, j * LANES : (j + 1) * LANES
            ]
        return carry

    lax.fori_loop(0, INNER // rows, step, 0)
    head[...] = flat[0:HEAD_ROWS, :]
    tail[...] = flat[OUT_ROWS - TAIL_ROWS : OUT_ROWS, :]
    permute_units(table, flat, N1 * UNITS, HEAD_ROWS, out)

    def add_local(i, carry):
        out[i * slots + slots - 1] = local[...]
        return carry

    lax.fori_loop(0, out.shape[0] // slots, add_local, 0)
    half = keep.shape[0]
    copy_all([(out.at[pl.ds(0, half)], keep), (out.at[pl.ds(half, half)], send)], sem)


def pack_out(table, mixed_out, grad, local, devices, slots):
    return pl.pallas_call(
        partial(pack_out_kernel, slots=slots),
        out_shape=(
            shape((devices * slots // 2, UNIT, LANES), jnp.float32),
            shape((devices * slots // 2, UNIT, LANES), jnp.float32),
            shape((HEAD_ROWS, LANES), jnp.float32),
            shape((TAIL_ROWS, LANES), jnp.float32),
        ),
        in_specs=[SMEM, VMEM, VMEM, VMEM],
        out_specs=(ANY, ANY, VMEM, VMEM),
        scratch_shapes=[
            pltpu.VMEM((256, mixed_out.shape[0]), jnp.bfloat16),
            pltpu.VMEM((OUT_ROWS, LANES), jnp.float32),
            pltpu.VMEM((devices * slots, UNIT, LANES), jnp.float32),
            pltpu.SemaphoreType.DMA((2,)),
        ],
        compiler_params=params(),
    )(table, mixed_out, grad, local)


def adam_kernel(
    table, row_block, row_used, scale, got, late, master, first, second,
    o_first, o_second, o_master, flat, held, limit, used,
):
    capacity = master.shape[0]

    def step(i, carry):
        for u in range(UNITS):
            at = table[i * UNITS + u]
            rows = pl.ds(pl.multiple_of(i * BROWS + u * UNIT, UNIT), UNIT)
            flat[rows, :] = held[at]
        limit[pl.ds(i, 1), :] = jnp.full((1, LANES), END_OUT - row_block[i] * PBLOCK, jnp.int32)
        used[pl.ds(i, 1), :] = jnp.full((1, LANES), row_used[i], jnp.int32)
        return carry

    held[0 : got.shape[0]] = got[...]
    held[got.shape[0] :] = late[...]
    lax.fori_loop(0, capacity, step, 0)
    lane = lax.broadcasted_iota(jnp.int32, (capacity, LANES), 1)
    divisor = scale[0]
    for j in range(BROWS):
        cols = slice(j * LANES, (j + 1) * LANES)
        grad = jnp.where(used[...] > 0, flat[pl.ds(j, capacity, stride=BROWS), :], 0.0) / divisor
        matrix = lane + j * LANES < limit[...]
        weights = master[:, cols]
        new_first = BETA_ONE * first[:, cols] + (1.0 - BETA_ONE) * grad
        new_second = BETA_TWO * second[:, cols] + (1.0 - BETA_TWO) * grad * grad
        normal = (
            new_first
            / (1.0 - BETA_ONE**STEP)
            / (jnp.sqrt(new_second / (1.0 - BETA_TWO**STEP)) + ADAM_EPS)
        )
        rate = jnp.where(matrix, MATRIX_RATE, VECTOR_RATE)
        decay = jnp.where(matrix, WEIGHT_DECAY, 0.0)
        o_first[:, cols] = new_first
        o_second[:, cols] = new_second
        o_master[:, cols] = weights - rate * (normal + decay * weights)


def adam(table, row_block, row_used, divisor, got, late, master, first, second):
    capacity = master.shape[0]
    return pl.pallas_call(
        adam_kernel,
        out_shape=(shape(master.shape, jnp.float32),) * 3,
        in_specs=[SMEM] * 4 + [VMEM] * 5,
        out_specs=(VMEM,) * 3,
        scratch_shapes=[
            pltpu.VMEM((capacity * BROWS, LANES), jnp.float32),
            pltpu.VMEM((got.shape[0] + late.shape[0], UNIT, LANES), jnp.float32),
            pltpu.VMEM((capacity, LANES), jnp.int32),
            pltpu.VMEM((capacity, LANES), jnp.int32),
        ],
        compiler_params=params(),
    )(
        table, row_block, row_used.astype(jnp.int32), divisor.reshape(1), got, late, master, first, second
    )


def doubled(values, step):
    return jnp.concatenate([values, exchange(values, step)], axis=0)


def gather_steps(values, order):
    for step in order[:0:-1]:
        values = doubled(values, step)
    return values, exchange(values, order[0])


def reduce_step(kept, got, step, extra=None):
    half = kept.shape[0] // 2
    given = kept[half:] + got[half:]
    if extra is None:
        return kept[:half] + got[:half], exchange(given, step)
    arrived = exchange(jnp.concatenate([given, extra]), step)
    return kept[:half] + got[:half], arrived[:half], extra + arrived[half:]


CHUNK = 128
PAIRS = HEADS // 2
MIXW = INNER + 2 * NSTATE
DT_AT = INNER + CONVCH
F32 = jnp.float32
BF16 = jnp.bfloat16
NN = (((1,), (0,)), ((), ()))
NT = (((1,), (1,)), ((), ()))


def dot(a, b, dims=NN):
    return lax.dot_general(a, b, dims, preferred_element_type=F32)


def split(v):
    high = v.astype(BF16)
    return high, (v - high.astype(F32)).astype(BF16)


def dot3(a, b, dims=NN):
    ah, al = a
    bh, bl = b
    return dot(ah, bh, dims) + (dot(ah, bl, dims) + dot(al, bh, dims))


def heads_gather():
    return jnp.asarray(np.repeat(np.eye(HEADS, LANES, dtype=np.float32), HEADDIM, axis=0), BF16)


def three_parts(v):
    high = v.astype(BF16).astype(F32)
    rest = v - high
    middle = rest.astype(BF16).astype(F32)
    low = rest - middle
    return (high + pltpu.roll(middle, 32, 1) + pltpu.roll(low, 64, 1)).astype(BF16)


def triangle_sum(tri, v):
    parts = dot(tri, three_parts(v))
    lane = lax.broadcasted_iota(jnp.int32, parts.shape, 1)
    total = parts + pltpu.roll(parts, LANES - 32, 1) + pltpu.roll(parts, LANES - 64, 1)
    return jnp.where(lane < HEADS, total, 0.0)


def chunk_decays(dt, dt_bias, a_log):
    lane = lax.broadcasted_iota(jnp.int32, (CHUNK, LANES), 1)
    row = lax.broadcasted_iota(jnp.int32, (CHUNK, LANES), 0)
    shifted = dt + dt_bias
    delta = jnp.where(
        lane < HEADS, jnp.maximum(shifted, 0.0) + jnp.log1p(jnp.exp(-jnp.abs(shifted))), 0.0
    )
    rate = -jnp.exp(a_log)
    lower = (row >= lane).astype(BF16)
    cum = triangle_sum(lower, delta * rate)
    last = cum[CHUNK - 1 : CHUNK, :]
    return shifted, delta, rate, cum, last


def pair_mask():
    lane = lax.broadcasted_iota(jnp.int32, (CHUNK, LANES), 1)
    low = (lane < HEADDIM).astype(F32)
    return low.astype(BF16), (1.0 - low).astype(BF16)


QUADS = HEADS // 4
QWIDTH = 4 * HEADDIM


def sigmoid(v):
    return 0.5 * jnp.tanh(0.5 * v) + 0.5


def silu(v):
    return v * sigmoid(v)


def side_by_side(v):
    high, low = split(v)
    return jnp.concatenate([high, low], axis=1), high


def dot_parts(a, b):
    ahl, ah = a
    bh, bl = b
    return dot(ahl, jnp.concatenate([bh, bh], axis=0)) + dot(ah, bl)


def dot_turned(a, b):
    ah, al = a
    bh, bl = b
    both = dot(ah, jnp.concatenate([bh, bl], axis=0), NT)
    n = bh.shape[0]
    return both[:, :n] + both[:, n:] + dot(al, bh, NT)


def widen(delta, cum, quad):
    lane = lax.broadcasted_iota(jnp.int32, (CHUNK, LANES), 1)
    over = lambda v, h: jnp.broadcast_to(v[:, h : h + 1], (CHUNK, LANES))
    first = 4 * quad
    columns = [over(cum, first + k) for k in range(4)]
    rates = [over(delta, first + k) for k in range(4)]
    pair = lambda vs: jnp.concatenate(
        [jnp.where(lane < HEADDIM, vs[0], vs[1]), jnp.where(lane < HEADDIM, vs[2], vs[3])], axis=1
    )
    return pair(rates), pair(columns), columns


def pair_rows(parts, j, low, high):
    cols = slice(j * LANES, (j + 1) * LANES)
    return [jnp.concatenate([p[:, cols] * low, p[:, cols] * high], axis=0) for p in parts]


def scan_chunk(mixed, dt, dt_bias, a_log, skip, state, put):
    _, delta, _, cum, last = chunk_decays(dt, dt_bias, a_log)
    lane = lax.broadcasted_iota(jnp.int32, (CHUNK, LANES), 1)
    row = lax.broadcasted_iota(jnp.int32, (CHUNK, LANES), 0)
    bias = jnp.where(row >= lane, 0.0, -1e30)
    cum_t = cum.T
    inputs_b = mixed[:, INNER : INNER + NSTATE]
    readout = mixed[:, INNER + NSTATE :]
    affinity = dot3(split(readout), split(inputs_b), NT)
    readout_parts = side_by_side(readout)
    b_parts = side_by_side(inputs_b.T)
    low, high = pair_mask()
    for quad in range(QUADS):
        cols = slice(quad * QWIDTH, (quad + 1) * QWIDTH)
        wide_delta, wide_cum, columns = widen(delta, cum, quad)
        values = mixed[:, cols]
        scaled = values * wide_delta
        parts = split(scaled)
        outs = []
        for j in range(2):
            right_h, right_l = pair_rows(parts, j, low, high)
            left = []
            for k in range(2):
                h = 4 * quad + 2 * j + k
                within = jnp.exp(columns[2 * j + k] - cum_t[h : h + 1, :] + bias)
                left.append(split(affinity * within))
            left_h = jnp.concatenate([left[0][0], left[1][0]], axis=1)
            left_l = jnp.concatenate([left[0][1], left[1][1]], axis=1)
            both = dot(left_h, jnp.concatenate([right_h, right_l], axis=1))
            outs.append(both[:, :LANES] + both[:, LANES:] + dot(left_l, right_h))
        carried = state[:, cols]
        grown = jnp.exp(wide_cum)
        out = jnp.concatenate(outs, axis=1) + dot_parts(readout_parts, split(carried)) * grown
        tail = jnp.exp(wide_cum[CHUNK - 1 :] - wide_cum)
        state[:, cols] = carried * grown[CHUNK - 1 :] + dot_parts(b_parts, split(scaled * tail))
        put(quad, out + skip[:, cols] * values)


FORWARD_ROWS = 2 * CHUNK


def forward_kernel(
    tokens, w_in, norm_gain, conv_weight, conv_bias, dt_bias, a_log, skip, gain,
    hidden, projected, mixed, ssm, mixed_out, states, state, before,
):
    @pl.when(pl.program_id(0) == 0)
    def _():
        state[...] = jnp.zeros_like(state)
        before[...] = jnp.zeros_like(before)

    x = tokens[...].astype(F32)
    inverse = lax.rsqrt(jnp.mean(x * x, axis=1, keepdims=True) + NORM_EPS)
    h = (x * inverse * norm_gain[...]).astype(BF16)
    hidden[...] = h
    projected[:, DT_AT:] = dot(h, w_in[:, DT_AT:])
    wide = 2 * LANES
    for tile in range(CONVCH // wide):
        at = tile * wide
        product = dot(h, w_in[:, INNER + at : INNER + at + wide])
        projected[:, INNER + at : INNER + at + wide] = product
        for half in range(2):
            cols = slice(at + half * LANES, at + (half + 1) * LANES)
            rows = product[:, half * LANES : (half + 1) * LANES]
            earlier = before[:, cols]
            terms = [down(rows, earlier, KCONV - 1 - k) for k in range(KCONV - 1)] + [rows]
            before[:, cols] = rows[FORWARD_ROWS - 8 :]
            mixed[:, cols] = silu(conv_sum(terms, conv_weight[:, cols], conv_bias[:, cols]))
    for tile in range(INNER // wide):
        cols = slice(tile * wide, (tile + 1) * wide)
        projected[:, cols] = dot(h, w_in[:, cols])
    for sub in range(FORWARD_ROWS // CHUNK):
        rows = slice(sub * CHUNK, (sub + 1) * CHUNK)
        states[sub] = state[...]
        squares = [jnp.zeros((CHUNK, LANES), F32)]

        def put(quad, out, rows=rows, squares=squares):
            cols = slice(quad * QWIDTH, (quad + 1) * QWIDTH)
            ssm[rows, cols] = out
            gated = out * silu(projected[rows, cols])
            first, second = gated[:, :LANES], gated[:, LANES:]
            squares[0] = squares[0] + first * first + second * second

        scan_chunk(
            mixed[rows, :], projected[rows, DT_AT:], dt_bias[...], a_log[...], skip, state, put
        )
        rho = lax.rsqrt(jnp.sum(squares[0], axis=1, keepdims=True) * (1.0 / INNER) + NORM_EPS)
        for j in range(PAIRS):
            cols = slice(j * LANES, (j + 1) * LANES)
            gated = ssm[rows, cols] * silu(projected[rows, cols])
            mixed_out[rows, cols] = (gated * rho * gain[:, cols]).astype(BF16)


def forward(tokens, w_in, norm_gain, conv_weight, conv_bias, dt_bias, a_log, skip, gain):
    length = tokens.shape[0]
    by_row = lambda width: pl.BlockSpec((FORWARD_ROWS, width), lambda i: (i, 0))
    whole = lambda v: pl.BlockSpec(v.shape, lambda i: (0,) * v.ndim)
    per_step = FORWARD_ROWS // CHUNK
    return pl.pallas_call(
        forward_kernel,
        grid=(length // FORWARD_ROWS,),
        out_shape=(
            shape((length, D), BF16),
            shape((length, WIDE), F32),
            shape((length, MIXW), F32),
            shape((length, INNER), F32),
            shape((length, INNER), BF16),
            shape((length // CHUNK, NSTATE, INNER), F32),
        ),
        in_specs=[by_row(D)]
        + [
            whole(v)
            for v in (w_in, norm_gain, conv_weight, conv_bias, dt_bias, a_log, skip, gain)
        ],
        out_specs=(
            by_row(D),
            by_row(WIDE),
            by_row(MIXW),
            by_row(INNER),
            by_row(INNER),
            pl.BlockSpec((per_step, NSTATE, INNER), lambda i: (i, 0, 0)),
        ),
        scratch_shapes=[pltpu.VMEM((NSTATE, INNER), F32), pltpu.VMEM((8, MIXW), F32)],
        compiler_params=params(),
        cost_estimate=cost(33),
    )(tokens, w_in, norm_gain, conv_weight, conv_bias, dt_bias, a_log, skip, gain)


def scan_backward_kernel(
    mixed, dt, ssm, grad, states, dt_bias, a_log, skip, gather, held,
    grad_mixed, grad_dt, sums, skip_sums, grad_state, left, right,
):
    @pl.when(pl.program_id(0) == 0)
    def _():
        grad_state[...] = jnp.zeros_like(grad_state)
        sums[...] = jnp.zeros_like(sums)
        skip_sums[...] = jnp.zeros_like(skip_sums)

    shifted, delta, rate, cum, last = chunk_decays(dt[...], dt_bias[...], a_log[...])
    lane = lax.broadcasted_iota(jnp.int32, (CHUNK, LANES), 1)
    row = lax.broadcasted_iota(jnp.int32, (CHUNK, LANES), 0)
    bias = jnp.where(lane >= row, 0.0, -1e30)
    heads = lane < HEADS
    cum_t = cum.T
    inputs_b = mixed[:, INNER : INNER + NSTATE]
    readout = mixed[:, INNER + NSTATE :]
    b_parts, c_parts = split(inputs_b), split(readout)
    b_wide = side_by_side(inputs_b)
    c_turned = side_by_side(readout.T)
    affinity = dot3(b_parts, c_parts, NT)
    low, high = pair_mask()
    grad_affinity = jnp.zeros((CHUNK, CHUNK), F32)
    grad_b = jnp.zeros((CHUNK, NSTATE), F32)
    grad_c = jnp.zeros((CHUNK, NSTATE), F32)
    last_row = lax.broadcasted_iota(jnp.int32, (CHUNK, QWIDTH), 0) == CHUNK - 1
    for quad in range(QUADS):
        cols = slice(quad * QWIDTH, (quad + 1) * QWIDTH)
        wide_delta, wide_cum, columns = widen(delta, cum, quad)
        grown = jnp.exp(wide_cum)
        tail = jnp.exp(wide_cum[CHUNK - 1 :] - wide_cum)
        end = grown[CHUNK - 1 :]
        values = mixed[:, cols]
        pulled = grad[:, cols]
        scaled = values * wide_delta
        x_parts, p_parts = split(scaled), split(pulled)
        outs = []
        for j in range(2):
            half = slice(j * LANES, (j + 1) * LANES)
            xh, xl = x_parts[0][:, half], x_parts[1][:, half]
            right_h, right_l = pair_rows(p_parts, j, low, high)
            pull = dot(
                jnp.concatenate([xh, xl], axis=1),
                jnp.concatenate([right_h, right_h], axis=1),
                NT,
            ) + dot(xh, right_l, NT)
            kernels = []
            for k in range(2):
                h = 4 * quad + 2 * j + k
                within = jnp.exp(cum_t[h : h + 1, :] - columns[2 * j + k] + bias)
                kernels.append(split(affinity * within))
                grad_affinity = grad_affinity + within * pull[:, k * CHUNK : (k + 1) * CHUNK]
            kernel_h = jnp.concatenate([kernels[0][0], kernels[1][0]], axis=1)
            kernel_l = jnp.concatenate([kernels[0][1], kernels[1][1]], axis=1)
            both = dot(kernel_h, jnp.concatenate([right_h, right_l], axis=1))
            outs.append(both[:, :LANES] + both[:, LANES:] + dot(kernel_l, right_h))
        late = grad_state[:, cols]
        late_parts = split(late)
        early = states[0, :, cols]
        from_state = dot_parts(b_wide, late_parts) * tail
        grad_scaled = jnp.concatenate(outs, axis=1) + from_state
        pulled_cum = split(pulled * grown)
        grad_c = grad_c + dot_turned(pulled_cum, split(early))
        grad_b = grad_b + dot_turned(split(scaled * tail), late_parts)
        grad_state[:, cols] = late * end + dot_parts(c_turned, pulled_cum)
        grad_mixed[:, cols] = grad_scaled * wide_delta + skip[:, cols] * pulled
        skip_sums[:, cols] += jnp.sum(pulled * values, axis=0, keepdims=True)
        left[:, cols] = grad_scaled * values
        inner = pulled * (ssm[:, cols] - skip[:, cols] * values) - scaled * grad_scaled
        extra = jnp.sum(scaled * from_state, axis=0, keepdims=True) + end * jnp.sum(
            late * early, axis=0, keepdims=True
        )
        right[:, cols] = inner + jnp.where(last_row, extra, 0.0)
    ga_parts = split(grad_affinity)
    grad_mixed[:, INNER : INNER + NSTATE] = grad_b + dot3(ga_parts, c_parts)
    grad_mixed[:, INNER + NSTATE :] = grad_c + dot3(split(grad_affinity.T), b_parts)

    def by_head(v):
        high, low = split(v)
        g = gather[...]
        return dot(high, g) + dot(low, g)

    direct = by_head(left[...])
    grad_cum = by_head(right[...])
    upper = (lane >= row).astype(BF16)
    after = triangle_sum(upper, grad_cum)
    grad_delta = direct + rate * after
    grad_raw = jnp.where(heads, grad_delta * sigmoid(shifted), 0.0)
    grad_dt[...] = grad_raw.astype(BF16)
    sums[0:1, :] += jnp.sum(grad_raw, axis=0, keepdims=True)
    sums[1:2, :] += rate * jnp.sum(delta * after, axis=0, keepdims=True)


def scan_backward(mixed, projected, ssm, grad, states, dt_bias, a_log, skip, gather, held):
    length = mixed.shape[0]
    chunks = length // CHUNK
    whole = lambda v: pl.BlockSpec(v.shape, lambda i: (0,) * v.ndim)
    back = lambda i: (chunks - 1 - i, 0)
    return pl.pallas_call(
        scan_backward_kernel,
        grid=(chunks,),
        out_shape=(
            shape((length, MIXW), F32),
            shape(held.shape, BF16),
            shape((8, LANES), F32),
            shape((1, INNER), F32),
        ),
        in_specs=[
            pl.BlockSpec((CHUNK, MIXW), back),
            pl.BlockSpec((CHUNK, LANES), lambda i: (chunks - 1 - i, DT_AT // LANES)),
            pl.BlockSpec((CHUNK, INNER), back),
            pl.BlockSpec((CHUNK, INNER), back),
            pl.BlockSpec((1, NSTATE, INNER), lambda i: (chunks - 1 - i, 0, 0)),
        ]
        + [whole(v) for v in (dt_bias, a_log, skip, gather)]
        + [ANY],
        out_specs=(
            pl.BlockSpec((CHUNK, MIXW), back),
            pl.BlockSpec((CHUNK, LANES), lambda i: (chunks - 1 - i, DT_AT // LANES)),
            pl.BlockSpec((8, LANES), lambda i: (0, 0)),
            pl.BlockSpec((1, INNER), lambda i: (0, 0)),
        ),
        scratch_shapes=[pltpu.VMEM((NSTATE, INNER), F32)] + [pltpu.VMEM((CHUNK, INNER), F32)] * 2,
        compiler_params=params(),
        input_output_aliases={9: 1},
        cost_estimate=cost(35),
    )(mixed, projected, ssm, grad, states, dt_bias, a_log, skip, gather, held)


ROWS_AT_ONCE = 128
CONV_TILES = 2


def down(v, before, by):
    moved = pltpu.roll(v, by, 0)
    row = lax.broadcasted_iota(jnp.int32, (8, LANES), 0)
    top = jnp.where(row < by, pltpu.roll(before, by, 0), moved[:8])
    return jnp.concatenate([top, moved[8:]], axis=0)


def up(v, after, by):
    rows = v.shape[0]
    moved = pltpu.roll(v, rows - by, 0)
    row = lax.broadcasted_iota(jnp.int32, (8, LANES), 0)
    end = jnp.where(row < 8 - by, moved[rows - 8 :], pltpu.roll(after, 8 - by, 0))
    return jnp.concatenate([moved[: rows - 8], end], axis=0)


def conv_terms(conv_in, at, cols):
    rows = conv_in[at : at + ROWS_AT_ONCE, cols]
    before = conv_in[at - 8 : at, cols] if at else jnp.zeros((8, LANES), F32)
    return [down(rows, before, KCONV - 1 - k) for k in range(KCONV - 1)] + [rows]


def conv_sum(terms, weight, bias):
    total = bias + terms[KCONV - 1] * weight[KCONV - 1 : KCONV]
    for k in range(KCONV - 1):
        total = total + terms[k] * weight[k : k + 1]
    return total


def conv_backward_kernel(conv_in, grad, weight, bias, held, out, sums):
    length = conv_in.shape[0]
    for tile in range(CONV_TILES):
        cols = slice(tile * LANES, (tile + 1) * LANES)
        w, b = weight[:, cols], bias[:, cols]
        totals = [jnp.zeros((1, LANES), F32)] * (KCONV + 1)
        after = jnp.zeros((8, LANES), F32)
        for at in range(length - ROWS_AT_ONCE, -1, -ROWS_AT_ONCE):
            terms = conv_terms(conv_in, at, cols)
            value = conv_sum(terms, w, b)
            sig = sigmoid(value)
            g = grad[at : at + ROWS_AT_ONCE, cols] * (sig * (1.0 + value * (1.0 - sig)))
            for k in range(KCONV):
                totals[k] = totals[k] + jnp.sum(g * terms[k], axis=0, keepdims=True)
            totals[KCONV] = totals[KCONV] + jnp.sum(g, axis=0, keepdims=True)
            total = g * w[KCONV - 1 : KCONV]
            for k in range(KCONV - 1):
                total = total + up(g, after, KCONV - 1 - k) * w[k : k + 1]
            after = g[:8]
            out[at : at + ROWS_AT_ONCE, cols] = total.astype(BF16)
        for k in range(KCONV + 1):
            sums[k : k + 1, cols] = totals[k]


def conv_backward(projected, grad_mixed, weight, bias, held):
    length = projected.shape[0]
    width = CONV_TILES * LANES
    return pl.pallas_call(
        conv_backward_kernel,
        grid=(CONVCH // width,),
        out_shape=(shape(held.shape, BF16), shape((8, CONVCH), F32)),
        in_specs=[
            pl.BlockSpec((length, width), lambda i: (0, INNER // width + i)),
            pl.BlockSpec((length, width), lambda i: (0, i)),
            pl.BlockSpec((KCONV, width), lambda i: (0, i)),
            pl.BlockSpec((1, width), lambda i: (0, i)),
            ANY,
        ],
        out_specs=(
            pl.BlockSpec((length, width), lambda i: (0, INNER // width + i)),
            pl.BlockSpec((8, width), lambda i: (0, i)),
        ),
        input_output_aliases={4: 0},
        compiler_params=params(),
        cost_estimate=cost(12),
    )(projected, grad_mixed, weight, bias, held)


def loss_kernel(
    limit, mixed_out, w_out, tokens, teacher, mask, block_out, grad_result, grad_branch, error
):
    step = pl.program_id(0)

    @pl.when(step == 0)
    def _():
        error[...] = jnp.zeros_like(error)

    rows = tokens.shape[0]
    result = tokens[...].astype(F32) + dot(mixed_out[...], w_out[...])
    position = step * rows + lax.broadcasted_iota(jnp.int32, (rows, 1), 0)
    valid = (position < limit[0]).astype(F32)
    turned = jnp.broadcast_to(mask[...].astype(F32), (LANES, rows)).T
    weight = valid * turned[:, 0:1]
    block_out[...] = (result * valid).astype(BF16)
    misfit = result - teacher[...].astype(F32)
    pulled = 2.0 * weight * misfit
    grad_result[...] = pulled
    errors = jnp.sum(0.5 * pulled * misfit, axis=0, keepdims=True)
    for j in range(D // LANES):
        error[j : j + 1, :] += errors[:, j * LANES : (j + 1) * LANES]
    error[D // LANES : D // LANES + 1, :] += jnp.sum(valid * turned, axis=0, keepdims=True)
    grad_branch[...] = pulled.astype(BF16)


def loss_part(limit, mixed_out, w_out, tokens, teacher, mask):
    length = tokens.shape[0]
    rows = 256
    by_row = lambda width: pl.BlockSpec((rows, width), lambda i: (i, 0))
    return pl.pallas_call(
        loss_kernel,
        grid=(length // rows,),
        out_shape=(
            shape((length, D), BF16),
            shape((length, D), F32),
            shape((length, D), BF16),
            shape((8, LANES), F32),
        ),
        in_specs=[
            SMEM,
            by_row(INNER),
            pl.BlockSpec(w_out.shape, lambda i: (0, 0)),
            by_row(D),
            by_row(D),
            pl.BlockSpec((1, rows), lambda i: (0, i)),
        ],
        out_specs=(by_row(D), by_row(D), by_row(D), pl.BlockSpec((8, LANES), lambda i: (0, 0))),
        compiler_params=params(),
        cost_estimate=cost(8),
    )(limit, mixed_out, w_out, tokens, teacher, mask)


def gate_kernel(grad_branch, w_out, ssm, gate, gain, grad_ssm, grad_gate, gain_sums):
    @pl.when(pl.program_id(0) == 0)
    def _():
        gain_sums[...] = jnp.zeros_like(gain_sums)

    grad_mixed = dot(grad_branch[...], w_out[...], NT)
    g = gate[...]
    sig = sigmoid(g)
    act = g * sig
    inner = ssm[...]
    gated = inner * act
    rho = lax.rsqrt(jnp.mean(gated * gated, axis=1, keepdims=True) + NORM_EPS)
    unit = gated * rho
    gain_sums[...] += jnp.sum(unit * grad_mixed, axis=0, keepdims=True)
    grad_unit = grad_mixed * gain[...]
    share = jnp.mean(grad_unit * unit, axis=1, keepdims=True)
    grad_gated = rho * (grad_unit - unit * share)
    grad_ssm[...] = grad_gated * act
    grad_gate[...] = (grad_gated * inner * (sig * (1.0 + g * (1.0 - sig)))).astype(BF16)


def gate_part(grad_branch, w_out, ssm, projected, gain):
    length = ssm.shape[0]
    rows = 256
    by_row = lambda width: pl.BlockSpec((rows, width), lambda i: (i, 0))
    whole = lambda v: pl.BlockSpec(v.shape, lambda i: (0,) * v.ndim)
    return pl.pallas_call(
        gate_kernel,
        grid=(length // rows,),
        out_shape=(shape((length, INNER), F32), shape((length, WIDE), BF16), shape((1, INNER), F32)),
        in_specs=[by_row(D), whole(w_out), by_row(INNER), by_row(INNER), whole(gain)],
        out_specs=(by_row(INNER), by_row(INNER), pl.BlockSpec((1, INNER), lambda i: (0, 0))),
        compiler_params=params(),
        cost_estimate=cost(12),
    )(grad_branch, w_out, ssm, projected, gain)


def input_kernel(grad_low, w_in, tokens, norm_gain, grad_result, out, sums):
    @pl.when(pl.program_id(0) == 0)
    def _():
        sums[...] = jnp.zeros_like(sums)

    x = tokens[...].astype(F32)
    inverse = lax.rsqrt(jnp.mean(x * x, axis=1, keepdims=True) + NORM_EPS)
    unit = x * inverse
    grad_hidden = dot(grad_low[...], w_in[...], NT)
    sums[...] += jnp.sum(grad_hidden * unit, axis=0, keepdims=True)
    pulled = grad_hidden * norm_gain[...]
    share = jnp.mean(pulled * unit, axis=1, keepdims=True)
    out[...] = grad_result[...] + inverse * (pulled - unit * share)


def input_backward(grad_low, w_in, tokens, norm_gain, grad_result):
    length = tokens.shape[0]
    rows = 256
    by_row = lambda width: pl.BlockSpec((rows, width), lambda i: (i, 0))
    whole = lambda v: pl.BlockSpec(v.shape, lambda i: (0,) * v.ndim)
    return pl.pallas_call(
        input_kernel,
        grid=(length // rows,),
        out_shape=(shape((length, D), F32), shape((1, D), F32)),
        in_specs=[by_row(WIDE), whole(w_in), by_row(D), whole(norm_gain), by_row(D)],
        out_specs=(by_row(D), pl.BlockSpec((1, D), lambda i: (0, 0))),
        compiler_params=params(),
        cost_estimate=cost(15),
    )(grad_low, w_in, tokens, norm_gain, grad_result)


def vector_kernel(tail, conv_sums, sums, skip_sums, norm_sums, gate_sums, gather, out, taps):
    tiles = CONVCH // LANES
    out[...] = jnp.zeros_like(out)
    out[0:TAIL_ROWS, :] = tail[...]
    for k in range(KCONV):
        for i in range(tiles):
            taps[k * 16 + i : k * 16 + i + 1, :] = conv_sums[k : k + 1, i * LANES : (i + 1) * LANES]
    row = lax.broadcasted_iota(jnp.int32, (LANES, LANES), 0)
    col = lax.broadcasted_iota(jnp.int32, (LANES, LANES), 1)
    per_tile = LANES // KCONV

    def exact(v, chosen):
        high = v.astype(BF16)
        rest = v - high.astype(F32)
        middle = rest.astype(BF16)
        low = (rest - middle.astype(F32)).astype(BF16)
        return dot(high, chosen) + (dot(middle, chosen) + dot(low, chosen))

    for q in range(KCONV):
        total = jnp.zeros((tiles, LANES), F32)
        for k in range(KCONV):
            chosen = (col == KCONV * (row % per_tile) + k) & (row // per_tile == q)
            total = total + exact(taps[k * 16 : k * 16 + tiles, :], chosen.astype(BF16))
        out[pl.ds(TAIL_ROWS + q, tiles, stride=KCONV), :] = total
    bias_at = TAIL_ROWS + tiles * KCONV
    for i in range(tiles):
        out[bias_at + i : bias_at + i + 1, :] = conv_sums[KCONV : KCONV + 1, i * LANES : (i + 1) * LANES]
    lane = lax.broadcasted_iota(jnp.int32, (1, LANES), 1)
    skip = exact(jnp.broadcast_to(skip_sums[...], (8, INNER)), gather[...])[0:1, :]
    parts = [sums[0:1, :], sums[1:2, :], skip]
    parts = [jnp.where(lane < HEADS, v, 0.0) for v in parts]
    before = parts[0] + pltpu.roll(parts[1], HEADS, 1) + pltpu.roll(parts[2], 2 * HEADS, 1)
    at, shift = bias_at + tiles, 3 * HEADS
    for source in (norm_sums, gate_sums):
        for j in range(source.shape[1] // LANES):
            here = pltpu.roll(source[:, j * LANES : (j + 1) * LANES], shift, 1)
            out[at : at + 1, :] = jnp.where(lane < shift, before, here)
            before = here
            at += 1
    out[at : at + 1, :] = jnp.where(lane < shift, before, 0.0)


def pack_vectors(tail, conv_sums, sums, skip_sums, norm_sums, gate_sums, gather):
    return pl.pallas_call(
        vector_kernel,
        out_shape=shape(((NBLK - MID1) * BROWS, LANES), F32),
        in_specs=[VMEM] * 7,
        out_specs=VMEM,
        scratch_shapes=[pltpu.VMEM((KCONV * 16, LANES), F32)],
        compiler_params=params(),
    )(tail, conv_sums, sums, skip_sums, norm_sums, gate_sums, gather)


def body(tokens, teacher, lengths, loss_mask, owners, master, first_moment, second_moment):
    capacity = master.shape[0]
    dp, fsdp = lax.axis_size("dp"), lax.axis_size("fsdp")
    devices = dp * fsdp
    me = lax.axis_index(AXES).astype(jnp.int32)
    x_first, y_first, z_first = step_orders(dp, fsdp)
    tie = lambda *values: lax.optimization_barrier(values)

    sent = send_blocks(owners, master, devices, me)
    at_home = lax.all_to_all(sent, AXES, 0, 0, tiled=True)
    owners, tokens, loss_mask, _ = tie(owners, tokens, loss_mask, sent)
    plan = make_plan(owners, capacity, devices, me)
    streams = cut(even(plan["slots"], 3), (x_first, y_first, z_first))
    table = stream_places(plan["home"], plan["slot"], me, streams, devices)
    u0, u1 = plan["unit_slots"]
    sizes = [-(-u0 // 5)] * 4
    unit_streams = cut(sizes + [u0 - sum(sizes)], (x_first, y_first, x_first, y_first, z_first))
    unit_table = stream_places(plan["unit_home"], plan["unit_slot"], me, unit_streams, devices)
    unit_table = unit_table[:MID0].reshape(-1)
    unit_table1 = place_of(plan["unit_home"] ^ me, x_first) * (u1 + 1) + plan["unit_slot"]
    unit_table1 = unit_table1[MID0:MID1].reshape(-1)
    inputs, target = tokens[0], teacher[0]
    (at_home, table, unit_table, unit_table1, received, back_table, row_from, row_block,
     row_used) = tie(
        at_home, table, unit_table, unit_table1, plan["received"], plan["back"],
        plan["row_from"], plan["row_block"], plan["row_used"],
    )
    mine = pick_blocks(received, at_home, [size for _, size, _ in streams])
    parts = []
    for values, (_, _, order) in zip(mine, streams):
        parts += gather_steps(values, order)
    (input_weight, output_weight, conv_weight, conv_bias, dt_bias, a_log, skip, norm_gain,
     gate_gain) = unpack(table, parts)
    gather = heads_gather()
    hidden, projected, mixed, ssm, mixed_out, states = forward(
        inputs, input_weight, norm_gain, conv_weight, conv_bias, dt_bias, a_log, skip, gate_gain
    )
    block_out, grad_result, grad_branch, local = loss_part(
        lengths, mixed_out, output_weight, inputs, target, loss_mask
    )
    keep1, send1, head, tail = pack_out(
        unit_table1, mixed_out, grad_branch, local, devices, u1 + 1
    )
    grad_branch, send1 = tie(grad_branch, send1)
    got1 = exchange(send1, x_first[0])
    grad_ssm, grad_low, grad_gate = gate_part(grad_branch, output_weight, ssm, projected, gate_gain)
    grad_ssm, keep1, got1 = tie(grad_ssm, keep1, got1)
    keep1, got1 = reduce_step(keep1, got1, x_first[1])
    grad_mixed, grad_low, sums, skip_sums = scan_backward(
        mixed, projected, ssm, grad_ssm, states, dt_bias, a_log, skip, gather, grad_low
    )
    grad_mixed, keep1, got1 = tie(grad_mixed, keep1, got1)
    steps1 = x_first[2:]
    for step in steps1[:1]:
        keep1, got1 = reduce_step(keep1, got1, step)
    grad_low, conv_sums = conv_backward(projected, grad_mixed, conv_weight, conv_bias, grad_low)
    grad_low, keep1, got1 = tie(grad_low, keep1, got1)
    for step in steps1[1:2]:
        keep1, got1 = reduce_step(keep1, got1, step)
    halves = []
    for _, size, _ in unit_streams:
        halves += [devices * size // 2] * 2
    packed = list(pack_in(unit_table, hidden, grad_low, head, halves))
    packed[0], keep1, got1 = tie(packed[0], keep1, got1)
    kept = packed[::2]
    got = [exchange(v, order[0]) for v, (_, _, order) in zip(packed[1::2], unit_streams)]
    *got, grad_low, conv_sums, tail = tie(*got, grad_low, conv_sums, tail)
    last = len(unit_streams) - 1
    apart = fold([[kept[last], got[last]]])
    apart = [apart[0], *exchange_quarters(apart, z_first[1:3])]
    for i, (_, _, order) in enumerate(unit_streams[:last]):
        kept[i], got[i] = reduce_step(kept[i], got[i], order[1])
    for step in steps1[2:3]:
        keep1, got1 = reduce_step(keep1, got1, step)
    input_grad, norm_sums = input_backward(grad_low, input_weight, inputs, norm_gain, grad_result)
    grad_vec = pack_vectors(tail, conv_sums, sums, skip_sums, norm_sums, grad_gate, gather)
    grad_vec = grad_vec.reshape((NBLK - MID1) * UNITS, UNIT, LANES)
    *got, got1, grad_vec, input_grad, a0, a1, a2, a3 = tie(
        *got[:last], got1, grad_vec, input_grad, *apart
    )
    for step in steps1[3:]:
        keep1, got1 = reduce_step(keep1, got1, step)
    for k in range(2, len(x_first) - 2):
        for i, (_, _, order) in enumerate(unit_streams[:last]):
            if i == 0:
                kept[i], got[i], grad_vec = reduce_step(kept[i], got[i], order[k], grad_vec)
            else:
                kept[i], got[i] = reduce_step(kept[i], got[i], order[k])
    apart = [a0, a1, a2, a3]
    for step in z_first[3:-2]:
        apart = reduce_step(apart[0] + a1 + a2, a3, step) if len(apart) > 2 else reduce_step(*apart, step)
    apart = fold([apart])
    apart = [apart[0], *exchange_quarters(apart, z_first[-2:])]
    stay = fold(list(zip(kept[:last], got)), grad_vec)
    arrived = exchange_quarters(stay, x_first[-2:])
    n = stay[0].shape[0]
    back = units_to_owners(back_table, [[stay[0], *arrived], apart, [keep1, got1]])
    grad_vec = grad_vec + (arrived[0][n:] + (arrived[1][n:] + arrived[2][n:]))
    back, grad_vec = tie(back, grad_vec)
    returned = lax.all_to_all(back, AXES, 0, 0, tiled=True)
    for step in x_first[:2]:
        grad_vec = grad_vec + exchange(grad_vec, step)
    local_sums = keep1[u1] + got1[u1]
    error_sum = jnp.sum(local_sums[: D // LANES])
    divisor = local_sums[D // LANES, 0] * D
    new_first, new_second, new_master = adam(
        row_from,
        row_block,
        row_used,
        divisor,
        returned,
        grad_vec,
        master,
        first_moment,
        second_moment,
    )
    mean_loss = error_sum / divisor
    return (block_out[None], input_grad[None], mean_loss, new_first, new_second, new_master)


def solution(mesh):
    return jax.shard_map(
        body,
        mesh=mesh,
        in_specs=(
            P(AXES, None, None),
            P(AXES, None, None),
            P(AXES),
            P(AXES, None),
            P(),
            P(AXES, None),
            P(AXES, None),
            P(AXES, None),
        ),
        out_specs=(
            P(AXES, None, None),
            P(AXES, None, None),
            P(),
            P(AXES, None),
            P(AXES, None),
            P(AXES, None),
        ),
        check_vma=False,
    )
```

```python
from functools import partial

import jax
import jax.numpy as jnp
import numpy as np
from jax import lax
from jax.experimental import pallas as pl
from jax.experimental.pallas import tpu as pltpu
from jax.sharding import PartitionSpec as P

D = 768
INNER = 1536
NSTATE = 128
HEADDIM = 64
KCONV = 4
SCAN_LEN = 256
PBLOCK = 4096
STEP = 10
HEADS = 24
CONVCH = 1792
PROJ = 3352
PTOT = 3765320
NBLK = 920

LANES = 128
BROWS = PBLOCK // LANES
UNIT = 8
UNITS = BROWS // UNIT
END_IN = D * PROJ
END_OUT = END_IN + INNER * D
MID0 = -(-END_IN // PBLOCK)
MID1 = END_OUT // PBLOCK
N0 = MID0 + NBLK - MID1
N1 = MID1 - MID0
F0_ROWS = N0 * BROWS
IN_ROWS = END_IN // LANES
HEAD_ROWS = MID0 * BROWS - IN_ROWS
TAIL_ROWS = (END_OUT - MID1 * PBLOCK) // LANES
OUT_ROWS = INNER * D // LANES
VEC_ROWS = (NBLK - MID1) * BROWS - TAIL_ROWS
VEC_AT = MID0 * BROWS + TAIL_ROWS
GROUP = 16
GROUPS = D // GROUP
GROUP_ROWS = GROUP * PROJ // LANES
COL_TILES = -(-PROJ // LANES)
WIDE = COL_TILES * LANES
OUT_TILES = D // LANES

NORM_EPS = 1e-05
ADAM_EPS = 1e-08
BETA_ONE = 0.9
BETA_TWO = 0.999
MATRIX_RATE = 0.03
VECTOR_RATE = 0.2
WEIGHT_DECAY = 0.1
PRECISE = lax.Precision.HIGHEST
AXES = ("dp", "fsdp")
VMEM_LIMIT = 60 * 1024 * 1024


def bits_of(count):
    return count.bit_length() - 1


def step_orders(dp, fsdp):
    wide = [("dp", i) for i in range(bits_of(dp))]
    narrow = [("fsdp", i) for i in range(bits_of(fsdp))]
    first = wide[:2] + narrow + wide[2:]
    second = wide[:1] + narrow + wide[1:]
    third = wide[:1] + wide[2:] + wide[1:2] + narrow
    return first, second, third


def cut(sizes, orders):
    streams, at = [], 0
    for size, order in zip(sizes, orders):
        if size:
            streams.append((at, size, order))
        at += size
    return streams


def even(total, parts):
    return [total // parts + (i < total % parts) for i in range(parts)]


def exchange(values, *steps):
    axes = {axis for axis, _ in steps}
    if len(axes) == 1:
        (axis,) = axes
        mask = sum(1 << bit for _, bit in steps)
        pairs = [(i, i ^ mask) for i in range(lax.axis_size(axis))]
        return lax.ppermute(values, axis, pairs)
    low = bits_of(lax.axis_size("fsdp"))
    mask = sum(1 << (bit + (low if axis == "dp" else 0)) for axis, bit in steps)
    count = lax.axis_size("dp") * lax.axis_size("fsdp")
    return lax.ppermute(values, AXES, [(i, i ^ mask) for i in range(count)])


def place_of(relative, order):
    shift_of = {"dp": bits_of(lax.axis_size("fsdp")), "fsdp": 0}
    place = jnp.zeros_like(relative)
    for axis, bit in order:
        place = place * 2 + ((relative >> (shift_of[axis] + bit)) & 1)
    return place


def class_counts(owners, devices):
    block = jnp.arange(NBLK, dtype=jnp.int32)
    mid = ((block >= MID0) & (block < MID1))[None, :]
    device = jnp.arange(devices, dtype=jnp.int32)
    below = owners[None, :] < device[:, None]
    owned = owners[None, :] == device[:, None]

    def total(mask):
        return jnp.sum(mask.astype(jnp.int32), axis=1)

    start = (total(below & ~mid), total(below & mid))
    count = (total(owned & ~mid), total(owned & mid))
    return start, count, total(owned & (block < MID0)[None, :])


def my_counts(owners, me):
    block = jnp.arange(NBLK, dtype=jnp.int32)
    mid = (block >= MID0) & (block < MID1)
    below, owned = owners < me, owners == me
    total = lambda mask: jnp.sum(mask.astype(jnp.int32))
    start = (total(below & ~mid), total(below & mid))
    count = (total(owned & ~mid), total(owned & mid))
    return start, count, total(owned & (block < MID0))


def pair_lanes(capacity, devices):
    return -(-capacity // devices)


def make_plan(owners, capacity, devices, me):
    block = jnp.arange(NBLK, dtype=jnp.int32)
    mid = (block >= MID0) & (block < MID1)
    same = mid[:, None] == mid[None, :]
    before = (owners[None, :] < owners[:, None]) | (
        (owners[None, :] == owners[:, None]) & (block[None, :] < block[:, None])
    )
    order = jnp.sum(before.astype(jnp.int32), axis=1)
    order_in_class = jnp.sum((same & before).astype(jnp.int32), axis=1)
    home, slot = order % devices, order // devices
    device = jnp.arange(devices, dtype=jnp.int32)
    start, count, _ = class_counts(owners, devices)
    my_start, my_count, my_early = my_counts(owners, me)
    pair = pair_lanes(capacity, devices)

    slots = -(-NBLK // devices)
    wanted = me + devices * jnp.arange(slots, dtype=jnp.int32)
    first = start[0] + start[1]
    ends = first + count[0] + count[1]
    owner = jnp.sum((ends[None, :] <= wanted[:, None]).astype(jnp.int32), axis=1)
    owner = jnp.minimum(owner, devices - 1)
    base = jnp.sum(jnp.where(device[None, :] == owner[:, None], first[None, :], 0), axis=1)
    received = owner * pair + jnp.clip((wanted - base) // devices, 0, pair - 1)

    back_pair = (UNITS * capacity + 2 * (devices - 1)) // devices
    unit = UNITS * order_in_class[:, None] + jnp.arange(UNITS, dtype=jnp.int32)[None, :]
    unit_home, unit_slot = unit % devices, unit // devices
    unit_slots = (-(-UNITS * N0 // devices), -(-UNITS * N1 // devices))
    lane = jnp.arange(back_pair, dtype=jnp.int32)

    def units_back(kind):
        turn = lane if kind == 0 else back_pair - 1 - lane
        first = UNITS * start[kind][:, None]
        k = (me - first) % devices + turn[None, :] * devices
        return k < UNITS * count[kind][:, None], (first + k) // devices

    valid0, slot0 = units_back(0)
    valid1, slot1 = units_back(1)
    back = jnp.where(valid0, slot0, jnp.where(valid1, unit_slots[0] + slot1, 0)).reshape(-1)

    row = jnp.arange(capacity, dtype=jnp.int32)
    is_mid = (row >= my_early) & (row < my_early + my_count[1])
    k = jnp.where(is_mid, row - my_early, jnp.where(row < my_early, row, row - my_count[1]))
    first = UNITS * jnp.where(is_mid, my_start[1], my_start[0])
    k = UNITS * k[:, None] + jnp.arange(UNITS, dtype=jnp.int32)[None, :]
    turn = k // devices
    row_from = ((first[:, None] + k) % devices) * back_pair + jnp.where(
        is_mid[:, None], back_pair - 1 - turn, turn
    )
    row_used = row < my_count[0] + my_count[1]
    mine = (owners == me)[None, :]
    rank = jnp.sum((mine & (block[None, :] < block[:, None])).astype(jnp.int32), axis=1)
    row_block = jnp.sum(
        jnp.where(mine & (rank[None, :] == row[:, None]), block[None, :], 0), axis=1
    )
    late = devices * back_pair + UNITS * (row_block - MID1)
    late = late[:, None] + jnp.arange(UNITS, dtype=jnp.int32)[None, :]
    row_from = jnp.where((row_block >= MID1)[:, None], late, row_from)
    row_from = jnp.where(row_used[:, None], row_from, 0).reshape(-1)
    return dict(
        home=home, slot=slot, slots=slots,
        received=received, unit_home=unit_home, unit_slot=unit_slot,
        unit_slots=unit_slots, back=back, row_from=row_from,
        row_used=row_used, row_block=row_block,
    )


def stream_places(home, slot, me, streams, devices):
    relative = home ^ me
    place = jnp.zeros_like(slot)
    for begin, size, order in streams:
        inside = (slot >= begin) & (slot < begin + size)
        at = devices * begin + place_of(relative, order) * size + slot - begin
        place = jnp.where(inside, at, place)
    return place


def cost(microseconds):
    return pl.CostEstimate(
        flops=int(microseconds * 1e9), bytes_accessed=int(microseconds * 3e6), transcendentals=0
    )


ANY = pl.BlockSpec(memory_space=pl.ANY)
VMEM = pl.BlockSpec(memory_space=pltpu.VMEM)
SMEM = pl.BlockSpec(memory_space=pltpu.SMEM)


def params(**extra):
    return pltpu.CompilerParams(vmem_limit_bytes=VMEM_LIMIT, **extra)


def shape(dims, dtype):
    return jax.ShapeDtypeStruct(dims, dtype)


def send_kernel(my_index, owners, master, out, flat, *, devices):
    capacity = master.shape[0]
    me = my_index[0]
    for j in range(BROWS):
        flat[pl.ds(j, capacity, stride=BROWS), :] = master[:, j * LANES : (j + 1) * LANES]
    held = owners[...]
    below, owned = held < me, held == me

    def total(mask):
        return jnp.sum(jnp.where(mask, 1.0, 0.0)).astype(jnp.int32)

    start, count = total(below), total(owned)
    pair = out.shape[0] // devices

    def step(home, carry):
        for s in range(pair):
            k = lax.rem(home - start + devices * NBLK, devices) + s * devices
            row = jnp.where(k < count, k, 0)
            rows = pl.ds(pl.multiple_of(row * BROWS, BROWS), BROWS)
            out[home * pair + s] = flat[rows, :].astype(out.dtype)
        return carry

    lax.fori_loop(0, devices, step, 0)


def send_blocks(owners, master, devices, me):
    rows = -(-NBLK // (8 * LANES)) * 8
    held = jnp.pad(owners, (0, rows * LANES - NBLK), constant_values=1 << 20).reshape(rows, LANES)
    count = devices * pair_lanes(master.shape[0], devices)
    return pl.pallas_call(
        partial(send_kernel, devices=devices),
        out_shape=shape((count, BROWS, LANES), jnp.bfloat16),
        in_specs=[SMEM, VMEM, VMEM],
        out_specs=VMEM,
        scratch_shapes=[pltpu.VMEM((master.shape[0] * BROWS, LANES), jnp.float32)],
        compiler_params=params(),
    )(me.reshape(1), held, master)


def pick_kernel(table, source, *outs):
    at = 0
    for out in outs:

        def step(i, carry, out=out, at=at):
            out[i] = source[table[at + i]]
            return carry

        lax.fori_loop(0, out.shape[0], step, 0)
        at += out.shape[0]


def pick_blocks(table, source, sizes):
    return pl.pallas_call(
        pick_kernel,
        out_shape=tuple(shape((n,) + source.shape[1:], source.dtype) for n in sizes),
        in_specs=[SMEM, VMEM],
        out_specs=(VMEM,) * len(sizes),
        compiler_params=params(),
    )(table, source)


def back_kernel(table, *refs, sizes):
    sources, (out, held) = refs[:-2], refs[-2:]
    at = i = 0
    for size in sizes:
        n = sources[i].shape[0]
        total = sources[i][...]
        for k in range(1, size):
            total = total + sources[i + k][0:n]
        held[at : at + n] = total
        at += n
        i += size

    def step(i, carry):
        for u in range(8):
            out[i * 8 + u] = held[table[i * 8 + u]]
        return carry

    total = out.shape[0]
    lax.fori_loop(0, total // 8, step, 0)


def units_to_owners(table, groups):
    return pl.pallas_call(
        partial(back_kernel, sizes=[len(g) for g in groups]),
        out_shape=shape((table.shape[0], UNIT, LANES), jnp.float32),
        in_specs=[SMEM] + [VMEM] * sum(len(g) for g in groups),
        out_specs=VMEM,
        scratch_shapes=[pltpu.VMEM((sum(g[0].shape[0] for g in groups), UNIT, LANES), jnp.float32)],
        compiler_params=params(),
    )(table, *[v for g in groups for v in g])


def row_start(rho):
    return (PROJ * rho) // LANES, (PROJ * rho) % LANES


def copy_all(pairs, sem):
    copies = [pltpu.make_async_copy(a, b, sem.at[i]) for i, (a, b) in enumerate(pairs)]
    for c in copies:
        c.start()
    for c in copies:
        c.wait()


def spread_blocks(table, first, held, flat, count, first_row):
    def one(i):
        at = pl.multiple_of(first_row + i * BROWS, 16)
        flat[pl.ds(at, BROWS), :] = held[table[first + i]].astype(jnp.float32)

    def step(i, carry):
        for u in range(4):
            one(i * 4 + u)
        return carry

    lax.fori_loop(0, count // 4, step, 0)
    for i in range(count // 4 * 4, count):
        one(i)


def unpack_vectors(flat, conv_weight, conv_bias, dt_bias, a_log, skip, norm_gain, gate_gain):
    bf16, f32 = jnp.bfloat16, jnp.float32
    tiles = CONVCH // LANES
    row = lax.broadcasted_iota(jnp.int32, (LANES, LANES), 0)
    col = lax.broadcasted_iota(jnp.int32, (LANES, LANES), 1)
    per_tile = LANES // KCONV
    for k in range(KCONV):
        total = jnp.zeros((tiles, LANES), f32)
        for q in range(KCONV):
            rows = flat[pl.ds(VEC_AT + q, tiles, stride=KCONV), :].astype(bf16)
            chosen = (row == KCONV * (col % per_tile) + k) & (col // per_tile == q)
            total = total + jnp.dot(rows, chosen.astype(bf16), preferred_element_type=f32)
        for i in range(tiles):
            conv_weight[k : k + 1, i * LANES : (i + 1) * LANES] = total[i : i + 1, :]
    bias_at = VEC_AT + tiles * KCONV
    for i in range(tiles):
        conv_bias[:, i * LANES : (i + 1) * LANES] = flat[bias_at + i : bias_at + i + 1, :]
    at = bias_at + tiles
    lane = lax.broadcasted_iota(jnp.int32, (8, LANES), 1)
    first = flat[at : at + 8, :]
    three = []
    for i in range(3):
        moved = pltpu.roll(first, LANES - i * HEADS, 1) if i else first
        three.append(jnp.where(lane < HEADS, moved, 0.0))
    dt_bias[...] = three[0][0:1, :]
    a_log[...] = three[1][0:1, :]
    for j in range(INNER // LANES):
        h = lax.broadcasted_iota(jnp.int32, (LANES, LANES), 0)
        c = lax.broadcasted_iota(jnp.int32, (LANES, LANES), 1) + j * LANES
        spread = (h == c // HEADDIM).astype(bf16)
        wide = jnp.dot(three[2].astype(bf16), spread, preferred_element_type=f32)
        skip[:, j * LANES : (j + 1) * LANES] = wide[0:1, :]
    shift = 3 * HEADS
    for out, begin, width in ((norm_gain, at, D), (gate_gain, at + D // LANES, INNER)):
        for j in range(width // LANES):
            x = pltpu.roll(flat[begin + j : begin + j + 1, :], LANES - shift, 1)
            y = pltpu.roll(flat[begin + j + 1 : begin + j + 2, :], LANES - shift, 1)
            out[:, j * LANES : (j + 1) * LANES] = jnp.where(lane[0:1] < LANES - shift, x, y)


def unpack_kernel(table, *refs):
    parts, outs, scratch = refs[:-14], refs[-14:-5], refs[-5:]
    w_in, w_out, *vectors = outs
    held, flat, flat_out, tile, sem = scratch
    pairs, at = [], 0
    for part in parts:
        pairs.append((part, held.at[pl.ds(at, part.shape[0])]))
        at += part.shape[0]
    copy_all(pairs, sem)
    spread_blocks(table, 0, held, flat, MID0, 0)
    spread_blocks(table, MID1, held, flat, NBLK - MID1, MID0 * BROWS)
    spread_blocks(table, MID0, held, flat_out, N1, HEAD_ROWS)
    flat_out[0:HEAD_ROWS, :] = flat[IN_ROWS : IN_ROWS + HEAD_ROWS, :]
    flat_out[OUT_ROWS - TAIL_ROWS :, :] = flat[MID0 * BROWS : MID0 * BROWS + TAIL_ROWS, :]
    unpack_vectors(flat, *vectors)
    rows = 128

    def out_step(i, carry):
        at = pl.multiple_of(i * rows, rows)
        for j in range(OUT_TILES):
            x = flat_out[pl.ds(at * OUT_TILES + j, rows, stride=OUT_TILES), :]
            w_out[pl.ds(at, rows), j * LANES : (j + 1) * LANES] = x.astype(jnp.bfloat16)
        return carry

    lax.fori_loop(0, INNER // rows, out_step, 0)
    lane = lax.broadcasted_iota(jnp.int32, (GROUPS, LANES), 1)

    def columns(j):
        for rho in range(GROUP):
            c, s = row_start(rho)
            x = flat[pl.ds(c + j, GROUPS, stride=GROUP_ROWS), :]
            if s:
                y = flat[pl.ds(c + j + 1, GROUPS, stride=GROUP_ROWS), :]
                x = jnp.where(
                    lane < LANES - s,
                    pltpu.roll(x, LANES - s, 1),
                    pltpu.roll(y, LANES - s, 1),
                )
            tile[pl.ds(rho, GROUPS, stride=GROUP), :] = x

    def step(j, carry):
        columns(j)
        w_in[:, pl.ds(pl.multiple_of(j * LANES, LANES), LANES)] = tile[...].astype(jnp.bfloat16)
        return carry

    lax.fori_loop(0, COL_TILES - 1, step, 0)
    columns(COL_TILES - 1)
    last = (COL_TILES - 1) * LANES
    inside = lax.broadcasted_iota(jnp.int32, (D, LANES), 1) < PROJ - last
    w_in[:, last:] = jnp.where(inside, tile[...], 0.0).astype(jnp.bfloat16)


def unpack(table, parts):
    held = sum(part.shape[0] for part in parts)
    f32 = jnp.float32
    return pl.pallas_call(
        unpack_kernel,
        out_shape=(
            shape((D, WIDE), jnp.bfloat16),
            shape((INNER, D), jnp.bfloat16),
            shape((KCONV, CONVCH), f32),
            shape((1, CONVCH), f32),
            shape((1, LANES), f32),
            shape((1, LANES), f32),
            shape((1, INNER), f32),
            shape((1, D), f32),
            shape((1, INNER), f32),
        ),
        in_specs=[SMEM] + [ANY] * len(parts),
        out_specs=(VMEM,) * 9,
        scratch_shapes=[
            pltpu.VMEM((held, BROWS, LANES), jnp.bfloat16),
            pltpu.VMEM((F0_ROWS, LANES), f32),
            pltpu.VMEM((OUT_ROWS, LANES), f32),
            pltpu.VMEM((D, LANES), f32),
            pltpu.SemaphoreType.DMA((len(parts),)),
        ],
        compiler_params=params(),
        cost_estimate=cost(20),
    )(table, *parts)


def permute_units(table, flat, count, first_row, staged):
    many = 16

    def step(i, carry):
        for u in range(many):
            at = pl.multiple_of(first_row + (i * many + u) * UNIT, UNIT)
            staged[table[i * many + u]] = flat[pl.ds(at, UNIT), :]
        return carry

    lax.fori_loop(0, count // many, step, 0)
    for i in range(count // many * many, count):
        staged[table[i]] = flat[first_row + i * UNIT : first_row + (i + 1) * UNIT, :]


def pack_in_kernel(table, hidden, grad, head, *refs):
    outs, (turned, tiles, flat, staged, sem) = refs[:-5], refs[-5:]
    turned[...] = hidden[...].T
    lane = lax.broadcasted_iota(jnp.int32, (GROUPS, LANES), 1)

    def product(p, count):
        at = p * 2 * LANES
        at = at if isinstance(at, int) else pl.multiple_of(at, 2 * LANES)
        return jnp.dot(
            turned[...], grad[:, pl.ds(at, count * LANES)], preferred_element_type=jnp.float32
        )

    def put(p, value):
        for k in range(value.shape[1] // LANES):
            at = (p * 2 + k) * D
            at = at if isinstance(at, int) else pl.multiple_of(at, D)
            tiles[pl.ds(at, D), :] = value[:, k * LANES : (k + 1) * LANES]

    def load(rho, j):
        return tiles[pl.ds(j * D + rho, GROUPS, stride=GROUP), :]

    def whole(rho, i):
        first = -(-PROJ * rho // LANES)
        col0 = first * LANES - PROJ * rho
        x = load(rho, i)
        if col0:
            x = jnp.where(
                lane < LANES - col0,
                pltpu.roll(x, LANES - col0, 1),
                pltpu.roll(load(rho, i + 1), LANES - col0, 1),
            )
        flat[pl.ds(first + i, GROUPS, stride=GROUP_ROWS), :] = x

    put(0, product(0, 2))
    put(1, product(1, 2))
    pairs = COL_TILES // 2

    def step(p, carry):
        for i in range(2):
            for rho in range(GROUP):
                whole(rho, p * 2 + i)
        put(p + 2, product(p + 2, 2))
        return carry

    lax.fori_loop(0, pairs - 2, step, 0)
    put(pairs, product(pairs, COL_TILES % 2))
    for rho in range(GROUP):
        first = -(-PROJ * rho // LANES)
        col0 = first * LANES - PROJ * rho
        full = (PROJ - col0) // LANES
        for i in range((pairs - 2) * 2, full):
            whole(rho, i)
        left = PROJ - col0 - full * LANES
        if left:
            begin = col0 + full * LANES
            j, s = begin // LANES, begin % LANES
            x = pltpu.roll(load(rho, j), LANES - s, 1) if s else load(rho, j)
            if s + left > LANES:
                x = jnp.where(lane < LANES - s, x, pltpu.roll(load(rho, j + 1), LANES - s, 1))
            y = pltpu.roll(load(rho + 1, 0), left, 1)
            flat[pl.ds(first + full, GROUPS, stride=GROUP_ROWS), :] = jnp.where(lane < left, x, y)
    flat[IN_ROWS : IN_ROWS + HEAD_ROWS, :] = head[...]
    permute_units(table, flat, MID0 * UNITS, 0, staged)
    copies, at = [], 0
    for out in outs:
        copies.append((staged.at[pl.ds(at, out.shape[0])], out))
        at += out.shape[0]
    copy_all(copies, sem)


def pack_in(table, hidden, grad, head, sizes):
    return pl.pallas_call(
        pack_in_kernel,
        out_shape=tuple(shape((n, UNIT, LANES), jnp.float32) for n in sizes),
        in_specs=[SMEM, VMEM, VMEM, VMEM],
        out_specs=(ANY,) * len(sizes),
        scratch_shapes=[
            pltpu.VMEM((D, hidden.shape[0]), jnp.bfloat16),
            pltpu.VMEM((COL_TILES * D, LANES), jnp.float32),
            pltpu.VMEM((MID0 * BROWS, LANES), jnp.float32),
            pltpu.VMEM((sum(sizes), UNIT, LANES), jnp.float32),
            pltpu.SemaphoreType.DMA((len(sizes),)),
        ],
        compiler_params=params(),
        cost_estimate=cost(20),
    )(table, hidden, grad, head)


def pack_out_kernel(
    table, mixed_out, grad, local, keep, send, head, tail, turned, flat, out, sem, *, slots
):
    rows = 256

    def step(i, carry):
        at = pl.multiple_of(i * rows, rows)
        turned[...] = mixed_out[:, pl.ds(at, rows)].T
        product = jnp.dot(turned[...], grad[...], preferred_element_type=jnp.float32)
        for j in range(OUT_TILES):
            flat[pl.ds(at * OUT_TILES + j, rows, stride=OUT_TILES), :] = product[
                :, j * LANES : (j + 1) * LANES
            ]
        return carry

    lax.fori_loop(0, INNER // rows, step, 0)
    head[...] = flat[0:HEAD_ROWS, :]
    tail[...] = flat[OUT_ROWS - TAIL_ROWS : OUT_ROWS, :]
    permute_units(table, flat, N1 * UNITS, HEAD_ROWS, out)

    def add_local(i, carry):
        out[i * slots + slots - 1] = local[...]
        return carry

    lax.fori_loop(0, out.shape[0] // slots, add_local, 0)
    half = keep.shape[0]
    copy_all([(out.at[pl.ds(0, half)], keep), (out.at[pl.ds(half, half)], send)], sem)


def pack_out(table, mixed_out, grad, local, devices, slots):
    return pl.pallas_call(
        partial(pack_out_kernel, slots=slots),
        out_shape=(
            shape((devices * slots // 2, UNIT, LANES), jnp.float32),
            shape((devices * slots // 2, UNIT, LANES), jnp.float32),
            shape((HEAD_ROWS, LANES), jnp.float32),
            shape((TAIL_ROWS, LANES), jnp.float32),
        ),
        in_specs=[SMEM, VMEM, VMEM, VMEM],
        out_specs=(ANY, ANY, VMEM, VMEM),
        scratch_shapes=[
            pltpu.VMEM((256, mixed_out.shape[0]), jnp.bfloat16),
            pltpu.VMEM((OUT_ROWS, LANES), jnp.float32),
            pltpu.VMEM((devices * slots, UNIT, LANES), jnp.float32),
            pltpu.SemaphoreType.DMA((2,)),
        ],
        compiler_params=params(),
    )(table, mixed_out, grad, local)


def adam_kernel(
    table, row_block, row_used, scale, got, late, master, first, second,
    o_first, o_second, o_master, flat, held, limit, used,
):
    capacity = master.shape[0]

    def step(i, carry):
        for u in range(UNITS):
            at = table[i * UNITS + u]
            rows = pl.ds(pl.multiple_of(i * BROWS + u * UNIT, UNIT), UNIT)
            flat[rows, :] = held[at]
        limit[pl.ds(i, 1), :] = jnp.full((1, LANES), END_OUT - row_block[i] * PBLOCK, jnp.int32)
        used[pl.ds(i, 1), :] = jnp.full((1, LANES), row_used[i], jnp.int32)
        return carry

    held[0 : got.shape[0]] = got[...]
    held[got.shape[0] :] = late[...]
    lax.fori_loop(0, capacity, step, 0)
    lane = lax.broadcasted_iota(jnp.int32, (capacity, LANES), 1)
    divisor = scale[0]
    for j in range(BROWS):
        cols = slice(j * LANES, (j + 1) * LANES)
        grad = jnp.where(used[...] > 0, flat[pl.ds(j, capacity, stride=BROWS), :], 0.0) / divisor
        matrix = lane + j * LANES < limit[...]
        weights = master[:, cols]
        new_first = BETA_ONE * first[:, cols] + (1.0 - BETA_ONE) * grad
        new_second = BETA_TWO * second[:, cols] + (1.0 - BETA_TWO) * grad * grad
        normal = (
            new_first
            / (1.0 - BETA_ONE**STEP)
            / (jnp.sqrt(new_second / (1.0 - BETA_TWO**STEP)) + ADAM_EPS)
        )
        rate = jnp.where(matrix, MATRIX_RATE, VECTOR_RATE)
        decay = jnp.where(matrix, WEIGHT_DECAY, 0.0)
        o_first[:, cols] = new_first
        o_second[:, cols] = new_second
        o_master[:, cols] = weights - rate * (normal + decay * weights)


def adam(table, row_block, row_used, divisor, got, late, master, first, second):
    capacity = master.shape[0]
    return pl.pallas_call(
        adam_kernel,
        out_shape=(shape(master.shape, jnp.float32),) * 3,
        in_specs=[SMEM] * 4 + [VMEM] * 5,
        out_specs=(VMEM,) * 3,
        scratch_shapes=[
            pltpu.VMEM((capacity * BROWS, LANES), jnp.float32),
            pltpu.VMEM((got.shape[0] + late.shape[0], UNIT, LANES), jnp.float32),
            pltpu.VMEM((capacity, LANES), jnp.int32),
            pltpu.VMEM((capacity, LANES), jnp.int32),
        ],
        compiler_params=params(),
    )(
        table, row_block, row_used.astype(jnp.int32), divisor.reshape(1), got, late, master, first, second
    )


def doubled(values, step):
    return jnp.concatenate([values, exchange(values, step)], axis=0)


def gather_steps(values, order):
    for step in order[:0:-1]:
        values = doubled(values, step)
    return values, exchange(values, order[0])


def reduce_step(kept, got, step, extra=None):
    half = kept.shape[0] // 2
    given = kept[half:] + got[half:]
    if extra is None:
        return kept[:half] + got[:half], exchange(given, step)
    arrived = exchange(jnp.concatenate([given, extra]), step)
    return kept[:half] + got[:half], arrived[:half], extra + arrived[half:]


CHUNK = 128
PAIRS = HEADS // 2
MIXW = INNER + 2 * NSTATE
DT_AT = INNER + CONVCH
F32 = jnp.float32
BF16 = jnp.bfloat16
NN = (((1,), (0,)), ((), ()))
NT = (((1,), (1,)), ((), ()))


def dot(a, b, dims=NN):
    return lax.dot_general(a, b, dims, preferred_element_type=F32)


def split(v):
    high = v.astype(BF16)
    return high, (v - high.astype(F32)).astype(BF16)


def dot3(a, b, dims=NN):
    ah, al = a
    bh, bl = b
    return dot(ah, bh, dims) + (dot(ah, bl, dims) + dot(al, bh, dims))


def heads_gather():
    return jnp.asarray(np.repeat(np.eye(HEADS, LANES, dtype=np.float32), HEADDIM, axis=0), BF16)


def three_parts(v):
    high = v.astype(BF16).astype(F32)
    rest = v - high
    middle = rest.astype(BF16).astype(F32)
    low = rest - middle
    return (high + pltpu.roll(middle, 32, 1) + pltpu.roll(low, 64, 1)).astype(BF16)


def triangle_sum(tri, v):
    parts = dot(tri, three_parts(v))
    lane = lax.broadcasted_iota(jnp.int32, parts.shape, 1)
    total = parts + pltpu.roll(parts, LANES - 32, 1) + pltpu.roll(parts, LANES - 64, 1)
    return jnp.where(lane < HEADS, total, 0.0)


def chunk_decays(dt, dt_bias, a_log):
    lane = lax.broadcasted_iota(jnp.int32, (CHUNK, LANES), 1)
    row = lax.broadcasted_iota(jnp.int32, (CHUNK, LANES), 0)
    shifted = dt + dt_bias
    delta = jnp.where(
        lane < HEADS, jnp.maximum(shifted, 0.0) + jnp.log1p(jnp.exp(-jnp.abs(shifted))), 0.0
    )
    rate = -jnp.exp(a_log)
    lower = (row >= lane).astype(BF16)
    cum = triangle_sum(lower, delta * rate)
    last = cum[CHUNK - 1 : CHUNK, :]
    return shifted, delta, rate, cum, last


def pair_mask():
    lane = lax.broadcasted_iota(jnp.int32, (CHUNK, LANES), 1)
    low = (lane < HEADDIM).astype(F32)
    return low.astype(BF16), (1.0 - low).astype(BF16)


QUADS = HEADS // 4
QWIDTH = 4 * HEADDIM


def sigmoid(v):
    return 0.5 * jnp.tanh(0.5 * v) + 0.5


def silu(v):
    return v * sigmoid(v)


def side_by_side(v):
    high, low = split(v)
    return jnp.concatenate([high, low], axis=1), high


def dot_parts(a, b):
    ahl, ah = a
    bh, bl = b
    return dot(ahl, jnp.concatenate([bh, bh], axis=0)) + dot(ah, bl)


def dot_turned(a, b):
    ah, al = a
    bh, bl = b
    both = dot(ah, jnp.concatenate([bh, bl], axis=0), NT)
    n = bh.shape[0]
    return both[:, :n] + both[:, n:] + dot(al, bh, NT)


def widen(delta, cum, quad):
    lane = lax.broadcasted_iota(jnp.int32, (CHUNK, LANES), 1)
    over = lambda v, h: jnp.broadcast_to(v[:, h : h + 1], (CHUNK, LANES))
    first = 4 * quad
    columns = [over(cum, first + k) for k in range(4)]
    rates = [over(delta, first + k) for k in range(4)]
    pair = lambda vs: jnp.concatenate(
        [jnp.where(lane < HEADDIM, vs[0], vs[1]), jnp.where(lane < HEADDIM, vs[2], vs[3])], axis=1
    )
    return pair(rates), pair(columns), columns


def pair_rows(parts, j, low, high):
    cols = slice(j * LANES, (j + 1) * LANES)
    return [jnp.concatenate([p[:, cols] * low, p[:, cols] * high], axis=0) for p in parts]


def scan_chunk(mixed, dt, dt_bias, a_log, skip, state, put):
    _, delta, _, cum, last = chunk_decays(dt, dt_bias, a_log)
    lane = lax.broadcasted_iota(jnp.int32, (CHUNK, LANES), 1)
    row = lax.broadcasted_iota(jnp.int32, (CHUNK, LANES), 0)
    bias = jnp.where(row >= lane, 0.0, -1e30)
    cum_t = cum.T
    inputs_b = mixed[:, INNER : INNER + NSTATE]
    readout = mixed[:, INNER + NSTATE :]
    affinity = dot3(split(readout), split(inputs_b), NT)
    readout_parts = side_by_side(readout)
    b_parts = side_by_side(inputs_b.T)
    low, high = pair_mask()
    for quad in range(QUADS):
        cols = slice(quad * QWIDTH, (quad + 1) * QWIDTH)
        wide_delta, wide_cum, columns = widen(delta, cum, quad)
        values = mixed[:, cols]
        scaled = values * wide_delta
        parts = split(scaled)
        outs = []
        for j in range(2):
            right_h, right_l = pair_rows(parts, j, low, high)
            left = []
            for k in range(2):
                h = 4 * quad + 2 * j + k
                within = jnp.exp(columns[2 * j + k] - cum_t[h : h + 1, :] + bias)
                left.append(split(affinity * within))
            left_h = jnp.concatenate([left[0][0], left[1][0]], axis=1)
            left_l = jnp.concatenate([left[0][1], left[1][1]], axis=1)
            both = dot(left_h, jnp.concatenate([right_h, right_l], axis=1))
            outs.append(both[:, :LANES] + both[:, LANES:] + dot(left_l, right_h))
        carried = state[:, cols]
        grown = jnp.exp(wide_cum)
        out = jnp.concatenate(outs, axis=1) + dot_parts(readout_parts, split(carried)) * grown
        tail = jnp.exp(wide_cum[CHUNK - 1 :] - wide_cum)
        state[:, cols] = carried * grown[CHUNK - 1 :] + dot_parts(b_parts, split(scaled * tail))
        put(quad, out + skip[:, cols] * values)


FORWARD_ROWS = 2 * CHUNK


def forward_kernel(
    tokens, w_in, norm_gain, conv_weight, conv_bias, dt_bias, a_log, skip, gain,
    hidden, projected, mixed, ssm, mixed_out, states, state, before,
):
    @pl.when(pl.program_id(0) == 0)
    def _():
        state[...] = jnp.zeros_like(state)
        before[...] = jnp.zeros_like(before)

    x = tokens[...].astype(F32)
    inverse = lax.rsqrt(jnp.mean(x * x, axis=1, keepdims=True) + NORM_EPS)
    h = (x * inverse * norm_gain[...]).astype(BF16)
    hidden[...] = h
    projected[:, DT_AT:] = dot(h, w_in[:, DT_AT:])
    wide = 2 * LANES
    for tile in range(CONVCH // wide):
        at = tile * wide
        product = dot(h, w_in[:, INNER + at : INNER + at + wide])
        projected[:, INNER + at : INNER + at + wide] = product
        for half in range(2):
            cols = slice(at + half * LANES, at + (half + 1) * LANES)
            rows = product[:, half * LANES : (half + 1) * LANES]
            earlier = before[:, cols]
            terms = [down(rows, earlier, KCONV - 1 - k) for k in range(KCONV - 1)] + [rows]
            before[:, cols] = rows[FORWARD_ROWS - 8 :]
            mixed[:, cols] = silu(conv_sum(terms, conv_weight[:, cols], conv_bias[:, cols]))
    for tile in range(INNER // wide):
        cols = slice(tile * wide, (tile + 1) * wide)
        projected[:, cols] = dot(h, w_in[:, cols])
    for sub in range(FORWARD_ROWS // CHUNK):
        rows = slice(sub * CHUNK, (sub + 1) * CHUNK)
        states[sub] = state[...]
        squares = [jnp.zeros((CHUNK, LANES), F32)]

        def put(quad, out, rows=rows, squares=squares):
            cols = slice(quad * QWIDTH, (quad + 1) * QWIDTH)
            ssm[rows, cols] = out
            gated = out * silu(projected[rows, cols])
            first, second = gated[:, :LANES], gated[:, LANES:]
            squares[0] = squares[0] + first * first + second * second

        scan_chunk(
            mixed[rows, :], projected[rows, DT_AT:], dt_bias[...], a_log[...], skip, state, put
        )
        rho = lax.rsqrt(jnp.sum(squares[0], axis=1, keepdims=True) * (1.0 / INNER) + NORM_EPS)
        for j in range(PAIRS):
            cols = slice(j * LANES, (j + 1) * LANES)
            gated = ssm[rows, cols] * silu(projected[rows, cols])
            mixed_out[rows, cols] = (gated * rho * gain[:, cols]).astype(BF16)


def forward(tokens, w_in, norm_gain, conv_weight, conv_bias, dt_bias, a_log, skip, gain):
    length = tokens.shape[0]
    by_row = lambda width: pl.BlockSpec((FORWARD_ROWS, width), lambda i: (i, 0))
    whole = lambda v: pl.BlockSpec(v.shape, lambda i: (0,) * v.ndim)
    per_step = FORWARD_ROWS // CHUNK
    return pl.pallas_call(
        forward_kernel,
        grid=(length // FORWARD_ROWS,),
        out_shape=(
            shape((length, D), BF16),
            shape((length, WIDE), F32),
            shape((length, MIXW), F32),
            shape((length, INNER), F32),
            shape((length, INNER), BF16),
            shape((length // CHUNK, NSTATE, INNER), F32),
        ),
        in_specs=[by_row(D)]
        + [
            whole(v)
            for v in (w_in, norm_gain, conv_weight, conv_bias, dt_bias, a_log, skip, gain)
        ],
        out_specs=(
            by_row(D),
            by_row(WIDE),
            by_row(MIXW),
            by_row(INNER),
            by_row(INNER),
            pl.BlockSpec((per_step, NSTATE, INNER), lambda i: (i, 0, 0)),
        ),
        scratch_shapes=[pltpu.VMEM((NSTATE, INNER), F32), pltpu.VMEM((8, MIXW), F32)],
        compiler_params=params(),
        cost_estimate=cost(33),
    )(tokens, w_in, norm_gain, conv_weight, conv_bias, dt_bias, a_log, skip, gain)


def scan_backward_kernel(
    mixed, dt, ssm, grad, states, dt_bias, a_log, skip, gather, held,
    grad_mixed, grad_dt, sums, skip_sums, grad_state, left, right,
):
    @pl.when(pl.program_id(0) == 0)
    def _():
        grad_state[...] = jnp.zeros_like(grad_state)
        sums[...] = jnp.zeros_like(sums)
        skip_sums[...] = jnp.zeros_like(skip_sums)

    shifted, delta, rate, cum, last = chunk_decays(dt[...], dt_bias[...], a_log[...])
    lane = lax.broadcasted_iota(jnp.int32, (CHUNK, LANES), 1)
    row = lax.broadcasted_iota(jnp.int32, (CHUNK, LANES), 0)
    bias = jnp.where(lane >= row, 0.0, -1e30)
    heads = lane < HEADS
    cum_t = cum.T
    inputs_b = mixed[:, INNER : INNER + NSTATE]
    readout = mixed[:, INNER + NSTATE :]
    b_parts, c_parts = split(inputs_b), split(readout)
    b_wide = side_by_side(inputs_b)
    c_turned = side_by_side(readout.T)
    affinity = dot3(b_parts, c_parts, NT)
    low, high = pair_mask()
    grad_affinity = jnp.zeros((CHUNK, CHUNK), F32)
    grad_b = jnp.zeros((CHUNK, NSTATE), F32)
    grad_c = jnp.zeros((CHUNK, NSTATE), F32)
    last_row = lax.broadcasted_iota(jnp.int32, (CHUNK, QWIDTH), 0) == CHUNK - 1
    for quad in range(QUADS):
        cols = slice(quad * QWIDTH, (quad + 1) * QWIDTH)
        wide_delta, wide_cum, columns = widen(delta, cum, quad)
        grown = jnp.exp(wide_cum)
        tail = jnp.exp(wide_cum[CHUNK - 1 :] - wide_cum)
        end = grown[CHUNK - 1 :]
        values = mixed[:, cols]
        pulled = grad[:, cols]
        scaled = values * wide_delta
        x_parts, p_parts = split(scaled), split(pulled)
        outs = []
        for j in range(2):
            half = slice(j * LANES, (j + 1) * LANES)
            xh, xl = x_parts[0][:, half], x_parts[1][:, half]
            right_h, right_l = pair_rows(p_parts, j, low, high)
            pull = dot(
                jnp.concatenate([xh, xl], axis=1),
                jnp.concatenate([right_h, right_h], axis=1),
                NT,
            ) + dot(xh, right_l, NT)
            kernels = []
            for k in range(2):
                h = 4 * quad + 2 * j + k
                within = jnp.exp(cum_t[h : h + 1, :] - columns[2 * j + k] + bias)
                kernels.append(split(affinity * within))
                grad_affinity = grad_affinity + within * pull[:, k * CHUNK : (k + 1) * CHUNK]
            kernel_h = jnp.concatenate([kernels[0][0], kernels[1][0]], axis=1)
            kernel_l = jnp.concatenate([kernels[0][1], kernels[1][1]], axis=1)
            both = dot(kernel_h, jnp.concatenate([right_h, right_l], axis=1))
            outs.append(both[:, :LANES] + both[:, LANES:] + dot(kernel_l, right_h))
        late = grad_state[:, cols]
        late_parts = split(late)
        early = states[0, :, cols]
        from_state = dot_parts(b_wide, late_parts) * tail
        grad_scaled = jnp.concatenate(outs, axis=1) + from_state
        pulled_cum = split(pulled * grown)
        grad_c = grad_c + dot_turned(pulled_cum, split(early))
        grad_b = grad_b + dot_turned(split(scaled * tail), late_parts)
        grad_state[:, cols] = late * end + dot_parts(c_turned, pulled_cum)
        grad_mixed[:, cols] = grad_scaled * wide_delta + skip[:, cols] * pulled
        skip_sums[:, cols] += jnp.sum(pulled * values, axis=0, keepdims=True)
        left[:, cols] = grad_scaled * values
        inner = pulled * (ssm[:, cols] - skip[:, cols] * values) - scaled * grad_scaled
        extra = jnp.sum(scaled * from_state, axis=0, keepdims=True) + end * jnp.sum(
            late * early, axis=0, keepdims=True
        )
        right[:, cols] = inner + jnp.where(last_row, extra, 0.0)
    ga_parts = split(grad_affinity)
    grad_mixed[:, INNER : INNER + NSTATE] = grad_b + dot3(ga_parts, c_parts)
    grad_mixed[:, INNER + NSTATE :] = grad_c + dot3(split(grad_affinity.T), b_parts)

    def by_head(v):
        high, low = split(v)
        g = gather[...]
        return dot(high, g) + dot(low, g)

    direct = by_head(left[...])
    grad_cum = by_head(right[...])
    upper = (lane >= row).astype(BF16)
    after = triangle_sum(upper, grad_cum)
    grad_delta = direct + rate * after
    grad_raw = jnp.where(heads, grad_delta * sigmoid(shifted), 0.0)
    grad_dt[...] = grad_raw.astype(BF16)
    sums[0:1, :] += jnp.sum(grad_raw, axis=0, keepdims=True)
    sums[1:2, :] += rate * jnp.sum(delta * after, axis=0, keepdims=True)


def scan_backward(mixed, projected, ssm, grad, states, dt_bias, a_log, skip, gather, held):
    length = mixed.shape[0]
    chunks = length // CHUNK
    whole = lambda v: pl.BlockSpec(v.shape, lambda i: (0,) * v.ndim)
    back = lambda i: (chunks - 1 - i, 0)
    return pl.pallas_call(
        scan_backward_kernel,
        grid=(chunks,),
        out_shape=(
            shape((length, MIXW), F32),
            shape(held.shape, BF16),
            shape((8, LANES), F32),
            shape((1, INNER), F32),
        ),
        in_specs=[
            pl.BlockSpec((CHUNK, MIXW), back),
            pl.BlockSpec((CHUNK, LANES), lambda i: (chunks - 1 - i, DT_AT // LANES)),
            pl.BlockSpec((CHUNK, INNER), back),
            pl.BlockSpec((CHUNK, INNER), back),
            pl.BlockSpec((1, NSTATE, INNER), lambda i: (chunks - 1 - i, 0, 0)),
        ]
        + [whole(v) for v in (dt_bias, a_log, skip, gather)]
        + [ANY],
        out_specs=(
            pl.BlockSpec((CHUNK, MIXW), back),
            pl.BlockSpec((CHUNK, LANES), lambda i: (chunks - 1 - i, DT_AT // LANES)),
            pl.BlockSpec((8, LANES), lambda i: (0, 0)),
            pl.BlockSpec((1, INNER), lambda i: (0, 0)),
        ),
        scratch_shapes=[pltpu.VMEM((NSTATE, INNER), F32)] + [pltpu.VMEM((CHUNK, INNER), F32)] * 2,
        compiler_params=params(),
        input_output_aliases={9: 1},
        cost_estimate=cost(35),
    )(mixed, projected, ssm, grad, states, dt_bias, a_log, skip, gather, held)


ROWS_AT_ONCE = 128
CONV_TILES = 2


def down(v, before, by):
    moved = pltpu.roll(v, by, 0)
    row = lax.broadcasted_iota(jnp.int32, (8, LANES), 0)
    top = jnp.where(row < by, pltpu.roll(before, by, 0), moved[:8])
    return jnp.concatenate([top, moved[8:]], axis=0)


def up(v, after, by):
    rows = v.shape[0]
    moved = pltpu.roll(v, rows - by, 0)
    row = lax.broadcasted_iota(jnp.int32, (8, LANES), 0)
    end = jnp.where(row < 8 - by, moved[rows - 8 :], pltpu.roll(after, 8 - by, 0))
    return jnp.concatenate([moved[: rows - 8], end], axis=0)


def conv_terms(conv_in, at, cols):
    rows = conv_in[at : at + ROWS_AT_ONCE, cols]
    before = conv_in[at - 8 : at, cols] if at else jnp.zeros((8, LANES), F32)
    return [down(rows, before, KCONV - 1 - k) for k in range(KCONV - 1)] + [rows]


def conv_sum(terms, weight, bias):
    total = bias + terms[KCONV - 1] * weight[KCONV - 1 : KCONV]
    for k in range(KCONV - 1):
        total = total + terms[k] * weight[k : k + 1]
    return total


def conv_backward_kernel(conv_in, grad, weight, bias, held, out, sums):
    length = conv_in.shape[0]
    for tile in range(CONV_TILES):
        cols = slice(tile * LANES, (tile + 1) * LANES)
        w, b = weight[:, cols], bias[:, cols]
        totals = [jnp.zeros((1, LANES), F32)] * (KCONV + 1)
        after = jnp.zeros((8, LANES), F32)
        for at in range(length - ROWS_AT_ONCE, -1, -ROWS_AT_ONCE):
            terms = conv_terms(conv_in, at, cols)
            value = conv_sum(terms, w, b)
            sig = sigmoid(value)
            g = grad[at : at + ROWS_AT_ONCE, cols] * (sig * (1.0 + value * (1.0 - sig)))
            for k in range(KCONV):
                totals[k] = totals[k] + jnp.sum(g * terms[k], axis=0, keepdims=True)
            totals[KCONV] = totals[KCONV] + jnp.sum(g, axis=0, keepdims=True)
            total = g * w[KCONV - 1 : KCONV]
            for k in range(KCONV - 1):
                total = total + up(g, after, KCONV - 1 - k) * w[k : k + 1]
            after = g[:8]
            out[at : at + ROWS_AT_ONCE, cols] = total.astype(BF16)
        for k in range(KCONV + 1):
            sums[k : k + 1, cols] = totals[k]


def conv_backward(projected, grad_mixed, weight, bias, held):
    length = projected.shape[0]
    width = CONV_TILES * LANES
    return pl.pallas_call(
        conv_backward_kernel,
        grid=(CONVCH // width,),
        out_shape=(shape(held.shape, BF16), shape((8, CONVCH), F32)),
        in_specs=[
            pl.BlockSpec((length, width), lambda i: (0, INNER // width + i)),
            pl.BlockSpec((length, width), lambda i: (0, i)),
            pl.BlockSpec((KCONV, width), lambda i: (0, i)),
            pl.BlockSpec((1, width), lambda i: (0, i)),
            ANY,
        ],
        out_specs=(
            pl.BlockSpec((length, width), lambda i: (0, INNER // width + i)),
            pl.BlockSpec((8, width), lambda i: (0, i)),
        ),
        input_output_aliases={4: 0},
        compiler_params=params(),
        cost_estimate=cost(12),
    )(projected, grad_mixed, weight, bias, held)


def loss_kernel(
    limit, mixed_out, w_out, tokens, teacher, mask, block_out, grad_result, grad_branch, error
):
    step = pl.program_id(0)

    @pl.when(step == 0)
    def _():
        error[...] = jnp.zeros_like(error)

    rows = tokens.shape[0]
    result = tokens[...].astype(F32) + dot(mixed_out[...], w_out[...])
    position = step * rows + lax.broadcasted_iota(jnp.int32, (rows, 1), 0)
    valid = (position < limit[0]).astype(F32)
    turned = jnp.broadcast_to(mask[...].astype(F32), (LANES, rows)).T
    weight = valid * turned[:, 0:1]
    block_out[...] = (result * valid).astype(BF16)
    misfit = result - teacher[...].astype(F32)
    pulled = 2.0 * weight * misfit
    grad_result[...] = pulled
    errors = jnp.sum(0.5 * pulled * misfit, axis=0, keepdims=True)
    for j in range(D // LANES):
        error[j : j + 1, :] += errors[:, j * LANES : (j + 1) * LANES]
    error[D // LANES : D // LANES + 1, :] += jnp.sum(valid * turned, axis=0, keepdims=True)
    grad_branch[...] = pulled.astype(BF16)


def loss_part(limit, mixed_out, w_out, tokens, teacher, mask):
    length = tokens.shape[0]
    rows = 256
    by_row = lambda width: pl.BlockSpec((rows, width), lambda i: (i, 0))
    return pl.pallas_call(
        loss_kernel,
        grid=(length // rows,),
        out_shape=(
            shape((length, D), BF16),
            shape((length, D), F32),
            shape((length, D), BF16),
            shape((8, LANES), F32),
        ),
        in_specs=[
            SMEM,
            by_row(INNER),
            pl.BlockSpec(w_out.shape, lambda i: (0, 0)),
            by_row(D),
            by_row(D),
            pl.BlockSpec((1, rows), lambda i: (0, i)),
        ],
        out_specs=(by_row(D), by_row(D), by_row(D), pl.BlockSpec((8, LANES), lambda i: (0, 0))),
        compiler_params=params(),
        cost_estimate=cost(8),
    )(limit, mixed_out, w_out, tokens, teacher, mask)


def gate_kernel(grad_branch, w_out, ssm, gate, gain, grad_ssm, grad_gate, gain_sums):
    @pl.when(pl.program_id(0) == 0)
    def _():
        gain_sums[...] = jnp.zeros_like(gain_sums)

    grad_mixed = dot(grad_branch[...], w_out[...], NT)
    g = gate[...]
    sig = sigmoid(g)
    act = g * sig
    inner = ssm[...]
    gated = inner * act
    rho = lax.rsqrt(jnp.mean(gated * gated, axis=1, keepdims=True) + NORM_EPS)
    unit = gated * rho
    gain_sums[...] += jnp.sum(unit * grad_mixed, axis=0, keepdims=True)
    grad_unit = grad_mixed * gain[...]
    share = jnp.mean(grad_unit * unit, axis=1, keepdims=True)
    grad_gated = rho * (grad_unit - unit * share)
    grad_ssm[...] = grad_gated * act
    grad_gate[...] = (grad_gated * inner * (sig * (1.0 + g * (1.0 - sig)))).astype(BF16)


def gate_part(grad_branch, w_out, ssm, projected, gain):
    length = ssm.shape[0]
    rows = 256
    by_row = lambda width: pl.BlockSpec((rows, width), lambda i: (i, 0))
    whole = lambda v: pl.BlockSpec(v.shape, lambda i: (0,) * v.ndim)
    return pl.pallas_call(
        gate_kernel,
        grid=(length // rows,),
        out_shape=(shape((length, INNER), F32), shape((length, WIDE), BF16), shape((1, INNER), F32)),
        in_specs=[by_row(D), whole(w_out), by_row(INNER), by_row(INNER), whole(gain)],
        out_specs=(by_row(INNER), by_row(INNER), pl.BlockSpec((1, INNER), lambda i: (0, 0))),
        compiler_params=params(),
        cost_estimate=cost(12),
    )(grad_branch, w_out, ssm, projected, gain)


def input_kernel(grad_low, w_in, tokens, norm_gain, grad_result, out, sums):
    @pl.when(pl.program_id(0) == 0)
    def _():
        sums[...] = jnp.zeros_like(sums)

    x = tokens[...].astype(F32)
    inverse = lax.rsqrt(jnp.mean(x * x, axis=1, keepdims=True) + NORM_EPS)
    unit = x * inverse
    grad_hidden = dot(grad_low[...], w_in[...], NT)
    sums[...] += jnp.sum(grad_hidden * unit, axis=0, keepdims=True)
    pulled = grad_hidden * norm_gain[...]
    share = jnp.mean(pulled * unit, axis=1, keepdims=True)
    out[...] = grad_result[...] + inverse * (pulled - unit * share)


def input_backward(grad_low, w_in, tokens, norm_gain, grad_result):
    length = tokens.shape[0]
    rows = 256
    by_row = lambda width: pl.BlockSpec((rows, width), lambda i: (i, 0))
    whole = lambda v: pl.BlockSpec(v.shape, lambda i: (0,) * v.ndim)
    return pl.pallas_call(
        input_kernel,
        grid=(length // rows,),
        out_shape=(shape((length, D), F32), shape((1, D), F32)),
        in_specs=[by_row(WIDE), whole(w_in), by_row(D), whole(norm_gain), by_row(D)],
        out_specs=(by_row(D), pl.BlockSpec((1, D), lambda i: (0, 0))),
        compiler_params=params(),
        cost_estimate=cost(15),
    )(grad_low, w_in, tokens, norm_gain, grad_result)


def vector_kernel(tail, conv_sums, sums, skip_sums, norm_sums, gate_sums, gather, out, taps):
    tiles = CONVCH // LANES
    out[...] = jnp.zeros_like(out)
    out[0:TAIL_ROWS, :] = tail[...]
    for k in range(KCONV):
        for i in range(tiles):
            taps[k * 16 + i : k * 16 + i + 1, :] = conv_sums[k : k + 1, i * LANES : (i + 1) * LANES]
    row = lax.broadcasted_iota(jnp.int32, (LANES, LANES), 0)
    col = lax.broadcasted_iota(jnp.int32, (LANES, LANES), 1)
    per_tile = LANES // KCONV

    def exact(v, chosen):
        high = v.astype(BF16)
        rest = v - high.astype(F32)
        middle = rest.astype(BF16)
        low = (rest - middle.astype(F32)).astype(BF16)
        return dot(high, chosen) + (dot(middle, chosen) + dot(low, chosen))

    for q in range(KCONV):
        total = jnp.zeros((tiles, LANES), F32)
        for k in range(KCONV):
            chosen = (col == KCONV * (row % per_tile) + k) & (row // per_tile == q)
            total = total + exact(taps[k * 16 : k * 16 + tiles, :], chosen.astype(BF16))
        out[pl.ds(TAIL_ROWS + q, tiles, stride=KCONV), :] = total
    bias_at = TAIL_ROWS + tiles * KCONV
    for i in range(tiles):
        out[bias_at + i : bias_at + i + 1, :] = conv_sums[KCONV : KCONV + 1, i * LANES : (i + 1) * LANES]
    lane = lax.broadcasted_iota(jnp.int32, (1, LANES), 1)
    skip = exact(jnp.broadcast_to(skip_sums[...], (8, INNER)), gather[...])[0:1, :]
    parts = [sums[0:1, :], sums[1:2, :], skip]
    parts = [jnp.where(lane < HEADS, v, 0.0) for v in parts]
    before = parts[0] + pltpu.roll(parts[1], HEADS, 1) + pltpu.roll(parts[2], 2 * HEADS, 1)
    at, shift = bias_at + tiles, 3 * HEADS
    for source in (norm_sums, gate_sums):
        for j in range(source.shape[1] // LANES):
            here = pltpu.roll(source[:, j * LANES : (j + 1) * LANES], shift, 1)
            out[at : at + 1, :] = jnp.where(lane < shift, before, here)
            before = here
            at += 1
    out[at : at + 1, :] = jnp.where(lane < shift, before, 0.0)


def pack_vectors(tail, conv_sums, sums, skip_sums, norm_sums, gate_sums, gather):
    return pl.pallas_call(
        vector_kernel,
        out_shape=shape(((NBLK - MID1) * BROWS, LANES), F32),
        in_specs=[VMEM] * 7,
        out_specs=VMEM,
        scratch_shapes=[pltpu.VMEM((KCONV * 16, LANES), F32)],
        compiler_params=params(),
    )(tail, conv_sums, sums, skip_sums, norm_sums, gate_sums, gather)


def body(tokens, teacher, lengths, loss_mask, owners, master, first_moment, second_moment):
    capacity = master.shape[0]
    dp, fsdp = lax.axis_size("dp"), lax.axis_size("fsdp")
    devices = dp * fsdp
    me = lax.axis_index(AXES).astype(jnp.int32)
    x_first, y_first, z_first = step_orders(dp, fsdp)
    tie = lambda *values: lax.optimization_barrier(values)

    sent = send_blocks(owners, master, devices, me)
    at_home = lax.all_to_all(sent, AXES, 0, 0, tiled=True)
    owners, tokens, loss_mask, _ = tie(owners, tokens, loss_mask, sent)
    plan = make_plan(owners, capacity, devices, me)
    streams = cut(even(plan["slots"], 3), (x_first, y_first, z_first))
    table = stream_places(plan["home"], plan["slot"], me, streams, devices)
    u0, u1 = plan["unit_slots"]
    sizes = [-(-u0 // 5)] * 4
    unit_streams = cut(sizes + [u0 - sum(sizes)], (x_first, y_first, x_first, y_first, z_first))
    unit_table = stream_places(plan["unit_home"], plan["unit_slot"], me, unit_streams, devices)
    unit_table = unit_table[:MID0].reshape(-1)
    unit_table1 = place_of(plan["unit_home"] ^ me, x_first) * (u1 + 1) + plan["unit_slot"]
    unit_table1 = unit_table1[MID0:MID1].reshape(-1)
    inputs, target = tokens[0], teacher[0]
    (at_home, table, unit_table, unit_table1, received, back_table, row_from, row_block,
     row_used) = tie(
        at_home, table, unit_table, unit_table1, plan["received"], plan["back"],
        plan["row_from"], plan["row_block"], plan["row_used"],
    )
    mine = pick_blocks(received, at_home, [size for _, size, _ in streams])
    parts = []
    for values, (_, _, order) in zip(mine, streams):
        parts += gather_steps(values, order)
    (input_weight, output_weight, conv_weight, conv_bias, dt_bias, a_log, skip, norm_gain,
     gate_gain) = unpack(table, parts)
    gather = heads_gather()
    hidden, projected, mixed, ssm, mixed_out, states = forward(
        inputs, input_weight, norm_gain, conv_weight, conv_bias, dt_bias, a_log, skip, gate_gain
    )
    block_out, grad_result, grad_branch, local = loss_part(
        lengths, mixed_out, output_weight, inputs, target, loss_mask
    )
    keep1, send1, head, tail = pack_out(
        unit_table1, mixed_out, grad_branch, local, devices, u1 + 1
    )
    grad_branch, send1 = tie(grad_branch, send1)
    got1 = exchange(send1, x_first[0])
    grad_ssm, grad_low, grad_gate = gate_part(grad_branch, output_weight, ssm, projected, gate_gain)
    grad_ssm, keep1, got1 = tie(grad_ssm, keep1, got1)
    keep1, got1 = reduce_step(keep1, got1, x_first[1])
    grad_mixed, grad_low, sums, skip_sums = scan_backward(
        mixed, projected, ssm, grad_ssm, states, dt_bias, a_log, skip, gather, grad_low
    )
    grad_mixed, keep1, got1 = tie(grad_mixed, keep1, got1)
    steps1 = x_first[2:]
    for step in steps1[:1]:
        keep1, got1 = reduce_step(keep1, got1, step)
    grad_low, conv_sums = conv_backward(projected, grad_mixed, conv_weight, conv_bias, grad_low)
    grad_low, keep1, got1 = tie(grad_low, keep1, got1)
    for step in steps1[1:2]:
        keep1, got1 = reduce_step(keep1, got1, step)
    halves = []
    for _, size, _ in unit_streams:
        halves += [devices * size // 2] * 2
    packed = list(pack_in(unit_table, hidden, grad_low, head, halves))
    packed[0], keep1, got1 = tie(packed[0], keep1, got1)
    kept = packed[::2]
    got = [exchange(v, order[0]) for v, (_, _, order) in zip(packed[1::2], unit_streams)]
    *got, grad_low, conv_sums, tail = tie(*got, grad_low, conv_sums, tail)
    for i, (_, _, order) in enumerate(unit_streams):
        kept[i], got[i] = reduce_step(kept[i], got[i], order[1])
    for step in steps1[2:3]:
        keep1, got1 = reduce_step(keep1, got1, step)
    input_grad, norm_sums = input_backward(grad_low, input_weight, inputs, norm_gain, grad_result)
    grad_vec = pack_vectors(tail, conv_sums, sums, skip_sums, norm_sums, grad_gate, gather)
    grad_vec = grad_vec.reshape((NBLK - MID1) * UNITS, UNIT, LANES)
    *got, got1, grad_vec, input_grad = tie(*got, got1, grad_vec, input_grad)
    for step in steps1[3:]:
        keep1, got1 = reduce_step(keep1, got1, step)
    for k in range(2, len(x_first)):
        for i, (_, _, order) in enumerate(unit_streams):
            if i == 0:
                kept[i], got[i], grad_vec = reduce_step(kept[i], got[i], order[k], grad_vec)
            else:
                kept[i], got[i] = reduce_step(kept[i], got[i], order[k])
    back = units_to_owners(back_table, list(zip(kept + [keep1], got + [got1])))
    back, grad_vec = tie(back, grad_vec)
    returned = lax.all_to_all(back, AXES, 0, 0, tiled=True)
    for step in x_first[:2]:
        grad_vec = grad_vec + exchange(grad_vec, step)
    local_sums = keep1[u1] + got1[u1]
    error_sum = jnp.sum(local_sums[: D // LANES])
    divisor = local_sums[D // LANES, 0] * D
    new_first, new_second, new_master = adam(
        row_from,
        row_block,
        row_used,
        divisor,
        returned,
        grad_vec,
        master,
        first_moment,
        second_moment,
    )
    mean_loss = error_sum / divisor
    return (block_out[None], input_grad[None], mean_loss, new_first, new_second, new_master)


def solution(mesh):
    return jax.shard_map(
        body,
        mesh=mesh,
        in_specs=(
            P(AXES, None, None),
            P(AXES, None, None),
            P(AXES),
            P(AXES, None),
            P(),
            P(AXES, None),
            P(AXES, None),
            P(AXES, None),
        ),
        out_specs=(
            P(AXES, None, None),
            P(AXES, None, None),
            P(),
            P(AXES, None),
            P(AXES, None),
            P(AXES, None),
        ),
        check_vma=False,
    )
```

```python
from functools import partial

import jax
import jax.numpy as jnp
import numpy as np
from jax import lax
from jax.experimental import pallas as pl
from jax.experimental.pallas import tpu as pltpu
from jax.sharding import PartitionSpec as P

D = 768
INNER = 1536
NSTATE = 128
HEADDIM = 64
KCONV = 4
SCAN_LEN = 256
PBLOCK = 4096
STEP = 10
HEADS = 24
CONVCH = 1792
PROJ = 3352
PTOT = 3765320
NBLK = 920

LANES = 128
BROWS = PBLOCK // LANES
UNIT = 8
UNITS = BROWS // UNIT
END_IN = D * PROJ
END_OUT = END_IN + INNER * D
MID0 = -(-END_IN // PBLOCK)
MID1 = END_OUT // PBLOCK
N0 = MID0 + NBLK - MID1
N1 = MID1 - MID0
F0_ROWS = N0 * BROWS
IN_ROWS = END_IN // LANES
HEAD_ROWS = MID0 * BROWS - IN_ROWS
TAIL_ROWS = (END_OUT - MID1 * PBLOCK) // LANES
OUT_ROWS = INNER * D // LANES
VEC_ROWS = (NBLK - MID1) * BROWS - TAIL_ROWS
VEC_AT = MID0 * BROWS + TAIL_ROWS
GROUP = 16
GROUPS = D // GROUP
GROUP_ROWS = GROUP * PROJ // LANES
COL_TILES = -(-PROJ // LANES)
WIDE = COL_TILES * LANES
OUT_TILES = D // LANES

NORM_EPS = 1e-05
ADAM_EPS = 1e-08
BETA_ONE = 0.9
BETA_TWO = 0.999
MATRIX_RATE = 0.03
VECTOR_RATE = 0.2
WEIGHT_DECAY = 0.1
PRECISE = lax.Precision.HIGHEST
AXES = ("dp", "fsdp")
VMEM_LIMIT = 60 * 1024 * 1024


def bits_of(count):
    return count.bit_length() - 1


def step_orders(dp, fsdp):
    wide = [("dp", i) for i in range(bits_of(dp))]
    narrow = [("fsdp", i) for i in range(bits_of(fsdp))]
    first = wide[:2] + narrow + wide[2:]
    second = wide[:1] + narrow + wide[1:]
    third = wide[:1] + wide[2:] + wide[1:2] + narrow
    return first, second, third


def cut(sizes, orders):
    streams, at = [], 0
    for size, order in zip(sizes, orders):
        if size:
            streams.append((at, size, order))
        at += size
    return streams


def even(total, parts):
    return [total // parts + (i < total % parts) for i in range(parts)]


def exchange(values, *steps):
    axes = {axis for axis, _ in steps}
    if len(axes) == 1:
        (axis,) = axes
        mask = sum(1 << bit for _, bit in steps)
        pairs = [(i, i ^ mask) for i in range(lax.axis_size(axis))]
        return lax.ppermute(values, axis, pairs)
    low = bits_of(lax.axis_size("fsdp"))
    mask = sum(1 << (bit + (low if axis == "dp" else 0)) for axis, bit in steps)
    count = lax.axis_size("dp") * lax.axis_size("fsdp")
    return lax.ppermute(values, AXES, [(i, i ^ mask) for i in range(count)])


def place_of(relative, order):
    shift_of = {"dp": bits_of(lax.axis_size("fsdp")), "fsdp": 0}
    place = jnp.zeros_like(relative)
    for axis, bit in order:
        place = place * 2 + ((relative >> (shift_of[axis] + bit)) & 1)
    return place


def class_counts(owners, devices):
    block = jnp.arange(NBLK, dtype=jnp.int32)
    mid = ((block >= MID0) & (block < MID1))[None, :]
    device = jnp.arange(devices, dtype=jnp.int32)
    below = owners[None, :] < device[:, None]
    owned = owners[None, :] == device[:, None]

    def total(mask):
        return jnp.sum(mask.astype(jnp.int32), axis=1)

    start = (total(below & ~mid), total(below & mid))
    count = (total(owned & ~mid), total(owned & mid))
    return start, count, total(owned & (block < MID0)[None, :])


def my_counts(owners, me):
    block = jnp.arange(NBLK, dtype=jnp.int32)
    mid = (block >= MID0) & (block < MID1)
    below, owned = owners < me, owners == me
    total = lambda mask: jnp.sum(mask.astype(jnp.int32))
    start = (total(below & ~mid), total(below & mid))
    count = (total(owned & ~mid), total(owned & mid))
    return start, count, total(owned & (block < MID0))


def pair_lanes(capacity, devices):
    return -(-capacity // devices)


def make_plan(owners, capacity, devices, me):
    block = jnp.arange(NBLK, dtype=jnp.int32)
    mid = (block >= MID0) & (block < MID1)
    same = mid[:, None] == mid[None, :]
    before = (owners[None, :] < owners[:, None]) | (
        (owners[None, :] == owners[:, None]) & (block[None, :] < block[:, None])
    )
    order = jnp.sum(before.astype(jnp.int32), axis=1)
    order_in_class = jnp.sum((same & before).astype(jnp.int32), axis=1)
    home, slot = order % devices, order // devices
    device = jnp.arange(devices, dtype=jnp.int32)
    start, count, _ = class_counts(owners, devices)
    my_start, my_count, my_early = my_counts(owners, me)
    pair = pair_lanes(capacity, devices)

    slots = -(-NBLK // devices)
    wanted = me + devices * jnp.arange(slots, dtype=jnp.int32)
    first = start[0] + start[1]
    ends = first + count[0] + count[1]
    owner = jnp.sum((ends[None, :] <= wanted[:, None]).astype(jnp.int32), axis=1)
    owner = jnp.minimum(owner, devices - 1)
    base = jnp.sum(jnp.where(device[None, :] == owner[:, None], first[None, :], 0), axis=1)
    received = owner * pair + jnp.clip((wanted - base) // devices, 0, pair - 1)

    back_pair = (UNITS * capacity + 2 * (devices - 1)) // devices
    unit = UNITS * order_in_class[:, None] + jnp.arange(UNITS, dtype=jnp.int32)[None, :]
    unit_home, unit_slot = unit % devices, unit // devices
    unit_slots = (-(-UNITS * N0 // devices), -(-UNITS * N1 // devices))
    lane = jnp.arange(back_pair, dtype=jnp.int32)

    def units_back(kind):
        turn = lane if kind == 0 else back_pair - 1 - lane
        first = UNITS * start[kind][:, None]
        k = (me - first) % devices + turn[None, :] * devices
        return k < UNITS * count[kind][:, None], (first + k) // devices

    valid0, slot0 = units_back(0)
    valid1, slot1 = units_back(1)
    back = jnp.where(valid0, slot0, jnp.where(valid1, unit_slots[0] + slot1, 0)).reshape(-1)

    row = jnp.arange(capacity, dtype=jnp.int32)
    is_mid = (row >= my_early) & (row < my_early + my_count[1])
    k = jnp.where(is_mid, row - my_early, jnp.where(row < my_early, row, row - my_count[1]))
    first = UNITS * jnp.where(is_mid, my_start[1], my_start[0])
    k = UNITS * k[:, None] + jnp.arange(UNITS, dtype=jnp.int32)[None, :]
    turn = k // devices
    row_from = ((first[:, None] + k) % devices) * back_pair + jnp.where(
        is_mid[:, None], back_pair - 1 - turn, turn
    )
    row_used = row < my_count[0] + my_count[1]
    mine = (owners == me)[None, :]
    rank = jnp.sum((mine & (block[None, :] < block[:, None])).astype(jnp.int32), axis=1)
    row_block = jnp.sum(
        jnp.where(mine & (rank[None, :] == row[:, None]), block[None, :], 0), axis=1
    )
    late = devices * back_pair + UNITS * (row_block - MID1)
    late = late[:, None] + jnp.arange(UNITS, dtype=jnp.int32)[None, :]
    row_from = jnp.where((row_block >= MID1)[:, None], late, row_from)
    row_from = jnp.where(row_used[:, None], row_from, 0).reshape(-1)
    return dict(
        home=home, slot=slot, slots=slots,
        received=received, unit_home=unit_home, unit_slot=unit_slot,
        unit_slots=unit_slots, back=back, row_from=row_from,
        row_used=row_used, row_block=row_block,
    )


def stream_places(home, slot, me, streams, devices):
    relative = home ^ me
    place = jnp.zeros_like(slot)
    for begin, size, order in streams:
        inside = (slot >= begin) & (slot < begin + size)
        at = devices * begin + place_of(relative, order) * size + slot - begin
        place = jnp.where(inside, at, place)
    return place


def cost(microseconds):
    return pl.CostEstimate(
        flops=int(microseconds * 1e9), bytes_accessed=int(microseconds * 3e6), transcendentals=0
    )


ANY = pl.BlockSpec(memory_space=pl.ANY)
VMEM = pl.BlockSpec(memory_space=pltpu.VMEM)
SMEM = pl.BlockSpec(memory_space=pltpu.SMEM)


def params(**extra):
    return pltpu.CompilerParams(vmem_limit_bytes=VMEM_LIMIT, **extra)


def shape(dims, dtype):
    return jax.ShapeDtypeStruct(dims, dtype)


def send_kernel(my_index, owners, master, out, flat, *, devices):
    capacity = master.shape[0]
    me = my_index[0]
    for j in range(BROWS):
        flat[pl.ds(j, capacity, stride=BROWS), :] = master[:, j * LANES : (j + 1) * LANES]
    held = owners[...]
    below, owned = held < me, held == me

    def total(mask):
        return jnp.sum(jnp.where(mask, 1.0, 0.0)).astype(jnp.int32)

    start, count = total(below), total(owned)
    pair = out.shape[0] // devices

    def step(home, carry):
        for s in range(pair):
            k = lax.rem(home - start + devices * NBLK, devices) + s * devices
            row = jnp.where(k < count, k, 0)
            rows = pl.ds(pl.multiple_of(row * BROWS, BROWS), BROWS)
            out[home * pair + s] = flat[rows, :].astype(out.dtype)
        return carry

    lax.fori_loop(0, devices, step, 0)


def send_blocks(owners, master, devices, me):
    rows = -(-NBLK // (8 * LANES)) * 8
    held = jnp.pad(owners, (0, rows * LANES - NBLK), constant_values=1 << 20).reshape(rows, LANES)
    count = devices * pair_lanes(master.shape[0], devices)
    return pl.pallas_call(
        partial(send_kernel, devices=devices),
        out_shape=shape((count, BROWS, LANES), jnp.bfloat16),
        in_specs=[SMEM, VMEM, VMEM],
        out_specs=VMEM,
        scratch_shapes=[pltpu.VMEM((master.shape[0] * BROWS, LANES), jnp.float32)],
        compiler_params=params(),
    )(me.reshape(1), held, master)


def pick_kernel(table, source, *outs):
    at = 0
    for out in outs:

        def step(i, carry, out=out, at=at):
            out[i] = source[table[at + i]]
            return carry

        lax.fori_loop(0, out.shape[0], step, 0)
        at += out.shape[0]


def pick_blocks(table, source, sizes):
    return pl.pallas_call(
        pick_kernel,
        out_shape=tuple(shape((n,) + source.shape[1:], source.dtype) for n in sizes),
        in_specs=[SMEM, VMEM],
        out_specs=(VMEM,) * len(sizes),
        compiler_params=params(),
    )(table, source)


def back_kernel(table, *refs, sizes):
    sources, (out, held) = refs[:-2], refs[-2:]
    at = i = 0
    for size in sizes:
        n = sources[i].shape[0]
        total = sources[i][...]
        for k in range(1, size):
            total = total + sources[i + k][0:n]
        held[at : at + n] = total
        at += n
        i += size

    def step(i, carry):
        for u in range(8):
            out[i * 8 + u] = held[table[i * 8 + u]]
        return carry

    total = out.shape[0]
    lax.fori_loop(0, total // 8, step, 0)


def units_to_owners(table, groups):
    return pl.pallas_call(
        partial(back_kernel, sizes=[len(g) for g in groups]),
        out_shape=shape((table.shape[0], UNIT, LANES), jnp.float32),
        in_specs=[SMEM] + [VMEM] * sum(len(g) for g in groups),
        out_specs=VMEM,
        scratch_shapes=[pltpu.VMEM((sum(g[0].shape[0] for g in groups), UNIT, LANES), jnp.float32)],
        compiler_params=params(),
    )(table, *[v for g in groups for v in g])


def row_start(rho):
    return (PROJ * rho) // LANES, (PROJ * rho) % LANES


def copy_all(pairs, sem):
    copies = [pltpu.make_async_copy(a, b, sem.at[i]) for i, (a, b) in enumerate(pairs)]
    for c in copies:
        c.start()
    for c in copies:
        c.wait()


def spread_blocks(table, first, held, flat, count, first_row):
    def one(i):
        at = pl.multiple_of(first_row + i * BROWS, 16)
        flat[pl.ds(at, BROWS), :] = held[table[first + i]].astype(jnp.float32)

    def step(i, carry):
        for u in range(4):
            one(i * 4 + u)
        return carry

    lax.fori_loop(0, count // 4, step, 0)
    for i in range(count // 4 * 4, count):
        one(i)


def unpack_vectors(flat, conv_weight, conv_bias, dt_bias, a_log, skip, norm_gain, gate_gain):
    bf16, f32 = jnp.bfloat16, jnp.float32
    tiles = CONVCH // LANES
    row = lax.broadcasted_iota(jnp.int32, (LANES, LANES), 0)
    col = lax.broadcasted_iota(jnp.int32, (LANES, LANES), 1)
    per_tile = LANES // KCONV
    for k in range(KCONV):
        total = jnp.zeros((tiles, LANES), f32)
        for q in range(KCONV):
            rows = flat[pl.ds(VEC_AT + q, tiles, stride=KCONV), :].astype(bf16)
            chosen = (row == KCONV * (col % per_tile) + k) & (col // per_tile == q)
            total = total + jnp.dot(rows, chosen.astype(bf16), preferred_element_type=f32)
        for i in range(tiles):
            conv_weight[k : k + 1, i * LANES : (i + 1) * LANES] = total[i : i + 1, :]
    bias_at = VEC_AT + tiles * KCONV
    for i in range(tiles):
        conv_bias[:, i * LANES : (i + 1) * LANES] = flat[bias_at + i : bias_at + i + 1, :]
    at = bias_at + tiles
    lane = lax.broadcasted_iota(jnp.int32, (8, LANES), 1)
    first = flat[at : at + 8, :]
    three = []
    for i in range(3):
        moved = pltpu.roll(first, LANES - i * HEADS, 1) if i else first
        three.append(jnp.where(lane < HEADS, moved, 0.0))
    dt_bias[...] = three[0][0:1, :]
    a_log[...] = three[1][0:1, :]
    for j in range(INNER // LANES):
        h = lax.broadcasted_iota(jnp.int32, (LANES, LANES), 0)
        c = lax.broadcasted_iota(jnp.int32, (LANES, LANES), 1) + j * LANES
        spread = (h == c // HEADDIM).astype(bf16)
        wide = jnp.dot(three[2].astype(bf16), spread, preferred_element_type=f32)
        skip[:, j * LANES : (j + 1) * LANES] = wide[0:1, :]
    shift = 3 * HEADS
    for out, begin, width in ((norm_gain, at, D), (gate_gain, at + D // LANES, INNER)):
        for j in range(width // LANES):
            x = pltpu.roll(flat[begin + j : begin + j + 1, :], LANES - shift, 1)
            y = pltpu.roll(flat[begin + j + 1 : begin + j + 2, :], LANES - shift, 1)
            out[:, j * LANES : (j + 1) * LANES] = jnp.where(lane[0:1] < LANES - shift, x, y)


def unpack_kernel(table, *refs):
    parts, outs, scratch = refs[:-14], refs[-14:-5], refs[-5:]
    w_in, w_out, *vectors = outs
    held, flat, flat_out, tile, sem = scratch
    pairs, at = [], 0
    for part in parts:
        pairs.append((part, held.at[pl.ds(at, part.shape[0])]))
        at += part.shape[0]
    copy_all(pairs, sem)
    spread_blocks(table, 0, held, flat, MID0, 0)
    spread_blocks(table, MID1, held, flat, NBLK - MID1, MID0 * BROWS)
    spread_blocks(table, MID0, held, flat_out, N1, HEAD_ROWS)
    flat_out[0:HEAD_ROWS, :] = flat[IN_ROWS : IN_ROWS + HEAD_ROWS, :]
    flat_out[OUT_ROWS - TAIL_ROWS :, :] = flat[MID0 * BROWS : MID0 * BROWS + TAIL_ROWS, :]
    unpack_vectors(flat, *vectors)
    rows = 128

    def out_step(i, carry):
        at = pl.multiple_of(i * rows, rows)
        for j in range(OUT_TILES):
            x = flat_out[pl.ds(at * OUT_TILES + j, rows, stride=OUT_TILES), :]
            w_out[pl.ds(at, rows), j * LANES : (j + 1) * LANES] = x.astype(jnp.bfloat16)
        return carry

    lax.fori_loop(0, INNER // rows, out_step, 0)
    lane = lax.broadcasted_iota(jnp.int32, (GROUPS, LANES), 1)

    def columns(j):
        for rho in range(GROUP):
            c, s = row_start(rho)
            x = flat[pl.ds(c + j, GROUPS, stride=GROUP_ROWS), :]
            if s:
                y = flat[pl.ds(c + j + 1, GROUPS, stride=GROUP_ROWS), :]
                x = jnp.where(
                    lane < LANES - s,
                    pltpu.roll(x, LANES - s, 1),
                    pltpu.roll(y, LANES - s, 1),
                )
            tile[pl.ds(rho, GROUPS, stride=GROUP), :] = x

    def step(j, carry):
        columns(j)
        w_in[:, pl.ds(pl.multiple_of(j * LANES, LANES), LANES)] = tile[...].astype(jnp.bfloat16)
        return carry

    lax.fori_loop(0, COL_TILES - 1, step, 0)
    columns(COL_TILES - 1)
    last = (COL_TILES - 1) * LANES
    inside = lax.broadcasted_iota(jnp.int32, (D, LANES), 1) < PROJ - last
    w_in[:, last:] = jnp.where(inside, tile[...], 0.0).astype(jnp.bfloat16)


def unpack(table, parts):
    held = sum(part.shape[0] for part in parts)
    f32 = jnp.float32
    return pl.pallas_call(
        unpack_kernel,
        out_shape=(
            shape((D, WIDE), jnp.bfloat16),
            shape((INNER, D), jnp.bfloat16),
            shape((KCONV, CONVCH), f32),
            shape((1, CONVCH), f32),
            shape((1, LANES), f32),
            shape((1, LANES), f32),
            shape((1, INNER), f32),
            shape((1, D), f32),
            shape((1, INNER), f32),
        ),
        in_specs=[SMEM] + [ANY] * len(parts),
        out_specs=(VMEM,) * 9,
        scratch_shapes=[
            pltpu.VMEM((held, BROWS, LANES), jnp.bfloat16),
            pltpu.VMEM((F0_ROWS, LANES), f32),
            pltpu.VMEM((OUT_ROWS, LANES), f32),
            pltpu.VMEM((D, LANES), f32),
            pltpu.SemaphoreType.DMA((len(parts),)),
        ],
        compiler_params=params(),
        cost_estimate=cost(20),
    )(table, *parts)


def permute_units(table, flat, count, first_row, staged):
    many = 16

    def step(i, carry):
        for u in range(many):
            at = pl.multiple_of(first_row + (i * many + u) * UNIT, UNIT)
            staged[table[i * many + u]] = flat[pl.ds(at, UNIT), :]
        return carry

    lax.fori_loop(0, count // many, step, 0)
    for i in range(count // many * many, count):
        staged[table[i]] = flat[first_row + i * UNIT : first_row + (i + 1) * UNIT, :]


def pack_in_kernel(table, hidden, grad, head, *refs):
    outs, (turned, tiles, flat, staged, sem) = refs[:-5], refs[-5:]
    turned[...] = hidden[...].T
    lane = lax.broadcasted_iota(jnp.int32, (GROUPS, LANES), 1)

    def product(p, count):
        at = p * 2 * LANES
        at = at if isinstance(at, int) else pl.multiple_of(at, 2 * LANES)
        return jnp.dot(
            turned[...], grad[:, pl.ds(at, count * LANES)], preferred_element_type=jnp.float32
        )

    def put(p, value):
        for k in range(value.shape[1] // LANES):
            at = (p * 2 + k) * D
            at = at if isinstance(at, int) else pl.multiple_of(at, D)
            tiles[pl.ds(at, D), :] = value[:, k * LANES : (k + 1) * LANES]

    def load(rho, j):
        return tiles[pl.ds(j * D + rho, GROUPS, stride=GROUP), :]

    def whole(rho, i):
        first = -(-PROJ * rho // LANES)
        col0 = first * LANES - PROJ * rho
        x = load(rho, i)
        if col0:
            x = jnp.where(
                lane < LANES - col0,
                pltpu.roll(x, LANES - col0, 1),
                pltpu.roll(load(rho, i + 1), LANES - col0, 1),
            )
        flat[pl.ds(first + i, GROUPS, stride=GROUP_ROWS), :] = x

    put(0, product(0, 2))
    put(1, product(1, 2))
    pairs = COL_TILES // 2

    def step(p, carry):
        for i in range(2):
            for rho in range(GROUP):
                whole(rho, p * 2 + i)
        put(p + 2, product(p + 2, 2))
        return carry

    lax.fori_loop(0, pairs - 2, step, 0)
    put(pairs, product(pairs, COL_TILES % 2))
    for rho in range(GROUP):
        first = -(-PROJ * rho // LANES)
        col0 = first * LANES - PROJ * rho
        full = (PROJ - col0) // LANES
        for i in range((pairs - 2) * 2, full):
            whole(rho, i)
        left = PROJ - col0 - full * LANES
        if left:
            begin = col0 + full * LANES
            j, s = begin // LANES, begin % LANES
            x = pltpu.roll(load(rho, j), LANES - s, 1) if s else load(rho, j)
            if s + left > LANES:
                x = jnp.where(lane < LANES - s, x, pltpu.roll(load(rho, j + 1), LANES - s, 1))
            y = pltpu.roll(load(rho + 1, 0), left, 1)
            flat[pl.ds(first + full, GROUPS, stride=GROUP_ROWS), :] = jnp.where(lane < left, x, y)
    flat[IN_ROWS : IN_ROWS + HEAD_ROWS, :] = head[...]
    permute_units(table, flat, MID0 * UNITS, 0, staged)
    copies, at = [], 0
    for out in outs:
        copies.append((staged.at[pl.ds(at, out.shape[0])], out))
        at += out.shape[0]
    copy_all(copies, sem)


def pack_in(table, hidden, grad, head, sizes):
    return pl.pallas_call(
        pack_in_kernel,
        out_shape=tuple(shape((n, UNIT, LANES), jnp.float32) for n in sizes),
        in_specs=[SMEM, VMEM, VMEM, VMEM],
        out_specs=(ANY,) * len(sizes),
        scratch_shapes=[
            pltpu.VMEM((D, hidden.shape[0]), jnp.bfloat16),
            pltpu.VMEM((COL_TILES * D, LANES), jnp.float32),
            pltpu.VMEM((MID0 * BROWS, LANES), jnp.float32),
            pltpu.VMEM((sum(sizes), UNIT, LANES), jnp.float32),
            pltpu.SemaphoreType.DMA((len(sizes),)),
        ],
        compiler_params=params(),
        cost_estimate=cost(20),
    )(table, hidden, grad, head)


def pack_out_kernel(
    table, mixed_out, grad, local, keep, send, head, tail, turned, flat, out, sem, *, slots
):
    rows = 256

    def step(i, carry):
        at = pl.multiple_of(i * rows, rows)
        turned[...] = mixed_out[:, pl.ds(at, rows)].T
        product = jnp.dot(turned[...], grad[...], preferred_element_type=jnp.float32)
        for j in range(OUT_TILES):
            flat[pl.ds(at * OUT_TILES + j, rows, stride=OUT_TILES), :] = product[
                :, j * LANES : (j + 1) * LANES
            ]
        return carry

    lax.fori_loop(0, INNER // rows, step, 0)
    head[...] = flat[0:HEAD_ROWS, :]
    tail[...] = flat[OUT_ROWS - TAIL_ROWS : OUT_ROWS, :]
    permute_units(table, flat, N1 * UNITS, HEAD_ROWS, out)

    def add_local(i, carry):
        out[i * slots + slots - 1] = local[...]
        return carry

    lax.fori_loop(0, out.shape[0] // slots, add_local, 0)
    half = keep.shape[0]
    copy_all([(out.at[pl.ds(0, half)], keep), (out.at[pl.ds(half, half)], send)], sem)


def pack_out(table, mixed_out, grad, local, devices, slots):
    return pl.pallas_call(
        partial(pack_out_kernel, slots=slots),
        out_shape=(
            shape((devices * slots // 2, UNIT, LANES), jnp.float32),
            shape((devices * slots // 2, UNIT, LANES), jnp.float32),
            shape((HEAD_ROWS, LANES), jnp.float32),
            shape((TAIL_ROWS, LANES), jnp.float32),
        ),
        in_specs=[SMEM, VMEM, VMEM, VMEM],
        out_specs=(ANY, ANY, VMEM, VMEM),
        scratch_shapes=[
            pltpu.VMEM((256, mixed_out.shape[0]), jnp.bfloat16),
            pltpu.VMEM((OUT_ROWS, LANES), jnp.float32),
            pltpu.VMEM((devices * slots, UNIT, LANES), jnp.float32),
            pltpu.SemaphoreType.DMA((2,)),
        ],
        compiler_params=params(),
    )(table, mixed_out, grad, local)


def adam_kernel(
    table, row_block, row_used, scale, got, late, master, first, second,
    o_first, o_second, o_master, flat, held, limit, used,
):
    capacity = master.shape[0]

    def step(i, carry):
        for u in range(UNITS):
            at = table[i * UNITS + u]
            rows = pl.ds(pl.multiple_of(i * BROWS + u * UNIT, UNIT), UNIT)
            flat[rows, :] = held[at]
        limit[pl.ds(i, 1), :] = jnp.full((1, LANES), END_OUT - row_block[i] * PBLOCK, jnp.int32)
        used[pl.ds(i, 1), :] = jnp.full((1, LANES), row_used[i], jnp.int32)
        return carry

    held[0 : got.shape[0]] = got[...]
    held[got.shape[0] :] = late[...]
    lax.fori_loop(0, capacity, step, 0)
    lane = lax.broadcasted_iota(jnp.int32, (capacity, LANES), 1)
    divisor = scale[0]
    for j in range(BROWS):
        cols = slice(j * LANES, (j + 1) * LANES)
        grad = jnp.where(used[...] > 0, flat[pl.ds(j, capacity, stride=BROWS), :], 0.0) / divisor
        matrix = lane + j * LANES < limit[...]
        weights = master[:, cols]
        new_first = BETA_ONE * first[:, cols] + (1.0 - BETA_ONE) * grad
        new_second = BETA_TWO * second[:, cols] + (1.0 - BETA_TWO) * grad * grad
        normal = (
            new_first
            / (1.0 - BETA_ONE**STEP)
            / (jnp.sqrt(new_second / (1.0 - BETA_TWO**STEP)) + ADAM_EPS)
        )
        rate = jnp.where(matrix, MATRIX_RATE, VECTOR_RATE)
        decay = jnp.where(matrix, WEIGHT_DECAY, 0.0)
        o_first[:, cols] = new_first
        o_second[:, cols] = new_second
        o_master[:, cols] = weights - rate * (normal + decay * weights)


def adam(table, row_block, row_used, divisor, got, late, master, first, second):
    capacity = master.shape[0]
    return pl.pallas_call(
        adam_kernel,
        out_shape=(shape(master.shape, jnp.float32),) * 3,
        in_specs=[SMEM] * 4 + [VMEM] * 5,
        out_specs=(VMEM,) * 3,
        scratch_shapes=[
            pltpu.VMEM((capacity * BROWS, LANES), jnp.float32),
            pltpu.VMEM((got.shape[0] + late.shape[0], UNIT, LANES), jnp.float32),
            pltpu.VMEM((capacity, LANES), jnp.int32),
            pltpu.VMEM((capacity, LANES), jnp.int32),
        ],
        compiler_params=params(),
    )(
        table, row_block, row_used.astype(jnp.int32), divisor.reshape(1), got, late, master, first, second
    )


def doubled(values, step):
    return jnp.concatenate([values, exchange(values, step)], axis=0)


def gather_steps(values, order):
    for step in order[:0:-1]:
        values = doubled(values, step)
    return values, exchange(values, order[0])


def reduce_step(kept, got, step, extra=None):
    half = kept.shape[0] // 2
    given = kept[half:] + got[half:]
    if extra is None:
        return kept[:half] + got[:half], exchange(given, step)
    arrived = exchange(jnp.concatenate([given, extra]), step)
    return kept[:half] + got[:half], arrived[:half], extra + arrived[half:]


CHUNK = 128
PAIRS = HEADS // 2
MIXW = INNER + 2 * NSTATE
DT_AT = INNER + CONVCH
F32 = jnp.float32
BF16 = jnp.bfloat16
NN = (((1,), (0,)), ((), ()))
NT = (((1,), (1,)), ((), ()))


def dot(a, b, dims=NN):
    return lax.dot_general(a, b, dims, preferred_element_type=F32)


def split(v):
    high = v.astype(BF16)
    return high, (v - high.astype(F32)).astype(BF16)


def dot3(a, b, dims=NN):
    ah, al = a
    bh, bl = b
    return dot(ah, bh, dims) + (dot(ah, bl, dims) + dot(al, bh, dims))


def heads_gather():
    return jnp.asarray(np.repeat(np.eye(HEADS, LANES, dtype=np.float32), HEADDIM, axis=0), BF16)


def three_parts(v):
    high = v.astype(BF16).astype(F32)
    rest = v - high
    middle = rest.astype(BF16).astype(F32)
    low = rest - middle
    return (high + pltpu.roll(middle, 32, 1) + pltpu.roll(low, 64, 1)).astype(BF16)


def triangle_sum(tri, v):
    parts = dot(tri, three_parts(v))
    lane = lax.broadcasted_iota(jnp.int32, parts.shape, 1)
    total = parts + pltpu.roll(parts, LANES - 32, 1) + pltpu.roll(parts, LANES - 64, 1)
    return jnp.where(lane < HEADS, total, 0.0)


def chunk_decays(dt, dt_bias, a_log):
    lane = lax.broadcasted_iota(jnp.int32, (CHUNK, LANES), 1)
    row = lax.broadcasted_iota(jnp.int32, (CHUNK, LANES), 0)
    shifted = dt + dt_bias
    delta = jnp.where(
        lane < HEADS, jnp.maximum(shifted, 0.0) + jnp.log1p(jnp.exp(-jnp.abs(shifted))), 0.0
    )
    rate = -jnp.exp(a_log)
    lower = (row >= lane).astype(BF16)
    cum = triangle_sum(lower, delta * rate)
    last = cum[CHUNK - 1 : CHUNK, :]
    return shifted, delta, rate, cum, last


def pair_mask():
    lane = lax.broadcasted_iota(jnp.int32, (CHUNK, LANES), 1)
    low = (lane < HEADDIM).astype(F32)
    return low.astype(BF16), (1.0 - low).astype(BF16)


QUADS = HEADS // 4
QWIDTH = 4 * HEADDIM


def sigmoid(v):
    return 0.5 * jnp.tanh(0.5 * v) + 0.5


def silu(v):
    return v * sigmoid(v)


def side_by_side(v):
    high, low = split(v)
    return jnp.concatenate([high, low], axis=1), high


def dot_parts(a, b):
    ahl, ah = a
    bh, bl = b
    return dot(ahl, jnp.concatenate([bh, bh], axis=0)) + dot(ah, bl)


def dot_turned(a, b):
    ah, al = a
    bh, bl = b
    both = dot(ah, jnp.concatenate([bh, bl], axis=0), NT)
    n = bh.shape[0]
    return both[:, :n] + both[:, n:] + dot(al, bh, NT)


def widen(delta, cum, quad):
    lane = lax.broadcasted_iota(jnp.int32, (CHUNK, LANES), 1)
    over = lambda v, h: jnp.broadcast_to(v[:, h : h + 1], (CHUNK, LANES))
    first = 4 * quad
    columns = [over(cum, first + k) for k in range(4)]
    rates = [over(delta, first + k) for k in range(4)]
    pair = lambda vs: jnp.concatenate(
        [jnp.where(lane < HEADDIM, vs[0], vs[1]), jnp.where(lane < HEADDIM, vs[2], vs[3])], axis=1
    )
    return pair(rates), pair(columns), columns


def pair_rows(parts, j, low, high):
    cols = slice(j * LANES, (j + 1) * LANES)
    return [jnp.concatenate([p[:, cols] * low, p[:, cols] * high], axis=0) for p in parts]


def scan_chunk(mixed, dt, dt_bias, a_log, skip, state, put):
    _, delta, _, cum, last = chunk_decays(dt, dt_bias, a_log)
    lane = lax.broadcasted_iota(jnp.int32, (CHUNK, LANES), 1)
    row = lax.broadcasted_iota(jnp.int32, (CHUNK, LANES), 0)
    bias = jnp.where(row >= lane, 0.0, -1e30)
    cum_t = cum.T
    inputs_b = mixed[:, INNER : INNER + NSTATE]
    readout = mixed[:, INNER + NSTATE :]
    affinity = dot3(split(readout), split(inputs_b), NT)
    readout_parts = side_by_side(readout)
    b_parts = side_by_side(inputs_b.T)
    low, high = pair_mask()
    for quad in range(QUADS):
        cols = slice(quad * QWIDTH, (quad + 1) * QWIDTH)
        wide_delta, wide_cum, columns = widen(delta, cum, quad)
        values = mixed[:, cols]
        scaled = values * wide_delta
        parts = split(scaled)
        outs = []
        for j in range(2):
            right_h, right_l = pair_rows(parts, j, low, high)
            left = []
            for k in range(2):
                h = 4 * quad + 2 * j + k
                within = jnp.exp(columns[2 * j + k] - cum_t[h : h + 1, :] + bias)
                left.append(split(affinity * within))
            left_h = jnp.concatenate([left[0][0], left[1][0]], axis=1)
            left_l = jnp.concatenate([left[0][1], left[1][1]], axis=1)
            both = dot(left_h, jnp.concatenate([right_h, right_l], axis=1))
            outs.append(both[:, :LANES] + both[:, LANES:] + dot(left_l, right_h))
        carried = state[:, cols]
        grown = jnp.exp(wide_cum)
        out = jnp.concatenate(outs, axis=1) + dot_parts(readout_parts, split(carried)) * grown
        tail = jnp.exp(wide_cum[CHUNK - 1 :] - wide_cum)
        state[:, cols] = carried * grown[CHUNK - 1 :] + dot_parts(b_parts, split(scaled * tail))
        put(quad, out + skip[:, cols] * values)


FORWARD_ROWS = 2 * CHUNK


def forward_kernel(
    tokens, w_in, norm_gain, conv_weight, conv_bias, dt_bias, a_log, skip, gain,
    hidden, gate, conv_in, dt, ssm, mixed_out, states, state, before, mixed, shift,
):
    @pl.when(pl.program_id(0) == 0)
    def _():
        state[...] = jnp.zeros_like(state)
        before[...] = jnp.zeros_like(before)

    x = tokens[...].astype(F32)
    inverse = lax.rsqrt(jnp.mean(x * x, axis=1, keepdims=True) + NORM_EPS)
    h = (x * inverse * norm_gain[...]).astype(BF16)
    hidden[...] = h
    dt[...] = dot(h, w_in[:, DT_AT:])
    wide = 2 * LANES
    for tile in range(CONVCH // wide):
        at = tile * wide
        product = dot(h, w_in[:, INNER + at : INNER + at + wide])
        conv_in[:, at : at + wide] = product
        for half in range(2):
            cols = slice(at + half * LANES, at + (half + 1) * LANES)
            rows = product[:, half * LANES : (half + 1) * LANES]
            earlier = before[:, cols]
            terms = moved_down(shift.at[tile * 2 + half], rows, earlier) + [rows]
            before[:, cols] = rows[FORWARD_ROWS - 8 :]
            mixed[:, cols] = silu(conv_sum(terms, conv_weight[:, cols], conv_bias[:, cols]))
    for tile in range(INNER // wide):
        cols = slice(tile * wide, (tile + 1) * wide)
        gate[:, cols] = dot(h, w_in[:, cols])
    for sub in range(FORWARD_ROWS // CHUNK):
        rows = slice(sub * CHUNK, (sub + 1) * CHUNK)
        states[sub] = state[...]
        squares = [jnp.zeros((CHUNK, LANES), F32)]

        def put(quad, out, rows=rows, squares=squares):
            cols = slice(quad * QWIDTH, (quad + 1) * QWIDTH)
            ssm[rows, cols] = out
            gated = out * silu(gate[rows, cols])
            first, second = gated[:, :LANES], gated[:, LANES:]
            squares[0] = squares[0] + first * first + second * second

        scan_chunk(
            mixed[rows, :], dt[rows, :], dt_bias[...], a_log[...], skip, state, put
        )
        rho = lax.rsqrt(jnp.sum(squares[0], axis=1, keepdims=True) * (1.0 / INNER) + NORM_EPS)
        for j in range(PAIRS):
            cols = slice(j * LANES, (j + 1) * LANES)
            gated = ssm[rows, cols] * silu(gate[rows, cols])
            mixed_out[rows, cols] = (gated * rho * gain[:, cols]).astype(BF16)


def forward(tokens, w_in, norm_gain, conv_weight, conv_bias, dt_bias, a_log, skip, gain):
    length = tokens.shape[0]
    by_row = lambda width: pl.BlockSpec((FORWARD_ROWS, width), lambda i: (i, 0))
    whole = lambda v: pl.BlockSpec(v.shape, lambda i: (0,) * v.ndim)
    per_step = FORWARD_ROWS // CHUNK
    return pl.pallas_call(
        forward_kernel,
        grid=(length // FORWARD_ROWS,),
        out_shape=(
            shape((length, D), BF16),
            shape((length, INNER), F32),
            shape((length, MIXW), F32),
            shape((length, LANES), F32),
            shape((length, INNER), F32),
            shape((length, INNER), BF16),
            shape((length // CHUNK, NSTATE, INNER), F32),
        ),
        in_specs=[by_row(D)]
        + [
            whole(v)
            for v in (w_in, norm_gain, conv_weight, conv_bias, dt_bias, a_log, skip, gain)
        ],
        out_specs=(
            by_row(D),
            by_row(INNER),
            by_row(MIXW),
            by_row(LANES),
            by_row(INNER),
            by_row(INNER),
            pl.BlockSpec((per_step, NSTATE, INNER), lambda i: (i, 0, 0)),
        ),
        scratch_shapes=[
            pltpu.VMEM((NSTATE, INNER), F32),
            pltpu.VMEM((8, MIXW), F32),
            pltpu.VMEM((FORWARD_ROWS, MIXW), F32),
            pltpu.VMEM((MIXW // LANES, FORWARD_ROWS + 8, LANES), F32),
        ],
        compiler_params=params(),
        cost_estimate=cost(33),
    )(tokens, w_in, norm_gain, conv_weight, conv_bias, dt_bias, a_log, skip, gain)


def eights(v):
    return jnp.sum(v.reshape(v.shape[0] // 8, 8, v.shape[1]), axis=0)


def backward_kernel(
    conv_in, earlier, dt, ssm, grad, grad_gate, states, conv_weight, conv_bias, dt_bias, a_log, skip,
    gather, grad_low, sums, skip_sums, conv_sums,
    grad_state, to_sum, mixed, slope, grad_mixed, following, shift,
):
    @pl.when(pl.program_id(0) == 0)
    def _():
        grad_state[...] = jnp.zeros_like(grad_state)
        sums[...] = jnp.zeros_like(sums)
        skip_sums[...] = jnp.zeros_like(skip_sums)
        conv_sums[...] = jnp.zeros_like(conv_sums)
        following[...] = jnp.zeros_like(following)

    begins = pl.program_id(0) == pl.num_programs(0) - 1

    for tile in range(MIXW // LANES):
        cols = slice(tile * LANES, (tile + 1) * LANES)
        rows = conv_in[:, cols]
        before = jnp.where(begins, 0.0, earlier[:, cols])
        terms = moved_down(shift.at[tile], rows, before) + [rows]
        value = conv_sum(terms, conv_weight[:, cols], conv_bias[:, cols])
        sig = sigmoid(value)
        mixed[:, cols] = value * sig
        slope[:, cols] = sig * (1.0 + value * (1.0 - sig))

    shifted, delta, rate, cum, last = chunk_decays(dt[...], dt_bias[...], a_log[...])
    lane = lax.broadcasted_iota(jnp.int32, (CHUNK, LANES), 1)
    row = lax.broadcasted_iota(jnp.int32, (CHUNK, LANES), 0)
    bias = jnp.where(lane >= row, 0.0, -1e30)
    heads = lane < HEADS
    cum_t = cum.T
    inputs_b = mixed[:, INNER : INNER + NSTATE]
    readout = mixed[:, INNER + NSTATE :]
    b_parts, c_parts = split(inputs_b), split(readout)
    b_wide = side_by_side(inputs_b)
    c_turned = side_by_side(readout.T)
    affinity = dot3(b_parts, c_parts, NT)
    low, high = pair_mask()
    grad_affinity = jnp.zeros((CHUNK, CHUNK), F32)
    grad_b = jnp.zeros((CHUNK, NSTATE), F32)
    grad_c = jnp.zeros((CHUNK, NSTATE), F32)
    last_row = lax.broadcasted_iota(jnp.int32, (CHUNK, QWIDTH), 0) == CHUNK - 1
    for quad in range(QUADS):
        cols = slice(quad * QWIDTH, (quad + 1) * QWIDTH)
        wide_delta, wide_cum, columns = widen(delta, cum, quad)
        grown = jnp.exp(wide_cum)
        tail = jnp.exp(wide_cum[CHUNK - 1 :] - wide_cum)
        end = grown[CHUNK - 1 :]
        values = mixed[:, cols]
        pulled = grad[:, cols]
        scaled = values * wide_delta
        x_parts, p_parts = split(scaled), split(pulled)
        outs = []
        for j in range(2):
            half = slice(j * LANES, (j + 1) * LANES)
            xh, xl = x_parts[0][:, half], x_parts[1][:, half]
            right_h, right_l = pair_rows(p_parts, j, low, high)
            pull = dot(
                jnp.concatenate([xh, xl], axis=1),
                jnp.concatenate([right_h, right_h], axis=1),
                NT,
            ) + dot(xh, right_l, NT)
            kernels = []
            for k in range(2):
                h = 4 * quad + 2 * j + k
                within = jnp.exp(cum_t[h : h + 1, :] - columns[2 * j + k] + bias)
                kernels.append(split(affinity * within))
                grad_affinity = grad_affinity + within * pull[:, k * CHUNK : (k + 1) * CHUNK]
            kernel_h = jnp.concatenate([kernels[0][0], kernels[1][0]], axis=1)
            kernel_l = jnp.concatenate([kernels[0][1], kernels[1][1]], axis=1)
            both = dot(kernel_h, jnp.concatenate([right_h, right_l], axis=1))
            outs.append(both[:, :LANES] + both[:, LANES:] + dot(kernel_l, right_h))
        late = grad_state[:, cols]
        late_parts = split(late)
        early = states[0, :, cols]
        from_state = dot_parts(b_wide, late_parts) * tail
        grad_scaled = jnp.concatenate(outs, axis=1) + from_state
        pulled_cum = split(pulled * grown)
        grad_c = grad_c + dot_turned(pulled_cum, split(early))
        grad_b = grad_b + dot_turned(split(scaled * tail), late_parts)
        grad_state[:, cols] = late * end + dot_parts(c_turned, pulled_cum)
        grad_mixed[:, cols] = grad_scaled * wide_delta + skip[:, cols] * pulled
        skip_sums[:, cols] += jnp.sum(pulled * values, axis=0, keepdims=True)
        to_sum[:CHUNK, cols] = grad_scaled * values
        inner = pulled * (ssm[:, cols] - skip[:, cols] * values) - scaled * grad_scaled
        extra = jnp.sum(scaled * from_state, axis=0, keepdims=True) + end * jnp.sum(
            late * early, axis=0, keepdims=True
        )
        to_sum[CHUNK:, cols] = inner + jnp.where(last_row, extra, 0.0)
    ga_parts = split(grad_affinity)
    grad_mixed[:, INNER : INNER + NSTATE] = grad_b + dot3(ga_parts, c_parts)
    grad_mixed[:, INNER + NSTATE :] = grad_c + dot3(split(grad_affinity.T), b_parts)


    def by_head(v):
        high, low = split(v)
        return dot(high, gather[...]) + dot(low, gather[...])

    direct, grad_cum = by_head(to_sum[:CHUNK, :]), by_head(to_sum[CHUNK:, :])
    upper = (lane >= row).astype(BF16)
    after = triangle_sum(upper, grad_cum)
    grad_delta = direct + rate * after
    grad_raw = jnp.where(heads, grad_delta * sigmoid(shifted), 0.0)
    grad_low[:, DT_AT:] = grad_raw.astype(BF16)
    sums[0:1, :] += jnp.sum(grad_raw, axis=0, keepdims=True)
    sums[1:2, :] += rate * jnp.sum(delta * after, axis=0, keepdims=True)
    grad_low[:, :INNER] = grad_gate[...]
    for tile in range(MIXW // LANES):
        cols = slice(tile * LANES, (tile + 1) * LANES)
        w = conv_weight[:, cols]
        g = grad_mixed[:, cols] * slope[:, cols]
        rows = conv_in[:, cols]
        later = following[:, cols]
        total = jnp.zeros((CHUNK, LANES), F32)
        arriving = moved_up(shift.at[tile], g, later) + [g]
        for k in range(KCONV):
            conv_sums[8 * k : 8 * k + 8, cols] += eights(rows * arriving[k])
            total = total + arriving[k] * w[k : k + 1]
        conv_sums[8 * KCONV :, cols] += eights(g)
        following[:, cols] = g[:8]
        grad_low[:, INNER + tile * LANES : INNER + (tile + 1) * LANES] = total.astype(BF16)


def backward(
    conv_in, dt, ssm, grad, grad_gate, states, conv_weight, conv_bias, dt_bias, a_log, skip, gather
):
    length = conv_in.shape[0]
    chunks = length // CHUNK
    whole = lambda v: pl.BlockSpec(v.shape, lambda i: (0,) * v.ndim)
    by_row = lambda width: pl.BlockSpec((CHUNK, width), lambda i: (chunks - 1 - i, 0))
    return pl.pallas_call(
        backward_kernel,
        grid=(chunks,),
        out_shape=(
            shape((length, WIDE), BF16),
            shape((8, LANES), F32),
            shape((1, INNER), F32),
            shape((8 * (KCONV + 1), MIXW), F32),
        ),
        in_specs=[
            by_row(MIXW),
            pl.BlockSpec((8, MIXW), lambda i: (jnp.maximum((chunks - 1 - i) * (CHUNK // 8) - 1, 0), 0)),
            by_row(LANES),
            by_row(INNER),
            by_row(INNER),
            by_row(INNER),
            pl.BlockSpec((1, NSTATE, INNER), lambda i: (chunks - 1 - i, 0, 0)),
        ]
        + [whole(v) for v in (conv_weight, conv_bias, dt_bias, a_log, skip, gather)],
        out_specs=(
            by_row(WIDE),
            pl.BlockSpec((8, LANES), lambda i: (0, 0)),
            pl.BlockSpec((1, INNER), lambda i: (0, 0)),
            pl.BlockSpec((8 * (KCONV + 1), MIXW), lambda i: (0, 0)),
        ),
        scratch_shapes=[pltpu.VMEM((NSTATE, INNER), F32)]
        + [pltpu.VMEM((2 * CHUNK, INNER), F32)]
        + [pltpu.VMEM((CHUNK, MIXW), F32)] * 3
        + [pltpu.VMEM((8, MIXW), F32), pltpu.VMEM((MIXW // LANES, CHUNK + 8, LANES), F32)],
        compiler_params=params(),
        cost_estimate=cost(43),
    )(
        conv_in, conv_in, dt, ssm, grad, grad_gate, states,
        conv_weight, conv_bias, dt_bias, a_log, skip, gather,
    )


def moved_down(scratch, v, before):
    rows = v.shape[0]
    scratch[0:8, :] = before
    scratch[8 : 8 + rows, :] = v
    return [scratch[8 - by : 8 - by + rows, :] for by in range(KCONV - 1, 0, -1)]


def moved_up(scratch, v, behind):
    rows = v.shape[0]
    scratch[0:rows, :] = v
    scratch[rows : rows + 8, :] = behind
    return [scratch[by : by + rows, :] for by in range(KCONV - 1, 0, -1)]


def conv_sum(terms, weight, bias):
    total = bias + terms[KCONV - 1] * weight[KCONV - 1 : KCONV]
    for k in range(KCONV - 1):
        total = total + terms[k] * weight[k : k + 1]
    return total


def loss_kernel(
    limit, mixed_out, w_out, tokens, teacher, mask, block_out, grad_result, grad_branch, error
):
    step = pl.program_id(0)

    @pl.when(step == 0)
    def _():
        error[...] = jnp.zeros_like(error)

    rows = tokens.shape[0]
    result = tokens[...].astype(F32) + dot(mixed_out[...], w_out[...])
    position = step * rows + lax.broadcasted_iota(jnp.int32, (rows, 1), 0)
    valid = (position < limit[0]).astype(F32)
    turned = jnp.broadcast_to(mask[...].astype(F32), (LANES, rows)).T
    weight = valid * turned[:, 0:1]
    block_out[...] = (result * valid).astype(BF16)
    misfit = result - teacher[...].astype(F32)
    pulled = 2.0 * weight * misfit
    grad_result[...] = pulled
    errors = jnp.sum(0.5 * pulled * misfit, axis=0, keepdims=True)
    for j in range(D // LANES):
        error[j : j + 1, :] += errors[:, j * LANES : (j + 1) * LANES]
    error[D // LANES : D // LANES + 1, :] += jnp.sum(valid * turned, axis=0, keepdims=True)
    grad_branch[...] = pulled.astype(BF16)


def loss_part(limit, mixed_out, w_out, tokens, teacher, mask):
    length = tokens.shape[0]
    rows = 256
    by_row = lambda width: pl.BlockSpec((rows, width), lambda i: (i, 0))
    return pl.pallas_call(
        loss_kernel,
        grid=(length // rows,),
        out_shape=(
            shape((length, D), BF16),
            shape((length, D), F32),
            shape((length, D), BF16),
            shape((8, LANES), F32),
        ),
        in_specs=[
            SMEM,
            by_row(INNER),
            pl.BlockSpec(w_out.shape, lambda i: (0, 0)),
            by_row(D),
            by_row(D),
            pl.BlockSpec((1, rows), lambda i: (0, i)),
        ],
        out_specs=(by_row(D), by_row(D), by_row(D), pl.BlockSpec((8, LANES), lambda i: (0, 0))),
        compiler_params=params(),
        cost_estimate=cost(8),
    )(limit, mixed_out, w_out, tokens, teacher, mask)


def gate_kernel(grad_branch, w_out, ssm, gate, gain, grad_ssm, grad_gate, gain_sums):
    @pl.when(pl.program_id(0) == 0)
    def _():
        gain_sums[...] = jnp.zeros_like(gain_sums)

    grad_mixed = dot(grad_branch[...], w_out[...], NT)
    g = gate[...]
    sig = sigmoid(g)
    act = g * sig
    inner = ssm[...]
    gated = inner * act
    rho = lax.rsqrt(jnp.mean(gated * gated, axis=1, keepdims=True) + NORM_EPS)
    unit = gated * rho
    gain_sums[...] += jnp.sum(unit * grad_mixed, axis=0, keepdims=True)
    grad_unit = grad_mixed * gain[...]
    share = jnp.mean(grad_unit * unit, axis=1, keepdims=True)
    grad_gated = rho * (grad_unit - unit * share)
    grad_ssm[...] = grad_gated * act
    grad_gate[...] = (grad_gated * inner * (sig * (1.0 + g * (1.0 - sig)))).astype(BF16)


def gate_part(grad_branch, w_out, ssm, gate, gain):
    length = ssm.shape[0]
    rows = 256
    by_row = lambda width: pl.BlockSpec((rows, width), lambda i: (i, 0))
    whole = lambda v: pl.BlockSpec(v.shape, lambda i: (0,) * v.ndim)
    return pl.pallas_call(
        gate_kernel,
        grid=(length // rows,),
        out_shape=(shape((length, INNER), F32), shape((length, INNER), BF16), shape((1, INNER), F32)),
        in_specs=[by_row(D), whole(w_out), by_row(INNER), by_row(INNER), whole(gain)],
        out_specs=(by_row(INNER), by_row(INNER), pl.BlockSpec((1, INNER), lambda i: (0, 0))),
        compiler_params=params(),
        cost_estimate=cost(12),
    )(grad_branch, w_out, ssm, gate, gain)


def input_kernel(grad_low, w_in, tokens, norm_gain, grad_result, out, sums):
    @pl.when(pl.program_id(0) == 0)
    def _():
        sums[...] = jnp.zeros_like(sums)

    x = tokens[...].astype(F32)
    inverse = lax.rsqrt(jnp.mean(x * x, axis=1, keepdims=True) + NORM_EPS)
    unit = x * inverse
    grad_hidden = dot(grad_low[...], w_in[...], NT)
    sums[...] += jnp.sum(grad_hidden * unit, axis=0, keepdims=True)
    pulled = grad_hidden * norm_gain[...]
    share = jnp.mean(pulled * unit, axis=1, keepdims=True)
    out[...] = grad_result[...] + inverse * (pulled - unit * share)


def input_backward(grad_low, w_in, tokens, norm_gain, grad_result):
    length = tokens.shape[0]
    rows = 256
    by_row = lambda width: pl.BlockSpec((rows, width), lambda i: (i, 0))
    whole = lambda v: pl.BlockSpec(v.shape, lambda i: (0,) * v.ndim)
    return pl.pallas_call(
        input_kernel,
        grid=(length // rows,),
        out_shape=(shape((length, D), F32), shape((1, D), F32)),
        in_specs=[by_row(WIDE), whole(w_in), by_row(D), whole(norm_gain), by_row(D)],
        out_specs=(by_row(D), pl.BlockSpec((1, D), lambda i: (0, 0))),
        compiler_params=params(),
        cost_estimate=cost(15),
    )(grad_low, w_in, tokens, norm_gain, grad_result)


def vector_kernel(tail, conv_sums, sums, skip_sums, norm_sums, gate_sums, gather, out, taps):
    tiles = CONVCH // LANES
    out[...] = jnp.zeros_like(out)
    out[0:TAIL_ROWS, :] = tail[...]
    for k in range(KCONV):
        for i in range(tiles):
            partial_sums = conv_sums[8 * k : 8 * k + 8, i * LANES : (i + 1) * LANES]
            taps[k * 16 + i : k * 16 + i + 1, :] = jnp.sum(partial_sums, axis=0, keepdims=True)
    row = lax.broadcasted_iota(jnp.int32, (LANES, LANES), 0)
    col = lax.broadcasted_iota(jnp.int32, (LANES, LANES), 1)
    per_tile = LANES // KCONV

    def exact(v, chosen):
        high = v.astype(BF16)
        rest = v - high.astype(F32)
        middle = rest.astype(BF16)
        low = (rest - middle.astype(F32)).astype(BF16)
        return dot(high, chosen) + (dot(middle, chosen) + dot(low, chosen))

    for q in range(KCONV):
        total = jnp.zeros((tiles, LANES), F32)
        for k in range(KCONV):
            chosen = (col == KCONV * (row % per_tile) + k) & (row // per_tile == q)
            total = total + exact(taps[k * 16 : k * 16 + tiles, :], chosen.astype(BF16))
        out[pl.ds(TAIL_ROWS + q, tiles, stride=KCONV), :] = total
    bias_at = TAIL_ROWS + tiles * KCONV
    for i in range(tiles):
        partial_sums = conv_sums[8 * KCONV :, i * LANES : (i + 1) * LANES]
        out[bias_at + i : bias_at + i + 1, :] = jnp.sum(partial_sums, axis=0, keepdims=True)
    lane = lax.broadcasted_iota(jnp.int32, (1, LANES), 1)
    skip = exact(jnp.broadcast_to(skip_sums[...], (8, INNER)), gather[...])[0:1, :]
    parts = [sums[0:1, :], sums[1:2, :], skip]
    parts = [jnp.where(lane < HEADS, v, 0.0) for v in parts]
    before = parts[0] + pltpu.roll(parts[1], HEADS, 1) + pltpu.roll(parts[2], 2 * HEADS, 1)
    at, shift = bias_at + tiles, 3 * HEADS
    for source in (norm_sums, gate_sums):
        for j in range(source.shape[1] // LANES):
            here = pltpu.roll(source[:, j * LANES : (j + 1) * LANES], shift, 1)
            out[at : at + 1, :] = jnp.where(lane < shift, before, here)
            before = here
            at += 1
    out[at : at + 1, :] = jnp.where(lane < shift, before, 0.0)


def pack_vectors(tail, conv_sums, sums, skip_sums, norm_sums, gate_sums, gather):
    return pl.pallas_call(
        vector_kernel,
        out_shape=shape(((NBLK - MID1) * BROWS, LANES), F32),
        in_specs=[VMEM] * 7,
        out_specs=VMEM,
        scratch_shapes=[pltpu.VMEM((KCONV * 16, LANES), F32)],
        compiler_params=params(),
    )(tail, conv_sums, sums, skip_sums, norm_sums, gate_sums, gather)


def body(tokens, teacher, lengths, loss_mask, owners, master, first_moment, second_moment):
    capacity = master.shape[0]
    dp, fsdp = lax.axis_size("dp"), lax.axis_size("fsdp")
    devices = dp * fsdp
    me = lax.axis_index(AXES).astype(jnp.int32)
    x_first, y_first, z_first = step_orders(dp, fsdp)
    tie = lambda *values: lax.optimization_barrier(values)

    sent = send_blocks(owners, master, devices, me)
    at_home = lax.all_to_all(sent, AXES, 0, 0, tiled=True)
    owners, tokens, loss_mask, _ = tie(owners, tokens, loss_mask, sent)
    plan = make_plan(owners, capacity, devices, me)
    streams = cut(even(plan["slots"], 3), (x_first, y_first, z_first))
    table = stream_places(plan["home"], plan["slot"], me, streams, devices)
    u0, u1 = plan["unit_slots"]
    sizes = [-(-u0 // 5)] * 4
    unit_streams = cut(sizes + [u0 - sum(sizes)], (x_first, y_first, x_first, y_first, z_first))
    unit_table = stream_places(plan["unit_home"], plan["unit_slot"], me, unit_streams, devices)
    unit_table = unit_table[:MID0].reshape(-1)
    order1 = x_first[:2] + x_first[2 + bits_of(fsdp) :] + x_first[2 : 2 + bits_of(fsdp)]
    unit_table1 = place_of(plan["unit_home"] ^ me, order1) * (u1 + 1) + plan["unit_slot"]
    unit_table1 = unit_table1[MID0:MID1].reshape(-1)
    inputs, target = tokens[0], teacher[0]
    (at_home, table, unit_table, unit_table1, received, back_table, row_from, row_block,
     row_used) = tie(
        at_home, table, unit_table, unit_table1, plan["received"], plan["back"],
        plan["row_from"], plan["row_block"], plan["row_used"],
    )
    mine = pick_blocks(received, at_home, [size for _, size, _ in streams])
    parts = []
    for values, (_, _, order) in zip(mine, streams):
        parts += gather_steps(values, order)
    (input_weight, output_weight, conv_weight, conv_bias, dt_bias, a_log, skip, norm_gain,
     gate_gain) = unpack(table, parts)
    gather = heads_gather()
    hidden, gate, conv_in, dt, ssm, mixed_out, states = forward(
        inputs, input_weight, norm_gain, conv_weight, conv_bias, dt_bias, a_log, skip, gate_gain
    )
    block_out, grad_result, grad_branch, local = loss_part(
        lengths, mixed_out, output_weight, inputs, target, loss_mask
    )
    keep1, send1, head, tail = pack_out(
        unit_table1, mixed_out, grad_branch, local, devices, u1 + 1
    )
    grad_branch, send1 = tie(grad_branch, send1)
    got1 = exchange(send1, order1[0])
    grad_ssm, grad_gate, gain_sums = gate_part(grad_branch, output_weight, ssm, gate, gate_gain)
    grad_ssm, keep1, got1 = tie(grad_ssm, keep1, got1)
    keep1, got1 = reduce_step(keep1, got1, order1[1])
    grad_low, sums, skip_sums, conv_sums = backward(
        conv_in, dt, ssm, grad_ssm, grad_gate, states,
        conv_weight, conv_bias, dt_bias, a_log, skip, gather,
    )
    grad_low, keep1, got1 = tie(grad_low, keep1, got1)
    steps1 = order1[2:]
    for step in steps1[:1]:
        keep1, got1 = reduce_step(keep1, got1, step)
    halves = []
    for _, size, _ in unit_streams:
        halves += [devices * size // 2] * 2
    packed = list(pack_in(unit_table, hidden, grad_low, head, halves))
    packed[0], keep1, got1 = tie(packed[0], keep1, got1)
    kept = packed[::2]
    got = [exchange(v, order[0]) for v, (_, _, order) in zip(packed[1::2], unit_streams)]
    *got, grad_low, conv_sums, tail = tie(*got, grad_low, conv_sums, tail)
    for i, (_, _, order) in enumerate(unit_streams):
        kept[i], got[i] = reduce_step(kept[i], got[i], order[1])
    for step in steps1[1:2]:
        keep1, got1 = reduce_step(keep1, got1, step)
    input_grad, norm_sums = input_backward(grad_low, input_weight, inputs, norm_gain, grad_result)
    grad_vec = pack_vectors(tail, conv_sums, sums, skip_sums, norm_sums, gain_sums, gather)
    grad_vec = grad_vec.reshape((NBLK - MID1) * UNITS, UNIT, LANES)
    *got, got1, grad_vec, input_grad = tie(*got, got1, grad_vec, input_grad)
    for step in steps1[2:]:
        keep1, got1 = reduce_step(keep1, got1, step)
    for k in range(2, len(x_first)):
        for i, (_, _, order) in enumerate(unit_streams):
            if i == 0:
                kept[i], got[i], grad_vec = reduce_step(kept[i], got[i], order[k], grad_vec)
            else:
                kept[i], got[i] = reduce_step(kept[i], got[i], order[k])
    back = units_to_owners(back_table, list(zip(kept + [keep1], got + [got1])))
    back, grad_vec = tie(back, grad_vec)
    returned = lax.all_to_all(back, AXES, 0, 0, tiled=True)
    for step in x_first[:2]:
        grad_vec = grad_vec + exchange(grad_vec, step)
    local_sums = keep1[u1] + got1[u1]
    error_sum = jnp.sum(local_sums[: D // LANES])
    divisor = local_sums[D // LANES, 0] * D
    new_first, new_second, new_master = adam(
        row_from,
        row_block,
        row_used,
        divisor,
        returned,
        grad_vec,
        master,
        first_moment,
        second_moment,
    )
    mean_loss = error_sum / divisor
    return (block_out[None], input_grad[None], mean_loss, new_first, new_second, new_master)


def solution(mesh):
    return jax.shard_map(
        body,
        mesh=mesh,
        in_specs=(
            P(AXES, None, None),
            P(AXES, None, None),
            P(AXES),
            P(AXES, None),
            P(),
            P(AXES, None),
            P(AXES, None),
            P(AXES, None),
        ),
        out_specs=(
            P(AXES, None, None),
            P(AXES, None, None),
            P(),
            P(AXES, None),
            P(AXES, None),
            P(AXES, None),
        ),
        check_vma=False,
    )
```

```python
from functools import partial

import jax
import jax.numpy as jnp
import numpy as np
from jax import lax
from jax.experimental import pallas as pl
from jax.experimental.pallas import tpu as pltpu
from jax.sharding import PartitionSpec as P

D = 768
INNER = 1536
NSTATE = 128
HEADDIM = 64
KCONV = 4
SCAN_LEN = 256
PBLOCK = 4096
STEP = 10
HEADS = 24
CONVCH = 1792
PROJ = 3352
PTOT = 3765320
NBLK = 920

LANES = 128
BROWS = PBLOCK // LANES
UNIT = 8
UNITS = BROWS // UNIT
END_IN = D * PROJ
END_OUT = END_IN + INNER * D
MID0 = -(-END_IN // PBLOCK)
MID1 = END_OUT // PBLOCK
N0 = MID0 + NBLK - MID1
N1 = MID1 - MID0
F0_ROWS = N0 * BROWS
IN_ROWS = END_IN // LANES
HEAD_ROWS = MID0 * BROWS - IN_ROWS
TAIL_ROWS = (END_OUT - MID1 * PBLOCK) // LANES
OUT_ROWS = INNER * D // LANES
VEC_ROWS = (NBLK - MID1) * BROWS - TAIL_ROWS
VEC_AT = MID0 * BROWS + TAIL_ROWS
GROUP = 16
GROUPS = D // GROUP
GROUP_ROWS = GROUP * PROJ // LANES
COL_TILES = -(-PROJ // LANES)
WIDE = COL_TILES * LANES
OUT_TILES = D // LANES

NORM_EPS = 1e-05
ADAM_EPS = 1e-08
BETA_ONE = 0.9
BETA_TWO = 0.999
MATRIX_RATE = 0.03
VECTOR_RATE = 0.2
WEIGHT_DECAY = 0.1
PRECISE = lax.Precision.HIGHEST
AXES = ("dp", "fsdp")
VMEM_LIMIT = 60 * 1024 * 1024


def bits_of(count):
    return count.bit_length() - 1


def step_orders(dp, fsdp):
    wide = [("dp", i) for i in range(bits_of(dp))]
    narrow = [("fsdp", i) for i in range(bits_of(fsdp))]
    first = wide[:2] + narrow + wide[2:]
    second = wide[:1] + narrow + wide[1:]
    third = wide[:1] + wide[2:] + wide[1:2] + narrow
    return first, second, third


def cut(sizes, orders):
    streams, at = [], 0
    for size, order in zip(sizes, orders):
        if size:
            streams.append((at, size, order))
        at += size
    return streams


def even(total, parts):
    return [total // parts + (i < total % parts) for i in range(parts)]


def exchange(values, *steps):
    axes = {axis for axis, _ in steps}
    if len(axes) == 1:
        (axis,) = axes
        mask = sum(1 << bit for _, bit in steps)
        pairs = [(i, i ^ mask) for i in range(lax.axis_size(axis))]
        return lax.ppermute(values, axis, pairs)
    low = bits_of(lax.axis_size("fsdp"))
    mask = sum(1 << (bit + (low if axis == "dp" else 0)) for axis, bit in steps)
    count = lax.axis_size("dp") * lax.axis_size("fsdp")
    return lax.ppermute(values, AXES, [(i, i ^ mask) for i in range(count)])


def place_of(relative, order):
    shift_of = {"dp": bits_of(lax.axis_size("fsdp")), "fsdp": 0}
    place = jnp.zeros_like(relative)
    for axis, bit in order:
        place = place * 2 + ((relative >> (shift_of[axis] + bit)) & 1)
    return place


def class_counts(owners, devices):
    block = jnp.arange(NBLK, dtype=jnp.int32)
    mid = ((block >= MID0) & (block < MID1))[None, :]
    device = jnp.arange(devices, dtype=jnp.int32)
    below = owners[None, :] < device[:, None]
    owned = owners[None, :] == device[:, None]

    def total(mask):
        return jnp.sum(mask.astype(jnp.int32), axis=1)

    start = (total(below & ~mid), total(below & mid))
    count = (total(owned & ~mid), total(owned & mid))
    return start, count, total(owned & (block < MID0)[None, :])


def my_counts(owners, me):
    block = jnp.arange(NBLK, dtype=jnp.int32)
    mid = (block >= MID0) & (block < MID1)
    below, owned = owners < me, owners == me
    total = lambda mask: jnp.sum(mask.astype(jnp.int32))
    start = (total(below & ~mid), total(below & mid))
    count = (total(owned & ~mid), total(owned & mid))
    return start, count, total(owned & (block < MID0))


def pair_lanes(capacity, devices):
    return -(-capacity // devices)


def make_plan(owners, capacity, devices, me):
    block = jnp.arange(NBLK, dtype=jnp.int32)
    mid = (block >= MID0) & (block < MID1)
    same = mid[:, None] == mid[None, :]
    before = (owners[None, :] < owners[:, None]) | (
        (owners[None, :] == owners[:, None]) & (block[None, :] < block[:, None])
    )
    order = jnp.sum(before.astype(jnp.int32), axis=1)
    order_in_class = jnp.sum((same & before).astype(jnp.int32), axis=1)
    home, slot = order % devices, order // devices
    device = jnp.arange(devices, dtype=jnp.int32)
    start, count, _ = class_counts(owners, devices)
    my_start, my_count, my_early = my_counts(owners, me)
    pair = pair_lanes(capacity, devices)

    slots = -(-NBLK // devices)
    wanted = me + devices * jnp.arange(slots, dtype=jnp.int32)
    first = start[0] + start[1]
    ends = first + count[0] + count[1]
    owner = jnp.sum((ends[None, :] <= wanted[:, None]).astype(jnp.int32), axis=1)
    owner = jnp.minimum(owner, devices - 1)
    base = jnp.sum(jnp.where(device[None, :] == owner[:, None], first[None, :], 0), axis=1)
    received = owner * pair + jnp.clip((wanted - base) // devices, 0, pair - 1)

    back_pair = (UNITS * capacity + 2 * (devices - 1)) // devices
    unit = UNITS * order_in_class[:, None] + jnp.arange(UNITS, dtype=jnp.int32)[None, :]
    unit_home, unit_slot = unit % devices, unit // devices
    unit_slots = (-(-UNITS * N0 // devices), -(-UNITS * N1 // devices))
    lane = jnp.arange(back_pair, dtype=jnp.int32)

    def units_back(kind):
        turn = lane if kind == 0 else back_pair - 1 - lane
        first = UNITS * start[kind][:, None]
        k = (me - first) % devices + turn[None, :] * devices
        return k < UNITS * count[kind][:, None], (first + k) // devices

    valid0, slot0 = units_back(0)
    valid1, slot1 = units_back(1)
    back = jnp.where(valid0, slot0, jnp.where(valid1, unit_slots[0] + slot1, 0)).reshape(-1)

    row = jnp.arange(capacity, dtype=jnp.int32)
    is_mid = (row >= my_early) & (row < my_early + my_count[1])
    k = jnp.where(is_mid, row - my_early, jnp.where(row < my_early, row, row - my_count[1]))
    first = UNITS * jnp.where(is_mid, my_start[1], my_start[0])
    k = UNITS * k[:, None] + jnp.arange(UNITS, dtype=jnp.int32)[None, :]
    turn = k // devices
    row_from = ((first[:, None] + k) % devices) * back_pair + jnp.where(
        is_mid[:, None], back_pair - 1 - turn, turn
    )
    row_used = row < my_count[0] + my_count[1]
    mine = (owners == me)[None, :]
    rank = jnp.sum((mine & (block[None, :] < block[:, None])).astype(jnp.int32), axis=1)
    row_block = jnp.sum(
        jnp.where(mine & (rank[None, :] == row[:, None]), block[None, :], 0), axis=1
    )
    late = devices * back_pair + UNITS * (row_block - MID1)
    late = late[:, None] + jnp.arange(UNITS, dtype=jnp.int32)[None, :]
    row_from = jnp.where((row_block >= MID1)[:, None], late, row_from)
    row_from = jnp.where(row_used[:, None], row_from, 0).reshape(-1)
    return dict(
        home=home, slot=slot, slots=slots,
        received=received, unit_home=unit_home, unit_slot=unit_slot,
        unit_slots=unit_slots, back=back, row_from=row_from,
        row_used=row_used, row_block=row_block,
    )


def stream_places(home, slot, me, streams, devices):
    relative = home ^ me
    place = jnp.zeros_like(slot)
    for begin, size, order in streams:
        inside = (slot >= begin) & (slot < begin + size)
        at = devices * begin + place_of(relative, order) * size + slot - begin
        place = jnp.where(inside, at, place)
    return place


def cost(microseconds):
    return pl.CostEstimate(
        flops=int(microseconds * 1e9), bytes_accessed=int(microseconds * 3e6), transcendentals=0
    )


ANY = pl.BlockSpec(memory_space=pl.ANY)
VMEM = pl.BlockSpec(memory_space=pltpu.VMEM)
SMEM = pl.BlockSpec(memory_space=pltpu.SMEM)


def params(**extra):
    return pltpu.CompilerParams(vmem_limit_bytes=VMEM_LIMIT, **extra)


def shape(dims, dtype):
    return jax.ShapeDtypeStruct(dims, dtype)


def send_kernel(my_index, owners, master, out, flat, *, devices):
    capacity = master.shape[0]
    me = my_index[0]
    for j in range(BROWS):
        flat[pl.ds(j, capacity, stride=BROWS), :] = master[:, j * LANES : (j + 1) * LANES]
    held = owners[...]
    below, owned = held < me, held == me

    def total(mask):
        return jnp.sum(jnp.where(mask, 1.0, 0.0)).astype(jnp.int32)

    start, count = total(below), total(owned)
    pair = out.shape[0] // devices

    def step(home, carry):
        for s in range(pair):
            k = lax.rem(home - start + devices * NBLK, devices) + s * devices
            row = jnp.where(k < count, k, 0)
            rows = pl.ds(pl.multiple_of(row * BROWS, BROWS), BROWS)
            out[home * pair + s] = flat[rows, :].astype(out.dtype)
        return carry

    lax.fori_loop(0, devices, step, 0)


def send_blocks(owners, master, devices, me):
    rows = -(-NBLK // (8 * LANES)) * 8
    held = jnp.pad(owners, (0, rows * LANES - NBLK), constant_values=1 << 20).reshape(rows, LANES)
    count = devices * pair_lanes(master.shape[0], devices)
    return pl.pallas_call(
        partial(send_kernel, devices=devices),
        out_shape=shape((count, BROWS, LANES), jnp.bfloat16),
        in_specs=[SMEM, VMEM, VMEM],
        out_specs=VMEM,
        scratch_shapes=[pltpu.VMEM((master.shape[0] * BROWS, LANES), jnp.float32)],
        compiler_params=params(),
    )(me.reshape(1), held, master)


def pick_kernel(table, source, *outs):
    at = 0
    for out in outs:

        def step(i, carry, out=out, at=at):
            out[i] = source[table[at + i]]
            return carry

        lax.fori_loop(0, out.shape[0], step, 0)
        at += out.shape[0]


def pick_blocks(table, source, sizes):
    return pl.pallas_call(
        pick_kernel,
        out_shape=tuple(shape((n,) + source.shape[1:], source.dtype) for n in sizes),
        in_specs=[SMEM, VMEM],
        out_specs=(VMEM,) * len(sizes),
        compiler_params=params(),
    )(table, source)


def back_kernel(table, *refs, sizes):
    sources, (out, held) = refs[:-2], refs[-2:]
    at = i = 0
    for size in sizes:
        n = sources[i].shape[0]
        total = sources[i][...]
        for k in range(1, size):
            total = total + sources[i + k][0:n]
        held[at : at + n] = total
        at += n
        i += size

    def step(i, carry):
        for u in range(8):
            out[i * 8 + u] = held[table[i * 8 + u]]
        return carry

    total = out.shape[0]
    lax.fori_loop(0, total // 8, step, 0)


def units_to_owners(table, groups):
    return pl.pallas_call(
        partial(back_kernel, sizes=[len(g) for g in groups]),
        out_shape=shape((table.shape[0], UNIT, LANES), jnp.float32),
        in_specs=[SMEM] + [VMEM] * sum(len(g) for g in groups),
        out_specs=VMEM,
        scratch_shapes=[pltpu.VMEM((sum(g[0].shape[0] for g in groups), UNIT, LANES), jnp.float32)],
        compiler_params=params(),
    )(table, *[v for g in groups for v in g])


def fold_kernel(*refs, sizes, extra):
    sources, outs = refs[: sum(sizes) + extra], refs[sum(sizes) + extra :]
    at = i = 0
    for size in sizes:
        n = sources[i].shape[0] // 4
        for p in range(4):
            rows = slice(p * n, (p + 1) * n)
            total = sources[i][rows]
            for k in range(1, size):
                total = total + sources[i + k][rows]
            outs[p][at : at + n] = total
        at += n
        i += size
    if extra:
        for p in range(1, 4):
            outs[p][at:] = sources[-1][...]


def fold(groups, extra=None):
    n = sum(g[0].shape[0] // 4 for g in groups)
    more = 0 if extra is None else extra.shape[0]
    values = [v for g in groups for v in g] + ([] if extra is None else [extra])
    return pl.pallas_call(
        partial(fold_kernel, sizes=[len(g) for g in groups], extra=int(extra is not None)),
        out_shape=[shape((n + (more if p else 0), UNIT, LANES), jnp.float32) for p in range(4)],
        in_specs=[VMEM] * len(values),
        out_specs=[VMEM] * 4,
        compiler_params=params(),
    )(*values)


def exchange_quarters(given, steps):
    return [exchange(given[1], steps[1]), exchange(given[2], steps[0]), exchange(given[3], *steps)]


def row_start(rho):
    return (PROJ * rho) // LANES, (PROJ * rho) % LANES


def copy_all(pairs, sem):
    copies = [pltpu.make_async_copy(a, b, sem.at[i]) for i, (a, b) in enumerate(pairs)]
    for c in copies:
        c.start()
    for c in copies:
        c.wait()


def spread_blocks(table, first, held, flat, count, first_row):
    def one(i):
        at = pl.multiple_of(first_row + i * BROWS, 16)
        flat[pl.ds(at, BROWS), :] = held[table[first + i]].astype(jnp.float32)

    def step(i, carry):
        for u in range(4):
            one(i * 4 + u)
        return carry

    lax.fori_loop(0, count // 4, step, 0)
    for i in range(count // 4 * 4, count):
        one(i)


def unpack_vectors(flat, conv_weight, conv_bias, dt_bias, a_log, skip, norm_gain, gate_gain):
    bf16, f32 = jnp.bfloat16, jnp.float32
    tiles = CONVCH // LANES
    row = lax.broadcasted_iota(jnp.int32, (LANES, LANES), 0)
    col = lax.broadcasted_iota(jnp.int32, (LANES, LANES), 1)
    per_tile = LANES // KCONV
    for k in range(KCONV):
        total = jnp.zeros((tiles, LANES), f32)
        for q in range(KCONV):
            rows = flat[pl.ds(VEC_AT + q, tiles, stride=KCONV), :].astype(bf16)
            chosen = (row == KCONV * (col % per_tile) + k) & (col // per_tile == q)
            total = total + jnp.dot(rows, chosen.astype(bf16), preferred_element_type=f32)
        for i in range(tiles):
            conv_weight[k : k + 1, i * LANES : (i + 1) * LANES] = total[i : i + 1, :]
    bias_at = VEC_AT + tiles * KCONV
    for i in range(tiles):
        conv_bias[:, i * LANES : (i + 1) * LANES] = flat[bias_at + i : bias_at + i + 1, :]
    at = bias_at + tiles
    lane = lax.broadcasted_iota(jnp.int32, (8, LANES), 1)
    first = flat[at : at + 8, :]
    three = []
    for i in range(3):
        moved = pltpu.roll(first, LANES - i * HEADS, 1) if i else first
        three.append(jnp.where(lane < HEADS, moved, 0.0))
    dt_bias[...] = three[0][0:1, :]
    a_log[...] = three[1][0:1, :]
    for j in range(INNER // LANES):
        h = lax.broadcasted_iota(jnp.int32, (LANES, LANES), 0)
        c = lax.broadcasted_iota(jnp.int32, (LANES, LANES), 1) + j * LANES
        spread = (h == c // HEADDIM).astype(bf16)
        wide = jnp.dot(three[2].astype(bf16), spread, preferred_element_type=f32)
        skip[:, j * LANES : (j + 1) * LANES] = wide[0:1, :]
    shift = 3 * HEADS
    for out, begin, width in ((norm_gain, at, D), (gate_gain, at + D // LANES, INNER)):
        for j in range(width // LANES):
            x = pltpu.roll(flat[begin + j : begin + j + 1, :], LANES - shift, 1)
            y = pltpu.roll(flat[begin + j + 1 : begin + j + 2, :], LANES - shift, 1)
            out[:, j * LANES : (j + 1) * LANES] = jnp.where(lane[0:1] < LANES - shift, x, y)


def unpack_kernel(table, *refs):
    parts, outs, scratch = refs[:-14], refs[-14:-5], refs[-5:]
    w_in, w_out, *vectors = outs
    held, flat, flat_out, tile, sem = scratch
    pairs, at = [], 0
    for part in parts:
        pairs.append((part, held.at[pl.ds(at, part.shape[0])]))
        at += part.shape[0]
    copy_all(pairs, sem)
    spread_blocks(table, 0, held, flat, MID0, 0)
    spread_blocks(table, MID1, held, flat, NBLK - MID1, MID0 * BROWS)
    spread_blocks(table, MID0, held, flat_out, N1, HEAD_ROWS)
    flat_out[0:HEAD_ROWS, :] = flat[IN_ROWS : IN_ROWS + HEAD_ROWS, :]
    flat_out[OUT_ROWS - TAIL_ROWS :, :] = flat[MID0 * BROWS : MID0 * BROWS + TAIL_ROWS, :]
    unpack_vectors(flat, *vectors)
    rows = 128

    def out_step(i, carry):
        at = pl.multiple_of(i * rows, rows)
        for j in range(OUT_TILES):
            x = flat_out[pl.ds(at * OUT_TILES + j, rows, stride=OUT_TILES), :]
            w_out[pl.ds(at, rows), j * LANES : (j + 1) * LANES] = x.astype(jnp.bfloat16)
        return carry

    lax.fori_loop(0, INNER // rows, out_step, 0)
    lane = lax.broadcasted_iota(jnp.int32, (GROUPS, LANES), 1)

    def columns(j):
        for rho in range(GROUP):
            c, s = row_start(rho)
            x = flat[pl.ds(c + j, GROUPS, stride=GROUP_ROWS), :]
            if s:
                y = flat[pl.ds(c + j + 1, GROUPS, stride=GROUP_ROWS), :]
                x = jnp.where(
                    lane < LANES - s,
                    pltpu.roll(x, LANES - s, 1),
                    pltpu.roll(y, LANES - s, 1),
                )
            tile[pl.ds(rho, GROUPS, stride=GROUP), :] = x

    def step(j, carry):
        columns(j)
        w_in[:, pl.ds(pl.multiple_of(j * LANES, LANES), LANES)] = tile[...].astype(jnp.bfloat16)
        return carry

    lax.fori_loop(0, COL_TILES - 1, step, 0)
    columns(COL_TILES - 1)
    last = (COL_TILES - 1) * LANES
    inside = lax.broadcasted_iota(jnp.int32, (D, LANES), 1) < PROJ - last
    w_in[:, last:] = jnp.where(inside, tile[...], 0.0).astype(jnp.bfloat16)


def unpack(table, parts):
    held = sum(part.shape[0] for part in parts)
    f32 = jnp.float32
    return pl.pallas_call(
        unpack_kernel,
        out_shape=(
            shape((D, WIDE), jnp.bfloat16),
            shape((INNER, D), jnp.bfloat16),
            shape((KCONV, CONVCH), f32),
            shape((1, CONVCH), f32),
            shape((1, LANES), f32),
            shape((1, LANES), f32),
            shape((1, INNER), f32),
            shape((1, D), f32),
            shape((1, INNER), f32),
        ),
        in_specs=[SMEM] + [ANY] * len(parts),
        out_specs=(VMEM,) * 9,
        scratch_shapes=[
            pltpu.VMEM((held, BROWS, LANES), jnp.bfloat16),
            pltpu.VMEM((F0_ROWS, LANES), f32),
            pltpu.VMEM((OUT_ROWS, LANES), f32),
            pltpu.VMEM((D, LANES), f32),
            pltpu.SemaphoreType.DMA((len(parts),)),
        ],
        compiler_params=params(),
        cost_estimate=cost(20),
    )(table, *parts)


def permute_units(table, flat, count, first_row, staged):
    many = 16

    def step(i, carry):
        for u in range(many):
            at = pl.multiple_of(first_row + (i * many + u) * UNIT, UNIT)
            staged[table[i * many + u]] = flat[pl.ds(at, UNIT), :]
        return carry

    lax.fori_loop(0, count // many, step, 0)
    for i in range(count // many * many, count):
        staged[table[i]] = flat[first_row + i * UNIT : first_row + (i + 1) * UNIT, :]


def pack_in_kernel(table, hidden, grad, head, *refs):
    outs, (turned, tiles, flat, staged, sem) = refs[:-5], refs[-5:]
    turned[...] = hidden[...].T
    lane = lax.broadcasted_iota(jnp.int32, (GROUPS, LANES), 1)

    def product(p, count):
        at = p * 2 * LANES
        at = at if isinstance(at, int) else pl.multiple_of(at, 2 * LANES)
        return jnp.dot(
            turned[...], grad[:, pl.ds(at, count * LANES)], preferred_element_type=jnp.float32
        )

    def put(p, value):
        for k in range(value.shape[1] // LANES):
            at = (p * 2 + k) * D
            at = at if isinstance(at, int) else pl.multiple_of(at, D)
            tiles[pl.ds(at, D), :] = value[:, k * LANES : (k + 1) * LANES]

    def load(rho, j):
        return tiles[pl.ds(j * D + rho, GROUPS, stride=GROUP), :]

    def whole(rho, i):
        first = -(-PROJ * rho // LANES)
        col0 = first * LANES - PROJ * rho
        x = load(rho, i)
        if col0:
            x = jnp.where(
                lane < LANES - col0,
                pltpu.roll(x, LANES - col0, 1),
                pltpu.roll(load(rho, i + 1), LANES - col0, 1),
            )
        flat[pl.ds(first + i, GROUPS, stride=GROUP_ROWS), :] = x

    put(0, product(0, 2))
    put(1, product(1, 2))
    pairs = COL_TILES // 2

    def step(p, carry):
        for i in range(2):
            for rho in range(GROUP):
                whole(rho, p * 2 + i)
        put(p + 2, product(p + 2, 2))
        return carry

    lax.fori_loop(0, pairs - 2, step, 0)
    put(pairs, product(pairs, COL_TILES % 2))
    for rho in range(GROUP):
        first = -(-PROJ * rho // LANES)
        col0 = first * LANES - PROJ * rho
        full = (PROJ - col0) // LANES
        for i in range((pairs - 2) * 2, full):
            whole(rho, i)
        left = PROJ - col0 - full * LANES
        if left:
            begin = col0 + full * LANES
            j, s = begin // LANES, begin % LANES
            x = pltpu.roll(load(rho, j), LANES - s, 1) if s else load(rho, j)
            if s + left > LANES:
                x = jnp.where(lane < LANES - s, x, pltpu.roll(load(rho, j + 1), LANES - s, 1))
            y = pltpu.roll(load(rho + 1, 0), left, 1)
            flat[pl.ds(first + full, GROUPS, stride=GROUP_ROWS), :] = jnp.where(lane < left, x, y)
    flat[IN_ROWS : IN_ROWS + HEAD_ROWS, :] = head[...]
    permute_units(table, flat, MID0 * UNITS, 0, staged)
    copies, at = [], 0
    for out in outs:
        copies.append((staged.at[pl.ds(at, out.shape[0])], out))
        at += out.shape[0]
    copy_all(copies, sem)


def pack_in(table, hidden, grad, head, sizes):
    return pl.pallas_call(
        pack_in_kernel,
        out_shape=tuple(shape((n, UNIT, LANES), jnp.float32) for n in sizes),
        in_specs=[SMEM, VMEM, VMEM, VMEM],
        out_specs=(ANY,) * len(sizes),
        scratch_shapes=[
            pltpu.VMEM((D, hidden.shape[0]), jnp.bfloat16),
            pltpu.VMEM((COL_TILES * D, LANES), jnp.float32),
            pltpu.VMEM((MID0 * BROWS, LANES), jnp.float32),
            pltpu.VMEM((sum(sizes), UNIT, LANES), jnp.float32),
            pltpu.SemaphoreType.DMA((len(sizes),)),
        ],
        compiler_params=params(),
        cost_estimate=cost(20),
    )(table, hidden, grad, head)


def pack_out_kernel(
    table, mixed_out, grad, local, keep, send, head, tail, turned, flat, out, sem, *, slots
):
    rows = 256

    def step(i, carry):
        at = pl.multiple_of(i * rows, rows)
        turned[...] = mixed_out[:, pl.ds(at, rows)].T
        product = jnp.dot(turned[...], grad[...], preferred_element_type=jnp.float32)
        for j in range(OUT_TILES):
            flat[pl.ds(at * OUT_TILES + j, rows, stride=OUT_TILES), :] = product[
                :, j * LANES : (j + 1) * LANES
            ]
        return carry

    lax.fori_loop(0, INNER // rows, step, 0)
    head[...] = flat[0:HEAD_ROWS, :]
    tail[...] = flat[OUT_ROWS - TAIL_ROWS : OUT_ROWS, :]
    permute_units(table, flat, N1 * UNITS, HEAD_ROWS, out)

    def add_local(i, carry):
        out[i * slots + slots - 1] = local[...]
        return carry

    lax.fori_loop(0, out.shape[0] // slots, add_local, 0)
    half = keep.shape[0]
    copy_all([(out.at[pl.ds(0, half)], keep), (out.at[pl.ds(half, half)], send)], sem)


def pack_out(table, mixed_out, grad, local, devices, slots):
    return pl.pallas_call(
        partial(pack_out_kernel, slots=slots),
        out_shape=(
            shape((devices * slots // 2, UNIT, LANES), jnp.float32),
            shape((devices * slots // 2, UNIT, LANES), jnp.float32),
            shape((HEAD_ROWS, LANES), jnp.float32),
            shape((TAIL_ROWS, LANES), jnp.float32),
        ),
        in_specs=[SMEM, VMEM, VMEM, VMEM],
        out_specs=(ANY, ANY, VMEM, VMEM),
        scratch_shapes=[
            pltpu.VMEM((256, mixed_out.shape[0]), jnp.bfloat16),
            pltpu.VMEM((OUT_ROWS, LANES), jnp.float32),
            pltpu.VMEM((devices * slots, UNIT, LANES), jnp.float32),
            pltpu.SemaphoreType.DMA((2,)),
        ],
        compiler_params=params(),
    )(table, mixed_out, grad, local)


def adam_kernel(
    table, row_block, row_used, scale, got, late, master, first, second,
    o_first, o_second, o_master, flat, held, limit, used,
):
    capacity = master.shape[0]

    def step(i, carry):
        for u in range(UNITS):
            at = table[i * UNITS + u]
            rows = pl.ds(pl.multiple_of(i * BROWS + u * UNIT, UNIT), UNIT)
            flat[rows, :] = held[at]
        limit[pl.ds(i, 1), :] = jnp.full((1, LANES), END_OUT - row_block[i] * PBLOCK, jnp.int32)
        used[pl.ds(i, 1), :] = jnp.full((1, LANES), row_used[i], jnp.int32)
        return carry

    held[0 : got.shape[0]] = got[...]
    held[got.shape[0] :] = late[...]
    lax.fori_loop(0, capacity, step, 0)
    lane = lax.broadcasted_iota(jnp.int32, (capacity, LANES), 1)
    divisor = scale[0]
    for j in range(BROWS):
        cols = slice(j * LANES, (j + 1) * LANES)
        grad = jnp.where(used[...] > 0, flat[pl.ds(j, capacity, stride=BROWS), :], 0.0) / divisor
        matrix = lane + j * LANES < limit[...]
        weights = master[:, cols]
        new_first = BETA_ONE * first[:, cols] + (1.0 - BETA_ONE) * grad
        new_second = BETA_TWO * second[:, cols] + (1.0 - BETA_TWO) * grad * grad
        normal = (
            new_first
            / (1.0 - BETA_ONE**STEP)
            / (jnp.sqrt(new_second / (1.0 - BETA_TWO**STEP)) + ADAM_EPS)
        )
        rate = jnp.where(matrix, MATRIX_RATE, VECTOR_RATE)
        decay = jnp.where(matrix, WEIGHT_DECAY, 0.0)
        o_first[:, cols] = new_first
        o_second[:, cols] = new_second
        o_master[:, cols] = weights - rate * (normal + decay * weights)


def adam(table, row_block, row_used, divisor, got, late, master, first, second):
    capacity = master.shape[0]
    return pl.pallas_call(
        adam_kernel,
        out_shape=(shape(master.shape, jnp.float32),) * 3,
        in_specs=[SMEM] * 4 + [VMEM] * 5,
        out_specs=(VMEM,) * 3,
        scratch_shapes=[
            pltpu.VMEM((capacity * BROWS, LANES), jnp.float32),
            pltpu.VMEM((got.shape[0] + late.shape[0], UNIT, LANES), jnp.float32),
            pltpu.VMEM((capacity, LANES), jnp.int32),
            pltpu.VMEM((capacity, LANES), jnp.int32),
        ],
        compiler_params=params(),
    )(
        table, row_block, row_used.astype(jnp.int32), divisor.reshape(1), got, late, master, first, second
    )


def doubled(values, step):
    return jnp.concatenate([values, exchange(values, step)], axis=0)


def gather_steps(values, order):
    for step in order[:0:-1]:
        values = doubled(values, step)
    return values, exchange(values, order[0])


def reduce_step(kept, got, step, extra=None):
    half = kept.shape[0] // 2
    given = kept[half:] + got[half:]
    if extra is None:
        return kept[:half] + got[:half], exchange(given, step)
    arrived = exchange(jnp.concatenate([given, extra]), step)
    return kept[:half] + got[:half], arrived[:half], extra + arrived[half:]


CHUNK = 128
PAIRS = HEADS // 2
MIXW = INNER + 2 * NSTATE
DT_AT = INNER + CONVCH
F32 = jnp.float32
BF16 = jnp.bfloat16
NN = (((1,), (0,)), ((), ()))
NT = (((1,), (1,)), ((), ()))


def dot(a, b, dims=NN):
    return lax.dot_general(a, b, dims, preferred_element_type=F32)


def split(v):
    high = v.astype(BF16)
    return high, (v - high.astype(F32)).astype(BF16)


def dot3(a, b, dims=NN):
    ah, al = a
    bh, bl = b
    return dot(ah, bh, dims) + (dot(ah, bl, dims) + dot(al, bh, dims))


def heads_gather():
    return jnp.asarray(np.repeat(np.eye(HEADS, LANES, dtype=np.float32), HEADDIM, axis=0), BF16)


def three_parts(v):
    high = v.astype(BF16).astype(F32)
    rest = v - high
    middle = rest.astype(BF16).astype(F32)
    low = rest - middle
    return (high + pltpu.roll(middle, 32, 1) + pltpu.roll(low, 64, 1)).astype(BF16)


def triangle_sum(tri, v):
    parts = dot(tri, three_parts(v))
    lane = lax.broadcasted_iota(jnp.int32, parts.shape, 1)
    total = parts + pltpu.roll(parts, LANES - 32, 1) + pltpu.roll(parts, LANES - 64, 1)
    return jnp.where(lane < HEADS, total, 0.0)


def chunk_decays(dt, dt_bias, a_log):
    lane = lax.broadcasted_iota(jnp.int32, (CHUNK, LANES), 1)
    row = lax.broadcasted_iota(jnp.int32, (CHUNK, LANES), 0)
    shifted = dt + dt_bias
    delta = jnp.where(
        lane < HEADS, jnp.maximum(shifted, 0.0) + jnp.log1p(jnp.exp(-jnp.abs(shifted))), 0.0
    )
    rate = -jnp.exp(a_log)
    lower = (row >= lane).astype(BF16)
    cum = triangle_sum(lower, delta * rate)
    last = cum[CHUNK - 1 : CHUNK, :]
    return shifted, delta, rate, cum, last


def pair_mask():
    lane = lax.broadcasted_iota(jnp.int32, (CHUNK, LANES), 1)
    low = (lane < HEADDIM).astype(F32)
    return low.astype(BF16), (1.0 - low).astype(BF16)


QUADS = HEADS // 4
QWIDTH = 4 * HEADDIM


def sigmoid(v):
    return 0.5 * jnp.tanh(0.5 * v) + 0.5


def silu(v):
    return v * sigmoid(v)


def side_by_side(v):
    high, low = split(v)
    return jnp.concatenate([high, low], axis=1), high


def dot_parts(a, b):
    ahl, ah = a
    bh, bl = b
    return dot(ahl, jnp.concatenate([bh, bh], axis=0)) + dot(ah, bl)


def dot_turned(a, b):
    ah, al = a
    bh, bl = b
    both = dot(ah, jnp.concatenate([bh, bl], axis=0), NT)
    n = bh.shape[0]
    return both[:, :n] + both[:, n:] + dot(al, bh, NT)


def widen(delta, cum, quad):
    lane = lax.broadcasted_iota(jnp.int32, (CHUNK, LANES), 1)
    over = lambda v, h: jnp.broadcast_to(v[:, h : h + 1], (CHUNK, LANES))
    first = 4 * quad
    columns = [over(cum, first + k) for k in range(4)]
    rates = [over(delta, first + k) for k in range(4)]
    pair = lambda vs: jnp.concatenate(
        [jnp.where(lane < HEADDIM, vs[0], vs[1]), jnp.where(lane < HEADDIM, vs[2], vs[3])], axis=1
    )
    return pair(rates), pair(columns), columns


def pair_rows(parts, j, low, high):
    cols = slice(j * LANES, (j + 1) * LANES)
    return [jnp.concatenate([p[:, cols] * low, p[:, cols] * high], axis=0) for p in parts]


def scan_chunk(mixed, dt, dt_bias, a_log, skip, state, put):
    _, delta, _, cum, last = chunk_decays(dt, dt_bias, a_log)
    lane = lax.broadcasted_iota(jnp.int32, (CHUNK, LANES), 1)
    row = lax.broadcasted_iota(jnp.int32, (CHUNK, LANES), 0)
    bias = jnp.where(row >= lane, 0.0, -1e30)
    cum_t = cum.T
    inputs_b = mixed[:, INNER : INNER + NSTATE]
    readout = mixed[:, INNER + NSTATE :]
    affinity = dot3(split(readout), split(inputs_b), NT)
    readout_parts = side_by_side(readout)
    b_parts = side_by_side(inputs_b.T)
    low, high = pair_mask()
    for quad in range(QUADS):
        cols = slice(quad * QWIDTH, (quad + 1) * QWIDTH)
        wide_delta, wide_cum, columns = widen(delta, cum, quad)
        values = mixed[:, cols]
        scaled = values * wide_delta
        parts = split(scaled)
        outs = []
        for j in range(2):
            right_h, right_l = pair_rows(parts, j, low, high)
            left = []
            for k in range(2):
                h = 4 * quad + 2 * j + k
                within = jnp.exp(columns[2 * j + k] - cum_t[h : h + 1, :] + bias)
                left.append(split(affinity * within))
            left_h = jnp.concatenate([left[0][0], left[1][0]], axis=1)
            left_l = jnp.concatenate([left[0][1], left[1][1]], axis=1)
            both = dot(left_h, jnp.concatenate([right_h, right_l], axis=1))
            outs.append(both[:, :LANES] + both[:, LANES:] + dot(left_l, right_h))
        carried = state[:, cols]
        grown = jnp.exp(wide_cum)
        out = jnp.concatenate(outs, axis=1) + dot_parts(readout_parts, split(carried)) * grown
        tail = jnp.exp(wide_cum[CHUNK - 1 :] - wide_cum)
        state[:, cols] = carried * grown[CHUNK - 1 :] + dot_parts(b_parts, split(scaled * tail))
        put(quad, out + skip[:, cols] * values)


FORWARD_ROWS = 2 * CHUNK


def forward_kernel(
    tokens, w_in, norm_gain, conv_weight, conv_bias, dt_bias, a_log, skip, gain,
    hidden, gate, conv_in, dt, ssm, mixed_out, states, state, before, mixed, shift,
):
    @pl.when(pl.program_id(0) == 0)
    def _():
        state[...] = jnp.zeros_like(state)
        before[...] = jnp.zeros_like(before)

    x = tokens[...].astype(F32)
    inverse = lax.rsqrt(jnp.mean(x * x, axis=1, keepdims=True) + NORM_EPS)
    h = (x * inverse * norm_gain[...]).astype(BF16)
    hidden[...] = h
    dt[...] = dot(h, w_in[:, DT_AT:])
    wide = 2 * LANES
    for tile in range(CONVCH // wide):
        at = tile * wide
        product = dot(h, w_in[:, INNER + at : INNER + at + wide])
        conv_in[:, at : at + wide] = product
        for half in range(2):
            cols = slice(at + half * LANES, at + (half + 1) * LANES)
            rows = product[:, half * LANES : (half + 1) * LANES]
            earlier = before[:, cols]
            terms = moved_down(shift.at[tile * 2 + half], rows, earlier) + [rows]
            before[:, cols] = rows[FORWARD_ROWS - 8 :]
            mixed[:, cols] = silu(conv_sum(terms, conv_weight[:, cols], conv_bias[:, cols]))
    for tile in range(INNER // wide):
        cols = slice(tile * wide, (tile + 1) * wide)
        gate[:, cols] = dot(h, w_in[:, cols])
    for sub in range(FORWARD_ROWS // CHUNK):
        rows = slice(sub * CHUNK, (sub + 1) * CHUNK)
        states[sub] = state[...]
        squares = [jnp.zeros((CHUNK, LANES), F32)]

        def put(quad, out, rows=rows, squares=squares):
            cols = slice(quad * QWIDTH, (quad + 1) * QWIDTH)
            ssm[rows, cols] = out
            gated = out * silu(gate[rows, cols])
            first, second = gated[:, :LANES], gated[:, LANES:]
            squares[0] = squares[0] + first * first + second * second

        scan_chunk(
            mixed[rows, :], dt[rows, :], dt_bias[...], a_log[...], skip, state, put
        )
        rho = lax.rsqrt(jnp.sum(squares[0], axis=1, keepdims=True) * (1.0 / INNER) + NORM_EPS)
        for j in range(PAIRS):
            cols = slice(j * LANES, (j + 1) * LANES)
            gated = ssm[rows, cols] * silu(gate[rows, cols])
            mixed_out[rows, cols] = (gated * rho * gain[:, cols]).astype(BF16)


def forward(tokens, w_in, norm_gain, conv_weight, conv_bias, dt_bias, a_log, skip, gain):
    length = tokens.shape[0]
    by_row = lambda width: pl.BlockSpec((FORWARD_ROWS, width), lambda i: (i, 0))
    whole = lambda v: pl.BlockSpec(v.shape, lambda i: (0,) * v.ndim)
    per_step = FORWARD_ROWS // CHUNK
    return pl.pallas_call(
        forward_kernel,
        grid=(length // FORWARD_ROWS,),
        out_shape=(
            shape((length, D), BF16),
            shape((length, INNER), F32),
            shape((length, MIXW), F32),
            shape((length, LANES), F32),
            shape((length, INNER), F32),
            shape((length, INNER), BF16),
            shape((length // CHUNK, NSTATE, INNER), F32),
        ),
        in_specs=[by_row(D)]
        + [
            whole(v)
            for v in (w_in, norm_gain, conv_weight, conv_bias, dt_bias, a_log, skip, gain)
        ],
        out_specs=(
            by_row(D),
            by_row(INNER),
            by_row(MIXW),
            by_row(LANES),
            by_row(INNER),
            by_row(INNER),
            pl.BlockSpec((per_step, NSTATE, INNER), lambda i: (i, 0, 0)),
        ),
        scratch_shapes=[
            pltpu.VMEM((NSTATE, INNER), F32),
            pltpu.VMEM((8, MIXW), F32),
            pltpu.VMEM((FORWARD_ROWS, MIXW), F32),
            pltpu.VMEM((MIXW // LANES, FORWARD_ROWS + 8, LANES), F32),
        ],
        compiler_params=params(),
        cost_estimate=cost(33),
    )(tokens, w_in, norm_gain, conv_weight, conv_bias, dt_bias, a_log, skip, gain)


def eights(v):
    return jnp.sum(v.reshape(v.shape[0] // 8, 8, v.shape[1]), axis=0)


def backward_kernel(
    conv_in, earlier, dt, ssm, grad, grad_gate, states, conv_weight, conv_bias, dt_bias, a_log, skip,
    gather, grad_low, sums, skip_sums, conv_sums,
    grad_state, to_sum, mixed, slope, grad_mixed, following, shift,
):
    @pl.when(pl.program_id(0) == 0)
    def _():
        grad_state[...] = jnp.zeros_like(grad_state)
        sums[...] = jnp.zeros_like(sums)
        skip_sums[...] = jnp.zeros_like(skip_sums)
        conv_sums[...] = jnp.zeros_like(conv_sums)
        following[...] = jnp.zeros_like(following)

    begins = pl.program_id(0) == pl.num_programs(0) - 1

    for tile in range(MIXW // LANES):
        cols = slice(tile * LANES, (tile + 1) * LANES)
        rows = conv_in[:, cols]
        before = jnp.where(begins, 0.0, earlier[:, cols])
        terms = moved_down(shift.at[tile], rows, before) + [rows]
        value = conv_sum(terms, conv_weight[:, cols], conv_bias[:, cols])
        sig = sigmoid(value)
        mixed[:, cols] = value * sig
        slope[:, cols] = sig * (1.0 + value * (1.0 - sig))

    shifted, delta, rate, cum, last = chunk_decays(dt[...], dt_bias[...], a_log[...])
    lane = lax.broadcasted_iota(jnp.int32, (CHUNK, LANES), 1)
    row = lax.broadcasted_iota(jnp.int32, (CHUNK, LANES), 0)
    bias = jnp.where(lane >= row, 0.0, -1e30)
    heads = lane < HEADS
    cum_t = cum.T
    inputs_b = mixed[:, INNER : INNER + NSTATE]
    readout = mixed[:, INNER + NSTATE :]
    b_parts, c_parts = split(inputs_b), split(readout)
    b_wide = side_by_side(inputs_b)
    c_turned = side_by_side(readout.T)
    affinity = dot3(b_parts, c_parts, NT)
    low, high = pair_mask()
    grad_affinity = jnp.zeros((CHUNK, CHUNK), F32)
    grad_b = jnp.zeros((CHUNK, NSTATE), F32)
    grad_c = jnp.zeros((CHUNK, NSTATE), F32)
    last_row = lax.broadcasted_iota(jnp.int32, (CHUNK, QWIDTH), 0) == CHUNK - 1
    for quad in range(QUADS):
        cols = slice(quad * QWIDTH, (quad + 1) * QWIDTH)
        wide_delta, wide_cum, columns = widen(delta, cum, quad)
        grown = jnp.exp(wide_cum)
        tail = jnp.exp(wide_cum[CHUNK - 1 :] - wide_cum)
        end = grown[CHUNK - 1 :]
        values = mixed[:, cols]
        pulled = grad[:, cols]
        scaled = values * wide_delta
        x_parts, p_parts = split(scaled), split(pulled)
        outs = []
        for j in range(2):
            half = slice(j * LANES, (j + 1) * LANES)
            xh, xl = x_parts[0][:, half], x_parts[1][:, half]
            right_h, right_l = pair_rows(p_parts, j, low, high)
            pull = dot(
                jnp.concatenate([xh, xl], axis=1),
                jnp.concatenate([right_h, right_h], axis=1),
                NT,
            ) + dot(xh, right_l, NT)
            kernels = []
            for k in range(2):
                h = 4 * quad + 2 * j + k
                within = jnp.exp(cum_t[h : h + 1, :] - columns[2 * j + k] + bias)
                kernels.append(split(affinity * within))
                grad_affinity = grad_affinity + within * pull[:, k * CHUNK : (k + 1) * CHUNK]
            kernel_h = jnp.concatenate([kernels[0][0], kernels[1][0]], axis=1)
            kernel_l = jnp.concatenate([kernels[0][1], kernels[1][1]], axis=1)
            both = dot(kernel_h, jnp.concatenate([right_h, right_l], axis=1))
            outs.append(both[:, :LANES] + both[:, LANES:] + dot(kernel_l, right_h))
        late = grad_state[:, cols]
        late_parts = split(late)
        early = states[0, :, cols]
        from_state = dot_parts(b_wide, late_parts) * tail
        grad_scaled = jnp.concatenate(outs, axis=1) + from_state
        pulled_cum = split(pulled * grown)
        grad_c = grad_c + dot_turned(pulled_cum, split(early))
        grad_b = grad_b + dot_turned(split(scaled * tail), late_parts)
        grad_state[:, cols] = late * end + dot_parts(c_turned, pulled_cum)
        grad_mixed[:, cols] = grad_scaled * wide_delta + skip[:, cols] * pulled
        skip_sums[:, cols] += jnp.sum(pulled * values, axis=0, keepdims=True)
        to_sum[:CHUNK, cols] = grad_scaled * values
        inner = pulled * (ssm[:, cols] - skip[:, cols] * values) - scaled * grad_scaled
        extra = jnp.sum(scaled * from_state, axis=0, keepdims=True) + end * jnp.sum(
            late * early, axis=0, keepdims=True
        )
        to_sum[CHUNK:, cols] = inner + jnp.where(last_row, extra, 0.0)
    ga_parts = split(grad_affinity)
    grad_mixed[:, INNER : INNER + NSTATE] = grad_b + dot3(ga_parts, c_parts)
    grad_mixed[:, INNER + NSTATE :] = grad_c + dot3(split(grad_affinity.T), b_parts)


    def by_head(v):
        high, low = split(v)
        return dot(high, gather[...]) + dot(low, gather[...])

    direct, grad_cum = by_head(to_sum[:CHUNK, :]), by_head(to_sum[CHUNK:, :])
    upper = (lane >= row).astype(BF16)
    after = triangle_sum(upper, grad_cum)
    grad_delta = direct + rate * after
    grad_raw = jnp.where(heads, grad_delta * sigmoid(shifted), 0.0)
    grad_low[:, DT_AT:] = grad_raw.astype(BF16)
    sums[0:1, :] += jnp.sum(grad_raw, axis=0, keepdims=True)
    sums[1:2, :] += rate * jnp.sum(delta * after, axis=0, keepdims=True)
    grad_low[:, :INNER] = grad_gate[...]
    for tile in range(MIXW // LANES):
        cols = slice(tile * LANES, (tile + 1) * LANES)
        w = conv_weight[:, cols]
        g = grad_mixed[:, cols] * slope[:, cols]
        rows = conv_in[:, cols]
        later = following[:, cols]
        total = jnp.zeros((CHUNK, LANES), F32)
        arriving = moved_up(shift.at[tile], g, later) + [g]
        for k in range(KCONV):
            conv_sums[8 * k : 8 * k + 8, cols] += eights(rows * arriving[k])
            total = total + arriving[k] * w[k : k + 1]
        conv_sums[8 * KCONV :, cols] += eights(g)
        following[:, cols] = g[:8]
        grad_low[:, INNER + tile * LANES : INNER + (tile + 1) * LANES] = total.astype(BF16)


def backward(
    conv_in, dt, ssm, grad, grad_gate, states, conv_weight, conv_bias, dt_bias, a_log, skip, gather
):
    length = conv_in.shape[0]
    chunks = length // CHUNK
    whole = lambda v: pl.BlockSpec(v.shape, lambda i: (0,) * v.ndim)
    by_row = lambda width: pl.BlockSpec((CHUNK, width), lambda i: (chunks - 1 - i, 0))
    return pl.pallas_call(
        backward_kernel,
        grid=(chunks,),
        out_shape=(
            shape((length, WIDE), BF16),
            shape((8, LANES), F32),
            shape((1, INNER), F32),
            shape((8 * (KCONV + 1), MIXW), F32),
        ),
        in_specs=[
            by_row(MIXW),
            pl.BlockSpec((8, MIXW), lambda i: (jnp.maximum((chunks - 1 - i) * (CHUNK // 8) - 1, 0), 0)),
            by_row(LANES),
            by_row(INNER),
            by_row(INNER),
            by_row(INNER),
            pl.BlockSpec((1, NSTATE, INNER), lambda i: (chunks - 1 - i, 0, 0)),
        ]
        + [whole(v) for v in (conv_weight, conv_bias, dt_bias, a_log, skip, gather)],
        out_specs=(
            by_row(WIDE),
            pl.BlockSpec((8, LANES), lambda i: (0, 0)),
            pl.BlockSpec((1, INNER), lambda i: (0, 0)),
            pl.BlockSpec((8 * (KCONV + 1), MIXW), lambda i: (0, 0)),
        ),
        scratch_shapes=[pltpu.VMEM((NSTATE, INNER), F32)]
        + [pltpu.VMEM((2 * CHUNK, INNER), F32)]
        + [pltpu.VMEM((CHUNK, MIXW), F32)] * 3
        + [pltpu.VMEM((8, MIXW), F32), pltpu.VMEM((MIXW // LANES, CHUNK + 8, LANES), F32)],
        compiler_params=params(),
        cost_estimate=cost(43),
    )(
        conv_in, conv_in, dt, ssm, grad, grad_gate, states,
        conv_weight, conv_bias, dt_bias, a_log, skip, gather,
    )


def moved_down(scratch, v, before):
    rows = v.shape[0]
    scratch[0:8, :] = before
    scratch[8 : 8 + rows, :] = v
    return [scratch[8 - by : 8 - by + rows, :] for by in range(KCONV - 1, 0, -1)]


def moved_up(scratch, v, behind):
    rows = v.shape[0]
    scratch[0:rows, :] = v
    scratch[rows : rows + 8, :] = behind
    return [scratch[by : by + rows, :] for by in range(KCONV - 1, 0, -1)]


def conv_sum(terms, weight, bias):
    total = bias + terms[KCONV - 1] * weight[KCONV - 1 : KCONV]
    for k in range(KCONV - 1):
        total = total + terms[k] * weight[k : k + 1]
    return total


def loss_kernel(
    limit, mixed_out, w_out, tokens, teacher, mask, block_out, grad_result, grad_branch, error
):
    step = pl.program_id(0)

    @pl.when(step == 0)
    def _():
        error[...] = jnp.zeros_like(error)

    rows = tokens.shape[0]
    result = tokens[...].astype(F32) + dot(mixed_out[...], w_out[...])
    position = step * rows + lax.broadcasted_iota(jnp.int32, (rows, 1), 0)
    valid = (position < limit[0]).astype(F32)
    turned = jnp.broadcast_to(mask[...].astype(F32), (LANES, rows)).T
    weight = valid * turned[:, 0:1]
    block_out[...] = (result * valid).astype(BF16)
    misfit = result - teacher[...].astype(F32)
    pulled = 2.0 * weight * misfit
    grad_result[...] = pulled
    errors = jnp.sum(0.5 * pulled * misfit, axis=0, keepdims=True)
    for j in range(D // LANES):
        error[j : j + 1, :] += errors[:, j * LANES : (j + 1) * LANES]
    error[D // LANES : D // LANES + 1, :] += jnp.sum(valid * turned, axis=0, keepdims=True)
    grad_branch[...] = pulled.astype(BF16)


def loss_part(limit, mixed_out, w_out, tokens, teacher, mask):
    length = tokens.shape[0]
    rows = 256
    by_row = lambda width: pl.BlockSpec((rows, width), lambda i: (i, 0))
    return pl.pallas_call(
        loss_kernel,
        grid=(length // rows,),
        out_shape=(
            shape((length, D), BF16),
            shape((length, D), F32),
            shape((length, D), BF16),
            shape((8, LANES), F32),
        ),
        in_specs=[
            SMEM,
            by_row(INNER),
            pl.BlockSpec(w_out.shape, lambda i: (0, 0)),
            by_row(D),
            by_row(D),
            pl.BlockSpec((1, rows), lambda i: (0, i)),
        ],
        out_specs=(by_row(D), by_row(D), by_row(D), pl.BlockSpec((8, LANES), lambda i: (0, 0))),
        compiler_params=params(),
        cost_estimate=cost(8),
    )(limit, mixed_out, w_out, tokens, teacher, mask)


def gate_kernel(grad_branch, w_out, ssm, gate, gain, grad_ssm, grad_gate, gain_sums):
    @pl.when(pl.program_id(0) == 0)
    def _():
        gain_sums[...] = jnp.zeros_like(gain_sums)

    grad_mixed = dot(grad_branch[...], w_out[...], NT)
    g = gate[...]
    sig = sigmoid(g)
    act = g * sig
    inner = ssm[...]
    gated = inner * act
    rho = lax.rsqrt(jnp.mean(gated * gated, axis=1, keepdims=True) + NORM_EPS)
    unit = gated * rho
    gain_sums[...] += jnp.sum(unit * grad_mixed, axis=0, keepdims=True)
    grad_unit = grad_mixed * gain[...]
    share = jnp.mean(grad_unit * unit, axis=1, keepdims=True)
    grad_gated = rho * (grad_unit - unit * share)
    grad_ssm[...] = grad_gated * act
    grad_gate[...] = (grad_gated * inner * (sig * (1.0 + g * (1.0 - sig)))).astype(BF16)


def gate_part(grad_branch, w_out, ssm, gate, gain):
    length = ssm.shape[0]
    rows = 256
    by_row = lambda width: pl.BlockSpec((rows, width), lambda i: (i, 0))
    whole = lambda v: pl.BlockSpec(v.shape, lambda i: (0,) * v.ndim)
    return pl.pallas_call(
        gate_kernel,
        grid=(length // rows,),
        out_shape=(shape((length, INNER), F32), shape((length, INNER), BF16), shape((1, INNER), F32)),
        in_specs=[by_row(D), whole(w_out), by_row(INNER), by_row(INNER), whole(gain)],
        out_specs=(by_row(INNER), by_row(INNER), pl.BlockSpec((1, INNER), lambda i: (0, 0))),
        compiler_params=params(),
        cost_estimate=cost(12),
    )(grad_branch, w_out, ssm, gate, gain)


def input_kernel(grad_low, w_in, tokens, norm_gain, grad_result, out, sums):
    @pl.when(pl.program_id(0) == 0)
    def _():
        sums[...] = jnp.zeros_like(sums)

    x = tokens[...].astype(F32)
    inverse = lax.rsqrt(jnp.mean(x * x, axis=1, keepdims=True) + NORM_EPS)
    unit = x * inverse
    grad_hidden = dot(grad_low[...], w_in[...], NT)
    sums[...] += jnp.sum(grad_hidden * unit, axis=0, keepdims=True)
    pulled = grad_hidden * norm_gain[...]
    share = jnp.mean(pulled * unit, axis=1, keepdims=True)
    out[...] = grad_result[...] + inverse * (pulled - unit * share)


def input_backward(grad_low, w_in, tokens, norm_gain, grad_result):
    length = tokens.shape[0]
    rows = 256
    by_row = lambda width: pl.BlockSpec((rows, width), lambda i: (i, 0))
    whole = lambda v: pl.BlockSpec(v.shape, lambda i: (0,) * v.ndim)
    return pl.pallas_call(
        input_kernel,
        grid=(length // rows,),
        out_shape=(shape((length, D), F32), shape((1, D), F32)),
        in_specs=[by_row(WIDE), whole(w_in), by_row(D), whole(norm_gain), by_row(D)],
        out_specs=(by_row(D), pl.BlockSpec((1, D), lambda i: (0, 0))),
        compiler_params=params(),
        cost_estimate=cost(15),
    )(grad_low, w_in, tokens, norm_gain, grad_result)


def vector_kernel(tail, conv_sums, sums, skip_sums, norm_sums, gate_sums, gather, out, taps):
    tiles = CONVCH // LANES
    out[...] = jnp.zeros_like(out)
    out[0:TAIL_ROWS, :] = tail[...]
    for k in range(KCONV):
        for i in range(tiles):
            partial_sums = conv_sums[8 * k : 8 * k + 8, i * LANES : (i + 1) * LANES]
            taps[k * 16 + i : k * 16 + i + 1, :] = jnp.sum(partial_sums, axis=0, keepdims=True)
    row = lax.broadcasted_iota(jnp.int32, (LANES, LANES), 0)
    col = lax.broadcasted_iota(jnp.int32, (LANES, LANES), 1)
    per_tile = LANES // KCONV

    def exact(v, chosen):
        high = v.astype(BF16)
        rest = v - high.astype(F32)
        middle = rest.astype(BF16)
        low = (rest - middle.astype(F32)).astype(BF16)
        return dot(high, chosen) + (dot(middle, chosen) + dot(low, chosen))

    for q in range(KCONV):
        total = jnp.zeros((tiles, LANES), F32)
        for k in range(KCONV):
            chosen = (col == KCONV * (row % per_tile) + k) & (row // per_tile == q)
            total = total + exact(taps[k * 16 : k * 16 + tiles, :], chosen.astype(BF16))
        out[pl.ds(TAIL_ROWS + q, tiles, stride=KCONV), :] = total
    bias_at = TAIL_ROWS + tiles * KCONV
    for i in range(tiles):
        partial_sums = conv_sums[8 * KCONV :, i * LANES : (i + 1) * LANES]
        out[bias_at + i : bias_at + i + 1, :] = jnp.sum(partial_sums, axis=0, keepdims=True)
    lane = lax.broadcasted_iota(jnp.int32, (1, LANES), 1)
    skip = exact(jnp.broadcast_to(skip_sums[...], (8, INNER)), gather[...])[0:1, :]
    parts = [sums[0:1, :], sums[1:2, :], skip]
    parts = [jnp.where(lane < HEADS, v, 0.0) for v in parts]
    before = parts[0] + pltpu.roll(parts[1], HEADS, 1) + pltpu.roll(parts[2], 2 * HEADS, 1)
    at, shift = bias_at + tiles, 3 * HEADS
    for source in (norm_sums, gate_sums):
        for j in range(source.shape[1] // LANES):
            here = pltpu.roll(source[:, j * LANES : (j + 1) * LANES], shift, 1)
            out[at : at + 1, :] = jnp.where(lane < shift, before, here)
            before = here
            at += 1
    out[at : at + 1, :] = jnp.where(lane < shift, before, 0.0)


def pack_vectors(tail, conv_sums, sums, skip_sums, norm_sums, gate_sums, gather):
    return pl.pallas_call(
        vector_kernel,
        out_shape=shape(((NBLK - MID1) * BROWS, LANES), F32),
        in_specs=[VMEM] * 7,
        out_specs=VMEM,
        scratch_shapes=[pltpu.VMEM((KCONV * 16, LANES), F32)],
        compiler_params=params(),
    )(tail, conv_sums, sums, skip_sums, norm_sums, gate_sums, gather)


def body(tokens, teacher, lengths, loss_mask, owners, master, first_moment, second_moment):
    capacity = master.shape[0]
    dp, fsdp = lax.axis_size("dp"), lax.axis_size("fsdp")
    devices = dp * fsdp
    me = lax.axis_index(AXES).astype(jnp.int32)
    x_first, y_first, z_first = step_orders(dp, fsdp)
    tie = lambda *values: lax.optimization_barrier(values)

    sent = send_blocks(owners, master, devices, me)
    at_home = lax.all_to_all(sent, AXES, 0, 0, tiled=True)
    owners, tokens, loss_mask, _ = tie(owners, tokens, loss_mask, sent)
    plan = make_plan(owners, capacity, devices, me)
    streams = cut(even(plan["slots"], 3), (x_first, y_first, z_first))
    table = stream_places(plan["home"], plan["slot"], me, streams, devices)
    u0, u1 = plan["unit_slots"]
    sizes = [-(-u0 // 5)] * 4
    unit_streams = cut(sizes + [u0 - sum(sizes)], (x_first, y_first, x_first, y_first, z_first))
    unit_table = stream_places(plan["unit_home"], plan["unit_slot"], me, unit_streams, devices)
    unit_table = unit_table[:MID0].reshape(-1)
    order1 = x_first[:2] + x_first[2 + bits_of(fsdp) :] + x_first[2 : 2 + bits_of(fsdp)]
    unit_table1 = place_of(plan["unit_home"] ^ me, order1) * (u1 + 1) + plan["unit_slot"]
    unit_table1 = unit_table1[MID0:MID1].reshape(-1)
    inputs, target = tokens[0], teacher[0]
    (at_home, table, unit_table, unit_table1, received, back_table, row_from, row_block,
     row_used) = tie(
        at_home, table, unit_table, unit_table1, plan["received"], plan["back"],
        plan["row_from"], plan["row_block"], plan["row_used"],
    )
    mine = pick_blocks(received, at_home, [size for _, size, _ in streams])
    parts = []
    for values, (_, _, order) in zip(mine, streams):
        parts += gather_steps(values, order)
    (input_weight, output_weight, conv_weight, conv_bias, dt_bias, a_log, skip, norm_gain,
     gate_gain) = unpack(table, parts)
    gather = heads_gather()
    hidden, gate, conv_in, dt, ssm, mixed_out, states = forward(
        inputs, input_weight, norm_gain, conv_weight, conv_bias, dt_bias, a_log, skip, gate_gain
    )
    block_out, grad_result, grad_branch, local = loss_part(
        lengths, mixed_out, output_weight, inputs, target, loss_mask
    )
    keep1, send1, head, tail = pack_out(
        unit_table1, mixed_out, grad_branch, local, devices, u1 + 1
    )
    grad_branch, send1 = tie(grad_branch, send1)
    got1 = exchange(send1, order1[0])
    grad_ssm, grad_gate, gain_sums = gate_part(grad_branch, output_weight, ssm, gate, gate_gain)
    grad_ssm, keep1, got1 = tie(grad_ssm, keep1, got1)
    keep1, got1 = reduce_step(keep1, got1, order1[1])
    grad_low, sums, skip_sums, conv_sums = backward(
        conv_in, dt, ssm, grad_ssm, grad_gate, states,
        conv_weight, conv_bias, dt_bias, a_log, skip, gather,
    )
    grad_low, keep1, got1 = tie(grad_low, keep1, got1)
    steps1 = order1[2:]
    for step in steps1[:1]:
        keep1, got1 = reduce_step(keep1, got1, step)
    halves = []
    for _, size, _ in unit_streams:
        halves += [devices * size // 2] * 2
    packed = list(pack_in(unit_table, hidden, grad_low, head, halves))
    packed[0], keep1, got1 = tie(packed[0], keep1, got1)
    kept = packed[::2]
    got = [exchange(v, order[0]) for v, (_, _, order) in zip(packed[1::2], unit_streams)]
    *got, grad_low, conv_sums, tail = tie(*got, grad_low, conv_sums, tail)
    for i, (_, _, order) in enumerate(unit_streams):
        kept[i], got[i] = reduce_step(kept[i], got[i], order[1])
    for step in steps1[1:2]:
        keep1, got1 = reduce_step(keep1, got1, step)
    input_grad, norm_sums = input_backward(grad_low, input_weight, inputs, norm_gain, grad_result)
    grad_vec = pack_vectors(tail, conv_sums, sums, skip_sums, norm_sums, gain_sums, gather)
    grad_vec = grad_vec.reshape((NBLK - MID1) * UNITS, UNIT, LANES)
    *got, got1, grad_vec, input_grad = tie(*got, got1, grad_vec, input_grad)
    for step in steps1[2:]:
        keep1, got1 = reduce_step(keep1, got1, step)
    last = len(unit_streams) - 1
    for k in range(2, len(x_first) - 2):
        kept[last], got[last] = reduce_step(kept[last], got[last], z_first[k])
        for i, (_, _, order) in enumerate(unit_streams[:last]):
            if i == 0:
                kept[i], got[i], grad_vec = reduce_step(kept[i], got[i], order[k], grad_vec)
            else:
                kept[i], got[i] = reduce_step(kept[i], got[i], order[k])
    stay = fold(list(zip(kept[:last], got[:last])), grad_vec)
    arrived = exchange_quarters(stay, x_first[-2:])
    for step in z_first[-2:]:
        kept[last], got[last] = reduce_step(kept[last], got[last], step)
    back = units_to_owners(
        back_table, [[stay[0], *arrived], [kept[last], got[last]], [keep1, got1]]
    )
    n = stay[0].shape[0]
    grad_vec = grad_vec + (arrived[0][n:] + (arrived[1][n:] + arrived[2][n:]))
    back, grad_vec = tie(back, grad_vec)
    returned = lax.all_to_all(back, AXES, 0, 0, tiled=True)
    for step in x_first[:2]:
        grad_vec = grad_vec + exchange(grad_vec, step)
    local_sums = keep1[u1] + got1[u1]
    error_sum = jnp.sum(local_sums[: D // LANES])
    divisor = local_sums[D // LANES, 0] * D
    new_first, new_second, new_master = adam(
        row_from,
        row_block,
        row_used,
        divisor,
        returned,
        grad_vec,
        master,
        first_moment,
        second_moment,
    )
    mean_loss = error_sum / divisor
    return (block_out[None], input_grad[None], mean_loss, new_first, new_second, new_master)


def solution(mesh):
    return jax.shard_map(
        body,
        mesh=mesh,
        in_specs=(
            P(AXES, None, None),
            P(AXES, None, None),
            P(AXES),
            P(AXES, None),
            P(),
            P(AXES, None),
            P(AXES, None),
            P(AXES, None),
        ),
        out_specs=(
            P(AXES, None, None),
            P(AXES, None, None),
            P(),
            P(AXES, None),
            P(AXES, None),
            P(AXES, None),
        ),
        check_vma=False,
    )
```

```python
from functools import partial

import jax
import jax.numpy as jnp
import numpy as np
from jax import lax
from jax.experimental import pallas as pl
from jax.experimental.pallas import tpu as pltpu
from jax.sharding import PartitionSpec as P

D = 768
INNER = 1536
NSTATE = 128
HEADDIM = 64
KCONV = 4
SCAN_LEN = 256
PBLOCK = 4096
STEP = 10
HEADS = 24
CONVCH = 1792
PROJ = 3352
PTOT = 3765320
NBLK = 920

LANES = 128
BROWS = PBLOCK // LANES
UNIT = 8
UNITS = BROWS // UNIT
END_IN = D * PROJ
END_OUT = END_IN + INNER * D
MID0 = -(-END_IN // PBLOCK)
MID1 = END_OUT // PBLOCK
N0 = MID0 + NBLK - MID1
N1 = MID1 - MID0
F0_ROWS = N0 * BROWS
IN_ROWS = END_IN // LANES
HEAD_ROWS = MID0 * BROWS - IN_ROWS
TAIL_ROWS = (END_OUT - MID1 * PBLOCK) // LANES
OUT_ROWS = INNER * D // LANES
VEC_ROWS = (NBLK - MID1) * BROWS - TAIL_ROWS
VEC_AT = MID0 * BROWS + TAIL_ROWS
GROUP = 16
GROUPS = D // GROUP
GROUP_ROWS = GROUP * PROJ // LANES
COL_TILES = -(-PROJ // LANES)
WIDE = COL_TILES * LANES
OUT_TILES = D // LANES

NORM_EPS = 1e-05
ADAM_EPS = 1e-08
BETA_ONE = 0.9
BETA_TWO = 0.999
MATRIX_RATE = 0.03
VECTOR_RATE = 0.2
WEIGHT_DECAY = 0.1
PRECISE = lax.Precision.HIGHEST
AXES = ("dp", "fsdp")
VMEM_LIMIT = 60 * 1024 * 1024


def bits_of(count):
    return count.bit_length() - 1


def step_orders(dp, fsdp):
    wide = [("dp", i) for i in range(bits_of(dp))]
    narrow = [("fsdp", i) for i in range(bits_of(fsdp))]
    first = wide[:2] + narrow + wide[2:]
    second = wide[:1] + narrow + wide[1:]
    third = wide[:1] + wide[2:] + wide[1:2] + narrow
    return first, second, third


def cut(sizes, orders):
    streams, at = [], 0
    for size, order in zip(sizes, orders):
        if size:
            streams.append((at, size, order))
        at += size
    return streams


def even(total, parts):
    return [total // parts + (i < total % parts) for i in range(parts)]


def exchange(values, *steps):
    axes = {axis for axis, _ in steps}
    if len(axes) == 1:
        (axis,) = axes
        mask = sum(1 << bit for _, bit in steps)
        pairs = [(i, i ^ mask) for i in range(lax.axis_size(axis))]
        return lax.ppermute(values, axis, pairs)
    low = bits_of(lax.axis_size("fsdp"))
    mask = sum(1 << (bit + (low if axis == "dp" else 0)) for axis, bit in steps)
    count = lax.axis_size("dp") * lax.axis_size("fsdp")
    return lax.ppermute(values, AXES, [(i, i ^ mask) for i in range(count)])


def place_of(relative, order):
    shift_of = {"dp": bits_of(lax.axis_size("fsdp")), "fsdp": 0}
    place = jnp.zeros_like(relative)
    for axis, bit in order:
        place = place * 2 + ((relative >> (shift_of[axis] + bit)) & 1)
    return place


def class_counts(owners, devices):
    block = jnp.arange(NBLK, dtype=jnp.int32)
    mid = ((block >= MID0) & (block < MID1))[None, :]
    device = jnp.arange(devices, dtype=jnp.int32)
    below = owners[None, :] < device[:, None]
    owned = owners[None, :] == device[:, None]

    def total(mask):
        return jnp.sum(mask.astype(jnp.int32), axis=1)

    start = (total(below & ~mid), total(below & mid))
    count = (total(owned & ~mid), total(owned & mid))
    return start, count, total(owned & (block < MID0)[None, :])


def my_counts(owners, me):
    block = jnp.arange(NBLK, dtype=jnp.int32)
    mid = (block >= MID0) & (block < MID1)
    below, owned = owners < me, owners == me
    total = lambda mask: jnp.sum(mask.astype(jnp.int32))
    start = (total(below & ~mid), total(below & mid))
    count = (total(owned & ~mid), total(owned & mid))
    return start, count, total(owned & (block < MID0))


def pair_lanes(capacity, devices):
    return -(-capacity // devices)


def make_plan(owners, capacity, devices, me):
    block = jnp.arange(NBLK, dtype=jnp.int32)
    mid = (block >= MID0) & (block < MID1)
    same = mid[:, None] == mid[None, :]
    before = (owners[None, :] < owners[:, None]) | (
        (owners[None, :] == owners[:, None]) & (block[None, :] < block[:, None])
    )
    order = jnp.sum(before.astype(jnp.int32), axis=1)
    order_in_class = jnp.sum((same & before).astype(jnp.int32), axis=1)
    home, slot = order % devices, order // devices
    device = jnp.arange(devices, dtype=jnp.int32)
    start, count, _ = class_counts(owners, devices)
    my_start, my_count, my_early = my_counts(owners, me)
    pair = pair_lanes(capacity, devices)

    slots = -(-NBLK // devices)
    wanted = me + devices * jnp.arange(slots, dtype=jnp.int32)
    first = start[0] + start[1]
    ends = first + count[0] + count[1]
    owner = jnp.sum((ends[None, :] <= wanted[:, None]).astype(jnp.int32), axis=1)
    owner = jnp.minimum(owner, devices - 1)
    base = jnp.sum(jnp.where(device[None, :] == owner[:, None], first[None, :], 0), axis=1)
    received = owner * pair + jnp.clip((wanted - base) // devices, 0, pair - 1)

    back_pair = (UNITS * capacity + 2 * (devices - 1)) // devices
    unit = UNITS * order_in_class[:, None] + jnp.arange(UNITS, dtype=jnp.int32)[None, :]
    unit_home, unit_slot = unit % devices, unit // devices
    unit_slots = (-(-UNITS * N0 // devices), -(-UNITS * N1 // devices))
    lane = jnp.arange(back_pair, dtype=jnp.int32)

    def units_back(kind):
        turn = lane if kind == 0 else back_pair - 1 - lane
        first = UNITS * start[kind][:, None]
        k = (me - first) % devices + turn[None, :] * devices
        return k < UNITS * count[kind][:, None], (first + k) // devices

    valid0, slot0 = units_back(0)
    valid1, slot1 = units_back(1)
    back = jnp.where(valid0, slot0, jnp.where(valid1, unit_slots[0] + slot1, 0)).reshape(-1)

    row = jnp.arange(capacity, dtype=jnp.int32)
    is_mid = (row >= my_early) & (row < my_early + my_count[1])
    k = jnp.where(is_mid, row - my_early, jnp.where(row < my_early, row, row - my_count[1]))
    first = UNITS * jnp.where(is_mid, my_start[1], my_start[0])
    k = UNITS * k[:, None] + jnp.arange(UNITS, dtype=jnp.int32)[None, :]
    turn = k // devices
    row_from = ((first[:, None] + k) % devices) * back_pair + jnp.where(
        is_mid[:, None], back_pair - 1 - turn, turn
    )
    row_used = row < my_count[0] + my_count[1]
    mine = (owners == me)[None, :]
    rank = jnp.sum((mine & (block[None, :] < block[:, None])).astype(jnp.int32), axis=1)
    row_block = jnp.sum(
        jnp.where(mine & (rank[None, :] == row[:, None]), block[None, :], 0), axis=1
    )
    late = devices * back_pair + UNITS * (row_block - MID1)
    late = late[:, None] + jnp.arange(UNITS, dtype=jnp.int32)[None, :]
    row_from = jnp.where((row_block >= MID1)[:, None], late, row_from)
    row_from = jnp.where(row_used[:, None], row_from, 0).reshape(-1)
    return dict(
        home=home, slot=slot, slots=slots,
        received=received, unit_home=unit_home, unit_slot=unit_slot,
        unit_slots=unit_slots, back=back, row_from=row_from,
        row_used=row_used, row_block=row_block,
    )


def stream_places(home, slot, me, streams, devices):
    relative = home ^ me
    place = jnp.zeros_like(slot)
    for begin, size, order in streams:
        inside = (slot >= begin) & (slot < begin + size)
        at = devices * begin + place_of(relative, order) * size + slot - begin
        place = jnp.where(inside, at, place)
    return place


def cost(microseconds):
    return pl.CostEstimate(
        flops=int(microseconds * 1e9), bytes_accessed=int(microseconds * 3e6), transcendentals=0
    )


ANY = pl.BlockSpec(memory_space=pl.ANY)
VMEM = pl.BlockSpec(memory_space=pltpu.VMEM)
SMEM = pl.BlockSpec(memory_space=pltpu.SMEM)


def params(**extra):
    return pltpu.CompilerParams(vmem_limit_bytes=VMEM_LIMIT, **extra)


def shape(dims, dtype):
    return jax.ShapeDtypeStruct(dims, dtype)


def send_kernel(my_index, owners, master, out, flat, *, devices):
    capacity = master.shape[0]
    me = my_index[0]
    for j in range(BROWS):
        flat[pl.ds(j, capacity, stride=BROWS), :] = master[:, j * LANES : (j + 1) * LANES]
    held = owners[...]
    below, owned = held < me, held == me

    def total(mask):
        return jnp.sum(jnp.where(mask, 1.0, 0.0)).astype(jnp.int32)

    start, count = total(below), total(owned)
    pair = out.shape[0] // devices

    def step(home, carry):
        for s in range(pair):
            k = lax.rem(home - start + devices * NBLK, devices) + s * devices
            row = jnp.where(k < count, k, 0)
            rows = pl.ds(pl.multiple_of(row * BROWS, BROWS), BROWS)
            out[home * pair + s] = flat[rows, :].astype(out.dtype)
        return carry

    lax.fori_loop(0, devices, step, 0)


def send_blocks(owners, master, devices, me):
    rows = -(-NBLK // (8 * LANES)) * 8
    held = jnp.pad(owners, (0, rows * LANES - NBLK), constant_values=1 << 20).reshape(rows, LANES)
    count = devices * pair_lanes(master.shape[0], devices)
    return pl.pallas_call(
        partial(send_kernel, devices=devices),
        out_shape=shape((count, BROWS, LANES), jnp.bfloat16),
        in_specs=[SMEM, VMEM, VMEM],
        out_specs=VMEM,
        scratch_shapes=[pltpu.VMEM((master.shape[0] * BROWS, LANES), jnp.float32)],
        compiler_params=params(),
    )(me.reshape(1), held, master)


def pick_kernel(table, source, *outs):
    at = 0
    for out in outs:

        def step(i, carry, out=out, at=at):
            out[i] = source[table[at + i]]
            return carry

        lax.fori_loop(0, out.shape[0], step, 0)
        at += out.shape[0]


def pick_blocks(table, source, sizes):
    return pl.pallas_call(
        pick_kernel,
        out_shape=tuple(shape((n,) + source.shape[1:], source.dtype) for n in sizes),
        in_specs=[SMEM, VMEM],
        out_specs=(VMEM,) * len(sizes),
        compiler_params=params(),
    )(table, source)


def back_kernel(table, *refs, sizes):
    sources, (out, held) = refs[:-2], refs[-2:]
    at = i = 0
    for size in sizes:
        n = sources[i].shape[0]
        total = sources[i][...]
        for k in range(1, size):
            total = total + sources[i + k][0:n]
        held[at : at + n] = total
        at += n
        i += size

    def step(i, carry):
        for u in range(8):
            out[i * 8 + u] = held[table[i * 8 + u]]
        return carry

    total = out.shape[0]
    lax.fori_loop(0, total // 8, step, 0)


def units_to_owners(table, groups):
    return pl.pallas_call(
        partial(back_kernel, sizes=[len(g) for g in groups]),
        out_shape=shape((table.shape[0], UNIT, LANES), jnp.float32),
        in_specs=[SMEM] + [VMEM] * sum(len(g) for g in groups),
        out_specs=VMEM,
        scratch_shapes=[pltpu.VMEM((sum(g[0].shape[0] for g in groups), UNIT, LANES), jnp.float32)],
        compiler_params=params(),
    )(table, *[v for g in groups for v in g])


def row_start(rho):
    return (PROJ * rho) // LANES, (PROJ * rho) % LANES


def copy_all(pairs, sem):
    copies = [pltpu.make_async_copy(a, b, sem.at[i]) for i, (a, b) in enumerate(pairs)]
    for c in copies:
        c.start()
    for c in copies:
        c.wait()


def spread_blocks(table, first, held, flat, count, first_row):
    def one(i):
        at = pl.multiple_of(first_row + i * BROWS, 16)
        flat[pl.ds(at, BROWS), :] = held[table[first + i]].astype(jnp.float32)

    def step(i, carry):
        for u in range(4):
            one(i * 4 + u)
        return carry

    lax.fori_loop(0, count // 4, step, 0)
    for i in range(count // 4 * 4, count):
        one(i)


def unpack_vectors(flat, conv_weight, conv_bias, dt_bias, a_log, skip, norm_gain, gate_gain):
    bf16, f32 = jnp.bfloat16, jnp.float32
    tiles = CONVCH // LANES
    row = lax.broadcasted_iota(jnp.int32, (LANES, LANES), 0)
    col = lax.broadcasted_iota(jnp.int32, (LANES, LANES), 1)
    per_tile = LANES // KCONV
    for k in range(KCONV):
        total = jnp.zeros((tiles, LANES), f32)
        for q in range(KCONV):
            rows = flat[pl.ds(VEC_AT + q, tiles, stride=KCONV), :].astype(bf16)
            chosen = (row == KCONV * (col % per_tile) + k) & (col // per_tile == q)
            total = total + jnp.dot(rows, chosen.astype(bf16), preferred_element_type=f32)
        for i in range(tiles):
            conv_weight[k : k + 1, i * LANES : (i + 1) * LANES] = total[i : i + 1, :]
    bias_at = VEC_AT + tiles * KCONV
    for i in range(tiles):
        conv_bias[:, i * LANES : (i + 1) * LANES] = flat[bias_at + i : bias_at + i + 1, :]
    at = bias_at + tiles
    lane = lax.broadcasted_iota(jnp.int32, (8, LANES), 1)
    first = flat[at : at + 8, :]
    three = []
    for i in range(3):
        moved = pltpu.roll(first, LANES - i * HEADS, 1) if i else first
        three.append(jnp.where(lane < HEADS, moved, 0.0))
    dt_bias[...] = three[0][0:1, :]
    a_log[...] = three[1][0:1, :]
    for j in range(INNER // LANES):
        h = lax.broadcasted_iota(jnp.int32, (LANES, LANES), 0)
        c = lax.broadcasted_iota(jnp.int32, (LANES, LANES), 1) + j * LANES
        spread = (h == c // HEADDIM).astype(bf16)
        wide = jnp.dot(three[2].astype(bf16), spread, preferred_element_type=f32)
        skip[:, j * LANES : (j + 1) * LANES] = wide[0:1, :]
    shift = 3 * HEADS
    for out, begin, width in ((norm_gain, at, D), (gate_gain, at + D // LANES, INNER)):
        for j in range(width // LANES):
            x = pltpu.roll(flat[begin + j : begin + j + 1, :], LANES - shift, 1)
            y = pltpu.roll(flat[begin + j + 1 : begin + j + 2, :], LANES - shift, 1)
            out[:, j * LANES : (j + 1) * LANES] = jnp.where(lane[0:1] < LANES - shift, x, y)


def unpack_weights(table, parts, w_in, w_out, vectors, held, flat, flat_out, tile, sem):
    pairs, at = [], 0
    for part in parts:
        pairs.append((part, held.at[pl.ds(at, part.shape[0])]))
        at += part.shape[0]
    copy_all(pairs, sem)
    spread_blocks(table, 0, held, flat, MID0, 0)
    spread_blocks(table, MID1, held, flat, NBLK - MID1, MID0 * BROWS)
    spread_blocks(table, MID0, held, flat_out, N1, HEAD_ROWS)
    flat_out[0:HEAD_ROWS, :] = flat[IN_ROWS : IN_ROWS + HEAD_ROWS, :]
    flat_out[OUT_ROWS - TAIL_ROWS :, :] = flat[MID0 * BROWS : MID0 * BROWS + TAIL_ROWS, :]
    unpack_vectors(flat, *vectors)
    rows = 128

    def out_step(i, carry):
        at = pl.multiple_of(i * rows, rows)
        for j in range(OUT_TILES):
            x = flat_out[pl.ds(at * OUT_TILES + j, rows, stride=OUT_TILES), :]
            w_out[pl.ds(at, rows), j * LANES : (j + 1) * LANES] = x.astype(jnp.bfloat16)
        return carry

    lax.fori_loop(0, INNER // rows, out_step, 0)
    lane = lax.broadcasted_iota(jnp.int32, (GROUPS, LANES), 1)

    def columns(j):
        for rho in range(GROUP):
            c, s = row_start(rho)
            x = flat[pl.ds(c + j, GROUPS, stride=GROUP_ROWS), :]
            if s:
                y = flat[pl.ds(c + j + 1, GROUPS, stride=GROUP_ROWS), :]
                x = jnp.where(
                    lane < LANES - s,
                    pltpu.roll(x, LANES - s, 1),
                    pltpu.roll(y, LANES - s, 1),
                )
            tile[pl.ds(rho, GROUPS, stride=GROUP), :] = x

    def step(j, carry):
        columns(j)
        w_in[:, pl.ds(pl.multiple_of(j * LANES, LANES), LANES)] = tile[...].astype(jnp.bfloat16)
        return carry

    lax.fori_loop(0, COL_TILES - 1, step, 0)
    columns(COL_TILES - 1)
    last = (COL_TILES - 1) * LANES
    inside = lax.broadcasted_iota(jnp.int32, (D, LANES), 1) < PROJ - last
    w_in[:, last:] = jnp.where(inside, tile[...], 0.0).astype(jnp.bfloat16)


def unpack_scratch(held, count):
    return [
        pltpu.VMEM((held, BROWS, LANES), jnp.bfloat16),
        pltpu.VMEM((F0_ROWS, LANES), jnp.float32),
        pltpu.VMEM((OUT_ROWS, LANES), jnp.float32),
        pltpu.VMEM((D, LANES), jnp.float32),
        pltpu.SemaphoreType.DMA((count,)),
    ]


def permute_units(table, flat, count, first_row, staged):
    many = 16

    def step(i, carry):
        for u in range(many):
            at = pl.multiple_of(first_row + (i * many + u) * UNIT, UNIT)
            staged[table[i * many + u]] = flat[pl.ds(at, UNIT), :]
        return carry

    lax.fori_loop(0, count // many, step, 0)
    for i in range(count // many * many, count):
        staged[table[i]] = flat[first_row + i * UNIT : first_row + (i + 1) * UNIT, :]


def pack_in_kernel(table, hidden, grad, head, *refs):
    outs, (turned, tiles, flat, staged, sem) = refs[:-5], refs[-5:]
    turned[...] = hidden[...].T
    lane = lax.broadcasted_iota(jnp.int32, (GROUPS, LANES), 1)

    def product(p, count):
        at = p * 2 * LANES
        at = at if isinstance(at, int) else pl.multiple_of(at, 2 * LANES)
        return jnp.dot(
            turned[...], grad[:, pl.ds(at, count * LANES)], preferred_element_type=jnp.float32
        )

    def put(p, value):
        for k in range(value.shape[1] // LANES):
            at = (p * 2 + k) * D
            at = at if isinstance(at, int) else pl.multiple_of(at, D)
            tiles[pl.ds(at, D), :] = value[:, k * LANES : (k + 1) * LANES]

    def load(rho, j):
        return tiles[pl.ds(j * D + rho, GROUPS, stride=GROUP), :]

    def whole(rho, i):
        first = -(-PROJ * rho // LANES)
        col0 = first * LANES - PROJ * rho
        x = load(rho, i)
        if col0:
            x = jnp.where(
                lane < LANES - col0,
                pltpu.roll(x, LANES - col0, 1),
                pltpu.roll(load(rho, i + 1), LANES - col0, 1),
            )
        flat[pl.ds(first + i, GROUPS, stride=GROUP_ROWS), :] = x

    put(0, product(0, 2))
    put(1, product(1, 2))
    pairs = COL_TILES // 2

    def step(p, carry):
        for i in range(2):
            for rho in range(GROUP):
                whole(rho, p * 2 + i)
        put(p + 2, product(p + 2, 2))
        return carry

    lax.fori_loop(0, pairs - 2, step, 0)
    put(pairs, product(pairs, COL_TILES % 2))
    for rho in range(GROUP):
        first = -(-PROJ * rho // LANES)
        col0 = first * LANES - PROJ * rho
        full = (PROJ - col0) // LANES
        for i in range((pairs - 2) * 2, full):
            whole(rho, i)
        left = PROJ - col0 - full * LANES
        if left:
            begin = col0 + full * LANES
            j, s = begin // LANES, begin % LANES
            x = pltpu.roll(load(rho, j), LANES - s, 1) if s else load(rho, j)
            if s + left > LANES:
                x = jnp.where(lane < LANES - s, x, pltpu.roll(load(rho, j + 1), LANES - s, 1))
            y = pltpu.roll(load(rho + 1, 0), left, 1)
            flat[pl.ds(first + full, GROUPS, stride=GROUP_ROWS), :] = jnp.where(lane < left, x, y)
    flat[IN_ROWS : IN_ROWS + HEAD_ROWS, :] = head[...]
    permute_units(table, flat, MID0 * UNITS, 0, staged)
    copies, at = [], 0
    for out in outs:
        copies.append((staged.at[pl.ds(at, out.shape[0])], out))
        at += out.shape[0]
    copy_all(copies, sem)


def pack_in(table, hidden, grad, head, sizes):
    return pl.pallas_call(
        pack_in_kernel,
        out_shape=tuple(shape((n, UNIT, LANES), jnp.float32) for n in sizes),
        in_specs=[SMEM, VMEM, VMEM, VMEM],
        out_specs=(ANY,) * len(sizes),
        scratch_shapes=[
            pltpu.VMEM((D, hidden.shape[0]), jnp.bfloat16),
            pltpu.VMEM((COL_TILES * D, LANES), jnp.float32),
            pltpu.VMEM((MID0 * BROWS, LANES), jnp.float32),
            pltpu.VMEM((sum(sizes), UNIT, LANES), jnp.float32),
            pltpu.SemaphoreType.DMA((len(sizes),)),
        ],
        compiler_params=params(),
        cost_estimate=cost(20),
    )(table, hidden, grad, head)


def pack_out_kernel(
    table, mixed_out, grad, local, keep, send, head, tail, turned, flat, out, sem, *, slots
):
    rows = 256

    def step(i, carry):
        at = pl.multiple_of(i * rows, rows)
        turned[...] = mixed_out[:, pl.ds(at, rows)].T
        product = jnp.dot(turned[...], grad[...], preferred_element_type=jnp.float32)
        for j in range(OUT_TILES):
            flat[pl.ds(at * OUT_TILES + j, rows, stride=OUT_TILES), :] = product[
                :, j * LANES : (j + 1) * LANES
            ]
        return carry

    lax.fori_loop(0, INNER // rows, step, 0)
    head[...] = flat[0:HEAD_ROWS, :]
    tail[...] = flat[OUT_ROWS - TAIL_ROWS : OUT_ROWS, :]
    permute_units(table, flat, N1 * UNITS, HEAD_ROWS, out)

    def add_local(i, carry):
        out[i * slots + slots - 1] = local[...]
        return carry

    lax.fori_loop(0, out.shape[0] // slots, add_local, 0)
    half = keep.shape[0]
    copy_all([(out.at[pl.ds(0, half)], keep), (out.at[pl.ds(half, half)], send)], sem)


def pack_out(table, mixed_out, grad, local, devices, slots):
    return pl.pallas_call(
        partial(pack_out_kernel, slots=slots),
        out_shape=(
            shape((devices * slots // 2, UNIT, LANES), jnp.float32),
            shape((devices * slots // 2, UNIT, LANES), jnp.float32),
            shape((HEAD_ROWS, LANES), jnp.float32),
            shape((TAIL_ROWS, LANES), jnp.float32),
        ),
        in_specs=[SMEM, VMEM, VMEM, VMEM],
        out_specs=(ANY, ANY, VMEM, VMEM),
        scratch_shapes=[
            pltpu.VMEM((256, mixed_out.shape[0]), jnp.bfloat16),
            pltpu.VMEM((OUT_ROWS, LANES), jnp.float32),
            pltpu.VMEM((devices * slots, UNIT, LANES), jnp.float32),
            pltpu.SemaphoreType.DMA((2,)),
        ],
        compiler_params=params(),
    )(table, mixed_out, grad, local)


def adam_kernel(
    table, row_block, row_used, scale, got, late, master, first, second,
    o_first, o_second, o_master, flat, held, limit, used,
):
    capacity = master.shape[0]

    def step(i, carry):
        for u in range(UNITS):
            at = table[i * UNITS + u]
            rows = pl.ds(pl.multiple_of(i * BROWS + u * UNIT, UNIT), UNIT)
            flat[rows, :] = held[at]
        limit[pl.ds(i, 1), :] = jnp.full((1, LANES), END_OUT - row_block[i] * PBLOCK, jnp.int32)
        used[pl.ds(i, 1), :] = jnp.full((1, LANES), row_used[i], jnp.int32)
        return carry

    held[0 : got.shape[0]] = got[...]
    held[got.shape[0] :] = late[...]
    lax.fori_loop(0, capacity, step, 0)
    lane = lax.broadcasted_iota(jnp.int32, (capacity, LANES), 1)
    divisor = scale[0]
    for j in range(BROWS):
        cols = slice(j * LANES, (j + 1) * LANES)
        grad = jnp.where(used[...] > 0, flat[pl.ds(j, capacity, stride=BROWS), :], 0.0) / divisor
        matrix = lane + j * LANES < limit[...]
        weights = master[:, cols]
        new_first = BETA_ONE * first[:, cols] + (1.0 - BETA_ONE) * grad
        new_second = BETA_TWO * second[:, cols] + (1.0 - BETA_TWO) * grad * grad
        normal = (
            new_first
            / (1.0 - BETA_ONE**STEP)
            / (jnp.sqrt(new_second / (1.0 - BETA_TWO**STEP)) + ADAM_EPS)
        )
        rate = jnp.where(matrix, MATRIX_RATE, VECTOR_RATE)
        decay = jnp.where(matrix, WEIGHT_DECAY, 0.0)
        o_first[:, cols] = new_first
        o_second[:, cols] = new_second
        o_master[:, cols] = weights - rate * (normal + decay * weights)


def adam(table, row_block, row_used, divisor, got, late, master, first, second):
    capacity = master.shape[0]
    return pl.pallas_call(
        adam_kernel,
        out_shape=(shape(master.shape, jnp.float32),) * 3,
        in_specs=[SMEM] * 4 + [VMEM] * 5,
        out_specs=(VMEM,) * 3,
        scratch_shapes=[
            pltpu.VMEM((capacity * BROWS, LANES), jnp.float32),
            pltpu.VMEM((got.shape[0] + late.shape[0], UNIT, LANES), jnp.float32),
            pltpu.VMEM((capacity, LANES), jnp.int32),
            pltpu.VMEM((capacity, LANES), jnp.int32),
        ],
        compiler_params=params(),
    )(
        table, row_block, row_used.astype(jnp.int32), divisor.reshape(1), got, late, master, first, second
    )


def doubled(values, step):
    return jnp.concatenate([values, exchange(values, step)], axis=0)


def gather_steps(values, order):
    for step in order[:0:-1]:
        values = doubled(values, step)
    return values, exchange(values, order[0])


def reduce_step(kept, got, step, extra=None):
    half = kept.shape[0] // 2
    given = kept[half:] + got[half:]
    if extra is None:
        return kept[:half] + got[:half], exchange(given, step)
    arrived = exchange(jnp.concatenate([given, extra]), step)
    return kept[:half] + got[:half], arrived[:half], extra + arrived[half:]


CHUNK = 128
PAIRS = HEADS // 2
MIXW = INNER + 2 * NSTATE
DT_AT = INNER + CONVCH
F32 = jnp.float32
BF16 = jnp.bfloat16
NN = (((1,), (0,)), ((), ()))
NT = (((1,), (1,)), ((), ()))


def dot(a, b, dims=NN):
    return lax.dot_general(a, b, dims, preferred_element_type=F32)


def split(v):
    high = v.astype(BF16)
    return high, (v - high.astype(F32)).astype(BF16)


def dot3(a, b, dims=NN):
    ah, al = a
    bh, bl = b
    return dot(ah, bh, dims) + (dot(ah, bl, dims) + dot(al, bh, dims))


def heads_gather():
    return jnp.asarray(np.repeat(np.eye(HEADS, LANES, dtype=np.float32), HEADDIM, axis=0), BF16)


def three_parts(v):
    high = v.astype(BF16).astype(F32)
    rest = v - high
    middle = rest.astype(BF16).astype(F32)
    low = rest - middle
    return (high + pltpu.roll(middle, 32, 1) + pltpu.roll(low, 64, 1)).astype(BF16)


def triangle_sum(tri, v):
    parts = dot(tri, three_parts(v))
    lane = lax.broadcasted_iota(jnp.int32, parts.shape, 1)
    total = parts + pltpu.roll(parts, LANES - 32, 1) + pltpu.roll(parts, LANES - 64, 1)
    return jnp.where(lane < HEADS, total, 0.0)


def chunk_decays(dt, dt_bias, a_log):
    lane = lax.broadcasted_iota(jnp.int32, (CHUNK, LANES), 1)
    row = lax.broadcasted_iota(jnp.int32, (CHUNK, LANES), 0)
    shifted = dt + dt_bias
    delta = jnp.where(
        lane < HEADS, jnp.maximum(shifted, 0.0) + jnp.log1p(jnp.exp(-jnp.abs(shifted))), 0.0
    )
    rate = -jnp.exp(a_log)
    lower = (row >= lane).astype(BF16)
    cum = triangle_sum(lower, delta * rate)
    last = cum[CHUNK - 1 : CHUNK, :]
    return shifted, delta, rate, cum, last


def pair_mask():
    lane = lax.broadcasted_iota(jnp.int32, (CHUNK, LANES), 1)
    low = (lane < HEADDIM).astype(F32)
    return low.astype(BF16), (1.0 - low).astype(BF16)


QUADS = HEADS // 4
QWIDTH = 4 * HEADDIM


def sigmoid(v):
    return 0.5 * jnp.tanh(0.5 * v) + 0.5


def silu(v):
    return v * sigmoid(v)


def side_by_side(v):
    high, low = split(v)
    return jnp.concatenate([high, low], axis=1), high


def dot_parts(a, b):
    ahl, ah = a
    bh, bl = b
    return dot(ahl, jnp.concatenate([bh, bh], axis=0)) + dot(ah, bl)


def dot_turned(a, b):
    ah, al = a
    bh, bl = b
    both = dot(ah, jnp.concatenate([bh, bl], axis=0), NT)
    n = bh.shape[0]
    return both[:, :n] + both[:, n:] + dot(al, bh, NT)


def widen(delta, cum, quad):
    lane = lax.broadcasted_iota(jnp.int32, (CHUNK, LANES), 1)
    over = lambda v, h: jnp.broadcast_to(v[:, h : h + 1], (CHUNK, LANES))
    first = 4 * quad
    columns = [over(cum, first + k) for k in range(4)]
    rates = [over(delta, first + k) for k in range(4)]
    pair = lambda vs: jnp.concatenate(
        [jnp.where(lane < HEADDIM, vs[0], vs[1]), jnp.where(lane < HEADDIM, vs[2], vs[3])], axis=1
    )
    return pair(rates), pair(columns), columns


def pair_rows(parts, j, low, high):
    cols = slice(j * LANES, (j + 1) * LANES)
    return [jnp.concatenate([p[:, cols] * low, p[:, cols] * high], axis=0) for p in parts]


def scan_chunk(mixed, dt, dt_bias, a_log, skip, state, put):
    _, delta, _, cum, last = chunk_decays(dt, dt_bias, a_log)
    lane = lax.broadcasted_iota(jnp.int32, (CHUNK, LANES), 1)
    row = lax.broadcasted_iota(jnp.int32, (CHUNK, LANES), 0)
    bias = jnp.where(row >= lane, 0.0, -1e30)
    cum_t = cum.T
    inputs_b = mixed[:, INNER : INNER + NSTATE]
    readout = mixed[:, INNER + NSTATE :]
    affinity = dot3(split(readout), split(inputs_b), NT)
    readout_parts = side_by_side(readout)
    b_parts = side_by_side(inputs_b.T)
    low, high = pair_mask()
    for quad in range(QUADS):
        cols = slice(quad * QWIDTH, (quad + 1) * QWIDTH)
        wide_delta, wide_cum, columns = widen(delta, cum, quad)
        values = mixed[:, cols]
        scaled = values * wide_delta
        parts = split(scaled)
        outs = []
        for j in range(2):
            right_h, right_l = pair_rows(parts, j, low, high)
            left = []
            for k in range(2):
                h = 4 * quad + 2 * j + k
                within = jnp.exp(columns[2 * j + k] - cum_t[h : h + 1, :] + bias)
                left.append(split(affinity * within))
            left_h = jnp.concatenate([left[0][0], left[1][0]], axis=1)
            left_l = jnp.concatenate([left[0][1], left[1][1]], axis=1)
            both = dot(left_h, jnp.concatenate([right_h, right_l], axis=1))
            outs.append(both[:, :LANES] + both[:, LANES:] + dot(left_l, right_h))
        carried = state[:, cols]
        grown = jnp.exp(wide_cum)
        out = jnp.concatenate(outs, axis=1) + dot_parts(readout_parts, split(carried)) * grown
        tail = jnp.exp(wide_cum[CHUNK - 1 :] - wide_cum)
        state[:, cols] = carried * grown[CHUNK - 1 :] + dot_parts(b_parts, split(scaled * tail))
        put(quad, out + skip[:, cols] * values)


FORWARD_ROWS = 2 * CHUNK


def forward_kernel(table, tokens, *refs, count):
    parts, refs = refs[:count], refs[count:]
    (w_in_kept, w_out_kept, conv_weight, conv_bias, dt_bias, a_log, skip, norm_gain, gain,
     hidden, gate, conv_in, dt, ssm, mixed_out, states) = refs[:16]
    w_in, w_out, state, before, mixed, shift, out_sem, *scratch = refs[16:]
    keep = [
        pltpu.make_async_copy(w_in, w_in_kept, out_sem.at[0]),
        pltpu.make_async_copy(w_out, w_out_kept, out_sem.at[1]),
    ]

    @pl.when(pl.program_id(0) == 0)
    def _():
        vectors = (conv_weight, conv_bias, dt_bias, a_log, skip, norm_gain, gain)
        unpack_weights(table, parts, w_in, w_out, vectors, *scratch)
        for copy in keep:
            copy.start()
        state[...] = jnp.zeros_like(state)
        before[...] = jnp.zeros_like(before)

    x = tokens[...].astype(F32)
    inverse = lax.rsqrt(jnp.mean(x * x, axis=1, keepdims=True) + NORM_EPS)
    h = (x * inverse * norm_gain[...]).astype(BF16)
    hidden[...] = h
    dt[...] = dot(h, w_in[:, DT_AT:])
    wide = 2 * LANES
    for tile in range(CONVCH // wide):
        at = tile * wide
        product = dot(h, w_in[:, INNER + at : INNER + at + wide])
        conv_in[:, at : at + wide] = product
        for half in range(2):
            cols = slice(at + half * LANES, at + (half + 1) * LANES)
            rows = product[:, half * LANES : (half + 1) * LANES]
            earlier = before[:, cols]
            terms = moved_down(shift.at[tile * 2 + half], rows, earlier) + [rows]
            before[:, cols] = rows[FORWARD_ROWS - 8 :]
            mixed[:, cols] = silu(conv_sum(terms, conv_weight[:, cols], conv_bias[:, cols]))
    for tile in range(INNER // wide):
        cols = slice(tile * wide, (tile + 1) * wide)
        gate[:, cols] = dot(h, w_in[:, cols])
    for sub in range(FORWARD_ROWS // CHUNK):
        rows = slice(sub * CHUNK, (sub + 1) * CHUNK)
        states[sub] = state[...]
        squares = [jnp.zeros((CHUNK, LANES), F32)]

        def put(quad, out, rows=rows, squares=squares):
            cols = slice(quad * QWIDTH, (quad + 1) * QWIDTH)
            ssm[rows, cols] = out
            gated = out * silu(gate[rows, cols])
            first, second = gated[:, :LANES], gated[:, LANES:]
            squares[0] = squares[0] + first * first + second * second

        scan_chunk(
            mixed[rows, :], dt[rows, :], dt_bias[...], a_log[...], skip, state, put
        )
        rho = lax.rsqrt(jnp.sum(squares[0], axis=1, keepdims=True) * (1.0 / INNER) + NORM_EPS)
        for j in range(PAIRS):
            cols = slice(j * LANES, (j + 1) * LANES)
            gated = ssm[rows, cols] * silu(gate[rows, cols])
            mixed_out[rows, cols] = (gated * rho * gain[:, cols]).astype(BF16)

    @pl.when(pl.program_id(0) == pl.num_programs(0) - 1)
    def _():
        for copy in keep:
            copy.wait()


def forward(table, tokens, parts):
    length = tokens.shape[0]
    by_row = lambda width: pl.BlockSpec((FORWARD_ROWS, width), lambda i: (i, 0))
    per_step = FORWARD_ROWS // CHUNK
    vectors = [(KCONV, CONVCH), (1, CONVCH), (1, LANES), (1, LANES), (1, INNER), (1, D), (1, INNER)]
    return pl.pallas_call(
        partial(forward_kernel, count=len(parts)),
        grid=(length // FORWARD_ROWS,),
        out_shape=[shape((D, WIDE), BF16), shape((INNER, D), BF16)]
        + [shape(v, F32) for v in vectors]
        + [
            shape((length, D), BF16),
            shape((length, INNER), F32),
            shape((length, MIXW), F32),
            shape((length, LANES), F32),
            shape((length, INNER), F32),
            shape((length, INNER), BF16),
            shape((length // CHUNK, NSTATE, INNER), F32),
        ],
        in_specs=[SMEM, by_row(D)] + [ANY] * len(parts),
        out_specs=[ANY, ANY]
        + [pl.BlockSpec(v, lambda i: (0, 0)) for v in vectors]
        + [
            by_row(D),
            by_row(INNER),
            by_row(MIXW),
            by_row(LANES),
            by_row(INNER),
            by_row(INNER),
            pl.BlockSpec((per_step, NSTATE, INNER), lambda i: (i, 0, 0)),
        ],
        scratch_shapes=[
            pltpu.VMEM((D, WIDE), BF16),
            pltpu.VMEM((INNER, D), BF16),
            pltpu.VMEM((NSTATE, INNER), F32),
            pltpu.VMEM((8, MIXW), F32),
            pltpu.VMEM((FORWARD_ROWS, MIXW), F32),
            pltpu.VMEM((MIXW // LANES, FORWARD_ROWS + 8, LANES), F32),
            pltpu.SemaphoreType.DMA((2,)),
        ]
        + unpack_scratch(sum(part.shape[0] for part in parts), len(parts)),
        compiler_params=params(),
        cost_estimate=cost(50),
    )(table, tokens, *parts)


def eights(v):
    return jnp.sum(v.reshape(v.shape[0] // 8, 8, v.shape[1]), axis=0)


def backward_kernel(
    conv_in, earlier, dt, ssm, grad, grad_gate, states, conv_weight, conv_bias, dt_bias, a_log, skip,
    gather, grad_low, sums, skip_sums, conv_sums,
    grad_state, to_sum, mixed, slope, grad_mixed, following, shift,
):
    @pl.when(pl.program_id(0) == 0)
    def _():
        grad_state[...] = jnp.zeros_like(grad_state)
        sums[...] = jnp.zeros_like(sums)
        skip_sums[...] = jnp.zeros_like(skip_sums)
        conv_sums[...] = jnp.zeros_like(conv_sums)
        following[...] = jnp.zeros_like(following)

    begins = pl.program_id(0) == pl.num_programs(0) - 1

    for tile in range(MIXW // LANES):
        cols = slice(tile * LANES, (tile + 1) * LANES)
        rows = conv_in[:, cols]
        before = jnp.where(begins, 0.0, earlier[:, cols])
        terms = moved_down(shift.at[tile], rows, before) + [rows]
        value = conv_sum(terms, conv_weight[:, cols], conv_bias[:, cols])
        sig = sigmoid(value)
        mixed[:, cols] = value * sig
        slope[:, cols] = sig * (1.0 + value * (1.0 - sig))

    shifted, delta, rate, cum, last = chunk_decays(dt[...], dt_bias[...], a_log[...])
    lane = lax.broadcasted_iota(jnp.int32, (CHUNK, LANES), 1)
    row = lax.broadcasted_iota(jnp.int32, (CHUNK, LANES), 0)
    bias = jnp.where(lane >= row, 0.0, -1e30)
    heads = lane < HEADS
    cum_t = cum.T
    inputs_b = mixed[:, INNER : INNER + NSTATE]
    readout = mixed[:, INNER + NSTATE :]
    b_parts, c_parts = split(inputs_b), split(readout)
    b_wide = side_by_side(inputs_b)
    c_turned = side_by_side(readout.T)
    affinity = dot3(b_parts, c_parts, NT)
    low, high = pair_mask()
    grad_affinity = jnp.zeros((CHUNK, CHUNK), F32)
    grad_b = jnp.zeros((CHUNK, NSTATE), F32)
    grad_c = jnp.zeros((CHUNK, NSTATE), F32)
    last_row = lax.broadcasted_iota(jnp.int32, (CHUNK, QWIDTH), 0) == CHUNK - 1
    for quad in range(QUADS):
        cols = slice(quad * QWIDTH, (quad + 1) * QWIDTH)
        wide_delta, wide_cum, columns = widen(delta, cum, quad)
        grown = jnp.exp(wide_cum)
        tail = jnp.exp(wide_cum[CHUNK - 1 :] - wide_cum)
        end = grown[CHUNK - 1 :]
        values = mixed[:, cols]
        pulled = grad[:, cols]
        scaled = values * wide_delta
        x_parts, p_parts = split(scaled), split(pulled)
        outs = []
        for j in range(2):
            half = slice(j * LANES, (j + 1) * LANES)
            xh, xl = x_parts[0][:, half], x_parts[1][:, half]
            right_h, right_l = pair_rows(p_parts, j, low, high)
            pull = dot(
                jnp.concatenate([xh, xl], axis=1),
                jnp.concatenate([right_h, right_h], axis=1),
                NT,
            ) + dot(xh, right_l, NT)
            kernels = []
            for k in range(2):
                h = 4 * quad + 2 * j + k
                within = jnp.exp(cum_t[h : h + 1, :] - columns[2 * j + k] + bias)
                kernels.append(split(affinity * within))
                grad_affinity = grad_affinity + within * pull[:, k * CHUNK : (k + 1) * CHUNK]
            kernel_h = jnp.concatenate([kernels[0][0], kernels[1][0]], axis=1)
            kernel_l = jnp.concatenate([kernels[0][1], kernels[1][1]], axis=1)
            both = dot(kernel_h, jnp.concatenate([right_h, right_l], axis=1))
            outs.append(both[:, :LANES] + both[:, LANES:] + dot(kernel_l, right_h))
        late = grad_state[:, cols]
        late_parts = split(late)
        early = states[0, :, cols]
        from_state = dot_parts(b_wide, late_parts) * tail
        grad_scaled = jnp.concatenate(outs, axis=1) + from_state
        pulled_cum = split(pulled * grown)
        grad_c = grad_c + dot_turned(pulled_cum, split(early))
        grad_b = grad_b + dot_turned(split(scaled * tail), late_parts)
        grad_state[:, cols] = late * end + dot_parts(c_turned, pulled_cum)
        grad_mixed[:, cols] = grad_scaled * wide_delta + skip[:, cols] * pulled
        skip_sums[:, cols] += jnp.sum(pulled * values, axis=0, keepdims=True)
        to_sum[:CHUNK, cols] = grad_scaled * values
        inner = pulled * (ssm[:, cols] - skip[:, cols] * values) - scaled * grad_scaled
        extra = jnp.sum(scaled * from_state, axis=0, keepdims=True) + end * jnp.sum(
            late * early, axis=0, keepdims=True
        )
        to_sum[CHUNK:, cols] = inner + jnp.where(last_row, extra, 0.0)
    ga_parts = split(grad_affinity)
    grad_mixed[:, INNER : INNER + NSTATE] = grad_b + dot3(ga_parts, c_parts)
    grad_mixed[:, INNER + NSTATE :] = grad_c + dot3(split(grad_affinity.T), b_parts)


    def by_head(v):
        high, low = split(v)
        return dot(high, gather[...]) + dot(low, gather[...])

    direct, grad_cum = by_head(to_sum[:CHUNK, :]), by_head(to_sum[CHUNK:, :])
    upper = (lane >= row).astype(BF16)
    after = triangle_sum(upper, grad_cum)
    grad_delta = direct + rate * after
    grad_raw = jnp.where(heads, grad_delta * sigmoid(shifted), 0.0)
    grad_low[:, DT_AT:] = grad_raw.astype(BF16)
    sums[0:1, :] += jnp.sum(grad_raw, axis=0, keepdims=True)
    sums[1:2, :] += rate * jnp.sum(delta * after, axis=0, keepdims=True)
    grad_low[:, :INNER] = grad_gate[...]
    for tile in range(MIXW // LANES):
        cols = slice(tile * LANES, (tile + 1) * LANES)
        w = conv_weight[:, cols]
        g = grad_mixed[:, cols] * slope[:, cols]
        rows = conv_in[:, cols]
        later = following[:, cols]
        total = jnp.zeros((CHUNK, LANES), F32)
        arriving = moved_up(shift.at[tile], g, later) + [g]
        for k in range(KCONV):
            conv_sums[8 * k : 8 * k + 8, cols] += eights(rows * arriving[k])
            total = total + arriving[k] * w[k : k + 1]
        conv_sums[8 * KCONV :, cols] += eights(g)
        following[:, cols] = g[:8]
        grad_low[:, INNER + tile * LANES : INNER + (tile + 1) * LANES] = total.astype(BF16)


def backward(
    conv_in, dt, ssm, grad, grad_gate, states, conv_weight, conv_bias, dt_bias, a_log, skip, gather
):
    length = conv_in.shape[0]
    chunks = length // CHUNK
    whole = lambda v: pl.BlockSpec(v.shape, lambda i: (0,) * v.ndim)
    by_row = lambda width: pl.BlockSpec((CHUNK, width), lambda i: (chunks - 1 - i, 0))
    return pl.pallas_call(
        backward_kernel,
        grid=(chunks,),
        out_shape=(
            shape((length, WIDE), BF16),
            shape((8, LANES), F32),
            shape((1, INNER), F32),
            shape((8 * (KCONV + 1), MIXW), F32),
        ),
        in_specs=[
            by_row(MIXW),
            pl.BlockSpec((8, MIXW), lambda i: (jnp.maximum((chunks - 1 - i) * (CHUNK // 8) - 1, 0), 0)),
            by_row(LANES),
            by_row(INNER),
            by_row(INNER),
            by_row(INNER),
            pl.BlockSpec((1, NSTATE, INNER), lambda i: (chunks - 1 - i, 0, 0)),
        ]
        + [whole(v) for v in (conv_weight, conv_bias, dt_bias, a_log, skip, gather)],
        out_specs=(
            by_row(WIDE),
            pl.BlockSpec((8, LANES), lambda i: (0, 0)),
            pl.BlockSpec((1, INNER), lambda i: (0, 0)),
            pl.BlockSpec((8 * (KCONV + 1), MIXW), lambda i: (0, 0)),
        ),
        scratch_shapes=[pltpu.VMEM((NSTATE, INNER), F32)]
        + [pltpu.VMEM((2 * CHUNK, INNER), F32)]
        + [pltpu.VMEM((CHUNK, MIXW), F32)] * 3
        + [pltpu.VMEM((8, MIXW), F32), pltpu.VMEM((MIXW // LANES, CHUNK + 8, LANES), F32)],
        compiler_params=params(),
        cost_estimate=cost(43),
    )(
        conv_in, conv_in, dt, ssm, grad, grad_gate, states,
        conv_weight, conv_bias, dt_bias, a_log, skip, gather,
    )


def moved_down(scratch, v, before):
    rows = v.shape[0]
    scratch[0:8, :] = before
    scratch[8 : 8 + rows, :] = v
    return [scratch[8 - by : 8 - by + rows, :] for by in range(KCONV - 1, 0, -1)]


def moved_up(scratch, v, behind):
    rows = v.shape[0]
    scratch[0:rows, :] = v
    scratch[rows : rows + 8, :] = behind
    return [scratch[by : by + rows, :] for by in range(KCONV - 1, 0, -1)]


def conv_sum(terms, weight, bias):
    total = bias + terms[KCONV - 1] * weight[KCONV - 1 : KCONV]
    for k in range(KCONV - 1):
        total = total + terms[k] * weight[k : k + 1]
    return total


def loss_kernel(
    limit, mixed_out, w_out, tokens, teacher, mask, block_out, grad_result, grad_branch, error
):
    step = pl.program_id(0)

    @pl.when(step == 0)
    def _():
        error[...] = jnp.zeros_like(error)

    rows = tokens.shape[0]
    result = tokens[...].astype(F32) + dot(mixed_out[...], w_out[...])
    position = step * rows + lax.broadcasted_iota(jnp.int32, (rows, 1), 0)
    valid = (position < limit[0]).astype(F32)
    turned = jnp.broadcast_to(mask[...].astype(F32), (LANES, rows)).T
    weight = valid * turned[:, 0:1]
    block_out[...] = (result * valid).astype(BF16)
    misfit = result - teacher[...].astype(F32)
    pulled = 2.0 * weight * misfit
    grad_result[...] = pulled
    errors = jnp.sum(0.5 * pulled * misfit, axis=0, keepdims=True)
    for j in range(D // LANES):
        error[j : j + 1, :] += errors[:, j * LANES : (j + 1) * LANES]
    error[D // LANES : D // LANES + 1, :] += jnp.sum(valid * turned, axis=0, keepdims=True)
    grad_branch[...] = pulled.astype(BF16)


def loss_part(limit, mixed_out, w_out, tokens, teacher, mask):
    length = tokens.shape[0]
    rows = 256
    by_row = lambda width: pl.BlockSpec((rows, width), lambda i: (i, 0))
    return pl.pallas_call(
        loss_kernel,
        grid=(length // rows,),
        out_shape=(
            shape((length, D), BF16),
            shape((length, D), F32),
            shape((length, D), BF16),
            shape((8, LANES), F32),
        ),
        in_specs=[
            SMEM,
            by_row(INNER),
            pl.BlockSpec(w_out.shape, lambda i: (0, 0)),
            by_row(D),
            by_row(D),
            pl.BlockSpec((1, rows), lambda i: (0, i)),
        ],
        out_specs=(by_row(D), by_row(D), by_row(D), pl.BlockSpec((8, LANES), lambda i: (0, 0))),
        compiler_params=params(),
        cost_estimate=cost(8),
    )(limit, mixed_out, w_out, tokens, teacher, mask)


def gate_kernel(grad_branch, w_out, ssm, gate, gain, grad_ssm, grad_gate, gain_sums):
    @pl.when(pl.program_id(0) == 0)
    def _():
        gain_sums[...] = jnp.zeros_like(gain_sums)

    grad_mixed = dot(grad_branch[...], w_out[...], NT)
    g = gate[...]
    sig = sigmoid(g)
    act = g * sig
    inner = ssm[...]
    gated = inner * act
    rho = lax.rsqrt(jnp.mean(gated * gated, axis=1, keepdims=True) + NORM_EPS)
    unit = gated * rho
    gain_sums[...] += jnp.sum(unit * grad_mixed, axis=0, keepdims=True)
    grad_unit = grad_mixed * gain[...]
    share = jnp.mean(grad_unit * unit, axis=1, keepdims=True)
    grad_gated = rho * (grad_unit - unit * share)
    grad_ssm[...] = grad_gated * act
    grad_gate[...] = (grad_gated * inner * (sig * (1.0 + g * (1.0 - sig)))).astype(BF16)


def gate_part(grad_branch, w_out, ssm, gate, gain):
    length = ssm.shape[0]
    rows = 256
    by_row = lambda width: pl.BlockSpec((rows, width), lambda i: (i, 0))
    whole = lambda v: pl.BlockSpec(v.shape, lambda i: (0,) * v.ndim)
    return pl.pallas_call(
        gate_kernel,
        grid=(length // rows,),
        out_shape=(shape((length, INNER), F32), shape((length, INNER), BF16), shape((1, INNER), F32)),
        in_specs=[by_row(D), whole(w_out), by_row(INNER), by_row(INNER), whole(gain)],
        out_specs=(by_row(INNER), by_row(INNER), pl.BlockSpec((1, INNER), lambda i: (0, 0))),
        compiler_params=params(),
        cost_estimate=cost(12),
    )(grad_branch, w_out, ssm, gate, gain)


def input_kernel(grad_low, w_in, tokens, norm_gain, grad_result, out, sums):
    @pl.when(pl.program_id(0) == 0)
    def _():
        sums[...] = jnp.zeros_like(sums)

    x = tokens[...].astype(F32)
    inverse = lax.rsqrt(jnp.mean(x * x, axis=1, keepdims=True) + NORM_EPS)
    unit = x * inverse
    grad_hidden = dot(grad_low[...], w_in[...], NT)
    sums[...] += jnp.sum(grad_hidden * unit, axis=0, keepdims=True)
    pulled = grad_hidden * norm_gain[...]
    share = jnp.mean(pulled * unit, axis=1, keepdims=True)
    out[...] = grad_result[...] + inverse * (pulled - unit * share)


def input_backward(grad_low, w_in, tokens, norm_gain, grad_result):
    length = tokens.shape[0]
    rows = 256
    by_row = lambda width: pl.BlockSpec((rows, width), lambda i: (i, 0))
    whole = lambda v: pl.BlockSpec(v.shape, lambda i: (0,) * v.ndim)
    return pl.pallas_call(
        input_kernel,
        grid=(length // rows,),
        out_shape=(shape((length, D), F32), shape((1, D), F32)),
        in_specs=[by_row(WIDE), whole(w_in), by_row(D), whole(norm_gain), by_row(D)],
        out_specs=(by_row(D), pl.BlockSpec((1, D), lambda i: (0, 0))),
        compiler_params=params(),
        cost_estimate=cost(15),
    )(grad_low, w_in, tokens, norm_gain, grad_result)


def vector_kernel(tail, conv_sums, sums, skip_sums, norm_sums, gate_sums, gather, out, taps):
    tiles = CONVCH // LANES
    out[...] = jnp.zeros_like(out)
    out[0:TAIL_ROWS, :] = tail[...]
    for k in range(KCONV):
        for i in range(tiles):
            partial_sums = conv_sums[8 * k : 8 * k + 8, i * LANES : (i + 1) * LANES]
            taps[k * 16 + i : k * 16 + i + 1, :] = jnp.sum(partial_sums, axis=0, keepdims=True)
    row = lax.broadcasted_iota(jnp.int32, (LANES, LANES), 0)
    col = lax.broadcasted_iota(jnp.int32, (LANES, LANES), 1)
    per_tile = LANES // KCONV

    def exact(v, chosen):
        high = v.astype(BF16)
        rest = v - high.astype(F32)
        middle = rest.astype(BF16)
        low = (rest - middle.astype(F32)).astype(BF16)
        return dot(high, chosen) + (dot(middle, chosen) + dot(low, chosen))

    for q in range(KCONV):
        total = jnp.zeros((tiles, LANES), F32)
        for k in range(KCONV):
            chosen = (col == KCONV * (row % per_tile) + k) & (row // per_tile == q)
            total = total + exact(taps[k * 16 : k * 16 + tiles, :], chosen.astype(BF16))
        out[pl.ds(TAIL_ROWS + q, tiles, stride=KCONV), :] = total
    bias_at = TAIL_ROWS + tiles * KCONV
    for i in range(tiles):
        partial_sums = conv_sums[8 * KCONV :, i * LANES : (i + 1) * LANES]
        out[bias_at + i : bias_at + i + 1, :] = jnp.sum(partial_sums, axis=0, keepdims=True)
    lane = lax.broadcasted_iota(jnp.int32, (1, LANES), 1)
    skip = exact(jnp.broadcast_to(skip_sums[...], (8, INNER)), gather[...])[0:1, :]
    parts = [sums[0:1, :], sums[1:2, :], skip]
    parts = [jnp.where(lane < HEADS, v, 0.0) for v in parts]
    before = parts[0] + pltpu.roll(parts[1], HEADS, 1) + pltpu.roll(parts[2], 2 * HEADS, 1)
    at, shift = bias_at + tiles, 3 * HEADS
    for source in (norm_sums, gate_sums):
        for j in range(source.shape[1] // LANES):
            here = pltpu.roll(source[:, j * LANES : (j + 1) * LANES], shift, 1)
            out[at : at + 1, :] = jnp.where(lane < shift, before, here)
            before = here
            at += 1
    out[at : at + 1, :] = jnp.where(lane < shift, before, 0.0)


def pack_vectors(tail, conv_sums, sums, skip_sums, norm_sums, gate_sums, gather):
    return pl.pallas_call(
        vector_kernel,
        out_shape=shape(((NBLK - MID1) * BROWS, LANES), F32),
        in_specs=[VMEM] * 7,
        out_specs=VMEM,
        scratch_shapes=[pltpu.VMEM((KCONV * 16, LANES), F32)],
        compiler_params=params(),
    )(tail, conv_sums, sums, skip_sums, norm_sums, gate_sums, gather)


def body(tokens, teacher, lengths, loss_mask, owners, master, first_moment, second_moment):
    capacity = master.shape[0]
    dp, fsdp = lax.axis_size("dp"), lax.axis_size("fsdp")
    devices = dp * fsdp
    me = lax.axis_index(AXES).astype(jnp.int32)
    x_first, y_first, z_first = step_orders(dp, fsdp)
    tie = lambda *values: lax.optimization_barrier(values)

    sent = send_blocks(owners, master, devices, me)
    at_home = lax.all_to_all(sent, AXES, 0, 0, tiled=True)
    owners, tokens, loss_mask, _ = tie(owners, tokens, loss_mask, sent)
    plan = make_plan(owners, capacity, devices, me)
    streams = cut(even(plan["slots"], 3), (x_first, y_first, z_first))
    table = stream_places(plan["home"], plan["slot"], me, streams, devices)
    u0, u1 = plan["unit_slots"]
    sizes = [-(-u0 // 5)] * 4
    unit_streams = cut(sizes + [u0 - sum(sizes)], (x_first, y_first, x_first, y_first, z_first))
    unit_table = stream_places(plan["unit_home"], plan["unit_slot"], me, unit_streams, devices)
    unit_table = unit_table[:MID0].reshape(-1)
    order1 = x_first[:2] + x_first[2 + bits_of(fsdp) :] + x_first[2 : 2 + bits_of(fsdp)]
    unit_table1 = place_of(plan["unit_home"] ^ me, order1) * (u1 + 1) + plan["unit_slot"]
    unit_table1 = unit_table1[MID0:MID1].reshape(-1)
    inputs, target = tokens[0], teacher[0]
    at_home, table, received = tie(at_home, table, plan["received"])
    mine = pick_blocks(received, at_home, [size for _, size, _ in streams])
    parts = []
    for values, (_, _, order) in zip(mine, streams):
        parts += gather_steps(values, order)
    *parts, unit_table, unit_table1, back_table, row_from, row_block, row_used = tie(
        *parts, unit_table, unit_table1, plan["back"], plan["row_from"], plan["row_block"],
        plan["row_used"],
    )
    (input_weight, output_weight, conv_weight, conv_bias, dt_bias, a_log, skip, norm_gain,
     gate_gain, hidden, gate, conv_in, dt, ssm, mixed_out, states) = forward(
        table, inputs, parts
    )
    gather = heads_gather()
    block_out, grad_result, grad_branch, local = loss_part(
        lengths, mixed_out, output_weight, inputs, target, loss_mask
    )
    keep1, send1, head, tail = pack_out(
        unit_table1, mixed_out, grad_branch, local, devices, u1 + 1
    )
    grad_branch, send1 = tie(grad_branch, send1)
    got1 = exchange(send1, order1[0])
    grad_ssm, grad_gate, gain_sums = gate_part(grad_branch, output_weight, ssm, gate, gate_gain)
    grad_ssm, keep1, got1 = tie(grad_ssm, keep1, got1)
    keep1, got1 = reduce_step(keep1, got1, order1[1])
    grad_low, sums, skip_sums, conv_sums = backward(
        conv_in, dt, ssm, grad_ssm, grad_gate, states,
        conv_weight, conv_bias, dt_bias, a_log, skip, gather,
    )
    grad_low, keep1, got1 = tie(grad_low, keep1, got1)
    steps1 = order1[2:]
    for step in steps1[:1]:
        keep1, got1 = reduce_step(keep1, got1, step)
    halves = []
    for _, size, _ in unit_streams:
        halves += [devices * size // 2] * 2
    packed = list(pack_in(unit_table, hidden, grad_low, head, halves))
    packed[0], keep1, got1 = tie(packed[0], keep1, got1)
    kept = packed[::2]
    got = [exchange(v, order[0]) for v, (_, _, order) in zip(packed[1::2], unit_streams)]
    *got, grad_low, conv_sums, tail = tie(*got, grad_low, conv_sums, tail)
    for i, (_, _, order) in enumerate(unit_streams):
        kept[i], got[i] = reduce_step(kept[i], got[i], order[1])
    for step in steps1[1:2]:
        keep1, got1 = reduce_step(keep1, got1, step)
    input_grad, norm_sums = input_backward(grad_low, input_weight, inputs, norm_gain, grad_result)
    grad_vec = pack_vectors(tail, conv_sums, sums, skip_sums, norm_sums, gain_sums, gather)
    grad_vec = grad_vec.reshape((NBLK - MID1) * UNITS, UNIT, LANES)
    *got, got1, grad_vec, input_grad = tie(*got, got1, grad_vec, input_grad)
    for step in steps1[2:]:
        keep1, got1 = reduce_step(keep1, got1, step)
    for k in range(2, len(x_first)):
        for i, (_, _, order) in enumerate(unit_streams):
            if i == 0:
                kept[i], got[i], grad_vec = reduce_step(kept[i], got[i], order[k], grad_vec)
            else:
                kept[i], got[i] = reduce_step(kept[i], got[i], order[k])
    back = units_to_owners(back_table, list(zip(kept + [keep1], got + [got1])))
    back, grad_vec = tie(back, grad_vec)
    returned = lax.all_to_all(back, AXES, 0, 0, tiled=True)
    for step in x_first[:2]:
        grad_vec = grad_vec + exchange(grad_vec, step)
    local_sums = keep1[u1] + got1[u1]
    error_sum = jnp.sum(local_sums[: D // LANES])
    divisor = local_sums[D // LANES, 0] * D
    new_first, new_second, new_master = adam(
        row_from,
        row_block,
        row_used,
        divisor,
        returned,
        grad_vec,
        master,
        first_moment,
        second_moment,
    )
    mean_loss = error_sum / divisor
    return (block_out[None], input_grad[None], mean_loss, new_first, new_second, new_master)


def solution(mesh):
    return jax.shard_map(
        body,
        mesh=mesh,
        in_specs=(
            P(AXES, None, None),
            P(AXES, None, None),
            P(AXES),
            P(AXES, None),
            P(),
            P(AXES, None),
            P(AXES, None),
            P(AXES, None),
        ),
        out_specs=(
            P(AXES, None, None),
            P(AXES, None, None),
            P(),
            P(AXES, None),
            P(AXES, None),
            P(AXES, None),
        ),
        check_vma=False,
    )
```

```python
from functools import partial

import jax
import jax.numpy as jnp
import numpy as np
from jax import lax
from jax.experimental import pallas as pl
from jax.experimental.pallas import tpu as pltpu
from jax.sharding import PartitionSpec as P

D = 768
INNER = 1536
NSTATE = 128
HEADDIM = 64
KCONV = 4
SCAN_LEN = 256
PBLOCK = 4096
STEP = 10
HEADS = 24
CONVCH = 1792
PROJ = 3352
PTOT = 3765320
NBLK = 920

LANES = 128
BROWS = PBLOCK // LANES
UNIT = 8
UNITS = BROWS // UNIT
END_IN = D * PROJ
END_OUT = END_IN + INNER * D
MID0 = -(-END_IN // PBLOCK)
MID1 = END_OUT // PBLOCK
N0 = MID0 + NBLK - MID1
N1 = MID1 - MID0
F0_ROWS = N0 * BROWS
IN_ROWS = END_IN // LANES
HEAD_ROWS = MID0 * BROWS - IN_ROWS
TAIL_ROWS = (END_OUT - MID1 * PBLOCK) // LANES
OUT_ROWS = INNER * D // LANES
VEC_ROWS = (NBLK - MID1) * BROWS - TAIL_ROWS
VEC_AT = MID0 * BROWS + TAIL_ROWS
GROUP = 16
GROUPS = D // GROUP
GROUP_ROWS = GROUP * PROJ // LANES
COL_TILES = -(-PROJ // LANES)
WIDE = COL_TILES * LANES
OUT_TILES = D // LANES

NORM_EPS = 1e-05
ADAM_EPS = 1e-08
BETA_ONE = 0.9
BETA_TWO = 0.999
MATRIX_RATE = 0.03
VECTOR_RATE = 0.2
WEIGHT_DECAY = 0.1
PRECISE = lax.Precision.HIGHEST
AXES = ("dp", "fsdp")
VMEM_LIMIT = 60 * 1024 * 1024


def bits_of(count):
    return count.bit_length() - 1


def step_orders(dp, fsdp):
    wide = [("dp", i) for i in range(bits_of(dp))]
    narrow = [("fsdp", i) for i in range(bits_of(fsdp))]
    first = wide[:2] + narrow + wide[2:]
    second = wide[:1] + narrow + wide[1:]
    third = wide[:1] + wide[2:] + wide[1:2] + narrow
    return first, second, third


def cut(sizes, orders):
    streams, at = [], 0
    for size, order in zip(sizes, orders):
        if size:
            streams.append((at, size, order))
        at += size
    return streams


def even(total, parts):
    return [total // parts + (i < total % parts) for i in range(parts)]


def exchange(values, *steps):
    axes = {axis for axis, _ in steps}
    if len(axes) == 1:
        (axis,) = axes
        mask = sum(1 << bit for _, bit in steps)
        pairs = [(i, i ^ mask) for i in range(lax.axis_size(axis))]
        return lax.ppermute(values, axis, pairs)
    low = bits_of(lax.axis_size("fsdp"))
    mask = sum(1 << (bit + (low if axis == "dp" else 0)) for axis, bit in steps)
    count = lax.axis_size("dp") * lax.axis_size("fsdp")
    return lax.ppermute(values, AXES, [(i, i ^ mask) for i in range(count)])


def place_of(relative, order):
    shift_of = {"dp": bits_of(lax.axis_size("fsdp")), "fsdp": 0}
    place = jnp.zeros_like(relative)
    for axis, bit in order:
        place = place * 2 + ((relative >> (shift_of[axis] + bit)) & 1)
    return place


def class_counts(owners, devices):
    block = jnp.arange(NBLK, dtype=jnp.int32)
    mid = ((block >= MID0) & (block < MID1))[None, :]
    device = jnp.arange(devices, dtype=jnp.int32)
    below = owners[None, :] < device[:, None]
    owned = owners[None, :] == device[:, None]

    def total(mask):
        return jnp.sum(mask.astype(jnp.int32), axis=1)

    start = (total(below & ~mid), total(below & mid))
    count = (total(owned & ~mid), total(owned & mid))
    return start, count, total(owned & (block < MID0)[None, :])


def my_counts(owners, me):
    block = jnp.arange(NBLK, dtype=jnp.int32)
    mid = (block >= MID0) & (block < MID1)
    below, owned = owners < me, owners == me
    total = lambda mask: jnp.sum(mask.astype(jnp.int32))
    start = (total(below & ~mid), total(below & mid))
    count = (total(owned & ~mid), total(owned & mid))
    return start, count, total(owned & (block < MID0))


def pair_lanes(capacity, devices):
    return -(-capacity // devices)


def make_plan(owners, capacity, devices, me):
    block = jnp.arange(NBLK, dtype=jnp.int32)
    mid = (block >= MID0) & (block < MID1)
    same = mid[:, None] == mid[None, :]
    before = (owners[None, :] < owners[:, None]) | (
        (owners[None, :] == owners[:, None]) & (block[None, :] < block[:, None])
    )
    order = jnp.sum(before.astype(jnp.int32), axis=1)
    order_in_class = jnp.sum((same & before).astype(jnp.int32), axis=1)
    home, slot = order % devices, order // devices
    device = jnp.arange(devices, dtype=jnp.int32)
    start, count, _ = class_counts(owners, devices)
    my_start, my_count, my_early = my_counts(owners, me)
    pair = pair_lanes(capacity, devices)

    slots = -(-NBLK // devices)
    wanted = me + devices * jnp.arange(slots, dtype=jnp.int32)
    first = start[0] + start[1]
    ends = first + count[0] + count[1]
    owner = jnp.sum((ends[None, :] <= wanted[:, None]).astype(jnp.int32), axis=1)
    owner = jnp.minimum(owner, devices - 1)
    base = jnp.sum(jnp.where(device[None, :] == owner[:, None], first[None, :], 0), axis=1)
    received = owner * pair + jnp.clip((wanted - base) // devices, 0, pair - 1)

    back_pair = (UNITS * capacity + 2 * (devices - 1)) // devices
    unit = UNITS * order_in_class[None, :] + jnp.arange(UNITS, dtype=jnp.int32)[:, None]
    unit_home, unit_slot = unit % devices, unit // devices
    unit_slots = (-(-UNITS * N0 // devices), -(-UNITS * N1 // devices))
    lane = jnp.arange(back_pair, dtype=jnp.int32)

    def units_back(kind):
        turn = lane if kind == 0 else back_pair - 1 - lane
        first = UNITS * start[kind][:, None]
        k = (me - first) % devices + turn[None, :] * devices
        return k < UNITS * count[kind][:, None], (first + k) // devices

    valid0, slot0 = units_back(0)
    valid1, slot1 = units_back(1)
    back = jnp.where(valid0, slot0, jnp.where(valid1, unit_slots[0] + slot1, 0)).reshape(-1)

    row = jnp.arange(capacity, dtype=jnp.int32)
    is_mid = (row >= my_early) & (row < my_early + my_count[1])
    k = jnp.where(is_mid, row - my_early, jnp.where(row < my_early, row, row - my_count[1]))
    first = UNITS * jnp.where(is_mid, my_start[1], my_start[0])
    k = UNITS * k[None, :] + jnp.arange(UNITS, dtype=jnp.int32)[:, None]
    turn = k // devices
    row_from = ((first[None, :] + k) % devices) * back_pair + jnp.where(
        is_mid[None, :], back_pair - 1 - turn, turn
    )
    row_used = row < my_count[0] + my_count[1]
    mine = (owners == me)[None, :]
    rank = jnp.sum((mine & (block[None, :] < block[:, None])).astype(jnp.int32), axis=1)
    row_block = jnp.sum(
        jnp.where(mine & (rank[None, :] == row[:, None]), block[None, :], 0), axis=1
    )
    late = devices * back_pair + UNITS * (row_block - MID1)
    late = late[None, :] + jnp.arange(UNITS, dtype=jnp.int32)[:, None]
    row_from = jnp.where((row_block >= MID1)[None, :], late, row_from)
    row_from = jnp.where(row_used[None, :], row_from, 0)
    return dict(
        home=home, slot=slot, slots=slots,
        received=received, unit_home=unit_home, unit_slot=unit_slot,
        unit_slots=unit_slots, back=back, row_from=row_from,
        row_used=row_used, row_block=row_block,
    )


def stream_places(home, slot, me, streams, devices):
    relative = home ^ me
    place = jnp.zeros_like(slot)
    for begin, size, order in streams:
        inside = (slot >= begin) & (slot < begin + size)
        at = devices * begin + place_of(relative, order) * size + slot - begin
        place = jnp.where(inside, at, place)
    return place


def cost(microseconds):
    return pl.CostEstimate(
        flops=int(microseconds * 1e9), bytes_accessed=int(microseconds * 3e6), transcendentals=0
    )


ANY = pl.BlockSpec(memory_space=pl.ANY)
VMEM = pl.BlockSpec(memory_space=pltpu.VMEM)
SMEM = pl.BlockSpec(memory_space=pltpu.SMEM)


def params(**extra):
    return pltpu.CompilerParams(vmem_limit_bytes=VMEM_LIMIT, **extra)


def shape(dims, dtype):
    return jax.ShapeDtypeStruct(dims, dtype)


def send_kernel(my_index, owners, master, out, flat, *, devices):
    capacity = master.shape[0]
    me = my_index[0]
    for j in range(BROWS):
        flat[pl.ds(j, capacity, stride=BROWS), :] = master[:, j * LANES : (j + 1) * LANES]
    held = owners[...]
    below, owned = held < me, held == me

    def total(mask):
        return jnp.sum(jnp.where(mask, 1.0, 0.0)).astype(jnp.int32)

    start, count = total(below), total(owned)
    pair = out.shape[0] // devices

    def step(home, carry):
        for s in range(pair):
            k = lax.rem(home - start + devices * NBLK, devices) + s * devices
            row = jnp.where(k < count, k, 0)
            rows = pl.ds(pl.multiple_of(row * BROWS, BROWS), BROWS)
            out[home * pair + s] = flat[rows, :].astype(out.dtype)
        return carry

    lax.fori_loop(0, devices, step, 0)


def send_blocks(owners, master, devices, me):
    rows = -(-NBLK // (8 * LANES)) * 8
    held = jnp.pad(owners, (0, rows * LANES - NBLK), constant_values=1 << 20).reshape(rows, LANES)
    count = devices * pair_lanes(master.shape[0], devices)
    return pl.pallas_call(
        partial(send_kernel, devices=devices),
        out_shape=shape((count, BROWS, LANES), jnp.bfloat16),
        in_specs=[SMEM, VMEM, VMEM],
        out_specs=VMEM,
        scratch_shapes=[pltpu.VMEM((master.shape[0] * BROWS, LANES), jnp.float32)],
        compiler_params=params(),
    )(me.reshape(1), held, master)


def pick_kernel(table, source, *outs):
    at = 0
    for out in outs:

        def step(i, carry, out=out, at=at):
            out[i] = source[table[at + i]]
            return carry

        lax.fori_loop(0, out.shape[0], step, 0)
        at += out.shape[0]


def pick_blocks(table, source, sizes):
    return pl.pallas_call(
        pick_kernel,
        out_shape=tuple(shape((n,) + source.shape[1:], source.dtype) for n in sizes),
        in_specs=[SMEM, VMEM],
        out_specs=(VMEM,) * len(sizes),
        compiler_params=params(),
    )(table, source)


def back_kernel(table, *refs, sizes):
    sources, (out, held) = refs[:-2], refs[-2:]
    at = i = 0
    for size in sizes:
        n = sources[i].shape[0]
        total = sources[i][...]
        for k in range(1, size):
            total = total + sources[i + k][0:n]
        held[at : at + n] = total
        at += n
        i += size

    def step(i, carry):
        for u in range(8):
            out[i * 8 + u] = held[table[i * 8 + u]]
        return carry

    total = out.shape[0]
    lax.fori_loop(0, total // 8, step, 0)


def units_to_owners(table, groups):
    return pl.pallas_call(
        partial(back_kernel, sizes=[len(g) for g in groups]),
        out_shape=shape((table.shape[0], UNIT, LANES), jnp.float32),
        in_specs=[SMEM] + [VMEM] * sum(len(g) for g in groups),
        out_specs=VMEM,
        scratch_shapes=[pltpu.VMEM((sum(g[0].shape[0] for g in groups), UNIT, LANES), jnp.float32)],
        compiler_params=params(),
    )(table, *[v for g in groups for v in g])


def row_start(rho):
    return (PROJ * rho) // LANES, (PROJ * rho) % LANES


def copy_all(pairs, sem):
    copies = [pltpu.make_async_copy(a, b, sem.at[i]) for i, (a, b) in enumerate(pairs)]
    for c in copies:
        c.start()
    for c in copies:
        c.wait()


def spread_blocks(table, first, held, flat, count, first_row):
    def one(i):
        at = pl.multiple_of(first_row + i * BROWS, 16)
        flat[pl.ds(at, BROWS), :] = held[table[first + i]].astype(jnp.float32)

    def step(i, carry):
        for u in range(4):
            one(i * 4 + u)
        return carry

    lax.fori_loop(0, count // 4, step, 0)
    for i in range(count // 4 * 4, count):
        one(i)


def unpack_vectors(flat, conv_weight, conv_bias, dt_bias, a_log, skip, norm_gain, gate_gain):
    bf16, f32 = jnp.bfloat16, jnp.float32
    tiles = CONVCH // LANES
    row = lax.broadcasted_iota(jnp.int32, (LANES, LANES), 0)
    col = lax.broadcasted_iota(jnp.int32, (LANES, LANES), 1)
    per_tile = LANES // KCONV
    for k in range(KCONV):
        total = jnp.zeros((tiles, LANES), f32)
        for q in range(KCONV):
            rows = flat[pl.ds(VEC_AT + q, tiles, stride=KCONV), :].astype(bf16)
            chosen = (row == KCONV * (col % per_tile) + k) & (col // per_tile == q)
            total = total + jnp.dot(rows, chosen.astype(bf16), preferred_element_type=f32)
        for i in range(tiles):
            conv_weight[k : k + 1, i * LANES : (i + 1) * LANES] = total[i : i + 1, :]
    bias_at = VEC_AT + tiles * KCONV
    for i in range(tiles):
        conv_bias[:, i * LANES : (i + 1) * LANES] = flat[bias_at + i : bias_at + i + 1, :]
    at = bias_at + tiles
    lane = lax.broadcasted_iota(jnp.int32, (8, LANES), 1)
    first = flat[at : at + 8, :]
    three = []
    for i in range(3):
        moved = pltpu.roll(first, LANES - i * HEADS, 1) if i else first
        three.append(jnp.where(lane < HEADS, moved, 0.0))
    dt_bias[...] = three[0][0:1, :]
    a_log[...] = three[1][0:1, :]
    for j in range(INNER // LANES):
        h = lax.broadcasted_iota(jnp.int32, (LANES, LANES), 0)
        c = lax.broadcasted_iota(jnp.int32, (LANES, LANES), 1) + j * LANES
        spread = (h == c // HEADDIM).astype(bf16)
        wide = jnp.dot(three[2].astype(bf16), spread, preferred_element_type=f32)
        skip[:, j * LANES : (j + 1) * LANES] = wide[0:1, :]
    shift = 3 * HEADS
    for out, begin, width in ((norm_gain, at, D), (gate_gain, at + D // LANES, INNER)):
        for j in range(width // LANES):
            x = pltpu.roll(flat[begin + j : begin + j + 1, :], LANES - shift, 1)
            y = pltpu.roll(flat[begin + j + 1 : begin + j + 2, :], LANES - shift, 1)
            out[:, j * LANES : (j + 1) * LANES] = jnp.where(lane[0:1] < LANES - shift, x, y)


def unpack_weights(table, parts, w_in, w_out, vectors, held, flat, flat_out, tile, sem):
    pairs, at = [], 0
    for part in parts:
        pairs.append((part, held.at[pl.ds(at, part.shape[0])]))
        at += part.shape[0]
    copy_all(pairs, sem)
    spread_blocks(table, 0, held, flat, MID0, 0)
    spread_blocks(table, MID1, held, flat, NBLK - MID1, MID0 * BROWS)
    spread_blocks(table, MID0, held, flat_out, N1, HEAD_ROWS)
    flat_out[0:HEAD_ROWS, :] = flat[IN_ROWS : IN_ROWS + HEAD_ROWS, :]
    flat_out[OUT_ROWS - TAIL_ROWS :, :] = flat[MID0 * BROWS : MID0 * BROWS + TAIL_ROWS, :]
    unpack_vectors(flat, *vectors)
    rows = 128

    def out_step(i, carry):
        at = pl.multiple_of(i * rows, rows)
        for j in range(OUT_TILES):
            x = flat_out[pl.ds(at * OUT_TILES + j, rows, stride=OUT_TILES), :]
            w_out[pl.ds(at, rows), j * LANES : (j + 1) * LANES] = x.astype(jnp.bfloat16)
        return carry

    lax.fori_loop(0, INNER // rows, out_step, 0)
    lane = lax.broadcasted_iota(jnp.int32, (GROUPS, LANES), 1)

    def columns(j):
        for rho in range(GROUP):
            c, s = row_start(rho)
            x = flat[pl.ds(c + j, GROUPS, stride=GROUP_ROWS), :]
            if s:
                y = flat[pl.ds(c + j + 1, GROUPS, stride=GROUP_ROWS), :]
                x = jnp.where(
                    lane < LANES - s,
                    pltpu.roll(x, LANES - s, 1),
                    pltpu.roll(y, LANES - s, 1),
                )
            tile[pl.ds(rho, GROUPS, stride=GROUP), :] = x

    def step(j, carry):
        columns(j)
        w_in[:, pl.ds(pl.multiple_of(j * LANES, LANES), LANES)] = tile[...].astype(jnp.bfloat16)
        return carry

    lax.fori_loop(0, COL_TILES - 1, step, 0)
    columns(COL_TILES - 1)
    last = (COL_TILES - 1) * LANES
    inside = lax.broadcasted_iota(jnp.int32, (D, LANES), 1) < PROJ - last
    w_in[:, last:] = jnp.where(inside, tile[...], 0.0).astype(jnp.bfloat16)


def unpack_scratch(held, count):
    return [
        pltpu.VMEM((held, BROWS, LANES), jnp.bfloat16),
        pltpu.VMEM((F0_ROWS, LANES), jnp.float32),
        pltpu.VMEM((OUT_ROWS, LANES), jnp.float32),
        pltpu.VMEM((D, LANES), jnp.float32),
        pltpu.SemaphoreType.DMA((count,)),
    ]


def permute_units(table, flat, count, first_row, staged):
    many = 4

    def one(i):
        for u in range(UNITS):
            at = first_row + i * BROWS + u * UNIT
            at = at if isinstance(at, int) else pl.multiple_of(at, UNIT)
            staged[table[u, i]] = flat[pl.ds(at, UNIT), :]

    def step(i, carry):
        for b in range(many):
            one(i * many + b)
        return carry

    lax.fori_loop(0, count // many, step, 0)
    for i in range(count // many * many, count):
        one(i)


def pack_in_kernel(table, hidden, grad, head, *refs):
    outs, (turned, tiles, flat, staged, sem) = refs[:-5], refs[-5:]
    turned[...] = hidden[...].T
    lane = lax.broadcasted_iota(jnp.int32, (GROUPS, LANES), 1)

    def product(p, count):
        at = p * 2 * LANES
        at = at if isinstance(at, int) else pl.multiple_of(at, 2 * LANES)
        return jnp.dot(
            turned[...], grad[:, pl.ds(at, count * LANES)], preferred_element_type=jnp.float32
        )

    def put(p, value):
        for k in range(value.shape[1] // LANES):
            at = (p * 2 + k) * D
            at = at if isinstance(at, int) else pl.multiple_of(at, D)
            tiles[pl.ds(at, D), :] = value[:, k * LANES : (k + 1) * LANES]

    def load(rho, j):
        return tiles[pl.ds(j * D + rho, GROUPS, stride=GROUP), :]

    def whole(rho, i):
        first = -(-PROJ * rho // LANES)
        col0 = first * LANES - PROJ * rho
        x = load(rho, i)
        if col0:
            x = jnp.where(
                lane < LANES - col0,
                pltpu.roll(x, LANES - col0, 1),
                pltpu.roll(load(rho, i + 1), LANES - col0, 1),
            )
        flat[pl.ds(first + i, GROUPS, stride=GROUP_ROWS), :] = x

    put(0, product(0, 2))
    put(1, product(1, 2))
    pairs = COL_TILES // 2

    def step(p, carry):
        for i in range(2):
            for rho in range(GROUP):
                whole(rho, p * 2 + i)
        put(p + 2, product(p + 2, 2))
        return carry

    lax.fori_loop(0, pairs - 2, step, 0)
    put(pairs, product(pairs, COL_TILES % 2))
    for rho in range(GROUP):
        first = -(-PROJ * rho // LANES)
        col0 = first * LANES - PROJ * rho
        full = (PROJ - col0) // LANES
        for i in range((pairs - 2) * 2, full):
            whole(rho, i)
        left = PROJ - col0 - full * LANES
        if left:
            begin = col0 + full * LANES
            j, s = begin // LANES, begin % LANES
            x = pltpu.roll(load(rho, j), LANES - s, 1) if s else load(rho, j)
            if s + left > LANES:
                x = jnp.where(lane < LANES - s, x, pltpu.roll(load(rho, j + 1), LANES - s, 1))
            y = pltpu.roll(load(rho + 1, 0), left, 1)
            flat[pl.ds(first + full, GROUPS, stride=GROUP_ROWS), :] = jnp.where(lane < left, x, y)
    flat[IN_ROWS : IN_ROWS + HEAD_ROWS, :] = head[...]
    permute_units(table, flat, MID0, 0, staged)
    copies, at = [], 0
    for out in outs:
        copies.append((staged.at[pl.ds(at, out.shape[0])], out))
        at += out.shape[0]
    copy_all(copies, sem)


def pack_in(table, hidden, grad, head, sizes):
    return pl.pallas_call(
        pack_in_kernel,
        out_shape=tuple(shape((n, UNIT, LANES), jnp.float32) for n in sizes),
        in_specs=[SMEM, VMEM, VMEM, VMEM],
        out_specs=(ANY,) * len(sizes),
        scratch_shapes=[
            pltpu.VMEM((D, hidden.shape[0]), jnp.bfloat16),
            pltpu.VMEM((COL_TILES * D, LANES), jnp.float32),
            pltpu.VMEM((MID0 * BROWS, LANES), jnp.float32),
            pltpu.VMEM((sum(sizes), UNIT, LANES), jnp.float32),
            pltpu.SemaphoreType.DMA((len(sizes),)),
        ],
        compiler_params=params(),
        cost_estimate=cost(20),
    )(table, hidden, grad, head)


def pack_out_kernel(
    table, mixed_out, grad, local, keep, send, head, tail, turned, flat, out, sem, *, slots
):
    rows = 256

    def step(i, carry):
        at = pl.multiple_of(i * rows, rows)
        turned[...] = mixed_out[:, pl.ds(at, rows)].T
        product = jnp.dot(turned[...], grad[...], preferred_element_type=jnp.float32)
        for j in range(OUT_TILES):
            flat[pl.ds(at * OUT_TILES + j, rows, stride=OUT_TILES), :] = product[
                :, j * LANES : (j + 1) * LANES
            ]
        return carry

    lax.fori_loop(0, INNER // rows, step, 0)
    head[...] = flat[0:HEAD_ROWS, :]
    tail[...] = flat[OUT_ROWS - TAIL_ROWS : OUT_ROWS, :]
    permute_units(table, flat, N1, HEAD_ROWS, out)

    def add_local(i, carry):
        out[i * slots + slots - 1] = local[...]
        return carry

    lax.fori_loop(0, out.shape[0] // slots, add_local, 0)
    half = keep.shape[0]
    copy_all([(out.at[pl.ds(0, half)], keep), (out.at[pl.ds(half, half)], send)], sem)


def pack_out(table, mixed_out, grad, local, devices, slots):
    return pl.pallas_call(
        partial(pack_out_kernel, slots=slots),
        out_shape=(
            shape((devices * slots // 2, UNIT, LANES), jnp.float32),
            shape((devices * slots // 2, UNIT, LANES), jnp.float32),
            shape((HEAD_ROWS, LANES), jnp.float32),
            shape((TAIL_ROWS, LANES), jnp.float32),
        ),
        in_specs=[SMEM, VMEM, VMEM, VMEM],
        out_specs=(ANY, ANY, VMEM, VMEM),
        scratch_shapes=[
            pltpu.VMEM((256, mixed_out.shape[0]), jnp.bfloat16),
            pltpu.VMEM((OUT_ROWS, LANES), jnp.float32),
            pltpu.VMEM((devices * slots, UNIT, LANES), jnp.float32),
            pltpu.SemaphoreType.DMA((2,)),
        ],
        compiler_params=params(),
    )(table, mixed_out, grad, local)


def adam_kernel(
    table, row_block, row_used, scale, got, late, master, first, second,
    o_first, o_second, o_master, flat, held, limit, used,
):
    capacity = master.shape[0]

    def step(i, carry):
        for u in range(UNITS):
            at = table[u, i]
            rows = pl.ds(pl.multiple_of(i * BROWS + u * UNIT, UNIT), UNIT)
            flat[rows, :] = held[at]
        limit[pl.ds(i, 1), :] = jnp.full((1, LANES), END_OUT - row_block[i] * PBLOCK, jnp.int32)
        used[pl.ds(i, 1), :] = jnp.full((1, LANES), row_used[i], jnp.int32)
        return carry

    held[0 : got.shape[0]] = got[...]
    held[got.shape[0] :] = late[...]
    lax.fori_loop(0, capacity, step, 0)
    lane = lax.broadcasted_iota(jnp.int32, (capacity, LANES), 1)
    divisor = scale[0]
    for j in range(BROWS):
        cols = slice(j * LANES, (j + 1) * LANES)
        grad = jnp.where(used[...] > 0, flat[pl.ds(j, capacity, stride=BROWS), :], 0.0) / divisor
        matrix = lane + j * LANES < limit[...]
        weights = master[:, cols]
        new_first = BETA_ONE * first[:, cols] + (1.0 - BETA_ONE) * grad
        new_second = BETA_TWO * second[:, cols] + (1.0 - BETA_TWO) * grad * grad
        normal = (
            new_first
            / (1.0 - BETA_ONE**STEP)
            / (jnp.sqrt(new_second / (1.0 - BETA_TWO**STEP)) + ADAM_EPS)
        )
        rate = jnp.where(matrix, MATRIX_RATE, VECTOR_RATE)
        decay = jnp.where(matrix, WEIGHT_DECAY, 0.0)
        o_first[:, cols] = new_first
        o_second[:, cols] = new_second
        o_master[:, cols] = weights - rate * (normal + decay * weights)


def adam(table, row_block, row_used, divisor, got, late, master, first, second):
    capacity = master.shape[0]
    return pl.pallas_call(
        adam_kernel,
        out_shape=(shape(master.shape, jnp.float32),) * 3,
        in_specs=[SMEM] * 4 + [VMEM] * 5,
        out_specs=(VMEM,) * 3,
        scratch_shapes=[
            pltpu.VMEM((capacity * BROWS, LANES), jnp.float32),
            pltpu.VMEM((got.shape[0] + late.shape[0], UNIT, LANES), jnp.float32),
            pltpu.VMEM((capacity, LANES), jnp.int32),
            pltpu.VMEM((capacity, LANES), jnp.int32),
        ],
        compiler_params=params(),
    )(
        table, row_block, row_used.astype(jnp.int32), divisor.reshape(1), got, late, master, first, second
    )


def doubled(values, step):
    return jnp.concatenate([values, exchange(values, step)], axis=0)


def gather_steps(values, order):
    for step in order[:0:-1]:
        values = doubled(values, step)
    return values, exchange(values, order[0])


def reduce_step(kept, got, step, extra=None):
    half = kept.shape[0] // 2
    given = kept[half:] + got[half:]
    if extra is None:
        return kept[:half] + got[:half], exchange(given, step)
    arrived = exchange(jnp.concatenate([given, extra]), step)
    return kept[:half] + got[:half], arrived[:half], extra + arrived[half:]


CHUNK = 128
PAIRS = HEADS // 2
MIXW = INNER + 2 * NSTATE
DT_AT = INNER + CONVCH
F32 = jnp.float32
BF16 = jnp.bfloat16
NN = (((1,), (0,)), ((), ()))
NT = (((1,), (1,)), ((), ()))


def dot(a, b, dims=NN):
    return lax.dot_general(a, b, dims, preferred_element_type=F32)


def split(v):
    high = v.astype(BF16)
    return high, (v - high.astype(F32)).astype(BF16)


def dot3(a, b, dims=NN):
    ah, al = a
    bh, bl = b
    return dot(ah, bh, dims) + (dot(ah, bl, dims) + dot(al, bh, dims))


def heads_gather():
    return jnp.asarray(np.repeat(np.eye(HEADS, LANES, dtype=np.float32), HEADDIM, axis=0), BF16)


def three_parts(v):
    high = v.astype(BF16).astype(F32)
    rest = v - high
    middle = rest.astype(BF16).astype(F32)
    low = rest - middle
    return (high + pltpu.roll(middle, 32, 1) + pltpu.roll(low, 64, 1)).astype(BF16)


def triangle_sum(tri, v):
    parts = dot(tri, three_parts(v))
    lane = lax.broadcasted_iota(jnp.int32, parts.shape, 1)
    total = parts + pltpu.roll(parts, LANES - 32, 1) + pltpu.roll(parts, LANES - 64, 1)
    return jnp.where(lane < HEADS, total, 0.0)


def chunk_decays(dt, dt_bias, a_log):
    lane = lax.broadcasted_iota(jnp.int32, (CHUNK, LANES), 1)
    row = lax.broadcasted_iota(jnp.int32, (CHUNK, LANES), 0)
    shifted = dt + dt_bias
    delta = jnp.where(
        lane < HEADS, jnp.maximum(shifted, 0.0) + jnp.log1p(jnp.exp(-jnp.abs(shifted))), 0.0
    )
    rate = -jnp.exp(a_log)
    lower = (row >= lane).astype(BF16)
    cum = triangle_sum(lower, delta * rate)
    last = cum[CHUNK - 1 : CHUNK, :]
    return shifted, delta, rate, cum, last


def pair_mask():
    lane = lax.broadcasted_iota(jnp.int32, (CHUNK, LANES), 1)
    low = (lane < HEADDIM).astype(F32)
    return low.astype(BF16), (1.0 - low).astype(BF16)


QUADS = HEADS // 4
QWIDTH = 4 * HEADDIM


def sigmoid(v):
    return 0.5 * jnp.tanh(0.5 * v) + 0.5


def silu(v):
    return v * sigmoid(v)


def side_by_side(v):
    high, low = split(v)
    return jnp.concatenate([high, low], axis=1), high


def dot_parts(a, b):
    ahl, ah = a
    bh, bl = b
    return dot(ahl, jnp.concatenate([bh, bh], axis=0)) + dot(ah, bl)


def dot_turned(a, b):
    ah, al = a
    bh, bl = b
    both = dot(ah, jnp.concatenate([bh, bl], axis=0), NT)
    n = bh.shape[0]
    return both[:, :n] + both[:, n:] + dot(al, bh, NT)


def widen(delta, cum, quad):
    lane = lax.broadcasted_iota(jnp.int32, (CHUNK, LANES), 1)
    over = lambda v, h: jnp.broadcast_to(v[:, h : h + 1], (CHUNK, LANES))
    first = 4 * quad
    columns = [over(cum, first + k) for k in range(4)]
    rates = [over(delta, first + k) for k in range(4)]
    pair = lambda vs: jnp.concatenate(
        [jnp.where(lane < HEADDIM, vs[0], vs[1]), jnp.where(lane < HEADDIM, vs[2], vs[3])], axis=1
    )
    return pair(rates), pair(columns), columns


def pair_rows(parts, j, low, high):
    cols = slice(j * LANES, (j + 1) * LANES)
    return [jnp.concatenate([p[:, cols] * low, p[:, cols] * high], axis=0) for p in parts]


def scan_chunk(mixed, dt, dt_bias, a_log, skip, state, put):
    _, delta, _, cum, last = chunk_decays(dt, dt_bias, a_log)
    lane = lax.broadcasted_iota(jnp.int32, (CHUNK, LANES), 1)
    row = lax.broadcasted_iota(jnp.int32, (CHUNK, LANES), 0)
    bias = jnp.where(row >= lane, 0.0, -1e30)
    cum_t = cum.T
    inputs_b = mixed[:, INNER : INNER + NSTATE]
    readout = mixed[:, INNER + NSTATE :]
    affinity = dot3(split(readout), split(inputs_b), NT)
    readout_parts = side_by_side(readout)
    b_parts = side_by_side(inputs_b.T)
    low, high = pair_mask()
    for quad in range(QUADS):
        cols = slice(quad * QWIDTH, (quad + 1) * QWIDTH)
        wide_delta, wide_cum, columns = widen(delta, cum, quad)
        values = mixed[:, cols]
        scaled = values * wide_delta
        parts = split(scaled)
        outs = []
        for j in range(2):
            right_h, right_l = pair_rows(parts, j, low, high)
            left = []
            for k in range(2):
                h = 4 * quad + 2 * j + k
                within = jnp.exp(columns[2 * j + k] - cum_t[h : h + 1, :] + bias)
                left.append(split(affinity * within))
            left_h = jnp.concatenate([left[0][0], left[1][0]], axis=1)
            left_l = jnp.concatenate([left[0][1], left[1][1]], axis=1)
            both = dot(left_h, jnp.concatenate([right_h, right_l], axis=1))
            outs.append(both[:, :LANES] + both[:, LANES:] + dot(left_l, right_h))
        carried = state[:, cols]
        grown = jnp.exp(wide_cum)
        out = jnp.concatenate(outs, axis=1) + dot_parts(readout_parts, split(carried)) * grown
        tail = jnp.exp(wide_cum[CHUNK - 1 :] - wide_cum)
        state[:, cols] = carried * grown[CHUNK - 1 :] + dot_parts(b_parts, split(scaled * tail))
        put(quad, out + skip[:, cols] * values)


FORWARD_ROWS = 2 * CHUNK


def forward_kernel(table, tokens, *refs, count):
    parts, refs = refs[:count], refs[count:]
    (w_in_kept, w_out_kept, conv_weight, conv_bias, dt_bias, a_log, skip, norm_gain, gain,
     hidden, gate, conv_in, dt, ssm, mixed_out, states) = refs[:16]
    w_in, w_out, state, before, mixed, shift, out_sem, *scratch = refs[16:]
    keep = [
        pltpu.make_async_copy(w_in, w_in_kept, out_sem.at[0]),
        pltpu.make_async_copy(w_out, w_out_kept, out_sem.at[1]),
    ]

    @pl.when(pl.program_id(0) == 0)
    def _():
        vectors = (conv_weight, conv_bias, dt_bias, a_log, skip, norm_gain, gain)
        unpack_weights(table, parts, w_in, w_out, vectors, *scratch)
        for copy in keep:
            copy.start()
        state[...] = jnp.zeros_like(state)
        before[...] = jnp.zeros_like(before)

    x = tokens[...].astype(F32)
    inverse = lax.rsqrt(jnp.mean(x * x, axis=1, keepdims=True) + NORM_EPS)
    h = (x * inverse * norm_gain[...]).astype(BF16)
    hidden[...] = h
    dt[...] = dot(h, w_in[:, DT_AT:])
    wide = 2 * LANES
    for tile in range(CONVCH // wide):
        at = tile * wide
        product = dot(h, w_in[:, INNER + at : INNER + at + wide])
        conv_in[:, at : at + wide] = product
        for half in range(2):
            cols = slice(at + half * LANES, at + (half + 1) * LANES)
            rows = product[:, half * LANES : (half + 1) * LANES]
            earlier = before[:, cols]
            terms = moved_down(shift.at[tile * 2 + half], rows, earlier) + [rows]
            before[:, cols] = rows[FORWARD_ROWS - 8 :]
            mixed[:, cols] = silu(conv_sum(terms, conv_weight[:, cols], conv_bias[:, cols]))
    for tile in range(INNER // wide):
        cols = slice(tile * wide, (tile + 1) * wide)
        gate[:, cols] = dot(h, w_in[:, cols])
    for sub in range(FORWARD_ROWS // CHUNK):
        rows = slice(sub * CHUNK, (sub + 1) * CHUNK)
        states[sub] = state[...]
        squares = [jnp.zeros((CHUNK, LANES), F32)]

        def put(quad, out, rows=rows, squares=squares):
            cols = slice(quad * QWIDTH, (quad + 1) * QWIDTH)
            ssm[rows, cols] = out
            gated = out * silu(gate[rows, cols])
            first, second = gated[:, :LANES], gated[:, LANES:]
            squares[0] = squares[0] + first * first + second * second

        scan_chunk(
            mixed[rows, :], dt[rows, :], dt_bias[...], a_log[...], skip, state, put
        )
        rho = lax.rsqrt(jnp.sum(squares[0], axis=1, keepdims=True) * (1.0 / INNER) + NORM_EPS)
        for j in range(PAIRS):
            cols = slice(j * LANES, (j + 1) * LANES)
            gated = ssm[rows, cols] * silu(gate[rows, cols])
            mixed_out[rows, cols] = (gated * rho * gain[:, cols]).astype(BF16)

    @pl.when(pl.program_id(0) == pl.num_programs(0) - 1)
    def _():
        for copy in keep:
            copy.wait()


def forward(table, tokens, parts):
    length = tokens.shape[0]
    by_row = lambda width: pl.BlockSpec((FORWARD_ROWS, width), lambda i: (i, 0))
    per_step = FORWARD_ROWS // CHUNK
    vectors = [(KCONV, CONVCH), (1, CONVCH), (1, LANES), (1, LANES), (1, INNER), (1, D), (1, INNER)]
    return pl.pallas_call(
        partial(forward_kernel, count=len(parts)),
        grid=(length // FORWARD_ROWS,),
        out_shape=[shape((D, WIDE), BF16), shape((INNER, D), BF16)]
        + [shape(v, F32) for v in vectors]
        + [
            shape((length, D), BF16),
            shape((length, INNER), F32),
            shape((length, MIXW), F32),
            shape((length, LANES), F32),
            shape((length, INNER), F32),
            shape((length, INNER), BF16),
            shape((length // CHUNK, NSTATE, INNER), F32),
        ],
        in_specs=[SMEM, by_row(D)] + [ANY] * len(parts),
        out_specs=[ANY, ANY]
        + [pl.BlockSpec(v, lambda i: (0, 0)) for v in vectors]
        + [
            by_row(D),
            by_row(INNER),
            by_row(MIXW),
            by_row(LANES),
            by_row(INNER),
            by_row(INNER),
            pl.BlockSpec((per_step, NSTATE, INNER), lambda i: (i, 0, 0)),
        ],
        scratch_shapes=[
            pltpu.VMEM((D, WIDE), BF16),
            pltpu.VMEM((INNER, D), BF16),
            pltpu.VMEM((NSTATE, INNER), F32),
            pltpu.VMEM((8, MIXW), F32),
            pltpu.VMEM((FORWARD_ROWS, MIXW), F32),
            pltpu.VMEM((MIXW // LANES, FORWARD_ROWS + 8, LANES), F32),
            pltpu.SemaphoreType.DMA((2,)),
        ]
        + unpack_scratch(sum(part.shape[0] for part in parts), len(parts)),
        compiler_params=params(),
        cost_estimate=cost(50),
    )(table, tokens, *parts)


def eights(v):
    return jnp.sum(v.reshape(v.shape[0] // 8, 8, v.shape[1]), axis=0)


def backward_kernel(
    conv_in, earlier, dt, ssm, grad, grad_gate, states, conv_weight, conv_bias, dt_bias, a_log, skip,
    gather, grad_low, sums, skip_sums, conv_sums,
    grad_state, to_sum, mixed, slope, grad_mixed, following, shift,
):
    @pl.when(pl.program_id(0) == 0)
    def _():
        grad_state[...] = jnp.zeros_like(grad_state)
        sums[...] = jnp.zeros_like(sums)
        skip_sums[...] = jnp.zeros_like(skip_sums)
        conv_sums[...] = jnp.zeros_like(conv_sums)
        following[...] = jnp.zeros_like(following)

    begins = pl.program_id(0) == pl.num_programs(0) - 1

    for tile in range(MIXW // LANES):
        cols = slice(tile * LANES, (tile + 1) * LANES)
        rows = conv_in[:, cols]
        before = jnp.where(begins, 0.0, earlier[:, cols])
        terms = moved_down(shift.at[tile], rows, before) + [rows]
        value = conv_sum(terms, conv_weight[:, cols], conv_bias[:, cols])
        sig = sigmoid(value)
        mixed[:, cols] = value * sig
        slope[:, cols] = sig * (1.0 + value * (1.0 - sig))

    shifted, delta, rate, cum, last = chunk_decays(dt[...], dt_bias[...], a_log[...])
    lane = lax.broadcasted_iota(jnp.int32, (CHUNK, LANES), 1)
    row = lax.broadcasted_iota(jnp.int32, (CHUNK, LANES), 0)
    bias = jnp.where(lane >= row, 0.0, -1e30)
    heads = lane < HEADS
    cum_t = cum.T
    inputs_b = mixed[:, INNER : INNER + NSTATE]
    readout = mixed[:, INNER + NSTATE :]
    b_parts, c_parts = split(inputs_b), split(readout)
    b_wide = side_by_side(inputs_b)
    c_turned = side_by_side(readout.T)
    affinity = dot3(b_parts, c_parts, NT)
    low, high = pair_mask()
    grad_affinity = jnp.zeros((CHUNK, CHUNK), F32)
    grad_b = jnp.zeros((CHUNK, NSTATE), F32)
    grad_c = jnp.zeros((CHUNK, NSTATE), F32)
    last_row = lax.broadcasted_iota(jnp.int32, (CHUNK, QWIDTH), 0) == CHUNK - 1
    for quad in range(QUADS):
        cols = slice(quad * QWIDTH, (quad + 1) * QWIDTH)
        wide_delta, wide_cum, columns = widen(delta, cum, quad)
        grown = jnp.exp(wide_cum)
        tail = jnp.exp(wide_cum[CHUNK - 1 :] - wide_cum)
        end = grown[CHUNK - 1 :]
        values = mixed[:, cols]
        pulled = grad[:, cols]
        scaled = values * wide_delta
        x_parts, p_parts = split(scaled), split(pulled)
        outs = []
        for j in range(2):
            half = slice(j * LANES, (j + 1) * LANES)
            xh, xl = x_parts[0][:, half], x_parts[1][:, half]
            right_h, right_l = pair_rows(p_parts, j, low, high)
            pull = dot(
                jnp.concatenate([xh, xl], axis=1),
                jnp.concatenate([right_h, right_h], axis=1),
                NT,
            ) + dot(xh, right_l, NT)
            kernels = []
            for k in range(2):
                h = 4 * quad + 2 * j + k
                within = jnp.exp(cum_t[h : h + 1, :] - columns[2 * j + k] + bias)
                kernels.append(split(affinity * within))
                grad_affinity = grad_affinity + within * pull[:, k * CHUNK : (k + 1) * CHUNK]
            kernel_h = jnp.concatenate([kernels[0][0], kernels[1][0]], axis=1)
            kernel_l = jnp.concatenate([kernels[0][1], kernels[1][1]], axis=1)
            both = dot(kernel_h, jnp.concatenate([right_h, right_l], axis=1))
            outs.append(both[:, :LANES] + both[:, LANES:] + dot(kernel_l, right_h))
        late = grad_state[:, cols]
        late_parts = split(late)
        early = states[0, :, cols]
        from_state = dot_parts(b_wide, late_parts) * tail
        grad_scaled = jnp.concatenate(outs, axis=1) + from_state
        pulled_cum = split(pulled * grown)
        grad_c = grad_c + dot_turned(pulled_cum, split(early))
        grad_b = grad_b + dot_turned(split(scaled * tail), late_parts)
        grad_state[:, cols] = late * end + dot_parts(c_turned, pulled_cum)
        grad_mixed[:, cols] = grad_scaled * wide_delta + skip[:, cols] * pulled
        skip_sums[:, cols] += jnp.sum(pulled * values, axis=0, keepdims=True)
        to_sum[:CHUNK, cols] = grad_scaled * values
        inner = pulled * (ssm[:, cols] - skip[:, cols] * values) - scaled * grad_scaled
        extra = jnp.sum(scaled * from_state, axis=0, keepdims=True) + end * jnp.sum(
            late * early, axis=0, keepdims=True
        )
        to_sum[CHUNK:, cols] = inner + jnp.where(last_row, extra, 0.0)
    ga_parts = split(grad_affinity)
    grad_mixed[:, INNER : INNER + NSTATE] = grad_b + dot3(ga_parts, c_parts)
    grad_mixed[:, INNER + NSTATE :] = grad_c + dot3(split(grad_affinity.T), b_parts)


    def by_head(v):
        high, low = split(v)
        return dot(high, gather[...]) + dot(low, gather[...])

    direct, grad_cum = by_head(to_sum[:CHUNK, :]), by_head(to_sum[CHUNK:, :])
    upper = (lane >= row).astype(BF16)
    after = triangle_sum(upper, grad_cum)
    grad_delta = direct + rate * after
    grad_raw = jnp.where(heads, grad_delta * sigmoid(shifted), 0.0)
    grad_low[:, DT_AT:] = grad_raw.astype(BF16)
    sums[0:1, :] += jnp.sum(grad_raw, axis=0, keepdims=True)
    sums[1:2, :] += rate * jnp.sum(delta * after, axis=0, keepdims=True)
    grad_low[:, :INNER] = grad_gate[...]
    for tile in range(MIXW // LANES):
        cols = slice(tile * LANES, (tile + 1) * LANES)
        w = conv_weight[:, cols]
        g = grad_mixed[:, cols] * slope[:, cols]
        rows = conv_in[:, cols]
        later = following[:, cols]
        total = jnp.zeros((CHUNK, LANES), F32)
        arriving = moved_up(shift.at[tile], g, later) + [g]
        for k in range(KCONV):
            conv_sums[8 * k : 8 * k + 8, cols] += eights(rows * arriving[k])
            total = total + arriving[k] * w[k : k + 1]
        conv_sums[8 * KCONV :, cols] += eights(g)
        following[:, cols] = g[:8]
        grad_low[:, INNER + tile * LANES : INNER + (tile + 1) * LANES] = total.astype(BF16)


def backward(
    conv_in, dt, ssm, grad, grad_gate, states, conv_weight, conv_bias, dt_bias, a_log, skip, gather
):
    length = conv_in.shape[0]
    chunks = length // CHUNK
    whole = lambda v: pl.BlockSpec(v.shape, lambda i: (0,) * v.ndim)
    by_row = lambda width: pl.BlockSpec((CHUNK, width), lambda i: (chunks - 1 - i, 0))
    return pl.pallas_call(
        backward_kernel,
        grid=(chunks,),
        out_shape=(
            shape((length, WIDE), BF16),
            shape((8, LANES), F32),
            shape((1, INNER), F32),
            shape((8 * (KCONV + 1), MIXW), F32),
        ),
        in_specs=[
            by_row(MIXW),
            pl.BlockSpec((8, MIXW), lambda i: (jnp.maximum((chunks - 1 - i) * (CHUNK // 8) - 1, 0), 0)),
            by_row(LANES),
            by_row(INNER),
            by_row(INNER),
            by_row(INNER),
            pl.BlockSpec((1, NSTATE, INNER), lambda i: (chunks - 1 - i, 0, 0)),
        ]
        + [whole(v) for v in (conv_weight, conv_bias, dt_bias, a_log, skip, gather)],
        out_specs=(
            by_row(WIDE),
            pl.BlockSpec((8, LANES), lambda i: (0, 0)),
            pl.BlockSpec((1, INNER), lambda i: (0, 0)),
            pl.BlockSpec((8 * (KCONV + 1), MIXW), lambda i: (0, 0)),
        ),
        scratch_shapes=[pltpu.VMEM((NSTATE, INNER), F32)]
        + [pltpu.VMEM((2 * CHUNK, INNER), F32)]
        + [pltpu.VMEM((CHUNK, MIXW), F32)] * 3
        + [pltpu.VMEM((8, MIXW), F32), pltpu.VMEM((MIXW // LANES, CHUNK + 8, LANES), F32)],
        compiler_params=params(),
        cost_estimate=cost(43),
    )(
        conv_in, conv_in, dt, ssm, grad, grad_gate, states,
        conv_weight, conv_bias, dt_bias, a_log, skip, gather,
    )


def moved_down(scratch, v, before):
    rows = v.shape[0]
    scratch[0:8, :] = before
    scratch[8 : 8 + rows, :] = v
    return [scratch[8 - by : 8 - by + rows, :] for by in range(KCONV - 1, 0, -1)]


def moved_up(scratch, v, behind):
    rows = v.shape[0]
    scratch[0:rows, :] = v
    scratch[rows : rows + 8, :] = behind
    return [scratch[by : by + rows, :] for by in range(KCONV - 1, 0, -1)]


def conv_sum(terms, weight, bias):
    total = bias + terms[KCONV - 1] * weight[KCONV - 1 : KCONV]
    for k in range(KCONV - 1):
        total = total + terms[k] * weight[k : k + 1]
    return total


def loss_kernel(
    limit, mixed_out, w_out, tokens, teacher, mask, block_out, grad_result, grad_branch, error
):
    step = pl.program_id(0)

    @pl.when(step == 0)
    def _():
        error[...] = jnp.zeros_like(error)

    rows = tokens.shape[0]
    result = tokens[...].astype(F32) + dot(mixed_out[...], w_out[...])
    position = step * rows + lax.broadcasted_iota(jnp.int32, (rows, 1), 0)
    valid = (position < limit[0]).astype(F32)
    turned = jnp.broadcast_to(mask[...].astype(F32), (LANES, rows)).T
    weight = valid * turned[:, 0:1]
    block_out[...] = (result * valid).astype(BF16)
    misfit = result - teacher[...].astype(F32)
    pulled = 2.0 * weight * misfit
    grad_result[...] = pulled
    errors = jnp.sum(0.5 * pulled * misfit, axis=0, keepdims=True)
    for j in range(D // LANES):
        error[j : j + 1, :] += errors[:, j * LANES : (j + 1) * LANES]
    error[D // LANES : D // LANES + 1, :] += jnp.sum(valid * turned, axis=0, keepdims=True)
    grad_branch[...] = pulled.astype(BF16)


def loss_part(limit, mixed_out, w_out, tokens, teacher, mask):
    length = tokens.shape[0]
    rows = 256
    by_row = lambda width: pl.BlockSpec((rows, width), lambda i: (i, 0))
    return pl.pallas_call(
        loss_kernel,
        grid=(length // rows,),
        out_shape=(
            shape((length, D), BF16),
            shape((length, D), F32),
            shape((length, D), BF16),
            shape((8, LANES), F32),
        ),
        in_specs=[
            SMEM,
            by_row(INNER),
            pl.BlockSpec(w_out.shape, lambda i: (0, 0)),
            by_row(D),
            by_row(D),
            pl.BlockSpec((1, rows), lambda i: (0, i)),
        ],
        out_specs=(by_row(D), by_row(D), by_row(D), pl.BlockSpec((8, LANES), lambda i: (0, 0))),
        compiler_params=params(),
        cost_estimate=cost(8),
    )(limit, mixed_out, w_out, tokens, teacher, mask)


def gate_kernel(grad_branch, w_out, ssm, gate, gain, grad_ssm, grad_gate, gain_sums):
    @pl.when(pl.program_id(0) == 0)
    def _():
        gain_sums[...] = jnp.zeros_like(gain_sums)

    grad_mixed = dot(grad_branch[...], w_out[...], NT)
    g = gate[...]
    sig = sigmoid(g)
    act = g * sig
    inner = ssm[...]
    gated = inner * act
    rho = lax.rsqrt(jnp.mean(gated * gated, axis=1, keepdims=True) + NORM_EPS)
    unit = gated * rho
    gain_sums[...] += jnp.sum(unit * grad_mixed, axis=0, keepdims=True)
    grad_unit = grad_mixed * gain[...]
    share = jnp.mean(grad_unit * unit, axis=1, keepdims=True)
    grad_gated = rho * (grad_unit - unit * share)
    grad_ssm[...] = grad_gated * act
    grad_gate[...] = (grad_gated * inner * (sig * (1.0 + g * (1.0 - sig)))).astype(BF16)


def gate_part(grad_branch, w_out, ssm, gate, gain):
    length = ssm.shape[0]
    rows = 256
    by_row = lambda width: pl.BlockSpec((rows, width), lambda i: (i, 0))
    whole = lambda v: pl.BlockSpec(v.shape, lambda i: (0,) * v.ndim)
    return pl.pallas_call(
        gate_kernel,
        grid=(length // rows,),
        out_shape=(shape((length, INNER), F32), shape((length, INNER), BF16), shape((1, INNER), F32)),
        in_specs=[by_row(D), whole(w_out), by_row(INNER), by_row(INNER), whole(gain)],
        out_specs=(by_row(INNER), by_row(INNER), pl.BlockSpec((1, INNER), lambda i: (0, 0))),
        compiler_params=params(),
        cost_estimate=cost(12),
    )(grad_branch, w_out, ssm, gate, gain)


def input_kernel(grad_low, w_in, tokens, norm_gain, grad_result, out, sums):
    @pl.when(pl.program_id(0) == 0)
    def _():
        sums[...] = jnp.zeros_like(sums)

    x = tokens[...].astype(F32)
    inverse = lax.rsqrt(jnp.mean(x * x, axis=1, keepdims=True) + NORM_EPS)
    unit = x * inverse
    grad_hidden = dot(grad_low[...], w_in[...], NT)
    sums[...] += jnp.sum(grad_hidden * unit, axis=0, keepdims=True)
    pulled = grad_hidden * norm_gain[...]
    share = jnp.mean(pulled * unit, axis=1, keepdims=True)
    out[...] = grad_result[...] + inverse * (pulled - unit * share)


def input_backward(grad_low, w_in, tokens, norm_gain, grad_result):
    length = tokens.shape[0]
    rows = 256
    by_row = lambda width: pl.BlockSpec((rows, width), lambda i: (i, 0))
    whole = lambda v: pl.BlockSpec(v.shape, lambda i: (0,) * v.ndim)
    return pl.pallas_call(
        input_kernel,
        grid=(length // rows,),
        out_shape=(shape((length, D), F32), shape((1, D), F32)),
        in_specs=[by_row(WIDE), whole(w_in), by_row(D), whole(norm_gain), by_row(D)],
        out_specs=(by_row(D), pl.BlockSpec((1, D), lambda i: (0, 0))),
        compiler_params=params(),
        cost_estimate=cost(15),
    )(grad_low, w_in, tokens, norm_gain, grad_result)


def vector_kernel(tail, conv_sums, sums, skip_sums, norm_sums, gate_sums, gather, out, taps):
    tiles = CONVCH // LANES
    out[...] = jnp.zeros_like(out)
    out[0:TAIL_ROWS, :] = tail[...]
    for k in range(KCONV):
        for i in range(tiles):
            partial_sums = conv_sums[8 * k : 8 * k + 8, i * LANES : (i + 1) * LANES]
            taps[k * 16 + i : k * 16 + i + 1, :] = jnp.sum(partial_sums, axis=0, keepdims=True)
    row = lax.broadcasted_iota(jnp.int32, (LANES, LANES), 0)
    col = lax.broadcasted_iota(jnp.int32, (LANES, LANES), 1)
    per_tile = LANES // KCONV

    def exact(v, chosen):
        high = v.astype(BF16)
        rest = v - high.astype(F32)
        middle = rest.astype(BF16)
        low = (rest - middle.astype(F32)).astype(BF16)
        return dot(high, chosen) + (dot(middle, chosen) + dot(low, chosen))

    for q in range(KCONV):
        total = jnp.zeros((tiles, LANES), F32)
        for k in range(KCONV):
            chosen = (col == KCONV * (row % per_tile) + k) & (row // per_tile == q)
            total = total + exact(taps[k * 16 : k * 16 + tiles, :], chosen.astype(BF16))
        out[pl.ds(TAIL_ROWS + q, tiles, stride=KCONV), :] = total
    bias_at = TAIL_ROWS + tiles * KCONV
    for i in range(tiles):
        partial_sums = conv_sums[8 * KCONV :, i * LANES : (i + 1) * LANES]
        out[bias_at + i : bias_at + i + 1, :] = jnp.sum(partial_sums, axis=0, keepdims=True)
    lane = lax.broadcasted_iota(jnp.int32, (1, LANES), 1)
    skip = exact(jnp.broadcast_to(skip_sums[...], (8, INNER)), gather[...])[0:1, :]
    parts = [sums[0:1, :], sums[1:2, :], skip]
    parts = [jnp.where(lane < HEADS, v, 0.0) for v in parts]
    before = parts[0] + pltpu.roll(parts[1], HEADS, 1) + pltpu.roll(parts[2], 2 * HEADS, 1)
    at, shift = bias_at + tiles, 3 * HEADS
    for source in (norm_sums, gate_sums):
        for j in range(source.shape[1] // LANES):
            here = pltpu.roll(source[:, j * LANES : (j + 1) * LANES], shift, 1)
            out[at : at + 1, :] = jnp.where(lane < shift, before, here)
            before = here
            at += 1
    out[at : at + 1, :] = jnp.where(lane < shift, before, 0.0)


def pack_vectors(tail, conv_sums, sums, skip_sums, norm_sums, gate_sums, gather):
    return pl.pallas_call(
        vector_kernel,
        out_shape=shape(((NBLK - MID1) * BROWS, LANES), F32),
        in_specs=[VMEM] * 7,
        out_specs=VMEM,
        scratch_shapes=[pltpu.VMEM((KCONV * 16, LANES), F32)],
        compiler_params=params(),
    )(tail, conv_sums, sums, skip_sums, norm_sums, gate_sums, gather)


def body(tokens, teacher, lengths, loss_mask, owners, master, first_moment, second_moment):
    capacity = master.shape[0]
    dp, fsdp = lax.axis_size("dp"), lax.axis_size("fsdp")
    devices = dp * fsdp
    me = lax.axis_index(AXES).astype(jnp.int32)
    x_first, y_first, z_first = step_orders(dp, fsdp)
    tie = lambda *values: lax.optimization_barrier(values)

    sent = send_blocks(owners, master, devices, me)
    at_home = lax.all_to_all(sent, AXES, 0, 0, tiled=True)
    owners, tokens, loss_mask, _ = tie(owners, tokens, loss_mask, sent)
    plan = make_plan(owners, capacity, devices, me)
    streams = cut(even(plan["slots"], 3), (x_first, y_first, z_first))
    table = stream_places(plan["home"], plan["slot"], me, streams, devices)
    u0, u1 = plan["unit_slots"]
    sizes = [-(-u0 // 5)] * 4
    unit_streams = cut(sizes + [u0 - sum(sizes)], (x_first, y_first, x_first, y_first, z_first))
    unit_table = stream_places(plan["unit_home"], plan["unit_slot"], me, unit_streams, devices)
    unit_table = unit_table[:, :MID0]
    order1 = x_first[:2] + x_first[2 + bits_of(fsdp) :] + x_first[2 : 2 + bits_of(fsdp)]
    unit_table1 = place_of(plan["unit_home"] ^ me, order1) * (u1 + 1) + plan["unit_slot"]
    unit_table1 = unit_table1[:, MID0:MID1]
    inputs, target = tokens[0], teacher[0]
    at_home, table, received = tie(at_home, table, plan["received"])
    mine = pick_blocks(received, at_home, [size for _, size, _ in streams])
    parts = []
    for i, (values, (_, _, order)) in enumerate(zip(mine, streams)):
        steps = order[:0:-1]
        for k, step in enumerate(steps):
            if i == 0 and k == len(steps) - 1:
                (values, unit_table, unit_table1, back_table, row_from, row_block, row_used) = tie(
                    values, unit_table, unit_table1, plan["back"], plan["row_from"],
                    plan["row_block"], plan["row_used"],
                )
            values = doubled(values, step)
        parts += [values, exchange(values, order[0])]
    (input_weight, output_weight, conv_weight, conv_bias, dt_bias, a_log, skip, norm_gain,
     gate_gain, hidden, gate, conv_in, dt, ssm, mixed_out, states) = forward(
        table, inputs, parts
    )
    gather = heads_gather()
    block_out, grad_result, grad_branch, local = loss_part(
        lengths, mixed_out, output_weight, inputs, target, loss_mask
    )
    keep1, send1, head, tail = pack_out(
        unit_table1, mixed_out, grad_branch, local, devices, u1 + 1
    )
    grad_branch, send1 = tie(grad_branch, send1)
    got1 = exchange(send1, order1[0])
    grad_ssm, grad_gate, gain_sums = gate_part(grad_branch, output_weight, ssm, gate, gate_gain)
    grad_ssm, keep1, got1 = tie(grad_ssm, keep1, got1)
    keep1, got1 = reduce_step(keep1, got1, order1[1])
    grad_low, sums, skip_sums, conv_sums = backward(
        conv_in, dt, ssm, grad_ssm, grad_gate, states,
        conv_weight, conv_bias, dt_bias, a_log, skip, gather,
    )
    grad_low, keep1, got1 = tie(grad_low, keep1, got1)
    steps1 = order1[2:]
    for step in steps1[:1]:
        keep1, got1 = reduce_step(keep1, got1, step)
    halves = []
    for _, size, _ in unit_streams:
        halves += [devices * size // 2] * 2
    packed = list(pack_in(unit_table, hidden, grad_low, head, halves))
    packed[0], keep1, got1 = tie(packed[0], keep1, got1)
    kept = packed[::2]
    got = [exchange(v, order[0]) for v, (_, _, order) in zip(packed[1::2], unit_streams)]
    *got, grad_low, conv_sums, tail = tie(*got, grad_low, conv_sums, tail)
    for i, (_, _, order) in enumerate(unit_streams):
        kept[i], got[i] = reduce_step(kept[i], got[i], order[1])
    for step in steps1[1:2]:
        keep1, got1 = reduce_step(keep1, got1, step)
    input_grad, norm_sums = input_backward(grad_low, input_weight, inputs, norm_gain, grad_result)
    grad_vec = pack_vectors(tail, conv_sums, sums, skip_sums, norm_sums, gain_sums, gather)
    grad_vec = grad_vec.reshape((NBLK - MID1) * UNITS, UNIT, LANES)
    *got, got1, grad_vec, input_grad = tie(*got, got1, grad_vec, input_grad)
    for step in steps1[2:]:
        keep1, got1 = reduce_step(keep1, got1, step)
    for k in range(2, len(x_first)):
        for i, (_, _, order) in enumerate(unit_streams):
            if i == 0:
                kept[i], got[i], grad_vec = reduce_step(kept[i], got[i], order[k], grad_vec)
            else:
                kept[i], got[i] = reduce_step(kept[i], got[i], order[k])
    back = units_to_owners(back_table, list(zip(kept + [keep1], got + [got1])))
    back, grad_vec = tie(back, grad_vec)
    returned = lax.all_to_all(back, AXES, 0, 0, tiled=True)
    for step in x_first[:2]:
        grad_vec = grad_vec + exchange(grad_vec, step)
    local_sums = keep1[u1] + got1[u1]
    error_sum = jnp.sum(local_sums[: D // LANES])
    divisor = local_sums[D // LANES, 0] * D
    new_first, new_second, new_master = adam(
        row_from,
        row_block,
        row_used,
        divisor,
        returned,
        grad_vec,
        master,
        first_moment,
        second_moment,
    )
    mean_loss = error_sum / divisor
    return (block_out[None], input_grad[None], mean_loss, new_first, new_second, new_master)


def solution(mesh):
    return jax.shard_map(
        body,
        mesh=mesh,
        in_specs=(
            P(AXES, None, None),
            P(AXES, None, None),
            P(AXES),
            P(AXES, None),
            P(),
            P(AXES, None),
            P(AXES, None),
            P(AXES, None),
        ),
        out_specs=(
            P(AXES, None, None),
            P(AXES, None, None),
            P(),
            P(AXES, None),
            P(AXES, None),
            P(AXES, None),
        ),
        check_vma=False,
    )
```

```python
from functools import partial

import jax
import jax.numpy as jnp
import numpy as np
from jax import lax
from jax.experimental import pallas as pl
from jax.experimental.pallas import tpu as pltpu
from jax.sharding import PartitionSpec as P

D = 768
INNER = 1536
NSTATE = 128
HEADDIM = 64
KCONV = 4
SCAN_LEN = 256
PBLOCK = 4096
STEP = 10
HEADS = 24
CONVCH = 1792
PROJ = 3352
PTOT = 3765320
NBLK = 920

LANES = 128
BROWS = PBLOCK // LANES
UNIT = 8
UNITS = BROWS // UNIT
END_IN = D * PROJ
END_OUT = END_IN + INNER * D
MID0 = -(-END_IN // PBLOCK)
MID1 = END_OUT // PBLOCK
N0 = MID0 + NBLK - MID1
N1 = MID1 - MID0
F0_ROWS = N0 * BROWS
IN_ROWS = END_IN // LANES
HEAD_ROWS = MID0 * BROWS - IN_ROWS
TAIL_ROWS = (END_OUT - MID1 * PBLOCK) // LANES
OUT_ROWS = INNER * D // LANES
VEC_ROWS = (NBLK - MID1) * BROWS - TAIL_ROWS
VEC_AT = MID0 * BROWS + TAIL_ROWS
GROUP = 16
GROUPS = D // GROUP
GROUP_ROWS = GROUP * PROJ // LANES
COL_TILES = -(-PROJ // LANES)
WIDE = COL_TILES * LANES
OUT_TILES = D // LANES

NORM_EPS = 1e-05
ADAM_EPS = 1e-08
BETA_ONE = 0.9
BETA_TWO = 0.999
MATRIX_RATE = 0.03
VECTOR_RATE = 0.2
WEIGHT_DECAY = 0.1
PRECISE = lax.Precision.HIGHEST
AXES = ("dp", "fsdp")
VMEM_LIMIT = 60 * 1024 * 1024


def bits_of(count):
    return count.bit_length() - 1


def step_orders(dp, fsdp):
    wide = [("dp", i) for i in range(bits_of(dp))]
    narrow = [("fsdp", i) for i in range(bits_of(fsdp))]
    first = wide[:2] + narrow + wide[2:]
    second = wide[:1] + narrow + wide[1:]
    third = wide[:1] + wide[2:] + wide[1:2] + narrow
    return first, second, third


def cut(sizes, orders):
    streams, at = [], 0
    for size, order in zip(sizes, orders):
        if size:
            streams.append((at, size, order))
        at += size
    return streams


def even(total, parts):
    return [total // parts + (i < total % parts) for i in range(parts)]


def exchange(values, *steps):
    axes = {axis for axis, _ in steps}
    if len(axes) == 1:
        (axis,) = axes
        mask = sum(1 << bit for _, bit in steps)
        pairs = [(i, i ^ mask) for i in range(lax.axis_size(axis))]
        return lax.ppermute(values, axis, pairs)
    low = bits_of(lax.axis_size("fsdp"))
    mask = sum(1 << (bit + (low if axis == "dp" else 0)) for axis, bit in steps)
    count = lax.axis_size("dp") * lax.axis_size("fsdp")
    return lax.ppermute(values, AXES, [(i, i ^ mask) for i in range(count)])


def place_of(relative, order):
    shift_of = {"dp": bits_of(lax.axis_size("fsdp")), "fsdp": 0}
    place = jnp.zeros_like(relative)
    for axis, bit in order:
        place = place * 2 + ((relative >> (shift_of[axis] + bit)) & 1)
    return place


def class_counts(owners, devices):
    block = jnp.arange(NBLK, dtype=jnp.int32)
    mid = ((block >= MID0) & (block < MID1))[None, :]
    device = jnp.arange(devices, dtype=jnp.int32)
    below = owners[None, :] < device[:, None]
    owned = owners[None, :] == device[:, None]

    def total(mask):
        return jnp.sum(mask.astype(jnp.int32), axis=1)

    start = (total(below & ~mid), total(below & mid))
    count = (total(owned & ~mid), total(owned & mid))
    return start, count, total(owned & (block < MID0)[None, :])


def my_counts(owners, me):
    block = jnp.arange(NBLK, dtype=jnp.int32)
    mid = (block >= MID0) & (block < MID1)
    below, owned = owners < me, owners == me
    total = lambda mask: jnp.sum(mask.astype(jnp.int32))
    start = (total(below & ~mid), total(below & mid))
    count = (total(owned & ~mid), total(owned & mid))
    return start, count, total(owned & (block < MID0))


def pair_lanes(capacity, devices):
    return -(-capacity // devices)


def make_plan(owners, capacity, devices, me):
    block = jnp.arange(NBLK, dtype=jnp.int32)
    mid = (block >= MID0) & (block < MID1)
    same = mid[:, None] == mid[None, :]
    before = (owners[None, :] < owners[:, None]) | (
        (owners[None, :] == owners[:, None]) & (block[None, :] < block[:, None])
    )
    order = jnp.sum(before.astype(jnp.int32), axis=1)
    order_in_class = jnp.sum((same & before).astype(jnp.int32), axis=1)
    home, slot = order % devices, order // devices
    device = jnp.arange(devices, dtype=jnp.int32)
    start, count, _ = class_counts(owners, devices)
    my_start, my_count, my_early = my_counts(owners, me)
    pair = pair_lanes(capacity, devices)

    slots = -(-NBLK // devices)
    wanted = me + devices * jnp.arange(slots, dtype=jnp.int32)
    first = start[0] + start[1]
    ends = first + count[0] + count[1]
    owner = jnp.sum((ends[None, :] <= wanted[:, None]).astype(jnp.int32), axis=1)
    owner = jnp.minimum(owner, devices - 1)
    base = jnp.sum(jnp.where(device[None, :] == owner[:, None], first[None, :], 0), axis=1)
    received = owner * pair + jnp.clip((wanted - base) // devices, 0, pair - 1)

    back_pair = (UNITS * capacity + 2 * (devices - 1)) // devices
    unit_slots = (-(-UNITS * N0 // devices), -(-UNITS * N1 // devices))
    lane = jnp.arange(back_pair, dtype=jnp.int32)

    def units_back(kind):
        turn = lane if kind == 0 else back_pair - 1 - lane
        first = UNITS * start[kind][:, None]
        k = (me - first) % devices + turn[None, :] * devices
        return k < UNITS * count[kind][:, None], (first + k) // devices

    valid0, slot0 = units_back(0)
    valid1, slot1 = units_back(1)
    back = jnp.where(valid0, slot0, jnp.where(valid1, unit_slots[0] + slot1, 0)).reshape(-1)

    row = jnp.arange(capacity, dtype=jnp.int32)
    is_mid = (row >= my_early) & (row < my_early + my_count[1])
    k = jnp.where(is_mid, row - my_early, jnp.where(row < my_early, row, row - my_count[1]))
    first = UNITS * jnp.where(is_mid, my_start[1], my_start[0])
    row_used = row < my_count[0] + my_count[1]
    mine = (owners == me)[None, :]
    rank = jnp.sum((mine & (block[None, :] < block[:, None])).astype(jnp.int32), axis=1)
    row_block = jnp.sum(
        jnp.where(mine & (rank[None, :] == row[:, None]), block[None, :], 0), axis=1
    )
    row_from = []
    for u in range(UNITS):
        unit = UNITS * k + u
        turn = unit // devices
        at = ((first + unit) % devices) * back_pair + jnp.where(is_mid, back_pair - 1 - turn, turn)
        late = devices * back_pair + UNITS * (row_block - MID1) + u
        at = jnp.where(row_block >= MID1, late, at)
        row_from.append(jnp.where(row_used, at, 0))
    return dict(
        home=home, slot=slot, slots=slots,
        received=received, order=order_in_class,
        unit_slots=unit_slots, back=back, row_from=quarters(row_from),
        row_used=row_used, row_block=row_block,
    )


def quarters(tables):
    width = -(-tables[0].shape[0] // LANES) * LANES
    return jnp.concatenate([jnp.pad(t, (0, width - t.shape[0])) for t in tables])


def stream_places(home, slot, me, streams, devices):
    relative = home ^ me
    place = jnp.zeros_like(slot)
    for begin, size, order in streams:
        inside = (slot >= begin) & (slot < begin + size)
        at = devices * begin + place_of(relative, order) * size + slot - begin
        place = jnp.where(inside, at, place)
    return place


def cost(microseconds):
    return pl.CostEstimate(
        flops=int(microseconds * 1e9), bytes_accessed=int(microseconds * 3e6), transcendentals=0
    )


ANY = pl.BlockSpec(memory_space=pl.ANY)
VMEM = pl.BlockSpec(memory_space=pltpu.VMEM)
SMEM = pl.BlockSpec(memory_space=pltpu.SMEM)


def params(**extra):
    return pltpu.CompilerParams(vmem_limit_bytes=VMEM_LIMIT, **extra)


def shape(dims, dtype):
    return jax.ShapeDtypeStruct(dims, dtype)


def send_kernel(my_index, owners, master, out, flat, *, devices):
    capacity = master.shape[0]
    me = my_index[0]
    for j in range(BROWS):
        flat[pl.ds(j, capacity, stride=BROWS), :] = master[:, j * LANES : (j + 1) * LANES]
    held = owners[...]
    below, owned = held < me, held == me

    def total(mask):
        return jnp.sum(jnp.where(mask, 1.0, 0.0)).astype(jnp.int32)

    start, count = total(below), total(owned)
    pair = out.shape[0] // devices

    def step(home, carry):
        for s in range(pair):
            k = lax.rem(home - start + devices * NBLK, devices) + s * devices
            row = jnp.where(k < count, k, 0)
            rows = pl.ds(pl.multiple_of(row * BROWS, BROWS), BROWS)
            out[home * pair + s] = flat[rows, :].astype(out.dtype)
        return carry

    lax.fori_loop(0, devices, step, 0)


def send_blocks(owners, master, devices, me):
    rows = -(-NBLK // (8 * LANES)) * 8
    held = jnp.pad(owners, (0, rows * LANES - NBLK), constant_values=1 << 20).reshape(rows, LANES)
    count = devices * pair_lanes(master.shape[0], devices)
    return pl.pallas_call(
        partial(send_kernel, devices=devices),
        out_shape=shape((count, BROWS, LANES), jnp.bfloat16),
        in_specs=[SMEM, VMEM, VMEM],
        out_specs=VMEM,
        scratch_shapes=[pltpu.VMEM((master.shape[0] * BROWS, LANES), jnp.float32)],
        compiler_params=params(),
    )(me.reshape(1), held, master)


def pick_kernel(table, source, *outs):
    at = 0
    for out in outs:

        def step(i, carry, out=out, at=at):
            out[i] = source[table[at + i]]
            return carry

        lax.fori_loop(0, out.shape[0], step, 0)
        at += out.shape[0]


def pick_blocks(table, source, sizes):
    return pl.pallas_call(
        pick_kernel,
        out_shape=tuple(shape((n,) + source.shape[1:], source.dtype) for n in sizes),
        in_specs=[SMEM, VMEM],
        out_specs=(VMEM,) * len(sizes),
        compiler_params=params(),
    )(table, source)


def back_kernel(table, *refs, sizes):
    sources, (out, held) = refs[:-2], refs[-2:]
    at = i = 0
    for size in sizes:
        n = sources[i].shape[0]
        total = sources[i][...]
        for k in range(1, size):
            total = total + sources[i + k][0:n]
        held[at : at + n] = total
        at += n
        i += size

    def step(i, carry):
        for u in range(8):
            out[i * 8 + u] = held[table[i * 8 + u]]
        return carry

    total = out.shape[0]
    lax.fori_loop(0, total // 8, step, 0)


def units_to_owners(table, groups):
    return pl.pallas_call(
        partial(back_kernel, sizes=[len(g) for g in groups]),
        out_shape=shape((table.shape[0], UNIT, LANES), jnp.float32),
        in_specs=[SMEM] + [VMEM] * sum(len(g) for g in groups),
        out_specs=VMEM,
        scratch_shapes=[pltpu.VMEM((sum(g[0].shape[0] for g in groups), UNIT, LANES), jnp.float32)],
        compiler_params=params(),
    )(table, *[v for g in groups for v in g])


def row_start(rho):
    return (PROJ * rho) // LANES, (PROJ * rho) % LANES


def copy_all(pairs, sem):
    copies = [pltpu.make_async_copy(a, b, sem.at[i]) for i, (a, b) in enumerate(pairs)]
    for c in copies:
        c.start()
    for c in copies:
        c.wait()


def spread_blocks(table, first, held, flat, count, first_row):
    def one(i):
        at = pl.multiple_of(first_row + i * BROWS, 16)
        flat[pl.ds(at, BROWS), :] = held[table[first + i]].astype(jnp.float32)

    def step(i, carry):
        for u in range(4):
            one(i * 4 + u)
        return carry

    lax.fori_loop(0, count // 4, step, 0)
    for i in range(count // 4 * 4, count):
        one(i)


def unpack_vectors(flat, conv_weight, conv_bias, dt_bias, a_log, skip, norm_gain, gate_gain):
    bf16, f32 = jnp.bfloat16, jnp.float32
    tiles = CONVCH // LANES
    row = lax.broadcasted_iota(jnp.int32, (LANES, LANES), 0)
    col = lax.broadcasted_iota(jnp.int32, (LANES, LANES), 1)
    per_tile = LANES // KCONV
    for k in range(KCONV):
        total = jnp.zeros((tiles, LANES), f32)
        for q in range(KCONV):
            rows = flat[pl.ds(VEC_AT + q, tiles, stride=KCONV), :].astype(bf16)
            chosen = (row == KCONV * (col % per_tile) + k) & (col // per_tile == q)
            total = total + jnp.dot(rows, chosen.astype(bf16), preferred_element_type=f32)
        for i in range(tiles):
            conv_weight[k : k + 1, i * LANES : (i + 1) * LANES] = total[i : i + 1, :]
    bias_at = VEC_AT + tiles * KCONV
    for i in range(tiles):
        conv_bias[:, i * LANES : (i + 1) * LANES] = flat[bias_at + i : bias_at + i + 1, :]
    at = bias_at + tiles
    lane = lax.broadcasted_iota(jnp.int32, (8, LANES), 1)
    first = flat[at : at + 8, :]
    three = []
    for i in range(3):
        moved = pltpu.roll(first, LANES - i * HEADS, 1) if i else first
        three.append(jnp.where(lane < HEADS, moved, 0.0))
    dt_bias[...] = three[0][0:1, :]
    a_log[...] = three[1][0:1, :]
    for j in range(INNER // LANES):
        h = lax.broadcasted_iota(jnp.int32, (LANES, LANES), 0)
        c = lax.broadcasted_iota(jnp.int32, (LANES, LANES), 1) + j * LANES
        spread = (h == c // HEADDIM).astype(bf16)
        wide = jnp.dot(three[2].astype(bf16), spread, preferred_element_type=f32)
        skip[:, j * LANES : (j + 1) * LANES] = wide[0:1, :]
    shift = 3 * HEADS
    for out, begin, width in ((norm_gain, at, D), (gate_gain, at + D // LANES, INNER)):
        for j in range(width // LANES):
            x = pltpu.roll(flat[begin + j : begin + j + 1, :], LANES - shift, 1)
            y = pltpu.roll(flat[begin + j + 1 : begin + j + 2, :], LANES - shift, 1)
            out[:, j * LANES : (j + 1) * LANES] = jnp.where(lane[0:1] < LANES - shift, x, y)


def unpack_weights(table, parts, w_in, w_out, vectors, held, flat, flat_out, tile, sem):
    pairs, at = [], 0
    for part in parts:
        pairs.append((part, held.at[pl.ds(at, part.shape[0])]))
        at += part.shape[0]
    copy_all(pairs, sem)
    spread_blocks(table, 0, held, flat, MID0, 0)
    spread_blocks(table, MID1, held, flat, NBLK - MID1, MID0 * BROWS)
    spread_blocks(table, MID0, held, flat_out, N1, HEAD_ROWS)
    flat_out[0:HEAD_ROWS, :] = flat[IN_ROWS : IN_ROWS + HEAD_ROWS, :]
    flat_out[OUT_ROWS - TAIL_ROWS :, :] = flat[MID0 * BROWS : MID0 * BROWS + TAIL_ROWS, :]
    unpack_vectors(flat, *vectors)
    rows = 128

    def out_step(i, carry):
        at = pl.multiple_of(i * rows, rows)
        for j in range(OUT_TILES):
            x = flat_out[pl.ds(at * OUT_TILES + j, rows, stride=OUT_TILES), :]
            w_out[pl.ds(at, rows), j * LANES : (j + 1) * LANES] = x.astype(jnp.bfloat16)
        return carry

    lax.fori_loop(0, INNER // rows, out_step, 0)
    lane = lax.broadcasted_iota(jnp.int32, (GROUPS, LANES), 1)

    def columns(j):
        for rho in range(GROUP):
            c, s = row_start(rho)
            x = flat[pl.ds(c + j, GROUPS, stride=GROUP_ROWS), :]
            if s:
                y = flat[pl.ds(c + j + 1, GROUPS, stride=GROUP_ROWS), :]
                x = jnp.where(
                    lane < LANES - s,
                    pltpu.roll(x, LANES - s, 1),
                    pltpu.roll(y, LANES - s, 1),
                )
            tile[pl.ds(rho, GROUPS, stride=GROUP), :] = x

    def step(j, carry):
        columns(j)
        w_in[:, pl.ds(pl.multiple_of(j * LANES, LANES), LANES)] = tile[...].astype(jnp.bfloat16)
        return carry

    lax.fori_loop(0, COL_TILES - 1, step, 0)
    columns(COL_TILES - 1)
    last = (COL_TILES - 1) * LANES
    inside = lax.broadcasted_iota(jnp.int32, (D, LANES), 1) < PROJ - last
    w_in[:, last:] = jnp.where(inside, tile[...], 0.0).astype(jnp.bfloat16)


def unpack_scratch(held, count):
    return [
        pltpu.VMEM((held, BROWS, LANES), jnp.bfloat16),
        pltpu.VMEM((F0_ROWS, LANES), jnp.float32),
        pltpu.VMEM((OUT_ROWS, LANES), jnp.float32),
        pltpu.VMEM((D, LANES), jnp.float32),
        pltpu.SemaphoreType.DMA((count,)),
    ]


def permute_units(table, flat, count, first_row, staged):
    many = 4
    width = table.shape[0] // UNITS

    def one(i):
        for u in range(UNITS):
            at = first_row + i * BROWS + u * UNIT
            at = at if isinstance(at, int) else pl.multiple_of(at, UNIT)
            staged[table[u * width + i]] = flat[pl.ds(at, UNIT), :]

    def step(i, carry):
        for b in range(many):
            one(i * many + b)
        return carry

    lax.fori_loop(0, count // many, step, 0)
    for i in range(count // many * many, count):
        one(i)


def pack_in_kernel(table, hidden, grad, head, *refs):
    outs, (turned, tiles, flat, staged, sem) = refs[:-5], refs[-5:]
    turned[...] = hidden[...].T
    lane = lax.broadcasted_iota(jnp.int32, (GROUPS, LANES), 1)

    def product(p, count):
        at = p * 2 * LANES
        at = at if isinstance(at, int) else pl.multiple_of(at, 2 * LANES)
        return jnp.dot(
            turned[...], grad[:, pl.ds(at, count * LANES)], preferred_element_type=jnp.float32
        )

    def put(p, value):
        for k in range(value.shape[1] // LANES):
            at = (p * 2 + k) * D
            at = at if isinstance(at, int) else pl.multiple_of(at, D)
            tiles[pl.ds(at, D), :] = value[:, k * LANES : (k + 1) * LANES]

    def load(rho, j):
        return tiles[pl.ds(j * D + rho, GROUPS, stride=GROUP), :]

    def whole(rho, i):
        first = -(-PROJ * rho // LANES)
        col0 = first * LANES - PROJ * rho
        x = load(rho, i)
        if col0:
            x = jnp.where(
                lane < LANES - col0,
                pltpu.roll(x, LANES - col0, 1),
                pltpu.roll(load(rho, i + 1), LANES - col0, 1),
            )
        flat[pl.ds(first + i, GROUPS, stride=GROUP_ROWS), :] = x

    put(0, product(0, 2))
    put(1, product(1, 2))
    pairs = COL_TILES // 2

    def step(p, carry):
        for i in range(2):
            for rho in range(GROUP):
                whole(rho, p * 2 + i)
        put(p + 2, product(p + 2, 2))
        return carry

    lax.fori_loop(0, pairs - 2, step, 0)
    put(pairs, product(pairs, COL_TILES % 2))
    for rho in range(GROUP):
        first = -(-PROJ * rho // LANES)
        col0 = first * LANES - PROJ * rho
        full = (PROJ - col0) // LANES
        for i in range((pairs - 2) * 2, full):
            whole(rho, i)
        left = PROJ - col0 - full * LANES
        if left:
            begin = col0 + full * LANES
            j, s = begin // LANES, begin % LANES
            x = pltpu.roll(load(rho, j), LANES - s, 1) if s else load(rho, j)
            if s + left > LANES:
                x = jnp.where(lane < LANES - s, x, pltpu.roll(load(rho, j + 1), LANES - s, 1))
            y = pltpu.roll(load(rho + 1, 0), left, 1)
            flat[pl.ds(first + full, GROUPS, stride=GROUP_ROWS), :] = jnp.where(lane < left, x, y)
    flat[IN_ROWS : IN_ROWS + HEAD_ROWS, :] = head[...]
    permute_units(table, flat, MID0, 0, staged)
    copies, at = [], 0
    for out in outs:
        copies.append((staged.at[pl.ds(at, out.shape[0])], out))
        at += out.shape[0]
    copy_all(copies, sem)


def pack_in(table, hidden, grad, head, sizes):
    return pl.pallas_call(
        pack_in_kernel,
        out_shape=tuple(shape((n, UNIT, LANES), jnp.float32) for n in sizes),
        in_specs=[SMEM, VMEM, VMEM, VMEM],
        out_specs=(ANY,) * len(sizes),
        scratch_shapes=[
            pltpu.VMEM((D, hidden.shape[0]), jnp.bfloat16),
            pltpu.VMEM((COL_TILES * D, LANES), jnp.float32),
            pltpu.VMEM((MID0 * BROWS, LANES), jnp.float32),
            pltpu.VMEM((sum(sizes), UNIT, LANES), jnp.float32),
            pltpu.SemaphoreType.DMA((len(sizes),)),
        ],
        compiler_params=params(),
        cost_estimate=cost(20),
    )(table, hidden, grad, head)


def pack_out_kernel(
    table, mixed_out, grad, local, keep, send, head, tail, turned, flat, out, sem, *, slots
):
    rows = 256

    def step(i, carry):
        at = pl.multiple_of(i * rows, rows)
        turned[...] = mixed_out[:, pl.ds(at, rows)].T
        product = jnp.dot(turned[...], grad[...], preferred_element_type=jnp.float32)
        for j in range(OUT_TILES):
            flat[pl.ds(at * OUT_TILES + j, rows, stride=OUT_TILES), :] = product[
                :, j * LANES : (j + 1) * LANES
            ]
        return carry

    lax.fori_loop(0, INNER // rows, step, 0)
    head[...] = flat[0:HEAD_ROWS, :]
    tail[...] = flat[OUT_ROWS - TAIL_ROWS : OUT_ROWS, :]
    permute_units(table, flat, N1, HEAD_ROWS, out)

    def add_local(i, carry):
        out[i * slots + slots - 1] = local[...]
        return carry

    lax.fori_loop(0, out.shape[0] // slots, add_local, 0)
    half = keep.shape[0]
    copy_all([(out.at[pl.ds(0, half)], keep), (out.at[pl.ds(half, half)], send)], sem)


def pack_out(table, mixed_out, grad, local, devices, slots):
    return pl.pallas_call(
        partial(pack_out_kernel, slots=slots),
        out_shape=(
            shape((devices * slots // 2, UNIT, LANES), jnp.float32),
            shape((devices * slots // 2, UNIT, LANES), jnp.float32),
            shape((HEAD_ROWS, LANES), jnp.float32),
            shape((TAIL_ROWS, LANES), jnp.float32),
        ),
        in_specs=[SMEM, VMEM, VMEM, VMEM],
        out_specs=(ANY, ANY, VMEM, VMEM),
        scratch_shapes=[
            pltpu.VMEM((256, mixed_out.shape[0]), jnp.bfloat16),
            pltpu.VMEM((OUT_ROWS, LANES), jnp.float32),
            pltpu.VMEM((devices * slots, UNIT, LANES), jnp.float32),
            pltpu.SemaphoreType.DMA((2,)),
        ],
        compiler_params=params(),
    )(table, mixed_out, grad, local)


def adam_kernel(
    table, row_block, row_used, scale, got, late, master, first, second,
    o_first, o_second, o_master, flat, held, limit, used,
):
    capacity = master.shape[0]

    def step(i, carry):
        for u in range(UNITS):
            at = table[u * (table.shape[0] // UNITS) + i]
            rows = pl.ds(pl.multiple_of(i * BROWS + u * UNIT, UNIT), UNIT)
            flat[rows, :] = held[at]
        limit[pl.ds(i, 1), :] = jnp.full((1, LANES), END_OUT - row_block[i] * PBLOCK, jnp.int32)
        used[pl.ds(i, 1), :] = jnp.full((1, LANES), row_used[i], jnp.int32)
        return carry

    held[0 : got.shape[0]] = got[...]
    held[got.shape[0] :] = late[...]
    lax.fori_loop(0, capacity, step, 0)
    lane = lax.broadcasted_iota(jnp.int32, (capacity, LANES), 1)
    divisor = scale[0]
    for j in range(BROWS):
        cols = slice(j * LANES, (j + 1) * LANES)
        grad = jnp.where(used[...] > 0, flat[pl.ds(j, capacity, stride=BROWS), :], 0.0) / divisor
        matrix = lane + j * LANES < limit[...]
        weights = master[:, cols]
        new_first = BETA_ONE * first[:, cols] + (1.0 - BETA_ONE) * grad
        new_second = BETA_TWO * second[:, cols] + (1.0 - BETA_TWO) * grad * grad
        normal = (
            new_first
            / (1.0 - BETA_ONE**STEP)
            / (jnp.sqrt(new_second / (1.0 - BETA_TWO**STEP)) + ADAM_EPS)
        )
        rate = jnp.where(matrix, MATRIX_RATE, VECTOR_RATE)
        decay = jnp.where(matrix, WEIGHT_DECAY, 0.0)
        o_first[:, cols] = new_first
        o_second[:, cols] = new_second
        o_master[:, cols] = weights - rate * (normal + decay * weights)


def adam(table, row_block, row_used, divisor, got, late, master, first, second):
    capacity = master.shape[0]
    return pl.pallas_call(
        adam_kernel,
        out_shape=(shape(master.shape, jnp.float32),) * 3,
        in_specs=[SMEM] * 4 + [VMEM] * 5,
        out_specs=(VMEM,) * 3,
        scratch_shapes=[
            pltpu.VMEM((capacity * BROWS, LANES), jnp.float32),
            pltpu.VMEM((got.shape[0] + late.shape[0], UNIT, LANES), jnp.float32),
            pltpu.VMEM((capacity, LANES), jnp.int32),
            pltpu.VMEM((capacity, LANES), jnp.int32),
        ],
        compiler_params=params(),
    )(
        table, row_block, row_used.astype(jnp.int32), divisor.reshape(1), got, late, master, first, second
    )


def doubled(values, step):
    return jnp.concatenate([values, exchange(values, step)], axis=0)


def gather_steps(values, order):
    for step in order[:0:-1]:
        values = doubled(values, step)
    return values, exchange(values, order[0])


def reduce_step(kept, got, step, extra=None):
    half = kept.shape[0] // 2
    given = kept[half:] + got[half:]
    if extra is None:
        return kept[:half] + got[:half], exchange(given, step)
    arrived = exchange(jnp.concatenate([given, extra]), step)
    return kept[:half] + got[:half], arrived[:half], extra + arrived[half:]


CHUNK = 128
PAIRS = HEADS // 2
MIXW = INNER + 2 * NSTATE
DT_AT = INNER + CONVCH
F32 = jnp.float32
BF16 = jnp.bfloat16
NN = (((1,), (0,)), ((), ()))
NT = (((1,), (1,)), ((), ()))


def dot(a, b, dims=NN):
    return lax.dot_general(a, b, dims, preferred_element_type=F32)


def split(v):
    high = v.astype(BF16)
    return high, (v - high.astype(F32)).astype(BF16)


def dot3(a, b, dims=NN):
    ah, al = a
    bh, bl = b
    return dot(ah, bh, dims) + (dot(ah, bl, dims) + dot(al, bh, dims))


def heads_gather():
    return jnp.asarray(np.repeat(np.eye(HEADS, LANES, dtype=np.float32), HEADDIM, axis=0), BF16)


def three_parts(v):
    high = v.astype(BF16).astype(F32)
    rest = v - high
    middle = rest.astype(BF16).astype(F32)
    low = rest - middle
    return (high + pltpu.roll(middle, 32, 1) + pltpu.roll(low, 64, 1)).astype(BF16)


def triangle_sum(tri, v):
    parts = dot(tri, three_parts(v))
    lane = lax.broadcasted_iota(jnp.int32, parts.shape, 1)
    total = parts + pltpu.roll(parts, LANES - 32, 1) + pltpu.roll(parts, LANES - 64, 1)
    return jnp.where(lane < HEADS, total, 0.0)


def chunk_decays(dt, dt_bias, a_log):
    lane = lax.broadcasted_iota(jnp.int32, (CHUNK, LANES), 1)
    row = lax.broadcasted_iota(jnp.int32, (CHUNK, LANES), 0)
    shifted = dt + dt_bias
    delta = jnp.where(
        lane < HEADS, jnp.maximum(shifted, 0.0) + jnp.log1p(jnp.exp(-jnp.abs(shifted))), 0.0
    )
    rate = -jnp.exp(a_log)
    lower = (row >= lane).astype(BF16)
    cum = triangle_sum(lower, delta * rate)
    last = cum[CHUNK - 1 : CHUNK, :]
    return shifted, delta, rate, cum, last


def pair_mask():
    lane = lax.broadcasted_iota(jnp.int32, (CHUNK, LANES), 1)
    low = (lane < HEADDIM).astype(F32)
    return low.astype(BF16), (1.0 - low).astype(BF16)


QUADS = HEADS // 4
QWIDTH = 4 * HEADDIM


def sigmoid(v):
    return 0.5 * jnp.tanh(0.5 * v) + 0.5


def silu(v):
    return v * sigmoid(v)


def side_by_side(v):
    high, low = split(v)
    return jnp.concatenate([high, low], axis=1), high


def dot_parts(a, b):
    ahl, ah = a
    bh, bl = b
    return dot(ahl, jnp.concatenate([bh, bh], axis=0)) + dot(ah, bl)


def dot_turned(a, b):
    ah, al = a
    bh, bl = b
    both = dot(ah, jnp.concatenate([bh, bl], axis=0), NT)
    n = bh.shape[0]
    return both[:, :n] + both[:, n:] + dot(al, bh, NT)


def widen(delta, cum, quad):
    lane = lax.broadcasted_iota(jnp.int32, (CHUNK, LANES), 1)
    over = lambda v, h: jnp.broadcast_to(v[:, h : h + 1], (CHUNK, LANES))
    first = 4 * quad
    columns = [over(cum, first + k) for k in range(4)]
    rates = [over(delta, first + k) for k in range(4)]
    pair = lambda vs: jnp.concatenate(
        [jnp.where(lane < HEADDIM, vs[0], vs[1]), jnp.where(lane < HEADDIM, vs[2], vs[3])], axis=1
    )
    return pair(rates), pair(columns), columns


def pair_rows(parts, j, low, high):
    cols = slice(j * LANES, (j + 1) * LANES)
    return [jnp.concatenate([p[:, cols] * low, p[:, cols] * high], axis=0) for p in parts]


def scan_chunk(mixed, dt, dt_bias, a_log, skip, state, put):
    _, delta, _, cum, last = chunk_decays(dt, dt_bias, a_log)
    lane = lax.broadcasted_iota(jnp.int32, (CHUNK, LANES), 1)
    row = lax.broadcasted_iota(jnp.int32, (CHUNK, LANES), 0)
    bias = jnp.where(row >= lane, 0.0, -1e30)
    cum_t = cum.T
    inputs_b = mixed[:, INNER : INNER + NSTATE]
    readout = mixed[:, INNER + NSTATE :]
    affinity = dot3(split(readout), split(inputs_b), NT)
    readout_parts = side_by_side(readout)
    b_parts = side_by_side(inputs_b.T)
    low, high = pair_mask()
    for quad in range(QUADS):
        cols = slice(quad * QWIDTH, (quad + 1) * QWIDTH)
        wide_delta, wide_cum, columns = widen(delta, cum, quad)
        values = mixed[:, cols]
        scaled = values * wide_delta
        parts = split(scaled)
        outs = []
        for j in range(2):
            right_h, right_l = pair_rows(parts, j, low, high)
            left = []
            for k in range(2):
                h = 4 * quad + 2 * j + k
                within = jnp.exp(columns[2 * j + k] - cum_t[h : h + 1, :] + bias)
                left.append(split(affinity * within))
            left_h = jnp.concatenate([left[0][0], left[1][0]], axis=1)
            left_l = jnp.concatenate([left[0][1], left[1][1]], axis=1)
            both = dot(left_h, jnp.concatenate([right_h, right_l], axis=1))
            outs.append(both[:, :LANES] + both[:, LANES:] + dot(left_l, right_h))
        carried = state[:, cols]
        grown = jnp.exp(wide_cum)
        out = jnp.concatenate(outs, axis=1) + dot_parts(readout_parts, split(carried)) * grown
        tail = jnp.exp(wide_cum[CHUNK - 1 :] - wide_cum)
        state[:, cols] = carried * grown[CHUNK - 1 :] + dot_parts(b_parts, split(scaled * tail))
        put(quad, out + skip[:, cols] * values)


FORWARD_ROWS = 2 * CHUNK


def forward_kernel(table, tokens, *refs, count):
    parts, refs = refs[:count], refs[count:]
    (w_in_kept, w_out_kept, conv_weight, conv_bias, dt_bias, a_log, skip, norm_gain, gain,
     hidden, gate, conv_in, dt, ssm, mixed_out, states) = refs[:16]
    w_in, w_out, state, before, mixed, shift, out_sem, *scratch = refs[16:]
    keep = [
        pltpu.make_async_copy(w_in, w_in_kept, out_sem.at[0]),
        pltpu.make_async_copy(w_out, w_out_kept, out_sem.at[1]),
    ]

    @pl.when(pl.program_id(0) == 0)
    def _():
        vectors = (conv_weight, conv_bias, dt_bias, a_log, skip, norm_gain, gain)
        unpack_weights(table, parts, w_in, w_out, vectors, *scratch)
        for copy in keep:
            copy.start()
        state[...] = jnp.zeros_like(state)
        before[...] = jnp.zeros_like(before)

    x = tokens[...].astype(F32)
    inverse = lax.rsqrt(jnp.mean(x * x, axis=1, keepdims=True) + NORM_EPS)
    h = (x * inverse * norm_gain[...]).astype(BF16)
    hidden[...] = h
    dt[...] = dot(h, w_in[:, DT_AT:])
    wide = 2 * LANES
    for tile in range(CONVCH // wide):
        at = tile * wide
        product = dot(h, w_in[:, INNER + at : INNER + at + wide])
        conv_in[:, at : at + wide] = product
        for half in range(2):
            cols = slice(at + half * LANES, at + (half + 1) * LANES)
            rows = product[:, half * LANES : (half + 1) * LANES]
            earlier = before[:, cols]
            terms = moved_down(shift.at[tile * 2 + half], rows, earlier) + [rows]
            before[:, cols] = rows[FORWARD_ROWS - 8 :]
            mixed[:, cols] = silu(conv_sum(terms, conv_weight[:, cols], conv_bias[:, cols]))
    for tile in range(INNER // wide):
        cols = slice(tile * wide, (tile + 1) * wide)
        gate[:, cols] = dot(h, w_in[:, cols])
    for sub in range(FORWARD_ROWS // CHUNK):
        rows = slice(sub * CHUNK, (sub + 1) * CHUNK)
        states[sub] = state[...]
        squares = [jnp.zeros((CHUNK, LANES), F32)]

        def put(quad, out, rows=rows, squares=squares):
            cols = slice(quad * QWIDTH, (quad + 1) * QWIDTH)
            ssm[rows, cols] = out
            gated = out * silu(gate[rows, cols])
            first, second = gated[:, :LANES], gated[:, LANES:]
            squares[0] = squares[0] + first * first + second * second

        scan_chunk(
            mixed[rows, :], dt[rows, :], dt_bias[...], a_log[...], skip, state, put
        )
        rho = lax.rsqrt(jnp.sum(squares[0], axis=1, keepdims=True) * (1.0 / INNER) + NORM_EPS)
        for j in range(PAIRS):
            cols = slice(j * LANES, (j + 1) * LANES)
            gated = ssm[rows, cols] * silu(gate[rows, cols])
            mixed_out[rows, cols] = (gated * rho * gain[:, cols]).astype(BF16)

    @pl.when(pl.program_id(0) == pl.num_programs(0) - 1)
    def _():
        for copy in keep:
            copy.wait()


def forward(table, tokens, parts):
    length = tokens.shape[0]
    by_row = lambda width: pl.BlockSpec((FORWARD_ROWS, width), lambda i: (i, 0))
    per_step = FORWARD_ROWS // CHUNK
    vectors = [(KCONV, CONVCH), (1, CONVCH), (1, LANES), (1, LANES), (1, INNER), (1, D), (1, INNER)]
    return pl.pallas_call(
        partial(forward_kernel, count=len(parts)),
        grid=(length // FORWARD_ROWS,),
        out_shape=[shape((D, WIDE), BF16), shape((INNER, D), BF16)]
        + [shape(v, F32) for v in vectors]
        + [
            shape((length, D), BF16),
            shape((length, INNER), F32),
            shape((length, MIXW), F32),
            shape((length, LANES), F32),
            shape((length, INNER), F32),
            shape((length, INNER), BF16),
            shape((length // CHUNK, NSTATE, INNER), F32),
        ],
        in_specs=[SMEM, by_row(D)] + [ANY] * len(parts),
        out_specs=[ANY, ANY]
        + [pl.BlockSpec(v, lambda i: (0, 0)) for v in vectors]
        + [
            by_row(D),
            by_row(INNER),
            by_row(MIXW),
            by_row(LANES),
            by_row(INNER),
            by_row(INNER),
            pl.BlockSpec((per_step, NSTATE, INNER), lambda i: (i, 0, 0)),
        ],
        scratch_shapes=[
            pltpu.VMEM((D, WIDE), BF16),
            pltpu.VMEM((INNER, D), BF16),
            pltpu.VMEM((NSTATE, INNER), F32),
            pltpu.VMEM((8, MIXW), F32),
            pltpu.VMEM((FORWARD_ROWS, MIXW), F32),
            pltpu.VMEM((MIXW // LANES, FORWARD_ROWS + 8, LANES), F32),
            pltpu.SemaphoreType.DMA((2,)),
        ]
        + unpack_scratch(sum(part.shape[0] for part in parts), len(parts)),
        compiler_params=params(),
        cost_estimate=cost(50),
    )(table, tokens, *parts)


def eights(v):
    return jnp.sum(v.reshape(v.shape[0] // 8, 8, v.shape[1]), axis=0)


def backward_kernel(
    conv_in, earlier, dt, ssm, grad, grad_gate, states, conv_weight, conv_bias, dt_bias, a_log, skip,
    gather, grad_low, sums, skip_sums, conv_sums,
    grad_state, to_sum, mixed, slope, grad_mixed, following, shift,
):
    @pl.when(pl.program_id(0) == 0)
    def _():
        grad_state[...] = jnp.zeros_like(grad_state)
        sums[...] = jnp.zeros_like(sums)
        skip_sums[...] = jnp.zeros_like(skip_sums)
        conv_sums[...] = jnp.zeros_like(conv_sums)
        following[...] = jnp.zeros_like(following)

    begins = pl.program_id(0) == pl.num_programs(0) - 1

    for tile in range(MIXW // LANES):
        cols = slice(tile * LANES, (tile + 1) * LANES)
        rows = conv_in[:, cols]
        before = jnp.where(begins, 0.0, earlier[:, cols])
        terms = moved_down(shift.at[tile], rows, before) + [rows]
        value = conv_sum(terms, conv_weight[:, cols], conv_bias[:, cols])
        sig = sigmoid(value)
        mixed[:, cols] = value * sig
        slope[:, cols] = sig * (1.0 + value * (1.0 - sig))

    shifted, delta, rate, cum, last = chunk_decays(dt[...], dt_bias[...], a_log[...])
    lane = lax.broadcasted_iota(jnp.int32, (CHUNK, LANES), 1)
    row = lax.broadcasted_iota(jnp.int32, (CHUNK, LANES), 0)
    bias = jnp.where(lane >= row, 0.0, -1e30)
    heads = lane < HEADS
    cum_t = cum.T
    inputs_b = mixed[:, INNER : INNER + NSTATE]
    readout = mixed[:, INNER + NSTATE :]
    b_parts, c_parts = split(inputs_b), split(readout)
    b_wide = side_by_side(inputs_b)
    c_turned = side_by_side(readout.T)
    affinity = dot3(b_parts, c_parts, NT)
    low, high = pair_mask()
    grad_affinity = jnp.zeros((CHUNK, CHUNK), F32)
    grad_b = jnp.zeros((CHUNK, NSTATE), F32)
    grad_c = jnp.zeros((CHUNK, NSTATE), F32)
    last_row = lax.broadcasted_iota(jnp.int32, (CHUNK, QWIDTH), 0) == CHUNK - 1
    for quad in range(QUADS):
        cols = slice(quad * QWIDTH, (quad + 1) * QWIDTH)
        wide_delta, wide_cum, columns = widen(delta, cum, quad)
        grown = jnp.exp(wide_cum)
        tail = jnp.exp(wide_cum[CHUNK - 1 :] - wide_cum)
        end = grown[CHUNK - 1 :]
        values = mixed[:, cols]
        pulled = grad[:, cols]
        scaled = values * wide_delta
        x_parts, p_parts = split(scaled), split(pulled)
        outs = []
        for j in range(2):
            half = slice(j * LANES, (j + 1) * LANES)
            xh, xl = x_parts[0][:, half], x_parts[1][:, half]
            right_h, right_l = pair_rows(p_parts, j, low, high)
            pull = dot(
                jnp.concatenate([xh, xl], axis=1),
                jnp.concatenate([right_h, right_h], axis=1),
                NT,
            ) + dot(xh, right_l, NT)
            kernels = []
            for k in range(2):
                h = 4 * quad + 2 * j + k
                within = jnp.exp(cum_t[h : h + 1, :] - columns[2 * j + k] + bias)
                kernels.append(split(affinity * within))
                grad_affinity = grad_affinity + within * pull[:, k * CHUNK : (k + 1) * CHUNK]
            kernel_h = jnp.concatenate([kernels[0][0], kernels[1][0]], axis=1)
            kernel_l = jnp.concatenate([kernels[0][1], kernels[1][1]], axis=1)
            both = dot(kernel_h, jnp.concatenate([right_h, right_l], axis=1))
            outs.append(both[:, :LANES] + both[:, LANES:] + dot(kernel_l, right_h))
        late = grad_state[:, cols]
        late_parts = split(late)
        early = states[0, :, cols]
        from_state = dot_parts(b_wide, late_parts) * tail
        grad_scaled = jnp.concatenate(outs, axis=1) + from_state
        pulled_cum = split(pulled * grown)
        grad_c = grad_c + dot_turned(pulled_cum, split(early))
        grad_b = grad_b + dot_turned(split(scaled * tail), late_parts)
        grad_state[:, cols] = late * end + dot_parts(c_turned, pulled_cum)
        grad_mixed[:, cols] = grad_scaled * wide_delta + skip[:, cols] * pulled
        skip_sums[:, cols] += jnp.sum(pulled * values, axis=0, keepdims=True)
        to_sum[:CHUNK, cols] = grad_scaled * values
        inner = pulled * (ssm[:, cols] - skip[:, cols] * values) - scaled * grad_scaled
        extra = jnp.sum(scaled * from_state, axis=0, keepdims=True) + end * jnp.sum(
            late * early, axis=0, keepdims=True
        )
        to_sum[CHUNK:, cols] = inner + jnp.where(last_row, extra, 0.0)
    ga_parts = split(grad_affinity)
    grad_mixed[:, INNER : INNER + NSTATE] = grad_b + dot3(ga_parts, c_parts)
    grad_mixed[:, INNER + NSTATE :] = grad_c + dot3(split(grad_affinity.T), b_parts)


    def by_head(v):
        high, low = split(v)
        return dot(high, gather[...]) + dot(low, gather[...])

    direct, grad_cum = by_head(to_sum[:CHUNK, :]), by_head(to_sum[CHUNK:, :])
    upper = (lane >= row).astype(BF16)
    after = triangle_sum(upper, grad_cum)
    grad_delta = direct + rate * after
    grad_raw = jnp.where(heads, grad_delta * sigmoid(shifted), 0.0)
    grad_low[:, DT_AT:] = grad_raw.astype(BF16)
    sums[0:1, :] += jnp.sum(grad_raw, axis=0, keepdims=True)
    sums[1:2, :] += rate * jnp.sum(delta * after, axis=0, keepdims=True)
    grad_low[:, :INNER] = grad_gate[...]
    for tile in range(MIXW // LANES):
        cols = slice(tile * LANES, (tile + 1) * LANES)
        w = conv_weight[:, cols]
        g = grad_mixed[:, cols] * slope[:, cols]
        rows = conv_in[:, cols]
        later = following[:, cols]
        total = jnp.zeros((CHUNK, LANES), F32)
        arriving = moved_up(shift.at[tile], g, later) + [g]
        for k in range(KCONV):
            conv_sums[8 * k : 8 * k + 8, cols] += eights(rows * arriving[k])
            total = total + arriving[k] * w[k : k + 1]
        conv_sums[8 * KCONV :, cols] += eights(g)
        following[:, cols] = g[:8]
        grad_low[:, INNER + tile * LANES : INNER + (tile + 1) * LANES] = total.astype(BF16)


def backward(
    conv_in, dt, ssm, grad, grad_gate, states, conv_weight, conv_bias, dt_bias, a_log, skip, gather
):
    length = conv_in.shape[0]
    chunks = length // CHUNK
    whole = lambda v: pl.BlockSpec(v.shape, lambda i: (0,) * v.ndim)
    by_row = lambda width: pl.BlockSpec((CHUNK, width), lambda i: (chunks - 1 - i, 0))
    return pl.pallas_call(
        backward_kernel,
        grid=(chunks,),
        out_shape=(
            shape((length, WIDE), BF16),
            shape((8, LANES), F32),
            shape((1, INNER), F32),
            shape((8 * (KCONV + 1), MIXW), F32),
        ),
        in_specs=[
            by_row(MIXW),
            pl.BlockSpec((8, MIXW), lambda i: (jnp.maximum((chunks - 1 - i) * (CHUNK // 8) - 1, 0), 0)),
            by_row(LANES),
            by_row(INNER),
            by_row(INNER),
            by_row(INNER),
            pl.BlockSpec((1, NSTATE, INNER), lambda i: (chunks - 1 - i, 0, 0)),
        ]
        + [whole(v) for v in (conv_weight, conv_bias, dt_bias, a_log, skip, gather)],
        out_specs=(
            by_row(WIDE),
            pl.BlockSpec((8, LANES), lambda i: (0, 0)),
            pl.BlockSpec((1, INNER), lambda i: (0, 0)),
            pl.BlockSpec((8 * (KCONV + 1), MIXW), lambda i: (0, 0)),
        ),
        scratch_shapes=[pltpu.VMEM((NSTATE, INNER), F32)]
        + [pltpu.VMEM((2 * CHUNK, INNER), F32)]
        + [pltpu.VMEM((CHUNK, MIXW), F32)] * 3
        + [pltpu.VMEM((8, MIXW), F32), pltpu.VMEM((MIXW // LANES, CHUNK + 8, LANES), F32)],
        compiler_params=params(),
        cost_estimate=cost(43),
    )(
        conv_in, conv_in, dt, ssm, grad, grad_gate, states,
        conv_weight, conv_bias, dt_bias, a_log, skip, gather,
    )


def moved_down(scratch, v, before):
    rows = v.shape[0]
    scratch[0:8, :] = before
    scratch[8 : 8 + rows, :] = v
    return [scratch[8 - by : 8 - by + rows, :] for by in range(KCONV - 1, 0, -1)]


def moved_up(scratch, v, behind):
    rows = v.shape[0]
    scratch[0:rows, :] = v
    scratch[rows : rows + 8, :] = behind
    return [scratch[by : by + rows, :] for by in range(KCONV - 1, 0, -1)]


def conv_sum(terms, weight, bias):
    total = bias + terms[KCONV - 1] * weight[KCONV - 1 : KCONV]
    for k in range(KCONV - 1):
        total = total + terms[k] * weight[k : k + 1]
    return total


def loss_kernel(
    limit, mixed_out, w_out, tokens, teacher, mask, block_out, grad_result, grad_branch, error
):
    step = pl.program_id(0)

    @pl.when(step == 0)
    def _():
        error[...] = jnp.zeros_like(error)

    rows = tokens.shape[0]
    result = tokens[...].astype(F32) + dot(mixed_out[...], w_out[...])
    position = step * rows + lax.broadcasted_iota(jnp.int32, (rows, 1), 0)
    valid = (position < limit[0]).astype(F32)
    turned = jnp.broadcast_to(mask[...].astype(F32), (LANES, rows)).T
    weight = valid * turned[:, 0:1]
    block_out[...] = (result * valid).astype(BF16)
    misfit = result - teacher[...].astype(F32)
    pulled = 2.0 * weight * misfit
    grad_result[...] = pulled
    errors = jnp.sum(0.5 * pulled * misfit, axis=0, keepdims=True)
    for j in range(D // LANES):
        error[j : j + 1, :] += errors[:, j * LANES : (j + 1) * LANES]
    error[D // LANES : D // LANES + 1, :] += jnp.sum(valid * turned, axis=0, keepdims=True)
    grad_branch[...] = pulled.astype(BF16)


def loss_part(limit, mixed_out, w_out, tokens, teacher, mask):
    length = tokens.shape[0]
    rows = 256
    by_row = lambda width: pl.BlockSpec((rows, width), lambda i: (i, 0))
    return pl.pallas_call(
        loss_kernel,
        grid=(length // rows,),
        out_shape=(
            shape((length, D), BF16),
            shape((length, D), F32),
            shape((length, D), BF16),
            shape((8, LANES), F32),
        ),
        in_specs=[
            SMEM,
            by_row(INNER),
            pl.BlockSpec(w_out.shape, lambda i: (0, 0)),
            by_row(D),
            by_row(D),
            pl.BlockSpec((1, rows), lambda i: (0, i)),
        ],
        out_specs=(by_row(D), by_row(D), by_row(D), pl.BlockSpec((8, LANES), lambda i: (0, 0))),
        compiler_params=params(),
        cost_estimate=cost(8),
    )(limit, mixed_out, w_out, tokens, teacher, mask)


def gate_kernel(grad_branch, w_out, ssm, gate, gain, grad_ssm, grad_gate, gain_sums):
    @pl.when(pl.program_id(0) == 0)
    def _():
        gain_sums[...] = jnp.zeros_like(gain_sums)

    grad_mixed = dot(grad_branch[...], w_out[...], NT)
    g = gate[...]
    sig = sigmoid(g)
    act = g * sig
    inner = ssm[...]
    gated = inner * act
    rho = lax.rsqrt(jnp.mean(gated * gated, axis=1, keepdims=True) + NORM_EPS)
    unit = gated * rho
    gain_sums[...] += jnp.sum(unit * grad_mixed, axis=0, keepdims=True)
    grad_unit = grad_mixed * gain[...]
    share = jnp.mean(grad_unit * unit, axis=1, keepdims=True)
    grad_gated = rho * (grad_unit - unit * share)
    grad_ssm[...] = grad_gated * act
    grad_gate[...] = (grad_gated * inner * (sig * (1.0 + g * (1.0 - sig)))).astype(BF16)


def gate_part(grad_branch, w_out, ssm, gate, gain):
    length = ssm.shape[0]
    rows = 256
    by_row = lambda width: pl.BlockSpec((rows, width), lambda i: (i, 0))
    whole = lambda v: pl.BlockSpec(v.shape, lambda i: (0,) * v.ndim)
    return pl.pallas_call(
        gate_kernel,
        grid=(length // rows,),
        out_shape=(shape((length, INNER), F32), shape((length, INNER), BF16), shape((1, INNER), F32)),
        in_specs=[by_row(D), whole(w_out), by_row(INNER), by_row(INNER), whole(gain)],
        out_specs=(by_row(INNER), by_row(INNER), pl.BlockSpec((1, INNER), lambda i: (0, 0))),
        compiler_params=params(),
        cost_estimate=cost(12),
    )(grad_branch, w_out, ssm, gate, gain)


def input_kernel(grad_low, w_in, tokens, norm_gain, grad_result, out, sums):
    @pl.when(pl.program_id(0) == 0)
    def _():
        sums[...] = jnp.zeros_like(sums)

    x = tokens[...].astype(F32)
    inverse = lax.rsqrt(jnp.mean(x * x, axis=1, keepdims=True) + NORM_EPS)
    unit = x * inverse
    grad_hidden = dot(grad_low[...], w_in[...], NT)
    sums[...] += jnp.sum(grad_hidden * unit, axis=0, keepdims=True)
    pulled = grad_hidden * norm_gain[...]
    share = jnp.mean(pulled * unit, axis=1, keepdims=True)
    out[...] = grad_result[...] + inverse * (pulled - unit * share)


def input_backward(grad_low, w_in, tokens, norm_gain, grad_result):
    length = tokens.shape[0]
    rows = 256
    by_row = lambda width: pl.BlockSpec((rows, width), lambda i: (i, 0))
    whole = lambda v: pl.BlockSpec(v.shape, lambda i: (0,) * v.ndim)
    return pl.pallas_call(
        input_kernel,
        grid=(length // rows,),
        out_shape=(shape((length, D), F32), shape((1, D), F32)),
        in_specs=[by_row(WIDE), whole(w_in), by_row(D), whole(norm_gain), by_row(D)],
        out_specs=(by_row(D), pl.BlockSpec((1, D), lambda i: (0, 0))),
        compiler_params=params(),
        cost_estimate=cost(15),
    )(grad_low, w_in, tokens, norm_gain, grad_result)


def vector_kernel(tail, conv_sums, sums, skip_sums, norm_sums, gate_sums, gather, out, taps):
    tiles = CONVCH // LANES
    out[...] = jnp.zeros_like(out)
    out[0:TAIL_ROWS, :] = tail[...]
    for k in range(KCONV):
        for i in range(tiles):
            partial_sums = conv_sums[8 * k : 8 * k + 8, i * LANES : (i + 1) * LANES]
            taps[k * 16 + i : k * 16 + i + 1, :] = jnp.sum(partial_sums, axis=0, keepdims=True)
    row = lax.broadcasted_iota(jnp.int32, (LANES, LANES), 0)
    col = lax.broadcasted_iota(jnp.int32, (LANES, LANES), 1)
    per_tile = LANES // KCONV

    def exact(v, chosen):
        high = v.astype(BF16)
        rest = v - high.astype(F32)
        middle = rest.astype(BF16)
        low = (rest - middle.astype(F32)).astype(BF16)
        return dot(high, chosen) + (dot(middle, chosen) + dot(low, chosen))

    for q in range(KCONV):
        total = jnp.zeros((tiles, LANES), F32)
        for k in range(KCONV):
            chosen = (col == KCONV * (row % per_tile) + k) & (row // per_tile == q)
            total = total + exact(taps[k * 16 : k * 16 + tiles, :], chosen.astype(BF16))
        out[pl.ds(TAIL_ROWS + q, tiles, stride=KCONV), :] = total
    bias_at = TAIL_ROWS + tiles * KCONV
    for i in range(tiles):
        partial_sums = conv_sums[8 * KCONV :, i * LANES : (i + 1) * LANES]
        out[bias_at + i : bias_at + i + 1, :] = jnp.sum(partial_sums, axis=0, keepdims=True)
    lane = lax.broadcasted_iota(jnp.int32, (1, LANES), 1)
    skip = exact(jnp.broadcast_to(skip_sums[...], (8, INNER)), gather[...])[0:1, :]
    parts = [sums[0:1, :], sums[1:2, :], skip]
    parts = [jnp.where(lane < HEADS, v, 0.0) for v in parts]
    before = parts[0] + pltpu.roll(parts[1], HEADS, 1) + pltpu.roll(parts[2], 2 * HEADS, 1)
    at, shift = bias_at + tiles, 3 * HEADS
    for source in (norm_sums, gate_sums):
        for j in range(source.shape[1] // LANES):
            here = pltpu.roll(source[:, j * LANES : (j + 1) * LANES], shift, 1)
            out[at : at + 1, :] = jnp.where(lane < shift, before, here)
            before = here
            at += 1
    out[at : at + 1, :] = jnp.where(lane < shift, before, 0.0)


def pack_vectors(tail, conv_sums, sums, skip_sums, norm_sums, gate_sums, gather):
    return pl.pallas_call(
        vector_kernel,
        out_shape=shape(((NBLK - MID1) * BROWS, LANES), F32),
        in_specs=[VMEM] * 7,
        out_specs=VMEM,
        scratch_shapes=[pltpu.VMEM((KCONV * 16, LANES), F32)],
        compiler_params=params(),
    )(tail, conv_sums, sums, skip_sums, norm_sums, gate_sums, gather)


def body(tokens, teacher, lengths, loss_mask, owners, master, first_moment, second_moment):
    capacity = master.shape[0]
    dp, fsdp = lax.axis_size("dp"), lax.axis_size("fsdp")
    devices = dp * fsdp
    me = lax.axis_index(AXES).astype(jnp.int32)
    x_first, y_first, z_first = step_orders(dp, fsdp)
    tie = lambda *values: lax.optimization_barrier(values)

    sent = send_blocks(owners, master, devices, me)
    at_home = lax.all_to_all(sent, AXES, 0, 0, tiled=True)
    owners, tokens, loss_mask, _ = tie(owners, tokens, loss_mask, sent)
    plan = make_plan(owners, capacity, devices, me)
    streams = cut(even(plan["slots"], 3), (x_first, y_first, z_first))
    table = stream_places(plan["home"], plan["slot"], me, streams, devices)
    u0, u1 = plan["unit_slots"]
    sizes = [-(-u0 // 5)] * 4
    unit_streams = cut(sizes + [u0 - sum(sizes)], (x_first, y_first, x_first, y_first, z_first))
    order1 = x_first[:2] + x_first[2 + bits_of(fsdp) :] + x_first[2 : 2 + bits_of(fsdp)]
    unit_table, unit_table1 = [], []
    for u in range(UNITS):
        unit = UNITS * plan["order"] + u
        home, slot = unit % devices, unit // devices
        unit_table.append(stream_places(home, slot, me, unit_streams, devices)[:MID0])
        unit_table1.append((place_of(home ^ me, order1) * (u1 + 1) + slot)[MID0:MID1])
    unit_table, unit_table1 = quarters(unit_table), quarters(unit_table1)
    inputs, target = tokens[0], teacher[0]
    (at_home, table, unit_table, unit_table1, received, back_table, row_from, row_block,
     row_used) = tie(
        at_home, table, unit_table, unit_table1, plan["received"], plan["back"],
        plan["row_from"], plan["row_block"], plan["row_used"],
    )
    mine = pick_blocks(received, at_home, [size for _, size, _ in streams])
    parts = []
    for values, (_, _, order) in zip(mine, streams):
        parts += gather_steps(values, order)
    (input_weight, output_weight, conv_weight, conv_bias, dt_bias, a_log, skip, norm_gain,
     gate_gain, hidden, gate, conv_in, dt, ssm, mixed_out, states) = forward(
        table, inputs, parts
    )
    gather = heads_gather()
    block_out, grad_result, grad_branch, local = loss_part(
        lengths, mixed_out, output_weight, inputs, target, loss_mask
    )
    keep1, send1, head, tail = pack_out(
        unit_table1, mixed_out, grad_branch, local, devices, u1 + 1
    )
    grad_branch, send1 = tie(grad_branch, send1)
    got1 = exchange(send1, order1[0])
    grad_ssm, grad_gate, gain_sums = gate_part(grad_branch, output_weight, ssm, gate, gate_gain)
    grad_ssm, keep1, got1 = tie(grad_ssm, keep1, got1)
    keep1, got1 = reduce_step(keep1, got1, order1[1])
    grad_low, sums, skip_sums, conv_sums = backward(
        conv_in, dt, ssm, grad_ssm, grad_gate, states,
        conv_weight, conv_bias, dt_bias, a_log, skip, gather,
    )
    grad_low, keep1, got1 = tie(grad_low, keep1, got1)
    steps1 = order1[2:]
    for step in steps1[:1]:
        keep1, got1 = reduce_step(keep1, got1, step)
    halves = []
    for _, size, _ in unit_streams:
        halves += [devices * size // 2] * 2
    packed = list(pack_in(unit_table, hidden, grad_low, head, halves))
    packed[0], keep1, got1 = tie(packed[0], keep1, got1)
    kept = packed[::2]
    got = [exchange(v, order[0]) for v, (_, _, order) in zip(packed[1::2], unit_streams)]
    *got, grad_low, conv_sums, tail = tie(*got, grad_low, conv_sums, tail)
    for i, (_, _, order) in enumerate(unit_streams):
        kept[i], got[i] = reduce_step(kept[i], got[i], order[1])
    for step in steps1[1:2]:
        keep1, got1 = reduce_step(keep1, got1, step)
    input_grad, norm_sums = input_backward(grad_low, input_weight, inputs, norm_gain, grad_result)
    grad_vec = pack_vectors(tail, conv_sums, sums, skip_sums, norm_sums, gain_sums, gather)
    grad_vec = grad_vec.reshape((NBLK - MID1) * UNITS, UNIT, LANES)
    *got, got1, grad_vec, input_grad = tie(*got, got1, grad_vec, input_grad)
    for step in steps1[2:]:
        keep1, got1 = reduce_step(keep1, got1, step)
    for k in range(2, len(x_first)):
        for i, (_, _, order) in enumerate(unit_streams):
            if i == 0:
                kept[i], got[i], grad_vec = reduce_step(kept[i], got[i], order[k], grad_vec)
            else:
                kept[i], got[i] = reduce_step(kept[i], got[i], order[k])
    back = units_to_owners(back_table, list(zip(kept + [keep1], got + [got1])))
    back, grad_vec = tie(back, grad_vec)
    returned = lax.all_to_all(back, AXES, 0, 0, tiled=True)
    for step in x_first[:2]:
        grad_vec = grad_vec + exchange(grad_vec, step)
    local_sums = keep1[u1] + got1[u1]
    error_sum = jnp.sum(local_sums[: D // LANES])
    divisor = local_sums[D // LANES, 0] * D
    new_first, new_second, new_master = adam(
        row_from,
        row_block,
        row_used,
        divisor,
        returned,
        grad_vec,
        master,
        first_moment,
        second_moment,
    )
    mean_loss = error_sum / divisor
    return (block_out[None], input_grad[None], mean_loss, new_first, new_second, new_master)


def solution(mesh):
    return jax.shard_map(
        body,
        mesh=mesh,
        in_specs=(
            P(AXES, None, None),
            P(AXES, None, None),
            P(AXES),
            P(AXES, None),
            P(),
            P(AXES, None),
            P(AXES, None),
            P(AXES, None),
        ),
        out_specs=(
            P(AXES, None, None),
            P(AXES, None, None),
            P(),
            P(AXES, None),
            P(AXES, None),
            P(AXES, None),
        ),
        check_vma=False,
    )
```

```python
from functools import partial

import jax
import jax.numpy as jnp
import numpy as np
from jax import lax
from jax.experimental import pallas as pl
from jax.experimental.pallas import tpu as pltpu
from jax.sharding import PartitionSpec as P

D = 768
INNER = 1536
NSTATE = 128
HEADDIM = 64
KCONV = 4
SCAN_LEN = 256
PBLOCK = 4096
STEP = 10
HEADS = 24
CONVCH = 1792
PROJ = 3352
PTOT = 3765320
NBLK = 920

LANES = 128
BROWS = PBLOCK // LANES
UNIT = 8
UNITS = BROWS // UNIT
END_IN = D * PROJ
END_OUT = END_IN + INNER * D
MID0 = -(-END_IN // PBLOCK)
MID1 = END_OUT // PBLOCK
N0 = MID0 + NBLK - MID1
N1 = MID1 - MID0
F0_ROWS = N0 * BROWS
IN_ROWS = END_IN // LANES
HEAD_ROWS = MID0 * BROWS - IN_ROWS
TAIL_ROWS = (END_OUT - MID1 * PBLOCK) // LANES
OUT_ROWS = INNER * D // LANES
VEC_ROWS = (NBLK - MID1) * BROWS - TAIL_ROWS
VEC_AT = MID0 * BROWS + TAIL_ROWS
GROUP = 16
GROUPS = D // GROUP
GROUP_ROWS = GROUP * PROJ // LANES
COL_TILES = -(-PROJ // LANES)
WIDE = COL_TILES * LANES
OUT_TILES = D // LANES

NORM_EPS = 1e-05
ADAM_EPS = 1e-08
BETA_ONE = 0.9
BETA_TWO = 0.999
MATRIX_RATE = 0.03
VECTOR_RATE = 0.2
WEIGHT_DECAY = 0.1
PRECISE = lax.Precision.HIGHEST
AXES = ("dp", "fsdp")
VMEM_LIMIT = 60 * 1024 * 1024


def bits_of(count):
    return count.bit_length() - 1


def step_orders(dp, fsdp):
    wide = [("dp", i) for i in range(bits_of(dp))]
    narrow = [("fsdp", i) for i in range(bits_of(fsdp))]
    first = wide[:2] + narrow + wide[2:]
    second = wide[:1] + narrow + wide[1:]
    third = wide[:1] + wide[2:] + wide[1:2] + narrow
    return first, second, third


def cut(sizes, orders):
    streams, at = [], 0
    for size, order in zip(sizes, orders):
        if size:
            streams.append((at, size, order))
        at += size
    return streams


def even(total, parts):
    return [total // parts + (i < total % parts) for i in range(parts)]


def exchange(values, *steps):
    axes = {axis for axis, _ in steps}
    if len(axes) == 1:
        (axis,) = axes
        mask = sum(1 << bit for _, bit in steps)
        pairs = [(i, i ^ mask) for i in range(lax.axis_size(axis))]
        return lax.ppermute(values, axis, pairs)
    low = bits_of(lax.axis_size("fsdp"))
    mask = sum(1 << (bit + (low if axis == "dp" else 0)) for axis, bit in steps)
    count = lax.axis_size("dp") * lax.axis_size("fsdp")
    return lax.ppermute(values, AXES, [(i, i ^ mask) for i in range(count)])


def place_of(relative, order):
    shift_of = {"dp": bits_of(lax.axis_size("fsdp")), "fsdp": 0}
    place = jnp.zeros_like(relative)
    for axis, bit in order:
        place = place * 2 + ((relative >> (shift_of[axis] + bit)) & 1)
    return place


def class_counts(owners, devices):
    block = jnp.arange(NBLK, dtype=jnp.int32)
    mid = ((block >= MID0) & (block < MID1))[None, :]
    device = jnp.arange(devices, dtype=jnp.int32)
    below = owners[None, :] < device[:, None]
    owned = owners[None, :] == device[:, None]

    def total(mask):
        return jnp.sum(mask.astype(jnp.int32), axis=1)

    start = (total(below & ~mid), total(below & mid))
    count = (total(owned & ~mid), total(owned & mid))
    return start, count, total(owned & (block < MID0)[None, :])


def my_counts(owners, me):
    block = jnp.arange(NBLK, dtype=jnp.int32)
    mid = (block >= MID0) & (block < MID1)
    below, owned = owners < me, owners == me
    total = lambda mask: jnp.sum(mask.astype(jnp.int32))
    start = (total(below & ~mid), total(below & mid))
    count = (total(owned & ~mid), total(owned & mid))
    return start, count, total(owned & (block < MID0))


def pair_lanes(capacity, devices):
    return -(-capacity // devices)


def make_plan(owners, capacity, devices, me):
    block = jnp.arange(NBLK, dtype=jnp.int32)
    mid = (block >= MID0) & (block < MID1)
    same = mid[:, None] == mid[None, :]
    before = (owners[None, :] < owners[:, None]) | (
        (owners[None, :] == owners[:, None]) & (block[None, :] < block[:, None])
    )
    order = jnp.sum(before.astype(jnp.int32), axis=1)
    order_in_class = jnp.sum((same & before).astype(jnp.int32), axis=1)
    home, slot = order % devices, order // devices
    device = jnp.arange(devices, dtype=jnp.int32)
    start, count, _ = class_counts(owners, devices)
    my_start, my_count, my_early = my_counts(owners, me)
    pair = pair_lanes(capacity, devices)

    slots = -(-NBLK // devices)
    wanted = me + devices * jnp.arange(slots, dtype=jnp.int32)
    first = start[0] + start[1]
    ends = first + count[0] + count[1]
    owner = jnp.sum((ends[None, :] <= wanted[:, None]).astype(jnp.int32), axis=1)
    owner = jnp.minimum(owner, devices - 1)
    base = jnp.sum(jnp.where(device[None, :] == owner[:, None], first[None, :], 0), axis=1)
    received = owner * pair + jnp.clip((wanted - base) // devices, 0, pair - 1)

    back_pair = (UNITS * capacity + 2 * (devices - 1)) // devices
    unit_slots = (-(-UNITS * N0 // devices), -(-UNITS * N1 // devices))
    lane = jnp.arange(back_pair, dtype=jnp.int32)

    def units_back(kind):
        turn = lane if kind == 0 else back_pair - 1 - lane
        first = UNITS * start[kind][:, None]
        k = (me - first) % devices + turn[None, :] * devices
        return k < UNITS * count[kind][:, None], (first + k) // devices

    valid0, slot0 = units_back(0)
    valid1, slot1 = units_back(1)
    back = jnp.where(valid0, slot0, jnp.where(valid1, unit_slots[0] + slot1, 0)).reshape(-1)

    row = jnp.arange(capacity, dtype=jnp.int32)
    is_mid = (row >= my_early) & (row < my_early + my_count[1])
    k = jnp.where(is_mid, row - my_early, jnp.where(row < my_early, row, row - my_count[1]))
    first = UNITS * jnp.where(is_mid, my_start[1], my_start[0])
    row_used = row < my_count[0] + my_count[1]
    mine = (owners == me)[None, :]
    rank = jnp.sum((mine & (block[None, :] < block[:, None])).astype(jnp.int32), axis=1)
    row_block = jnp.sum(
        jnp.where(mine & (rank[None, :] == row[:, None]), block[None, :], 0), axis=1
    )
    row_from = []
    for u in range(UNITS):
        unit = UNITS * k + u
        turn = unit // devices
        at = ((first + unit) % devices) * back_pair + jnp.where(is_mid, back_pair - 1 - turn, turn)
        late = devices * back_pair + UNITS * (row_block - MID1) + u
        at = jnp.where(row_block >= MID1, late, at)
        row_from.append(jnp.where(row_used, at, 0))
    return dict(
        home=home, slot=slot, slots=slots,
        received=received, order=order_in_class,
        unit_slots=unit_slots, back=back, row_from=quarters(row_from),
        row_used=row_used, row_block=row_block,
    )


def quarters(tables):
    width = -(-tables[0].shape[0] // LANES) * LANES
    return jnp.concatenate([jnp.pad(t, (0, width - t.shape[0])) for t in tables])


def stream_places(home, slot, me, streams, devices):
    relative = home ^ me
    place = jnp.zeros_like(slot)
    for begin, size, order in streams:
        inside = (slot >= begin) & (slot < begin + size)
        at = devices * begin + place_of(relative, order) * size + slot - begin
        place = jnp.where(inside, at, place)
    return place


def cost(microseconds):
    return pl.CostEstimate(
        flops=int(microseconds * 1e9), bytes_accessed=int(microseconds * 3e6), transcendentals=0
    )


ANY = pl.BlockSpec(memory_space=pl.ANY)
VMEM = pl.BlockSpec(memory_space=pltpu.VMEM)
SMEM = pl.BlockSpec(memory_space=pltpu.SMEM)


def params(**extra):
    return pltpu.CompilerParams(vmem_limit_bytes=VMEM_LIMIT, **extra)


def shape(dims, dtype):
    return jax.ShapeDtypeStruct(dims, dtype)


def send_kernel(my_index, owners, master, out, flat, *, devices):
    capacity = master.shape[0]
    me = my_index[0]
    for j in range(BROWS):
        flat[pl.ds(j, capacity, stride=BROWS), :] = master[:, j * LANES : (j + 1) * LANES]
    held = owners[...]
    below, owned = held < me, held == me

    def total(mask):
        return jnp.sum(jnp.where(mask, 1.0, 0.0)).astype(jnp.int32)

    start, count = total(below), total(owned)
    pair = out.shape[0] // devices

    def step(home, carry):
        for s in range(pair):
            k = lax.rem(home - start + devices * NBLK, devices) + s * devices
            row = jnp.where(k < count, k, 0)
            rows = pl.ds(pl.multiple_of(row * BROWS, BROWS), BROWS)
            out[home * pair + s] = flat[rows, :].astype(out.dtype)
        return carry

    lax.fori_loop(0, devices, step, 0)


def send_blocks(owners, master, devices, me):
    rows = -(-NBLK // (8 * LANES)) * 8
    held = jnp.pad(owners, (0, rows * LANES - NBLK), constant_values=1 << 20).reshape(rows, LANES)
    count = devices * pair_lanes(master.shape[0], devices)
    return pl.pallas_call(
        partial(send_kernel, devices=devices),
        out_shape=shape((count, BROWS, LANES), jnp.bfloat16),
        in_specs=[SMEM, VMEM, VMEM],
        out_specs=VMEM,
        scratch_shapes=[pltpu.VMEM((master.shape[0] * BROWS, LANES), jnp.float32)],
        compiler_params=params(),
    )(me.reshape(1), held, master)


def pick_kernel(table, source, *outs):
    at = 0
    for out in outs:

        def step(i, carry, out=out, at=at):
            out[i] = source[table[at + i]]
            return carry

        lax.fori_loop(0, out.shape[0], step, 0)
        at += out.shape[0]


def pick_blocks(table, source, sizes):
    return pl.pallas_call(
        pick_kernel,
        out_shape=tuple(shape((n,) + source.shape[1:], source.dtype) for n in sizes),
        in_specs=[SMEM, VMEM],
        out_specs=(VMEM,) * len(sizes),
        compiler_params=params(),
    )(table, source)


def back_kernel(table, *refs, sizes):
    sources, (out, held) = refs[:-2], refs[-2:]
    at = i = 0
    for size in sizes:
        n = sources[i].shape[0]
        total = sources[i][...]
        for k in range(1, size):
            total = total + sources[i + k][0:n]
        held[at : at + n] = total
        at += n
        i += size

    def step(i, carry):
        for u in range(8):
            out[i * 8 + u] = held[table[i * 8 + u]]
        return carry

    total = out.shape[0]
    lax.fori_loop(0, total // 8, step, 0)


def units_to_owners(table, groups):
    return pl.pallas_call(
        partial(back_kernel, sizes=[len(g) for g in groups]),
        out_shape=shape((table.shape[0], UNIT, LANES), jnp.float32),
        in_specs=[SMEM] + [VMEM] * sum(len(g) for g in groups),
        out_specs=VMEM,
        scratch_shapes=[pltpu.VMEM((sum(g[0].shape[0] for g in groups), UNIT, LANES), jnp.float32)],
        compiler_params=params(),
    )(table, *[v for g in groups for v in g])


def row_start(rho):
    return (PROJ * rho) // LANES, (PROJ * rho) % LANES


def copy_all(pairs, sem):
    copies = [pltpu.make_async_copy(a, b, sem.at[i]) for i, (a, b) in enumerate(pairs)]
    for c in copies:
        c.start()
    for c in copies:
        c.wait()


def spread_blocks(table, first, held, flat, count, first_row):
    def one(i):
        at = pl.multiple_of(first_row + i * BROWS, 16)
        flat[pl.ds(at, BROWS), :] = held[table[first + i]].astype(jnp.float32)

    def step(i, carry):
        for u in range(4):
            one(i * 4 + u)
        return carry

    lax.fori_loop(0, count // 4, step, 0)
    for i in range(count // 4 * 4, count):
        one(i)


def unpack_vectors(flat, conv_weight, conv_bias, dt_bias, a_log, skip, norm_gain, gate_gain):
    bf16, f32 = jnp.bfloat16, jnp.float32
    tiles = CONVCH // LANES
    row = lax.broadcasted_iota(jnp.int32, (LANES, LANES), 0)
    col = lax.broadcasted_iota(jnp.int32, (LANES, LANES), 1)
    per_tile = LANES // KCONV
    for k in range(KCONV):
        total = jnp.zeros((tiles, LANES), f32)
        for q in range(KCONV):
            rows = flat[pl.ds(VEC_AT + q, tiles, stride=KCONV), :].astype(bf16)
            chosen = (row == KCONV * (col % per_tile) + k) & (col // per_tile == q)
            total = total + jnp.dot(rows, chosen.astype(bf16), preferred_element_type=f32)
        for i in range(tiles):
            conv_weight[k : k + 1, i * LANES : (i + 1) * LANES] = total[i : i + 1, :]
    bias_at = VEC_AT + tiles * KCONV
    for i in range(tiles):
        conv_bias[:, i * LANES : (i + 1) * LANES] = flat[bias_at + i : bias_at + i + 1, :]
    at = bias_at + tiles
    lane = lax.broadcasted_iota(jnp.int32, (8, LANES), 1)
    first = flat[at : at + 8, :]
    three = []
    for i in range(3):
        moved = pltpu.roll(first, LANES - i * HEADS, 1) if i else first
        three.append(jnp.where(lane < HEADS, moved, 0.0))
    dt_bias[...] = three[0][0:1, :]
    a_log[...] = three[1][0:1, :]
    for j in range(INNER // LANES):
        h = lax.broadcasted_iota(jnp.int32, (LANES, LANES), 0)
        c = lax.broadcasted_iota(jnp.int32, (LANES, LANES), 1) + j * LANES
        spread = (h == c // HEADDIM).astype(bf16)
        wide = jnp.dot(three[2].astype(bf16), spread, preferred_element_type=f32)
        skip[:, j * LANES : (j + 1) * LANES] = wide[0:1, :]
    shift = 3 * HEADS
    for out, begin, width in ((norm_gain, at, D), (gate_gain, at + D // LANES, INNER)):
        for j in range(width // LANES):
            x = pltpu.roll(flat[begin + j : begin + j + 1, :], LANES - shift, 1)
            y = pltpu.roll(flat[begin + j + 1 : begin + j + 2, :], LANES - shift, 1)
            out[:, j * LANES : (j + 1) * LANES] = jnp.where(lane[0:1] < LANES - shift, x, y)


def unpack_weights(table, parts, w_in, w_out, vectors, held, flat, flat_out, tile, sem):
    pairs, at = [], 0
    for part in parts:
        pairs.append((part, held.at[pl.ds(at, part.shape[0])]))
        at += part.shape[0]
    copy_all(pairs, sem)
    spread_blocks(table, 0, held, flat, MID0, 0)
    spread_blocks(table, MID1, held, flat, NBLK - MID1, MID0 * BROWS)
    spread_blocks(table, MID0, held, flat_out, N1, HEAD_ROWS)
    flat_out[0:HEAD_ROWS, :] = flat[IN_ROWS : IN_ROWS + HEAD_ROWS, :]
    flat_out[OUT_ROWS - TAIL_ROWS :, :] = flat[MID0 * BROWS : MID0 * BROWS + TAIL_ROWS, :]
    unpack_vectors(flat, *vectors)
    rows = 128

    def out_step(i, carry):
        at = pl.multiple_of(i * rows, rows)
        for j in range(OUT_TILES):
            x = flat_out[pl.ds(at * OUT_TILES + j, rows, stride=OUT_TILES), :]
            w_out[pl.ds(at, rows), j * LANES : (j + 1) * LANES] = x.astype(jnp.bfloat16)
        return carry

    lax.fori_loop(0, INNER // rows, out_step, 0)
    lane = lax.broadcasted_iota(jnp.int32, (GROUPS, LANES), 1)

    def columns(j):
        for rho in range(GROUP):
            c, s = row_start(rho)
            x = flat[pl.ds(c + j, GROUPS, stride=GROUP_ROWS), :]
            if s:
                y = flat[pl.ds(c + j + 1, GROUPS, stride=GROUP_ROWS), :]
                x = jnp.where(
                    lane < LANES - s,
                    pltpu.roll(x, LANES - s, 1),
                    pltpu.roll(y, LANES - s, 1),
                )
            tile[pl.ds(rho, GROUPS, stride=GROUP), :] = x

    def step(j, carry):
        columns(j)
        w_in[:, pl.ds(pl.multiple_of(j * LANES, LANES), LANES)] = tile[...].astype(jnp.bfloat16)
        return carry

    lax.fori_loop(0, COL_TILES - 1, step, 0)
    columns(COL_TILES - 1)
    last = (COL_TILES - 1) * LANES
    inside = lax.broadcasted_iota(jnp.int32, (D, LANES), 1) < PROJ - last
    w_in[:, last:] = jnp.where(inside, tile[...], 0.0).astype(jnp.bfloat16)


def unpack_scratch(held, count):
    return [
        pltpu.VMEM((held, BROWS, LANES), jnp.bfloat16),
        pltpu.VMEM((F0_ROWS, LANES), jnp.float32),
        pltpu.VMEM((OUT_ROWS, LANES), jnp.float32),
        pltpu.VMEM((D, LANES), jnp.float32),
        pltpu.SemaphoreType.DMA((count,)),
    ]


def permute_units(table, flat, count, first_row, staged):
    many = 4
    width = table.shape[0] // UNITS

    def one(i):
        for u in range(UNITS):
            at = first_row + i * BROWS + u * UNIT
            at = at if isinstance(at, int) else pl.multiple_of(at, UNIT)
            staged[table[u * width + i]] = flat[pl.ds(at, UNIT), :]

    def step(i, carry):
        for b in range(many):
            one(i * many + b)
        return carry

    lax.fori_loop(0, count // many, step, 0)
    for i in range(count // many * many, count):
        one(i)


def pack_in_kernel(table, hidden, grad, head, *refs):
    outs, (turned, tiles, flat, staged, sem) = refs[:-5], refs[-5:]
    turned[...] = hidden[...].T
    lane = lax.broadcasted_iota(jnp.int32, (GROUPS, LANES), 1)

    def product(p, count):
        at = p * 2 * LANES
        at = at if isinstance(at, int) else pl.multiple_of(at, 2 * LANES)
        return jnp.dot(
            turned[...], grad[:, pl.ds(at, count * LANES)], preferred_element_type=jnp.float32
        )

    def put(p, value):
        for k in range(value.shape[1] // LANES):
            at = (p * 2 + k) * D
            at = at if isinstance(at, int) else pl.multiple_of(at, D)
            tiles[pl.ds(at, D), :] = value[:, k * LANES : (k + 1) * LANES]

    def load(rho, j):
        return tiles[pl.ds(j * D + rho, GROUPS, stride=GROUP), :]

    def whole(rho, i):
        first = -(-PROJ * rho // LANES)
        col0 = first * LANES - PROJ * rho
        x = load(rho, i)
        if col0:
            x = jnp.where(
                lane < LANES - col0,
                pltpu.roll(x, LANES - col0, 1),
                pltpu.roll(load(rho, i + 1), LANES - col0, 1),
            )
        flat[pl.ds(first + i, GROUPS, stride=GROUP_ROWS), :] = x

    put(0, product(0, 2))
    put(1, product(1, 2))
    pairs = COL_TILES // 2

    def step(p, carry):
        for i in range(2):
            for rho in range(GROUP):
                whole(rho, p * 2 + i)
        put(p + 2, product(p + 2, 2))
        return carry

    lax.fori_loop(0, pairs - 2, step, 0)
    put(pairs, product(pairs, COL_TILES % 2))
    for rho in range(GROUP):
        first = -(-PROJ * rho // LANES)
        col0 = first * LANES - PROJ * rho
        full = (PROJ - col0) // LANES
        for i in range((pairs - 2) * 2, full):
            whole(rho, i)
        left = PROJ - col0 - full * LANES
        if left:
            begin = col0 + full * LANES
            j, s = begin // LANES, begin % LANES
            x = pltpu.roll(load(rho, j), LANES - s, 1) if s else load(rho, j)
            if s + left > LANES:
                x = jnp.where(lane < LANES - s, x, pltpu.roll(load(rho, j + 1), LANES - s, 1))
            y = pltpu.roll(load(rho + 1, 0), left, 1)
            flat[pl.ds(first + full, GROUPS, stride=GROUP_ROWS), :] = jnp.where(lane < left, x, y)
    flat[IN_ROWS : IN_ROWS + HEAD_ROWS, :] = head[...]
    permute_units(table, flat, MID0, 0, staged)
    copies, at = [], 0
    for out in outs:
        copies.append((staged.at[pl.ds(at, out.shape[0])], out))
        at += out.shape[0]
    copy_all(copies, sem)


def pack_in(table, hidden, grad, head, sizes):
    return pl.pallas_call(
        pack_in_kernel,
        out_shape=tuple(shape((n, UNIT, LANES), jnp.float32) for n in sizes),
        in_specs=[SMEM, VMEM, VMEM, VMEM],
        out_specs=(ANY,) * len(sizes),
        scratch_shapes=[
            pltpu.VMEM((D, hidden.shape[0]), jnp.bfloat16),
            pltpu.VMEM((COL_TILES * D, LANES), jnp.float32),
            pltpu.VMEM((MID0 * BROWS, LANES), jnp.float32),
            pltpu.VMEM((sum(sizes), UNIT, LANES), jnp.float32),
            pltpu.SemaphoreType.DMA((len(sizes),)),
        ],
        compiler_params=params(),
        cost_estimate=cost(20),
    )(table, hidden, grad, head)


def pack_out_kernel(
    table, mixed_out, grad, local, keep, send, head, tail, turned, flat, out, sem, *, slots
):
    rows = 256

    def step(i, carry):
        at = pl.multiple_of(i * rows, rows)
        turned[...] = mixed_out[:, pl.ds(at, rows)].T
        product = jnp.dot(turned[...], grad[...], preferred_element_type=jnp.float32)
        for j in range(OUT_TILES):
            flat[pl.ds(at * OUT_TILES + j, rows, stride=OUT_TILES), :] = product[
                :, j * LANES : (j + 1) * LANES
            ]
        return carry

    lax.fori_loop(0, INNER // rows, step, 0)
    head[...] = flat[0:HEAD_ROWS, :]
    tail[...] = flat[OUT_ROWS - TAIL_ROWS : OUT_ROWS, :]
    permute_units(table, flat, N1, HEAD_ROWS, out)

    def add_local(i, carry):
        out[i * slots + slots - 1] = local[...]
        return carry

    lax.fori_loop(0, out.shape[0] // slots, add_local, 0)
    half = keep.shape[0]
    copy_all([(out.at[pl.ds(0, half)], keep), (out.at[pl.ds(half, half)], send)], sem)


def pack_out(table, mixed_out, grad, local, devices, slots):
    return pl.pallas_call(
        partial(pack_out_kernel, slots=slots),
        out_shape=(
            shape((devices * slots // 2, UNIT, LANES), jnp.float32),
            shape((devices * slots // 2, UNIT, LANES), jnp.float32),
            shape((HEAD_ROWS, LANES), jnp.float32),
            shape((TAIL_ROWS, LANES), jnp.float32),
        ),
        in_specs=[SMEM, VMEM, VMEM, VMEM],
        out_specs=(ANY, ANY, VMEM, VMEM),
        scratch_shapes=[
            pltpu.VMEM((256, mixed_out.shape[0]), jnp.bfloat16),
            pltpu.VMEM((OUT_ROWS, LANES), jnp.float32),
            pltpu.VMEM((devices * slots, UNIT, LANES), jnp.float32),
            pltpu.SemaphoreType.DMA((2,)),
        ],
        compiler_params=params(),
    )(table, mixed_out, grad, local)


def adam_kernel(
    table, row_block, row_used, scale, got, late, master, first, second,
    o_first, o_second, o_master, flat, held, limit, used,
):
    capacity = master.shape[0]

    def step(i, carry):
        for u in range(UNITS):
            at = table[u * (table.shape[0] // UNITS) + i]
            rows = pl.ds(pl.multiple_of(i * BROWS + u * UNIT, UNIT), UNIT)
            flat[rows, :] = held[at]
        limit[pl.ds(i, 1), :] = jnp.full((1, LANES), END_OUT - row_block[i] * PBLOCK, jnp.int32)
        used[pl.ds(i, 1), :] = jnp.full((1, LANES), row_used[i], jnp.int32)
        return carry

    held[0 : got.shape[0]] = got[...]
    held[got.shape[0] :] = late[...]
    lax.fori_loop(0, capacity, step, 0)
    lane = lax.broadcasted_iota(jnp.int32, (capacity, LANES), 1)
    divisor = scale[0]
    for j in range(BROWS):
        cols = slice(j * LANES, (j + 1) * LANES)
        grad = jnp.where(used[...] > 0, flat[pl.ds(j, capacity, stride=BROWS), :], 0.0) / divisor
        matrix = lane + j * LANES < limit[...]
        weights = master[:, cols]
        new_first = BETA_ONE * first[:, cols] + (1.0 - BETA_ONE) * grad
        new_second = BETA_TWO * second[:, cols] + (1.0 - BETA_TWO) * grad * grad
        normal = (
            new_first
            / (1.0 - BETA_ONE**STEP)
            / (jnp.sqrt(new_second / (1.0 - BETA_TWO**STEP)) + ADAM_EPS)
        )
        rate = jnp.where(matrix, MATRIX_RATE, VECTOR_RATE)
        decay = jnp.where(matrix, WEIGHT_DECAY, 0.0)
        o_first[:, cols] = new_first
        o_second[:, cols] = new_second
        o_master[:, cols] = weights - rate * (normal + decay * weights)


def adam(table, row_block, row_used, divisor, got, late, master, first, second):
    capacity = master.shape[0]
    return pl.pallas_call(
        adam_kernel,
        out_shape=(shape(master.shape, jnp.float32),) * 3,
        in_specs=[SMEM] * 4 + [VMEM] * 5,
        out_specs=(VMEM,) * 3,
        scratch_shapes=[
            pltpu.VMEM((capacity * BROWS, LANES), jnp.float32),
            pltpu.VMEM((got.shape[0] + late.shape[0], UNIT, LANES), jnp.float32),
            pltpu.VMEM((capacity, LANES), jnp.int32),
            pltpu.VMEM((capacity, LANES), jnp.int32),
        ],
        compiler_params=params(),
    )(
        table, row_block, row_used.astype(jnp.int32), divisor.reshape(1), got, late, master, first, second
    )


def doubled(values, step):
    return jnp.concatenate([values, exchange(values, step)], axis=0)


def gather_steps(values, order):
    for step in order[:0:-1]:
        values = doubled(values, step)
    return values, exchange(values, order[0])


def reduce_step(kept, got, step, extra=None):
    half = kept.shape[0] // 2
    given = kept[half:] + got[half:]
    if extra is None:
        return kept[:half] + got[:half], exchange(given, step)
    arrived = exchange(jnp.concatenate([given, extra]), step)
    return kept[:half] + got[:half], arrived[:half], extra + arrived[half:]


CHUNK = 128
PAIRS = HEADS // 2
MIXW = INNER + 2 * NSTATE
DT_AT = INNER + CONVCH
F32 = jnp.float32
BF16 = jnp.bfloat16
NN = (((1,), (0,)), ((), ()))
NT = (((1,), (1,)), ((), ()))


def dot(a, b, dims=NN):
    return lax.dot_general(a, b, dims, preferred_element_type=F32)


def split(v):
    high = v.astype(BF16)
    return high, (v - high.astype(F32)).astype(BF16)


def dot3(a, b, dims=NN):
    ah, al = a
    bh, bl = b
    return dot(ah, bh, dims) + (dot(ah, bl, dims) + dot(al, bh, dims))


def heads_gather():
    return jnp.asarray(np.repeat(np.eye(HEADS, LANES, dtype=np.float32), HEADDIM, axis=0), BF16)


def three_parts(v):
    high = v.astype(BF16).astype(F32)
    rest = v - high
    middle = rest.astype(BF16).astype(F32)
    low = rest - middle
    return (high + pltpu.roll(middle, 32, 1) + pltpu.roll(low, 64, 1)).astype(BF16)


def triangle_sum(tri, v):
    parts = dot(tri, three_parts(v))
    lane = lax.broadcasted_iota(jnp.int32, parts.shape, 1)
    total = parts + pltpu.roll(parts, LANES - 32, 1) + pltpu.roll(parts, LANES - 64, 1)
    return jnp.where(lane < HEADS, total, 0.0)


def chunk_decays(dt, dt_bias, a_log):
    lane = lax.broadcasted_iota(jnp.int32, (CHUNK, LANES), 1)
    row = lax.broadcasted_iota(jnp.int32, (CHUNK, LANES), 0)
    shifted = dt + dt_bias
    delta = jnp.where(
        lane < HEADS, jnp.maximum(shifted, 0.0) + jnp.log1p(jnp.exp(-jnp.abs(shifted))), 0.0
    )
    rate = -jnp.exp(a_log)
    lower = (row >= lane).astype(BF16)
    cum = triangle_sum(lower, delta * rate)
    last = cum[CHUNK - 1 : CHUNK, :]
    return shifted, delta, rate, cum, last


def pair_mask():
    lane = lax.broadcasted_iota(jnp.int32, (CHUNK, LANES), 1)
    low = (lane < HEADDIM).astype(F32)
    return low.astype(BF16), (1.0 - low).astype(BF16)


QUADS = HEADS // 4
QWIDTH = 4 * HEADDIM


def sigmoid(v):
    return 0.5 * jnp.tanh(0.5 * v) + 0.5


def silu(v):
    return v * sigmoid(v)


def side_by_side(v):
    high, low = split(v)
    return jnp.concatenate([high, low], axis=1), high


def dot_parts(a, b):
    ahl, ah = a
    bh, bl = b
    return dot(ahl, jnp.concatenate([bh, bh], axis=0)) + dot(ah, bl)


def dot_turned(a, b):
    ah, al = a
    bh, bl = b
    both = dot(ah, jnp.concatenate([bh, bl], axis=0), NT)
    n = bh.shape[0]
    return both[:, :n] + both[:, n:] + dot(al, bh, NT)


def widen(delta, cum, quad):
    lane = lax.broadcasted_iota(jnp.int32, (CHUNK, LANES), 1)
    over = lambda v, h: jnp.broadcast_to(v[:, h : h + 1], (CHUNK, LANES))
    first = 4 * quad
    columns = [over(cum, first + k) for k in range(4)]
    rates = [over(delta, first + k) for k in range(4)]
    pair = lambda vs: jnp.concatenate(
        [jnp.where(lane < HEADDIM, vs[0], vs[1]), jnp.where(lane < HEADDIM, vs[2], vs[3])], axis=1
    )
    return pair(rates), pair(columns), columns


def pair_rows(parts, j, low, high):
    cols = slice(j * LANES, (j + 1) * LANES)
    return [jnp.concatenate([p[:, cols] * low, p[:, cols] * high], axis=0) for p in parts]


def scan_chunk(mixed, dt, dt_bias, a_log, skip, state, put):
    _, delta, _, cum, last = chunk_decays(dt, dt_bias, a_log)
    lane = lax.broadcasted_iota(jnp.int32, (CHUNK, LANES), 1)
    row = lax.broadcasted_iota(jnp.int32, (CHUNK, LANES), 0)
    bias = jnp.where(row >= lane, 0.0, -1e30)
    cum_t = cum.T
    inputs_b = mixed[:, INNER : INNER + NSTATE]
    readout = mixed[:, INNER + NSTATE :]
    affinity = dot3(split(readout), split(inputs_b), NT)
    readout_parts = side_by_side(readout)
    b_parts = side_by_side(inputs_b.T)
    low, high = pair_mask()
    for quad in range(QUADS):
        cols = slice(quad * QWIDTH, (quad + 1) * QWIDTH)
        wide_delta, wide_cum, columns = widen(delta, cum, quad)
        values = mixed[:, cols]
        scaled = values * wide_delta
        parts = split(scaled)
        outs = []
        for j in range(2):
            right_h, right_l = pair_rows(parts, j, low, high)
            left = []
            for k in range(2):
                h = 4 * quad + 2 * j + k
                within = jnp.exp(columns[2 * j + k] - cum_t[h : h + 1, :] + bias)
                left.append(split(affinity * within))
            left_h = jnp.concatenate([left[0][0], left[1][0]], axis=1)
            left_l = jnp.concatenate([left[0][1], left[1][1]], axis=1)
            both = dot(left_h, jnp.concatenate([right_h, right_l], axis=1))
            outs.append(both[:, :LANES] + both[:, LANES:] + dot(left_l, right_h))
        carried = state[:, cols]
        grown = jnp.exp(wide_cum)
        out = jnp.concatenate(outs, axis=1) + dot_parts(readout_parts, split(carried)) * grown
        tail = jnp.exp(wide_cum[CHUNK - 1 :] - wide_cum)
        state[:, cols] = carried * grown[CHUNK - 1 :] + dot_parts(b_parts, split(scaled * tail))
        put(quad, out + skip[:, cols] * values)


FORWARD_ROWS = 2 * CHUNK


def forward_kernel(table, tokens, *refs, count):
    parts, refs = refs[:count], refs[count:]
    (w_in_kept, w_out_kept, conv_weight, conv_bias, dt_bias, a_log, skip, norm_gain, gain,
     hidden, gate, conv_in, dt, ssm, mixed_out, states) = refs[:16]
    w_in, w_out, state, before, mixed, shift, out_sem, *scratch = refs[16:]
    keep = [
        pltpu.make_async_copy(w_in, w_in_kept, out_sem.at[0]),
        pltpu.make_async_copy(w_out, w_out_kept, out_sem.at[1]),
    ]

    @pl.when(pl.program_id(0) == 0)
    def _():
        vectors = (conv_weight, conv_bias, dt_bias, a_log, skip, norm_gain, gain)
        unpack_weights(table, parts, w_in, w_out, vectors, *scratch)
        for copy in keep:
            copy.start()
        state[...] = jnp.zeros_like(state)
        before[...] = jnp.zeros_like(before)

    x = tokens[...].astype(F32)
    inverse = lax.rsqrt(jnp.mean(x * x, axis=1, keepdims=True) + NORM_EPS)
    h = (x * inverse * norm_gain[...]).astype(BF16)
    hidden[...] = h
    dt[...] = dot(h, w_in[:, DT_AT:])
    wide = 2 * LANES
    for tile in range(CONVCH // wide):
        at = tile * wide
        product = dot(h, w_in[:, INNER + at : INNER + at + wide])
        conv_in[:, at : at + wide] = product
        for half in range(2):
            cols = slice(at + half * LANES, at + (half + 1) * LANES)
            rows = product[:, half * LANES : (half + 1) * LANES]
            earlier = before[:, cols]
            terms = moved_down(shift.at[tile * 2 + half], rows, earlier) + [rows]
            before[:, cols] = rows[FORWARD_ROWS - 8 :]
            mixed[:, cols] = silu(conv_sum(terms, conv_weight[:, cols], conv_bias[:, cols]))
    for tile in range(INNER // wide):
        cols = slice(tile * wide, (tile + 1) * wide)
        gate[:, cols] = dot(h, w_in[:, cols])
    for sub in range(FORWARD_ROWS // CHUNK):
        rows = slice(sub * CHUNK, (sub + 1) * CHUNK)
        states[sub] = state[...]
        squares = [jnp.zeros((CHUNK, LANES), F32)]

        def put(quad, out, rows=rows, squares=squares):
            cols = slice(quad * QWIDTH, (quad + 1) * QWIDTH)
            ssm[rows, cols] = out
            gated = out * silu(gate[rows, cols])
            first, second = gated[:, :LANES], gated[:, LANES:]
            squares[0] = squares[0] + first * first + second * second

        scan_chunk(
            mixed[rows, :], dt[rows, :], dt_bias[...], a_log[...], skip, state, put
        )
        rho = lax.rsqrt(jnp.sum(squares[0], axis=1, keepdims=True) * (1.0 / INNER) + NORM_EPS)
        for j in range(PAIRS):
            cols = slice(j * LANES, (j + 1) * LANES)
            gated = ssm[rows, cols] * silu(gate[rows, cols])
            mixed_out[rows, cols] = (gated * rho * gain[:, cols]).astype(BF16)

    @pl.when(pl.program_id(0) == pl.num_programs(0) - 1)
    def _():
        for copy in keep:
            copy.wait()


def forward(table, tokens, parts):
    length = tokens.shape[0]
    by_row = lambda width: pl.BlockSpec((FORWARD_ROWS, width), lambda i: (i, 0))
    per_step = FORWARD_ROWS // CHUNK
    vectors = [(KCONV, CONVCH), (1, CONVCH), (1, LANES), (1, LANES), (1, INNER), (1, D), (1, INNER)]
    return pl.pallas_call(
        partial(forward_kernel, count=len(parts)),
        grid=(length // FORWARD_ROWS,),
        out_shape=[shape((D, WIDE), BF16), shape((INNER, D), BF16)]
        + [shape(v, F32) for v in vectors]
        + [
            shape((length, D), BF16),
            shape((length, INNER), F32),
            shape((length, MIXW), F32),
            shape((length, LANES), F32),
            shape((length, INNER), F32),
            shape((length, INNER), BF16),
            shape((length // CHUNK, NSTATE, INNER), F32),
        ],
        in_specs=[SMEM, by_row(D)] + [ANY] * len(parts),
        out_specs=[ANY, ANY]
        + [pl.BlockSpec(v, lambda i: (0, 0)) for v in vectors]
        + [
            by_row(D),
            by_row(INNER),
            by_row(MIXW),
            by_row(LANES),
            by_row(INNER),
            by_row(INNER),
            pl.BlockSpec((per_step, NSTATE, INNER), lambda i: (i, 0, 0)),
        ],
        scratch_shapes=[
            pltpu.VMEM((D, WIDE), BF16),
            pltpu.VMEM((INNER, D), BF16),
            pltpu.VMEM((NSTATE, INNER), F32),
            pltpu.VMEM((8, MIXW), F32),
            pltpu.VMEM((FORWARD_ROWS, MIXW), F32),
            pltpu.VMEM((MIXW // LANES, FORWARD_ROWS + 8, LANES), F32),
            pltpu.SemaphoreType.DMA((2,)),
        ]
        + unpack_scratch(sum(part.shape[0] for part in parts), len(parts)),
        compiler_params=params(),
        cost_estimate=cost(50),
    )(table, tokens, *parts)


def eights(v):
    return jnp.sum(v.reshape(v.shape[0] // 8, 8, v.shape[1]), axis=0)


def backward_kernel(
    conv_in, earlier, dt, ssm, grad, grad_gate, states, conv_weight, conv_bias, dt_bias, a_log, skip,
    gather, grad_low, sums, skip_sums, conv_sums,
    grad_state, to_sum, mixed, slope, grad_mixed, following, shift,
):
    @pl.when(pl.program_id(0) == 0)
    def _():
        grad_state[...] = jnp.zeros_like(grad_state)
        sums[...] = jnp.zeros_like(sums)
        skip_sums[...] = jnp.zeros_like(skip_sums)
        conv_sums[...] = jnp.zeros_like(conv_sums)
        following[...] = jnp.zeros_like(following)

    begins = pl.program_id(0) == pl.num_programs(0) - 1

    for tile in range(MIXW // LANES):
        cols = slice(tile * LANES, (tile + 1) * LANES)
        rows = conv_in[:, cols]
        before = jnp.where(begins, 0.0, earlier[:, cols])
        terms = moved_down(shift.at[tile], rows, before) + [rows]
        value = conv_sum(terms, conv_weight[:, cols], conv_bias[:, cols])
        sig = sigmoid(value)
        mixed[:, cols] = value * sig
        slope[:, cols] = sig * (1.0 + value * (1.0 - sig))

    shifted, delta, rate, cum, last = chunk_decays(dt[...], dt_bias[...], a_log[...])
    lane = lax.broadcasted_iota(jnp.int32, (CHUNK, LANES), 1)
    row = lax.broadcasted_iota(jnp.int32, (CHUNK, LANES), 0)
    bias = jnp.where(lane >= row, 0.0, -1e30)
    heads = lane < HEADS
    cum_t = cum.T
    inputs_b = mixed[:, INNER : INNER + NSTATE]
    readout = mixed[:, INNER + NSTATE :]
    b_parts, c_parts = split(inputs_b), split(readout)
    b_wide = side_by_side(inputs_b)
    c_turned = side_by_side(readout.T)
    affinity = dot3(b_parts, c_parts, NT)
    low, high = pair_mask()
    grad_affinity = jnp.zeros((CHUNK, CHUNK), F32)
    grad_b = jnp.zeros((CHUNK, NSTATE), F32)
    grad_c = jnp.zeros((CHUNK, NSTATE), F32)
    last_row = lax.broadcasted_iota(jnp.int32, (CHUNK, QWIDTH), 0) == CHUNK - 1
    for quad in range(QUADS):
        cols = slice(quad * QWIDTH, (quad + 1) * QWIDTH)
        wide_delta, wide_cum, columns = widen(delta, cum, quad)
        grown = jnp.exp(wide_cum)
        tail = jnp.exp(wide_cum[CHUNK - 1 :] - wide_cum)
        end = grown[CHUNK - 1 :]
        values = mixed[:, cols]
        pulled = grad[:, cols]
        scaled = values * wide_delta
        x_parts, p_parts = split(scaled), split(pulled)
        outs = []
        for j in range(2):
            half = slice(j * LANES, (j + 1) * LANES)
            xh, xl = x_parts[0][:, half], x_parts[1][:, half]
            right_h, right_l = pair_rows(p_parts, j, low, high)
            pull = dot(
                jnp.concatenate([xh, xl], axis=1),
                jnp.concatenate([right_h, right_h], axis=1),
                NT,
            ) + dot(xh, right_l, NT)
            kernels = []
            for k in range(2):
                h = 4 * quad + 2 * j + k
                within = jnp.exp(cum_t[h : h + 1, :] - columns[2 * j + k] + bias)
                kernels.append(split(affinity * within))
                grad_affinity = grad_affinity + within * pull[:, k * CHUNK : (k + 1) * CHUNK]
            kernel_h = jnp.concatenate([kernels[0][0], kernels[1][0]], axis=1)
            kernel_l = jnp.concatenate([kernels[0][1], kernels[1][1]], axis=1)
            both = dot(kernel_h, jnp.concatenate([right_h, right_l], axis=1))
            outs.append(both[:, :LANES] + both[:, LANES:] + dot(kernel_l, right_h))
        late = grad_state[:, cols]
        late_parts = split(late)
        early = states[0, :, cols]
        from_state = dot_parts(b_wide, late_parts) * tail
        grad_scaled = jnp.concatenate(outs, axis=1) + from_state
        pulled_cum = split(pulled * grown)
        grad_c = grad_c + dot_turned(pulled_cum, split(early))
        grad_b = grad_b + dot_turned(split(scaled * tail), late_parts)
        grad_state[:, cols] = late * end + dot_parts(c_turned, pulled_cum)
        grad_mixed[:, cols] = grad_scaled * wide_delta + skip[:, cols] * pulled
        skip_sums[:, cols] += jnp.sum(pulled * values, axis=0, keepdims=True)
        to_sum[:CHUNK, cols] = grad_scaled * values
        inner = pulled * (ssm[:, cols] - skip[:, cols] * values) - scaled * grad_scaled
        extra = jnp.sum(scaled * from_state, axis=0, keepdims=True) + end * jnp.sum(
            late * early, axis=0, keepdims=True
        )
        to_sum[CHUNK:, cols] = inner + jnp.where(last_row, extra, 0.0)
    ga_parts = split(grad_affinity)
    grad_mixed[:, INNER : INNER + NSTATE] = grad_b + dot3(ga_parts, c_parts)
    grad_mixed[:, INNER + NSTATE :] = grad_c + dot3(split(grad_affinity.T), b_parts)


    def by_head(v):
        high, low = split(v)
        return dot(high, gather[...]) + dot(low, gather[...])

    direct, grad_cum = by_head(to_sum[:CHUNK, :]), by_head(to_sum[CHUNK:, :])
    upper = (lane >= row).astype(BF16)
    after = triangle_sum(upper, grad_cum)
    grad_delta = direct + rate * after
    grad_raw = jnp.where(heads, grad_delta * sigmoid(shifted), 0.0)
    grad_low[:, DT_AT:] = grad_raw.astype(BF16)
    sums[0:1, :] += jnp.sum(grad_raw, axis=0, keepdims=True)
    sums[1:2, :] += rate * jnp.sum(delta * after, axis=0, keepdims=True)
    grad_low[:, :INNER] = grad_gate[...]
    for tile in range(MIXW // LANES):
        cols = slice(tile * LANES, (tile + 1) * LANES)
        w = conv_weight[:, cols]
        g = grad_mixed[:, cols] * slope[:, cols]
        rows = conv_in[:, cols]
        later = following[:, cols]
        total = jnp.zeros((CHUNK, LANES), F32)
        arriving = moved_up(shift.at[tile], g, later) + [g]
        for k in range(KCONV):
            conv_sums[8 * k : 8 * k + 8, cols] += eights(rows * arriving[k])
            total = total + arriving[k] * w[k : k + 1]
        conv_sums[8 * KCONV :, cols] += eights(g)
        following[:, cols] = g[:8]
        grad_low[:, INNER + tile * LANES : INNER + (tile + 1) * LANES] = total.astype(BF16)


def backward(
    conv_in, dt, ssm, grad, grad_gate, states, conv_weight, conv_bias, dt_bias, a_log, skip, gather
):
    length = conv_in.shape[0]
    chunks = length // CHUNK
    whole = lambda v: pl.BlockSpec(v.shape, lambda i: (0,) * v.ndim)
    by_row = lambda width: pl.BlockSpec((CHUNK, width), lambda i: (chunks - 1 - i, 0))
    return pl.pallas_call(
        backward_kernel,
        grid=(chunks,),
        out_shape=(
            shape((length, WIDE), BF16),
            shape((8, LANES), F32),
            shape((1, INNER), F32),
            shape((8 * (KCONV + 1), MIXW), F32),
        ),
        in_specs=[
            by_row(MIXW),
            pl.BlockSpec((8, MIXW), lambda i: (jnp.maximum((chunks - 1 - i) * (CHUNK // 8) - 1, 0), 0)),
            by_row(LANES),
            by_row(INNER),
            by_row(INNER),
            by_row(INNER),
            pl.BlockSpec((1, NSTATE, INNER), lambda i: (chunks - 1 - i, 0, 0)),
        ]
        + [whole(v) for v in (conv_weight, conv_bias, dt_bias, a_log, skip, gather)],
        out_specs=(
            by_row(WIDE),
            pl.BlockSpec((8, LANES), lambda i: (0, 0)),
            pl.BlockSpec((1, INNER), lambda i: (0, 0)),
            pl.BlockSpec((8 * (KCONV + 1), MIXW), lambda i: (0, 0)),
        ),
        scratch_shapes=[pltpu.VMEM((NSTATE, INNER), F32)]
        + [pltpu.VMEM((2 * CHUNK, INNER), F32)]
        + [pltpu.VMEM((CHUNK, MIXW), F32)] * 3
        + [pltpu.VMEM((8, MIXW), F32), pltpu.VMEM((MIXW // LANES, CHUNK + 8, LANES), F32)],
        compiler_params=params(),
        cost_estimate=cost(43),
    )(
        conv_in, conv_in, dt, ssm, grad, grad_gate, states,
        conv_weight, conv_bias, dt_bias, a_log, skip, gather,
    )


def moved_down(scratch, v, before):
    rows = v.shape[0]
    scratch[0:8, :] = before
    scratch[8 : 8 + rows, :] = v
    return [scratch[8 - by : 8 - by + rows, :] for by in range(KCONV - 1, 0, -1)]


def moved_up(scratch, v, behind):
    rows = v.shape[0]
    scratch[0:rows, :] = v
    scratch[rows : rows + 8, :] = behind
    return [scratch[by : by + rows, :] for by in range(KCONV - 1, 0, -1)]


def conv_sum(terms, weight, bias):
    total = bias + terms[KCONV - 1] * weight[KCONV - 1 : KCONV]
    for k in range(KCONV - 1):
        total = total + terms[k] * weight[k : k + 1]
    return total


def loss_kernel(
    limit, mixed_out, w_out, tokens, teacher, mask, block_out, grad_result, grad_branch, error
):
    step = pl.program_id(0)

    @pl.when(step == 0)
    def _():
        error[...] = jnp.zeros_like(error)

    rows = tokens.shape[0]
    result = tokens[...].astype(F32) + dot(mixed_out[...], w_out[...])
    position = step * rows + lax.broadcasted_iota(jnp.int32, (rows, 1), 0)
    valid = (position < limit[0]).astype(F32)
    turned = jnp.broadcast_to(mask[...].astype(F32), (LANES, rows)).T
    weight = valid * turned[:, 0:1]
    block_out[...] = (result * valid).astype(BF16)
    misfit = result - teacher[...].astype(F32)
    pulled = 2.0 * weight * misfit
    grad_result[...] = pulled
    errors = jnp.sum(0.5 * pulled * misfit, axis=0, keepdims=True)
    for j in range(D // LANES):
        error[j : j + 1, :] += errors[:, j * LANES : (j + 1) * LANES]
    error[D // LANES : D // LANES + 1, :] += jnp.sum(valid * turned, axis=0, keepdims=True)
    grad_branch[...] = pulled.astype(BF16)


def loss_part(limit, mixed_out, w_out, tokens, teacher, mask):
    length = tokens.shape[0]
    rows = 256
    by_row = lambda width: pl.BlockSpec((rows, width), lambda i: (i, 0))
    return pl.pallas_call(
        loss_kernel,
        grid=(length // rows,),
        out_shape=(
            shape((length, D), BF16),
            shape((length, D), F32),
            shape((length, D), BF16),
            shape((8, LANES), F32),
        ),
        in_specs=[
            SMEM,
            by_row(INNER),
            pl.BlockSpec(w_out.shape, lambda i: (0, 0)),
            by_row(D),
            by_row(D),
            pl.BlockSpec((1, rows), lambda i: (0, i)),
        ],
        out_specs=(by_row(D), by_row(D), by_row(D), pl.BlockSpec((8, LANES), lambda i: (0, 0))),
        compiler_params=params(),
        cost_estimate=cost(8),
    )(limit, mixed_out, w_out, tokens, teacher, mask)


def gate_kernel(grad_branch, w_out, ssm, gate, gain, grad_ssm, grad_gate, gain_sums):
    @pl.when(pl.program_id(0) == 0)
    def _():
        gain_sums[...] = jnp.zeros_like(gain_sums)

    grad_mixed = dot(grad_branch[...], w_out[...], NT)
    g = gate[...]
    sig = sigmoid(g)
    act = g * sig
    inner = ssm[...]
    gated = inner * act
    rho = lax.rsqrt(jnp.mean(gated * gated, axis=1, keepdims=True) + NORM_EPS)
    unit = gated * rho
    gain_sums[...] += jnp.sum(unit * grad_mixed, axis=0, keepdims=True)
    grad_unit = grad_mixed * gain[...]
    share = jnp.mean(grad_unit * unit, axis=1, keepdims=True)
    grad_gated = rho * (grad_unit - unit * share)
    grad_ssm[...] = grad_gated * act
    grad_gate[...] = (grad_gated * inner * (sig * (1.0 + g * (1.0 - sig)))).astype(BF16)


def gate_part(grad_branch, w_out, ssm, gate, gain):
    length = ssm.shape[0]
    rows = 256
    by_row = lambda width: pl.BlockSpec((rows, width), lambda i: (i, 0))
    whole = lambda v: pl.BlockSpec(v.shape, lambda i: (0,) * v.ndim)
    return pl.pallas_call(
        gate_kernel,
        grid=(length // rows,),
        out_shape=(shape((length, INNER), F32), shape((length, INNER), BF16), shape((1, INNER), F32)),
        in_specs=[by_row(D), whole(w_out), by_row(INNER), by_row(INNER), whole(gain)],
        out_specs=(by_row(INNER), by_row(INNER), pl.BlockSpec((1, INNER), lambda i: (0, 0))),
        compiler_params=params(),
        cost_estimate=cost(12),
    )(grad_branch, w_out, ssm, gate, gain)


def input_kernel(grad_low, w_in, tokens, norm_gain, grad_result, out, sums):
    @pl.when(pl.program_id(0) == 0)
    def _():
        sums[...] = jnp.zeros_like(sums)

    x = tokens[...].astype(F32)
    inverse = lax.rsqrt(jnp.mean(x * x, axis=1, keepdims=True) + NORM_EPS)
    unit = x * inverse
    grad_hidden = dot(grad_low[...], w_in[...], NT)
    sums[...] += jnp.sum(grad_hidden * unit, axis=0, keepdims=True)
    pulled = grad_hidden * norm_gain[...]
    share = jnp.mean(pulled * unit, axis=1, keepdims=True)
    out[...] = grad_result[...] + inverse * (pulled - unit * share)


def input_backward(grad_low, w_in, tokens, norm_gain, grad_result):
    length = tokens.shape[0]
    rows = 256
    by_row = lambda width: pl.BlockSpec((rows, width), lambda i: (i, 0))
    whole = lambda v: pl.BlockSpec(v.shape, lambda i: (0,) * v.ndim)
    return pl.pallas_call(
        input_kernel,
        grid=(length // rows,),
        out_shape=(shape((length, D), F32), shape((1, D), F32)),
        in_specs=[by_row(WIDE), whole(w_in), by_row(D), whole(norm_gain), by_row(D)],
        out_specs=(by_row(D), pl.BlockSpec((1, D), lambda i: (0, 0))),
        compiler_params=params(),
        cost_estimate=cost(15),
    )(grad_low, w_in, tokens, norm_gain, grad_result)


def vector_kernel(tail, conv_sums, sums, skip_sums, norm_sums, gate_sums, gather, out, taps):
    tiles = CONVCH // LANES
    out[...] = jnp.zeros_like(out)
    out[0:TAIL_ROWS, :] = tail[...]
    for k in range(KCONV):
        for i in range(tiles):
            partial_sums = conv_sums[8 * k : 8 * k + 8, i * LANES : (i + 1) * LANES]
            taps[k * 16 + i : k * 16 + i + 1, :] = jnp.sum(partial_sums, axis=0, keepdims=True)
    row = lax.broadcasted_iota(jnp.int32, (LANES, LANES), 0)
    col = lax.broadcasted_iota(jnp.int32, (LANES, LANES), 1)
    per_tile = LANES // KCONV

    def exact(v, chosen):
        high = v.astype(BF16)
        rest = v - high.astype(F32)
        middle = rest.astype(BF16)
        low = (rest - middle.astype(F32)).astype(BF16)
        return dot(high, chosen) + (dot(middle, chosen) + dot(low, chosen))

    for q in range(KCONV):
        total = jnp.zeros((tiles, LANES), F32)
        for k in range(KCONV):
            chosen = (col == KCONV * (row % per_tile) + k) & (row // per_tile == q)
            total = total + exact(taps[k * 16 : k * 16 + tiles, :], chosen.astype(BF16))
        out[pl.ds(TAIL_ROWS + q, tiles, stride=KCONV), :] = total
    bias_at = TAIL_ROWS + tiles * KCONV
    for i in range(tiles):
        partial_sums = conv_sums[8 * KCONV :, i * LANES : (i + 1) * LANES]
        out[bias_at + i : bias_at + i + 1, :] = jnp.sum(partial_sums, axis=0, keepdims=True)
    lane = lax.broadcasted_iota(jnp.int32, (1, LANES), 1)
    skip = exact(jnp.broadcast_to(skip_sums[...], (8, INNER)), gather[...])[0:1, :]
    parts = [sums[0:1, :], sums[1:2, :], skip]
    parts = [jnp.where(lane < HEADS, v, 0.0) for v in parts]
    before = parts[0] + pltpu.roll(parts[1], HEADS, 1) + pltpu.roll(parts[2], 2 * HEADS, 1)
    at, shift = bias_at + tiles, 3 * HEADS
    for source in (norm_sums, gate_sums):
        for j in range(source.shape[1] // LANES):
            here = pltpu.roll(source[:, j * LANES : (j + 1) * LANES], shift, 1)
            out[at : at + 1, :] = jnp.where(lane < shift, before, here)
            before = here
            at += 1
    out[at : at + 1, :] = jnp.where(lane < shift, before, 0.0)


def pack_vectors(tail, conv_sums, sums, skip_sums, norm_sums, gate_sums, gather):
    return pl.pallas_call(
        vector_kernel,
        out_shape=shape(((NBLK - MID1) * BROWS, LANES), F32),
        in_specs=[VMEM] * 7,
        out_specs=VMEM,
        scratch_shapes=[pltpu.VMEM((KCONV * 16, LANES), F32)],
        compiler_params=params(),
    )(tail, conv_sums, sums, skip_sums, norm_sums, gate_sums, gather)


def body(tokens, teacher, lengths, loss_mask, owners, master, first_moment, second_moment):
    capacity = master.shape[0]
    dp, fsdp = lax.axis_size("dp"), lax.axis_size("fsdp")
    devices = dp * fsdp
    me = lax.axis_index(AXES).astype(jnp.int32)
    x_first, y_first, z_first = step_orders(dp, fsdp)
    tie = lambda *values: lax.optimization_barrier(values)

    sent = send_blocks(owners, master, devices, me)
    at_home = lax.all_to_all(sent, AXES, 0, 0, tiled=True)
    owners, tokens, loss_mask, _ = tie(owners, tokens, loss_mask, sent)
    plan = make_plan(owners, capacity, devices, me)
    streams = cut(even(plan["slots"], 3), (x_first, y_first, z_first))
    table = stream_places(plan["home"], plan["slot"], me, streams, devices)
    u0, u1 = plan["unit_slots"]
    sizes = [3 * u0 // 16] * 4
    unit_streams = cut(sizes + [u0 - sum(sizes)], (x_first, y_first, x_first, y_first, z_first))
    order1 = x_first[:2] + x_first[2 + bits_of(fsdp) :] + x_first[2 : 2 + bits_of(fsdp)]
    unit_table, unit_table1 = [], []
    for u in range(UNITS):
        unit = UNITS * plan["order"] + u
        home, slot = unit % devices, unit // devices
        unit_table.append(stream_places(home, slot, me, unit_streams, devices)[:MID0])
        unit_table1.append((place_of(home ^ me, order1) * (u1 + 1) + slot)[MID0:MID1])
    unit_table, unit_table1 = quarters(unit_table), quarters(unit_table1)
    inputs, target = tokens[0], teacher[0]
    (at_home, table, unit_table, unit_table1, received, back_table, row_from, row_block,
     row_used) = tie(
        at_home, table, unit_table, unit_table1, plan["received"], plan["back"],
        plan["row_from"], plan["row_block"], plan["row_used"],
    )
    mine = pick_blocks(received, at_home, [size for _, size, _ in streams])
    parts = []
    for values, (_, _, order) in zip(mine, streams):
        parts += gather_steps(values, order)
    (input_weight, output_weight, conv_weight, conv_bias, dt_bias, a_log, skip, norm_gain,
     gate_gain, hidden, gate, conv_in, dt, ssm, mixed_out, states) = forward(
        table, inputs, parts
    )
    gather = heads_gather()
    block_out, grad_result, grad_branch, local = loss_part(
        lengths, mixed_out, output_weight, inputs, target, loss_mask
    )
    keep1, send1, head, tail = pack_out(
        unit_table1, mixed_out, grad_branch, local, devices, u1 + 1
    )
    grad_branch, send1 = tie(grad_branch, send1)
    got1 = exchange(send1, order1[0])
    grad_ssm, grad_gate, gain_sums = gate_part(grad_branch, output_weight, ssm, gate, gate_gain)
    grad_ssm, keep1, got1 = tie(grad_ssm, keep1, got1)
    keep1, got1 = reduce_step(keep1, got1, order1[1])
    grad_low, sums, skip_sums, conv_sums = backward(
        conv_in, dt, ssm, grad_ssm, grad_gate, states,
        conv_weight, conv_bias, dt_bias, a_log, skip, gather,
    )
    grad_low, keep1, got1 = tie(grad_low, keep1, got1)
    steps1 = order1[2:]
    for step in steps1[:1]:
        keep1, got1 = reduce_step(keep1, got1, step)
    halves = []
    for _, size, _ in unit_streams:
        halves += [devices * size // 2] * 2
    packed = list(pack_in(unit_table, hidden, grad_low, head, halves))
    packed[0], keep1, got1 = tie(packed[0], keep1, got1)
    kept = packed[::2]
    got = [exchange(v, order[0]) for v, (_, _, order) in zip(packed[1::2], unit_streams)]
    *got, grad_low, conv_sums, tail = tie(*got, grad_low, conv_sums, tail)
    for i, (_, _, order) in enumerate(unit_streams):
        kept[i], got[i] = reduce_step(kept[i], got[i], order[1])
    for step in steps1[1:2]:
        keep1, got1 = reduce_step(keep1, got1, step)
    input_grad, norm_sums = input_backward(grad_low, input_weight, inputs, norm_gain, grad_result)
    grad_vec = pack_vectors(tail, conv_sums, sums, skip_sums, norm_sums, gain_sums, gather)
    grad_vec = grad_vec.reshape((NBLK - MID1) * UNITS, UNIT, LANES)
    *got, got1, grad_vec, input_grad = tie(*got, got1, grad_vec, input_grad)
    for step in steps1[2:]:
        keep1, got1 = reduce_step(keep1, got1, step)
    for k in range(2, len(x_first)):
        for i, (_, _, order) in enumerate(unit_streams):
            if i == 0:
                kept[i], got[i], grad_vec = reduce_step(kept[i], got[i], order[k], grad_vec)
            else:
                kept[i], got[i] = reduce_step(kept[i], got[i], order[k])
    back = units_to_owners(back_table, list(zip(kept + [keep1], got + [got1])))
    back, grad_vec = tie(back, grad_vec)
    returned = lax.all_to_all(back, AXES, 0, 0, tiled=True)
    for step in x_first[:2]:
        grad_vec = grad_vec + exchange(grad_vec, step)
    local_sums = keep1[u1] + got1[u1]
    error_sum = jnp.sum(local_sums[: D // LANES])
    divisor = local_sums[D // LANES, 0] * D
    new_first, new_second, new_master = adam(
        row_from,
        row_block,
        row_used,
        divisor,
        returned,
        grad_vec,
        master,
        first_moment,
        second_moment,
    )
    mean_loss = error_sum / divisor
    return (block_out[None], input_grad[None], mean_loss, new_first, new_second, new_master)


def solution(mesh):
    return jax.shard_map(
        body,
        mesh=mesh,
        in_specs=(
            P(AXES, None, None),
            P(AXES, None, None),
            P(AXES),
            P(AXES, None),
            P(),
            P(AXES, None),
            P(AXES, None),
            P(AXES, None),
        ),
        out_specs=(
            P(AXES, None, None),
            P(AXES, None, None),
            P(),
            P(AXES, None),
            P(AXES, None),
            P(AXES, None),
        ),
        check_vma=False,
    )
```

```python
from functools import partial

import jax
import jax.numpy as jnp
import numpy as np
from jax import lax
from jax.experimental import pallas as pl
from jax.experimental.pallas import tpu as pltpu
from jax.sharding import PartitionSpec as P

D = 768
INNER = 1536
NSTATE = 128
HEADDIM = 64
KCONV = 4
SCAN_LEN = 256
PBLOCK = 4096
STEP = 10
HEADS = 24
CONVCH = 1792
PROJ = 3352
PTOT = 3765320
NBLK = 920

LANES = 128
BROWS = PBLOCK // LANES
UNIT = 8
UNITS = BROWS // UNIT
END_IN = D * PROJ
END_OUT = END_IN + INNER * D
MID0 = -(-END_IN // PBLOCK)
MID1 = END_OUT // PBLOCK
N0 = MID0 + NBLK - MID1
N1 = MID1 - MID0
F0_ROWS = N0 * BROWS
IN_ROWS = END_IN // LANES
HEAD_ROWS = MID0 * BROWS - IN_ROWS
TAIL_ROWS = (END_OUT - MID1 * PBLOCK) // LANES
OUT_ROWS = INNER * D // LANES
VEC_ROWS = (NBLK - MID1) * BROWS - TAIL_ROWS
VEC_AT = MID0 * BROWS + TAIL_ROWS
GROUP = 16
GROUPS = D // GROUP
GROUP_ROWS = GROUP * PROJ // LANES
COL_TILES = -(-PROJ // LANES)
WIDE = COL_TILES * LANES
OUT_TILES = D // LANES

NORM_EPS = 1e-05
ADAM_EPS = 1e-08
BETA_ONE = 0.9
BETA_TWO = 0.999
MATRIX_RATE = 0.03
VECTOR_RATE = 0.2
WEIGHT_DECAY = 0.1
PRECISE = lax.Precision.HIGHEST
AXES = ("dp", "fsdp")
VMEM_LIMIT = 60 * 1024 * 1024


def bits_of(count):
    return count.bit_length() - 1


def step_orders(dp, fsdp):
    wide = [("dp", i) for i in range(bits_of(dp))]
    narrow = [("fsdp", i) for i in range(bits_of(fsdp))]
    first = wide[:2] + narrow + wide[2:]
    second = wide[:1] + narrow + wide[1:]
    third = wide[:1] + wide[2:] + wide[1:2] + narrow
    return first, second, third


def cut(sizes, orders):
    streams, at = [], 0
    for size, order in zip(sizes, orders):
        if size:
            streams.append((at, size, order))
        at += size
    return streams


def even(total, parts):
    return [total // parts + (i < total % parts) for i in range(parts)]


def exchange(values, *steps):
    axes = {axis for axis, _ in steps}
    if len(axes) == 1:
        (axis,) = axes
        mask = sum(1 << bit for _, bit in steps)
        pairs = [(i, i ^ mask) for i in range(lax.axis_size(axis))]
        return lax.ppermute(values, axis, pairs)
    low = bits_of(lax.axis_size("fsdp"))
    mask = sum(1 << (bit + (low if axis == "dp" else 0)) for axis, bit in steps)
    count = lax.axis_size("dp") * lax.axis_size("fsdp")
    return lax.ppermute(values, AXES, [(i, i ^ mask) for i in range(count)])


def place_of(relative, order):
    shift_of = {"dp": bits_of(lax.axis_size("fsdp")), "fsdp": 0}
    place = jnp.zeros_like(relative)
    for axis, bit in order:
        place = place * 2 + ((relative >> (shift_of[axis] + bit)) & 1)
    return place


def class_counts(owners, devices):
    block = jnp.arange(NBLK, dtype=jnp.int32)
    mid = ((block >= MID0) & (block < MID1))[None, :]
    device = jnp.arange(devices, dtype=jnp.int32)
    below = owners[None, :] < device[:, None]
    owned = owners[None, :] == device[:, None]

    def total(mask):
        return jnp.sum(mask.astype(jnp.int32), axis=1)

    start = (total(below & ~mid), total(below & mid))
    count = (total(owned & ~mid), total(owned & mid))
    return start, count, total(owned & (block < MID0)[None, :])


def my_counts(owners, me):
    block = jnp.arange(NBLK, dtype=jnp.int32)
    mid = (block >= MID0) & (block < MID1)
    below, owned = owners < me, owners == me
    total = lambda mask: jnp.sum(mask.astype(jnp.int32))
    start = (total(below & ~mid), total(below & mid))
    count = (total(owned & ~mid), total(owned & mid))
    return start, count, total(owned & (block < MID0))


def pair_lanes(capacity, devices):
    return -(-capacity // devices)


def make_plan(owners, capacity, devices, me):
    block = jnp.arange(NBLK, dtype=jnp.int32)
    mid = (block >= MID0) & (block < MID1)
    same = mid[:, None] == mid[None, :]
    before = (owners[None, :] < owners[:, None]) | (
        (owners[None, :] == owners[:, None]) & (block[None, :] < block[:, None])
    )
    order = jnp.sum(before.astype(jnp.int32), axis=1)
    order_in_class = jnp.sum((same & before).astype(jnp.int32), axis=1)
    home, slot = order % devices, order // devices
    device = jnp.arange(devices, dtype=jnp.int32)
    start, count, _ = class_counts(owners, devices)
    my_start, my_count, my_early = my_counts(owners, me)
    pair = pair_lanes(capacity, devices)

    slots = -(-NBLK // devices)
    wanted = me + devices * jnp.arange(slots, dtype=jnp.int32)
    first = start[0] + start[1]
    ends = first + count[0] + count[1]
    owner = jnp.sum((ends[None, :] <= wanted[:, None]).astype(jnp.int32), axis=1)
    owner = jnp.minimum(owner, devices - 1)
    base = jnp.sum(jnp.where(device[None, :] == owner[:, None], first[None, :], 0), axis=1)
    received = owner * pair + jnp.clip((wanted - base) // devices, 0, pair - 1)

    back_pair = (UNITS * capacity + 2 * (devices - 1)) // devices
    unit_slots = (-(-UNITS * N0 // devices), -(-UNITS * N1 // devices))
    lane = jnp.arange(back_pair, dtype=jnp.int32)

    def units_back(kind):
        turn = lane if kind == 0 else back_pair - 1 - lane
        first = UNITS * start[kind][:, None]
        k = (me - first) % devices + turn[None, :] * devices
        return k < UNITS * count[kind][:, None], (first + k) // devices

    valid0, slot0 = units_back(0)
    valid1, slot1 = units_back(1)
    back = jnp.where(valid0, slot0, jnp.where(valid1, unit_slots[0] + slot1, 0)).reshape(-1)

    row = jnp.arange(capacity, dtype=jnp.int32)
    is_mid = (row >= my_early) & (row < my_early + my_count[1])
    k = jnp.where(is_mid, row - my_early, jnp.where(row < my_early, row, row - my_count[1]))
    first = UNITS * jnp.where(is_mid, my_start[1], my_start[0])
    row_used = row < my_count[0] + my_count[1]
    mine = (owners == me)[None, :]
    rank = jnp.sum((mine & (block[None, :] < block[:, None])).astype(jnp.int32), axis=1)
    row_block = jnp.sum(
        jnp.where(mine & (rank[None, :] == row[:, None]), block[None, :], 0), axis=1
    )
    row_from = []
    for u in range(UNITS):
        unit = UNITS * k + u
        turn = unit // devices
        at = ((first + unit) % devices) * back_pair + jnp.where(is_mid, back_pair - 1 - turn, turn)
        late = devices * back_pair + UNITS * (row_block - MID1) + u
        at = jnp.where(row_block >= MID1, late, at)
        row_from.append(jnp.where(row_used, at, 0))
    return dict(
        home=home, slot=slot, slots=slots,
        received=received, order=order_in_class,
        unit_slots=unit_slots, back=back, row_from=quarters(row_from),
        row_used=row_used, row_block=row_block,
    )


def quarters(tables):
    width = -(-tables[0].shape[0] // LANES) * LANES
    return jnp.concatenate([jnp.pad(t, (0, width - t.shape[0])) for t in tables])


def stream_places(home, slot, me, streams, devices):
    relative = home ^ me
    place = jnp.zeros_like(slot)
    for begin, size, order in streams:
        inside = (slot >= begin) & (slot < begin + size)
        at = devices * begin + place_of(relative, order) * size + slot - begin
        place = jnp.where(inside, at, place)
    return place


def cost(microseconds):
    return pl.CostEstimate(
        flops=int(microseconds * 1e9), bytes_accessed=int(microseconds * 3e6), transcendentals=0
    )


ANY = pl.BlockSpec(memory_space=pl.ANY)
VMEM = pl.BlockSpec(memory_space=pltpu.VMEM)
SMEM = pl.BlockSpec(memory_space=pltpu.SMEM)


def params(**extra):
    return pltpu.CompilerParams(vmem_limit_bytes=VMEM_LIMIT, **extra)


def shape(dims, dtype):
    return jax.ShapeDtypeStruct(dims, dtype)


def send_kernel(my_index, owners, master, out, flat, *, devices):
    capacity = master.shape[0]
    me = my_index[0]
    for j in range(BROWS):
        flat[pl.ds(j, capacity, stride=BROWS), :] = master[:, j * LANES : (j + 1) * LANES]
    held = owners[...]
    below, owned = held < me, held == me

    def total(mask):
        return jnp.sum(jnp.where(mask, 1.0, 0.0)).astype(jnp.int32)

    start, count = total(below), total(owned)
    pair = out.shape[0] // devices

    def step(home, carry):
        for s in range(pair):
            k = lax.rem(home - start + devices * NBLK, devices) + s * devices
            row = jnp.where(k < count, k, 0)
            rows = pl.ds(pl.multiple_of(row * BROWS, BROWS), BROWS)
            out[home * pair + s] = flat[rows, :].astype(out.dtype)
        return carry

    lax.fori_loop(0, devices, step, 0)


def send_blocks(owners, master, devices, me):
    rows = -(-NBLK // (8 * LANES)) * 8
    held = jnp.pad(owners, (0, rows * LANES - NBLK), constant_values=1 << 20).reshape(rows, LANES)
    count = devices * pair_lanes(master.shape[0], devices)
    return pl.pallas_call(
        partial(send_kernel, devices=devices),
        out_shape=shape((count, BROWS, LANES), jnp.bfloat16),
        in_specs=[SMEM, VMEM, VMEM],
        out_specs=VMEM,
        scratch_shapes=[pltpu.VMEM((master.shape[0] * BROWS, LANES), jnp.float32)],
        compiler_params=params(),
    )(me.reshape(1), held, master)


def pick_kernel(table, source, *outs):
    at = 0
    for out in outs:

        def step(i, carry, out=out, at=at):
            out[i] = source[table[at + i]]
            return carry

        lax.fori_loop(0, out.shape[0], step, 0)
        at += out.shape[0]


def pick_blocks(table, source, sizes):
    return pl.pallas_call(
        pick_kernel,
        out_shape=tuple(shape((n,) + source.shape[1:], source.dtype) for n in sizes),
        in_specs=[SMEM, VMEM],
        out_specs=(VMEM,) * len(sizes),
        compiler_params=params(),
    )(table, source)


def back_kernel(table, *refs, sizes):
    sources, (out, held) = refs[:-2], refs[-2:]
    at = i = 0
    for size in sizes:
        n = sources[i].shape[0]
        total = sources[i][...]
        for k in range(1, size):
            total = total + sources[i + k][0:n]
        held[at : at + n] = total
        at += n
        i += size

    def step(i, carry):
        for u in range(8):
            out[i * 8 + u] = held[table[i * 8 + u]]
        return carry

    total = out.shape[0]
    lax.fori_loop(0, total // 8, step, 0)


def units_to_owners(table, groups):
    return pl.pallas_call(
        partial(back_kernel, sizes=[len(g) for g in groups]),
        out_shape=shape((table.shape[0], UNIT, LANES), jnp.float32),
        in_specs=[SMEM] + [VMEM] * sum(len(g) for g in groups),
        out_specs=VMEM,
        scratch_shapes=[pltpu.VMEM((sum(g[0].shape[0] for g in groups), UNIT, LANES), jnp.float32)],
        compiler_params=params(),
    )(table, *[v for g in groups for v in g])


def row_start(rho):
    return (PROJ * rho) // LANES, (PROJ * rho) % LANES


def copy_all(pairs, sem):
    copies = [pltpu.make_async_copy(a, b, sem.at[i]) for i, (a, b) in enumerate(pairs)]
    for c in copies:
        c.start()
    for c in copies:
        c.wait()


def spread_blocks(table, first, held, flat, count, first_row):
    def one(i):
        at = pl.multiple_of(first_row + i * BROWS, 16)
        flat[pl.ds(at, BROWS), :] = held[table[first + i]].astype(jnp.float32)

    def step(i, carry):
        for u in range(16):
            one(i * 16 + u)
        return carry

    lax.fori_loop(0, count // 16, step, 0)
    for i in range(count // 16 * 16, count):
        one(i)


def unpack_vectors(flat, conv_weight, conv_bias, dt_bias, a_log, skip, norm_gain, gate_gain):
    bf16, f32 = jnp.bfloat16, jnp.float32
    tiles = CONVCH // LANES
    row = lax.broadcasted_iota(jnp.int32, (LANES, LANES), 0)
    col = lax.broadcasted_iota(jnp.int32, (LANES, LANES), 1)
    per_tile = LANES // KCONV
    for k in range(KCONV):
        total = jnp.zeros((tiles, LANES), f32)
        for q in range(KCONV):
            rows = flat[pl.ds(VEC_AT + q, tiles, stride=KCONV), :].astype(bf16)
            chosen = (row == KCONV * (col % per_tile) + k) & (col // per_tile == q)
            total = total + jnp.dot(rows, chosen.astype(bf16), preferred_element_type=f32)
        for i in range(tiles):
            conv_weight[k : k + 1, i * LANES : (i + 1) * LANES] = total[i : i + 1, :]
    bias_at = VEC_AT + tiles * KCONV
    for i in range(tiles):
        conv_bias[:, i * LANES : (i + 1) * LANES] = flat[bias_at + i : bias_at + i + 1, :]
    at = bias_at + tiles
    lane = lax.broadcasted_iota(jnp.int32, (8, LANES), 1)
    first = flat[at : at + 8, :]
    three = []
    for i in range(3):
        moved = pltpu.roll(first, LANES - i * HEADS, 1) if i else first
        three.append(jnp.where(lane < HEADS, moved, 0.0))
    dt_bias[...] = three[0][0:1, :]
    a_log[...] = three[1][0:1, :]
    for j in range(INNER // LANES):
        h = lax.broadcasted_iota(jnp.int32, (LANES, LANES), 0)
        c = lax.broadcasted_iota(jnp.int32, (LANES, LANES), 1) + j * LANES
        spread = (h == c // HEADDIM).astype(bf16)
        wide = jnp.dot(three[2].astype(bf16), spread, preferred_element_type=f32)
        skip[:, j * LANES : (j + 1) * LANES] = wide[0:1, :]
    shift = 3 * HEADS
    for out, begin, width in ((norm_gain, at, D), (gate_gain, at + D // LANES, INNER)):
        for j in range(width // LANES):
            x = pltpu.roll(flat[begin + j : begin + j + 1, :], LANES - shift, 1)
            y = pltpu.roll(flat[begin + j + 1 : begin + j + 2, :], LANES - shift, 1)
            out[:, j * LANES : (j + 1) * LANES] = jnp.where(lane[0:1] < LANES - shift, x, y)


def unpack_weights(table, parts, w_in, w_out, vectors, held, flat, flat_out, tile, sem):
    pairs, at = [], 0
    for part in parts:
        pairs.append((part, held.at[pl.ds(at, part.shape[0])]))
        at += part.shape[0]
    copy_all(pairs, sem)
    spread_blocks(table, 0, held, flat, MID0, 0)
    spread_blocks(table, MID1, held, flat, NBLK - MID1, MID0 * BROWS)
    spread_blocks(table, MID0, held, flat_out, N1, HEAD_ROWS)
    flat_out[0:HEAD_ROWS, :] = flat[IN_ROWS : IN_ROWS + HEAD_ROWS, :]
    flat_out[OUT_ROWS - TAIL_ROWS :, :] = flat[MID0 * BROWS : MID0 * BROWS + TAIL_ROWS, :]
    unpack_vectors(flat, *vectors)
    rows = 128

    def out_step(i, carry):
        at = pl.multiple_of(i * rows, rows)
        for j in range(OUT_TILES):
            x = flat_out[pl.ds(at * OUT_TILES + j, rows, stride=OUT_TILES), :]
            w_out[pl.ds(at, rows), j * LANES : (j + 1) * LANES] = x.astype(jnp.bfloat16)
        return carry

    lax.fori_loop(0, INNER // rows, out_step, 0)
    lane = lax.broadcasted_iota(jnp.int32, (GROUPS, LANES), 1)

    def columns(j):
        for rho in range(GROUP):
            c, s = row_start(rho)
            x = flat[pl.ds(c + j, GROUPS, stride=GROUP_ROWS), :]
            if s:
                y = flat[pl.ds(c + j + 1, GROUPS, stride=GROUP_ROWS), :]
                x = jnp.where(
                    lane < LANES - s,
                    pltpu.roll(x, LANES - s, 1),
                    pltpu.roll(y, LANES - s, 1),
                )
            tile[pl.ds(rho, GROUPS, stride=GROUP), :] = x

    def step(j, carry):
        columns(j)
        w_in[:, pl.ds(pl.multiple_of(j * LANES, LANES), LANES)] = tile[...].astype(jnp.bfloat16)
        return carry

    lax.fori_loop(0, COL_TILES - 1, step, 0)
    columns(COL_TILES - 1)
    last = (COL_TILES - 1) * LANES
    inside = lax.broadcasted_iota(jnp.int32, (D, LANES), 1) < PROJ - last
    w_in[:, last:] = jnp.where(inside, tile[...], 0.0).astype(jnp.bfloat16)


def unpack_scratch(held, count):
    return [
        pltpu.VMEM((held, BROWS, LANES), jnp.bfloat16),
        pltpu.VMEM((F0_ROWS, LANES), jnp.float32),
        pltpu.VMEM((OUT_ROWS, LANES), jnp.float32),
        pltpu.VMEM((D, LANES), jnp.float32),
        pltpu.SemaphoreType.DMA((count,)),
    ]


def permute_units(table, flat, count, first_row, staged):
    many = 16
    width = table.shape[0] // UNITS

    def one(i):
        for u in range(UNITS):
            at = first_row + i * BROWS + u * UNIT
            at = at if isinstance(at, int) else pl.multiple_of(at, UNIT)
            staged[table[u * width + i]] = flat[pl.ds(at, UNIT), :]

    def step(i, carry):
        for b in range(many):
            one(i * many + b)
        return carry

    lax.fori_loop(0, count // many, step, 0)
    for i in range(count // many * many, count):
        one(i)


def pack_in_kernel(table, hidden, grad, head, *refs):
    outs, (turned, tiles, flat, staged, sem) = refs[:-5], refs[-5:]
    turned[...] = hidden[...].T
    lane = lax.broadcasted_iota(jnp.int32, (GROUPS, LANES), 1)

    def product(p, count):
        at = p * 2 * LANES
        at = at if isinstance(at, int) else pl.multiple_of(at, 2 * LANES)
        return jnp.dot(
            turned[...], grad[:, pl.ds(at, count * LANES)], preferred_element_type=jnp.float32
        )

    def put(p, value):
        for k in range(value.shape[1] // LANES):
            at = (p * 2 + k) * D
            at = at if isinstance(at, int) else pl.multiple_of(at, D)
            tiles[pl.ds(at, D), :] = value[:, k * LANES : (k + 1) * LANES]

    def load(rho, j):
        return tiles[pl.ds(j * D + rho, GROUPS, stride=GROUP), :]

    def whole(rho, i):
        first = -(-PROJ * rho // LANES)
        col0 = first * LANES - PROJ * rho
        x = load(rho, i)
        if col0:
            x = jnp.where(
                lane < LANES - col0,
                pltpu.roll(x, LANES - col0, 1),
                pltpu.roll(load(rho, i + 1), LANES - col0, 1),
            )
        flat[pl.ds(first + i, GROUPS, stride=GROUP_ROWS), :] = x

    put(0, product(0, 2))
    put(1, product(1, 2))
    pairs = COL_TILES // 2

    def step(p, carry):
        for i in range(2):
            for rho in range(GROUP):
                whole(rho, p * 2 + i)
        put(p + 2, product(p + 2, 2))
        return carry

    lax.fori_loop(0, pairs - 2, step, 0)
    put(pairs, product(pairs, COL_TILES % 2))
    for rho in range(GROUP):
        first = -(-PROJ * rho // LANES)
        col0 = first * LANES - PROJ * rho
        full = (PROJ - col0) // LANES
        for i in range((pairs - 2) * 2, full):
            whole(rho, i)
        left = PROJ - col0 - full * LANES
        if left:
            begin = col0 + full * LANES
            j, s = begin // LANES, begin % LANES
            x = pltpu.roll(load(rho, j), LANES - s, 1) if s else load(rho, j)
            if s + left > LANES:
                x = jnp.where(lane < LANES - s, x, pltpu.roll(load(rho, j + 1), LANES - s, 1))
            y = pltpu.roll(load(rho + 1, 0), left, 1)
            flat[pl.ds(first + full, GROUPS, stride=GROUP_ROWS), :] = jnp.where(lane < left, x, y)
    flat[IN_ROWS : IN_ROWS + HEAD_ROWS, :] = head[...]
    permute_units(table, flat, MID0, 0, staged)
    copies, at = [], 0
    for out in outs:
        copies.append((staged.at[pl.ds(at, out.shape[0])], out))
        at += out.shape[0]
    copy_all(copies, sem)


def pack_in(table, hidden, grad, head, sizes):
    return pl.pallas_call(
        pack_in_kernel,
        out_shape=tuple(shape((n, UNIT, LANES), jnp.float32) for n in sizes),
        in_specs=[SMEM, VMEM, VMEM, VMEM],
        out_specs=(ANY,) * len(sizes),
        scratch_shapes=[
            pltpu.VMEM((D, hidden.shape[0]), jnp.bfloat16),
            pltpu.VMEM((COL_TILES * D, LANES), jnp.float32),
            pltpu.VMEM((MID0 * BROWS, LANES), jnp.float32),
            pltpu.VMEM((sum(sizes), UNIT, LANES), jnp.float32),
            pltpu.SemaphoreType.DMA((len(sizes),)),
        ],
        compiler_params=params(),
        cost_estimate=cost(20),
    )(table, hidden, grad, head)


def pack_out_kernel(
    table, mixed_out, grad, local, keep, send, head, tail, turned, flat, out, sem, *, slots
):
    rows = 256

    def step(i, carry):
        at = pl.multiple_of(i * rows, rows)
        turned[...] = mixed_out[:, pl.ds(at, rows)].T
        product = jnp.dot(turned[...], grad[...], preferred_element_type=jnp.float32)
        for j in range(OUT_TILES):
            flat[pl.ds(at * OUT_TILES + j, rows, stride=OUT_TILES), :] = product[
                :, j * LANES : (j + 1) * LANES
            ]
        return carry

    lax.fori_loop(0, INNER // rows, step, 0)
    head[...] = flat[0:HEAD_ROWS, :]
    tail[...] = flat[OUT_ROWS - TAIL_ROWS : OUT_ROWS, :]
    permute_units(table, flat, N1, HEAD_ROWS, out)

    def add_local(i, carry):
        out[i * slots + slots - 1] = local[...]
        return carry

    lax.fori_loop(0, out.shape[0] // slots, add_local, 0)
    half = keep.shape[0]
    copy_all([(out.at[pl.ds(0, half)], keep), (out.at[pl.ds(half, half)], send)], sem)


def pack_out(table, mixed_out, grad, local, devices, slots):
    return pl.pallas_call(
        partial(pack_out_kernel, slots=slots),
        out_shape=(
            shape((devices * slots // 2, UNIT, LANES), jnp.float32),
            shape((devices * slots // 2, UNIT, LANES), jnp.float32),
            shape((HEAD_ROWS, LANES), jnp.float32),
            shape((TAIL_ROWS, LANES), jnp.float32),
        ),
        in_specs=[SMEM, VMEM, VMEM, VMEM],
        out_specs=(ANY, ANY, VMEM, VMEM),
        scratch_shapes=[
            pltpu.VMEM((256, mixed_out.shape[0]), jnp.bfloat16),
            pltpu.VMEM((OUT_ROWS, LANES), jnp.float32),
            pltpu.VMEM((devices * slots, UNIT, LANES), jnp.float32),
            pltpu.SemaphoreType.DMA((2,)),
        ],
        compiler_params=params(),
    )(table, mixed_out, grad, local)


def adam_kernel(
    table, row_block, row_used, scale, got, late, master, first, second,
    o_first, o_second, o_master, flat, held, limit, used,
):
    capacity = master.shape[0]

    def step(i, carry):
        for u in range(UNITS):
            at = table[u * (table.shape[0] // UNITS) + i]
            rows = pl.ds(pl.multiple_of(i * BROWS + u * UNIT, UNIT), UNIT)
            flat[rows, :] = held[at]
        limit[pl.ds(i, 1), :] = jnp.full((1, LANES), END_OUT - row_block[i] * PBLOCK, jnp.int32)
        used[pl.ds(i, 1), :] = jnp.full((1, LANES), row_used[i], jnp.int32)
        return carry

    held[0 : got.shape[0]] = got[...]
    held[got.shape[0] :] = late[...]
    lax.fori_loop(0, capacity, step, 0)
    lane = lax.broadcasted_iota(jnp.int32, (capacity, LANES), 1)
    divisor = scale[0]
    for j in range(BROWS):
        cols = slice(j * LANES, (j + 1) * LANES)
        grad = jnp.where(used[...] > 0, flat[pl.ds(j, capacity, stride=BROWS), :], 0.0) / divisor
        matrix = lane + j * LANES < limit[...]
        weights = master[:, cols]
        new_first = BETA_ONE * first[:, cols] + (1.0 - BETA_ONE) * grad
        new_second = BETA_TWO * second[:, cols] + (1.0 - BETA_TWO) * grad * grad
        normal = (
            new_first
            / (1.0 - BETA_ONE**STEP)
            / (jnp.sqrt(new_second / (1.0 - BETA_TWO**STEP)) + ADAM_EPS)
        )
        rate = jnp.where(matrix, MATRIX_RATE, VECTOR_RATE)
        decay = jnp.where(matrix, WEIGHT_DECAY, 0.0)
        o_first[:, cols] = new_first
        o_second[:, cols] = new_second
        o_master[:, cols] = weights - rate * (normal + decay * weights)


def adam(table, row_block, row_used, divisor, got, late, master, first, second):
    capacity = master.shape[0]
    return pl.pallas_call(
        adam_kernel,
        out_shape=(shape(master.shape, jnp.float32),) * 3,
        in_specs=[SMEM] * 4 + [VMEM] * 5,
        out_specs=(VMEM,) * 3,
        scratch_shapes=[
            pltpu.VMEM((capacity * BROWS, LANES), jnp.float32),
            pltpu.VMEM((got.shape[0] + late.shape[0], UNIT, LANES), jnp.float32),
            pltpu.VMEM((capacity, LANES), jnp.int32),
            pltpu.VMEM((capacity, LANES), jnp.int32),
        ],
        compiler_params=params(),
    )(
        table, row_block, row_used.astype(jnp.int32), divisor.reshape(1), got, late, master, first, second
    )


def doubled(values, step):
    return jnp.concatenate([values, exchange(values, step)], axis=0)


def gather_steps(values, order):
    for step in order[:0:-1]:
        values = doubled(values, step)
    return values, exchange(values, order[0])


def reduce_step(kept, got, step, extra=None):
    half = kept.shape[0] // 2
    given = kept[half:] + got[half:]
    if extra is None:
        return kept[:half] + got[:half], exchange(given, step)
    arrived = exchange(jnp.concatenate([given, extra]), step)
    return kept[:half] + got[:half], arrived[:half], extra + arrived[half:]


CHUNK = 128
PAIRS = HEADS // 2
MIXW = INNER + 2 * NSTATE
DT_AT = INNER + CONVCH
F32 = jnp.float32
BF16 = jnp.bfloat16
NN = (((1,), (0,)), ((), ()))
NT = (((1,), (1,)), ((), ()))


def dot(a, b, dims=NN):
    return lax.dot_general(a, b, dims, preferred_element_type=F32)


def split(v):
    high = v.astype(BF16)
    return high, (v - high.astype(F32)).astype(BF16)


def dot3(a, b, dims=NN):
    ah, al = a
    bh, bl = b
    return dot(ah, bh, dims) + (dot(ah, bl, dims) + dot(al, bh, dims))


def heads_gather():
    return jnp.asarray(np.repeat(np.eye(HEADS, LANES, dtype=np.float32), HEADDIM, axis=0), BF16)


def three_parts(v):
    high = v.astype(BF16).astype(F32)
    rest = v - high
    middle = rest.astype(BF16).astype(F32)
    low = rest - middle
    return (high + pltpu.roll(middle, 32, 1) + pltpu.roll(low, 64, 1)).astype(BF16)


def triangle_sum(tri, v):
    parts = dot(tri, three_parts(v))
    lane = lax.broadcasted_iota(jnp.int32, parts.shape, 1)
    total = parts + pltpu.roll(parts, LANES - 32, 1) + pltpu.roll(parts, LANES - 64, 1)
    return jnp.where(lane < HEADS, total, 0.0)


def chunk_decays(dt, dt_bias, a_log):
    lane = lax.broadcasted_iota(jnp.int32, (CHUNK, LANES), 1)
    row = lax.broadcasted_iota(jnp.int32, (CHUNK, LANES), 0)
    shifted = dt + dt_bias
    delta = jnp.where(
        lane < HEADS, jnp.maximum(shifted, 0.0) + jnp.log1p(jnp.exp(-jnp.abs(shifted))), 0.0
    )
    rate = -jnp.exp(a_log)
    lower = (row >= lane).astype(BF16)
    cum = triangle_sum(lower, delta * rate)
    last = cum[CHUNK - 1 : CHUNK, :]
    return shifted, delta, rate, cum, last


def pair_mask():
    lane = lax.broadcasted_iota(jnp.int32, (CHUNK, LANES), 1)
    low = (lane < HEADDIM).astype(F32)
    return low.astype(BF16), (1.0 - low).astype(BF16)


QUADS = HEADS // 4
QWIDTH = 4 * HEADDIM


def sigmoid(v):
    return 0.5 * jnp.tanh(0.5 * v) + 0.5


def silu(v):
    return v * sigmoid(v)


def side_by_side(v):
    high, low = split(v)
    return jnp.concatenate([high, low], axis=1), high


def dot_parts(a, b):
    ahl, ah = a
    bh, bl = b
    return dot(ahl, jnp.concatenate([bh, bh], axis=0)) + dot(ah, bl)


def dot_turned(a, b):
    ah, al = a
    bh, bl = b
    both = dot(ah, jnp.concatenate([bh, bl], axis=0), NT)
    n = bh.shape[0]
    return both[:, :n] + both[:, n:] + dot(al, bh, NT)


def widen(delta, cum, quad):
    lane = lax.broadcasted_iota(jnp.int32, (CHUNK, LANES), 1)
    over = lambda v, h: jnp.broadcast_to(v[:, h : h + 1], (CHUNK, LANES))
    first = 4 * quad
    columns = [over(cum, first + k) for k in range(4)]
    rates = [over(delta, first + k) for k in range(4)]
    pair = lambda vs: jnp.concatenate(
        [jnp.where(lane < HEADDIM, vs[0], vs[1]), jnp.where(lane < HEADDIM, vs[2], vs[3])], axis=1
    )
    return pair(rates), pair(columns), columns


def pair_rows(parts, j, low, high):
    cols = slice(j * LANES, (j + 1) * LANES)
    return [jnp.concatenate([p[:, cols] * low, p[:, cols] * high], axis=0) for p in parts]


def scan_chunk(mixed, dt, dt_bias, a_log, skip, state, put):
    _, delta, _, cum, last = chunk_decays(dt, dt_bias, a_log)
    lane = lax.broadcasted_iota(jnp.int32, (CHUNK, LANES), 1)
    row = lax.broadcasted_iota(jnp.int32, (CHUNK, LANES), 0)
    bias = jnp.where(row >= lane, 0.0, -1e30)
    cum_t = cum.T
    inputs_b = mixed[:, INNER : INNER + NSTATE]
    readout = mixed[:, INNER + NSTATE :]
    affinity = dot3(split(readout), split(inputs_b), NT)
    readout_parts = side_by_side(readout)
    b_parts = side_by_side(inputs_b.T)
    low, high = pair_mask()
    for quad in range(QUADS):
        cols = slice(quad * QWIDTH, (quad + 1) * QWIDTH)
        wide_delta, wide_cum, columns = widen(delta, cum, quad)
        values = mixed[:, cols]
        scaled = values * wide_delta
        parts = split(scaled)
        outs = []
        for j in range(2):
            right_h, right_l = pair_rows(parts, j, low, high)
            left = []
            for k in range(2):
                h = 4 * quad + 2 * j + k
                within = jnp.exp(columns[2 * j + k] - cum_t[h : h + 1, :] + bias)
                left.append(split(affinity * within))
            left_h = jnp.concatenate([left[0][0], left[1][0]], axis=1)
            left_l = jnp.concatenate([left[0][1], left[1][1]], axis=1)
            both = dot(left_h, jnp.concatenate([right_h, right_l], axis=1))
            outs.append(both[:, :LANES] + both[:, LANES:] + dot(left_l, right_h))
        carried = state[:, cols]
        grown = jnp.exp(wide_cum)
        out = jnp.concatenate(outs, axis=1) + dot_parts(readout_parts, split(carried)) * grown
        tail = jnp.exp(wide_cum[CHUNK - 1 :] - wide_cum)
        state[:, cols] = carried * grown[CHUNK - 1 :] + dot_parts(b_parts, split(scaled * tail))
        put(quad, out + skip[:, cols] * values)


FORWARD_ROWS = 2 * CHUNK


def forward_kernel(table, tokens, *refs, count):
    parts, refs = refs[:count], refs[count:]
    (w_in_kept, w_out_kept, conv_weight, conv_bias, dt_bias, a_log, skip, norm_gain, gain,
     hidden, gate, conv_in, dt, ssm, mixed_out, states) = refs[:16]
    w_in, w_out, state, before, mixed, shift, out_sem, *scratch = refs[16:]
    keep = [
        pltpu.make_async_copy(w_in, w_in_kept, out_sem.at[0]),
        pltpu.make_async_copy(w_out, w_out_kept, out_sem.at[1]),
    ]

    @pl.when(pl.program_id(0) == 0)
    def _():
        vectors = (conv_weight, conv_bias, dt_bias, a_log, skip, norm_gain, gain)
        unpack_weights(table, parts, w_in, w_out, vectors, *scratch)
        for copy in keep:
            copy.start()
        state[...] = jnp.zeros_like(state)
        before[...] = jnp.zeros_like(before)

    x = tokens[...].astype(F32)
    inverse = lax.rsqrt(jnp.mean(x * x, axis=1, keepdims=True) + NORM_EPS)
    h = (x * inverse * norm_gain[...]).astype(BF16)
    hidden[...] = h
    dt[...] = dot(h, w_in[:, DT_AT:])
    wide = 2 * LANES
    for tile in range(CONVCH // wide):
        at = tile * wide
        product = dot(h, w_in[:, INNER + at : INNER + at + wide])
        conv_in[:, at : at + wide] = product
        for half in range(2):
            cols = slice(at + half * LANES, at + (half + 1) * LANES)
            rows = product[:, half * LANES : (half + 1) * LANES]
            earlier = before[:, cols]
            terms = moved_down(shift.at[tile * 2 + half], rows, earlier) + [rows]
            before[:, cols] = rows[FORWARD_ROWS - 8 :]
            mixed[:, cols] = silu(conv_sum(terms, conv_weight[:, cols], conv_bias[:, cols]))
    for tile in range(INNER // wide):
        cols = slice(tile * wide, (tile + 1) * wide)
        gate[:, cols] = dot(h, w_in[:, cols])
    for sub in range(FORWARD_ROWS // CHUNK):
        rows = slice(sub * CHUNK, (sub + 1) * CHUNK)
        states[sub] = state[...]
        squares = [jnp.zeros((CHUNK, LANES), F32)]

        def put(quad, out, rows=rows, squares=squares):
            cols = slice(quad * QWIDTH, (quad + 1) * QWIDTH)
            ssm[rows, cols] = out
            gated = out * silu(gate[rows, cols])
            first, second = gated[:, :LANES], gated[:, LANES:]
            squares[0] = squares[0] + first * first + second * second

        scan_chunk(
            mixed[rows, :], dt[rows, :], dt_bias[...], a_log[...], skip, state, put
        )
        rho = lax.rsqrt(jnp.sum(squares[0], axis=1, keepdims=True) * (1.0 / INNER) + NORM_EPS)
        for j in range(PAIRS):
            cols = slice(j * LANES, (j + 1) * LANES)
            gated = ssm[rows, cols] * silu(gate[rows, cols])
            mixed_out[rows, cols] = (gated * rho * gain[:, cols]).astype(BF16)

    @pl.when(pl.program_id(0) == pl.num_programs(0) - 1)
    def _():
        for copy in keep:
            copy.wait()


def forward(table, tokens, parts):
    length = tokens.shape[0]
    by_row = lambda width: pl.BlockSpec((FORWARD_ROWS, width), lambda i: (i, 0))
    per_step = FORWARD_ROWS // CHUNK
    vectors = [(KCONV, CONVCH), (1, CONVCH), (1, LANES), (1, LANES), (1, INNER), (1, D), (1, INNER)]
    return pl.pallas_call(
        partial(forward_kernel, count=len(parts)),
        grid=(length // FORWARD_ROWS,),
        out_shape=[shape((D, WIDE), BF16), shape((INNER, D), BF16)]
        + [shape(v, F32) for v in vectors]
        + [
            shape((length, D), BF16),
            shape((length, INNER), F32),
            shape((length, MIXW), F32),
            shape((length, LANES), F32),
            shape((length, INNER), F32),
            shape((length, INNER), BF16),
            shape((length // CHUNK, NSTATE, INNER), F32),
        ],
        in_specs=[SMEM, by_row(D)] + [ANY] * len(parts),
        out_specs=[ANY, ANY]
        + [pl.BlockSpec(v, lambda i: (0, 0)) for v in vectors]
        + [
            by_row(D),
            by_row(INNER),
            by_row(MIXW),
            by_row(LANES),
            by_row(INNER),
            by_row(INNER),
            pl.BlockSpec((per_step, NSTATE, INNER), lambda i: (i, 0, 0)),
        ],
        scratch_shapes=[
            pltpu.VMEM((D, WIDE), BF16),
            pltpu.VMEM((INNER, D), BF16),
            pltpu.VMEM((NSTATE, INNER), F32),
            pltpu.VMEM((8, MIXW), F32),
            pltpu.VMEM((FORWARD_ROWS, MIXW), F32),
            pltpu.VMEM((MIXW // LANES, FORWARD_ROWS + 8, LANES), F32),
            pltpu.SemaphoreType.DMA((2,)),
        ]
        + unpack_scratch(sum(part.shape[0] for part in parts), len(parts)),
        compiler_params=params(),
        cost_estimate=cost(50),
    )(table, tokens, *parts)


def eights(v):
    return jnp.sum(v.reshape(v.shape[0] // 8, 8, v.shape[1]), axis=0)


def backward_kernel(
    conv_in, earlier, dt, ssm, grad, grad_gate, states, conv_weight, conv_bias, dt_bias, a_log, skip,
    gather, grad_low, sums, skip_sums, conv_sums,
    grad_state, to_sum, mixed, slope, grad_mixed, following, shift,
):
    @pl.when(pl.program_id(0) == 0)
    def _():
        grad_state[...] = jnp.zeros_like(grad_state)
        sums[...] = jnp.zeros_like(sums)
        skip_sums[...] = jnp.zeros_like(skip_sums)
        conv_sums[...] = jnp.zeros_like(conv_sums)
        following[...] = jnp.zeros_like(following)

    begins = pl.program_id(0) == pl.num_programs(0) - 1

    for tile in range(MIXW // LANES):
        cols = slice(tile * LANES, (tile + 1) * LANES)
        rows = conv_in[:, cols]
        before = jnp.where(begins, 0.0, earlier[:, cols])
        terms = moved_down(shift.at[tile], rows, before) + [rows]
        value = conv_sum(terms, conv_weight[:, cols], conv_bias[:, cols])
        sig = sigmoid(value)
        mixed[:, cols] = value * sig
        slope[:, cols] = sig * (1.0 + value * (1.0 - sig))

    shifted, delta, rate, cum, last = chunk_decays(dt[...], dt_bias[...], a_log[...])
    lane = lax.broadcasted_iota(jnp.int32, (CHUNK, LANES), 1)
    row = lax.broadcasted_iota(jnp.int32, (CHUNK, LANES), 0)
    bias = jnp.where(lane >= row, 0.0, -1e30)
    heads = lane < HEADS
    cum_t = cum.T
    inputs_b = mixed[:, INNER : INNER + NSTATE]
    readout = mixed[:, INNER + NSTATE :]
    b_parts, c_parts = split(inputs_b), split(readout)
    b_wide = side_by_side(inputs_b)
    c_turned = side_by_side(readout.T)
    affinity = dot3(b_parts, c_parts, NT)
    low, high = pair_mask()
    grad_affinity = jnp.zeros((CHUNK, CHUNK), F32)
    grad_b = jnp.zeros((CHUNK, NSTATE), F32)
    grad_c = jnp.zeros((CHUNK, NSTATE), F32)
    last_row = lax.broadcasted_iota(jnp.int32, (CHUNK, QWIDTH), 0) == CHUNK - 1
    for quad in range(QUADS):
        cols = slice(quad * QWIDTH, (quad + 1) * QWIDTH)
        wide_delta, wide_cum, columns = widen(delta, cum, quad)
        grown = jnp.exp(wide_cum)
        tail = jnp.exp(wide_cum[CHUNK - 1 :] - wide_cum)
        end = grown[CHUNK - 1 :]
        values = mixed[:, cols]
        pulled = grad[:, cols]
        scaled = values * wide_delta
        x_parts, p_parts = split(scaled), split(pulled)
        outs = []
        for j in range(2):
            half = slice(j * LANES, (j + 1) * LANES)
            xh, xl = x_parts[0][:, half], x_parts[1][:, half]
            right_h, right_l = pair_rows(p_parts, j, low, high)
            pull = dot(
                jnp.concatenate([xh, xl], axis=1),
                jnp.concatenate([right_h, right_h], axis=1),
                NT,
            ) + dot(xh, right_l, NT)
            kernels = []
            for k in range(2):
                h = 4 * quad + 2 * j + k
                within = jnp.exp(cum_t[h : h + 1, :] - columns[2 * j + k] + bias)
                kernels.append(split(affinity * within))
                grad_affinity = grad_affinity + within * pull[:, k * CHUNK : (k + 1) * CHUNK]
            kernel_h = jnp.concatenate([kernels[0][0], kernels[1][0]], axis=1)
            kernel_l = jnp.concatenate([kernels[0][1], kernels[1][1]], axis=1)
            both = dot(kernel_h, jnp.concatenate([right_h, right_l], axis=1))
            outs.append(both[:, :LANES] + both[:, LANES:] + dot(kernel_l, right_h))
        late = grad_state[:, cols]
        late_parts = split(late)
        early = states[0, :, cols]
        from_state = dot_parts(b_wide, late_parts) * tail
        grad_scaled = jnp.concatenate(outs, axis=1) + from_state
        pulled_cum = split(pulled * grown)
        grad_c = grad_c + dot_turned(pulled_cum, split(early))
        grad_b = grad_b + dot_turned(split(scaled * tail), late_parts)
        grad_state[:, cols] = late * end + dot_parts(c_turned, pulled_cum)
        grad_mixed[:, cols] = grad_scaled * wide_delta + skip[:, cols] * pulled
        skip_sums[:, cols] += jnp.sum(pulled * values, axis=0, keepdims=True)
        to_sum[:CHUNK, cols] = grad_scaled * values
        inner = pulled * (ssm[:, cols] - skip[:, cols] * values) - scaled * grad_scaled
        extra = jnp.sum(scaled * from_state, axis=0, keepdims=True) + end * jnp.sum(
            late * early, axis=0, keepdims=True
        )
        to_sum[CHUNK:, cols] = inner + jnp.where(last_row, extra, 0.0)
    ga_parts = split(grad_affinity)
    grad_mixed[:, INNER : INNER + NSTATE] = grad_b + dot3(ga_parts, c_parts)
    grad_mixed[:, INNER + NSTATE :] = grad_c + dot3(split(grad_affinity.T), b_parts)


    def by_head(v):
        high, low = split(v)
        return dot(high, gather[...]) + dot(low, gather[...])

    direct, grad_cum = by_head(to_sum[:CHUNK, :]), by_head(to_sum[CHUNK:, :])
    upper = (lane >= row).astype(BF16)
    after = triangle_sum(upper, grad_cum)
    grad_delta = direct + rate * after
    grad_raw = jnp.where(heads, grad_delta * sigmoid(shifted), 0.0)
    grad_low[:, DT_AT:] = grad_raw.astype(BF16)
    sums[0:1, :] += jnp.sum(grad_raw, axis=0, keepdims=True)
    sums[1:2, :] += rate * jnp.sum(delta * after, axis=0, keepdims=True)
    grad_low[:, :INNER] = grad_gate[...]
    for tile in range(MIXW // LANES):
        cols = slice(tile * LANES, (tile + 1) * LANES)
        w = conv_weight[:, cols]
        g = grad_mixed[:, cols] * slope[:, cols]
        rows = conv_in[:, cols]
        later = following[:, cols]
        total = jnp.zeros((CHUNK, LANES), F32)
        arriving = moved_up(shift.at[tile], g, later) + [g]
        for k in range(KCONV):
            conv_sums[8 * k : 8 * k + 8, cols] += eights(rows * arriving[k])
            total = total + arriving[k] * w[k : k + 1]
        conv_sums[8 * KCONV :, cols] += eights(g)
        following[:, cols] = g[:8]
        grad_low[:, INNER + tile * LANES : INNER + (tile + 1) * LANES] = total.astype(BF16)


def backward(
    conv_in, dt, ssm, grad, grad_gate, states, conv_weight, conv_bias, dt_bias, a_log, skip, gather
):
    length = conv_in.shape[0]
    chunks = length // CHUNK
    whole = lambda v: pl.BlockSpec(v.shape, lambda i: (0,) * v.ndim)
    by_row = lambda width: pl.BlockSpec((CHUNK, width), lambda i: (chunks - 1 - i, 0))
    return pl.pallas_call(
        backward_kernel,
        grid=(chunks,),
        out_shape=(
            shape((length, WIDE), BF16),
            shape((8, LANES), F32),
            shape((1, INNER), F32),
            shape((8 * (KCONV + 1), MIXW), F32),
        ),
        in_specs=[
            by_row(MIXW),
            pl.BlockSpec((8, MIXW), lambda i: (jnp.maximum((chunks - 1 - i) * (CHUNK // 8) - 1, 0), 0)),
            by_row(LANES),
            by_row(INNER),
            by_row(INNER),
            by_row(INNER),
            pl.BlockSpec((1, NSTATE, INNER), lambda i: (chunks - 1 - i, 0, 0)),
        ]
        + [whole(v) for v in (conv_weight, conv_bias, dt_bias, a_log, skip, gather)],
        out_specs=(
            by_row(WIDE),
            pl.BlockSpec((8, LANES), lambda i: (0, 0)),
            pl.BlockSpec((1, INNER), lambda i: (0, 0)),
            pl.BlockSpec((8 * (KCONV + 1), MIXW), lambda i: (0, 0)),
        ),
        scratch_shapes=[pltpu.VMEM((NSTATE, INNER), F32)]
        + [pltpu.VMEM((2 * CHUNK, INNER), F32)]
        + [pltpu.VMEM((CHUNK, MIXW), F32)] * 3
        + [pltpu.VMEM((8, MIXW), F32), pltpu.VMEM((MIXW // LANES, CHUNK + 8, LANES), F32)],
        compiler_params=params(),
        cost_estimate=cost(43),
    )(
        conv_in, conv_in, dt, ssm, grad, grad_gate, states,
        conv_weight, conv_bias, dt_bias, a_log, skip, gather,
    )


def moved_down(scratch, v, before):
    rows = v.shape[0]
    scratch[0:8, :] = before
    scratch[8 : 8 + rows, :] = v
    return [scratch[8 - by : 8 - by + rows, :] for by in range(KCONV - 1, 0, -1)]


def moved_up(scratch, v, behind):
    rows = v.shape[0]
    scratch[0:rows, :] = v
    scratch[rows : rows + 8, :] = behind
    return [scratch[by : by + rows, :] for by in range(KCONV - 1, 0, -1)]


def conv_sum(terms, weight, bias):
    total = bias + terms[KCONV - 1] * weight[KCONV - 1 : KCONV]
    for k in range(KCONV - 1):
        total = total + terms[k] * weight[k : k + 1]
    return total


def loss_kernel(
    limit, mixed_out, w_out, tokens, teacher, mask, block_out, grad_result, grad_branch, error
):
    step = pl.program_id(0)

    @pl.when(step == 0)
    def _():
        error[...] = jnp.zeros_like(error)

    rows = tokens.shape[0]
    result = tokens[...].astype(F32) + dot(mixed_out[...], w_out[...])
    position = step * rows + lax.broadcasted_iota(jnp.int32, (rows, 1), 0)
    valid = (position < limit[0]).astype(F32)
    turned = jnp.broadcast_to(mask[...].astype(F32), (LANES, rows)).T
    weight = valid * turned[:, 0:1]
    block_out[...] = (result * valid).astype(BF16)
    misfit = result - teacher[...].astype(F32)
    pulled = 2.0 * weight * misfit
    grad_result[...] = pulled
    errors = jnp.sum(0.5 * pulled * misfit, axis=0, keepdims=True)
    for j in range(D // LANES):
        error[j : j + 1, :] += errors[:, j * LANES : (j + 1) * LANES]
    error[D // LANES : D // LANES + 1, :] += jnp.sum(valid * turned, axis=0, keepdims=True)
    grad_branch[...] = pulled.astype(BF16)


def loss_part(limit, mixed_out, w_out, tokens, teacher, mask):
    length = tokens.shape[0]
    rows = 512
    by_row = lambda width: pl.BlockSpec((rows, width), lambda i: (i, 0))
    return pl.pallas_call(
        loss_kernel,
        grid=(length // rows,),
        out_shape=(
            shape((length, D), BF16),
            shape((length, D), F32),
            shape((length, D), BF16),
            shape((8, LANES), F32),
        ),
        in_specs=[
            SMEM,
            by_row(INNER),
            pl.BlockSpec(w_out.shape, lambda i: (0, 0)),
            by_row(D),
            by_row(D),
            pl.BlockSpec((1, rows), lambda i: (0, i)),
        ],
        out_specs=(by_row(D), by_row(D), by_row(D), pl.BlockSpec((8, LANES), lambda i: (0, 0))),
        compiler_params=params(),
        cost_estimate=cost(8),
    )(limit, mixed_out, w_out, tokens, teacher, mask)


def gate_kernel(grad_branch, w_out, ssm, gate, gain, grad_ssm, grad_gate, gain_sums):
    @pl.when(pl.program_id(0) == 0)
    def _():
        gain_sums[...] = jnp.zeros_like(gain_sums)

    grad_mixed = dot(grad_branch[...], w_out[...], NT)
    g = gate[...]
    sig = sigmoid(g)
    act = g * sig
    inner = ssm[...]
    gated = inner * act
    rho = lax.rsqrt(jnp.mean(gated * gated, axis=1, keepdims=True) + NORM_EPS)
    unit = gated * rho
    gain_sums[...] += jnp.sum(unit * grad_mixed, axis=0, keepdims=True)
    grad_unit = grad_mixed * gain[...]
    share = jnp.mean(grad_unit * unit, axis=1, keepdims=True)
    grad_gated = rho * (grad_unit - unit * share)
    grad_ssm[...] = grad_gated * act
    grad_gate[...] = (grad_gated * inner * (sig * (1.0 + g * (1.0 - sig)))).astype(BF16)


def gate_part(grad_branch, w_out, ssm, gate, gain):
    length = ssm.shape[0]
    rows = 256
    by_row = lambda width: pl.BlockSpec((rows, width), lambda i: (i, 0))
    whole = lambda v: pl.BlockSpec(v.shape, lambda i: (0,) * v.ndim)
    return pl.pallas_call(
        gate_kernel,
        grid=(length // rows,),
        out_shape=(shape((length, INNER), F32), shape((length, INNER), BF16), shape((1, INNER), F32)),
        in_specs=[by_row(D), whole(w_out), by_row(INNER), by_row(INNER), whole(gain)],
        out_specs=(by_row(INNER), by_row(INNER), pl.BlockSpec((1, INNER), lambda i: (0, 0))),
        compiler_params=params(),
        cost_estimate=cost(12),
    )(grad_branch, w_out, ssm, gate, gain)


def input_kernel(grad_low, w_in, tokens, norm_gain, grad_result, out, sums):
    @pl.when(pl.program_id(0) == 0)
    def _():
        sums[...] = jnp.zeros_like(sums)

    x = tokens[...].astype(F32)
    inverse = lax.rsqrt(jnp.mean(x * x, axis=1, keepdims=True) + NORM_EPS)
    unit = x * inverse
    grad_hidden = dot(grad_low[...], w_in[...], NT)
    sums[...] += jnp.sum(grad_hidden * unit, axis=0, keepdims=True)
    pulled = grad_hidden * norm_gain[...]
    share = jnp.mean(pulled * unit, axis=1, keepdims=True)
    out[...] = grad_result[...] + inverse * (pulled - unit * share)


def input_backward(grad_low, w_in, tokens, norm_gain, grad_result):
    length = tokens.shape[0]
    rows = 256
    by_row = lambda width: pl.BlockSpec((rows, width), lambda i: (i, 0))
    whole = lambda v: pl.BlockSpec(v.shape, lambda i: (0,) * v.ndim)
    return pl.pallas_call(
        input_kernel,
        grid=(length // rows,),
        out_shape=(shape((length, D), F32), shape((1, D), F32)),
        in_specs=[by_row(WIDE), whole(w_in), by_row(D), whole(norm_gain), by_row(D)],
        out_specs=(by_row(D), pl.BlockSpec((1, D), lambda i: (0, 0))),
        compiler_params=params(),
        cost_estimate=cost(15),
    )(grad_low, w_in, tokens, norm_gain, grad_result)


def vector_kernel(tail, conv_sums, sums, skip_sums, norm_sums, gate_sums, gather, out, taps):
    tiles = CONVCH // LANES
    out[...] = jnp.zeros_like(out)
    out[0:TAIL_ROWS, :] = tail[...]
    for k in range(KCONV):
        for i in range(tiles):
            partial_sums = conv_sums[8 * k : 8 * k + 8, i * LANES : (i + 1) * LANES]
            taps[k * 16 + i : k * 16 + i + 1, :] = jnp.sum(partial_sums, axis=0, keepdims=True)
    row = lax.broadcasted_iota(jnp.int32, (LANES, LANES), 0)
    col = lax.broadcasted_iota(jnp.int32, (LANES, LANES), 1)
    per_tile = LANES // KCONV

    def exact(v, chosen):
        high = v.astype(BF16)
        rest = v - high.astype(F32)
        middle = rest.astype(BF16)
        low = (rest - middle.astype(F32)).astype(BF16)
        return dot(high, chosen) + (dot(middle, chosen) + dot(low, chosen))

    for q in range(KCONV):
        total = jnp.zeros((tiles, LANES), F32)
        for k in range(KCONV):
            chosen = (col == KCONV * (row % per_tile) + k) & (row // per_tile == q)
            total = total + exact(taps[k * 16 : k * 16 + tiles, :], chosen.astype(BF16))
        out[pl.ds(TAIL_ROWS + q, tiles, stride=KCONV), :] = total
    bias_at = TAIL_ROWS + tiles * KCONV
    for i in range(tiles):
        partial_sums = conv_sums[8 * KCONV :, i * LANES : (i + 1) * LANES]
        out[bias_at + i : bias_at + i + 1, :] = jnp.sum(partial_sums, axis=0, keepdims=True)
    lane = lax.broadcasted_iota(jnp.int32, (1, LANES), 1)
    skip = exact(jnp.broadcast_to(skip_sums[...], (8, INNER)), gather[...])[0:1, :]
    parts = [sums[0:1, :], sums[1:2, :], skip]
    parts = [jnp.where(lane < HEADS, v, 0.0) for v in parts]
    before = parts[0] + pltpu.roll(parts[1], HEADS, 1) + pltpu.roll(parts[2], 2 * HEADS, 1)
    at, shift = bias_at + tiles, 3 * HEADS
    for source in (norm_sums, gate_sums):
        for j in range(source.shape[1] // LANES):
            here = pltpu.roll(source[:, j * LANES : (j + 1) * LANES], shift, 1)
            out[at : at + 1, :] = jnp.where(lane < shift, before, here)
            before = here
            at += 1
    out[at : at + 1, :] = jnp.where(lane < shift, before, 0.0)


def pack_vectors(tail, conv_sums, sums, skip_sums, norm_sums, gate_sums, gather):
    return pl.pallas_call(
        vector_kernel,
        out_shape=shape(((NBLK - MID1) * BROWS, LANES), F32),
        in_specs=[VMEM] * 7,
        out_specs=VMEM,
        scratch_shapes=[pltpu.VMEM((KCONV * 16, LANES), F32)],
        compiler_params=params(),
    )(tail, conv_sums, sums, skip_sums, norm_sums, gate_sums, gather)


def body(tokens, teacher, lengths, loss_mask, owners, master, first_moment, second_moment):
    capacity = master.shape[0]
    dp, fsdp = lax.axis_size("dp"), lax.axis_size("fsdp")
    devices = dp * fsdp
    me = lax.axis_index(AXES).astype(jnp.int32)
    x_first, y_first, z_first = step_orders(dp, fsdp)
    tie = lambda *values: lax.optimization_barrier(values)

    sent = send_blocks(owners, master, devices, me)
    at_home = lax.all_to_all(sent, AXES, 0, 0, tiled=True)
    owners, tokens, loss_mask, _ = tie(owners, tokens, loss_mask, sent)
    plan = make_plan(owners, capacity, devices, me)
    streams = cut(even(plan["slots"], 3), (x_first, y_first, z_first))
    table = stream_places(plan["home"], plan["slot"], me, streams, devices)
    u0, u1 = plan["unit_slots"]
    sizes = [3 * u0 // 16] * 4
    unit_streams = cut(sizes + [u0 - sum(sizes)], (x_first, y_first, x_first, y_first, z_first))
    order1 = x_first[:2] + x_first[2 + bits_of(fsdp) :] + x_first[2 : 2 + bits_of(fsdp)]
    unit_table, unit_table1 = [], []
    for u in range(UNITS):
        unit = UNITS * plan["order"] + u
        home, slot = unit % devices, unit // devices
        unit_table.append(stream_places(home, slot, me, unit_streams, devices)[:MID0])
        unit_table1.append((place_of(home ^ me, order1) * (u1 + 1) + slot)[MID0:MID1])
    unit_table, unit_table1 = quarters(unit_table), quarters(unit_table1)
    inputs, target = tokens[0], teacher[0]
    (at_home, table, unit_table, unit_table1, received, back_table, row_from, row_block,
     row_used) = tie(
        at_home, table, unit_table, unit_table1, plan["received"], plan["back"],
        plan["row_from"], plan["row_block"], plan["row_used"],
    )
    mine = pick_blocks(received, at_home, [size for _, size, _ in streams])
    parts = []
    for values, (_, _, order) in zip(mine, streams):
        parts += gather_steps(values, order)
    (input_weight, output_weight, conv_weight, conv_bias, dt_bias, a_log, skip, norm_gain,
     gate_gain, hidden, gate, conv_in, dt, ssm, mixed_out, states) = forward(
        table, inputs, parts
    )
    gather = heads_gather()
    block_out, grad_result, grad_branch, local = loss_part(
        lengths, mixed_out, output_weight, inputs, target, loss_mask
    )
    keep1, send1, head, tail = pack_out(
        unit_table1, mixed_out, grad_branch, local, devices, u1 + 1
    )
    grad_branch, send1 = tie(grad_branch, send1)
    got1 = exchange(send1, order1[0])
    grad_ssm, grad_gate, gain_sums = gate_part(grad_branch, output_weight, ssm, gate, gate_gain)
    grad_ssm, keep1, got1 = tie(grad_ssm, keep1, got1)
    keep1, got1 = reduce_step(keep1, got1, order1[1])
    grad_low, sums, skip_sums, conv_sums = backward(
        conv_in, dt, ssm, grad_ssm, grad_gate, states,
        conv_weight, conv_bias, dt_bias, a_log, skip, gather,
    )
    grad_low, keep1, got1 = tie(grad_low, keep1, got1)
    steps1 = order1[2:]
    for step in steps1[:1]:
        keep1, got1 = reduce_step(keep1, got1, step)
    halves = []
    for _, size, _ in unit_streams:
        halves += [devices * size // 2] * 2
    packed = list(pack_in(unit_table, hidden, grad_low, head, halves))
    packed[0], keep1, got1 = tie(packed[0], keep1, got1)
    kept = packed[::2]
    got = [exchange(v, order[0]) for v, (_, _, order) in zip(packed[1::2], unit_streams)]
    *got, grad_low, conv_sums, tail = tie(*got, grad_low, conv_sums, tail)
    for i, (_, _, order) in enumerate(unit_streams):
        kept[i], got[i] = reduce_step(kept[i], got[i], order[1])
    for step in steps1[1:2]:
        keep1, got1 = reduce_step(keep1, got1, step)
    input_grad, norm_sums = input_backward(grad_low, input_weight, inputs, norm_gain, grad_result)
    grad_vec = pack_vectors(tail, conv_sums, sums, skip_sums, norm_sums, gain_sums, gather)
    grad_vec = grad_vec.reshape((NBLK - MID1) * UNITS, UNIT, LANES)
    *got, got1, grad_vec, input_grad = tie(*got, got1, grad_vec, input_grad)
    for step in steps1[2:]:
        keep1, got1 = reduce_step(keep1, got1, step)
    for k in range(2, len(x_first)):
        for i, (_, _, order) in enumerate(unit_streams):
            if i == 0:
                kept[i], got[i], grad_vec = reduce_step(kept[i], got[i], order[k], grad_vec)
            else:
                kept[i], got[i] = reduce_step(kept[i], got[i], order[k])
    back = units_to_owners(back_table, list(zip(kept + [keep1], got + [got1])))
    back, grad_vec = tie(back, grad_vec)
    returned = lax.all_to_all(back, AXES, 0, 0, tiled=True)
    for step in x_first[:2]:
        grad_vec = grad_vec + exchange(grad_vec, step)
    local_sums = keep1[u1] + got1[u1]
    error_sum = jnp.sum(local_sums[: D // LANES])
    divisor = local_sums[D // LANES, 0] * D
    new_first, new_second, new_master = adam(
        row_from,
        row_block,
        row_used,
        divisor,
        returned,
        grad_vec,
        master,
        first_moment,
        second_moment,
    )
    mean_loss = error_sum / divisor
    return (block_out[None], input_grad[None], mean_loss, new_first, new_second, new_master)


def solution(mesh):
    return jax.shard_map(
        body,
        mesh=mesh,
        in_specs=(
            P(AXES, None, None),
            P(AXES, None, None),
            P(AXES),
            P(AXES, None),
            P(),
            P(AXES, None),
            P(AXES, None),
            P(AXES, None),
        ),
        out_specs=(
            P(AXES, None, None),
            P(AXES, None, None),
            P(),
            P(AXES, None),
            P(AXES, None),
            P(AXES, None),
        ),
        check_vma=False,
    )
```

```python
from functools import partial

import jax
import jax.numpy as jnp
import numpy as np
from jax import lax
from jax.experimental import pallas as pl
from jax.experimental.pallas import tpu as pltpu
from jax.sharding import PartitionSpec as P

D = 768
INNER = 1536
NSTATE = 128
HEADDIM = 64
KCONV = 4
SCAN_LEN = 256
PBLOCK = 4096
STEP = 10
HEADS = 24
CONVCH = 1792
PROJ = 3352
PTOT = 3765320
NBLK = 920

LANES = 128
BROWS = PBLOCK // LANES
UNIT = 8
UNITS = BROWS // UNIT
END_IN = D * PROJ
END_OUT = END_IN + INNER * D
MID0 = -(-END_IN // PBLOCK)
MID1 = END_OUT // PBLOCK
N0 = MID0 + NBLK - MID1
N1 = MID1 - MID0
F0_ROWS = N0 * BROWS
IN_ROWS = END_IN // LANES
HEAD_ROWS = MID0 * BROWS - IN_ROWS
TAIL_ROWS = (END_OUT - MID1 * PBLOCK) // LANES
OUT_ROWS = INNER * D // LANES
VEC_ROWS = (NBLK - MID1) * BROWS - TAIL_ROWS
VEC_AT = MID0 * BROWS + TAIL_ROWS
GROUP = 16
GROUPS = D // GROUP
GROUP_ROWS = GROUP * PROJ // LANES
COL_TILES = -(-PROJ // LANES)
WIDE = COL_TILES * LANES
OUT_TILES = D // LANES

NORM_EPS = 1e-05
ADAM_EPS = 1e-08
BETA_ONE = 0.9
BETA_TWO = 0.999
MATRIX_RATE = 0.03
VECTOR_RATE = 0.2
WEIGHT_DECAY = 0.1
PRECISE = lax.Precision.HIGHEST
AXES = ("dp", "fsdp")
VMEM_LIMIT = 60 * 1024 * 1024


def bits_of(count):
    return count.bit_length() - 1


def step_orders(dp, fsdp):
    wide = [("dp", i) for i in range(bits_of(dp))]
    narrow = [("fsdp", i) for i in range(bits_of(fsdp))]
    first = wide[:2] + narrow + wide[2:]
    second = wide[:1] + narrow + wide[1:]
    third = wide[:1] + wide[2:] + wide[1:2] + narrow
    return first, second, third


def cut(sizes, orders):
    streams, at = [], 0
    for size, order in zip(sizes, orders):
        if size:
            streams.append((at, size, order))
        at += size
    return streams


def even(total, parts):
    return [total // parts + (i < total % parts) for i in range(parts)]


def exchange(values, *steps):
    axes = {axis for axis, _ in steps}
    if len(axes) == 1:
        (axis,) = axes
        mask = sum(1 << bit for _, bit in steps)
        pairs = [(i, i ^ mask) for i in range(lax.axis_size(axis))]
        return lax.ppermute(values, axis, pairs)
    low = bits_of(lax.axis_size("fsdp"))
    mask = sum(1 << (bit + (low if axis == "dp" else 0)) for axis, bit in steps)
    count = lax.axis_size("dp") * lax.axis_size("fsdp")
    return lax.ppermute(values, AXES, [(i, i ^ mask) for i in range(count)])


def place_of(relative, order):
    shift_of = {"dp": bits_of(lax.axis_size("fsdp")), "fsdp": 0}
    place = jnp.zeros_like(relative)
    for axis, bit in order:
        place = place * 2 + ((relative >> (shift_of[axis] + bit)) & 1)
    return place


def class_counts(owners, devices):
    block = jnp.arange(NBLK, dtype=jnp.int32)
    mid = ((block >= MID0) & (block < MID1))[None, :]
    device = jnp.arange(devices, dtype=jnp.int32)
    below = owners[None, :] < device[:, None]
    owned = owners[None, :] == device[:, None]

    def total(mask):
        return jnp.sum(mask.astype(jnp.int32), axis=1)

    start = (total(below & ~mid), total(below & mid))
    count = (total(owned & ~mid), total(owned & mid))
    return start, count, total(owned & (block < MID0)[None, :])


def my_counts(owners, me):
    block = jnp.arange(NBLK, dtype=jnp.int32)
    mid = (block >= MID0) & (block < MID1)
    below, owned = owners < me, owners == me
    total = lambda mask: jnp.sum(mask.astype(jnp.int32))
    start = (total(below & ~mid), total(below & mid))
    count = (total(owned & ~mid), total(owned & mid))
    return start, count, total(owned & (block < MID0))


def pair_lanes(capacity, devices):
    return -(-capacity // devices)


def make_plan(owners, capacity, devices, me):
    block = jnp.arange(NBLK, dtype=jnp.int32)
    mid = (block >= MID0) & (block < MID1)
    same = mid[:, None] == mid[None, :]
    before = (owners[None, :] < owners[:, None]) | (
        (owners[None, :] == owners[:, None]) & (block[None, :] < block[:, None])
    )
    order = jnp.sum(before.astype(jnp.int32), axis=1)
    order_in_class = jnp.sum((same & before).astype(jnp.int32), axis=1)
    home, slot = order % devices, order // devices
    device = jnp.arange(devices, dtype=jnp.int32)
    start, count, _ = class_counts(owners, devices)
    my_start, my_count, my_early = my_counts(owners, me)
    pair = pair_lanes(capacity, devices)

    slots = -(-NBLK // devices)
    wanted = me + devices * jnp.arange(slots, dtype=jnp.int32)
    first = start[0] + start[1]
    ends = first + count[0] + count[1]
    owner = jnp.sum((ends[None, :] <= wanted[:, None]).astype(jnp.int32), axis=1)
    owner = jnp.minimum(owner, devices - 1)
    base = jnp.sum(jnp.where(device[None, :] == owner[:, None], first[None, :], 0), axis=1)
    received = owner * pair + jnp.clip((wanted - base) // devices, 0, pair - 1)

    back_pair = (UNITS * capacity + 2 * (devices - 1)) // devices
    unit_slots = (-(-UNITS * N0 // devices), -(-UNITS * N1 // devices))
    lane = jnp.arange(back_pair, dtype=jnp.int32)

    def units_back(kind):
        turn = lane if kind == 0 else back_pair - 1 - lane
        first = UNITS * start[kind][:, None]
        k = (me - first) % devices + turn[None, :] * devices
        return k < UNITS * count[kind][:, None], (first + k) // devices

    valid0, slot0 = units_back(0)
    valid1, slot1 = units_back(1)
    back = jnp.where(valid0, slot0, jnp.where(valid1, unit_slots[0] + slot1, 0)).reshape(-1)

    row = jnp.arange(capacity, dtype=jnp.int32)
    is_mid = (row >= my_early) & (row < my_early + my_count[1])
    k = jnp.where(is_mid, row - my_early, jnp.where(row < my_early, row, row - my_count[1]))
    first = UNITS * jnp.where(is_mid, my_start[1], my_start[0])
    row_used = row < my_count[0] + my_count[1]
    mine = (owners == me)[None, :]
    rank = jnp.sum((mine & (block[None, :] < block[:, None])).astype(jnp.int32), axis=1)
    row_block = jnp.sum(
        jnp.where(mine & (rank[None, :] == row[:, None]), block[None, :], 0), axis=1
    )
    row_from = []
    for u in range(UNITS):
        unit = UNITS * k + u
        turn = unit // devices
        at = ((first + unit) % devices) * back_pair + jnp.where(is_mid, back_pair - 1 - turn, turn)
        late = devices * back_pair + UNITS * (row_block - MID1) + u
        at = jnp.where(row_block >= MID1, late, at)
        row_from.append(jnp.where(row_used, at, 0))
    return dict(
        home=home, slot=slot, slots=slots,
        received=received, order=order_in_class,
        unit_slots=unit_slots, back=back, row_from=quarters(row_from),
        row_used=row_used, row_block=row_block,
    )


def quarters(tables):
    width = -(-tables[0].shape[0] // LANES) * LANES
    return jnp.concatenate([jnp.pad(t, (0, width - t.shape[0])) for t in tables])


def stream_places(home, slot, me, streams, devices):
    relative = home ^ me
    place = jnp.zeros_like(slot)
    for begin, size, order in streams:
        inside = (slot >= begin) & (slot < begin + size)
        at = devices * begin + place_of(relative, order) * size + slot - begin
        place = jnp.where(inside, at, place)
    return place


def cost(microseconds):
    return pl.CostEstimate(
        flops=int(microseconds * 1e9), bytes_accessed=int(microseconds * 3e6), transcendentals=0
    )


ANY = pl.BlockSpec(memory_space=pl.ANY)
VMEM = pl.BlockSpec(memory_space=pltpu.VMEM)
SMEM = pl.BlockSpec(memory_space=pltpu.SMEM)


def params(**extra):
    return pltpu.CompilerParams(vmem_limit_bytes=VMEM_LIMIT, **extra)


def shape(dims, dtype):
    return jax.ShapeDtypeStruct(dims, dtype)


def send_kernel(my_index, owners, master, out, flat, *, devices):
    capacity = master.shape[0]
    me = my_index[0]
    for j in range(BROWS):
        flat[pl.ds(j, capacity, stride=BROWS), :] = master[:, j * LANES : (j + 1) * LANES]
    held = owners[...]
    below, owned = held < me, held == me

    def total(mask):
        return jnp.sum(jnp.where(mask, 1.0, 0.0)).astype(jnp.int32)

    start, count = total(below), total(owned)
    pair = out.shape[0] // devices

    def step(home, carry):
        for s in range(pair):
            k = lax.rem(home - start + devices * NBLK, devices) + s * devices
            row = jnp.where(k < count, k, 0)
            rows = pl.ds(pl.multiple_of(row * BROWS, BROWS), BROWS)
            out[home * pair + s] = flat[rows, :].astype(out.dtype)
        return carry

    lax.fori_loop(0, devices, step, 0)


def send_blocks(owners, master, devices, me):
    rows = -(-NBLK // (8 * LANES)) * 8
    held = jnp.pad(owners, (0, rows * LANES - NBLK), constant_values=1 << 20).reshape(rows, LANES)
    count = devices * pair_lanes(master.shape[0], devices)
    return pl.pallas_call(
        partial(send_kernel, devices=devices),
        out_shape=shape((count, BROWS, LANES), jnp.bfloat16),
        in_specs=[SMEM, VMEM, VMEM],
        out_specs=VMEM,
        scratch_shapes=[pltpu.VMEM((master.shape[0] * BROWS, LANES), jnp.float32)],
        compiler_params=params(),
    )(me.reshape(1), held, master)


def pick_kernel(table, source, *outs):
    at = 0
    for out in outs:

        def step(i, carry, out=out, at=at):
            out[i] = source[table[at + i]]
            return carry

        lax.fori_loop(0, out.shape[0], step, 0)
        at += out.shape[0]


def pick_blocks(table, source, sizes):
    return pl.pallas_call(
        pick_kernel,
        out_shape=tuple(shape((n,) + source.shape[1:], source.dtype) for n in sizes),
        in_specs=[SMEM, VMEM],
        out_specs=(VMEM,) * len(sizes),
        compiler_params=params(),
    )(table, source)


def back_kernel(table, *refs, sizes):
    sources, (out, held) = refs[:-2], refs[-2:]
    at = i = 0
    for size in sizes:
        n = sources[i].shape[0]
        total = sources[i][...]
        for k in range(1, size):
            total = total + sources[i + k][0:n]
        held[at : at + n] = total
        at += n
        i += size

    def step(i, carry):
        for u in range(16):
            out[i * 16 + u] = held[table[i * 16 + u]]
        return carry

    total = out.shape[0]
    lax.fori_loop(0, total // 16, step, 0)


def units_to_owners(table, groups):
    return pl.pallas_call(
        partial(back_kernel, sizes=[len(g) for g in groups]),
        out_shape=shape((table.shape[0], UNIT, LANES), jnp.float32),
        in_specs=[SMEM] + [VMEM] * sum(len(g) for g in groups),
        out_specs=VMEM,
        scratch_shapes=[pltpu.VMEM((sum(g[0].shape[0] for g in groups), UNIT, LANES), jnp.float32)],
        compiler_params=params(),
    )(table, *[v for g in groups for v in g])


def row_start(rho):
    return (PROJ * rho) // LANES, (PROJ * rho) % LANES


def copy_all(pairs, sem):
    copies = [pltpu.make_async_copy(a, b, sem.at[i]) for i, (a, b) in enumerate(pairs)]
    for c in copies:
        c.start()
    for c in copies:
        c.wait()


def spread_blocks(table, first, held, flat, count, first_row):
    def one(i):
        at = pl.multiple_of(first_row + i * BROWS, 16)
        flat[pl.ds(at, BROWS), :] = held[table[first + i]].astype(jnp.float32)

    def step(i, carry):
        for u in range(16):
            one(i * 16 + u)
        return carry

    lax.fori_loop(0, count // 16, step, 0)
    for i in range(count // 16 * 16, count):
        one(i)


def unpack_vectors(flat, conv_weight, conv_bias, dt_bias, a_log, skip, norm_gain, gate_gain):
    bf16, f32 = jnp.bfloat16, jnp.float32
    tiles = CONVCH // LANES
    row = lax.broadcasted_iota(jnp.int32, (LANES, LANES), 0)
    col = lax.broadcasted_iota(jnp.int32, (LANES, LANES), 1)
    per_tile = LANES // KCONV
    for k in range(KCONV):
        total = jnp.zeros((tiles, LANES), f32)
        for q in range(KCONV):
            rows = flat[pl.ds(VEC_AT + q, tiles, stride=KCONV), :].astype(bf16)
            chosen = (row == KCONV * (col % per_tile) + k) & (col // per_tile == q)
            total = total + jnp.dot(rows, chosen.astype(bf16), preferred_element_type=f32)
        for i in range(tiles):
            conv_weight[k : k + 1, i * LANES : (i + 1) * LANES] = total[i : i + 1, :]
    bias_at = VEC_AT + tiles * KCONV
    for i in range(tiles):
        conv_bias[:, i * LANES : (i + 1) * LANES] = flat[bias_at + i : bias_at + i + 1, :]
    at = bias_at + tiles
    lane = lax.broadcasted_iota(jnp.int32, (8, LANES), 1)
    first = flat[at : at + 8, :]
    three = []
    for i in range(3):
        moved = pltpu.roll(first, LANES - i * HEADS, 1) if i else first
        three.append(jnp.where(lane < HEADS, moved, 0.0))
    dt_bias[...] = three[0][0:1, :]
    a_log[...] = three[1][0:1, :]
    for j in range(INNER // LANES):
        h = lax.broadcasted_iota(jnp.int32, (LANES, LANES), 0)
        c = lax.broadcasted_iota(jnp.int32, (LANES, LANES), 1) + j * LANES
        spread = (h == c // HEADDIM).astype(bf16)
        wide = jnp.dot(three[2].astype(bf16), spread, preferred_element_type=f32)
        skip[:, j * LANES : (j + 1) * LANES] = wide[0:1, :]
    shift = 3 * HEADS
    for out, begin, width in ((norm_gain, at, D), (gate_gain, at + D // LANES, INNER)):
        for j in range(width // LANES):
            x = pltpu.roll(flat[begin + j : begin + j + 1, :], LANES - shift, 1)
            y = pltpu.roll(flat[begin + j + 1 : begin + j + 2, :], LANES - shift, 1)
            out[:, j * LANES : (j + 1) * LANES] = jnp.where(lane[0:1] < LANES - shift, x, y)


def unpack_weights(table, parts, w_in, w_out, vectors, held, flat, flat_out, tile, sem):
    pairs, at = [], 0
    for part in parts:
        pairs.append((part, held.at[pl.ds(at, part.shape[0])]))
        at += part.shape[0]
    copy_all(pairs, sem)
    spread_blocks(table, 0, held, flat, MID0, 0)
    spread_blocks(table, MID1, held, flat, NBLK - MID1, MID0 * BROWS)
    spread_blocks(table, MID0, held, flat_out, N1, HEAD_ROWS)
    flat_out[0:HEAD_ROWS, :] = flat[IN_ROWS : IN_ROWS + HEAD_ROWS, :]
    flat_out[OUT_ROWS - TAIL_ROWS :, :] = flat[MID0 * BROWS : MID0 * BROWS + TAIL_ROWS, :]
    unpack_vectors(flat, *vectors)
    rows = 128

    def out_step(i, carry):
        at = pl.multiple_of(i * rows, rows)
        for j in range(OUT_TILES):
            x = flat_out[pl.ds(at * OUT_TILES + j, rows, stride=OUT_TILES), :]
            w_out[pl.ds(at, rows), j * LANES : (j + 1) * LANES] = x.astype(jnp.bfloat16)
        return carry

    lax.fori_loop(0, INNER // rows, out_step, 0)
    lane = lax.broadcasted_iota(jnp.int32, (GROUPS, LANES), 1)

    def columns(j):
        for rho in range(GROUP):
            c, s = row_start(rho)
            x = flat[pl.ds(c + j, GROUPS, stride=GROUP_ROWS), :]
            if s:
                y = flat[pl.ds(c + j + 1, GROUPS, stride=GROUP_ROWS), :]
                x = jnp.where(
                    lane < LANES - s,
                    pltpu.roll(x, LANES - s, 1),
                    pltpu.roll(y, LANES - s, 1),
                )
            tile[pl.ds(rho, GROUPS, stride=GROUP), :] = x

    def step(j, carry):
        columns(j)
        w_in[:, pl.ds(pl.multiple_of(j * LANES, LANES), LANES)] = tile[...].astype(jnp.bfloat16)
        return carry

    lax.fori_loop(0, COL_TILES - 1, step, 0)
    columns(COL_TILES - 1)
    last = (COL_TILES - 1) * LANES
    inside = lax.broadcasted_iota(jnp.int32, (D, LANES), 1) < PROJ - last
    w_in[:, last:] = jnp.where(inside, tile[...], 0.0).astype(jnp.bfloat16)


def unpack_scratch(held, count):
    return [
        pltpu.VMEM((held, BROWS, LANES), jnp.bfloat16),
        pltpu.VMEM((F0_ROWS, LANES), jnp.float32),
        pltpu.VMEM((OUT_ROWS, LANES), jnp.float32),
        pltpu.VMEM((D, LANES), jnp.float32),
        pltpu.SemaphoreType.DMA((count,)),
    ]


def permute_units(table, flat, count, first_row, staged):
    many = 16
    width = table.shape[0] // UNITS

    def one(i):
        for u in range(UNITS):
            at = first_row + i * BROWS + u * UNIT
            at = at if isinstance(at, int) else pl.multiple_of(at, UNIT)
            staged[table[u * width + i]] = flat[pl.ds(at, UNIT), :]

    def step(i, carry):
        for b in range(many):
            one(i * many + b)
        return carry

    lax.fori_loop(0, count // many, step, 0)
    for i in range(count // many * many, count):
        one(i)


def pack_in_kernel(table, hidden, grad, head, *refs):
    outs, (turned, tiles, flat, staged, sem) = refs[:-5], refs[-5:]
    turned[...] = hidden[...].T
    lane = lax.broadcasted_iota(jnp.int32, (GROUPS, LANES), 1)

    def product(p, count):
        at = p * 2 * LANES
        at = at if isinstance(at, int) else pl.multiple_of(at, 2 * LANES)
        return jnp.dot(
            turned[...], grad[:, pl.ds(at, count * LANES)], preferred_element_type=jnp.float32
        )

    def put(p, value):
        for k in range(value.shape[1] // LANES):
            at = (p * 2 + k) * D
            at = at if isinstance(at, int) else pl.multiple_of(at, D)
            tiles[pl.ds(at, D), :] = value[:, k * LANES : (k + 1) * LANES]

    def load(rho, j):
        return tiles[pl.ds(j * D + rho, GROUPS, stride=GROUP), :]

    def whole(rho, i):
        first = -(-PROJ * rho // LANES)
        col0 = first * LANES - PROJ * rho
        x = load(rho, i)
        if col0:
            x = jnp.where(
                lane < LANES - col0,
                pltpu.roll(x, LANES - col0, 1),
                pltpu.roll(load(rho, i + 1), LANES - col0, 1),
            )
        flat[pl.ds(first + i, GROUPS, stride=GROUP_ROWS), :] = x

    put(0, product(0, 2))
    put(1, product(1, 2))
    pairs = COL_TILES // 2

    def step(p, carry):
        for i in range(2):
            for rho in range(GROUP):
                whole(rho, p * 2 + i)
        put(p + 2, product(p + 2, 2))
        return carry

    lax.fori_loop(0, pairs - 2, step, 0)
    put(pairs, product(pairs, COL_TILES % 2))
    for rho in range(GROUP):
        first = -(-PROJ * rho // LANES)
        col0 = first * LANES - PROJ * rho
        full = (PROJ - col0) // LANES
        for i in range((pairs - 2) * 2, full):
            whole(rho, i)
        left = PROJ - col0 - full * LANES
        if left:
            begin = col0 + full * LANES
            j, s = begin // LANES, begin % LANES
            x = pltpu.roll(load(rho, j), LANES - s, 1) if s else load(rho, j)
            if s + left > LANES:
                x = jnp.where(lane < LANES - s, x, pltpu.roll(load(rho, j + 1), LANES - s, 1))
            y = pltpu.roll(load(rho + 1, 0), left, 1)
            flat[pl.ds(first + full, GROUPS, stride=GROUP_ROWS), :] = jnp.where(lane < left, x, y)
    flat[IN_ROWS : IN_ROWS + HEAD_ROWS, :] = head[...]
    permute_units(table, flat, MID0, 0, staged)
    copies, at = [], 0
    for out in outs:
        copies.append((staged.at[pl.ds(at, out.shape[0])], out))
        at += out.shape[0]
    copy_all(copies, sem)


def pack_in(table, hidden, grad, head, sizes):
    return pl.pallas_call(
        pack_in_kernel,
        out_shape=tuple(shape((n, UNIT, LANES), jnp.float32) for n in sizes),
        in_specs=[SMEM, VMEM, VMEM, VMEM],
        out_specs=(ANY,) * len(sizes),
        scratch_shapes=[
            pltpu.VMEM((D, hidden.shape[0]), jnp.bfloat16),
            pltpu.VMEM((COL_TILES * D, LANES), jnp.float32),
            pltpu.VMEM((MID0 * BROWS, LANES), jnp.float32),
            pltpu.VMEM((sum(sizes), UNIT, LANES), jnp.float32),
            pltpu.SemaphoreType.DMA((len(sizes),)),
        ],
        compiler_params=params(),
        cost_estimate=cost(20),
    )(table, hidden, grad, head)


def pack_out_kernel(
    table, mixed_out, grad, local, keep, send, head, tail, turned, flat, out, sem, *, slots
):
    rows = 512

    def step(i, carry):
        at = pl.multiple_of(i * rows, rows)
        turned[...] = mixed_out[:, pl.ds(at, rows)].T
        product = jnp.dot(turned[...], grad[...], preferred_element_type=jnp.float32)
        for j in range(OUT_TILES):
            flat[pl.ds(at * OUT_TILES + j, rows, stride=OUT_TILES), :] = product[
                :, j * LANES : (j + 1) * LANES
            ]
        return carry

    lax.fori_loop(0, INNER // rows, step, 0)
    head[...] = flat[0:HEAD_ROWS, :]
    tail[...] = flat[OUT_ROWS - TAIL_ROWS : OUT_ROWS, :]
    permute_units(table, flat, N1, HEAD_ROWS, out)

    def add_local(i, carry):
        out[i * slots + slots - 1] = local[...]
        return carry

    lax.fori_loop(0, out.shape[0] // slots, add_local, 0)
    half = keep.shape[0]
    copy_all([(out.at[pl.ds(0, half)], keep), (out.at[pl.ds(half, half)], send)], sem)


def pack_out(table, mixed_out, grad, local, devices, slots):
    return pl.pallas_call(
        partial(pack_out_kernel, slots=slots),
        out_shape=(
            shape((devices * slots // 2, UNIT, LANES), jnp.float32),
            shape((devices * slots // 2, UNIT, LANES), jnp.float32),
            shape((HEAD_ROWS, LANES), jnp.float32),
            shape((TAIL_ROWS, LANES), jnp.float32),
        ),
        in_specs=[SMEM, VMEM, VMEM, VMEM],
        out_specs=(ANY, ANY, VMEM, VMEM),
        scratch_shapes=[
            pltpu.VMEM((512, mixed_out.shape[0]), jnp.bfloat16),
            pltpu.VMEM((OUT_ROWS, LANES), jnp.float32),
            pltpu.VMEM((devices * slots, UNIT, LANES), jnp.float32),
            pltpu.SemaphoreType.DMA((2,)),
        ],
        compiler_params=params(),
    )(table, mixed_out, grad, local)


def adam_kernel(
    table, row_block, row_used, scale, got, late, master, first, second,
    o_first, o_second, o_master, flat, held, limit, used,
):
    capacity = master.shape[0]

    def step(i, carry):
        for u in range(UNITS):
            at = table[u * (table.shape[0] // UNITS) + i]
            rows = pl.ds(pl.multiple_of(i * BROWS + u * UNIT, UNIT), UNIT)
            flat[rows, :] = held[at]
        limit[pl.ds(i, 1), :] = jnp.full((1, LANES), END_OUT - row_block[i] * PBLOCK, jnp.int32)
        used[pl.ds(i, 1), :] = jnp.full((1, LANES), row_used[i], jnp.int32)
        return carry

    held[0 : got.shape[0]] = got[...]
    held[got.shape[0] :] = late[...]
    lax.fori_loop(0, capacity, step, 0)
    lane = lax.broadcasted_iota(jnp.int32, (capacity, LANES), 1)
    divisor = scale[0]
    for j in range(BROWS):
        cols = slice(j * LANES, (j + 1) * LANES)
        grad = jnp.where(used[...] > 0, flat[pl.ds(j, capacity, stride=BROWS), :], 0.0) / divisor
        matrix = lane + j * LANES < limit[...]
        weights = master[:, cols]
        new_first = BETA_ONE * first[:, cols] + (1.0 - BETA_ONE) * grad
        new_second = BETA_TWO * second[:, cols] + (1.0 - BETA_TWO) * grad * grad
        normal = (
            new_first
            / (1.0 - BETA_ONE**STEP)
            / (jnp.sqrt(new_second / (1.0 - BETA_TWO**STEP)) + ADAM_EPS)
        )
        rate = jnp.where(matrix, MATRIX_RATE, VECTOR_RATE)
        decay = jnp.where(matrix, WEIGHT_DECAY, 0.0)
        o_first[:, cols] = new_first
        o_second[:, cols] = new_second
        o_master[:, cols] = weights - rate * (normal + decay * weights)


def adam(table, row_block, row_used, divisor, got, late, master, first, second):
    capacity = master.shape[0]
    return pl.pallas_call(
        adam_kernel,
        out_shape=(shape(master.shape, jnp.float32),) * 3,
        in_specs=[SMEM] * 4 + [VMEM] * 5,
        out_specs=(VMEM,) * 3,
        scratch_shapes=[
            pltpu.VMEM((capacity * BROWS, LANES), jnp.float32),
            pltpu.VMEM((got.shape[0] + late.shape[0], UNIT, LANES), jnp.float32),
            pltpu.VMEM((capacity, LANES), jnp.int32),
            pltpu.VMEM((capacity, LANES), jnp.int32),
        ],
        compiler_params=params(),
    )(
        table, row_block, row_used.astype(jnp.int32), divisor.reshape(1), got, late, master, first, second
    )


def doubled(values, step):
    return jnp.concatenate([values, exchange(values, step)], axis=0)


def gather_steps(values, order):
    for step in order[:0:-1]:
        values = doubled(values, step)
    return values, exchange(values, order[0])


def reduce_step(kept, got, step, extra=None):
    half = kept.shape[0] // 2
    given = kept[half:] + got[half:]
    if extra is None:
        return kept[:half] + got[:half], exchange(given, step)
    arrived = exchange(jnp.concatenate([given, extra]), step)
    return kept[:half] + got[:half], arrived[:half], extra + arrived[half:]


CHUNK = 128
PAIRS = HEADS // 2
MIXW = INNER + 2 * NSTATE
DT_AT = INNER + CONVCH
F32 = jnp.float32
BF16 = jnp.bfloat16
NN = (((1,), (0,)), ((), ()))
NT = (((1,), (1,)), ((), ()))


def dot(a, b, dims=NN):
    return lax.dot_general(a, b, dims, preferred_element_type=F32)


def split(v):
    high = v.astype(BF16)
    return high, (v - high.astype(F32)).astype(BF16)


def dot3(a, b, dims=NN):
    ah, al = a
    bh, bl = b
    return dot(ah, bh, dims) + (dot(ah, bl, dims) + dot(al, bh, dims))


def heads_gather():
    return jnp.asarray(np.repeat(np.eye(HEADS, LANES, dtype=np.float32), HEADDIM, axis=0), BF16)


def three_parts(v):
    high = v.astype(BF16).astype(F32)
    rest = v - high
    middle = rest.astype(BF16).astype(F32)
    low = rest - middle
    return (high + pltpu.roll(middle, 32, 1) + pltpu.roll(low, 64, 1)).astype(BF16)


def triangle_sum(tri, v):
    parts = dot(tri, three_parts(v))
    lane = lax.broadcasted_iota(jnp.int32, parts.shape, 1)
    total = parts + pltpu.roll(parts, LANES - 32, 1) + pltpu.roll(parts, LANES - 64, 1)
    return jnp.where(lane < HEADS, total, 0.0)


def chunk_decays(dt, dt_bias, a_log):
    lane = lax.broadcasted_iota(jnp.int32, (CHUNK, LANES), 1)
    row = lax.broadcasted_iota(jnp.int32, (CHUNK, LANES), 0)
    shifted = dt + dt_bias
    delta = jnp.where(
        lane < HEADS, jnp.maximum(shifted, 0.0) + jnp.log1p(jnp.exp(-jnp.abs(shifted))), 0.0
    )
    rate = -jnp.exp(a_log)
    lower = (row >= lane).astype(BF16)
    cum = triangle_sum(lower, delta * rate)
    last = cum[CHUNK - 1 : CHUNK, :]
    return shifted, delta, rate, cum, last


def pair_mask():
    lane = lax.broadcasted_iota(jnp.int32, (CHUNK, LANES), 1)
    low = (lane < HEADDIM).astype(F32)
    return low.astype(BF16), (1.0 - low).astype(BF16)


QUADS = HEADS // 4
QWIDTH = 4 * HEADDIM


def sigmoid(v):
    return 0.5 * jnp.tanh(0.5 * v) + 0.5


def silu(v):
    return v * sigmoid(v)


def side_by_side(v):
    high, low = split(v)
    return jnp.concatenate([high, low], axis=1), high


def dot_parts(a, b):
    ahl, ah = a
    bh, bl = b
    return dot(ahl, jnp.concatenate([bh, bh], axis=0)) + dot(ah, bl)


def dot_turned(a, b):
    ah, al = a
    bh, bl = b
    both = dot(ah, jnp.concatenate([bh, bl], axis=0), NT)
    n = bh.shape[0]
    return both[:, :n] + both[:, n:] + dot(al, bh, NT)


def widen(delta, cum, quad):
    lane = lax.broadcasted_iota(jnp.int32, (CHUNK, LANES), 1)
    over = lambda v, h: jnp.broadcast_to(v[:, h : h + 1], (CHUNK, LANES))
    first = 4 * quad
    columns = [over(cum, first + k) for k in range(4)]
    rates = [over(delta, first + k) for k in range(4)]
    pair = lambda vs: jnp.concatenate(
        [jnp.where(lane < HEADDIM, vs[0], vs[1]), jnp.where(lane < HEADDIM, vs[2], vs[3])], axis=1
    )
    return pair(rates), pair(columns), columns


def pair_rows(parts, j, low, high):
    cols = slice(j * LANES, (j + 1) * LANES)
    return [jnp.concatenate([p[:, cols] * low, p[:, cols] * high], axis=0) for p in parts]


def scan_chunk(mixed, dt, dt_bias, a_log, skip, state, put):
    _, delta, _, cum, last = chunk_decays(dt, dt_bias, a_log)
    lane = lax.broadcasted_iota(jnp.int32, (CHUNK, LANES), 1)
    row = lax.broadcasted_iota(jnp.int32, (CHUNK, LANES), 0)
    bias = jnp.where(row >= lane, 0.0, -1e30)
    cum_t = cum.T
    inputs_b = mixed[:, INNER : INNER + NSTATE]
    readout = mixed[:, INNER + NSTATE :]
    affinity = dot3(split(readout), split(inputs_b), NT)
    readout_parts = side_by_side(readout)
    b_parts = side_by_side(inputs_b.T)
    low, high = pair_mask()
    for quad in range(QUADS):
        cols = slice(quad * QWIDTH, (quad + 1) * QWIDTH)
        wide_delta, wide_cum, columns = widen(delta, cum, quad)
        values = mixed[:, cols]
        scaled = values * wide_delta
        parts = split(scaled)
        outs = []
        for j in range(2):
            right_h, right_l = pair_rows(parts, j, low, high)
            left = []
            for k in range(2):
                h = 4 * quad + 2 * j + k
                within = jnp.exp(columns[2 * j + k] - cum_t[h : h + 1, :] + bias)
                left.append(split(affinity * within))
            left_h = jnp.concatenate([left[0][0], left[1][0]], axis=1)
            left_l = jnp.concatenate([left[0][1], left[1][1]], axis=1)
            both = dot(left_h, jnp.concatenate([right_h, right_l], axis=1))
            outs.append(both[:, :LANES] + both[:, LANES:] + dot(left_l, right_h))
        carried = state[:, cols]
        grown = jnp.exp(wide_cum)
        out = jnp.concatenate(outs, axis=1) + dot_parts(readout_parts, split(carried)) * grown
        tail = jnp.exp(wide_cum[CHUNK - 1 :] - wide_cum)
        state[:, cols] = carried * grown[CHUNK - 1 :] + dot_parts(b_parts, split(scaled * tail))
        put(quad, out + skip[:, cols] * values)


FORWARD_ROWS = 2 * CHUNK


def forward_kernel(table, tokens, *refs, count):
    parts, refs = refs[:count], refs[count:]
    (w_in_kept, w_out_kept, conv_weight, conv_bias, dt_bias, a_log, skip, norm_gain, gain,
     hidden, gate, conv_in, dt, ssm, mixed_out, states) = refs[:16]
    w_in, w_out, state, before, mixed, shift, out_sem, *scratch = refs[16:]
    keep = [
        pltpu.make_async_copy(w_in, w_in_kept, out_sem.at[0]),
        pltpu.make_async_copy(w_out, w_out_kept, out_sem.at[1]),
    ]

    @pl.when(pl.program_id(0) == 0)
    def _():
        vectors = (conv_weight, conv_bias, dt_bias, a_log, skip, norm_gain, gain)
        unpack_weights(table, parts, w_in, w_out, vectors, *scratch)
        for copy in keep:
            copy.start()
        state[...] = jnp.zeros_like(state)
        before[...] = jnp.zeros_like(before)

    x = tokens[...].astype(F32)
    inverse = lax.rsqrt(jnp.mean(x * x, axis=1, keepdims=True) + NORM_EPS)
    h = (x * inverse * norm_gain[...]).astype(BF16)
    hidden[...] = h
    dt[...] = dot(h, w_in[:, DT_AT:])
    wide = 2 * LANES
    for tile in range(CONVCH // wide):
        at = tile * wide
        product = dot(h, w_in[:, INNER + at : INNER + at + wide])
        conv_in[:, at : at + wide] = product
        for half in range(2):
            cols = slice(at + half * LANES, at + (half + 1) * LANES)
            rows = product[:, half * LANES : (half + 1) * LANES]
            earlier = before[:, cols]
            terms = moved_down(shift.at[tile * 2 + half], rows, earlier) + [rows]
            before[:, cols] = rows[FORWARD_ROWS - 8 :]
            mixed[:, cols] = silu(conv_sum(terms, conv_weight[:, cols], conv_bias[:, cols]))
    for tile in range(INNER // wide):
        cols = slice(tile * wide, (tile + 1) * wide)
        gate[:, cols] = dot(h, w_in[:, cols])
    for sub in range(FORWARD_ROWS // CHUNK):
        rows = slice(sub * CHUNK, (sub + 1) * CHUNK)
        states[sub] = state[...]
        squares = [jnp.zeros((CHUNK, LANES), F32)]

        def put(quad, out, rows=rows, squares=squares):
            cols = slice(quad * QWIDTH, (quad + 1) * QWIDTH)
            ssm[rows, cols] = out
            gated = out * silu(gate[rows, cols])
            first, second = gated[:, :LANES], gated[:, LANES:]
            squares[0] = squares[0] + first * first + second * second

        scan_chunk(
            mixed[rows, :], dt[rows, :], dt_bias[...], a_log[...], skip, state, put
        )
        rho = lax.rsqrt(jnp.sum(squares[0], axis=1, keepdims=True) * (1.0 / INNER) + NORM_EPS)
        for j in range(PAIRS):
            cols = slice(j * LANES, (j + 1) * LANES)
            gated = ssm[rows, cols] * silu(gate[rows, cols])
            mixed_out[rows, cols] = (gated * rho * gain[:, cols]).astype(BF16)

    @pl.when(pl.program_id(0) == pl.num_programs(0) - 1)
    def _():
        for copy in keep:
            copy.wait()


def forward(table, tokens, parts):
    length = tokens.shape[0]
    by_row = lambda width: pl.BlockSpec((FORWARD_ROWS, width), lambda i: (i, 0))
    per_step = FORWARD_ROWS // CHUNK
    vectors = [(KCONV, CONVCH), (1, CONVCH), (1, LANES), (1, LANES), (1, INNER), (1, D), (1, INNER)]
    return pl.pallas_call(
        partial(forward_kernel, count=len(parts)),
        grid=(length // FORWARD_ROWS,),
        out_shape=[shape((D, WIDE), BF16), shape((INNER, D), BF16)]
        + [shape(v, F32) for v in vectors]
        + [
            shape((length, D), BF16),
            shape((length, INNER), F32),
            shape((length, MIXW), F32),
            shape((length, LANES), F32),
            shape((length, INNER), F32),
            shape((length, INNER), BF16),
            shape((length // CHUNK, NSTATE, INNER), F32),
        ],
        in_specs=[SMEM, by_row(D)] + [ANY] * len(parts),
        out_specs=[ANY, ANY]
        + [pl.BlockSpec(v, lambda i: (0, 0)) for v in vectors]
        + [
            by_row(D),
            by_row(INNER),
            by_row(MIXW),
            by_row(LANES),
            by_row(INNER),
            by_row(INNER),
            pl.BlockSpec((per_step, NSTATE, INNER), lambda i: (i, 0, 0)),
        ],
        scratch_shapes=[
            pltpu.VMEM((D, WIDE), BF16),
            pltpu.VMEM((INNER, D), BF16),
            pltpu.VMEM((NSTATE, INNER), F32),
            pltpu.VMEM((8, MIXW), F32),
            pltpu.VMEM((FORWARD_ROWS, MIXW), F32),
            pltpu.VMEM((MIXW // LANES, FORWARD_ROWS + 8, LANES), F32),
            pltpu.SemaphoreType.DMA((2,)),
        ]
        + unpack_scratch(sum(part.shape[0] for part in parts), len(parts)),
        compiler_params=params(),
        cost_estimate=cost(50),
    )(table, tokens, *parts)


def eights(v):
    return jnp.sum(v.reshape(v.shape[0] // 8, 8, v.shape[1]), axis=0)


def backward_kernel(
    conv_in, earlier, dt, ssm, grad, grad_gate, states, conv_weight, conv_bias, dt_bias, a_log, skip,
    gather, grad_low, sums, skip_sums, conv_sums,
    grad_state, to_sum, mixed, slope, grad_mixed, following, shift,
):
    @pl.when(pl.program_id(0) == 0)
    def _():
        grad_state[...] = jnp.zeros_like(grad_state)
        sums[...] = jnp.zeros_like(sums)
        skip_sums[...] = jnp.zeros_like(skip_sums)
        conv_sums[...] = jnp.zeros_like(conv_sums)
        following[...] = jnp.zeros_like(following)

    begins = pl.program_id(0) == pl.num_programs(0) - 1

    for tile in range(MIXW // LANES):
        cols = slice(tile * LANES, (tile + 1) * LANES)
        rows = conv_in[:, cols]
        before = jnp.where(begins, 0.0, earlier[:, cols])
        terms = moved_down(shift.at[tile], rows, before) + [rows]
        value = conv_sum(terms, conv_weight[:, cols], conv_bias[:, cols])
        sig = sigmoid(value)
        mixed[:, cols] = value * sig
        slope[:, cols] = sig * (1.0 + value * (1.0 - sig))

    shifted, delta, rate, cum, last = chunk_decays(dt[...], dt_bias[...], a_log[...])
    lane = lax.broadcasted_iota(jnp.int32, (CHUNK, LANES), 1)
    row = lax.broadcasted_iota(jnp.int32, (CHUNK, LANES), 0)
    bias = jnp.where(lane >= row, 0.0, -1e30)
    heads = lane < HEADS
    cum_t = cum.T
    inputs_b = mixed[:, INNER : INNER + NSTATE]
    readout = mixed[:, INNER + NSTATE :]
    b_parts, c_parts = split(inputs_b), split(readout)
    b_wide = side_by_side(inputs_b)
    c_turned = side_by_side(readout.T)
    affinity = dot3(b_parts, c_parts, NT)
    low, high = pair_mask()
    grad_affinity = jnp.zeros((CHUNK, CHUNK), F32)
    grad_b = jnp.zeros((CHUNK, NSTATE), F32)
    grad_c = jnp.zeros((CHUNK, NSTATE), F32)
    last_row = lax.broadcasted_iota(jnp.int32, (CHUNK, QWIDTH), 0) == CHUNK - 1
    for quad in range(QUADS):
        cols = slice(quad * QWIDTH, (quad + 1) * QWIDTH)
        wide_delta, wide_cum, columns = widen(delta, cum, quad)
        grown = jnp.exp(wide_cum)
        tail = jnp.exp(wide_cum[CHUNK - 1 :] - wide_cum)
        end = grown[CHUNK - 1 :]
        values = mixed[:, cols]
        pulled = grad[:, cols]
        scaled = values * wide_delta
        x_parts, p_parts = split(scaled), split(pulled)
        outs = []
        for j in range(2):
            half = slice(j * LANES, (j + 1) * LANES)
            xh, xl = x_parts[0][:, half], x_parts[1][:, half]
            right_h, right_l = pair_rows(p_parts, j, low, high)
            pull = dot(
                jnp.concatenate([xh, xl], axis=1),
                jnp.concatenate([right_h, right_h], axis=1),
                NT,
            ) + dot(xh, right_l, NT)
            kernels = []
            for k in range(2):
                h = 4 * quad + 2 * j + k
                within = jnp.exp(cum_t[h : h + 1, :] - columns[2 * j + k] + bias)
                kernels.append(split(affinity * within))
                grad_affinity = grad_affinity + within * pull[:, k * CHUNK : (k + 1) * CHUNK]
            kernel_h = jnp.concatenate([kernels[0][0], kernels[1][0]], axis=1)
            kernel_l = jnp.concatenate([kernels[0][1], kernels[1][1]], axis=1)
            both = dot(kernel_h, jnp.concatenate([right_h, right_l], axis=1))
            outs.append(both[:, :LANES] + both[:, LANES:] + dot(kernel_l, right_h))
        late = grad_state[:, cols]
        late_parts = split(late)
        early = states[0, :, cols]
        from_state = dot_parts(b_wide, late_parts) * tail
        grad_scaled = jnp.concatenate(outs, axis=1) + from_state
        pulled_cum = split(pulled * grown)
        grad_c = grad_c + dot_turned(pulled_cum, split(early))
        grad_b = grad_b + dot_turned(split(scaled * tail), late_parts)
        grad_state[:, cols] = late * end + dot_parts(c_turned, pulled_cum)
        grad_mixed[:, cols] = grad_scaled * wide_delta + skip[:, cols] * pulled
        skip_sums[:, cols] += jnp.sum(pulled * values, axis=0, keepdims=True)
        to_sum[:CHUNK, cols] = grad_scaled * values
        inner = pulled * (ssm[:, cols] - skip[:, cols] * values) - scaled * grad_scaled
        extra = jnp.sum(scaled * from_state, axis=0, keepdims=True) + end * jnp.sum(
            late * early, axis=0, keepdims=True
        )
        to_sum[CHUNK:, cols] = inner + jnp.where(last_row, extra, 0.0)
    ga_parts = split(grad_affinity)
    grad_mixed[:, INNER : INNER + NSTATE] = grad_b + dot3(ga_parts, c_parts)
    grad_mixed[:, INNER + NSTATE :] = grad_c + dot3(split(grad_affinity.T), b_parts)


    def by_head(v):
        high, low = split(v)
        return dot(high, gather[...]) + dot(low, gather[...])

    direct, grad_cum = by_head(to_sum[:CHUNK, :]), by_head(to_sum[CHUNK:, :])
    upper = (lane >= row).astype(BF16)
    after = triangle_sum(upper, grad_cum)
    grad_delta = direct + rate * after
    grad_raw = jnp.where(heads, grad_delta * sigmoid(shifted), 0.0)
    grad_low[:, DT_AT:] = grad_raw.astype(BF16)
    sums[0:1, :] += jnp.sum(grad_raw, axis=0, keepdims=True)
    sums[1:2, :] += rate * jnp.sum(delta * after, axis=0, keepdims=True)
    grad_low[:, :INNER] = grad_gate[...]
    for tile in range(MIXW // LANES):
        cols = slice(tile * LANES, (tile + 1) * LANES)
        w = conv_weight[:, cols]
        g = grad_mixed[:, cols] * slope[:, cols]
        rows = conv_in[:, cols]
        later = following[:, cols]
        total = jnp.zeros((CHUNK, LANES), F32)
        arriving = moved_up(shift.at[tile], g, later) + [g]
        for k in range(KCONV):
            conv_sums[8 * k : 8 * k + 8, cols] += eights(rows * arriving[k])
            total = total + arriving[k] * w[k : k + 1]
        conv_sums[8 * KCONV :, cols] += eights(g)
        following[:, cols] = g[:8]
        grad_low[:, INNER + tile * LANES : INNER + (tile + 1) * LANES] = total.astype(BF16)


def backward(
    conv_in, dt, ssm, grad, grad_gate, states, conv_weight, conv_bias, dt_bias, a_log, skip, gather
):
    length = conv_in.shape[0]
    chunks = length // CHUNK
    whole = lambda v: pl.BlockSpec(v.shape, lambda i: (0,) * v.ndim)
    by_row = lambda width: pl.BlockSpec((CHUNK, width), lambda i: (chunks - 1 - i, 0))
    return pl.pallas_call(
        backward_kernel,
        grid=(chunks,),
        out_shape=(
            shape((length, WIDE), BF16),
            shape((8, LANES), F32),
            shape((1, INNER), F32),
            shape((8 * (KCONV + 1), MIXW), F32),
        ),
        in_specs=[
            by_row(MIXW),
            pl.BlockSpec((8, MIXW), lambda i: (jnp.maximum((chunks - 1 - i) * (CHUNK // 8) - 1, 0), 0)),
            by_row(LANES),
            by_row(INNER),
            by_row(INNER),
            by_row(INNER),
            pl.BlockSpec((1, NSTATE, INNER), lambda i: (chunks - 1 - i, 0, 0)),
        ]
        + [whole(v) for v in (conv_weight, conv_bias, dt_bias, a_log, skip, gather)],
        out_specs=(
            by_row(WIDE),
            pl.BlockSpec((8, LANES), lambda i: (0, 0)),
            pl.BlockSpec((1, INNER), lambda i: (0, 0)),
            pl.BlockSpec((8 * (KCONV + 1), MIXW), lambda i: (0, 0)),
        ),
        scratch_shapes=[pltpu.VMEM((NSTATE, INNER), F32)]
        + [pltpu.VMEM((2 * CHUNK, INNER), F32)]
        + [pltpu.VMEM((CHUNK, MIXW), F32)] * 3
        + [pltpu.VMEM((8, MIXW), F32), pltpu.VMEM((MIXW // LANES, CHUNK + 8, LANES), F32)],
        compiler_params=params(),
        cost_estimate=cost(43),
    )(
        conv_in, conv_in, dt, ssm, grad, grad_gate, states,
        conv_weight, conv_bias, dt_bias, a_log, skip, gather,
    )


def moved_down(scratch, v, before):
    rows = v.shape[0]
    scratch[0:8, :] = before
    scratch[8 : 8 + rows, :] = v
    return [scratch[8 - by : 8 - by + rows, :] for by in range(KCONV - 1, 0, -1)]


def moved_up(scratch, v, behind):
    rows = v.shape[0]
    scratch[0:rows, :] = v
    scratch[rows : rows + 8, :] = behind
    return [scratch[by : by + rows, :] for by in range(KCONV - 1, 0, -1)]


def conv_sum(terms, weight, bias):
    total = bias + terms[KCONV - 1] * weight[KCONV - 1 : KCONV]
    for k in range(KCONV - 1):
        total = total + terms[k] * weight[k : k + 1]
    return total


def loss_kernel(
    limit, mixed_out, w_out, tokens, teacher, mask, block_out, grad_result, grad_branch, error
):
    step = pl.program_id(0)

    @pl.when(step == 0)
    def _():
        error[...] = jnp.zeros_like(error)

    rows = tokens.shape[0]
    result = tokens[...].astype(F32) + dot(mixed_out[...], w_out[...])
    position = step * rows + lax.broadcasted_iota(jnp.int32, (rows, 1), 0)
    valid = (position < limit[0]).astype(F32)
    turned = jnp.broadcast_to(mask[...].astype(F32), (LANES, rows)).T
    weight = valid * turned[:, 0:1]
    block_out[...] = (result * valid).astype(BF16)
    misfit = result - teacher[...].astype(F32)
    pulled = 2.0 * weight * misfit
    grad_result[...] = pulled
    errors = jnp.sum(0.5 * pulled * misfit, axis=0, keepdims=True)
    for j in range(D // LANES):
        error[j : j + 1, :] += errors[:, j * LANES : (j + 1) * LANES]
    error[D // LANES : D // LANES + 1, :] += jnp.sum(valid * turned, axis=0, keepdims=True)
    grad_branch[...] = pulled.astype(BF16)


def loss_part(limit, mixed_out, w_out, tokens, teacher, mask):
    length = tokens.shape[0]
    rows = 512
    by_row = lambda width: pl.BlockSpec((rows, width), lambda i: (i, 0))
    return pl.pallas_call(
        loss_kernel,
        grid=(length // rows,),
        out_shape=(
            shape((length, D), BF16),
            shape((length, D), F32),
            shape((length, D), BF16),
            shape((8, LANES), F32),
        ),
        in_specs=[
            SMEM,
            by_row(INNER),
            pl.BlockSpec(w_out.shape, lambda i: (0, 0)),
            by_row(D),
            by_row(D),
            pl.BlockSpec((1, rows), lambda i: (0, i)),
        ],
        out_specs=(by_row(D), by_row(D), by_row(D), pl.BlockSpec((8, LANES), lambda i: (0, 0))),
        compiler_params=params(),
        cost_estimate=cost(8),
    )(limit, mixed_out, w_out, tokens, teacher, mask)


def gate_kernel(grad_branch, w_out, ssm, gate, gain, grad_ssm, grad_gate, gain_sums):
    @pl.when(pl.program_id(0) == 0)
    def _():
        gain_sums[...] = jnp.zeros_like(gain_sums)

    grad_mixed = dot(grad_branch[...], w_out[...], NT)
    g = gate[...]
    sig = sigmoid(g)
    act = g * sig
    inner = ssm[...]
    gated = inner * act
    rho = lax.rsqrt(jnp.mean(gated * gated, axis=1, keepdims=True) + NORM_EPS)
    unit = gated * rho
    gain_sums[...] += jnp.sum(unit * grad_mixed, axis=0, keepdims=True)
    grad_unit = grad_mixed * gain[...]
    share = jnp.mean(grad_unit * unit, axis=1, keepdims=True)
    grad_gated = rho * (grad_unit - unit * share)
    grad_ssm[...] = grad_gated * act
    grad_gate[...] = (grad_gated * inner * (sig * (1.0 + g * (1.0 - sig)))).astype(BF16)


def gate_part(grad_branch, w_out, ssm, gate, gain):
    length = ssm.shape[0]
    rows = 256
    by_row = lambda width: pl.BlockSpec((rows, width), lambda i: (i, 0))
    whole = lambda v: pl.BlockSpec(v.shape, lambda i: (0,) * v.ndim)
    return pl.pallas_call(
        gate_kernel,
        grid=(length // rows,),
        out_shape=(shape((length, INNER), F32), shape((length, INNER), BF16), shape((1, INNER), F32)),
        in_specs=[by_row(D), whole(w_out), by_row(INNER), by_row(INNER), whole(gain)],
        out_specs=(by_row(INNER), by_row(INNER), pl.BlockSpec((1, INNER), lambda i: (0, 0))),
        compiler_params=params(),
        cost_estimate=cost(12),
    )(grad_branch, w_out, ssm, gate, gain)


def input_kernel(grad_low, w_in, tokens, norm_gain, grad_result, out, sums):
    @pl.when(pl.program_id(0) == 0)
    def _():
        sums[...] = jnp.zeros_like(sums)

    x = tokens[...].astype(F32)
    inverse = lax.rsqrt(jnp.mean(x * x, axis=1, keepdims=True) + NORM_EPS)
    unit = x * inverse
    grad_hidden = dot(grad_low[...], w_in[...], NT)
    sums[...] += jnp.sum(grad_hidden * unit, axis=0, keepdims=True)
    pulled = grad_hidden * norm_gain[...]
    share = jnp.mean(pulled * unit, axis=1, keepdims=True)
    out[...] = grad_result[...] + inverse * (pulled - unit * share)


def input_backward(grad_low, w_in, tokens, norm_gain, grad_result):
    length = tokens.shape[0]
    rows = 256
    by_row = lambda width: pl.BlockSpec((rows, width), lambda i: (i, 0))
    whole = lambda v: pl.BlockSpec(v.shape, lambda i: (0,) * v.ndim)
    return pl.pallas_call(
        input_kernel,
        grid=(length // rows,),
        out_shape=(shape((length, D), F32), shape((1, D), F32)),
        in_specs=[by_row(WIDE), whole(w_in), by_row(D), whole(norm_gain), by_row(D)],
        out_specs=(by_row(D), pl.BlockSpec((1, D), lambda i: (0, 0))),
        compiler_params=params(),
        cost_estimate=cost(15),
    )(grad_low, w_in, tokens, norm_gain, grad_result)


def vector_kernel(tail, conv_sums, sums, skip_sums, norm_sums, gate_sums, gather, out, taps):
    tiles = CONVCH // LANES
    out[...] = jnp.zeros_like(out)
    out[0:TAIL_ROWS, :] = tail[...]
    for k in range(KCONV):
        for i in range(tiles):
            partial_sums = conv_sums[8 * k : 8 * k + 8, i * LANES : (i + 1) * LANES]
            taps[k * 16 + i : k * 16 + i + 1, :] = jnp.sum(partial_sums, axis=0, keepdims=True)
    row = lax.broadcasted_iota(jnp.int32, (LANES, LANES), 0)
    col = lax.broadcasted_iota(jnp.int32, (LANES, LANES), 1)
    per_tile = LANES // KCONV

    def exact(v, chosen):
        high = v.astype(BF16)
        rest = v - high.astype(F32)
        middle = rest.astype(BF16)
        low = (rest - middle.astype(F32)).astype(BF16)
        return dot(high, chosen) + (dot(middle, chosen) + dot(low, chosen))

    for q in range(KCONV):
        total = jnp.zeros((tiles, LANES), F32)
        for k in range(KCONV):
            chosen = (col == KCONV * (row % per_tile) + k) & (row // per_tile == q)
            total = total + exact(taps[k * 16 : k * 16 + tiles, :], chosen.astype(BF16))
        out[pl.ds(TAIL_ROWS + q, tiles, stride=KCONV), :] = total
    bias_at = TAIL_ROWS + tiles * KCONV
    for i in range(tiles):
        partial_sums = conv_sums[8 * KCONV :, i * LANES : (i + 1) * LANES]
        out[bias_at + i : bias_at + i + 1, :] = jnp.sum(partial_sums, axis=0, keepdims=True)
    lane = lax.broadcasted_iota(jnp.int32, (1, LANES), 1)
    skip = exact(jnp.broadcast_to(skip_sums[...], (8, INNER)), gather[...])[0:1, :]
    parts = [sums[0:1, :], sums[1:2, :], skip]
    parts = [jnp.where(lane < HEADS, v, 0.0) for v in parts]
    before = parts[0] + pltpu.roll(parts[1], HEADS, 1) + pltpu.roll(parts[2], 2 * HEADS, 1)
    at, shift = bias_at + tiles, 3 * HEADS
    for source in (norm_sums, gate_sums):
        for j in range(source.shape[1] // LANES):
            here = pltpu.roll(source[:, j * LANES : (j + 1) * LANES], shift, 1)
            out[at : at + 1, :] = jnp.where(lane < shift, before, here)
            before = here
            at += 1
    out[at : at + 1, :] = jnp.where(lane < shift, before, 0.0)


def pack_vectors(tail, conv_sums, sums, skip_sums, norm_sums, gate_sums, gather):
    return pl.pallas_call(
        vector_kernel,
        out_shape=shape(((NBLK - MID1) * BROWS, LANES), F32),
        in_specs=[VMEM] * 7,
        out_specs=VMEM,
        scratch_shapes=[pltpu.VMEM((KCONV * 16, LANES), F32)],
        compiler_params=params(),
    )(tail, conv_sums, sums, skip_sums, norm_sums, gate_sums, gather)


def body(tokens, teacher, lengths, loss_mask, owners, master, first_moment, second_moment):
    capacity = master.shape[0]
    dp, fsdp = lax.axis_size("dp"), lax.axis_size("fsdp")
    devices = dp * fsdp
    me = lax.axis_index(AXES).astype(jnp.int32)
    x_first, y_first, z_first = step_orders(dp, fsdp)
    tie = lambda *values: lax.optimization_barrier(values)

    sent = send_blocks(owners, master, devices, me)
    at_home = lax.all_to_all(sent, AXES, 0, 0, tiled=True)
    owners, tokens, loss_mask, _ = tie(owners, tokens, loss_mask, sent)
    plan = make_plan(owners, capacity, devices, me)
    streams = cut(even(plan["slots"], 3), (x_first, y_first, z_first))
    table = stream_places(plan["home"], plan["slot"], me, streams, devices)
    u0, u1 = plan["unit_slots"]
    sizes = [3 * u0 // 16] * 4
    unit_streams = cut(sizes + [u0 - sum(sizes)], (x_first, y_first, x_first, y_first, z_first))
    order1 = x_first[:2] + x_first[2 + bits_of(fsdp) :] + x_first[2 : 2 + bits_of(fsdp)]
    unit_table, unit_table1 = [], []
    for u in range(UNITS):
        unit = UNITS * plan["order"] + u
        home, slot = unit % devices, unit // devices
        unit_table.append(stream_places(home, slot, me, unit_streams, devices)[:MID0])
        unit_table1.append((place_of(home ^ me, order1) * (u1 + 1) + slot)[MID0:MID1])
    unit_table, unit_table1 = quarters(unit_table), quarters(unit_table1)
    inputs, target = tokens[0], teacher[0]
    (at_home, table, unit_table, unit_table1, received, back_table, row_from, row_block,
     row_used) = tie(
        at_home, table, unit_table, unit_table1, plan["received"], plan["back"],
        plan["row_from"], plan["row_block"], plan["row_used"],
    )
    mine = pick_blocks(received, at_home, [size for _, size, _ in streams])
    parts = []
    for values, (_, _, order) in zip(mine, streams):
        parts += gather_steps(values, order)
    (input_weight, output_weight, conv_weight, conv_bias, dt_bias, a_log, skip, norm_gain,
     gate_gain, hidden, gate, conv_in, dt, ssm, mixed_out, states) = forward(
        table, inputs, parts
    )
    gather = heads_gather()
    block_out, grad_result, grad_branch, local = loss_part(
        lengths, mixed_out, output_weight, inputs, target, loss_mask
    )
    keep1, send1, head, tail = pack_out(
        unit_table1, mixed_out, grad_branch, local, devices, u1 + 1
    )
    grad_branch, send1 = tie(grad_branch, send1)
    got1 = exchange(send1, order1[0])
    grad_ssm, grad_gate, gain_sums = gate_part(grad_branch, output_weight, ssm, gate, gate_gain)
    grad_ssm, keep1, got1 = tie(grad_ssm, keep1, got1)
    keep1, got1 = reduce_step(keep1, got1, order1[1])
    grad_low, sums, skip_sums, conv_sums = backward(
        conv_in, dt, ssm, grad_ssm, grad_gate, states,
        conv_weight, conv_bias, dt_bias, a_log, skip, gather,
    )
    grad_low, keep1, got1 = tie(grad_low, keep1, got1)
    steps1 = order1[2:]
    for step in steps1[:1]:
        keep1, got1 = reduce_step(keep1, got1, step)
    halves = []
    for _, size, _ in unit_streams:
        halves += [devices * size // 2] * 2
    packed = list(pack_in(unit_table, hidden, grad_low, head, halves))
    packed[0], keep1, got1 = tie(packed[0], keep1, got1)
    kept = packed[::2]
    got = [exchange(v, order[0]) for v, (_, _, order) in zip(packed[1::2], unit_streams)]
    *got, grad_low, conv_sums, tail = tie(*got, grad_low, conv_sums, tail)
    for i, (_, _, order) in enumerate(unit_streams):
        kept[i], got[i] = reduce_step(kept[i], got[i], order[1])
    for step in steps1[1:2]:
        keep1, got1 = reduce_step(keep1, got1, step)
    input_grad, norm_sums = input_backward(grad_low, input_weight, inputs, norm_gain, grad_result)
    grad_vec = pack_vectors(tail, conv_sums, sums, skip_sums, norm_sums, gain_sums, gather)
    grad_vec = grad_vec.reshape((NBLK - MID1) * UNITS, UNIT, LANES)
    *got, got1, grad_vec, input_grad = tie(*got, got1, grad_vec, input_grad)
    for step in steps1[2:]:
        keep1, got1 = reduce_step(keep1, got1, step)
    for k in range(2, len(x_first)):
        for i, (_, _, order) in enumerate(unit_streams):
            if i == 0:
                kept[i], got[i], grad_vec = reduce_step(kept[i], got[i], order[k], grad_vec)
            else:
                kept[i], got[i] = reduce_step(kept[i], got[i], order[k])
    back = units_to_owners(back_table, list(zip(kept + [keep1], got + [got1])))
    back, grad_vec = tie(back, grad_vec)
    returned = lax.all_to_all(back, AXES, 0, 0, tiled=True)
    for step in x_first[:2]:
        grad_vec = grad_vec + exchange(grad_vec, step)
    local_sums = keep1[u1] + got1[u1]
    error_sum = jnp.sum(local_sums[: D // LANES])
    divisor = local_sums[D // LANES, 0] * D
    new_first, new_second, new_master = adam(
        row_from,
        row_block,
        row_used,
        divisor,
        returned,
        grad_vec,
        master,
        first_moment,
        second_moment,
    )
    mean_loss = error_sum / divisor
    return (block_out[None], input_grad[None], mean_loss, new_first, new_second, new_master)


def solution(mesh):
    return jax.shard_map(
        body,
        mesh=mesh,
        in_specs=(
            P(AXES, None, None),
            P(AXES, None, None),
            P(AXES),
            P(AXES, None),
            P(),
            P(AXES, None),
            P(AXES, None),
            P(AXES, None),
        ),
        out_specs=(
            P(AXES, None, None),
            P(AXES, None, None),
            P(),
            P(AXES, None),
            P(AXES, None),
            P(AXES, None),
        ),
        check_vma=False,
    )
```
